32 devices in a mesh: dp: 4 (over z), expert: 8 (over y, x, core).
Axes of the slice: x: 2, y: 2, z: 4, core: 2. Of those that a mesh axis runs over, the one named last changes fastest.
Arguments:
- tokens: bfloat16 [4096, 2048], P(('dp', 'expert')), may hold values from -6 to 6
- cotangent: bfloat16 [4096, 2048], P(('dp', 'expert')), may hold values from -6 to 6
- lengths: int32 [4], P('dp'), may hold values from 897 to 1024, as said below
- routes: int32 [4096, 6], P(('dp', 'expert')), may hold values from 0 to 15, all different within a row
- place_order: int32 [32, 768], P(('dp', 'expert')), may hold values from 0 to 767, each once within a row
- attn_gain: bfloat16 [2048], P(('dp', 'expert')), may hold values from 0.099609375 to 1.8984375
- w_query: bfloat16 [2048, 3072], P(('dp', 'expert')), may hold values from -0.125 to 0.125
- w_latent: bfloat16 [2048, 576], P(('dp', 'expert')), may hold values from -0.125 to 0.125
- latent_gain: bfloat16 [512], P(('dp', 'expert')), may hold values from 0.099609375 to 1.8984375
- w_expand: bfloat16 [512, 4096], P(('dp', 'expert')), may hold values from -0.25 to 0.25
- w_out: bfloat16 [2048, 2048], P(('dp', 'expert')), may hold values from -1 to 1
- ffn_gain: bfloat16 [2048], P(('dp', 'expert')), may hold values from 0.099609375 to 1.8984375
- w_router: bfloat16 [2048, 16], P(('dp', 'expert')), may hold values from -0.0625 to 0.0625
- shared_gate: bfloat16 [2048, 2816], P(('dp', 'expert')), may hold values from -0.125 to 0.125
- shared_up: bfloat16 [2048, 2816], P(('dp', 'expert')), may hold values from -0.125 to 0.125
- shared_down: bfloat16 [2048, 2816], P(('dp', 'expert')), may hold values from -0.109375 to 0.109375
- expert_gate: bfloat16 [16, 2048, 1408], P('expert', 'dp'), may hold values from -0.125 to 0.125
- expert_up: bfloat16 [16, 2048, 1408], P('expert', 'dp'), may hold values from -0.125 to 0.125
- expert_down: bfloat16 [16, 2048, 1408], P('expert', 'dp'), may hold values from -1.25 to 1.25
Outputs:
- out_tokens: bfloat16 [4096, 2048], P(('dp', 'expert'))
- grad_tokens: float32 [4096, 2048], P(('dp', 'expert'))
- grad_attn_gain: float32 [2048], P(('dp', 'expert'))
- grad_w_query: float32 [2048, 3072], P(('dp', 'expert'))
- grad_w_latent: float32 [2048, 576], P(('dp', 'expert'))
- grad_latent_gain: float32 [512], P(('dp', 'expert'))
- grad_w_expand: float32 [512, 4096], P(('dp', 'expert'))
- grad_w_out: float32 [2048, 2048], P(('dp', 'expert'))
- grad_ffn_gain: float32 [2048], P(('dp', 'expert'))
- grad_w_router: float32 [2048, 16], P(('dp', 'expert'))
- grad_shared_gate: float32 [2048, 2816], P(('dp', 'expert'))
- grad_shared_up: float32 [2048, 2816], P(('dp', 'expert'))
- grad_shared_down: float32 [2048, 2816], P(('dp', 'expert'))
- grad_expert_gate: float32 [16, 2048, 1408], P('expert', 'dp')
- grad_expert_up: float32 [16, 2048, 1408], P('expert', 'dp')
- grad_expert_down: float32 [16, 2048, 1408], P('expert', 'dp')
The draws below stay inside these ranges and needn't reach their ends.
Inputs may be any that keep to these rules, and one draw needn't show every extreme that they name: `lengths`: each group's length reaches the group's last device, and some group has the full 1024. `routes`: each row names 6 different experts. `place_order`: each device's row is a permutation.
All inputs are finite; a program needn't handle non-finite values.
Results may differ from the reference program's by a relative error of at most 0.02.
Values may be sent and summed in bfloat16 or wider, within the bound.
A program may use at most 448 MiB of HBM per device.

```python
import jax
import jax.numpy as jnp
from jax import lax

D = 2048
H = 16
DH = 128
DR = 64
DV = 128
KVR = 512
FFE = 1408
FFS = 2816
TOPK = 6
SEQ_LEN = 1024
EXPERTS = 16
ROWS = 128
TOKENS = 4096
CAP = 60
N_DP = 4
N_EXPERT = 8


def draw_lengths(key, part):
    key = jax.random.fold_in(key, 11)
    key_cut, key_full = jax.random.split(key)
    cut_rows = jax.random.randint(key_cut, (N_DP,), 0, ROWS)
    full_group = jax.random.randint(key_full, (), 0, N_DP)
    cut_rows = jnp.where(jnp.arange(N_DP) == full_group, 0, cut_rows)
    return (SEQ_LEN - cut_rows).astype(jnp.int32)


def steps_of(own_key, shape, pieces, smallest, top_value):
    level = 1.0
    for axis_at, parts in pieces:
        steps = jax.random.uniform(jax.random.fold_in(jax.random.fold_in(own_key, 6), axis_at), (parts,), jnp.float32, smallest / len(pieces), top_value / len(pieces))
        level = level * jnp.repeat(jnp.exp(steps), shape[axis_at] // parts).reshape((-1,) + (1,) * (len(shape) - 1 - axis_at))
    return level


def distinct(rng, rows, count, top, lift):
    sequence = jax.random.permutation(jax.random.fold_in(rng, 1), count)
    pull = sequence
    for power in range(3):
        pull = pull * pull // count
    pull = pull * lift // count
    lots = jax.random.randint(jax.random.fold_in(rng, 2), (rows, count), 0, 4096) + pull
    sure = jax.random.permutation(jax.random.fold_in(rng, 3), rows)[jnp.arange(count) % rows]
    lots = jnp.where(jnp.arange(rows)[:, None] == sure[None, :], 1 << 14, lots)
    score = lots * count + jnp.arange(count)
    return lax.top_k(score.astype(jnp.int32), top)[1].astype(jnp.int32)


def gaussian(own_key, shape, deviation, bound, cuts=(), held_as=jnp.bfloat16):
    level = steps_of(own_key, shape, cuts, -0.22, 0.18) if cuts else 1.0
    drawn = jax.random.normal(own_key, shape, jnp.float32) * deviation * level
    return jnp.minimum(jnp.maximum(drawn, -bound), bound).astype(held_as)


def setup_inputs(seed: int = 0) -> dict:
    streams_of = jax.random.split(jax.random.key(seed), 20)
    tokens = gaussian(streams_of[0], (TOKENS, D), 1.0, 6.0, ((0, 32),))
    cotangent = gaussian(streams_of[1], (TOKENS, D), 1.0, 6.0, ((0, 32),))
    lengths = draw_lengths(jax.random.fold_in(streams_of[19], 71), 0)
    routes = distinct(streams_of[3], TOKENS, EXPERTS, TOPK, 3072)
    place_order = jax.vmap(lambda own: jax.random.permutation(own, ROWS * TOPK))(jax.random.split(streams_of[4], (N_DP * N_EXPERT))).reshape((N_DP * N_EXPERT, ROWS * TOPK)).astype(jnp.int32)
    attn_gain = jnp.clip(1.0 + 0.18 * jax.random.normal(streams_of[5], (D,), jnp.float32), 0.099609375, 1.8984375).astype(jnp.bfloat16)
    w_query = gaussian(streams_of[6], (D, H * (DH + DR)), D ** -0.5, 0.125, ((0, 32),))
    w_latent = gaussian(streams_of[7], (D, KVR + DR), D ** -0.5, 0.125, ((0, 32),))
    latent_gain = jnp.clip(1.0 + 0.18 * jax.random.normal(streams_of[8], (KVR,), jnp.float32), 0.099609375, 1.8984375).astype(jnp.bfloat16)
    w_expand = gaussian(streams_of[9], (KVR, H * (DH + DV)), KVR ** -0.5, 0.25, ((0, 32),))
    w_out = gaussian(streams_of[10], (H * DV, D), (H * DV // 64) ** -0.5, 1.0, ((0, 32),))
    ffn_gain = jnp.clip(1.0 + 0.18 * jax.random.normal(streams_of[11], (D,), jnp.float32), 0.099609375, 1.8984375).astype(jnp.bfloat16)
    w_router = gaussian(streams_of[12], (D, EXPERTS), (4 * D) ** -0.5, 0.0625, ((0, 32),))
    shared_gate = gaussian(streams_of[13], (D, FFS), D ** -0.5, 0.125, ((0, 32),))
    shared_up = gaussian(streams_of[14], (D, FFS), D ** -0.5, 0.125, ((0, 32),))
    shared_down = gaussian(streams_of[15], (D, FFS), FFS ** -0.5, 0.109375, ((0, 32),))
    expert_gate = gaussian(streams_of[16], (EXPERTS, D, FFE), D ** -0.5, 0.125, ((0, 8), (1, 4)))
    expert_up = gaussian(streams_of[17], (EXPERTS, D, FFE), D ** -0.5, 0.125, ((0, 8), (1, 4)))
    expert_down = gaussian(streams_of[18], (EXPERTS, D, FFE), (FFE // 64) ** -0.5, 1.25, ((0, 8), (1, 4)))
    return {"tokens": tokens, "cotangent": cotangent, "lengths": lengths, "routes": routes, "place_order": place_order, "attn_gain": attn_gain, "w_query": w_query, "w_latent": w_latent, "latent_gain": latent_gain, "w_expand": w_expand, "w_out": w_out, "ffn_gain": ffn_gain, "w_router": w_router, "shared_gate": shared_gate, "shared_up": shared_up, "shared_down": shared_down, "expert_gate": expert_gate, "expert_up": expert_up, "expert_down": expert_down}


@jax.custom_vjp
def low(v):
    return lax.optimization_barrier(v.astype(jnp.bfloat16)).astype(jnp.float32)

@jax.custom_vjp
def low_back(v):
    return v

def low_keep(v):
    return (low(v), None)

def low_pass(kept, grad):
    return (grad,)

def back_keep(v):
    return (v, None)

def back_low(kept, grad):
    return (low(grad),)
low.defvjp(low_keep, low_pass)
low_back.defvjp(back_keep, back_low)
norm_eps = 1e-06
masked_score = -1e+30
exact_mode = lax.Precision.HIGHEST

def highest(pattern, left_side, right_side):
    return jnp.einsum(pattern, left_side, right_side, precision=exact_mode)

def rms_norm(values, scale_gain):
    return values * lax.rsqrt(lax.optimization_barrier(jnp.mean(values * values, axis=-1, keepdims=True)) + norm_eps) * scale_gain

def rotate(values, cos_table, sine_table):
    half_dim = values.shape[-1] // 2
    first_half = values[..., :half_dim]
    second_half = values[..., half_dim:]
    return jnp.concatenate([first_half * cos_table - second_half * sine_table, second_half * cos_table + first_half * sine_table], axis=-1)

def rope_tables(positions):
    half_dim = DR // 2
    inv_freq = 10000.0 ** (-(jnp.arange(half_dim).astype(jnp.float32) * 2.0) / DR)
    angles = positions.astype(jnp.float32)[:, None] * inv_freq[None, :]
    return (jnp.cos(angles), jnp.sin(angles))

def slot_places(route_rows, pair_order):
    pair_expert = route_rows.reshape(-1)
    earlier = pair_order[None, :] < pair_order[:, None]
    same_expert = pair_expert[None, :] == pair_expert[:, None]
    places = lax.optimization_barrier(jnp.sum((earlier & same_expert).astype(jnp.int32), axis=1))
    slot_index = jnp.where(places < CAP, pair_expert * CAP + places, -1)
    return slot_index.reshape(route_rows.shape).astype(jnp.int32)

def layer_group(group_tokens, weights, seq_length, group_routes, group_order):
    attn_gain, w_query, w_latent, latent_gain, w_expand, w_out, ffn_gain, w_router, shared_gate, shared_up, shared_down, expert_gate, expert_up, expert_down = weights
    cos_table, sine_table = rope_tables(jnp.arange(SEQ_LEN))
    normed = low(rms_norm(group_tokens, attn_gain))
    query_raw = low_back(highest('td,df->tf', normed, w_query)).reshape(SEQ_LEN, H, DH + DR)
    queries = low(jnp.concatenate([query_raw[..., :DH], rotate(query_raw[..., DH:], cos_table[:, None, :], sine_table[:, None, :])], axis=-1))
    latent_raw = low_back(highest('td,df->tf', normed, w_latent))
    latent_normed = low(rms_norm(latent_raw[:, :KVR], latent_gain))
    rope_keys = low(rotate(latent_raw[:, KVR:], cos_table, sine_table))
    expanded = low(highest('tc,cf->tf', latent_normed, w_expand)).reshape(SEQ_LEN, H, DH + DV)
    key_nope = expanded[..., :DH]
    value_rows = expanded[..., DH:]
    block_rows = min(512, SEQ_LEN)
    score_scale = (DH + DR) ** (-0.5)

    def attend(block_start):
        query_block = lax.dynamic_slice_in_dim(queries, block_start, block_rows, 0)
        raw_scores = low_back(highest('qhd,khd->hqk', query_block[..., :DH], key_nope) + highest('qhr,kr->hqk', query_block[..., DH:], rope_keys))
        query_pos = block_start + jnp.arange(block_rows)
        key_pos = jnp.arange(SEQ_LEN)
        allowed = (key_pos[None, :] <= query_pos[:, None]) & (key_pos[None, :] < seq_length)
        scores = jnp.where(allowed[None], raw_scores * score_scale, masked_score)
        top_score = lax.optimization_barrier(jnp.max(scores, axis=-1, keepdims=True))
        exp_scores = jnp.exp(scores - top_score)
        attn_probs = low(exp_scores / lax.optimization_barrier(jnp.sum(exp_scores, axis=-1, keepdims=True)))
        return low(low_back(highest('hqk,khv->qhv', attn_probs, value_rows)))
    block_starts = (jnp.arange(SEQ_LEN // block_rows) * block_rows).astype(jnp.int32)
    attended = lax.map(jax.checkpoint(attend), block_starts).reshape(SEQ_LEN, H * DV)
    residual = group_tokens + low_back(highest('tf,fd->td', attended, w_out))
    normed_two = low(rms_norm(residual, ffn_gain))
    logits = low_back(highest('td,de->te', normed_two, w_router))
    top_logit = lax.optimization_barrier(jnp.max(logits, axis=-1, keepdims=True))
    exp_logits = jnp.exp(logits - top_logit)
    router_probs = exp_logits / lax.optimization_barrier(jnp.sum(exp_logits, axis=-1, keepdims=True))
    chosen = (group_routes[..., None] == jnp.arange(EXPERTS)[None, None, :]).astype(jnp.float32)
    gate_values = lax.optimization_barrier(jnp.sum(router_probs[:, None, :] * chosen, axis=-1))
    shared_a = low_back(highest('td,df->tf', normed_two, shared_gate))
    shared_b = low_back(highest('td,df->tf', normed_two, shared_up))
    shared_hidden = low(jax.nn.silu(shared_a) * shared_b)
    shared_out = low_back(highest('tf,df->td', shared_hidden, shared_down))
    device_routes = group_routes.reshape(N_EXPERT, ROWS, TOPK)
    slot_index = jax.vmap(slot_places)(device_routes, group_order)
    pair_hot = (slot_index[..., None] == jnp.arange(EXPERTS * CAP)[None, None, None, :]).astype(jnp.float32)
    dispatch = lax.optimization_barrier(jnp.sum(pair_hot, axis=2))
    slots = low_back(highest('nre,nrd->ned', dispatch, normed_two.reshape(N_EXPERT, ROWS, D))).reshape(N_EXPERT, EXPERTS, CAP, D)
    expert_a = low_back(highest('necd,edf->necf', slots, expert_gate))
    expert_second_operand = low_back(highest('necd,edf->necf', slots, expert_up))
    expert_hidden = low(jax.nn.silu(expert_a) * expert_second_operand)
    expert_rows = low(low_back(highest('necf,edf->necd', expert_hidden, expert_down))).reshape(N_EXPERT, EXPERTS * CAP, D)
    pair_rows = highest('nrke,ned->nrkd', pair_hot, expert_rows).reshape(SEQ_LEN, TOPK, D)
    routed = lax.optimization_barrier(jnp.sum(gate_values[..., None] * pair_rows, axis=1))
    return residual + shared_out + routed

def reference(tokens, cotangent, lengths, routes, place_order, attn_gain, w_query, w_latent, latent_gain, w_expand, w_out, ffn_gain, w_router, shared_gate, shared_up, shared_down, expert_gate, expert_up, expert_down):
    weights = tuple((weight.astype(jnp.float32) for weight in (attn_gain, w_query, w_latent, latent_gain, w_expand, w_out, ffn_gain, w_router, shared_gate, shared_up, shared_down, expert_gate, expert_up, expert_down)))
    grouped = tokens.astype(jnp.float32).reshape(N_DP, SEQ_LEN, D)
    cot_groups = cotangent.astype(jnp.float32).reshape(N_DP, SEQ_LEN, D)
    route_groups = routes.reshape(N_DP, SEQ_LEN, TOPK)
    order_groups = place_order.reshape(N_DP, N_EXPERT, ROWS * TOPK)
    zero_grads = jax.tree.map(jnp.zeros_like, weights)

    def one_group(totals, inputs):
        group_tokens, group_cot, seq_length, group_routes, group_order = inputs

        def forward(tokens_in, weights_in):
            return layer_group(tokens_in, weights_in, seq_length, group_routes, group_order)
        result, pullback = jax.vjp(forward, group_tokens, weights)
        grad_in, grad_weights = pullback(group_cot)
        return (jax.tree.map(jnp.add, totals, grad_weights), (result, grad_in))
    totals, (results, grad_inputs) = lax.scan(one_group, zero_grads, (grouped, cot_groups, lengths, route_groups, order_groups))
    return (results.reshape(TOKENS, D).astype(jnp.bfloat16), grad_inputs.reshape(TOKENS, D), totals[0], totals[1], totals[2], totals[3], totals[4], totals[5], totals[6], totals[7], totals[8], totals[9], totals[10], totals[11], totals[12], totals[13])
```

```python
import jax
import jax.numpy as jnp
from jax import lax
from jax.experimental import pallas as pl
from jax.experimental.pallas import tpu as pltpu
from jax.sharding import PartitionSpec as P

H = 16
DH = 128
DR = 64
DV = 128
KVR = 512

norm_eps = 1e-06
masked_score = -1e30
MESH = pl.DeviceIdType.MESH
ANY = pl.BlockSpec(memory_space=pl.ANY)
VMEM = pl.BlockSpec(memory_space=pltpu.VMEM)
BF = jnp.bfloat16
F32 = jnp.float32


def rms_norm(values, scale_gain):
    return (
        values
        * lax.rsqrt(jnp.mean(values * values, axis=-1, keepdims=True) + norm_eps)
        * scale_gain
    )


def rotate(values, cos_table, sine_table):
    half_dim = values.shape[-1] // 2
    first_half = values[..., :half_dim]
    second_half = values[..., half_dim:]
    return jnp.concatenate(
        [
            first_half * cos_table - second_half * sine_table,
            second_half * cos_table + first_half * sine_table,
        ],
        axis=-1,
    )


def rope_tables(positions):
    half_dim = DR // 2
    inv_freq = 10000.0 ** (-(jnp.arange(half_dim).astype(F32) * 2.0) / DR)
    angles = positions.astype(F32)[:, None] * inv_freq[None, :]
    return (jnp.cos(angles), jnp.sin(angles))


def swiglu(gate_in, up_in):
    return jax.nn.silu(gate_in) * up_in


def mm(left, right):
    return jnp.dot(left, right, preferred_element_type=F32)


def mm_rows(left, right):
    return lax.dot_general(left, right, (((0,), (0,)), ((), ())), preferred_element_type=F32)


def mm_cols(left, right):
    return lax.dot_general(left, right, (((1,), (1,)), ((), ())), preferred_element_type=F32)


def slot_places(route_rows, pair_order, capacity):
    pair_expert = route_rows.reshape(-1)
    earlier = pair_order[None, :] < pair_order[:, None]
    same_expert = pair_expert[None, :] == pair_expert[:, None]
    places = jnp.sum((earlier & same_expert).astype(jnp.int32), axis=1)
    slot_index = jnp.where(places < capacity, pair_expert * capacity + places, -1)
    return slot_index.reshape(route_rows.shape)


def params(collective_id):
    return pltpu.CompilerParams(
        collective_id=collective_id, has_side_effects=True, vmem_limit_bytes=48 << 20
    )


def remote(src, dst, send_sem, recv_sem, device):
    return pltpu.make_async_remote_copy(
        src_ref=src,
        dst_ref=dst,
        send_sem=send_sem,
        recv_sem=recv_sem,
        device_id=device,
        device_id_type=MESH,
    )


def greet(devices):
    barrier = pltpu.get_barrier_semaphore()
    for device in devices:
        pl.semaphore_signal(barrier, inc=1, device_id=device, device_id_type=MESH)
    pl.semaphore_wait(barrier, len(devices))


def places(n_dp, n_ex):
    z = lax.axis_index("dp")
    e = lax.axis_index("expert")
    chips = n_ex // 2
    c, k = e // 2, lax.rem(e, 2)
    sibling = (z, e + 1 - 2 * k)
    same_core = [(z, lax.rem(c + i, chips) * 2 + k) for i in range(1, chips)]
    column = [(lax.rem(z + i, n_dp), e) for i in range(1, n_dp)]
    return z, e, c, k, sibling, same_core, column


def plane_gather(block, n_dp, n_ex, collective_id):
    chips = n_ex // 2

    def kernel(x_ref, o_ref, send, recv, sib_send, sib_recv, local):
        z, e, c, k, sibling, same_core, _ = places(n_dp, n_ex)
        greet(same_core + [sibling])
        far = []
        for i in range(1, chips):
            copy = remote(x_ref, o_ref.at[e], send.at[i], recv.at[i], same_core[i - 1])
            copy.start()
            far.append(copy)
        near = [remote(x_ref, o_ref.at[e], sib_send.at[0], sib_recv.at[0], sibling)]
        near[0].start()
        own = pltpu.make_async_copy(x_ref, o_ref.at[e], local)
        own.start()
        for i in range(1, chips):
            source = lax.rem(c + chips - i, chips) * 2 + k
            far[i - 1].wait_recv()
            copy = remote(
                o_ref.at[source], o_ref.at[source], sib_send.at[i], sib_recv.at[i], sibling
            )
            copy.start()
            near.append(copy)
        own.wait()
        for copy in far:
            copy.wait_send()
        for copy in near:
            copy.wait()

    return pl.pallas_call(
        kernel,
        out_shape=jax.ShapeDtypeStruct((n_ex,) + block.shape, block.dtype),
        in_specs=[ANY],
        out_specs=ANY,
        scratch_shapes=[pltpu.SemaphoreType.DMA((chips,))] * 4 + [pltpu.SemaphoreType.DMA],
        compiler_params=params(collective_id),
    )(block)


def plane_sum(blocks, n_dp, n_ex, collective_id):
    chips = n_ex // 2
    rows, cols = blocks.shape[1:]

    def kernel(x_ref, o_ref, from_sib, out_buf, from_far, send, recv, sib_send, sib_recv):
        z, e, c, k, sibling, same_core, _ = places(n_dp, n_ex)
        greet(same_core + [sibling])
        near = []
        for i in list(range(1, chips)) + [0]:
            chip = lax.rem(c + i, chips)
            copy = remote(
                x_ref.at[chip * 2 + 1 - k],
                from_sib.at[chip],
                sib_send.at[i],
                sib_recv.at[i],
                sibling,
            )
            copy.start()
            near.append(copy)
        far = []
        for i in range(1, chips):
            chip = lax.rem(c + i, chips)
            near[i - 1].wait_recv()
            out_buf[i] = (
                x_ref[chip * 2 + k].astype(F32) + from_sib[chip].astype(F32)
            ).astype(BF)
            copy = remote(out_buf.at[i], from_far.at[i], send.at[i], recv.at[i], same_core[i - 1])
            copy.start()
            far.append(copy)
        near[chips - 1].wait_recv()
        o_ref[...] = x_ref[e].astype(F32) + from_sib[c].astype(F32)
        for i in range(1, chips):
            far[i - 1].wait_recv()
            o_ref[...] += from_far[i].astype(F32)
        for copy in near:
            copy.wait_send()
        for copy in far:
            copy.wait_send()

    return pl.pallas_call(
        kernel,
        out_shape=jax.ShapeDtypeStruct((rows, cols), F32),
        in_specs=[VMEM],
        out_specs=VMEM,
        scratch_shapes=[pltpu.VMEM((chips, rows, cols), BF)] * 3
        + [pltpu.SemaphoreType.DMA((chips,))] * 4,
        compiler_params=params(collective_id),
    )(blocks)


def column_gather(block, n_dp, n_ex, collective_id):
    def kernel(x_ref, o_ref, send, recv, local):
        z, e, c, k, sibling, same_core, column = places(n_dp, n_ex)
        greet(column)
        copies = []
        for i in range(1, n_dp):
            copy = remote(x_ref, o_ref.at[z], send.at[i], recv.at[i], column[i - 1])
            copy.start()
            copies.append(copy)
        own = pltpu.make_async_copy(x_ref, o_ref.at[z], local)
        own.start()
        own.wait()
        for copy in copies:
            copy.wait()

    return pl.pallas_call(
        kernel,
        out_shape=jax.ShapeDtypeStruct((n_dp,) + block.shape, block.dtype),
        in_specs=[ANY],
        out_specs=ANY,
        scratch_shapes=[pltpu.SemaphoreType.DMA((n_dp,))] * 2 + [pltpu.SemaphoreType.DMA],
        compiler_params=params(collective_id),
    )(block)


def first_exchange(tok, heads_w, pack, n_dp, n_ex, collective_id):
    chips = n_ex // 2

    def kernel(
        tok_ref, wa_ref, pk_ref, tok_out, wa_out, pk_out,
        t_send, t_recv, ts_send, ts_recv, a_send, a_recv, az_send, az_recv,
        p_send, p_recv, pf_send, pf_recv, ps_send, ps_recv, local,
    ):
        z, e, c, k, sibling, same_core, column = places(n_dp, n_ex)
        plane = [(z, lax.rem(e + i, n_ex)) for i in range(1, n_ex)]
        greet(plane + column)
        wa_far, pk_col, tok_far = [], [], []
        for i in range(1, n_ex):
            copy = remote(
                wa_ref.at[lax.rem(e + i, n_ex)], wa_out.at[z, e],
                a_send.at[i], a_recv.at[i], plane[i - 1],
            )
            copy.start()
            wa_far.append(copy)
        for i in range(1, n_dp):
            copy = remote(pk_ref, pk_out.at[z, e], p_send.at[i], p_recv.at[i], column[i - 1])
            copy.start()
            pk_col.append(copy)
        for i in range(1, chips):
            copy = remote(tok_ref, tok_out.at[e], t_send.at[i], t_recv.at[i], same_core[i - 1])
            copy.start()
            tok_far.append(copy)
        near = [remote(tok_ref, tok_out.at[e], ts_send.at[0], ts_recv.at[0], sibling)]
        near[0].start()
        own = [
            pltpu.make_async_copy(wa_ref.at[e], wa_out.at[z, e], local.at[0]),
            pltpu.make_async_copy(pk_ref, pk_out.at[z, e], local.at[1]),
            pltpu.make_async_copy(tok_ref, tok_out.at[e], local.at[2]),
        ]
        for copy in own:
            copy.start()
        for copy in own:
            copy.wait()
        for copy in wa_far:
            copy.wait_recv()
        wa_col = []
        for i in range(1, n_dp):
            copy = remote(
                wa_out.at[z], wa_out.at[z], az_send.at[i], az_recv.at[i], column[i - 1]
            )
            copy.start()
            wa_col.append(copy)
        for copy in pk_col:
            copy.wait_recv()
        pk_far = []
        for i in range(1, chips):
            copy = remote(
                pk_out.at[:, e], pk_out.at[:, e], pf_send.at[i], pf_recv.at[i], same_core[i - 1]
            )
            copy.start()
            pk_far.append(copy)
        copy = remote(pk_out.at[:, e], pk_out.at[:, e], ps_send.at[0], ps_recv.at[0], sibling)
        copy.start()
        near.append(copy)
        for i in range(1, chips):
            source = lax.rem(c + chips - i, chips) * 2 + k
            tok_far[i - 1].wait_recv()
            copy = remote(
                tok_out.at[source], tok_out.at[source], ts_send.at[i], ts_recv.at[i], sibling
            )
            copy.start()
            near.append(copy)
            pk_far[i - 1].wait_recv()
            copy = remote(
                pk_out.at[:, source], pk_out.at[:, source], ps_send.at[i], ps_recv.at[i], sibling
            )
            copy.start()
            near.append(copy)
        for copy in near + wa_col:
            copy.wait()
        for copy in wa_far + pk_col + tok_far + pk_far:
            copy.wait_send()

    dma = pltpu.SemaphoreType.DMA
    return pl.pallas_call(
        kernel,
        out_shape=[
            jax.ShapeDtypeStruct((n_ex,) + tok.shape, tok.dtype),
            jax.ShapeDtypeStruct((n_dp,) + heads_w.shape, heads_w.dtype),
            jax.ShapeDtypeStruct((n_dp, n_ex) + pack.shape, pack.dtype),
        ],
        in_specs=[ANY] * 3,
        out_specs=[ANY] * 3,
        scratch_shapes=[dma((chips,))] * 4
        + [dma((n_ex,))] * 2
        + [dma((n_dp,))] * 4
        + [dma((chips,))] * 4
        + [dma((3,))],
        compiler_params=params(collective_id),
    )(tok, heads_w, pack)


def shards(
    tokens,
    cotangent,
    lengths,
    routes,
    place_order,
    attn_gain,
    w_query,
    w_latent,
    latent_gain,
    w_expand,
    w_out,
    ffn_gain,
    w_router,
    shared_gate,
    shared_up,
    shared_down,
    expert_gate,
    expert_up,
    expert_down,
):
    rows, width = tokens.shape
    n_dp = lax.axis_size("dp")
    n_ex = lax.axis_size("expert")
    chips = n_ex // 2
    z = lax.axis_index("dp")
    e = lax.axis_index("expert")
    chip, core = e // 2, lax.rem(e, 2)
    n_experts = w_router.shape[1]
    top_k = routes.shape[1]
    capacity = (rows * top_k * 5 + 4 * n_experts - 1) // (4 * n_experts)
    cap = (capacity + 15) // 16 * 16
    seq = rows * n_ex
    r = w_query.shape[0]
    rl = w_expand.shape[0]
    hp = H // n_ex
    parts = DV // r
    heads = [
        (d * n_ex + (j // parts) * parts) * r // DV
        for j in range(n_ex)
        for d in range(j % parts * hp, j % parts * hp + hp)
    ]
    heads_back = [heads.index(h) for h in range(H)]
    per_chip = n_experts // chips
    splits = n_dp // per_chip
    my_local = z // splits
    same_core_groups = [[2 * i + s for i in range(chips)] for s in range(2)]
    pair_groups = [[2 * i, 2 * i + 1] for i in range(chips)]
    sib_perm = [(i, i ^ 1) for i in range(n_ex)]
    part_groups = [[i * parts + m for m in range(parts)] for i in range(n_ex // parts)]
    ff_e = expert_gate.shape[2]
    ff_part = ff_e // splits
    half = expert_gate.shape[1] // 2
    ff_s = shared_gate.shape[1] // n_dp
    lat = KVR + DR
    head_cols = hp * (DH + DR)
    kv_cols = hp * (DH + DV)

    wq_send = jnp.take(w_query.reshape(r, H, DH + DR), jnp.array(heads), axis=1)
    wq_send = wq_send.reshape(r, n_ex, head_cols).transpose(1, 0, 2)
    we_send = jnp.take(w_expand.reshape(rl, H, DH + DV), jnp.array(heads), axis=1)
    we_send = we_send.reshape(rl, n_ex, kv_cols).transpose(1, 0, 2)
    we_send = we_send.reshape(n_ex, r, rl * kv_cols // r)
    wa_send = jnp.concatenate([wq_send, we_send], axis=-1)
    pack_cols = (lat + n_experts + 3 + 127) // 128 * 128
    pack = jnp.concatenate(
        [
            w_latent,
            w_router,
            attn_gain[:, None],
            ffn_gain[:, None],
            jnp.pad(latent_gain, (0, r - rl))[:, None],
            jnp.zeros((r, pack_cols - lat - n_experts - 3), BF),
        ],
        axis=1,
    )
    tok_all, wa_all, pk_all = first_exchange(tokens, wa_send, pack, n_dp, n_ex, 1)
    wq = wa_all[..., :head_cols].reshape(width, head_cols)
    wexp = wa_all[..., head_cols:].reshape(KVR, kv_cols)
    pk_flat = pk_all.reshape(width, pack_cols)
    w_lat = pk_flat[:, :lat]
    router = pk_flat[:, lat : lat + n_experts]
    gain_one = pk_flat[:, lat + n_experts].astype(F32)
    gain_two = pk_flat[:, lat + n_experts + 1].astype(F32)
    gain_lat = (
        pk_all[..., lat + n_experts + 2].reshape(n_dp * n_ex, r)[:, :rl].reshape(KVR).astype(F32)
    )

    def expert_half(weight, after):
        two = weight.reshape(-1, 2, half, ff_e).transpose(1, 0, 2, 3)
        two = lax.all_to_all(two, "expert", 0, 0, axis_index_groups=pair_groups, tiled=True)
        out = two.reshape(per_chip, half, splits, ff_part).transpose(0, 2, 1, 3)
        out = out.reshape(n_dp, half, ff_part)
        out, _ = lax.optimization_barrier((out, after))
        own = lax.all_to_all(out, "dp", 0, 0, tiled=True).reshape(width // 2, ff_part)
        return own, lax.ppermute(own, "expert", sib_perm)

    gate_w = expert_half(expert_gate, pk_all)
    up_w = expert_half(expert_up, gate_w[0])
    down_w = expert_half(expert_down, up_w[0])
    wo_send, _ = lax.optimization_barrier((w_out, pk_all))
    wo_col = lax.all_gather(wo_send, "dp", axis=0, tiled=False)
    wo_rows = lax.all_to_all(
        wo_col.reshape(parts, hp, r, width),
        "expert",
        0,
        0,
        axis_index_groups=part_groups,
        tiled=True,
    )
    wo_rows = wo_rows.transpose(1, 0, 2, 3).reshape(hp * DV, width)
    shared_send = jnp.stack(
        [w.reshape(r, n_dp, ff_s).transpose(1, 0, 2) for w in (shared_gate, shared_up, shared_down)],
        axis=1,
    )
    shared_send, _ = lax.optimization_barrier((shared_send, pk_all))
    shared_col = lax.all_to_all(shared_send, "dp", 0, 0, tiled=True)
    sgate, sup, sdown = (
        lax.all_gather(shared_col[:, i], "expert", axis=1, tiled=True).reshape(width, ff_s)
        for i in range(3)
    )

    slot_own = slot_places(routes, place_order[0], capacity)
    slot_col = lax.all_gather(slot_own, "dp", axis=0, tiled=False)
    slots_all = n_experts * capacity
    slot_ids = jnp.where(
        slot_col >= 0, slot_col + (jnp.arange(n_dp) * slots_all)[:, None, None], -1
    ).reshape(n_dp * rows, top_k)
    place = jnp.arange(cap)
    wanted = (
        (jnp.arange(chips) * per_chip + my_local)[:, None, None] * capacity
        + (jnp.arange(n_dp) * slots_all)[None, :, None]
        + place[None, None, :]
    )
    wanted = jnp.where(place[None, None, :] < capacity, wanted, -2).reshape(-1)
    n_slots = wanted.shape[0]
    hot = sum(
        (wanted[:, None] == slot_ids[None, :, j]).astype(BF) for j in range(top_k)
    )
    hot_t = sum(
        (slot_ids[:, j][:, None] == wanted[None, :]).astype(BF) for j in range(top_k)
    )
    cot_send, _ = lax.optimization_barrier((cotangent, pk_all))
    cot_col = lax.all_gather(cot_send, "dp", axis=0, tiled=True)

    def halves(values):
        cut = values.reshape(values.shape[0], n_dp, 2, half)
        first = cut[:, :, 0].reshape(values.shape[0], width // 2)
        second = cut[:, :, 1].reshape(values.shape[0], width // 2)
        return jnp.where(core == 0, first, second), jnp.where(core == 0, second, first)

    def whole(own, other):
        first = jnp.where(core == 0, own, other).reshape(own.shape[0], n_dp, 1, half)
        second = jnp.where(core == 0, other, own).reshape(own.shape[0], n_dp, 1, half)
        return jnp.concatenate([first, second], axis=2).reshape(own.shape[0], width)

    def between(values):
        return lax.all_to_all(
            values.reshape(chips, n_slots // chips, -1),
            "expert",
            0,
            0,
            axis_index_groups=same_core_groups,
            tiled=True,
        ).reshape(n_slots, -1)

    cot_halves = halves(cot_col)
    grad_in = [between(mm(hot, part).astype(BF)) for part in cot_halves]

    tok_plane = tok_all.reshape(seq, width)
    hidden_one = rms_norm(tok_plane.astype(F32), gain_one).astype(BF)
    positions = jnp.arange(seq)
    cos_table, sine_table = rope_tables(positions)
    query_raw = mm(hidden_one, wq).reshape(seq, hp, DH + DR)

    def make_queries(query_in):
        return jnp.concatenate(
            [
                query_in[..., :DH],
                rotate(query_in[..., DH:], cos_table[:, None, :], sine_table[:, None, :]),
            ],
            axis=-1,
        )

    query_rot, query_back = jax.vjp(make_queries, query_raw)
    queries = query_rot.astype(BF)
    latent_raw = mm(hidden_one, w_lat)
    latent_low = rms_norm(latent_raw[:, :KVR], gain_lat).astype(BF)
    rope_low = rotate(latent_raw[:, KVR:], cos_table, sine_table).astype(BF)
    expanded = mm(latent_low, wexp).astype(BF).reshape(seq, hp, DH + DV)
    score_scale = (DH + DR) ** (-0.5)
    allowed = (positions[None, :] <= positions[:, None]) & (positions[None, :] < lengths[0])
    attn_probs, probs_low, keys, attended = [], [], [], []
    for h in range(hp):
        key = jnp.concatenate([expanded[:, h, :DH], rope_low], axis=1)
        scores = jnp.where(allowed, mm_cols(queries[:, h], key) * score_scale, masked_score)
        top = jnp.max(scores, axis=-1, keepdims=True)
        exp_scores = jnp.exp(scores - top)
        probs = exp_scores / jnp.sum(exp_scores, axis=-1, keepdims=True)
        low = probs.astype(BF)
        attn_probs.append(probs)
        probs_low.append(low)
        keys.append(key)
        attended.append(mm(low, expanded[:, h, DH:]).astype(BF))
    attended = jnp.concatenate(attended, axis=1)
    out_part = mm(attended, wo_rows).astype(BF)
    tokens_f = tokens.astype(F32)
    residual = tokens_f + plane_sum(out_part.reshape(n_ex, rows, width), n_dp, n_ex, 2)
    normed_two, norm_two_back = jax.vjp(rms_norm, residual, gain_two)
    hidden_two = normed_two.astype(BF)
    x_col = column_gather(hidden_two, n_dp, n_ex, 3).reshape(n_dp * rows, width)

    x_halves = halves(x_col)
    x_in = [between(mm(hot, part).astype(BF)) for part in x_halves]
    router_halves = [part.T for part in halves(router.T)]

    def probs_of(logits):
        top = jnp.max(logits, axis=-1, keepdims=True)
        exp_logits = jnp.exp(logits - top)
        return exp_logits / jnp.sum(exp_logits, axis=-1, keepdims=True)

    shared_a = mm(x_col, sgate)
    shared_b = mm(x_col, sup)
    shared_hidden, shared_back = jax.vjp(swiglu, shared_a, shared_b)
    shared_hidden = shared_hidden.astype(BF)
    shared_out = mm_cols(shared_hidden, sdown)
    grad_sa, grad_sb = (v.astype(BF) for v in shared_back(mm(cot_col, sdown)))
    shared_grads = [
        mm_rows(x_col, grad_sa).astype(BF),
        mm_rows(x_col, grad_sb).astype(BF),
        mm_rows(cot_col, shared_hidden).astype(BF),
    ]
    shared_dx = mm_cols(grad_sa, sgate) + mm_cols(grad_sb, sup)

    expert_id = chip * per_chip + my_local
    slot_probs = probs_of(mm(x_in[0], router_halves[0]) + mm(x_in[1], router_halves[1]))
    slot_gate = jnp.sum(
        jnp.where(jnp.arange(n_experts)[None, :] == expert_id, slot_probs, 0.0),
        axis=1,
        keepdims=True,
    )
    expert_a = mm(x_in[0], gate_w[0]) + mm(x_in[1], gate_w[1])
    expert_b = mm(x_in[0], up_w[0]) + mm(x_in[1], up_w[1])
    expert_hidden, expert_back = jax.vjp(swiglu, expert_a, expert_b)
    expert_hidden = expert_hidden.astype(BF)
    rows_back = [between(mm_cols(expert_hidden, w).astype(BF)) for w in down_w]
    slot_grad = [(slot_gate * part.astype(F32)).astype(BF) for part in grad_in]
    grad_hidden = mm(slot_grad[0], down_w[0]) + mm(slot_grad[1], down_w[1])
    grad_ea, grad_eb = (v.astype(BF) for v in expert_back(grad_hidden))
    dx_back = [
        between((mm_cols(grad_ea, gw) + mm_cols(grad_eb, uw)).astype(BF))
        for gw, uw in zip(gate_w, up_w)
    ]

    def expert_sum(left, right):
        own, other = (mm_rows(a, b) for a, b in zip(left, right))
        got = lax.ppermute(other.astype(BF), "expert", sib_perm)
        total = (own + got.astype(F32)).astype(BF).reshape(n_dp, half, ff_part)
        back = lax.all_to_all(total, "dp", 0, 0, tiled=True)
        back = back.reshape(per_chip, splits, half, ff_part).transpose(0, 2, 1, 3)
        back = back.reshape(2, per_chip // 2, half, ff_e)
        back = lax.all_to_all(back, "expert", 0, 0, axis_index_groups=pair_groups, tiled=True)
        return back.transpose(1, 0, 2, 3).reshape(-1, 2 * half, ff_e).astype(F32)

    sum_egate = expert_sum(x_in, (grad_ea, grad_ea))
    sum_eup = expert_sum(x_in, (grad_eb, grad_eb))
    sum_edown = expert_sum(slot_grad, (expert_hidden, expert_hidden))

    col_probs = probs_of(mm(x_col, router))
    mine = jnp.arange(n_experts)[None, :] % per_chip == my_local
    col_gates = jnp.sum(
        jnp.where(mine, col_probs, 0.0).reshape(n_dp * rows, chips, per_chip), axis=-1
    )
    gate_hot = hot_t * jnp.repeat(col_gates, n_slots // chips, axis=1).astype(BF)
    routed = whole(*(mm(gate_hot, part) for part in rows_back))
    out_col = (routed + shared_out).astype(BF).reshape(n_dp, rows, width)
    dots = sum(mm_cols(a, b) for a, b in zip(cot_halves, rows_back)) * hot_t.astype(F32)
    dots = jnp.sum(dots.reshape(n_dp * rows, chips, n_slots // chips), axis=-1)
    grad_probs_col = jnp.where(mine, jnp.repeat(dots, per_chip, axis=1), 0.0)
    dx_col = whole(*(mm(hot_t, part) for part in dx_back)) + shared_dx
    dx_send = jnp.concatenate(
        [dx_col, grad_probs_col, jnp.zeros((n_dp * rows, 128 - n_experts), F32)], axis=1
    ).astype(BF)
    dx_got = lax.all_to_all(dx_send.reshape(n_dp, rows, width + 128), "dp", 0, 0, tiled=True)
    dx_sum = jnp.sum(dx_got.astype(F32), axis=0)
    out_got = lax.all_to_all(out_col, "dp", 0, 0, tiled=True)
    out_tokens = (residual + jnp.sum(out_got.astype(F32), axis=0)).astype(BF)

    router_probs = probs_of(mm(hidden_two, router))
    grad_probs = dx_sum[:, width : width + n_experts]
    grad_logits = (
        router_probs * (grad_probs - jnp.sum(grad_probs * router_probs, axis=-1, keepdims=True))
    ).astype(BF)
    grad_router = mm_rows(hidden_two, grad_logits)
    grad_hidden_two = dx_sum[:, :width] + mm_cols(grad_logits, router)
    grad_resid_norm, grad_gain_two = norm_two_back(grad_hidden_two)
    grad_residual = cotangent.astype(F32) + grad_resid_norm

    grad_attn = plane_gather(grad_residual.astype(BF), n_dp, n_ex, 4).reshape(seq, width)
    grad_attended = mm_cols(grad_attn, wo_rows).astype(BF)
    grad_wout = mm_rows(attended, grad_attn).astype(BF)
    grad_rope = 0.0
    grad_queries, grad_expanded = [], []
    for h in range(hp):
        gat = grad_attended[:, h * DV : (h + 1) * DV]
        probs = attn_probs[h]
        dp = mm_cols(gat, expanded[:, h, DH:])
        grad_scores = probs * (dp - jnp.sum(dp * probs, axis=-1, keepdims=True))
        grad_raw = jnp.where(allowed, grad_scores * score_scale, 0.0).astype(BF)
        grad_queries.append(mm(grad_raw, keys[h]))
        grad_key = mm_rows(grad_raw, queries[:, h])
        grad_rope = grad_rope + grad_key[:, DH:]
        grad_expanded += [grad_key[:, :DH], mm_rows(probs_low[h], gat)]
    grad_expanded = jnp.concatenate(grad_expanded, axis=1).astype(BF)
    (grad_query_raw,) = query_back(jnp.stack(grad_queries, axis=1))
    grad_query_low = grad_query_raw.reshape(seq, head_cols).astype(BF)
    grad_latent_part = jnp.concatenate([mm_cols(grad_expanded, wexp), grad_rope], axis=1)
    grad_part = jnp.concatenate(
        [
            mm_cols(grad_query_low, wq).astype(BF),
            grad_latent_part.astype(BF),
            jnp.zeros((seq, -lat % 128), BF),
        ],
        axis=1,
    )
    grad_sum = plane_sum(grad_part.reshape(n_ex, rows, -1), n_dp, n_ex, 5)
    own_start = e * rows
    latent_own = lax.dynamic_slice_in_dim(latent_raw, own_start, rows, 0)
    cos_own = lax.dynamic_slice_in_dim(cos_table, own_start, rows, 0)
    sine_own = lax.dynamic_slice_in_dim(sine_table, own_start, rows, 0)

    def make_latent(latent_in, gain_in):
        return (
            rms_norm(latent_in[:, :KVR], gain_in),
            rotate(latent_in[:, KVR:], cos_own, sine_own),
        )

    _, latent_back = jax.vjp(make_latent, latent_own, gain_lat)
    grad_latent_raw, grad_gain_lat = latent_back(
        (grad_sum[:, width : width + KVR], grad_sum[:, width + KVR : width + lat])
    )
    grad_latent_low = grad_latent_raw.astype(BF)
    _, norm_one_back = jax.vjp(rms_norm, tokens_f, gain_one)
    grad_hidden_one = grad_sum[:, :width] + mm_cols(grad_latent_low, w_lat)
    grad_tokens_norm, grad_gain_one = norm_one_back(grad_hidden_one)
    grad_tokens = grad_residual + grad_tokens_norm

    def column_sum(values):
        got = lax.all_to_all(values, "dp", 0, 0, tiled=True)
        return jnp.sum(got.astype(F32), axis=0)

    wout_back = lax.all_to_all(
        grad_wout.reshape(hp, parts, r, width).transpose(1, 0, 2, 3),
        "expert",
        0,
        0,
        axis_index_groups=part_groups,
        tiled=True,
    )
    sum_wout = column_sum(wout_back.reshape(n_dp, r, width))
    shared_sums = [
        lax.psum_scatter(
            grad.reshape(n_dp, n_ex, r, ff_s), "expert", scatter_dimension=1, tiled=True
        ).reshape(n_dp, r, ff_s)
        for grad in shared_grads
    ]
    shared_back_col = lax.all_to_all(jnp.stack(shared_sums, axis=1), "dp", 0, 0, tiled=True)
    sum_sgate, sum_sup, sum_sdown = (
        shared_back_col[:, i].transpose(1, 0, 2).reshape(r, n_dp * ff_s).astype(F32)
        for i in range(3)
    )
    grad_wq = mm_rows(hidden_one, grad_query_low).astype(BF).reshape(n_dp, n_ex, r, head_cols)
    grad_we = mm_rows(latent_low, grad_expanded).astype(BF)
    grad_we = grad_we.reshape(n_dp, n_ex, r, rl * kv_cols // r)
    heads_sum = column_sum(jnp.concatenate([grad_wq, grad_we], axis=-1)).astype(BF)
    heads_back_all = lax.all_to_all(heads_sum, "expert", 0, 0, tiled=True).astype(F32)
    sum_wq = heads_back_all[..., :head_cols].transpose(1, 0, 2).reshape(r, H, DH + DR)
    sum_wq = jnp.take(sum_wq, jnp.array(heads_back), axis=1).reshape(r, H * (DH + DR))
    sum_we = heads_back_all[..., head_cols:].reshape(n_ex, rl, kv_cols).transpose(1, 0, 2)
    sum_we = jnp.take(sum_we.reshape(rl, H, DH + DV), jnp.array(heads_back), axis=1)
    sum_we = sum_we.reshape(rl, H * (DH + DV))

    latent_plane = plane_gather(grad_latent_low, n_dp, n_ex, 6).reshape(seq, lat)
    hidden_cut = lax.dynamic_index_in_dim(
        hidden_one.reshape(seq, n_dp, n_ex, r), e, 2, keepdims=False
    )
    grad_wlat = mm_rows(hidden_cut.reshape(seq, n_dp * r), latent_plane).reshape(n_dp, r, lat)
    small = jnp.concatenate(
        [
            grad_router.reshape(n_dp, n_ex, r, n_experts),
            grad_gain_one.reshape(n_dp, n_ex, r, 1),
            grad_gain_two.reshape(n_dp, n_ex, r, 1),
            jnp.pad(grad_gain_lat.reshape(n_dp, n_ex, rl, 1), ((0, 0),) * 2 + ((0, r - rl), (0, 0))),
            jnp.zeros((n_dp, n_ex, r, pack_cols - lat - n_experts - 3), F32),
        ],
        axis=-1,
    ).transpose(1, 0, 2, 3)
    small = jnp.sum(lax.all_to_all(small, "expert", 0, 0, tiled=True), axis=0)
    pack_sum = column_sum(jnp.concatenate([grad_wlat, small], axis=-1).astype(BF))
    return (
        out_tokens,
        grad_tokens,
        pack_sum[:, lat + n_experts],
        sum_wq,
        pack_sum[:, :lat],
        pack_sum[:rl, lat + n_experts + 2],
        sum_we,
        sum_wout,
        pack_sum[:, lat + n_experts + 1],
        pack_sum[:, lat : lat + n_experts],
        sum_sgate,
        sum_sup,
        sum_sdown,
        sum_egate,
        sum_eup,
        sum_edown,
    )


def solution(mesh):
    both = ("dp", "expert")
    in_specs = (
        P(both, None),
        P(both, None),
        P("dp"),
        P(both, None),
        P(both, None),
        P(both),
        P(both, None),
        P(both, None),
        P(both),
        P(both, None),
        P(both, None),
        P(both),
        P(both, None),
        P(both, None),
        P(both, None),
        P(both, None),
        P("expert", "dp", None),
        P("expert", "dp", None),
        P("expert", "dp", None),
    )
    out_specs = (
        P(both, None),
        P(both, None),
        P(both),
        P(both, None),
        P(both, None),
        P(both),
        P(both, None),
        P(both, None),
        P(both),
        P(both, None),
        P(both, None),
        P(both, None),
        P(both, None),
        P("expert", "dp", None),
        P("expert", "dp", None),
        P("expert", "dp", None),
    )
    return jax.shard_map(shards, mesh=mesh, in_specs=in_specs, out_specs=out_specs, check_vma=False)
```

```python
import jax
import jax.numpy as jnp
from jax import lax
from jax.experimental import pallas as pl
from jax.experimental.pallas import tpu as pltpu
from jax.sharding import PartitionSpec as P

H = 16
DH = 128
DR = 64
DV = 128
KVR = 512

norm_eps = 1e-06
masked_score = -1e30
MESH = pl.DeviceIdType.MESH
ANY = pl.BlockSpec(memory_space=pl.ANY)
VMEM = pl.BlockSpec(memory_space=pltpu.VMEM)
BF = jnp.bfloat16
F32 = jnp.float32


def rms_norm(values, scale_gain):
    return (
        values
        * lax.rsqrt(jnp.mean(values * values, axis=-1, keepdims=True) + norm_eps)
        * scale_gain
    )


def rotate(values, cos_table, sine_table):
    half_dim = values.shape[-1] // 2
    first_half = values[..., :half_dim]
    second_half = values[..., half_dim:]
    return jnp.concatenate(
        [
            first_half * cos_table - second_half * sine_table,
            second_half * cos_table + first_half * sine_table,
        ],
        axis=-1,
    )


def rope_tables(positions):
    half_dim = DR // 2
    inv_freq = 10000.0 ** (-(jnp.arange(half_dim).astype(F32) * 2.0) / DR)
    angles = positions.astype(F32)[:, None] * inv_freq[None, :]
    return (jnp.cos(angles), jnp.sin(angles))


def swiglu(gate_in, up_in):
    return jax.nn.silu(gate_in) * up_in


def mm(left, right):
    return jnp.dot(left, right, preferred_element_type=F32)


def mm_rows(left, right):
    return lax.dot_general(left, right, (((0,), (0,)), ((), ())), preferred_element_type=F32)


def mm_cols(left, right):
    return lax.dot_general(left, right, (((1,), (1,)), ((), ())), preferred_element_type=F32)


def slot_places(route_rows, pair_order, capacity):
    pair_expert = route_rows.reshape(-1)
    earlier = pair_order[None, :] < pair_order[:, None]
    same_expert = pair_expert[None, :] == pair_expert[:, None]
    places = jnp.sum((earlier & same_expert).astype(jnp.int32), axis=1)
    slot_index = jnp.where(places < capacity, pair_expert * capacity + places, -1)
    return slot_index.reshape(route_rows.shape)


def params(collective_id):
    return pltpu.CompilerParams(
        collective_id=collective_id, has_side_effects=True, vmem_limit_bytes=48 << 20
    )


def remote(src, dst, send_sem, recv_sem, device):
    return pltpu.make_async_remote_copy(
        src_ref=src,
        dst_ref=dst,
        send_sem=send_sem,
        recv_sem=recv_sem,
        device_id=device,
        device_id_type=MESH,
    )


def greet(devices):
    barrier = pltpu.get_barrier_semaphore()
    for device in devices:
        pl.semaphore_signal(barrier, inc=1, device_id=device, device_id_type=MESH)
    pl.semaphore_wait(barrier, len(devices))


def places(n_dp, n_ex):
    z = lax.axis_index("dp")
    e = lax.axis_index("expert")
    chips = n_ex // 2
    c, k = e // 2, lax.rem(e, 2)
    sibling = (z, e + 1 - 2 * k)
    same_core = [(z, lax.rem(c + i, chips) * 2 + k) for i in range(1, chips)]
    column = [(lax.rem(z + i, n_dp), e) for i in range(1, n_dp)]
    return z, e, c, k, sibling, same_core, column


def plane_gather(block, n_dp, n_ex, collective_id):
    chips = n_ex // 2

    def kernel(x_ref, o_ref, send, recv, sib_send, sib_recv, local):
        z, e, c, k, sibling, same_core, _ = places(n_dp, n_ex)
        greet(same_core + [sibling])
        far = []
        for i in range(1, chips):
            copy = remote(x_ref, o_ref.at[e], send.at[i], recv.at[i], same_core[i - 1])
            copy.start()
            far.append(copy)
        near = [remote(x_ref, o_ref.at[e], sib_send.at[0], sib_recv.at[0], sibling)]
        near[0].start()
        own = pltpu.make_async_copy(x_ref, o_ref.at[e], local)
        own.start()
        for i in range(1, chips):
            source = lax.rem(c + chips - i, chips) * 2 + k
            far[i - 1].wait_recv()
            copy = remote(
                o_ref.at[source], o_ref.at[source], sib_send.at[i], sib_recv.at[i], sibling
            )
            copy.start()
            near.append(copy)
        own.wait()
        for copy in far:
            copy.wait_send()
        for copy in near:
            copy.wait()

    return pl.pallas_call(
        kernel,
        out_shape=jax.ShapeDtypeStruct((n_ex,) + block.shape, block.dtype),
        in_specs=[ANY],
        out_specs=ANY,
        scratch_shapes=[pltpu.SemaphoreType.DMA((chips,))] * 4 + [pltpu.SemaphoreType.DMA],
        compiler_params=params(collective_id),
    )(block)


def plane_sum(blocks, n_dp, n_ex, collective_id):
    chips = n_ex // 2
    rows, cols = blocks.shape[1:]

    def kernel(x_ref, o_ref, from_sib, out_buf, from_far, send, recv, sib_send, sib_recv):
        z, e, c, k, sibling, same_core, _ = places(n_dp, n_ex)
        greet(same_core + [sibling])
        near = []
        for i in list(range(1, chips)) + [0]:
            chip = lax.rem(c + i, chips)
            copy = remote(
                x_ref.at[chip * 2 + 1 - k],
                from_sib.at[chip],
                sib_send.at[i],
                sib_recv.at[i],
                sibling,
            )
            copy.start()
            near.append(copy)
        far = []
        for i in range(1, chips):
            chip = lax.rem(c + i, chips)
            near[i - 1].wait_recv()
            out_buf[i] = (
                x_ref[chip * 2 + k].astype(F32) + from_sib[chip].astype(F32)
            ).astype(BF)
            copy = remote(out_buf.at[i], from_far.at[i], send.at[i], recv.at[i], same_core[i - 1])
            copy.start()
            far.append(copy)
        near[chips - 1].wait_recv()
        o_ref[...] = x_ref[e].astype(F32) + from_sib[c].astype(F32)
        for i in range(1, chips):
            far[i - 1].wait_recv()
            o_ref[...] += from_far[i].astype(F32)
        for copy in near:
            copy.wait_send()
        for copy in far:
            copy.wait_send()

    return pl.pallas_call(
        kernel,
        out_shape=jax.ShapeDtypeStruct((rows, cols), F32),
        in_specs=[VMEM],
        out_specs=VMEM,
        scratch_shapes=[pltpu.VMEM((chips, rows, cols), BF)] * 3
        + [pltpu.SemaphoreType.DMA((chips,))] * 4,
        compiler_params=params(collective_id),
    )(blocks)


def column_gather(block, n_dp, n_ex, collective_id):
    def kernel(x_ref, o_ref, send, recv, local):
        z, e, c, k, sibling, same_core, column = places(n_dp, n_ex)
        greet(column)
        copies = []
        for i in range(1, n_dp):
            copy = remote(x_ref, o_ref.at[i], send.at[i], recv.at[i], column[i - 1])
            copy.start()
            copies.append(copy)
        own = pltpu.make_async_copy(x_ref, o_ref.at[0], local)
        own.start()
        own.wait()
        for copy in copies:
            copy.wait()

    return pl.pallas_call(
        kernel,
        out_shape=jax.ShapeDtypeStruct((n_dp,) + block.shape, block.dtype),
        in_specs=[ANY],
        out_specs=ANY,
        scratch_shapes=[pltpu.SemaphoreType.DMA((n_dp,))] * 2 + [pltpu.SemaphoreType.DMA],
        compiler_params=params(collective_id),
    )(block)


def first_exchange(tok, heads_w, pack, n_dp, n_ex, collective_id):
    chips = n_ex // 2

    def kernel(
        tok_ref, wa_ref, pk_ref, tok_out, wa_out, pk_out,
        t_send, t_recv, ts_send, ts_recv, a_send, a_recv, az_send, az_recv,
        p_send, p_recv, pf_send, pf_recv, ps_send, ps_recv, local,
    ):
        z, e, c, k, sibling, same_core, column = places(n_dp, n_ex)
        plane = [(z, lax.rem(e + i, n_ex)) for i in range(1, n_ex)]
        greet(plane + column)
        wa_far, pk_col, tok_far = [], [], []
        for i in range(1, n_ex):
            copy = remote(
                wa_ref.at[lax.rem(e + i, n_ex)], wa_out.at[z, e],
                a_send.at[i], a_recv.at[i], plane[i - 1],
            )
            copy.start()
            wa_far.append(copy)
        for i in range(1, n_dp):
            copy = remote(pk_ref, pk_out.at[z, e], p_send.at[i], p_recv.at[i], column[i - 1])
            copy.start()
            pk_col.append(copy)
        for i in range(1, chips):
            copy = remote(tok_ref, tok_out.at[e], t_send.at[i], t_recv.at[i], same_core[i - 1])
            copy.start()
            tok_far.append(copy)
        near = [remote(tok_ref, tok_out.at[e], ts_send.at[0], ts_recv.at[0], sibling)]
        near[0].start()
        own = [
            pltpu.make_async_copy(wa_ref.at[e], wa_out.at[z, e], local.at[0]),
            pltpu.make_async_copy(pk_ref, pk_out.at[z, e], local.at[1]),
            pltpu.make_async_copy(tok_ref, tok_out.at[e], local.at[2]),
        ]
        for copy in own:
            copy.start()
        for copy in own:
            copy.wait()
        for copy in wa_far:
            copy.wait_recv()
        wa_col = []
        for i in range(1, n_dp):
            copy = remote(
                wa_out.at[z], wa_out.at[z], az_send.at[i], az_recv.at[i], column[i - 1]
            )
            copy.start()
            wa_col.append(copy)
        for copy in pk_col:
            copy.wait_recv()
        pk_far = []
        for i in range(1, chips):
            copy = remote(
                pk_out.at[:, e], pk_out.at[:, e], pf_send.at[i], pf_recv.at[i], same_core[i - 1]
            )
            copy.start()
            pk_far.append(copy)
        copy = remote(pk_out.at[:, e], pk_out.at[:, e], ps_send.at[0], ps_recv.at[0], sibling)
        copy.start()
        near.append(copy)
        for i in range(1, chips):
            source = lax.rem(c + chips - i, chips) * 2 + k
            tok_far[i - 1].wait_recv()
            copy = remote(
                tok_out.at[source], tok_out.at[source], ts_send.at[i], ts_recv.at[i], sibling
            )
            copy.start()
            near.append(copy)
            pk_far[i - 1].wait_recv()
            copy = remote(
                pk_out.at[:, source], pk_out.at[:, source], ps_send.at[i], ps_recv.at[i], sibling
            )
            copy.start()
            near.append(copy)
        for copy in near + wa_col:
            copy.wait()
        for copy in wa_far + pk_col + tok_far + pk_far:
            copy.wait_send()

    dma = pltpu.SemaphoreType.DMA
    return pl.pallas_call(
        kernel,
        out_shape=[
            jax.ShapeDtypeStruct((n_ex,) + tok.shape, tok.dtype),
            jax.ShapeDtypeStruct((n_dp,) + heads_w.shape, heads_w.dtype),
            jax.ShapeDtypeStruct((n_dp, n_ex) + pack.shape, pack.dtype),
        ],
        in_specs=[ANY] * 3,
        out_specs=[ANY] * 3,
        scratch_shapes=[dma((chips,))] * 4
        + [dma((n_ex,))] * 2
        + [dma((n_dp,))] * 4
        + [dma((chips,))] * 4
        + [dma((3,))],
        compiler_params=params(collective_id),
    )(tok, heads_w, pack)


def shards(
    tokens,
    cotangent,
    lengths,
    routes,
    place_order,
    attn_gain,
    w_query,
    w_latent,
    latent_gain,
    w_expand,
    w_out,
    ffn_gain,
    w_router,
    shared_gate,
    shared_up,
    shared_down,
    expert_gate,
    expert_up,
    expert_down,
):
    rows, width = tokens.shape
    n_dp = lax.axis_size("dp")
    n_ex = lax.axis_size("expert")
    chips = n_ex // 2
    z = lax.axis_index("dp")
    e = lax.axis_index("expert")
    chip, core = e // 2, lax.rem(e, 2)
    n_experts = w_router.shape[1]
    top_k = routes.shape[1]
    capacity = (rows * top_k * 5 + 4 * n_experts - 1) // (4 * n_experts)
    cap = (capacity + 15) // 16 * 16
    seq = rows * n_ex
    r = w_query.shape[0]
    rl = w_expand.shape[0]
    hp = H // n_ex
    parts = DV // r
    heads = [
        (d * n_ex + (j // parts) * parts) * r // DV
        for j in range(n_ex)
        for d in range(j % parts * hp, j % parts * hp + hp)
    ]
    heads_back = [heads.index(h) for h in range(H)]
    per_chip = n_experts // chips
    splits = n_dp // per_chip
    my_local = z // splits
    sib_perm = [(i, i ^ 1) for i in range(n_ex)]
    part_groups = [[i * parts + m for m in range(parts)] for i in range(n_ex // parts)]
    ff_e = expert_gate.shape[2]
    ff_part = ff_e // splits
    half = expert_gate.shape[1] // 2
    ff_s = shared_gate.shape[1] // n_dp
    lat = KVR + DR
    head_cols = hp * (DH + DR)
    kv_cols = hp * (DH + DV)

    wq_send = jnp.take(w_query.reshape(r, H, DH + DR), jnp.array(heads), axis=1)
    wq_send = wq_send.reshape(r, n_ex, head_cols).transpose(1, 0, 2)
    we_send = jnp.take(w_expand.reshape(rl, H, DH + DV), jnp.array(heads), axis=1)
    we_send = we_send.reshape(rl, n_ex, kv_cols).transpose(1, 0, 2)
    we_send = we_send.reshape(n_ex, r, rl * kv_cols // r)
    wa_send = jnp.concatenate([wq_send, we_send], axis=-1)
    pack_cols = (lat + n_experts + 3 + 127) // 128 * 128
    pack = jnp.concatenate(
        [
            w_latent,
            w_router,
            attn_gain[:, None],
            ffn_gain[:, None],
            jnp.pad(latent_gain, (0, r - rl))[:, None],
            jnp.zeros((r, pack_cols - lat - n_experts - 3), BF),
        ],
        axis=1,
    )
    tok_all, wa_all, pk_all = first_exchange(tokens, wa_send, pack, n_dp, n_ex, 1)
    wq = wa_all[..., :head_cols].reshape(width, head_cols)
    wexp = wa_all[..., head_cols:].reshape(KVR, kv_cols)
    pk_flat = pk_all.reshape(width, pack_cols)
    w_lat = pk_flat[:, :lat]
    router = pk_flat[:, lat : lat + n_experts]
    gain_one = pk_flat[:, lat + n_experts].astype(F32)
    gain_two = pk_flat[:, lat + n_experts + 1].astype(F32)
    gain_lat = (
        pk_all[..., lat + n_experts + 2].reshape(n_dp * n_ex, r)[:, :rl].reshape(KVR).astype(F32)
    )

    def shift(values, step):
        return lax.ppermute(values, "dp", [(i, (i + step) % n_dp) for i in range(n_dp)])

    def before(step):
        return lax.rem(z + n_dp - step, n_dp)

    def after(step):
        return lax.rem(z + step, n_dp)

    def swap(values):
        return lax.ppermute(values, "expert", sib_perm)

    def pick(values, index, axis=0):
        return lax.dynamic_index_in_dim(values, index, axis, keepdims=False)

    def expert_half(weight, held):
        two = weight.reshape(-1, 2, half, ff_e)
        experts = jnp.concatenate([pick(two, core, 1), swap(pick(two, 1 - core, 1))], axis=0)
        experts = experts.reshape(per_chip, n_ex // 2, r, splits, ff_part)
        experts, _ = lax.optimization_barrier((experts, held))

        def block_for(index):
            expert = lax.rem(index // splits + per_chip - core * (per_chip // 2), per_chip)
            return pick(pick(experts, expert), lax.rem(index, splits), 2)

        own = jnp.zeros((n_ex // 2, n_dp, r, ff_part), BF)
        for i in range(n_dp):
            block = block_for(after(i))
            block = shift(block, i) if i else block
            own = lax.dynamic_update_index_in_dim(own, block, before(i), 1)
        own = own.reshape(width // 2, ff_part)
        return own, swap(own)

    gate_w = expert_half(expert_gate, pk_all)
    up_w = expert_half(expert_up, pk_all)
    down_w = expert_half(expert_down, pk_all)
    wo_send, _ = lax.optimization_barrier((w_out, pk_all))
    wo_col = lax.all_gather(wo_send, "dp", axis=0, tiled=False)
    wo_rows = lax.all_to_all(
        wo_col.reshape(parts, hp, r, width),
        "expert",
        0,
        0,
        axis_index_groups=part_groups,
        tiled=True,
    )
    wo_rows = wo_rows.transpose(1, 0, 2, 3).reshape(hp * DV, width)
    shared_send = [
        w.reshape(r, n_dp, ff_s).transpose(1, 0, 2) for w in (shared_gate, shared_up, shared_down)
    ]
    shared_send, _ = lax.optimization_barrier((shared_send, pk_all))

    def shared_whole(weight):
        mine = jnp.zeros((n_dp, r, ff_s), BF)
        for i in range(n_dp):
            block = pick(weight, after(i))
            block = shift(block, i) if i else block
            mine = lax.dynamic_update_index_in_dim(mine, block, before(i), 0)
        return lax.all_gather(mine, "expert", axis=0, tiled=False).reshape(width, ff_s)

    sgate, sup, sdown = (shared_whole(w) for w in shared_send)

    def to_owner_order(values):
        cut = values.reshape(values.shape[0], n_dp, n_ex, r)
        return cut.transpose(0, 2, 1, 3).reshape(values.shape)

    def from_owner_order(values):
        cut = values.reshape(values.shape[0], n_ex, n_dp, r)
        return cut.transpose(0, 2, 1, 3).reshape(values.shape)

    def column(values):
        return jnp.concatenate([values] + [shift(values, i) for i in range(1, n_dp)], axis=0)

    slot_own = slot_places(routes, place_order[0], capacity)
    slots_all = n_experts * capacity
    slot_ids = column(slot_own).reshape(n_dp, rows, top_k)
    slot_ids = jnp.where(
        slot_ids >= 0, slot_ids + (jnp.arange(n_dp) * slots_all)[:, None, None], -1
    ).reshape(n_dp * rows, top_k)
    place = jnp.arange(cap)
    far_experts = [(chip ^ m) * per_chip + my_local for m in range(chips)]
    wanted = (
        jnp.stack(far_experts)[:, None, None] * capacity
        + (jnp.arange(n_dp) * slots_all)[None, :, None]
        + place[None, None, :]
    )
    wanted = jnp.where(place[None, None, :] < capacity, wanted, -2).reshape(-1)
    n_slots = wanted.shape[0]
    per_far = n_slots // chips
    hot = sum(
        (wanted[:, None] == slot_ids[None, :, j]).astype(BF) for j in range(top_k)
    )
    hot_t = sum(
        (slot_ids[:, j][:, None] == wanted[None, :]).astype(BF) for j in range(top_k)
    )
    cot_send, _ = lax.optimization_barrier((to_owner_order(cotangent), pk_all))
    cot_col = column(cot_send)

    def halves(values):
        first, second = values[:, : width // 2], values[:, width // 2 :]
        return jnp.where(core == 0, first, second), jnp.where(core == 0, second, first)

    def whole(own, other):
        return jnp.concatenate(
            [jnp.where(core == 0, own, other), jnp.where(core == 0, other, own)], axis=1
        )

    def between(values):
        cut = values.reshape(chips, per_far, -1)
        got = [cut[0]]
        for m in range(1, chips):
            perm = [(i, i ^ (2 * m)) for i in range(n_ex)]
            got.append(lax.ppermute(cut[m], "expert", perm))
        return jnp.concatenate(got, axis=0)

    cot_halves = halves(cot_col)
    grad_in = [between(mm(hot, part).astype(BF)) for part in cot_halves]

    tok_plane = tok_all.reshape(seq, width)
    hidden_one = rms_norm(tok_plane.astype(F32), gain_one).astype(BF)
    positions = jnp.arange(seq)
    cos_table, sine_table = rope_tables(positions)
    query_raw = mm(hidden_one, wq).reshape(seq, hp, DH + DR)

    def make_queries(query_in):
        return jnp.concatenate(
            [
                query_in[..., :DH],
                rotate(query_in[..., DH:], cos_table[:, None, :], sine_table[:, None, :]),
            ],
            axis=-1,
        )

    query_rot, query_back = jax.vjp(make_queries, query_raw)
    queries = query_rot.astype(BF)
    latent_raw = mm(hidden_one, w_lat)
    latent_low = rms_norm(latent_raw[:, :KVR], gain_lat).astype(BF)
    rope_low = rotate(latent_raw[:, KVR:], cos_table, sine_table).astype(BF)
    expanded = mm(latent_low, wexp).astype(BF).reshape(seq, hp, DH + DV)
    score_scale = (DH + DR) ** (-0.5)
    allowed = (positions[None, :] <= positions[:, None]) & (positions[None, :] < lengths[0])
    attn_probs, probs_low, keys, attended = [], [], [], []
    for h in range(hp):
        key = jnp.concatenate([expanded[:, h, :DH], rope_low], axis=1)
        scores = jnp.where(allowed, mm_cols(queries[:, h], key) * score_scale, masked_score)
        top = jnp.max(scores, axis=-1, keepdims=True)
        exp_scores = jnp.exp(scores - top)
        probs = exp_scores / jnp.sum(exp_scores, axis=-1, keepdims=True)
        low = probs.astype(BF)
        attn_probs.append(probs)
        probs_low.append(low)
        keys.append(key)
        attended.append(mm(low, expanded[:, h, DH:]).astype(BF))
    attended = jnp.concatenate(attended, axis=1)
    out_part = mm(attended, wo_rows).astype(BF)
    tokens_f = tokens.astype(F32)
    residual = tokens_f + plane_sum(out_part.reshape(n_ex, rows, width), n_dp, n_ex, 2)
    normed_two, norm_two_back = jax.vjp(rms_norm, residual, gain_two)
    hidden_two = normed_two.astype(BF)
    x_col = column_gather(to_owner_order(hidden_two), n_dp, n_ex, 3).reshape(n_dp * rows, width)

    x_halves = halves(x_col)
    x_in = [between(mm(hot, part).astype(BF)) for part in x_halves]
    router_owner = to_owner_order(router.T).T
    router_halves = [part.T for part in halves(router_owner.T)]

    def probs_of(logits):
        top = jnp.max(logits, axis=-1, keepdims=True)
        exp_logits = jnp.exp(logits - top)
        return exp_logits / jnp.sum(exp_logits, axis=-1, keepdims=True)

    shared_a = mm(x_col, sgate)
    shared_b = mm(x_col, sup)
    shared_hidden, shared_back = jax.vjp(swiglu, shared_a, shared_b)
    shared_hidden = shared_hidden.astype(BF)
    shared_out = mm_cols(shared_hidden, sdown)
    grad_sa, grad_sb = (v.astype(BF) for v in shared_back(mm(cot_col, sdown)))
    shared_grads = [
        mm_rows(x_col, grad_sa).astype(BF),
        mm_rows(x_col, grad_sb).astype(BF),
        mm_rows(cot_col, shared_hidden).astype(BF),
    ]
    shared_dx = mm_cols(grad_sa, sgate) + mm_cols(grad_sb, sup)

    expert_id = chip * per_chip + my_local
    slot_probs = probs_of(mm(x_in[0], router_halves[0]) + mm(x_in[1], router_halves[1]))
    slot_gate = jnp.sum(
        jnp.where(jnp.arange(n_experts)[None, :] == expert_id, slot_probs, 0.0),
        axis=1,
        keepdims=True,
    )
    expert_a = mm(x_in[0], gate_w[0]) + mm(x_in[1], gate_w[1])
    expert_b = mm(x_in[0], up_w[0]) + mm(x_in[1], up_w[1])
    expert_hidden, expert_back = jax.vjp(swiglu, expert_a, expert_b)
    expert_hidden = expert_hidden.astype(BF)
    rows_back = [between(mm_cols(expert_hidden, w).astype(BF)) for w in down_w]
    slot_grad = [(slot_gate * part.astype(F32)).astype(BF) for part in grad_in]
    grad_hidden = mm(slot_grad[0], down_w[0]) + mm(slot_grad[1], down_w[1])
    grad_ea, grad_eb = (v.astype(BF) for v in expert_back(grad_hidden))
    dx_back = [
        between((mm_cols(grad_ea, gw) + mm_cols(grad_eb, uw)).astype(BF))
        for gw, uw in zip(gate_w, up_w)
    ]

    def expert_sum(left, right):
        own, other = (mm_rows(a, b) for a, b in zip(left, right))
        got = swap(other.astype(BF))
        total = (own + got.astype(F32)).astype(BF).reshape(n_ex // 2, n_dp, r, ff_part)
        back = jnp.zeros((n_dp, n_ex // 2, r, ff_part), BF)
        for i in range(n_dp):
            block = pick(total, before(i), 1)
            block = shift(block, -i) if i else block
            back = lax.dynamic_update_index_in_dim(back, block, after(i), 0)
        back = back.reshape(2, per_chip // 2, splits, half, ff_part).transpose(0, 1, 3, 2, 4)
        back = back.reshape(2, per_chip // 2, half, ff_e)
        keep, got = pick(back, core), swap(pick(back, 1 - core))
        halves_of = [jnp.where(core == 0, keep, got), jnp.where(core == 0, got, keep)]
        return jnp.concatenate(halves_of, axis=1).astype(F32)

    sum_egate = expert_sum(x_in, (grad_ea, grad_ea))
    sum_eup = expert_sum(x_in, (grad_eb, grad_eb))
    sum_edown = expert_sum(slot_grad, (expert_hidden, expert_hidden))

    col_probs = probs_of(mm(x_col, router_owner))
    expert_axis = jnp.arange(n_experts)[None, :]
    gates = [
        jnp.sum(jnp.where(expert_axis == expert, col_probs, 0.0), axis=1, keepdims=True)
        for expert in far_experts
    ]
    gate_hot = jnp.concatenate(
        [hot_t[:, m * per_far : (m + 1) * per_far] * gates[m].astype(BF) for m in range(chips)],
        axis=1,
    )
    out_col = (whole(*(mm(gate_hot, part) for part in rows_back)) + shared_out).astype(BF)
    dots = sum(mm_cols(a, b) for a, b in zip(cot_halves, rows_back)) * hot_t.astype(F32)
    dots = jnp.sum(dots.reshape(n_dp * rows, chips, per_far), axis=-1)
    grad_probs_col = sum(
        jnp.where(expert_axis == far_experts[m], dots[:, m : m + 1], 0.0) for m in range(chips)
    )
    dx_col = whole(*(mm(hot_t, part) for part in dx_back)) + shared_dx
    dx_send = jnp.concatenate(
        [dx_col, grad_probs_col, jnp.zeros((n_dp * rows, 128 - n_experts), F32)], axis=1
    ).astype(BF)

    def to_owners(values):
        cut = values.reshape(n_dp, rows, -1)
        got = [shift(cut[i], -i) for i in range(1, n_dp)]
        return sum((part.astype(F32) for part in got), cut[0].astype(F32))

    dx_sum = to_owners(dx_send)
    out_tokens = (residual + from_owner_order(to_owners(out_col))).astype(BF)

    router_probs = probs_of(mm(hidden_two, router))
    grad_probs = dx_sum[:, width : width + n_experts]
    grad_logits = (
        router_probs * (grad_probs - jnp.sum(grad_probs * router_probs, axis=-1, keepdims=True))
    ).astype(BF)
    grad_router = mm_rows(hidden_two, grad_logits)
    grad_hidden_two = from_owner_order(dx_sum[:, :width]) + mm_cols(grad_logits, router)
    grad_resid_norm, grad_gain_two = norm_two_back(grad_hidden_two)
    grad_residual = cotangent.astype(F32) + grad_resid_norm

    grad_attn = plane_gather(grad_residual.astype(BF), n_dp, n_ex, 4).reshape(seq, width)
    grad_attended = mm_cols(grad_attn, wo_rows).astype(BF)
    grad_wout = mm_rows(attended, grad_attn).astype(BF)
    grad_rope = 0.0
    grad_queries, grad_expanded = [], []
    for h in range(hp):
        gat = grad_attended[:, h * DV : (h + 1) * DV]
        probs = attn_probs[h]
        dp = mm_cols(gat, expanded[:, h, DH:])
        grad_scores = probs * (dp - jnp.sum(dp * probs, axis=-1, keepdims=True))
        grad_raw = jnp.where(allowed, grad_scores * score_scale, 0.0).astype(BF)
        grad_queries.append(mm(grad_raw, keys[h]))
        grad_key = mm_rows(grad_raw, queries[:, h])
        grad_rope = grad_rope + grad_key[:, DH:]
        grad_expanded += [grad_key[:, :DH], mm_rows(probs_low[h], gat)]
    grad_expanded = jnp.concatenate(grad_expanded, axis=1).astype(BF)
    (grad_query_raw,) = query_back(jnp.stack(grad_queries, axis=1))
    grad_query_low = grad_query_raw.reshape(seq, head_cols).astype(BF)
    grad_latent_part = jnp.concatenate([mm_cols(grad_expanded, wexp), grad_rope], axis=1)
    grad_part = jnp.concatenate(
        [
            mm_cols(grad_query_low, wq).astype(BF),
            grad_latent_part.astype(BF),
            jnp.zeros((seq, -lat % 128), BF),
        ],
        axis=1,
    )
    grad_sum = plane_sum(grad_part.reshape(n_ex, rows, -1), n_dp, n_ex, 5)
    own_start = e * rows
    latent_own = lax.dynamic_slice_in_dim(latent_raw, own_start, rows, 0)
    cos_own = lax.dynamic_slice_in_dim(cos_table, own_start, rows, 0)
    sine_own = lax.dynamic_slice_in_dim(sine_table, own_start, rows, 0)

    def make_latent(latent_in, gain_in):
        return (
            rms_norm(latent_in[:, :KVR], gain_in),
            rotate(latent_in[:, KVR:], cos_own, sine_own),
        )

    _, latent_back = jax.vjp(make_latent, latent_own, gain_lat)
    grad_latent_raw, grad_gain_lat = latent_back(
        (grad_sum[:, width : width + KVR], grad_sum[:, width + KVR : width + lat])
    )
    grad_latent_low = grad_latent_raw.astype(BF)
    _, norm_one_back = jax.vjp(rms_norm, tokens_f, gain_one)
    grad_hidden_one = grad_sum[:, :width] + mm_cols(grad_latent_low, w_lat)
    grad_tokens_norm, grad_gain_one = norm_one_back(grad_hidden_one)
    grad_tokens = grad_residual + grad_tokens_norm

    def column_sum(values):
        total = pick(values, z).astype(F32)
        for i in range(1, n_dp):
            total = total + shift(pick(values, before(i)), -i).astype(F32)
        return total

    wout_back = lax.all_to_all(
        grad_wout.reshape(hp, parts, r, width).transpose(1, 0, 2, 3),
        "expert",
        0,
        0,
        axis_index_groups=part_groups,
        tiled=True,
    )
    sum_wout = column_sum(wout_back.reshape(n_dp, r, width))
    def shared_sum(grad):
        grad = lax.psum_scatter(
            grad.reshape(n_ex, n_dp, r, ff_s), "expert", scatter_dimension=0, tiled=True
        ).reshape(n_dp, r, ff_s)
        back = jnp.zeros((n_dp, r, ff_s), BF)
        for i in range(n_dp):
            block = pick(grad, before(i))
            block = shift(block, -i) if i else block
            back = lax.dynamic_update_index_in_dim(back, block, after(i), 0)
        return back.transpose(1, 0, 2).reshape(r, n_dp * ff_s).astype(F32)

    sum_sgate, sum_sup, sum_sdown = (shared_sum(grad) for grad in shared_grads)
    grad_wq = mm_rows(hidden_one, grad_query_low).astype(BF).reshape(n_dp, n_ex, r, head_cols)
    grad_we = mm_rows(latent_low, grad_expanded).astype(BF)
    grad_we = grad_we.reshape(n_dp, n_ex, r, rl * kv_cols // r)
    heads_sum = column_sum(jnp.concatenate([grad_wq, grad_we], axis=-1)).astype(BF)
    heads_back_all = lax.all_to_all(heads_sum, "expert", 0, 0, tiled=True).astype(F32)
    sum_wq = heads_back_all[..., :head_cols].transpose(1, 0, 2).reshape(r, H, DH + DR)
    sum_wq = jnp.take(sum_wq, jnp.array(heads_back), axis=1).reshape(r, H * (DH + DR))
    sum_we = heads_back_all[..., head_cols:].reshape(n_ex, rl, kv_cols).transpose(1, 0, 2)
    sum_we = jnp.take(sum_we.reshape(rl, H, DH + DV), jnp.array(heads_back), axis=1)
    sum_we = sum_we.reshape(rl, H * (DH + DV))

    latent_plane = plane_gather(grad_latent_low, n_dp, n_ex, 6).reshape(seq, lat)
    grad_wlat = pick(mm_rows(hidden_one, latent_plane).reshape(n_dp, n_ex, r, lat), e, 1)
    small = jnp.concatenate(
        [
            grad_router.reshape(n_dp, n_ex, r, n_experts),
            grad_gain_one.reshape(n_dp, n_ex, r, 1),
            grad_gain_two.reshape(n_dp, n_ex, r, 1),
            jnp.pad(grad_gain_lat.reshape(n_dp, n_ex, rl, 1), ((0, 0),) * 2 + ((0, r - rl), (0, 0))),
            jnp.zeros((n_dp, n_ex, r, pack_cols - lat - n_experts - 3), F32),
        ],
        axis=-1,
    ).transpose(1, 0, 2, 3)
    small = jnp.sum(lax.all_to_all(small, "expert", 0, 0, tiled=True), axis=0)
    pack_sum = column_sum(jnp.concatenate([grad_wlat, small], axis=-1).astype(BF))
    return (
        out_tokens,
        grad_tokens,
        pack_sum[:, lat + n_experts],
        sum_wq,
        pack_sum[:, :lat],
        pack_sum[:rl, lat + n_experts + 2],
        sum_we,
        sum_wout,
        pack_sum[:, lat + n_experts + 1],
        pack_sum[:, lat : lat + n_experts],
        sum_sgate,
        sum_sup,
        sum_sdown,
        sum_egate,
        sum_eup,
        sum_edown,
    )


def solution(mesh):
    both = ("dp", "expert")
    in_specs = (
        P(both, None),
        P(both, None),
        P("dp"),
        P(both, None),
        P(both, None),
        P(both),
        P(both, None),
        P(both, None),
        P(both),
        P(both, None),
        P(both, None),
        P(both),
        P(both, None),
        P(both, None),
        P(both, None),
        P(both, None),
        P("expert", "dp", None),
        P("expert", "dp", None),
        P("expert", "dp", None),
    )
    out_specs = (
        P(both, None),
        P(both, None),
        P(both),
        P(both, None),
        P(both, None),
        P(both),
        P(both, None),
        P(both, None),
        P(both),
        P(both, None),
        P(both, None),
        P(both, None),
        P(both, None),
        P("expert", "dp", None),
        P("expert", "dp", None),
        P("expert", "dp", None),
    )
    return jax.shard_map(shards, mesh=mesh, in_specs=in_specs, out_specs=out_specs, check_vma=False)
```

```python
import jax
import jax.numpy as jnp
from jax import lax
from jax.experimental import pallas as pl
from jax.experimental.pallas import tpu as pltpu
from jax.sharding import PartitionSpec as P

H = 16
DH = 128
DR = 64
DV = 128
KVR = 512

norm_eps = 1e-06
masked_score = -1e30
MESH = pl.DeviceIdType.MESH
ANY = pl.BlockSpec(memory_space=pl.ANY)
VMEM = pl.BlockSpec(memory_space=pltpu.VMEM)
BF = jnp.bfloat16
F32 = jnp.float32


def rms_norm(values, scale_gain):
    return (
        values
        * lax.rsqrt(jnp.mean(values * values, axis=-1, keepdims=True) + norm_eps)
        * scale_gain
    )


def rotate(values, cos_table, sine_table):
    half_dim = values.shape[-1] // 2
    first_half = values[..., :half_dim]
    second_half = values[..., half_dim:]
    return jnp.concatenate(
        [
            first_half * cos_table - second_half * sine_table,
            second_half * cos_table + first_half * sine_table,
        ],
        axis=-1,
    )


def rope_tables(positions):
    half_dim = DR // 2
    inv_freq = 10000.0 ** (-(jnp.arange(half_dim).astype(F32) * 2.0) / DR)
    angles = positions.astype(F32)[:, None] * inv_freq[None, :]
    return (jnp.cos(angles), jnp.sin(angles))


def swiglu(gate_in, up_in):
    return jax.nn.silu(gate_in) * up_in


def mm(left, right):
    return jnp.dot(left, right, preferred_element_type=F32)


def mm_rows(left, right):
    return lax.dot_general(left, right, (((0,), (0,)), ((), ())), preferred_element_type=F32)


def mm_cols(left, right):
    return lax.dot_general(left, right, (((1,), (1,)), ((), ())), preferred_element_type=F32)


def slot_places(route_rows, pair_order, capacity):
    pair_expert = route_rows.reshape(-1)
    earlier = pair_order[None, :] < pair_order[:, None]
    same_expert = pair_expert[None, :] == pair_expert[:, None]
    places = jnp.sum((earlier & same_expert).astype(jnp.int32), axis=1)
    slot_index = jnp.where(places < capacity, pair_expert * capacity + places, -1)
    return slot_index.reshape(route_rows.shape)


def params(collective_id):
    return pltpu.CompilerParams(
        collective_id=collective_id, has_side_effects=True, vmem_limit_bytes=48 << 20
    )


def remote(src, dst, send_sem, recv_sem, device):
    return pltpu.make_async_remote_copy(
        src_ref=src,
        dst_ref=dst,
        send_sem=send_sem,
        recv_sem=recv_sem,
        device_id=device,
        device_id_type=MESH,
    )


def greet(devices):
    barrier = pltpu.get_barrier_semaphore()
    for device in devices:
        pl.semaphore_signal(barrier, inc=1, device_id=device, device_id_type=MESH)
    pl.semaphore_wait(barrier, len(devices))


def places(n_dp, n_ex):
    z = lax.axis_index("dp")
    e = lax.axis_index("expert")
    chips = n_ex // 2
    c, k = e // 2, lax.rem(e, 2)
    sibling = (z, e + 1 - 2 * k)
    same_core = [(z, lax.rem(c + i, chips) * 2 + k) for i in range(1, chips)]
    column = [(lax.rem(z + i, n_dp), e) for i in range(1, n_dp)]
    return z, e, c, k, sibling, same_core, column


def plane_gather(block, n_dp, n_ex, collective_id):
    chips = n_ex // 2

    def kernel(x_ref, o_ref, send, recv, sib_send, sib_recv, local):
        z, e, c, k, sibling, same_core, _ = places(n_dp, n_ex)
        greet(same_core + [sibling])
        far = []
        for i in range(1, chips):
            copy = remote(x_ref, o_ref.at[e], send.at[i], recv.at[i], same_core[i - 1])
            copy.start()
            far.append(copy)
        near = [remote(x_ref, o_ref.at[e], sib_send.at[0], sib_recv.at[0], sibling)]
        near[0].start()
        own = pltpu.make_async_copy(x_ref, o_ref.at[e], local)
        own.start()
        for i in range(1, chips):
            source = lax.rem(c + chips - i, chips) * 2 + k
            far[i - 1].wait_recv()
            copy = remote(
                o_ref.at[source], o_ref.at[source], sib_send.at[i], sib_recv.at[i], sibling
            )
            copy.start()
            near.append(copy)
        own.wait()
        for copy in far:
            copy.wait_send()
        for copy in near:
            copy.wait()

    return pl.pallas_call(
        kernel,
        out_shape=jax.ShapeDtypeStruct((n_ex,) + block.shape, block.dtype),
        in_specs=[ANY],
        out_specs=ANY,
        scratch_shapes=[pltpu.SemaphoreType.DMA((chips,))] * 4 + [pltpu.SemaphoreType.DMA],
        compiler_params=params(collective_id),
    )(block)


def plane_sum(arrays, n_dp, n_ex, collective_id):
    chips = n_ex // 2
    count = len(arrays)

    def kernel(*refs):
        x_refs, o_refs = refs[:count], refs[count : 2 * count]
        bufs = refs[2 * count : 5 * count]
        sems = refs[5 * count :]
        z, e, c, k, sibling, same_core, _ = places(n_dp, n_ex)
        greet(same_core + [sibling])
        near, far = {}, {}
        for i in list(range(1, chips)) + [0]:
            chip = lax.rem(c + i, chips)
            for j in range(count):
                near[i, j] = remote(
                    x_refs[j].at[chip * 2 + 1 - k],
                    bufs[3 * j].at[chip],
                    sems[4 * j].at[i],
                    sems[4 * j + 1].at[i],
                    sibling,
                )
                near[i, j].start()
        for i in range(1, chips):
            chip = lax.rem(c + i, chips)
            for j in range(count):
                from_sib, out_buf, from_far = bufs[3 * j : 3 * j + 3]
                near[i, j].wait_recv()
                out_buf[i] = (
                    x_refs[j][chip * 2 + k].astype(F32) + from_sib[chip].astype(F32)
                ).astype(BF)
                far[i, j] = remote(
                    out_buf.at[i],
                    from_far.at[i],
                    sems[4 * j + 2].at[i],
                    sems[4 * j + 3].at[i],
                    same_core[i - 1],
                )
                far[i, j].start()
        for j in range(count):
            near[0, j].wait_recv()
            o_refs[j][...] = x_refs[j][e].astype(F32) + bufs[3 * j][c].astype(F32)
        for i in range(1, chips):
            for j in range(count):
                far[i, j].wait_recv()
                o_refs[j][...] += bufs[3 * j + 2][i].astype(F32)
        for copy in list(near.values()) + list(far.values()):
            copy.wait_send()

    scratch = []
    for array in arrays:
        scratch += [pltpu.VMEM((chips,) + array.shape[1:], BF)] * 3
    scratch += [pltpu.SemaphoreType.DMA((chips,))] * (4 * count)
    return pl.pallas_call(
        kernel,
        out_shape=[jax.ShapeDtypeStruct(array.shape[1:], F32) for array in arrays],
        in_specs=[VMEM] * count,
        out_specs=[VMEM] * count,
        scratch_shapes=scratch,
        compiler_params=params(collective_id),
    )(*arrays)


def column_gather(block, n_dp, n_ex, collective_id):
    def kernel(x_ref, o_ref, send, recv, local):
        z, e, c, k, sibling, same_core, column = places(n_dp, n_ex)
        greet(column)
        copies = []
        for i in range(1, n_dp):
            copy = remote(x_ref, o_ref.at[i], send.at[i], recv.at[i], column[i - 1])
            copy.start()
            copies.append(copy)
        own = pltpu.make_async_copy(x_ref, o_ref.at[0], local)
        own.start()
        own.wait()
        for copy in copies:
            copy.wait()

    return pl.pallas_call(
        kernel,
        out_shape=jax.ShapeDtypeStruct((n_dp,) + block.shape, block.dtype),
        in_specs=[ANY],
        out_specs=ANY,
        scratch_shapes=[pltpu.SemaphoreType.DMA((n_dp,))] * 2 + [pltpu.SemaphoreType.DMA],
        compiler_params=params(collective_id),
    )(block)


def first_exchange(tok, heads_w, pack, n_dp, n_ex, collective_id):
    chips = n_ex // 2

    def kernel(
        tok_ref, wa_ref, pk_ref, tok_out, wa_out, pk_out,
        t_send, t_recv, ts_send, ts_recv, a_send, a_recv, az_send, az_recv,
        p_send, p_recv, pf_send, pf_recv, ps_send, ps_recv, local,
    ):
        z, e, c, k, sibling, same_core, column = places(n_dp, n_ex)
        plane = [(z, lax.rem(e + i, n_ex)) for i in range(1, n_ex)]
        greet(plane + column)
        wa_far, pk_col, tok_far = [], [], []
        for i in range(1, n_ex):
            copy = remote(
                wa_ref.at[lax.rem(e + i, n_ex)], wa_out.at[z, e],
                a_send.at[i], a_recv.at[i], plane[i - 1],
            )
            copy.start()
            wa_far.append(copy)
        for i in range(1, n_dp):
            copy = remote(pk_ref, pk_out.at[z, e], p_send.at[i], p_recv.at[i], column[i - 1])
            copy.start()
            pk_col.append(copy)
        for i in range(1, chips):
            copy = remote(tok_ref, tok_out.at[e], t_send.at[i], t_recv.at[i], same_core[i - 1])
            copy.start()
            tok_far.append(copy)
        near = [remote(tok_ref, tok_out.at[e], ts_send.at[0], ts_recv.at[0], sibling)]
        near[0].start()
        own = [
            pltpu.make_async_copy(wa_ref.at[e], wa_out.at[z, e], local.at[0]),
            pltpu.make_async_copy(pk_ref, pk_out.at[z, e], local.at[1]),
            pltpu.make_async_copy(tok_ref, tok_out.at[e], local.at[2]),
        ]
        for copy in own:
            copy.start()
        for copy in own:
            copy.wait()
        for copy in wa_far:
            copy.wait_recv()
        wa_col = []
        for i in range(1, n_dp):
            copy = remote(
                wa_out.at[z], wa_out.at[z], az_send.at[i], az_recv.at[i], column[i - 1]
            )
            copy.start()
            wa_col.append(copy)
        for copy in pk_col:
            copy.wait_recv()
        pk_far = []
        for i in range(1, chips):
            copy = remote(
                pk_out.at[:, e], pk_out.at[:, e], pf_send.at[i], pf_recv.at[i], same_core[i - 1]
            )
            copy.start()
            pk_far.append(copy)
        copy = remote(pk_out.at[:, e], pk_out.at[:, e], ps_send.at[0], ps_recv.at[0], sibling)
        copy.start()
        near.append(copy)
        for i in range(1, chips):
            source = lax.rem(c + chips - i, chips) * 2 + k
            tok_far[i - 1].wait_recv()
            copy = remote(
                tok_out.at[source], tok_out.at[source], ts_send.at[i], ts_recv.at[i], sibling
            )
            copy.start()
            near.append(copy)
            pk_far[i - 1].wait_recv()
            copy = remote(
                pk_out.at[:, source], pk_out.at[:, source], ps_send.at[i], ps_recv.at[i], sibling
            )
            copy.start()
            near.append(copy)
        for copy in near + wa_col:
            copy.wait()
        for copy in wa_far + pk_col + tok_far + pk_far:
            copy.wait_send()

    dma = pltpu.SemaphoreType.DMA
    return pl.pallas_call(
        kernel,
        out_shape=[
            jax.ShapeDtypeStruct((n_ex,) + tok.shape, tok.dtype),
            jax.ShapeDtypeStruct((n_dp,) + heads_w.shape, heads_w.dtype),
            jax.ShapeDtypeStruct((n_dp, n_ex) + pack.shape, pack.dtype),
        ],
        in_specs=[ANY] * 3,
        out_specs=[ANY] * 3,
        scratch_shapes=[dma((chips,))] * 4
        + [dma((n_ex,))] * 2
        + [dma((n_dp,))] * 4
        + [dma((chips,))] * 4
        + [dma((3,))],
        compiler_params=params(collective_id),
    )(tok, heads_w, pack)


def shards(
    tokens,
    cotangent,
    lengths,
    routes,
    place_order,
    attn_gain,
    w_query,
    w_latent,
    latent_gain,
    w_expand,
    w_out,
    ffn_gain,
    w_router,
    shared_gate,
    shared_up,
    shared_down,
    expert_gate,
    expert_up,
    expert_down,
):
    rows, width = tokens.shape
    n_dp = lax.axis_size("dp")
    n_ex = lax.axis_size("expert")
    chips = n_ex // 2
    z = lax.axis_index("dp")
    e = lax.axis_index("expert")
    chip, core = e // 2, lax.rem(e, 2)
    n_experts = w_router.shape[1]
    top_k = routes.shape[1]
    capacity = (rows * top_k * 5 + 4 * n_experts - 1) // (4 * n_experts)
    cap = (capacity + 15) // 16 * 16
    seq = rows * n_ex
    r = w_query.shape[0]
    rl = w_expand.shape[0]
    hp = H // n_ex
    parts = DV // r
    heads = [
        (d * n_ex + (j // parts) * parts) * r // DV
        for j in range(n_ex)
        for d in range(j % parts * hp, j % parts * hp + hp)
    ]
    heads_back = [heads.index(h) for h in range(H)]
    per_chip = n_experts // chips
    splits = n_dp // per_chip
    my_local = z // splits
    sib_perm = [(i, i ^ 1) for i in range(n_ex)]
    part_groups = [[i * parts + m for m in range(parts)] for i in range(n_ex // parts)]
    ff_e = expert_gate.shape[2]
    ff_part = ff_e // splits
    half = expert_gate.shape[1] // 2
    ff_s = shared_gate.shape[1] // n_dp
    lat = KVR + DR
    head_cols = hp * (DH + DR)
    kv_cols = hp * (DH + DV)

    wq_send = jnp.take(w_query.reshape(r, H, DH + DR), jnp.array(heads), axis=1)
    wq_send = wq_send.reshape(r, n_ex, head_cols).transpose(1, 0, 2)
    we_send = jnp.take(w_expand.reshape(rl, H, DH + DV), jnp.array(heads), axis=1)
    we_send = we_send.reshape(rl, n_ex, kv_cols).transpose(1, 0, 2)
    we_send = we_send.reshape(n_ex, r, rl * kv_cols // r)
    wa_send = jnp.concatenate([wq_send, we_send], axis=-1)
    pack_cols = (lat + n_experts + 3 + 127) // 128 * 128
    pack = jnp.concatenate(
        [
            w_latent,
            w_router,
            attn_gain[:, None],
            ffn_gain[:, None],
            jnp.pad(latent_gain, (0, r - rl))[:, None],
            jnp.zeros((r, pack_cols - lat - n_experts - 3), BF),
        ],
        axis=1,
    )
    tok_all, wa_all, pk_all = first_exchange(tokens, wa_send, pack, n_dp, n_ex, 1)
    wq = wa_all[..., :head_cols].reshape(width, head_cols)
    wexp = wa_all[..., head_cols:].reshape(KVR, kv_cols)
    pk_flat = pk_all.reshape(width, pack_cols)
    w_lat = pk_flat[:, :lat]
    router = pk_flat[:, lat : lat + n_experts]
    gain_one = pk_flat[:, lat + n_experts].astype(F32)
    gain_two = pk_flat[:, lat + n_experts + 1].astype(F32)
    gain_lat = (
        pk_all[..., lat + n_experts + 2].reshape(n_dp * n_ex, r)[:, :rl].reshape(KVR).astype(F32)
    )

    def shift(values, step):
        return lax.ppermute(values, "dp", [(i, (i + step) % n_dp) for i in range(n_dp)])

    def before(step):
        return lax.rem(z + n_dp - step, n_dp)

    def after(step):
        return lax.rem(z + step, n_dp)

    def swap(values):
        return lax.ppermute(values, "expert", sib_perm)

    def pick(values, index, axis=0):
        return lax.dynamic_index_in_dim(values, index, axis, keepdims=False)

    def shared_blocks(index):
        return jnp.stack([pick(w, index) for w in shared_cut])

    shared_cut = [
        w.reshape(r, n_dp, ff_s).transpose(1, 0, 2) for w in (shared_gate, shared_up, shared_down)
    ]
    shared_cut, _ = lax.optimization_barrier((shared_cut, pk_all))
    shared_mine = jnp.zeros((3, n_dp, r, ff_s), BF)
    for i in range(n_dp):
        block = shared_blocks(after(i))
        block = shift(block, i) if i else block
        shared_mine = lax.dynamic_update_index_in_dim(shared_mine, block, before(i), 1)
    sgate, sup, sdown = (
        lax.all_gather(shared_mine[i], "expert", axis=0, tiled=False).reshape(width, ff_s)
        for i in range(3)
    )

    expert_w = [w.reshape(-1, 2, half, ff_e) for w in (expert_gate, expert_up, expert_down)]
    kept = jnp.stack([pick(w, core, 1) for w in expert_w])
    given = jnp.stack([pick(w, 1 - core, 1) for w in expert_w])
    experts = jnp.concatenate([kept, swap(given)], axis=1)
    experts = experts.reshape(3, per_chip, n_ex // 2, r, splits, ff_part)
    experts, _ = lax.optimization_barrier((experts, pk_all))
    own = jnp.zeros((3, n_ex // 2, n_dp, r, ff_part), BF)
    for i in range(n_dp):
        to = after(i)
        expert = lax.rem(to // splits + per_chip - core * (per_chip // 2), per_chip)
        block = pick(pick(experts, expert, 1), lax.rem(to, splits), 3)
        block = shift(block, i) if i else block
        own = lax.dynamic_update_index_in_dim(own, block, before(i), 2)
    own = own.reshape(3, width // 2, ff_part)
    other = swap(own)
    gate_w, up_w, down_w = ((own[i], other[i]) for i in range(3))
    wo_send, _ = lax.optimization_barrier((w_out, pk_all))
    wo_col = lax.all_gather(wo_send, "dp", axis=0, tiled=False)
    wo_rows = lax.all_to_all(
        wo_col.reshape(parts, hp, r, width),
        "expert",
        0,
        0,
        axis_index_groups=part_groups,
        tiled=True,
    )
    wo_rows = wo_rows.transpose(1, 0, 2, 3).reshape(hp * DV, width)
    def to_owner_order(values):
        cut = values.reshape(values.shape[0], n_dp, n_ex, r)
        return cut.transpose(0, 2, 1, 3).reshape(values.shape)

    def from_owner_order(values):
        cut = values.reshape(values.shape[0], n_ex, n_dp, r)
        return cut.transpose(0, 2, 1, 3).reshape(values.shape)

    def column(values):
        return jnp.concatenate([values] + [shift(values, i) for i in range(1, n_dp)], axis=0)

    slot_own = slot_places(routes, place_order[0], capacity)
    slots_all = n_experts * capacity
    slot_ids = column(slot_own).reshape(n_dp, rows, top_k)
    slot_ids = jnp.where(
        slot_ids >= 0, slot_ids + (jnp.arange(n_dp) * slots_all)[:, None, None], -1
    ).reshape(n_dp * rows, top_k)
    place = jnp.arange(cap)
    far_experts = [(chip ^ m) * per_chip + my_local for m in range(chips)]
    wanted = (
        jnp.stack(far_experts)[:, None, None] * capacity
        + (jnp.arange(n_dp) * slots_all)[None, :, None]
        + place[None, None, :]
    )
    wanted = jnp.where(place[None, None, :] < capacity, wanted, -2).reshape(-1)
    n_slots = wanted.shape[0]
    per_far = n_slots // chips
    hot = sum(
        (wanted[:, None] == slot_ids[None, :, j]).astype(BF) for j in range(top_k)
    )
    hot_t = sum(
        (slot_ids[:, j][:, None] == wanted[None, :]).astype(BF) for j in range(top_k)
    )
    cot_send, _ = lax.optimization_barrier((to_owner_order(cotangent), pk_all))
    cot_col = column(cot_send)

    def turned(values):
        first, second = values[:, : width // 2], values[:, width // 2 :]
        return jnp.concatenate(
            [jnp.where(core == 0, first, second), jnp.where(core == 0, second, first)], axis=1
        )

    def between(values):
        cut = values.reshape(chips, per_far, -1)
        got = [cut[0]]
        for m in range(1, chips):
            perm = [(i, i ^ (2 * m)) for i in range(n_ex)]
            got.append(lax.ppermute(cut[m], "expert", perm))
        return jnp.concatenate(got, axis=0)

    cot_turned = turned(cot_col)
    grad_in = between(mm(hot, cot_turned).astype(BF))

    tok_plane = tok_all.reshape(seq, width)
    hidden_one = rms_norm(tok_plane.astype(F32), gain_one).astype(BF)
    positions = jnp.arange(seq)
    cos_table, sine_table = rope_tables(positions)
    query_raw = mm(hidden_one, wq).reshape(seq, hp, DH + DR)

    def make_queries(query_in):
        return jnp.concatenate(
            [
                query_in[..., :DH],
                rotate(query_in[..., DH:], cos_table[:, None, :], sine_table[:, None, :]),
            ],
            axis=-1,
        )

    query_rot, query_back = jax.vjp(make_queries, query_raw)
    queries = query_rot.astype(BF)
    latent_raw = mm(hidden_one, w_lat)
    latent_low = rms_norm(latent_raw[:, :KVR], gain_lat).astype(BF)
    rope_low = rotate(latent_raw[:, KVR:], cos_table, sine_table).astype(BF)
    expanded = mm(latent_low, wexp).astype(BF).reshape(seq, hp, DH + DV)
    score_scale = (DH + DR) ** (-0.5)
    allowed = (positions[None, :] <= positions[:, None]) & (positions[None, :] < lengths[0])
    attn_probs, probs_low, keys, attended = [], [], [], []
    for h in range(hp):
        key = jnp.concatenate([expanded[:, h, :DH], rope_low], axis=1)
        scores = jnp.where(allowed, mm_cols(queries[:, h], key) * score_scale, masked_score)
        top = jnp.max(scores, axis=-1, keepdims=True)
        exp_scores = jnp.exp(scores - top)
        probs = exp_scores / jnp.sum(exp_scores, axis=-1, keepdims=True)
        low = probs.astype(BF)
        attn_probs.append(probs)
        probs_low.append(low)
        keys.append(key)
        attended.append(mm(low, expanded[:, h, DH:]).astype(BF))
    attended = jnp.concatenate(attended, axis=1)
    out_part = mm(attended, wo_rows).astype(BF)
    tokens_f = tokens.astype(F32)
    residual = tokens_f + plane_sum([out_part.reshape(n_ex, rows, width)], n_dp, n_ex, 2)[0]
    normed_two, norm_two_back = jax.vjp(rms_norm, residual, gain_two)
    hidden_two = normed_two.astype(BF)
    x_col = column_gather(to_owner_order(hidden_two), n_dp, n_ex, 3).reshape(n_dp * rows, width)

    x_in = between(mm(hot, turned(x_col)).astype(BF))
    router_owner = to_owner_order(router.T).T
    router_turned = turned(router_owner.T).T

    def probs_of(logits):
        top = jnp.max(logits, axis=-1, keepdims=True)
        exp_logits = jnp.exp(logits - top)
        return exp_logits / jnp.sum(exp_logits, axis=-1, keepdims=True)

    shared_a = mm(x_col, sgate)
    shared_b = mm(x_col, sup)
    shared_hidden, shared_back = jax.vjp(swiglu, shared_a, shared_b)
    shared_hidden = shared_hidden.astype(BF)
    shared_out = mm_cols(shared_hidden, sdown)
    grad_sa, grad_sb = (v.astype(BF) for v in shared_back(mm(cot_col, sdown)))
    shared_grads = [
        mm_rows(x_col, grad_sa).astype(BF),
        mm_rows(x_col, grad_sb).astype(BF),
        mm_rows(cot_col, shared_hidden).astype(BF),
    ]
    shared_dx = mm_cols(grad_sa, sgate) + mm_cols(grad_sb, sup)

    expert_id = chip * per_chip + my_local
    slot_probs = probs_of(mm(x_in, router_turned))
    slot_gate = jnp.sum(
        jnp.where(jnp.arange(n_experts)[None, :] == expert_id, slot_probs, 0.0),
        axis=1,
        keepdims=True,
    )
    mid = width // 2

    def into(values, weight):
        return mm(values[:, :mid], weight[0]) + mm(values[:, mid:], weight[1])

    expert_a = into(x_in, gate_w)
    expert_b = into(x_in, up_w)
    expert_hidden, expert_back = jax.vjp(swiglu, expert_a, expert_b)
    expert_hidden = expert_hidden.astype(BF)
    rows_back = between(
        jnp.concatenate([mm_cols(expert_hidden, w).astype(BF) for w in down_w], axis=1)
    )
    slot_grad = (slot_gate * grad_in.astype(F32)).astype(BF)
    grad_hidden = into(slot_grad, down_w)
    grad_ea, grad_eb = (v.astype(BF) for v in expert_back(grad_hidden))
    dx_back = between(
        jnp.concatenate(
            [
                (mm_cols(grad_ea, gw) + mm_cols(grad_eb, uw)).astype(BF)
                for gw, uw in zip(gate_w, up_w)
            ],
            axis=1,
        )
    )
    sides = [(x_in, grad_ea), (x_in, grad_eb), (slot_grad, expert_hidden)]
    kept = jnp.stack([mm_rows(a[:, :mid], b).astype(BF) for a, b in sides])
    given = jnp.stack([mm_rows(a[:, mid:], b).astype(BF) for a, b in sides])
    expert_total = (kept.astype(F32) + swap(given).astype(F32)).astype(BF)
    expert_total = expert_total.reshape(3, n_ex // 2, n_dp, r, ff_part)

    col_probs = probs_of(mm(x_col, router_owner))
    expert_axis = jnp.arange(n_experts)[None, :]
    gates = [
        jnp.sum(jnp.where(expert_axis == expert, col_probs, 0.0), axis=1, keepdims=True)
        for expert in far_experts
    ]
    gate_hot = jnp.concatenate(
        [hot_t[:, m * per_far : (m + 1) * per_far] * gates[m].astype(BF) for m in range(chips)],
        axis=1,
    )
    out_col = (turned(mm(gate_hot, rows_back)) + shared_out).astype(BF)
    dots = mm_cols(cot_turned, rows_back) * hot_t.astype(F32)
    dots = jnp.sum(dots.reshape(n_dp * rows, chips, per_far), axis=-1)
    grad_probs_col = sum(
        jnp.where(expert_axis == far_experts[m], dots[:, m : m + 1], 0.0) for m in range(chips)
    )
    dx_col = turned(mm(hot_t, dx_back)) + shared_dx
    dx_send = jnp.concatenate(
        [dx_col, grad_probs_col, jnp.zeros((n_dp * rows, 128 - n_experts), F32)], axis=1
    ).astype(BF)

    def to_owners(values):
        cut = values.reshape(n_dp, rows, -1)
        got = [shift(cut[i], -i) for i in range(1, n_dp)]
        return sum((part.astype(F32) for part in got), cut[0].astype(F32))

    dx_sum = to_owners(dx_send)
    out_tokens = (residual + from_owner_order(to_owners(out_col))).astype(BF)

    router_probs = probs_of(mm(hidden_two, router))
    grad_probs = dx_sum[:, width : width + n_experts]
    grad_logits = (
        router_probs * (grad_probs - jnp.sum(grad_probs * router_probs, axis=-1, keepdims=True))
    ).astype(BF)
    grad_router = mm_rows(hidden_two, grad_logits)
    grad_hidden_two = from_owner_order(dx_sum[:, :width]) + mm_cols(grad_logits, router)
    grad_resid_norm, grad_gain_two = norm_two_back(grad_hidden_two)
    grad_residual = cotangent.astype(F32) + grad_resid_norm

    grad_attn_low, expert_total = lax.optimization_barrier(
        (grad_residual.astype(BF), expert_total)
    )
    grad_attn = plane_gather(grad_attn_low, n_dp, n_ex, 4).reshape(seq, width)
    expert_far = [pick(expert_total, z, 2)]
    for i in range(1, n_dp):
        expert_far.append(shift(pick(expert_total, before(i), 2), -i))
    grad_attended = mm_cols(grad_attn, wo_rows).astype(BF)
    grad_wout = mm_rows(attended, grad_attn).astype(BF)
    grad_rope = 0.0
    grad_queries, grad_expanded = [], []
    for h in range(hp):
        gat = grad_attended[:, h * DV : (h + 1) * DV]
        probs = attn_probs[h]
        dp = mm_cols(gat, expanded[:, h, DH:])
        grad_scores = probs * (dp - jnp.sum(dp * probs, axis=-1, keepdims=True))
        grad_raw = jnp.where(allowed, grad_scores * score_scale, 0.0).astype(BF)
        grad_queries.append(mm(grad_raw, keys[h]))
        grad_key = mm_rows(grad_raw, queries[:, h])
        grad_rope = grad_rope + grad_key[:, DH:]
        grad_expanded += [grad_key[:, :DH], mm_rows(probs_low[h], gat)]
    grad_expanded = jnp.concatenate(grad_expanded, axis=1).astype(BF)
    (grad_query_raw,) = query_back(jnp.stack(grad_queries, axis=1))
    grad_query_low = grad_query_raw.reshape(seq, head_cols).astype(BF)
    grad_latent_part = jnp.concatenate([mm_cols(grad_expanded, wexp), grad_rope], axis=1)
    grad_latent_part = jnp.pad(grad_latent_part, ((0, 0), (0, -lat % 128))).astype(BF)
    grad_query_part = mm_cols(grad_query_low, wq).astype(BF)
    (grad_query_part, grad_latent_part), expert_far[: n_dp // 2] = lax.optimization_barrier(
        ((grad_query_part, grad_latent_part), expert_far[: n_dp // 2])
    )
    grad_query_sum, grad_latent_sum = plane_sum(
        [grad_query_part.reshape(n_ex, rows, width), grad_latent_part.reshape(n_ex, rows, -1)],
        n_dp,
        n_ex,
        5,
    )
    own_start = e * rows
    latent_own = lax.dynamic_slice_in_dim(latent_raw, own_start, rows, 0)
    cos_own = lax.dynamic_slice_in_dim(cos_table, own_start, rows, 0)
    sine_own = lax.dynamic_slice_in_dim(sine_table, own_start, rows, 0)

    def make_latent(latent_in, gain_in):
        return (
            rms_norm(latent_in[:, :KVR], gain_in),
            rotate(latent_in[:, KVR:], cos_own, sine_own),
        )

    _, latent_back = jax.vjp(make_latent, latent_own, gain_lat)
    grad_latent_raw, grad_gain_lat = latent_back(
        (grad_latent_sum[:, :KVR], grad_latent_sum[:, KVR:lat])
    )
    grad_latent_low = grad_latent_raw.astype(BF)
    _, norm_one_back = jax.vjp(rms_norm, tokens_f, gain_one)
    grad_hidden_one = grad_query_sum + mm_cols(grad_latent_low, w_lat)
    grad_tokens_norm, grad_gain_one = norm_one_back(grad_hidden_one)
    grad_tokens = grad_residual + grad_tokens_norm

    def column_sum(values):
        total = pick(values, z).astype(F32)
        for i in range(1, n_dp):
            total = total + shift(pick(values, before(i)), -i).astype(F32)
        return total

    wout_back = lax.all_to_all(
        grad_wout.reshape(hp, parts, r, width).transpose(1, 0, 2, 3),
        "expert",
        0,
        0,
        axis_index_groups=part_groups,
        tiled=True,
    )
    sum_wout = column_sum(wout_back.reshape(n_dp, r, width))
    def in_order(blocks):
        stacked = jnp.stack(blocks)
        return [pick(stacked, lax.rem(j + n_dp - z, n_dp)) for j in range(n_dp)]

    shared_sums = jnp.stack(
        [
            lax.psum_scatter(
                grad.reshape(n_ex, n_dp, r, ff_s), "expert", scatter_dimension=0, tiled=True
            ).reshape(n_dp, r, ff_s)
            for grad in shared_grads
        ]
    )
    shared_far = [pick(shared_sums, z, 1)]
    for i in range(1, n_dp):
        shared_far.append(shift(pick(shared_sums, before(i), 1), -i))
    shared_far = in_order(shared_far)
    sum_sgate, sum_sup, sum_sdown = (
        jnp.concatenate([part[i] for part in shared_far], axis=1).astype(F32) for i in range(3)
    )
    expert_all = jnp.stack(in_order(expert_far), axis=1)
    expert_all = expert_all.reshape(3, 2, per_chip // 2, splits, half, ff_part)
    expert_all = expert_all.transpose(0, 1, 2, 4, 3, 5).reshape(3, 2, per_chip // 2, half, ff_e)
    keep, got = pick(expert_all, core, 1), swap(pick(expert_all, 1 - core, 1))
    sum_egate, sum_eup, sum_edown = (
        jnp.concatenate(
            [jnp.where(core == 0, keep[i], got[i]), jnp.where(core == 0, got[i], keep[i])], axis=1
        ).astype(F32)
        for i in range(3)
    )
    grad_wq = mm_rows(hidden_one, grad_query_low).astype(BF).reshape(n_dp, n_ex, r, head_cols)
    grad_we = mm_rows(latent_low, grad_expanded).astype(BF)
    grad_we = grad_we.reshape(n_dp, n_ex, r, rl * kv_cols // r)
    heads_sum = column_sum(jnp.concatenate([grad_wq, grad_we], axis=-1)).astype(BF)
    heads_back_all = lax.all_to_all(heads_sum, "expert", 0, 0, tiled=True).astype(F32)
    sum_wq = heads_back_all[..., :head_cols].transpose(1, 0, 2).reshape(r, H, DH + DR)
    sum_wq = jnp.take(sum_wq, jnp.array(heads_back), axis=1).reshape(r, H * (DH + DR))
    sum_we = heads_back_all[..., head_cols:].reshape(n_ex, rl, kv_cols).transpose(1, 0, 2)
    sum_we = jnp.take(sum_we.reshape(rl, H, DH + DV), jnp.array(heads_back), axis=1)
    sum_we = sum_we.reshape(rl, H * (DH + DV))

    latent_plane = plane_gather(grad_latent_low, n_dp, n_ex, 6).reshape(seq, lat)
    grad_wlat = pick(mm_rows(hidden_one, latent_plane).reshape(n_dp, n_ex, r, lat), e, 1)
    small = jnp.concatenate(
        [
            grad_router.reshape(n_dp, n_ex, r, n_experts),
            grad_gain_one.reshape(n_dp, n_ex, r, 1),
            grad_gain_two.reshape(n_dp, n_ex, r, 1),
            jnp.pad(grad_gain_lat.reshape(n_dp, n_ex, rl, 1), ((0, 0),) * 2 + ((0, r - rl), (0, 0))),
            jnp.zeros((n_dp, n_ex, r, pack_cols - lat - n_experts - 3), F32),
        ],
        axis=-1,
    ).transpose(1, 0, 2, 3)
    small = jnp.sum(lax.all_to_all(small, "expert", 0, 0, tiled=True), axis=0)
    pack_sum = column_sum(jnp.concatenate([grad_wlat, small], axis=-1).astype(BF))
    return (
        out_tokens,
        grad_tokens,
        pack_sum[:, lat + n_experts],
        sum_wq,
        pack_sum[:, :lat],
        pack_sum[:rl, lat + n_experts + 2],
        sum_we,
        sum_wout,
        pack_sum[:, lat + n_experts + 1],
        pack_sum[:, lat : lat + n_experts],
        sum_sgate,
        sum_sup,
        sum_sdown,
        sum_egate,
        sum_eup,
        sum_edown,
    )


def solution(mesh):
    both = ("dp", "expert")
    in_specs = (
        P(both, None),
        P(both, None),
        P("dp"),
        P(both, None),
        P(both, None),
        P(both),
        P(both, None),
        P(both, None),
        P(both),
        P(both, None),
        P(both, None),
        P(both),
        P(both, None),
        P(both, None),
        P(both, None),
        P(both, None),
        P("expert", "dp", None),
        P("expert", "dp", None),
        P("expert", "dp", None),
    )
    out_specs = (
        P(both, None),
        P(both, None),
        P(both),
        P(both, None),
        P(both, None),
        P(both),
        P(both, None),
        P(both, None),
        P(both),
        P(both, None),
        P(both, None),
        P(both, None),
        P(both, None),
        P("expert", "dp", None),
        P("expert", "dp", None),
        P("expert", "dp", None),
    )
    return jax.shard_map(shards, mesh=mesh, in_specs=in_specs, out_specs=out_specs, check_vma=False)
```

```python
import jax
import jax.numpy as jnp
from jax import lax
from jax.experimental import pallas as pl
from jax.experimental.pallas import tpu as pltpu
from jax.sharding import PartitionSpec as P

H = 16
DH = 128
DR = 64
DV = 128
KVR = 512

norm_eps = 1e-06
masked_score = -1e30
MESH = pl.DeviceIdType.MESH
ANY = pl.BlockSpec(memory_space=pl.ANY)
VMEM = pl.BlockSpec(memory_space=pltpu.VMEM)
BF = jnp.bfloat16
F32 = jnp.float32


def rms_norm(values, scale_gain):
    return (
        values
        * lax.rsqrt(jnp.mean(values * values, axis=-1, keepdims=True) + norm_eps)
        * scale_gain
    )


def rotate(values, cos_table, sine_table):
    half_dim = values.shape[-1] // 2
    first_half = values[..., :half_dim]
    second_half = values[..., half_dim:]
    return jnp.concatenate(
        [
            first_half * cos_table - second_half * sine_table,
            second_half * cos_table + first_half * sine_table,
        ],
        axis=-1,
    )


def rope_tables(positions):
    half_dim = DR // 2
    inv_freq = 10000.0 ** (-(jnp.arange(half_dim).astype(F32) * 2.0) / DR)
    angles = positions.astype(F32)[:, None] * inv_freq[None, :]
    return (jnp.cos(angles), jnp.sin(angles))


def swiglu(gate_in, up_in):
    return jax.nn.silu(gate_in) * up_in


def mm(left, right):
    return jnp.dot(left, right, preferred_element_type=F32)


def mm_rows(left, right):
    return lax.dot_general(left, right, (((0,), (0,)), ((), ())), preferred_element_type=F32)


def mm_cols(left, right):
    return lax.dot_general(left, right, (((1,), (1,)), ((), ())), preferred_element_type=F32)


def slot_places(route_rows, pair_order, capacity):
    pair_expert = route_rows.reshape(-1)
    earlier = pair_order[None, :] < pair_order[:, None]
    same_expert = pair_expert[None, :] == pair_expert[:, None]
    places = jnp.sum((earlier & same_expert).astype(jnp.int32), axis=1)
    slot_index = jnp.where(places < capacity, pair_expert * capacity + places, -1)
    return slot_index.reshape(route_rows.shape)


def params(collective_id):
    return pltpu.CompilerParams(
        collective_id=collective_id, has_side_effects=True, vmem_limit_bytes=48 << 20
    )


def remote(src, dst, send_sem, recv_sem, device):
    return pltpu.make_async_remote_copy(
        src_ref=src,
        dst_ref=dst,
        send_sem=send_sem,
        recv_sem=recv_sem,
        device_id=device,
        device_id_type=MESH,
    )


def greet(devices):
    barrier = pltpu.get_barrier_semaphore()
    for device in devices:
        pl.semaphore_signal(barrier, inc=1, device_id=device, device_id_type=MESH)
    pl.semaphore_wait(barrier, len(devices))


def places(n_dp, n_ex):
    z = lax.axis_index("dp")
    e = lax.axis_index("expert")
    chips = n_ex // 2
    c, k = e // 2, lax.rem(e, 2)
    sibling = (z, e + 1 - 2 * k)
    same_core = [(z, lax.rem(c + i, chips) * 2 + k) for i in range(1, chips)]
    column = [(lax.rem(z + i, n_dp), e) for i in range(1, n_dp)]
    return z, e, c, k, sibling, same_core, column


def plane_gather(block, n_dp, n_ex, collective_id):
    chips = n_ex // 2

    def kernel(x_ref, o_ref, send, recv, sib_send, sib_recv, local):
        z, e, c, k, sibling, same_core, _ = places(n_dp, n_ex)
        greet(same_core + [sibling])
        far = []
        for i in range(1, chips):
            copy = remote(x_ref, o_ref.at[e], send.at[i], recv.at[i], same_core[i - 1])
            copy.start()
            far.append(copy)
        near = [remote(x_ref, o_ref.at[e], sib_send.at[0], sib_recv.at[0], sibling)]
        near[0].start()
        own = pltpu.make_async_copy(x_ref, o_ref.at[e], local)
        own.start()
        for i in range(1, chips):
            source = lax.rem(c + chips - i, chips) * 2 + k
            far[i - 1].wait_recv()
            copy = remote(
                o_ref.at[source], o_ref.at[source], sib_send.at[i], sib_recv.at[i], sibling
            )
            copy.start()
            near.append(copy)
        own.wait()
        for copy in far:
            copy.wait_send()
        for copy in near:
            copy.wait()

    return pl.pallas_call(
        kernel,
        out_shape=jax.ShapeDtypeStruct((n_ex,) + block.shape, block.dtype),
        in_specs=[ANY],
        out_specs=ANY,
        scratch_shapes=[pltpu.SemaphoreType.DMA((chips,))] * 4 + [pltpu.SemaphoreType.DMA],
        compiler_params=params(collective_id),
    )(block)


def wait_recv(region, sem, device):
    remote(region, region, sem, sem, device).wait_recv()


def column_sum(array, n_dp, n_ex, inner, collective_id):
    shape = array.shape[1:]

    def kernel(x_ref, o_ref, buf, send, recv):
        z, e, c, k, sibling, same_core, _ = places(n_dp, n_ex)
        group = column_group(z, e, inner)
        greet(group[1:])
        copies = []
        for i in range(1, inner):
            copy = remote(x_ref.at[i], buf.at[i], send.at[i], recv.at[i], group[inner - i])
            copy.start()
            copies.append(copy)
        o_ref[...] = x_ref[0].astype(F32)
        for i in range(1, inner):
            copies[i - 1].wait_recv()
            o_ref[...] += buf[i].astype(F32)
        for copy in copies:
            copy.wait_send()

    return pl.pallas_call(
        kernel,
        out_shape=jax.ShapeDtypeStruct(shape, F32),
        in_specs=[VMEM],
        out_specs=VMEM,
        scratch_shapes=[pltpu.VMEM((inner,) + shape, BF)] + [pltpu.SemaphoreType.DMA((inner,))] * 2,
        compiler_params=params(collective_id),
    )(array)


def column_group(z, e, inner):
    start = z // inner * inner
    return [(start + lax.rem(z - start + i, inner), e) for i in range(inner)]


def first_exchange(tok, heads_w, pack, slot, cot, n_dp, n_ex, inner, collective_id):
    chips = n_ex // 2

    def kernel(
        tok_ref, wa_ref, pk_ref, sl_ref, co_ref, tok_out, wa_out, pk_out, sl_out, co_out,
        t_send, t_recv, ts_send, ts_recv, a_send, a_recv, az_send, az_recv,
        p_send, p_recv, pf_send, pf_recv, ps_send, ps_recv, s_send, s_recv, c_send, c_recv, local,
    ):
        z, e, c, k, sibling, same_core, column = places(n_dp, n_ex)
        plane = [(z, lax.rem(e + i, n_ex)) for i in range(1, n_ex)]
        group = column_group(z, e, inner)
        greet(plane + column)
        wa_far, pk_col, tok_far, near = [], [], [], []
        for i in range(1, n_ex):
            copy = remote(
                wa_ref.at[lax.rem(e + i, n_ex)], wa_out.at[z, e],
                a_send.at[i], a_recv.at[i], plane[i - 1],
            )
            copy.start()
            wa_far.append(copy)
        for i in range(1, n_dp):
            copy = remote(pk_ref, pk_out.at[z, e], p_send.at[i], p_recv.at[i], column[i - 1])
            copy.start()
            pk_col.append(copy)
        for i in range(1, inner):
            copy = remote(sl_ref, sl_out.at[i], s_send.at[i], s_recv.at[i], group[i])
            copy.start()
            near.append(copy)
        for i in range(1, chips):
            copy = remote(tok_ref, tok_out.at[e], t_send.at[i], t_recv.at[i], same_core[i - 1])
            copy.start()
            tok_far.append(copy)
        copy = remote(tok_ref, tok_out.at[e], ts_send.at[0], ts_recv.at[0], sibling)
        copy.start()
        near.append(copy)
        own = [
            pltpu.make_async_copy(wa_ref.at[e], wa_out.at[z, e], local.at[0]),
            pltpu.make_async_copy(pk_ref, pk_out.at[z, e], local.at[1]),
            pltpu.make_async_copy(tok_ref, tok_out.at[e], local.at[2]),
            pltpu.make_async_copy(sl_ref, sl_out.at[0], local.at[3]),
            pltpu.make_async_copy(co_ref, co_out.at[0], local.at[4]),
        ]
        for copy in own:
            copy.start()
        for copy in own:
            copy.wait()
        for copy in wa_far:
            copy.wait_recv()
        wa_col = []
        for i in range(1, n_dp):
            copy = remote(
                wa_out.at[z], wa_out.at[z], az_send.at[i], az_recv.at[i], column[i - 1]
            )
            copy.start()
            wa_col.append(copy)
        for i in range(1, inner):
            copy = remote(co_ref, co_out.at[i], c_send.at[i], c_recv.at[i], group[i])
            copy.start()
            near.append(copy)
        for copy in pk_col:
            copy.wait_recv()
        pk_far = []
        for i in range(1, chips):
            copy = remote(
                pk_out.at[:, e], pk_out.at[:, e], pf_send.at[i], pf_recv.at[i], same_core[i - 1]
            )
            copy.start()
            pk_far.append(copy)
        copy = remote(pk_out.at[:, e], pk_out.at[:, e], ps_send.at[0], ps_recv.at[0], sibling)
        copy.start()
        near.append(copy)
        for i in range(1, chips):
            source = lax.rem(c + chips - i, chips) * 2 + k
            tok_far[i - 1].wait_recv()
            copy = remote(
                tok_out.at[source], tok_out.at[source], ts_send.at[i], ts_recv.at[i], sibling
            )
            copy.start()
            near.append(copy)
            pk_far[i - 1].wait_recv()
            copy = remote(
                pk_out.at[:, source], pk_out.at[:, source], ps_send.at[i], ps_recv.at[i], sibling
            )
            copy.start()
            near.append(copy)
        for copy in near + wa_col:
            copy.wait()
        for copy in wa_far + pk_col + tok_far + pk_far:
            copy.wait_send()

    dma = pltpu.SemaphoreType.DMA
    return pl.pallas_call(
        kernel,
        out_shape=[
            jax.ShapeDtypeStruct((n_ex,) + tok.shape, tok.dtype),
            jax.ShapeDtypeStruct((n_dp,) + heads_w.shape, heads_w.dtype),
            jax.ShapeDtypeStruct((n_dp, n_ex) + pack.shape, pack.dtype),
            jax.ShapeDtypeStruct((inner,) + slot.shape, slot.dtype),
            jax.ShapeDtypeStruct((inner,) + cot.shape, cot.dtype),
        ],
        in_specs=[ANY] * 5,
        out_specs=[ANY] * 5,
        scratch_shapes=[dma((chips,))] * 4
        + [dma((n_ex,))] * 2
        + [dma((n_dp,))] * 4
        + [dma((chips,))] * 4
        + [dma((inner,))] * 4
        + [dma((5,))],
        compiler_params=params(collective_id),
    )(tok, heads_w, pack, slot, cot)


def forward_exchange(parts, tok, gain, slots, experts, shared, n_dp, n_ex, inner, collective_id):
    chips = n_ex // 2
    hh = n_ex // 2
    local_experts = experts[0].shape[0]
    rows, width = tok.shape

    def kernel(x_ref, tok_ref, gain_ref, slot_ref, *refs):
        e_in, s_in = refs[:3], refs[3:6]
        res_ref, xcol_ref, slot_out = refs[6:9]
        w_out, s_out = refs[9:12], refs[12:15]
        from_sib, out_buf, from_far, xbuf = refs[15:19]
        (
            near_s, near_r, far_s, far_r, x_s, x_r, g_s, g_r, we_s, we_r, wf_s, wf_r,
            sh_s, sh_r, sp_s, sp_r, sf_s, sf_r, local,
        ) = refs[19:]
        z, e, c, k, sibling, same_core, column = places(n_dp, n_ex)
        group = column_group(z, e, inner)
        sib_column = [(device[0], sibling[1]) for device in column]
        greet(same_core + [sibling] + column + sib_column)
        my_l = lax.rem(z, inner)

        def expert_sends(m, start):
            for i in list(range(1, n_dp)) + [0]:
                to = lax.rem(z + i, n_dp)
                expert = lax.rem(to, inner)

                def go(i=i, to=to, expert=expert):
                    for h in range(2):
                        src = e_in[m].at[lax.rem(expert, local_experts), pl.ds(h * hh, hh)]
                        dst = w_out[m].at[pl.ds(h * hh, hh), z]

                        def far(src=src, dst=dst, h=h):
                            copy = remote(
                                src, dst, we_s.at[m, i, h], we_r.at[m, z], (to, 2 * c + h)
                            )
                            if start:
                                copy.start()
                            else:
                                copy.wait_send()

                        if i:
                            far()
                        else:
                            pl.when(k != h)(far)
                            if start:

                                @pl.when(k == h)
                                def _(src=src, dst=dst):
                                    pltpu.make_async_copy(src, dst, we_r.at[m, z]).start()

                pl.when(expert // local_experts == k)(go)

        def expert_arrivals(m):
            for i in range(n_dp):
                d = lax.rem(z + n_dp - i, n_dp)
                region = w_out[m].at[pl.ds(k * hh, hh), d]
                if i:
                    wait_recv(region, we_r.at[m, d], sibling)
                else:
                    from_here = my_l // local_experts == k

                    @pl.when(from_here)
                    def _(region=region, d=d):
                        src = e_in[m].at[lax.rem(my_l, local_experts), pl.ds(k * hh, hh)]
                        pltpu.make_async_copy(src, region, we_r.at[m, d]).wait()

                    @pl.when(jnp.logical_not(from_here))
                    def _(region=region, d=d):
                        wait_recv(region, we_r.at[m, d], sibling)

                remote(region, region, wf_s.at[m, i], wf_r.at[m, i], sibling).start()

        near = []
        for i in list(range(1, chips)) + [0]:
            chip = lax.rem(c + i, chips)
            copy = remote(
                x_ref.at[chip * 2 + 1 - k], from_sib.at[chip], near_s.at[i], near_r.at[i], sibling
            )
            copy.start()
            near.append(copy)
        shared_copies = []
        for i in range(1, n_dp):
            for m in range(3):
                copy = remote(
                    s_in[m].at[lax.rem(lax.rem(z + i, n_dp), inner)], s_out[m].at[e, z],
                    sh_s.at[m, i], sh_r.at[m, i], column[i - 1],
                )
                copy.start()
                shared_copies.append(copy)
        own = [
            pltpu.make_async_copy(s_in[m].at[my_l], s_out[m].at[e, z], local.at[m])
            for m in range(3)
        ]
        own.append(pltpu.make_async_copy(slot_ref.at[0], slot_out.at[0], local.at[3]))
        for copy in own:
            copy.start()
        expert_sends(0, True)
        expert_sends(1, True)
        far = []
        for i in range(1, chips):
            chip = lax.rem(c + i, chips)
            near[i - 1].wait_recv()
            out_buf[i] = (
                x_ref[chip * 2 + k].astype(F32) + from_sib[chip].astype(F32)
            ).astype(BF)
            copy = remote(out_buf.at[i], from_far.at[i], far_s.at[i], far_r.at[i], same_core[i - 1])
            copy.start()
            far.append(copy)
        slot_copies = []
        for i in range(1, chips):
            copy = remote(slot_ref.at[i], slot_out.at[i], g_s.at[i], g_r.at[i], same_core[i - 1])
            copy.start()
            slot_copies.append(copy)
        near[chips - 1].wait_recv()
        res_ref[...] = x_ref[e].astype(F32) + from_sib[c].astype(F32) + tok_ref[...].astype(F32)
        for i in range(1, chips):
            far[i - 1].wait_recv()
            res_ref[...] += from_far[i].astype(F32)
        residual = res_ref[...]
        scale = lax.rsqrt(jnp.mean(residual * residual, axis=-1, keepdims=True) + norm_eps)
        xbuf[...] = (residual * scale * gain_ref[...]).astype(BF)
        x_copies = []
        for i in range(1, inner):
            copy = remote(xbuf, xcol_ref.at[i], x_s.at[i], x_r.at[i], group[i])
            copy.start()
            x_copies.append(copy)
        x_own = pltpu.make_async_copy(xbuf, xcol_ref.at[0], local.at[4])
        x_own.start()
        expert_sends(2, True)
        for copy in own:
            copy.wait()
        for copy in shared_copies:
            copy.wait_recv()
        plane, to_sib = [], []
        for m in range(3):
            block = s_out[m].at[e]
            for i in range(1, chips):
                copy = remote(block, block, sp_s.at[m, i], sp_r.at[m, i], same_core[i - 1])
                copy.start()
                plane.append(copy)
            copy = remote(block, block, sf_s.at[m, 0], sf_r.at[m, 0], sibling)
            copy.start()
            to_sib.append(copy)
        for m in range(3):
            for i in range(1, chips):
                plane[m * (chips - 1) + i - 1].wait_recv()
                block = s_out[m].at[lax.rem(c + chips - i, chips) * 2 + k]
                copy = remote(block, block, sf_s.at[m, i], sf_r.at[m, i], sibling)
                copy.start()
                to_sib.append(copy)
        for m in range(3):
            expert_arrivals(m)
        for copy in x_copies + slot_copies + to_sib:
            copy.wait()
        x_own.wait()
        for copy in plane + shared_copies + near + far:
            copy.wait_send()
        for m in range(3):
            expert_sends(m, False)
            for i in range(n_dp):
                d = lax.rem(z + n_dp - i, n_dp)
                mine = w_out[m].at[pl.ds(k * hh, hh), d]
                remote(mine, mine, wf_s.at[m, i], wf_r.at[m, i], sibling).wait_send()
                region = w_out[m].at[pl.ds((1 - k) * hh, hh), d]
                wait_recv(region, wf_r.at[m, i], sibling)

    dma = pltpu.SemaphoreType.DMA
    r, ff = experts[0].shape[2:]
    ff_s = shared[0].shape[2]
    outs = pl.pallas_call(
        kernel,
        out_shape=[
            jax.ShapeDtypeStruct((rows, width), F32),
            jax.ShapeDtypeStruct((inner, rows, width), BF),
            jax.ShapeDtypeStruct(slots.shape, BF),
        ]
        + [jax.ShapeDtypeStruct((n_ex, n_dp, r, ff), BF)] * 3
        + [jax.ShapeDtypeStruct((n_ex, n_dp, r, ff_s), BF)] * 3,
        in_specs=[VMEM] * 3 + [ANY] * 7,
        out_specs=[VMEM] + [ANY] * 8,
        scratch_shapes=[pltpu.VMEM((chips, rows, width), BF)] * 3
        + [pltpu.VMEM((rows, width), BF)]
        + [dma((chips,))] * 4
        + [dma((inner,))] * 2
        + [dma((chips,))] * 2
        + [dma((3, n_dp, 2)), dma((3, n_dp)), dma((3, n_dp)), dma((3, n_dp))]
        + [dma((3, n_dp))] * 2
        + [dma((3, chips))] * 4
        + [dma((5,))],
        compiler_params=params(collective_id),
    )(parts, tok, gain, slots, *experts, *shared)
    return outs[0], outs[1], outs[2], outs[3:6], outs[6:9]


class ExpertsBack:
    @staticmethod
    def scratch(total, n_dp, inner):
        n_ex, _, r, ff = total.shape
        dma = pltpu.SemaphoreType.DMA
        return [
            pltpu.VMEM((n_ex // 2, n_dp, r, ff), BF),
            pltpu.VMEM((n_ex // 2, n_dp, r, ff), BF),
            dma((n_dp,)),
            dma((n_dp,)),
            dma((n_dp,)),
            dma((n_dp,)),
            dma((n_dp // inner, 2, 2)),
        ]

    @staticmethod
    def out(total, n_dp, inner):
        n_ex, _, r, ff = total.shape
        return jax.ShapeDtypeStruct((n_dp // inner, 2, n_ex, r, ff), BF)

    def __init__(self, total, out, scratch, n_dp, n_ex, inner):
        self.total, self.out, self.n_dp, self.inner = total, out, n_dp, inner
        self.own, self.sib, self.near_s, self.near_r, self.load, self.send, self.recv = scratch
        self.z, self.e, self.c, self.k, self.sibling, _, _ = places(n_dp, n_ex)
        self.hh = n_ex // 2

    def near(self, i):
        d = lax.rem(self.z + i, self.n_dp)
        return remote(
            self.total.at[pl.ds((1 - self.k) * self.hh, self.hh), d],
            self.sib.at[:, d], self.near_s.at[i], self.near_r.at[i], self.sibling,
        )

    def loads(self, i):
        d = lax.rem(self.z + i, self.n_dp)
        return pltpu.make_async_copy(
            self.total.at[pl.ds(self.k * self.hh, self.hh), d], self.own.at[:, d], self.load.at[i]
        )

    def order(self):
        return list(range(1, self.n_dp)) + [0]

    def begin(self):
        for i in self.order():
            self.near(i).start()
            self.loads(i).start()

    def route(self, i):
        d = lax.rem(self.z + i, self.n_dp)
        expert = lax.rem(self.z, self.inner)
        dst = self.out.at[
            self.z // self.inner, lax.rem(expert, 2), pl.ds(self.k * self.hh, self.hh)
        ]
        sem = self.recv.at[self.z // self.inner, lax.rem(expert, 2), self.k]
        return self.own.at[:, d], dst, sem, d, expert // 2

    def stay(self):
        src, dst, sem, _, _ = self.route(0)
        return pltpu.make_async_copy(src, dst, sem)

    def go(self, i):
        src, dst, sem, d, core = self.route(i)
        return remote(src, dst, self.send.at[i], sem, (d, 2 * self.c + core))

    def here(self):
        return lax.rem(self.z, self.inner) // 2 == self.k

    def middle(self):
        for i in self.order():
            d = lax.rem(self.z + i, self.n_dp)
            self.near(i).wait_recv()
            self.loads(i).wait()
            for j in range(self.hh):
                self.own[j, d] = (
                    self.own[j, d].astype(F32) + self.sib[j, d].astype(F32)
                ).astype(BF)
            if i:
                self.go(i).start()
            else:
                pl.when(self.here())(lambda: self.stay().start())
                pl.when(jnp.logical_not(self.here()))(lambda: self.go(0).start())

    def end(self):
        for i in self.order():
            self.near(i).wait_send()
            if i:
                self.go(i).wait_send()
            else:
                pl.when(jnp.logical_not(self.here()))(lambda: self.go(0).wait_send())
        for o in range(self.n_dp // self.inner):
            for j in range(2):
                for h in range(2):
                    region = self.out.at[o, j, pl.ds(h * self.hh, self.hh)]
                    source = o * self.inner + 2 * self.k + j
                    here = jnp.logical_and(source == self.z, self.k == h)

                    @pl.when(here)
                    def _(region=region, o=o, j=j, h=h):
                        d = self.z
                        pltpu.make_async_copy(
                            self.own.at[:, d], region, self.recv.at[o, j, h]
                        ).wait()

                    @pl.when(jnp.logical_not(here))
                    def _(region=region, o=o, j=j, h=h):
                        wait_recv(region, self.recv.at[o, j, h], self.sibling)


def gather_and_sum(block, blocks, n_dp, n_ex, inner, collective_id):
    chips = n_ex // 2

    def kernel(x_ref, y_ref, o_ref, sum_ref, buf, send, recv, sib_send, sib_recv, c_send, c_recv, local):
        z, e, c, k, sibling, same_core, _ = places(n_dp, n_ex)
        group = column_group(z, e, inner)
        greet(same_core + [sibling] + group[1:])
        far, column = [], []
        for i in range(1, chips):
            copy = remote(x_ref, o_ref.at[e], send.at[i], recv.at[i], same_core[i - 1])
            copy.start()
            far.append(copy)
        for i in range(1, inner):
            copy = remote(y_ref.at[i], buf.at[i], c_send.at[i], c_recv.at[i], group[inner - i])
            copy.start()
            column.append(copy)
        near = [remote(x_ref, o_ref.at[e], sib_send.at[0], sib_recv.at[0], sibling)]
        near[0].start()
        own = pltpu.make_async_copy(x_ref, o_ref.at[e], local)
        own.start()
        for i in range(1, chips):
            source = lax.rem(c + chips - i, chips) * 2 + k
            far[i - 1].wait_recv()
            copy = remote(
                o_ref.at[source], o_ref.at[source], sib_send.at[i], sib_recv.at[i], sibling
            )
            copy.start()
            near.append(copy)
        sum_ref[...] = y_ref[0].astype(F32)
        for i in range(1, inner):
            column[i - 1].wait_recv()
            sum_ref[...] += buf[i].astype(F32)
        own.wait()
        for copy in far + column:
            copy.wait_send()
        for copy in near:
            copy.wait()

    dma = pltpu.SemaphoreType.DMA
    return pl.pallas_call(
        kernel,
        out_shape=[
            jax.ShapeDtypeStruct((n_ex,) + block.shape, block.dtype),
            jax.ShapeDtypeStruct(blocks.shape[1:], F32),
        ],
        in_specs=[ANY, VMEM],
        out_specs=[ANY, VMEM],
        scratch_shapes=[pltpu.VMEM(blocks.shape, BF)]
        + [dma((chips,))] * 4
        + [dma((inner,))] * 2
        + [dma],
        compiler_params=params(collective_id),
    )(block, blocks)


def plane_sum(arrays, totals, n_dp, n_ex, inner, collective_id):
    chips = n_ex // 2
    count, extra = len(arrays), len(totals)

    def kernel(*refs):
        x_refs, t_refs = refs[:count], refs[count : count + extra]
        refs = refs[count + extra :]
        o_refs, back_refs = refs[:count], refs[count : count + extra]
        refs = refs[count + extra :]
        bufs, sems, rest = refs[: 3 * count], refs[3 * count : 7 * count], refs[7 * count :]
        z, e, c, k, sibling, same_core, column = places(n_dp, n_ex)
        greet(
            same_core + [sibling] + (column + [(d[0], sibling[1]) for d in column] if extra else [])
        )
        backs = [
            ExpertsBack(t_refs[m], back_refs[m], rest[7 * m : 7 * m + 7], n_dp, n_ex, inner)
            for m in range(extra)
        ]
        near, far = {}, {}
        for i in list(range(1, chips)) + [0]:
            chip = lax.rem(c + i, chips)
            for j in range(count):
                near[i, j] = remote(
                    x_refs[j].at[chip * 2 + 1 - k],
                    bufs[3 * j].at[chip],
                    sems[4 * j].at[i],
                    sems[4 * j + 1].at[i],
                    sibling,
                )
                near[i, j].start()
        for back in backs:
            back.begin()
        for i in range(1, chips):
            chip = lax.rem(c + i, chips)
            for j in range(count):
                from_sib, out_buf, from_far = bufs[3 * j : 3 * j + 3]
                near[i, j].wait_recv()
                out_buf[i] = (
                    x_refs[j][chip * 2 + k].astype(F32) + from_sib[chip].astype(F32)
                ).astype(BF)
                far[i, j] = remote(
                    out_buf.at[i],
                    from_far.at[i],
                    sems[4 * j + 2].at[i],
                    sems[4 * j + 3].at[i],
                    same_core[i - 1],
                )
                far[i, j].start()
        for back in backs:
            back.middle()
        for j in range(count):
            near[0, j].wait_recv()
            o_refs[j][...] = x_refs[j][e].astype(F32) + bufs[3 * j][c].astype(F32)
        for i in range(1, chips):
            for j in range(count):
                far[i, j].wait_recv()
                o_refs[j][...] += bufs[3 * j + 2][i].astype(F32)
        for copy in list(near.values()) + list(far.values()):
            copy.wait_send()
        for back in backs:
            back.end()

    scratch = []
    for array in arrays:
        scratch += [pltpu.VMEM((chips,) + array.shape[1:], BF)] * 3
    scratch += [pltpu.SemaphoreType.DMA((chips,))] * (4 * count)
    for total in totals:
        scratch += ExpertsBack.scratch(total, n_dp, inner)
    outs = pl.pallas_call(
        kernel,
        out_shape=[jax.ShapeDtypeStruct(array.shape[1:], F32) for array in arrays]
        + [ExpertsBack.out(total, n_dp, inner) for total in totals],
        in_specs=[VMEM] * count + [ANY] * extra,
        out_specs=[VMEM] * count + [ANY] * extra,
        scratch_shapes=scratch,
        compiler_params=params(collective_id),
    )(*arrays, *totals)
    return outs[:count], outs[count:]


def last_exchange(arrays, totals, n_dp, n_ex, inner, collective_id):
    count, extra = len(arrays), len(totals)

    def kernel(*refs):
        x_refs, t_refs = refs[:count], refs[count : count + extra]
        refs = refs[count + extra :]
        o_refs, back_refs = refs[:count], refs[count : count + extra]
        refs = refs[count + extra :]
        sems, local, rest = refs[: 2 * count], refs[2 * count], refs[2 * count + 1 :]
        z, e, c, k, sibling, same_core, column = places(n_dp, n_ex)
        greet([sibling] + column + [(d[0], sibling[1]) for d in column])
        backs = [
            ExpertsBack(t_refs[m], back_refs[m], rest[7 * m : 7 * m + 7], n_dp, n_ex, inner)
            for m in range(extra)
        ]
        for back in backs:
            back.begin()
        copies = []
        for j in range(count):
            for i in range(1, n_dp):
                copy = remote(
                    x_refs[j].at[lax.rem(z + i, n_dp)], o_refs[j].at[z],
                    sems[2 * j].at[i], sems[2 * j + 1].at[i], column[i - 1],
                )
                copy.start()
                copies.append(copy)
            copy = pltpu.make_async_copy(x_refs[j].at[z], o_refs[j].at[z], local.at[j])
            copy.start()
            copies.append(copy)
        for back in backs:
            back.middle()
        for copy in copies:
            copy.wait()
        for back in backs:
            back.end()

    dma = pltpu.SemaphoreType.DMA
    scratch = [dma((n_dp,))] * (2 * count) + [dma((count,))]
    for total in totals:
        scratch += ExpertsBack.scratch(total, n_dp, inner)
    outs = pl.pallas_call(
        kernel,
        out_shape=[jax.ShapeDtypeStruct(array.shape, array.dtype) for array in arrays]
        + [ExpertsBack.out(total, n_dp, inner) for total in totals],
        in_specs=[ANY] * (count + extra),
        out_specs=[ANY] * (count + extra),
        scratch_shapes=scratch,
        compiler_params=params(collective_id),
    )(*arrays, *totals)
    return outs[:count], outs[count:]


def shards(
    tokens,
    cotangent,
    lengths,
    routes,
    place_order,
    attn_gain,
    w_query,
    w_latent,
    latent_gain,
    w_expand,
    w_out,
    ffn_gain,
    w_router,
    shared_gate,
    shared_up,
    shared_down,
    expert_gate,
    expert_up,
    expert_down,
):
    rows, width = tokens.shape
    n_dp = lax.axis_size("dp")
    n_ex = lax.axis_size("expert")
    chips = n_ex // 2
    z = lax.axis_index("dp")
    e = lax.axis_index("expert")
    chip = e // 2
    n_experts = w_router.shape[1]
    top_k = routes.shape[1]
    capacity = (rows * top_k * 5 + 4 * n_experts - 1) // (4 * n_experts)
    cap = (capacity + 15) // 16 * 16
    seq = rows * n_ex
    r = w_query.shape[0]
    rl = w_expand.shape[0]
    hp = H // n_ex
    parts = DV // r
    heads = [
        (d * n_ex + (j // parts) * parts) * r // DV
        for j in range(n_ex)
        for d in range(j % parts * hp, j % parts * hp + hp)
    ]
    heads_back = [heads.index(h) for h in range(H)]
    inner = n_experts // chips
    my_local = lax.rem(z, inner)
    part_groups = [[i * parts + m for m in range(parts)] for i in range(n_ex // parts)]
    ff_e = expert_gate.shape[2]
    ff_s = shared_gate.shape[1] // inner
    lat = KVR + DR
    head_cols = hp * (DH + DR)
    kv_cols = hp * (DH + DV)

    def to_owner_order(values):
        cut = values.reshape(values.shape[0], n_dp, n_ex, r)
        return cut.transpose(0, 2, 1, 3).reshape(values.shape)

    def from_owner_order(values):
        cut = values.reshape(values.shape[0], n_ex, n_dp, r)
        return cut.transpose(0, 2, 1, 3).reshape(values.shape)

    def pick(values, index, axis=0):
        return lax.dynamic_index_in_dim(values, index, axis, keepdims=False)

    wq_send = jnp.take(w_query.reshape(r, H, DH + DR), jnp.array(heads), axis=1)
    wq_send = wq_send.reshape(r, n_ex, head_cols).transpose(1, 0, 2)
    we_send = jnp.take(w_expand.reshape(rl, H, DH + DV), jnp.array(heads), axis=1)
    we_send = we_send.reshape(rl, n_ex, kv_cols).transpose(1, 0, 2)
    we_send = we_send.reshape(n_ex, r, rl * kv_cols // r)
    wa_send = jnp.concatenate([wq_send, we_send], axis=-1)
    pack_cols = (lat + n_experts + 3 + 127) // 128 * 128
    pack = jnp.concatenate(
        [
            w_latent,
            w_router,
            attn_gain[:, None],
            ffn_gain[:, None],
            jnp.pad(latent_gain, (0, r - rl))[:, None],
            jnp.zeros((r, pack_cols - lat - n_experts - 3), BF),
        ],
        axis=1,
    )
    slot_own = jnp.pad(
        slot_places(routes, place_order[0], capacity), ((0, 0), (0, 128 - top_k))
    )
    cot_owner = to_owner_order(cotangent)
    tok_all, wa_all, pk_all, slot_col, cot_col = first_exchange(
        tokens, wa_send, pack, slot_own, cot_owner, n_dp, n_ex, inner, 1
    )
    wq = wa_all[..., :head_cols].reshape(width, head_cols)
    wexp = wa_all[..., head_cols:].reshape(KVR, kv_cols)
    pk_flat = pk_all.reshape(width, pack_cols)
    w_lat = pk_flat[:, :lat]
    gain_one = pk_flat[:, lat + n_experts].astype(F32)
    gain_two = pk_all[..., lat + n_experts + 1].transpose(1, 0, 2).reshape(width).astype(F32)
    router = pk_all[..., lat : lat + n_experts].transpose(1, 0, 2, 3).reshape(width, n_experts)
    gain_lat = (
        pk_all[..., lat + n_experts + 2].reshape(n_dp * n_ex, r)[:, :rl].reshape(KVR).astype(F32)
    )
    wo_send, _ = lax.optimization_barrier((to_owner_order(w_out), pk_all))
    wo_col = lax.all_gather(wo_send, "dp", axis=0, tiled=False)
    wo_rows = lax.all_to_all(
        wo_col.reshape(parts, hp, r, width),
        "expert",
        0,
        0,
        axis_index_groups=part_groups,
        tiled=True,
    )
    wo_rows = wo_rows.transpose(1, 0, 2, 3).reshape(hp * DV, width)

    cot_col = cot_col.reshape(inner * rows, width)
    slots_all = n_experts * capacity
    slot_ids = slot_col[..., :top_k]
    slot_ids = jnp.where(
        slot_ids >= 0, slot_ids + (jnp.arange(inner) * slots_all)[:, None, None], -1
    ).reshape(inner * rows, top_k)
    place = jnp.arange(cap)
    far_experts = [lax.rem(chip + m, chips) * inner + my_local for m in range(chips)]
    wanted = (
        jnp.stack(far_experts)[:, None, None] * capacity
        + (jnp.arange(inner) * slots_all)[None, :, None]
        + place[None, None, :]
    )
    wanted = jnp.where(place[None, None, :] < capacity, wanted, -2).reshape(-1)
    n_slots = wanted.shape[0]
    per_far = n_slots // chips
    hot = sum((wanted[:, None] == slot_ids[None, :, j]).astype(BF) for j in range(top_k))
    hot_t = sum((slot_ids[:, j][:, None] == wanted[None, :]).astype(BF) for j in range(top_k))

    def between(values, way):
        cut = values.reshape(chips, per_far, -1)
        got = [cut[0]]
        for m in range(1, chips):
            perm = [(i, (i + 2 * m * way) % n_ex) for i in range(n_ex)]
            got.append(lax.ppermute(cut[m], "expert", perm))
        return jnp.concatenate(got, axis=0)

    grad_send = mm(hot, cot_col).astype(BF).reshape(chips, per_far, width)

    tok_plane = tok_all.reshape(seq, width)
    hidden_one = rms_norm(tok_plane.astype(F32), gain_one).astype(BF)
    positions = jnp.arange(seq)
    cos_table, sine_table = rope_tables(positions)
    query_raw = mm(hidden_one, wq).reshape(seq, hp, DH + DR)

    def make_queries(query_in):
        return jnp.concatenate(
            [
                query_in[..., :DH],
                rotate(query_in[..., DH:], cos_table[:, None, :], sine_table[:, None, :]),
            ],
            axis=-1,
        )

    query_rot, query_back = jax.vjp(make_queries, query_raw)
    queries = query_rot.astype(BF)
    latent_raw = mm(hidden_one, w_lat)
    latent_low = rms_norm(latent_raw[:, :KVR], gain_lat).astype(BF)
    rope_low = rotate(latent_raw[:, KVR:], cos_table, sine_table).astype(BF)
    expanded = mm(latent_low, wexp).astype(BF).reshape(seq, hp, DH + DV)
    score_scale = (DH + DR) ** (-0.5)
    allowed = (positions[None, :] <= positions[:, None]) & (positions[None, :] < lengths[0])
    attn_probs, probs_low, keys, attended = [], [], [], []
    for h in range(hp):
        key = jnp.concatenate([expanded[:, h, :DH], rope_low], axis=1)
        scores = jnp.where(allowed, mm_cols(queries[:, h], key) * score_scale, masked_score)
        top = jnp.max(scores, axis=-1, keepdims=True)
        exp_scores = jnp.exp(scores - top)
        probs = exp_scores / jnp.sum(exp_scores, axis=-1, keepdims=True)
        low = probs.astype(BF)
        attn_probs.append(probs)
        probs_low.append(low)
        keys.append(key)
        attended.append(mm(low, expanded[:, h, DH:]).astype(BF))
    attended = jnp.concatenate(attended, axis=1)
    out_part = mm(attended, wo_rows).astype(BF)
    residual, x_col, grad_in, (wg, wu, wd), (sgate, sup, sdown) = forward_exchange(
        out_part.reshape(n_ex, rows, width),
        to_owner_order(tokens),
        gain_two[None],
        grad_send,
        [w.reshape(-1, n_ex, r, ff_e) for w in (expert_gate, expert_up, expert_down)],
        [w.reshape(r, inner, ff_s).transpose(1, 0, 2) for w in (shared_gate, shared_up, shared_down)],
        n_dp,
        n_ex,
        inner,
        2,
    )
    wg, wu, wd = (w.reshape(width, ff_e) for w in (wg, wu, wd))
    sgate, sup, sdown = (w.reshape(width, ff_s) for w in (sgate, sup, sdown))
    hidden_two = x_col[0]
    x_col = x_col.reshape(inner * rows, width)
    grad_in = grad_in.reshape(n_slots, width)

    x_in = between(mm(hot, x_col).astype(BF), 1)

    def probs_of(logits):
        top = jnp.max(logits, axis=-1, keepdims=True)
        exp_logits = jnp.exp(logits - top)
        return exp_logits / jnp.sum(exp_logits, axis=-1, keepdims=True)

    shared_a = mm(x_col, sgate)
    shared_b = mm(x_col, sup)
    shared_hidden, shared_back = jax.vjp(swiglu, shared_a, shared_b)
    shared_hidden = shared_hidden.astype(BF)
    shared_out = mm_cols(shared_hidden, sdown)
    grad_sa, grad_sb = (v.astype(BF) for v in shared_back(mm(cot_col, sdown)))
    shared_grads = [
        mm_rows(x_col, grad_sa).astype(BF),
        mm_rows(x_col, grad_sb).astype(BF),
        mm_rows(cot_col, shared_hidden).astype(BF),
    ]
    shared_sums = [
        lax.psum_scatter(
            grad.reshape(n_ex, n_dp, r, ff_s), "expert", scatter_dimension=0, tiled=True
        ).reshape(n_dp, r, ff_s)
        for grad in shared_grads
    ]
    shared_dx = mm_cols(grad_sa, sgate) + mm_cols(grad_sb, sup)

    slot_probs = probs_of(mm(x_in, router))
    slot_gate = jnp.sum(
        jnp.where(jnp.arange(n_experts)[None, :] == far_experts[0], slot_probs, 0.0),
        axis=1,
        keepdims=True,
    )
    expert_a = mm(x_in, wg)
    expert_b = mm(x_in, wu)
    expert_hidden, expert_back = jax.vjp(swiglu, expert_a, expert_b)
    expert_hidden = expert_hidden.astype(BF)
    rows_back = between(mm_cols(expert_hidden, wd).astype(BF), -1)
    slot_grad = (slot_gate * grad_in.astype(F32)).astype(BF)
    grad_ea, grad_eb = (v.astype(BF) for v in expert_back(mm(slot_grad, wd)))
    dx_back = between((mm_cols(grad_ea, wg) + mm_cols(grad_eb, wu)).astype(BF), -1)
    expert_totals = [
        mm_rows(left, right).astype(BF).reshape(n_ex, n_dp, r, ff_e)
        for left, right in ((x_in, grad_ea), (x_in, grad_eb), (slot_grad, expert_hidden))
    ]

    col_probs = probs_of(mm(x_col, router))
    expert_axis = jnp.arange(n_experts)[None, :]
    gates = [
        jnp.sum(jnp.where(expert_axis == expert, col_probs, 0.0), axis=1, keepdims=True)
        for expert in far_experts
    ]
    gate_hot = jnp.concatenate(
        [hot_t[:, m * per_far : (m + 1) * per_far] * gates[m].astype(BF) for m in range(chips)],
        axis=1,
    )
    out_col = (mm(gate_hot, rows_back) + shared_out).astype(BF)
    dots = mm_cols(cot_col, rows_back) * hot_t.astype(F32)
    dots = jnp.sum(dots.reshape(inner * rows, chips, per_far), axis=-1)
    grad_probs_col = sum(
        jnp.where(expert_axis == far_experts[m], dots[:, m : m + 1], 0.0) for m in range(chips)
    )
    dx_col = mm(hot_t, dx_back) + shared_dx
    dx_send = jnp.concatenate(
        [dx_col, grad_probs_col, jnp.zeros((inner * rows, 128 - n_experts), F32)], axis=1
    ).astype(BF)
    dx_sum = column_sum(dx_send.reshape(inner, rows, width + 128), n_dp, n_ex, inner, 3)
    router_probs = col_probs[:rows]
    grad_probs = dx_sum[:, width : width + n_experts]
    grad_logits = (
        router_probs * (grad_probs - jnp.sum(grad_probs * router_probs, axis=-1, keepdims=True))
    ).astype(BF)
    grad_router = mm_rows(hidden_two, grad_logits)
    grad_hidden_two = dx_sum[:, :width] + mm_cols(grad_logits, router)
    _, norm_two_back = jax.vjp(rms_norm, residual, gain_two)
    grad_resid_norm, grad_gain_two = norm_two_back(grad_hidden_two)
    grad_residual = cot_owner.astype(F32) + grad_resid_norm

    grad_attn, out_sum = gather_and_sum(
        grad_residual.astype(BF), out_col.reshape(inner, rows, width), n_dp, n_ex, inner, 4
    )
    out_tokens = from_owner_order((residual + out_sum).astype(BF))
    grad_attn = grad_attn.reshape(seq, width)
    grad_attended = mm_cols(grad_attn, wo_rows).astype(BF)
    grad_wout = mm_rows(attended, grad_attn).astype(BF)
    grad_rope = 0.0
    grad_queries, grad_expanded = [], []
    for h in range(hp):
        gat = grad_attended[:, h * DV : (h + 1) * DV]
        probs = attn_probs[h]
        dp = mm_cols(gat, expanded[:, h, DH:])
        grad_scores = probs * (dp - jnp.sum(dp * probs, axis=-1, keepdims=True))
        grad_raw = jnp.where(allowed, grad_scores * score_scale, 0.0).astype(BF)
        grad_queries.append(mm(grad_raw, keys[h]))
        grad_key = mm_rows(grad_raw, queries[:, h])
        grad_rope = grad_rope + grad_key[:, DH:]
        grad_expanded += [grad_key[:, :DH], mm_rows(probs_low[h], gat)]
    grad_expanded = jnp.concatenate(grad_expanded, axis=1).astype(BF)
    (grad_query_raw,) = query_back(jnp.stack(grad_queries, axis=1))
    grad_query_low = grad_query_raw.reshape(seq, head_cols).astype(BF)
    grad_latent_part = jnp.concatenate([mm_cols(grad_expanded, wexp), grad_rope], axis=1)
    grad_latent_part = jnp.pad(grad_latent_part, ((0, 0), (0, -lat % 128))).astype(BF)
    grad_query_part = mm_cols(grad_query_low, wq).astype(BF)
    (grad_query_sum, grad_latent_sum), (down_back,) = plane_sum(
        [grad_query_part.reshape(n_ex, rows, width), grad_latent_part.reshape(n_ex, rows, -1)],
        expert_totals[2:],
        n_dp,
        n_ex,
        inner,
        5,
    )
    own_start = e * rows
    latent_own = lax.dynamic_slice_in_dim(latent_raw, own_start, rows, 0)
    cos_own = lax.dynamic_slice_in_dim(cos_table, own_start, rows, 0)
    sine_own = lax.dynamic_slice_in_dim(sine_table, own_start, rows, 0)

    def make_latent(latent_in, gain_in):
        return (
            rms_norm(latent_in[:, :KVR], gain_in),
            rotate(latent_in[:, KVR:], cos_own, sine_own),
        )

    _, latent_back = jax.vjp(make_latent, latent_own, gain_lat)
    grad_latent_raw, grad_gain_lat = latent_back(
        (grad_latent_sum[:, :KVR], grad_latent_sum[:, KVR:lat])
    )
    grad_latent_low = grad_latent_raw.astype(BF)
    _, norm_one_back = jax.vjp(rms_norm, tokens.astype(F32), gain_one)
    grad_hidden_one = grad_query_sum + mm_cols(grad_latent_low, w_lat)
    grad_tokens_norm, grad_gain_one = norm_one_back(grad_hidden_one)
    grad_tokens = from_owner_order(grad_residual) + grad_tokens_norm

    wout_back = lax.all_to_all(
        grad_wout.reshape(hp, parts, r, width).transpose(1, 0, 2, 3),
        "expert",
        0,
        0,
        axis_index_groups=part_groups,
        tiled=True,
    ).reshape(n_dp, r, width)
    grad_wq = mm_rows(hidden_one, grad_query_low).astype(BF).reshape(n_dp, n_ex, r, head_cols)
    grad_we = mm_rows(latent_low, grad_expanded).astype(BF)
    grad_we = grad_we.reshape(n_dp, n_ex, r, rl * kv_cols // r)
    heads_grad = jnp.concatenate([grad_wq, grad_we], axis=-1)
    latent_plane = plane_gather(grad_latent_low, n_dp, n_ex, 6).reshape(seq, lat)
    grad_wlat = pick(mm_rows(hidden_one, latent_plane).reshape(n_dp, n_ex, r, lat), e, 1)

    def by_owner(values):
        return values.reshape(n_ex, n_dp, r, -1).transpose(1, 0, 2, 3)

    small = jnp.concatenate(
        [
            by_owner(grad_router),
            grad_gain_one.reshape(n_dp, n_ex, r, 1),
            by_owner(grad_gain_two),
            jnp.pad(grad_gain_lat.reshape(n_dp, n_ex, rl, 1), ((0, 0),) * 2 + ((0, r - rl), (0, 0))),
            jnp.zeros((n_dp, n_ex, r, pack_cols - lat - n_experts - 3), F32),
        ],
        axis=-1,
    ).transpose(1, 0, 2, 3)
    small = jnp.sum(lax.all_to_all(small, "expert", 0, 0, tiled=True), axis=0)
    pack_grad = jnp.concatenate([grad_wlat, small], axis=-1).astype(BF)
    (heads_got, wout_got, pack_got, *shared_got), (gate_back, up_back) = last_exchange(
        [heads_grad, wout_back, pack_grad] + shared_sums, expert_totals[:2], n_dp, n_ex, inner, 7
    )

    def added(values):
        return jnp.sum(values.astype(F32), axis=0)

    heads_sum = added(heads_got).astype(BF)
    heads_all = lax.all_to_all(heads_sum, "expert", 0, 0, tiled=True).astype(F32)
    sum_wq = heads_all[..., :head_cols].transpose(1, 0, 2).reshape(r, H, DH + DR)
    sum_wq = jnp.take(sum_wq, jnp.array(heads_back), axis=1).reshape(r, H * (DH + DR))
    sum_we = heads_all[..., head_cols:].reshape(n_ex, rl, kv_cols).transpose(1, 0, 2)
    sum_we = jnp.take(sum_we.reshape(rl, H, DH + DV), jnp.array(heads_back), axis=1)
    sum_we = sum_we.reshape(rl, H * (DH + DV))
    sum_wout = from_owner_order(added(wout_got))
    pack_sum = added(pack_got)
    sum_sgate, sum_sup, sum_sdown = (
        added(got.reshape(n_dp // inner, inner, r, ff_s)).transpose(1, 0, 2).reshape(r, -1)
        for got in shared_got
    )
    sum_egate, sum_eup, sum_edown = (
        added(back).reshape(-1, n_ex * r, ff_e) for back in (gate_back, up_back, down_back)
    )
    return (
        out_tokens,
        grad_tokens,
        pack_sum[:, lat + n_experts],
        sum_wq,
        pack_sum[:, :lat],
        pack_sum[:rl, lat + n_experts + 2],
        sum_we,
        sum_wout,
        pack_sum[:, lat + n_experts + 1],
        pack_sum[:, lat : lat + n_experts],
        sum_sgate,
        sum_sup,
        sum_sdown,
        sum_egate,
        sum_eup,
        sum_edown,
    )


def solution(mesh):
    both = ("dp", "expert")
    in_specs = (
        P(both, None),
        P(both, None),
        P("dp"),
        P(both, None),
        P(both, None),
        P(both),
        P(both, None),
        P(both, None),
        P(both),
        P(both, None),
        P(both, None),
        P(both),
        P(both, None),
        P(both, None),
        P(both, None),
        P(both, None),
        P("expert", "dp", None),
        P("expert", "dp", None),
        P("expert", "dp", None),
    )
    out_specs = (
        P(both, None),
        P(both, None),
        P(both),
        P(both, None),
        P(both, None),
        P(both),
        P(both, None),
        P(both, None),
        P(both),
        P(both, None),
        P(both, None),
        P(both, None),
        P(both, None),
        P("expert", "dp", None),
        P("expert", "dp", None),
        P("expert", "dp", None),
    )
    return jax.shard_map(shards, mesh=mesh, in_specs=in_specs, out_specs=out_specs, check_vma=False)
```

```python
import jax
import jax.numpy as jnp
from jax import lax
from jax.experimental import pallas as pl
from jax.experimental.pallas import tpu as pltpu
from jax.sharding import PartitionSpec as P

H = 16
DH = 128
DR = 64
DV = 128
KVR = 512

norm_eps = 1e-06
masked_score = -1e30
MESH = pl.DeviceIdType.MESH
ANY = pl.BlockSpec(memory_space=pl.ANY)
VMEM = pl.BlockSpec(memory_space=pltpu.VMEM)
BF = jnp.bfloat16
F32 = jnp.float32


def rms_norm(values, scale_gain):
    return (
        values
        * lax.rsqrt(jnp.mean(values * values, axis=-1, keepdims=True) + norm_eps)
        * scale_gain
    )


def rotate(values, cos_table, sine_table):
    half_dim = values.shape[-1] // 2
    first_half = values[..., :half_dim]
    second_half = values[..., half_dim:]
    return jnp.concatenate(
        [
            first_half * cos_table - second_half * sine_table,
            second_half * cos_table + first_half * sine_table,
        ],
        axis=-1,
    )


def rope_tables(positions):
    half_dim = DR // 2
    inv_freq = 10000.0 ** (-(jnp.arange(half_dim).astype(F32) * 2.0) / DR)
    angles = positions.astype(F32)[:, None] * inv_freq[None, :]
    return (jnp.cos(angles), jnp.sin(angles))


def swiglu(gate_in, up_in):
    return jax.nn.silu(gate_in) * up_in


def mm(left, right):
    return jnp.dot(left, right, preferred_element_type=F32)


def mm_rows(left, right):
    return lax.dot_general(left, right, (((0,), (0,)), ((), ())), preferred_element_type=F32)


def mm_cols(left, right):
    return lax.dot_general(left, right, (((1,), (1,)), ((), ())), preferred_element_type=F32)


def slot_places(route_rows, pair_order, capacity):
    pair_expert = route_rows.reshape(-1)
    earlier = pair_order[None, :] < pair_order[:, None]
    same_expert = pair_expert[None, :] == pair_expert[:, None]
    places = jnp.sum((earlier & same_expert).astype(jnp.int32), axis=1)
    slot_index = jnp.where(places < capacity, pair_expert * capacity + places, -1)
    return slot_index.reshape(route_rows.shape)


def params(collective_id):
    return pltpu.CompilerParams(
        collective_id=collective_id, has_side_effects=True, vmem_limit_bytes=48 << 20
    )


def remote(src, dst, send_sem, recv_sem, device):
    return pltpu.make_async_remote_copy(
        src_ref=src,
        dst_ref=dst,
        send_sem=send_sem,
        recv_sem=recv_sem,
        device_id=device,
        device_id_type=MESH,
    )


def greet(devices):
    barrier = pltpu.get_barrier_semaphore()
    for device in devices:
        pl.semaphore_signal(barrier, inc=1, device_id=device, device_id_type=MESH)
    pl.semaphore_wait(barrier, len(devices))


def places(n_dp, n_ex):
    z = lax.axis_index("dp")
    e = lax.axis_index("expert")
    chips = n_ex // 2
    c, k = e // 2, lax.rem(e, 2)
    sibling = (z, e + 1 - 2 * k)
    same_core = [(z, lax.rem(c + i, chips) * 2 + k) for i in range(1, chips)]
    column = [(lax.rem(z + i, n_dp), e) for i in range(1, n_dp)]
    return z, e, c, k, sibling, same_core, column


def plane_gather(block, n_dp, n_ex, collective_id):
    chips = n_ex // 2

    def kernel(x_ref, o_ref, send, recv, sib_send, sib_recv, local):
        z, e, c, k, sibling, same_core, _ = places(n_dp, n_ex)
        greet(same_core + [sibling])
        far = []
        for i in range(1, chips):
            copy = remote(x_ref, o_ref.at[e], send.at[i], recv.at[i], same_core[i - 1])
            copy.start()
            far.append(copy)
        near = [remote(x_ref, o_ref.at[e], sib_send.at[0], sib_recv.at[0], sibling)]
        near[0].start()
        own = pltpu.make_async_copy(x_ref, o_ref.at[e], local)
        own.start()
        for i in range(1, chips):
            source = lax.rem(c + chips - i, chips) * 2 + k
            far[i - 1].wait_recv()
            copy = remote(
                o_ref.at[source], o_ref.at[source], sib_send.at[i], sib_recv.at[i], sibling
            )
            copy.start()
            near.append(copy)
        own.wait()
        for copy in far:
            copy.wait_send()
        for copy in near:
            copy.wait()

    return pl.pallas_call(
        kernel,
        out_shape=jax.ShapeDtypeStruct((n_ex,) + block.shape, block.dtype),
        in_specs=[ANY],
        out_specs=ANY,
        scratch_shapes=[pltpu.SemaphoreType.DMA((chips,))] * 4 + [pltpu.SemaphoreType.DMA],
        compiler_params=params(collective_id),
    )(block)


def wait_recv(region, sem, device):
    remote(region, region, sem, sem, device).wait_recv()


def column_sum(array, n_dp, n_ex, inner, collective_id):
    shape = array.shape[1:]

    def kernel(x_ref, o_ref, buf, send, recv):
        z, e, c, k, sibling, same_core, _ = places(n_dp, n_ex)
        group = column_group(z, e, inner)
        greet(group[1:])
        copies = []
        for i in range(1, inner):
            to = lax.rem(z + i, inner)
            copy = remote(x_ref.at[to], buf.at[i], send.at[i], recv.at[i], group[i])
            copy.start()
            copies.append(copy)
        o_ref[...] = x_ref[lax.rem(z, inner)].astype(F32)
        for i in range(1, inner):
            copies[i - 1].wait_recv()
            o_ref[...] += buf[i].astype(F32)
        for copy in copies:
            copy.wait_send()

    return pl.pallas_call(
        kernel,
        out_shape=jax.ShapeDtypeStruct(shape, F32),
        in_specs=[VMEM],
        out_specs=VMEM,
        scratch_shapes=[pltpu.VMEM((inner,) + shape, BF)] + [pltpu.SemaphoreType.DMA((inner,))] * 2,
        compiler_params=params(collective_id),
    )(array)


def column_group(z, e, inner):
    start = z // inner * inner
    return [(start + lax.rem(z - start + i, inner), e) for i in range(inner)]


def first_exchange(tok, heads_w, pack, n_dp, n_ex, collective_id):
    chips = n_ex // 2

    def kernel(
        tok_ref, wa_ref, pk_ref, tok_out, wa_out, pk_out,
        t_send, t_recv, ts_send, ts_recv, a_send, a_recv, az_send, az_recv,
        p_send, p_recv, pf_send, pf_recv, ps_send, ps_recv, local,
    ):
        z, e, c, k, sibling, same_core, column = places(n_dp, n_ex)
        plane = [(z, lax.rem(e + i, n_ex)) for i in range(1, n_ex)]
        greet(plane + column)
        wa_far, pk_col, tok_far, near = [], [], [], []
        for i in range(1, n_ex):
            copy = remote(
                wa_ref.at[lax.rem(e + i, n_ex)], wa_out.at[z, e],
                a_send.at[i], a_recv.at[i], plane[i - 1],
            )
            copy.start()
            wa_far.append(copy)
        for i in range(1, n_dp):
            copy = remote(pk_ref, pk_out.at[z, e], p_send.at[i], p_recv.at[i], column[i - 1])
            copy.start()
            pk_col.append(copy)
        for i in range(1, chips):
            copy = remote(tok_ref, tok_out.at[e], t_send.at[i], t_recv.at[i], same_core[i - 1])
            copy.start()
            tok_far.append(copy)
        copy = remote(tok_ref, tok_out.at[e], ts_send.at[0], ts_recv.at[0], sibling)
        copy.start()
        near.append(copy)
        own = [
            pltpu.make_async_copy(wa_ref.at[e], wa_out.at[z, e], local.at[0]),
            pltpu.make_async_copy(pk_ref, pk_out.at[z, e], local.at[1]),
            pltpu.make_async_copy(tok_ref, tok_out.at[e], local.at[2]),
        ]
        for copy in own:
            copy.start()
        for copy in own:
            copy.wait()
        for copy in wa_far:
            copy.wait_recv()
        wa_col = []
        for i in range(1, n_dp):
            copy = remote(
                wa_out.at[z], wa_out.at[z], az_send.at[i], az_recv.at[i], column[i - 1]
            )
            copy.start()
            wa_col.append(copy)
        for copy in pk_col:
            copy.wait_recv()
        pk_far = []
        for i in range(1, chips):
            copy = remote(
                pk_out.at[:, e], pk_out.at[:, e], pf_send.at[i], pf_recv.at[i], same_core[i - 1]
            )
            copy.start()
            pk_far.append(copy)
        copy = remote(pk_out.at[:, e], pk_out.at[:, e], ps_send.at[0], ps_recv.at[0], sibling)
        copy.start()
        near.append(copy)
        for i in range(1, chips):
            source = lax.rem(c + chips - i, chips) * 2 + k
            tok_far[i - 1].wait_recv()
            copy = remote(
                tok_out.at[source], tok_out.at[source], ts_send.at[i], ts_recv.at[i], sibling
            )
            copy.start()
            near.append(copy)
            pk_far[i - 1].wait_recv()
            copy = remote(
                pk_out.at[:, source], pk_out.at[:, source], ps_send.at[i], ps_recv.at[i], sibling
            )
            copy.start()
            near.append(copy)
        for copy in near + wa_col:
            copy.wait()
        for copy in wa_far + pk_col + tok_far + pk_far:
            copy.wait_send()

    dma = pltpu.SemaphoreType.DMA
    return pl.pallas_call(
        kernel,
        out_shape=[
            jax.ShapeDtypeStruct((n_ex,) + tok.shape, tok.dtype),
            jax.ShapeDtypeStruct((n_dp,) + heads_w.shape, heads_w.dtype),
            jax.ShapeDtypeStruct((n_dp, n_ex) + pack.shape, pack.dtype),
        ],
        in_specs=[ANY] * 3,
        out_specs=[ANY] * 3,
        scratch_shapes=[dma((chips,))] * 4
        + [dma((n_ex,))] * 2
        + [dma((n_dp,))] * 4
        + [dma((chips,))] * 4
        + [dma((3,))],
        compiler_params=params(collective_id),
    )(tok, heads_w, pack)


class ExpertsIn:
    @staticmethod
    def scratch(n_dp):
        dma = pltpu.SemaphoreType.DMA
        return [dma((n_dp, 2)), dma((n_dp,)), dma((n_dp,)), dma((n_dp,))]

    @staticmethod
    def out(weight, n_dp, n_ex):
        return jax.ShapeDtypeStruct((n_ex, n_dp) + weight.shape[2:], BF)

    def __init__(self, weight, out, scratch, n_dp, n_ex, inner):
        self.weight, self.out, self.n_dp, self.inner = weight, out, n_dp, inner
        self.send, self.recv, self.sib_send, self.sib_recv = scratch
        self.z, self.e, self.c, self.k, self.sibling, _, _ = places(n_dp, n_ex)
        self.hh = n_ex // 2
        self.local = weight.shape[0]

    def sends(self, start):
        for i in list(range(1, self.n_dp)) + [0]:
            to = lax.rem(self.z + i, self.n_dp)
            expert = lax.rem(to, self.inner)

            def go(i=i, to=to, expert=expert):
                for h in range(2):
                    src = self.weight.at[lax.rem(expert, self.local), pl.ds(h * self.hh, self.hh)]
                    dst = self.out.at[pl.ds(h * self.hh, self.hh), self.z]
                    sem = self.recv.at[self.z]

                    def far(src=src, dst=dst, h=h):
                        copy = remote(src, dst, self.send.at[i, h], sem, (to, 2 * self.c + h))
                        if start:
                            copy.start()
                        else:
                            copy.wait_send()

                    if i:
                        far()
                    else:
                        pl.when(self.k != h)(far)
                        if start:

                            @pl.when(self.k == h)
                            def _(src=src, dst=dst):
                                pltpu.make_async_copy(src, dst, sem).start()

            pl.when(expert // self.local == self.k)(go)

    def begin(self):
        self.sends(True)

    def pass_on(self):
        mine = lax.rem(self.z, self.inner)
        for i in range(self.n_dp):
            d = lax.rem(self.z + self.n_dp - i, self.n_dp)
            region = self.out.at[pl.ds(self.k * self.hh, self.hh), d]
            if i:
                wait_recv(region, self.recv.at[d], self.sibling)
            else:
                from_here = mine // self.local == self.k

                @pl.when(from_here)
                def _(region=region, d=d):
                    src = self.weight.at[
                        lax.rem(mine, self.local), pl.ds(self.k * self.hh, self.hh)
                    ]
                    pltpu.make_async_copy(src, region, self.recv.at[d]).wait()

                @pl.when(jnp.logical_not(from_here))
                def _(region=region, d=d):
                    wait_recv(region, self.recv.at[d], self.sibling)

            remote(
                region, region, self.sib_send.at[i], self.sib_recv.at[i], self.sibling
            ).start()

    def end(self):
        self.sends(False)
        for i in range(self.n_dp):
            d = lax.rem(self.z + self.n_dp - i, self.n_dp)
            mine = self.out.at[pl.ds(self.k * self.hh, self.hh), d]
            remote(
                mine, mine, self.sib_send.at[i], self.sib_recv.at[i], self.sibling
            ).wait_send()
            region = self.out.at[pl.ds((1 - self.k) * self.hh, self.hh), d]
            wait_recv(region, self.sib_recv.at[i], self.sibling)


def forward_exchange(parts, tok, gain, slots, experts, shared, n_dp, n_ex, inner, collective_id):
    chips = n_ex // 2
    rows, width = tok.shape
    count = len(experts)

    def kernel(x_ref, tok_ref, gain_ref, slot_ref, *refs):
        e_in, s_in = refs[:count], refs[count : count + 3]
        refs = refs[count + 3 :]
        res_ref, xcol_ref, slot_out = refs[:3]
        w_out, s_out = refs[3 : 3 + count], refs[3 + count : 6 + count]
        refs = refs[6 + count :]
        from_sib, out_buf, from_far, xbuf = refs[:4]
        (
            near_s, near_r, far_s, far_r, x_s, x_r, g_s, g_r,
            sh_s, sh_r, sp_s, sp_r, sf_s, sf_r, local,
        ) = refs[4:19]
        refs = refs[19:]
        z, e, c, k, sibling, same_core, column = places(n_dp, n_ex)
        group = column_group(z, e, inner)
        greet(same_core + [sibling] + column + [(device[0], sibling[1]) for device in column])
        my_l = lax.rem(z, inner)
        matrices = [
            ExpertsIn(e_in[m], w_out[m], refs[4 * m : 4 * m + 4], n_dp, n_ex, inner)
            for m in range(count)
        ]
        near = []
        for i in list(range(1, chips)) + [0]:
            chip = lax.rem(c + i, chips)
            copy = remote(
                x_ref.at[chip * 2 + 1 - k], from_sib.at[chip], near_s.at[i], near_r.at[i], sibling
            )
            copy.start()
            near.append(copy)
        shared_copies = []
        for i in range(1, n_dp):
            for m in range(3):
                copy = remote(
                    s_in[m].at[lax.rem(lax.rem(z + i, n_dp), inner)], s_out[m].at[e, z],
                    sh_s.at[m, i], sh_r.at[m, i], column[i - 1],
                )
                copy.start()
                shared_copies.append(copy)
        own = [
            pltpu.make_async_copy(s_in[m].at[my_l], s_out[m].at[e, z], local.at[m])
            for m in range(3)
        ]
        own.append(pltpu.make_async_copy(slot_ref.at[0], slot_out.at[0], local.at[3]))
        for copy in own:
            copy.start()
        matrices[0].begin()
        far = []
        for i in range(1, chips):
            chip = lax.rem(c + i, chips)
            near[i - 1].wait_recv()
            out_buf[i] = (
                x_ref[chip * 2 + k].astype(F32) + from_sib[chip].astype(F32)
            ).astype(BF)
            copy = remote(out_buf.at[i], from_far.at[i], far_s.at[i], far_r.at[i], same_core[i - 1])
            copy.start()
            far.append(copy)
        near[chips - 1].wait_recv()
        res_ref[...] = x_ref[e].astype(F32) + from_sib[c].astype(F32) + tok_ref[...].astype(F32)
        for i in range(1, chips):
            far[i - 1].wait_recv()
            res_ref[...] += from_far[i].astype(F32)
        residual = res_ref[...]
        scale = lax.rsqrt(jnp.mean(residual * residual, axis=-1, keepdims=True) + norm_eps)
        xbuf[...] = (residual * scale * gain_ref[...]).astype(BF)
        x_copies = []
        for i in range(1, inner):
            copy = remote(xbuf, xcol_ref.at[my_l], x_s.at[i], x_r.at[i], group[i])
            copy.start()
            x_copies.append(copy)
        x_own = pltpu.make_async_copy(xbuf, xcol_ref.at[my_l], local.at[4])
        x_own.start()
        for matrix in matrices[1:]:
            matrix.begin()
        slot_copies = []
        for i in range(1, chips):
            copy = remote(slot_ref.at[i], slot_out.at[i], g_s.at[i], g_r.at[i], same_core[i - 1])
            copy.start()
            slot_copies.append(copy)
        for copy in own:
            copy.wait()
        for copy in shared_copies:
            copy.wait_recv()
        plane, to_sib = [], []
        for m in range(3):
            block = s_out[m].at[e]
            for i in range(1, chips):
                copy = remote(block, block, sp_s.at[m, i], sp_r.at[m, i], same_core[i - 1])
                copy.start()
                plane.append(copy)
            copy = remote(block, block, sf_s.at[m, 0], sf_r.at[m, 0], sibling)
            copy.start()
            to_sib.append(copy)
        for m in range(3):
            for i in range(1, chips):
                plane[m * (chips - 1) + i - 1].wait_recv()
                block = s_out[m].at[lax.rem(c + chips - i, chips) * 2 + k]
                copy = remote(block, block, sf_s.at[m, i], sf_r.at[m, i], sibling)
                copy.start()
                to_sib.append(copy)
        for matrix in matrices:
            matrix.pass_on()
        for copy in x_copies + slot_copies + to_sib:
            copy.wait()
        x_own.wait()
        for copy in plane + shared_copies + near + far:
            copy.wait_send()
        for matrix in matrices:
            matrix.end()

    dma = pltpu.SemaphoreType.DMA
    r = shared[0].shape[1]
    ff_s = shared[0].shape[2]
    scratch = []
    for _ in experts:
        scratch += ExpertsIn.scratch(n_dp)
    outs = pl.pallas_call(
        kernel,
        out_shape=[
            jax.ShapeDtypeStruct((rows, width), F32),
            jax.ShapeDtypeStruct((inner, rows, width), BF),
            jax.ShapeDtypeStruct(slots.shape, BF),
        ]
        + [ExpertsIn.out(w, n_dp, n_ex) for w in experts]
        + [jax.ShapeDtypeStruct((n_ex, n_dp, r, ff_s), BF)] * 3,
        in_specs=[VMEM] * 3 + [ANY] * (4 + count),
        out_specs=[VMEM] + [ANY] * (5 + count),
        scratch_shapes=[pltpu.VMEM((chips, rows, width), BF)] * 3
        + [pltpu.VMEM((rows, width), BF)]
        + [dma((chips,))] * 4
        + [dma((inner,))] * 2
        + [dma((chips,))] * 2
        + [dma((3, n_dp))] * 2
        + [dma((3, chips))] * 4
        + [dma((5,))]
        + scratch,
        compiler_params=params(collective_id),
    )(parts, tok, gain, slots, *experts, *shared)
    return outs[0], outs[1], outs[2], outs[3 : 3 + count], outs[3 + count :]


def between(blocks, way, weights, totals, n_dp, n_ex, inner, collective_id):
    chips = n_ex // 2
    n_in, n_back = len(weights), len(totals)

    def kernel(x_ref, *refs):
        w_in, t_in = refs[:n_in], refs[n_in : n_in + n_back]
        refs = refs[n_in + n_back :]
        o_ref, w_out, t_out = refs[0], refs[1 : 1 + n_in], refs[1 + n_in : 1 + n_in + n_back]
        refs = refs[1 + n_in + n_back :]
        send, recv, local = refs[:3]
        z, e, c, k, sibling, same_core, column = places(n_dp, n_ex)
        greet(same_core + [sibling] + column + [(device[0], sibling[1]) for device in column])
        refs = refs[3:]
        works = [
            ExpertsIn(w_in[m], w_out[m], refs[4 * m : 4 * m + 4], n_dp, n_ex, inner)
            for m in range(n_in)
        ]
        refs = refs[4 * n_in :]
        works += [
            ExpertsBack(t_in[m], t_out[m], refs[7 * m : 7 * m + 7], n_dp, n_ex, inner)
            for m in range(n_back)
        ]
        copies = []
        for i in range(1, chips):
            to = same_core[i - 1] if way > 0 else same_core[chips - i - 1]
            copy = remote(x_ref.at[i], o_ref.at[i], send.at[i], recv.at[i], to)
            copy.start()
            copies.append(copy)
        copy = pltpu.make_async_copy(x_ref.at[0], o_ref.at[0], local)
        copy.start()
        copies.append(copy)
        for work in works:
            work.begin()
        for work in works:
            work.pass_on()
        for copy in copies:
            copy.wait()
        for work in works:
            work.end()

    dma = pltpu.SemaphoreType.DMA
    scratch = [dma((chips,)), dma((chips,)), dma]
    for _ in weights:
        scratch += ExpertsIn.scratch(n_dp)
    for total in totals:
        scratch += ExpertsBack.scratch(total, n_dp, inner)
    outs = pl.pallas_call(
        kernel,
        out_shape=[jax.ShapeDtypeStruct(blocks.shape, BF)]
        + [ExpertsIn.out(w, n_dp, n_ex) for w in weights]
        + [ExpertsBack.out(total, n_dp, inner) for total in totals],
        in_specs=[ANY] * (1 + n_in + n_back),
        out_specs=[ANY] * (1 + n_in + n_back),
        scratch_shapes=scratch,
        compiler_params=params(collective_id),
    )(blocks, *weights, *totals)
    return outs[0], outs[1:]


class ExpertsBack:
    @staticmethod
    def scratch(total, n_dp, inner):
        n_ex, _, r, ff = total.shape
        dma = pltpu.SemaphoreType.DMA
        return [
            pltpu.VMEM((n_ex // 2, n_dp, r, ff), BF),
            pltpu.VMEM((n_ex // 2, n_dp, r, ff), BF),
            dma((n_dp,)),
            dma((n_dp,)),
            dma((n_dp,)),
            dma((n_dp,)),
            dma((n_dp // inner, 2, 2)),
        ]

    @staticmethod
    def out(total, n_dp, inner):
        n_ex, _, r, ff = total.shape
        return jax.ShapeDtypeStruct((n_dp // inner, 2, n_ex, r, ff), BF)

    def __init__(self, total, out, scratch, n_dp, n_ex, inner):
        self.total, self.out, self.n_dp, self.inner = total, out, n_dp, inner
        self.own, self.sib, self.near_s, self.near_r, self.load, self.send, self.recv = scratch
        self.z, self.e, self.c, self.k, self.sibling, _, _ = places(n_dp, n_ex)
        self.hh = n_ex // 2

    def near(self, i):
        d = lax.rem(self.z + i, self.n_dp)
        return remote(
            self.total.at[pl.ds((1 - self.k) * self.hh, self.hh), d],
            self.sib.at[:, d], self.near_s.at[i], self.near_r.at[i], self.sibling,
        )

    def loads(self, i):
        d = lax.rem(self.z + i, self.n_dp)
        return pltpu.make_async_copy(
            self.total.at[pl.ds(self.k * self.hh, self.hh), d], self.own.at[:, d], self.load.at[i]
        )

    def order(self):
        return list(range(1, self.n_dp)) + [0]

    def begin(self):
        for i in self.order():
            self.near(i).start()
            self.loads(i).start()

    def route(self, i):
        d = lax.rem(self.z + i, self.n_dp)
        expert = lax.rem(self.z, self.inner)
        dst = self.out.at[
            self.z // self.inner, lax.rem(expert, 2), pl.ds(self.k * self.hh, self.hh)
        ]
        sem = self.recv.at[self.z // self.inner, lax.rem(expert, 2), self.k]
        return self.own.at[:, d], dst, sem, d, expert // 2

    def stay(self):
        src, dst, sem, _, _ = self.route(0)
        return pltpu.make_async_copy(src, dst, sem)

    def go(self, i):
        src, dst, sem, d, core = self.route(i)
        return remote(src, dst, self.send.at[i], sem, (d, 2 * self.c + core))

    def here(self):
        return lax.rem(self.z, self.inner) // 2 == self.k

    def pass_on(self):
        for i in self.order():
            d = lax.rem(self.z + i, self.n_dp)
            self.near(i).wait_recv()
            self.loads(i).wait()
            for j in range(self.hh):
                self.own[j, d] = (
                    self.own[j, d].astype(F32) + self.sib[j, d].astype(F32)
                ).astype(BF)
            if i:
                self.go(i).start()
            else:
                pl.when(self.here())(lambda: self.stay().start())
                pl.when(jnp.logical_not(self.here()))(lambda: self.go(0).start())

    def end(self):
        for i in self.order():
            self.near(i).wait_send()
            if i:
                self.go(i).wait_send()
            else:
                pl.when(jnp.logical_not(self.here()))(lambda: self.go(0).wait_send())
        for o in range(self.n_dp // self.inner):
            for j in range(2):
                for h in range(2):
                    region = self.out.at[o, j, pl.ds(h * self.hh, self.hh)]
                    source = o * self.inner + 2 * self.k + j
                    here = jnp.logical_and(source == self.z, self.k == h)

                    @pl.when(here)
                    def _(region=region, o=o, j=j, h=h):
                        d = self.z
                        pltpu.make_async_copy(
                            self.own.at[:, d], region, self.recv.at[o, j, h]
                        ).wait()

                    @pl.when(jnp.logical_not(here))
                    def _(region=region, o=o, j=j, h=h):
                        wait_recv(region, self.recv.at[o, j, h], self.sibling)


def plane_sum(arrays, totals, n_dp, n_ex, inner, collective_id):
    chips = n_ex // 2
    count, extra = len(arrays), len(totals)

    def kernel(*refs):
        x_refs, t_refs = refs[:count], refs[count : count + extra]
        refs = refs[count + extra :]
        o_refs, back_refs = refs[:count], refs[count : count + extra]
        refs = refs[count + extra :]
        bufs, sems, rest = refs[: 3 * count], refs[3 * count : 7 * count], refs[7 * count :]
        z, e, c, k, sibling, same_core, column = places(n_dp, n_ex)
        greet(
            same_core + [sibling] + (column + [(d[0], sibling[1]) for d in column] if extra else [])
        )
        backs = [
            ExpertsBack(t_refs[m], back_refs[m], rest[7 * m : 7 * m + 7], n_dp, n_ex, inner)
            for m in range(extra)
        ]
        near, far = {}, {}
        for i in list(range(1, chips)) + [0]:
            chip = lax.rem(c + i, chips)
            for j in range(count):
                near[i, j] = remote(
                    x_refs[j].at[chip * 2 + 1 - k],
                    bufs[3 * j].at[chip],
                    sems[4 * j].at[i],
                    sems[4 * j + 1].at[i],
                    sibling,
                )
                near[i, j].start()
        for back in backs:
            back.begin()
        for i in range(1, chips):
            chip = lax.rem(c + i, chips)
            for j in range(count):
                from_sib, out_buf, from_far = bufs[3 * j : 3 * j + 3]
                near[i, j].wait_recv()
                out_buf[i] = (
                    x_refs[j][chip * 2 + k].astype(F32) + from_sib[chip].astype(F32)
                ).astype(BF)
                far[i, j] = remote(
                    out_buf.at[i],
                    from_far.at[i],
                    sems[4 * j + 2].at[i],
                    sems[4 * j + 3].at[i],
                    same_core[i - 1],
                )
                far[i, j].start()
        for back in backs:
            back.pass_on()
        for j in range(count):
            near[0, j].wait_recv()
            o_refs[j][...] = x_refs[j][e].astype(F32) + bufs[3 * j][c].astype(F32)
        for i in range(1, chips):
            for j in range(count):
                far[i, j].wait_recv()
                o_refs[j][...] += bufs[3 * j + 2][i].astype(F32)
        for copy in list(near.values()) + list(far.values()):
            copy.wait_send()
        for back in backs:
            back.end()

    scratch = []
    for array in arrays:
        scratch += [pltpu.VMEM((chips,) + array.shape[1:], BF)] * 3
    scratch += [pltpu.SemaphoreType.DMA((chips,))] * (4 * count)
    for total in totals:
        scratch += ExpertsBack.scratch(total, n_dp, inner)
    outs = pl.pallas_call(
        kernel,
        out_shape=[jax.ShapeDtypeStruct(array.shape[1:], F32) for array in arrays]
        + [ExpertsBack.out(total, n_dp, inner) for total in totals],
        in_specs=[VMEM] * count + [ANY] * extra,
        out_specs=[VMEM] * count + [ANY] * extra,
        scratch_shapes=scratch,
        compiler_params=params(collective_id),
    )(*arrays, *totals)
    return outs[:count], outs[count:]


def last_exchange(heads, wout, pack, shared, totals, n_dp, n_ex, inner, collective_id):
    chips = n_ex // 2
    extra = len(totals)
    rows, cols = pack.shape[1:]
    r = rows // n_dp

    def kernel(heads_ref, wout_ref, pack_ref, *refs):
        sh_in, t_refs = refs[:3], refs[3 : 3 + extra]
        refs = refs[3 + extra :]
        heads_out, wout_out, pack_out = refs[:3]
        sh_out, back_refs = refs[3:6], refs[6 : 6 + extra]
        refs = refs[6 + extra :]
        hbuf, hsum, wbuf, psib, pout, pfar, psum, pbuf = refs[:8]
        (
            h_s, h_r, hp_s, hp_r, w_s, w_r, pn_s, pn_r, pf_s, pf_r, pc_s, pc_r, s_s, s_r, local,
        ) = refs[8:23]
        rest = refs[23:]
        z, e, c, k, sibling, same_core, column = places(n_dp, n_ex)
        plane = [(z, lax.rem(e + i, n_ex)) for i in range(1, n_ex)]
        greet(plane + column + [(d[0], sibling[1]) for d in column])
        backs = [
            ExpertsBack(t_refs[m], back_refs[m], rest[7 * m : 7 * m + 7], n_dp, n_ex, inner)
            for m in range(extra)
        ]
        near, far = [], []
        for i in list(range(1, chips)) + [0]:
            chip = lax.rem(c + i, chips)
            copy = remote(
                pack_ref.at[chip * 2 + 1 - k], psib.at[chip], pn_s.at[i], pn_r.at[i], sibling
            )
            copy.start()
            near.append(copy)
        heads_col, others = [], []
        for i in range(1, n_dp):
            to = lax.rem(z + i, n_dp)
            copy = remote(heads_ref.at[to], hbuf.at[i], h_s.at[i], h_r.at[i], column[i - 1])
            copy.start()
            heads_col.append(copy)
        for back in backs:
            back.begin()
        for i in range(1, chips):
            chip = lax.rem(c + i, chips)
            near[i - 1].wait_recv()
            pout[i] = (
                pack_ref[chip * 2 + k].astype(F32) + psib[chip].astype(F32)
            ).astype(BF)
            copy = remote(pout.at[i], pfar.at[i], pf_s.at[i], pf_r.at[i], same_core[i - 1])
            copy.start()
            far.append(copy)
        near[chips - 1].wait_recv()
        total = pack_ref[e].astype(F32) + psib[c].astype(F32)
        for i in range(1, chips):
            far[i - 1].wait_recv()
            total = total + pfar[i].astype(F32)
        psum[...] = total.astype(BF).reshape(n_dp, r, cols)
        pack_col, wout_col = [], []
        for i in range(1, n_dp):
            to = lax.rem(z + i, n_dp)
            copy = remote(psum.at[to], pbuf.at[i], pc_s.at[i], pc_r.at[i], column[i - 1])
            copy.start()
            pack_col.append(copy)
            copy = remote(wout_ref.at[to], wbuf.at[i], w_s.at[i], w_r.at[i], column[i - 1])
            copy.start()
            wout_col.append(copy)
            for m in range(3):
                copy = remote(
                    sh_in[m].at[to], sh_out[m].at[z], s_s.at[m, i], s_r.at[m, i], column[i - 1]
                )
                copy.start()
                others.append(copy)
        for m in range(3):
            copy = pltpu.make_async_copy(sh_in[m].at[z], sh_out[m].at[z], local.at[m])
            copy.start()
            others.append(copy)
        for copy in heads_col:
            copy.wait_recv()
        for j in range(n_ex):
            block = heads_ref[z, j].astype(F32)
            for i in range(1, n_dp):
                block = block + hbuf[i, j].astype(F32)
            hsum[j] = block.astype(BF)
        heads_plane = []
        for i in range(1, n_ex):
            copy = remote(
                hsum.at[lax.rem(e + i, n_ex)], heads_out.at[e], hp_s.at[i], hp_r.at[i],
                plane[i - 1],
            )
            copy.start()
            heads_plane.append(copy)
        keep = pltpu.make_async_copy(hsum.at[e], heads_out.at[e], local.at[3])
        keep.start()
        for back in backs:
            back.pass_on()
        for copy in wout_col + pack_col:
            copy.wait_recv()
        wout_sum = wout_ref[z].astype(F32)
        pack_sum = psum[z].astype(F32)
        for i in range(1, n_dp):
            wout_sum = wout_sum + wbuf[i].astype(F32)
            pack_sum = pack_sum + pbuf[i].astype(F32)
        wout_out[...] = wout_sum
        pack_out[...] = pack_sum
        for copy in near + far + heads_col + wout_col + pack_col:
            copy.wait_send()
        keep.wait()
        for copy in heads_plane + others:
            copy.wait()
        for back in backs:
            back.end()

    dma = pltpu.SemaphoreType.DMA
    scratch = [
        pltpu.VMEM(heads.shape, BF),
        pltpu.VMEM(heads.shape[1:], BF),
        pltpu.VMEM(wout.shape, BF),
        pltpu.VMEM((chips, rows, cols), BF),
        pltpu.VMEM((chips, rows, cols), BF),
        pltpu.VMEM((chips, rows, cols), BF),
        pltpu.VMEM((n_dp, r, cols), BF),
        pltpu.VMEM((n_dp, r, cols), BF),
        dma((n_dp,)), dma((n_dp,)), dma((n_ex,)), dma((n_ex,)), dma((n_dp,)), dma((n_dp,)),
        dma((chips,)), dma((chips,)), dma((chips,)), dma((chips,)), dma((n_dp,)), dma((n_dp,)),
        dma((3, n_dp)), dma((3, n_dp)), dma((4,)),
    ]
    for total in totals:
        scratch += ExpertsBack.scratch(total, n_dp, inner)
    outs = pl.pallas_call(
        kernel,
        out_shape=[
            jax.ShapeDtypeStruct(heads.shape[1:], BF),
            jax.ShapeDtypeStruct(wout.shape[1:], F32),
            jax.ShapeDtypeStruct((r, cols), F32),
        ]
        + [jax.ShapeDtypeStruct(array.shape, BF) for array in shared]
        + [ExpertsBack.out(total, n_dp, inner) for total in totals],
        in_specs=[VMEM] * 3 + [ANY] * (3 + extra),
        out_specs=[ANY, VMEM, VMEM] + [ANY] * (3 + extra),
        scratch_shapes=scratch,
        compiler_params=params(collective_id),
    )(heads, wout, pack, *shared, *totals)
    return outs[0], outs[1], outs[2], outs[3:6], outs[6:]


def shards(
    tokens,
    cotangent,
    lengths,
    routes,
    place_order,
    attn_gain,
    w_query,
    w_latent,
    latent_gain,
    w_expand,
    w_out,
    ffn_gain,
    w_router,
    shared_gate,
    shared_up,
    shared_down,
    expert_gate,
    expert_up,
    expert_down,
):
    rows, width = tokens.shape
    n_dp = lax.axis_size("dp")
    n_ex = lax.axis_size("expert")
    chips = n_ex // 2
    z = lax.axis_index("dp")
    e = lax.axis_index("expert")
    chip = e // 2
    n_experts = w_router.shape[1]
    top_k = routes.shape[1]
    capacity = (rows * top_k * 5 + 4 * n_experts - 1) // (4 * n_experts)
    cap = (capacity + 15) // 16 * 16
    seq = rows * n_ex
    r = w_query.shape[0]
    rl = w_expand.shape[0]
    hp = H // n_ex
    parts = DV // r
    heads = [
        (d * n_ex + (j // parts) * parts) * r // DV
        for j in range(n_ex)
        for d in range(j % parts * hp, j % parts * hp + hp)
    ]
    heads_back = [heads.index(h) for h in range(H)]
    inner = n_experts // chips
    my_local = lax.rem(z, inner)
    part_groups = [[i * parts + m for m in range(parts)] for i in range(n_ex // parts)]
    ff_e = expert_gate.shape[2]
    ff_s = shared_gate.shape[1] // inner
    lat = KVR + DR
    head_cols = hp * (DH + DR)
    kv_cols = hp * (DH + DV)

    def to_owner_order(values):
        cut = values.reshape(values.shape[0], n_dp, n_ex, r)
        return cut.transpose(0, 2, 1, 3).reshape(values.shape)

    def from_owner_order(values):
        cut = values.reshape(values.shape[0], n_ex, n_dp, r)
        return cut.transpose(0, 2, 1, 3).reshape(values.shape)

    def pick(values, index, axis=0):
        return lax.dynamic_index_in_dim(values, index, axis, keepdims=False)

    wq_send = jnp.take(w_query.reshape(r, H, DH + DR), jnp.array(heads), axis=1)
    wq_send = wq_send.reshape(r, n_ex, head_cols).transpose(1, 0, 2)
    we_send = jnp.take(w_expand.reshape(rl, H, DH + DV), jnp.array(heads), axis=1)
    we_send = we_send.reshape(rl, n_ex, kv_cols).transpose(1, 0, 2)
    we_send = we_send.reshape(n_ex, r, rl * kv_cols // r)
    wa_send = jnp.concatenate([wq_send, we_send], axis=-1)
    slot_own = slot_places(routes, place_order[0], capacity)
    slot_place = jnp.where(slot_own >= 0, slot_own - routes * capacity, -1)
    slot_cols = 2 * rows * top_k // r
    slot_pack = jnp.stack([routes, slot_place]).astype(BF).reshape(2, r, slot_cols // 2)
    small_cols = lat + n_experts + 3
    pack_cols = (small_cols + slot_cols + 127) // 128 * 128
    pack = jnp.concatenate(
        [
            w_latent,
            w_router,
            attn_gain[:, None],
            ffn_gain[:, None],
            jnp.pad(latent_gain, (0, r - rl))[:, None],
            slot_pack[0],
            slot_pack[1],
            jnp.zeros((r, pack_cols - small_cols - slot_cols), BF),
        ],
        axis=1,
    )
    cot_owner = to_owner_order(cotangent)
    tok_all, wa_all, pk_all = first_exchange(tokens, wa_send, pack, n_dp, n_ex, 1)
    wq = wa_all[..., :head_cols].reshape(width, head_cols)
    wexp = wa_all[..., head_cols:].reshape(KVR, kv_cols)
    pk_flat = pk_all.reshape(width, pack_cols)
    w_lat = pk_flat[:, :lat]
    gain_one = pk_flat[:, lat + n_experts].astype(F32)
    gain_two = pk_all[..., lat + n_experts + 1].transpose(1, 0, 2).reshape(width).astype(F32)
    router = pk_all[..., lat : lat + n_experts].transpose(1, 0, 2, 3).reshape(width, n_experts)
    gain_lat = (
        pk_all[..., lat + n_experts + 2].reshape(n_dp * n_ex, r)[:, :rl].reshape(KVR).astype(F32)
    )
    wo_send, _ = lax.optimization_barrier((to_owner_order(w_out), pk_all))
    wo_col = lax.all_gather(wo_send, "dp", axis=0, tiled=False)
    wo_rows = lax.all_to_all(
        wo_col.reshape(parts, hp, r, width),
        "expert",
        0,
        0,
        axis_index_groups=part_groups,
        tiled=True,
    )
    wo_rows = wo_rows.transpose(1, 0, 2, 3).reshape(hp * DV, width)

    col_groups = [[o * inner + i for i in range(inner)] for o in range(n_dp // inner)]
    cot_send, _ = lax.optimization_barrier((cot_owner, wo_col))
    cot_col = lax.all_gather(cot_send, "dp", axis=0, tiled=True, axis_index_groups=col_groups)
    slots_all = n_experts * capacity
    slot_col = pick(pk_all[..., small_cols : small_cols + slot_cols], e, 1)
    slot_col = lax.dynamic_slice_in_dim(slot_col, z - my_local, inner, 0).astype(jnp.int32)
    slot_col = slot_col.reshape(inner, r, 2, slot_cols // 2).transpose(2, 0, 1, 3)
    slot_col = slot_col.reshape(2, inner, rows, top_k)
    slot_ids = jnp.where(
        slot_col[1] >= 0,
        slot_col[0] * capacity + slot_col[1] + (jnp.arange(inner) * slots_all)[:, None, None],
        -1,
    ).reshape(inner * rows, top_k)
    place = jnp.arange(cap)
    far_experts = [lax.rem(chip + m, chips) * inner + my_local for m in range(chips)]
    wanted = (
        jnp.stack(far_experts)[:, None, None] * capacity
        + (jnp.arange(inner) * slots_all)[None, :, None]
        + place[None, None, :]
    )
    wanted = jnp.where(place[None, None, :] < capacity, wanted, -2).reshape(-1)
    n_slots = wanted.shape[0]
    per_far = n_slots // chips
    hot = sum((wanted[:, None] == slot_ids[None, :, j]).astype(BF) for j in range(top_k))
    hot_t = sum((slot_ids[:, j][:, None] == wanted[None, :]).astype(BF) for j in range(top_k))

    def through(values):
        cut = values.reshape(chips, per_far, -1)
        got = [cut[0]]
        for m in range(1, chips):
            perm = [(i, (i - 2 * m) % n_ex) for i in range(n_ex)]
            got.append(lax.ppermute(cut[m], "expert", perm))
        return jnp.concatenate(got, axis=0)

    grad_send = mm(hot, cot_col).astype(BF).reshape(chips, per_far, width)

    tok_plane = tok_all.reshape(seq, width)
    hidden_one = rms_norm(tok_plane.astype(F32), gain_one).astype(BF)
    positions = jnp.arange(seq)
    cos_table, sine_table = rope_tables(positions)
    query_raw = mm(hidden_one, wq).reshape(seq, hp, DH + DR)

    def make_queries(query_in):
        return jnp.concatenate(
            [
                query_in[..., :DH],
                rotate(query_in[..., DH:], cos_table[:, None, :], sine_table[:, None, :]),
            ],
            axis=-1,
        )

    query_rot, query_back = jax.vjp(make_queries, query_raw)
    queries = query_rot.astype(BF)
    latent_raw = mm(hidden_one, w_lat)
    latent_low = rms_norm(latent_raw[:, :KVR], gain_lat).astype(BF)
    rope_low = rotate(latent_raw[:, KVR:], cos_table, sine_table).astype(BF)
    expanded = mm(latent_low, wexp).astype(BF).reshape(seq, hp, DH + DV)
    score_scale = (DH + DR) ** (-0.5)
    allowed = (positions[None, :] <= positions[:, None]) & (positions[None, :] < lengths[0])
    attn_probs, probs_low, keys, attended = [], [], [], []
    for h in range(hp):
        key = jnp.concatenate([expanded[:, h, :DH], rope_low], axis=1)
        scores = jnp.where(allowed, mm_cols(queries[:, h], key) * score_scale, masked_score)
        top = jnp.max(scores, axis=-1, keepdims=True)
        exp_scores = jnp.exp(scores - top)
        probs = exp_scores / jnp.sum(exp_scores, axis=-1, keepdims=True)
        low = probs.astype(BF)
        attn_probs.append(probs)
        probs_low.append(low)
        keys.append(key)
        attended.append(mm(low, expanded[:, h, DH:]).astype(BF))
    attended = jnp.concatenate(attended, axis=1)
    out_part = mm(attended, wo_rows).astype(BF)
    residual, x_col, grad_in, (wg, wu), (sgate, sup, sdown) = forward_exchange(
        out_part.reshape(n_ex, rows, width),
        to_owner_order(tokens),
        gain_two[None],
        grad_send,
        [w.reshape(-1, n_ex, r, ff_e) for w in (expert_gate, expert_up)],
        [w.reshape(r, inner, ff_s).transpose(1, 0, 2) for w in (shared_gate, shared_up, shared_down)],
        n_dp,
        n_ex,
        inner,
        2,
    )
    sgate, sup, sdown = (w.reshape(width, ff_s) for w in (sgate, sup, sdown))
    hidden_two = pick(x_col, my_local)
    x_col = x_col.reshape(inner * rows, width)
    grad_in = grad_in.reshape(n_slots, width)

    x_in, (wd,) = between(
        mm(hot, x_col).astype(BF).reshape(chips, per_far, width),
        1,
        [expert_down.reshape(-1, n_ex, r, ff_e)],
        [],
        n_dp,
        n_ex,
        inner,
        8,
    )
    x_in = x_in.reshape(n_slots, width)
    wg, wu, wd = (w.reshape(width, ff_e) for w in (wg, wu, wd))

    def probs_of(logits):
        top = jnp.max(logits, axis=-1, keepdims=True)
        exp_logits = jnp.exp(logits - top)
        return exp_logits / jnp.sum(exp_logits, axis=-1, keepdims=True)

    shared_a = mm(x_col, sgate)
    shared_b = mm(x_col, sup)
    shared_hidden, shared_back = jax.vjp(swiglu, shared_a, shared_b)
    shared_hidden = shared_hidden.astype(BF)
    shared_out = mm_cols(shared_hidden, sdown)
    grad_sa, grad_sb = (v.astype(BF) for v in shared_back(mm(cot_col, sdown)))
    shared_grads = [
        mm_rows(x_col, grad_sa).astype(BF),
        mm_rows(x_col, grad_sb).astype(BF),
        mm_rows(cot_col, shared_hidden).astype(BF),
    ]
    shared_dx = mm_cols(grad_sa, sgate) + mm_cols(grad_sb, sup)

    slot_probs = probs_of(mm(x_in, router))
    slot_gate = jnp.sum(
        jnp.where(jnp.arange(n_experts)[None, :] == far_experts[0], slot_probs, 0.0),
        axis=1,
        keepdims=True,
    )
    expert_a = mm(x_in, wg)
    expert_b = mm(x_in, wu)
    expert_hidden, expert_back = jax.vjp(swiglu, expert_a, expert_b)
    expert_hidden = expert_hidden.astype(BF)
    rows_back = through(mm_cols(expert_hidden, wd).astype(BF))
    slot_grad = (slot_gate * grad_in.astype(F32)).astype(BF)
    grad_ea, grad_eb = (v.astype(BF) for v in expert_back(mm(slot_grad, wd)))
    expert_totals = [
        mm_rows(left, right).astype(BF).reshape(n_ex, n_dp, r, ff_e)
        for left, right in ((x_in, grad_ea), (x_in, grad_eb), (slot_grad, expert_hidden))
    ]
    dx_back, (down_back,) = between(
        (mm_cols(grad_ea, wg) + mm_cols(grad_eb, wu)).astype(BF).reshape(chips, per_far, width),
        -1,
        [],
        expert_totals[2:],
        n_dp,
        n_ex,
        inner,
        9,
    )
    dx_back = dx_back.reshape(n_slots, width)

    col_probs = probs_of(mm(x_col, router))
    expert_axis = jnp.arange(n_experts)[None, :]
    gates = [
        jnp.sum(jnp.where(expert_axis == expert, col_probs, 0.0), axis=1, keepdims=True)
        for expert in far_experts
    ]
    gate_hot = jnp.concatenate(
        [hot_t[:, m * per_far : (m + 1) * per_far] * gates[m].astype(BF) for m in range(chips)],
        axis=1,
    )
    out_col = (mm(gate_hot, rows_back) + shared_out).astype(BF)
    dots = mm_cols(cot_col, rows_back) * hot_t.astype(F32)
    dots = jnp.sum(dots.reshape(inner * rows, chips, per_far), axis=-1)
    grad_probs_col = sum(
        jnp.where(expert_axis == far_experts[m], dots[:, m : m + 1], 0.0) for m in range(chips)
    )
    dx_col = mm(hot_t, dx_back) + shared_dx
    dx_send = jnp.concatenate(
        [dx_col, grad_probs_col, jnp.zeros((inner * rows, 128 - n_experts), F32)], axis=1
    ).astype(BF)
    dx_sum = column_sum(dx_send.reshape(inner, rows, width + 128), n_dp, n_ex, inner, 3)
    router_probs = lax.dynamic_slice_in_dim(col_probs, my_local * rows, rows, 0)
    grad_probs = dx_sum[:, width : width + n_experts]
    grad_logits = (
        router_probs * (grad_probs - jnp.sum(grad_probs * router_probs, axis=-1, keepdims=True))
    ).astype(BF)
    grad_router = mm_rows(hidden_two, grad_logits)
    grad_hidden_two = dx_sum[:, :width] + mm_cols(grad_logits, router)
    _, norm_two_back = jax.vjp(rms_norm, residual, gain_two)
    grad_resid_norm, grad_gain_two = norm_two_back(grad_hidden_two)
    grad_residual = cot_owner.astype(F32) + grad_resid_norm

    grad_attn = plane_gather(grad_residual.astype(BF), n_dp, n_ex, 4).reshape(seq, width)
    out_sum = lax.psum_scatter(
        out_col, "dp", scatter_dimension=0, tiled=True, axis_index_groups=col_groups
    )
    out_tokens = from_owner_order((residual + out_sum.astype(F32)).astype(BF))
    shared_grads, _ = lax.optimization_barrier((shared_grads, grad_attn))
    shared_sums = [
        lax.psum_scatter(
            grad.reshape(n_ex, n_dp, r, ff_s), "expert", scatter_dimension=0, tiled=True
        ).reshape(n_dp, r, ff_s)
        for grad in shared_grads
    ]
    grad_attended = mm_cols(grad_attn, wo_rows).astype(BF)
    grad_wout = mm_rows(attended, grad_attn).astype(BF)
    grad_rope = 0.0
    grad_queries, grad_expanded = [], []
    for h in range(hp):
        gat = grad_attended[:, h * DV : (h + 1) * DV]
        probs = attn_probs[h]
        dp = mm_cols(gat, expanded[:, h, DH:])
        grad_scores = probs * (dp - jnp.sum(dp * probs, axis=-1, keepdims=True))
        grad_raw = jnp.where(allowed, grad_scores * score_scale, 0.0).astype(BF)
        grad_queries.append(mm(grad_raw, keys[h]))
        grad_key = mm_rows(grad_raw, queries[:, h])
        grad_rope = grad_rope + grad_key[:, DH:]
        grad_expanded += [grad_key[:, :DH], mm_rows(probs_low[h], gat)]
    grad_expanded = jnp.concatenate(grad_expanded, axis=1).astype(BF)
    (grad_query_raw,) = query_back(jnp.stack(grad_queries, axis=1))
    grad_query_low = grad_query_raw.reshape(seq, head_cols).astype(BF)
    grad_latent_part = jnp.concatenate([mm_cols(grad_expanded, wexp), grad_rope], axis=1)
    grad_latent_part = jnp.pad(grad_latent_part, ((0, 0), (0, -lat % 128))).astype(BF)
    grad_query_part = mm_cols(grad_query_low, wq).astype(BF)
    (grad_query_sum, grad_latent_sum), (gate_back,) = plane_sum(
        [grad_query_part.reshape(n_ex, rows, width), grad_latent_part.reshape(n_ex, rows, -1)],
        expert_totals[:1],
        n_dp,
        n_ex,
        inner,
        5,
    )
    own_start = e * rows
    latent_own = lax.dynamic_slice_in_dim(latent_raw, own_start, rows, 0)
    cos_own = lax.dynamic_slice_in_dim(cos_table, own_start, rows, 0)
    sine_own = lax.dynamic_slice_in_dim(sine_table, own_start, rows, 0)

    def make_latent(latent_in, gain_in):
        return (
            rms_norm(latent_in[:, :KVR], gain_in),
            rotate(latent_in[:, KVR:], cos_own, sine_own),
        )

    _, latent_back = jax.vjp(make_latent, latent_own, gain_lat)
    grad_latent_raw, grad_gain_lat = latent_back(
        (grad_latent_sum[:, :KVR], grad_latent_sum[:, KVR:lat])
    )
    grad_latent_low = grad_latent_raw.astype(BF)
    _, norm_one_back = jax.vjp(rms_norm, tokens.astype(F32), gain_one)
    grad_hidden_one = grad_query_sum + mm_cols(grad_latent_low, w_lat)
    grad_tokens_norm, grad_gain_one = norm_one_back(grad_hidden_one)
    grad_tokens = from_owner_order(grad_residual) + grad_tokens_norm

    wout_back = lax.all_to_all(
        grad_wout.reshape(hp, parts, r, width).transpose(1, 0, 2, 3),
        "expert",
        0,
        0,
        axis_index_groups=part_groups,
        tiled=True,
    ).reshape(n_dp, r, width)
    grad_wq = mm_rows(hidden_one, grad_query_low).astype(BF).reshape(n_dp, n_ex, r, head_cols)
    grad_we = mm_rows(latent_low, grad_expanded).astype(BF)
    grad_we = grad_we.reshape(n_dp, n_ex, r, rl * kv_cols // r)
    heads_grad = jnp.concatenate([grad_wq, grad_we], axis=-1)
    hidden_own = lax.dynamic_slice_in_dim(hidden_one, own_start, rows, 0)

    def by_owner(values):
        return values.reshape(n_ex, n_dp, r, -1).transpose(1, 0, 2, 3)

    pack_grad = jnp.concatenate(
        [
            mm_rows(hidden_own, grad_latent_low).reshape(n_dp, n_ex, r, lat),
            by_owner(grad_router),
            grad_gain_one.reshape(n_dp, n_ex, r, 1),
            by_owner(grad_gain_two),
            jnp.pad(grad_gain_lat.reshape(n_dp, n_ex, rl, 1), ((0, 0),) * 2 + ((0, r - rl), (0, 0))),
            jnp.zeros((n_dp, n_ex, r, -small_cols % 128), F32),
        ],
        axis=-1,
    ).astype(BF)
    pack_grad = pack_grad.transpose(1, 0, 2, 3).reshape(n_ex, n_dp * r, -1)
    heads_all, sum_wout, pack_sum, shared_got, (up_back,) = last_exchange(
        heads_grad, wout_back, pack_grad, shared_sums, expert_totals[1:2], n_dp, n_ex, inner, 7
    )

    def added(values):
        return jnp.sum(values.astype(F32), axis=0)

    heads_all = heads_all.astype(F32)
    sum_wq = heads_all[..., :head_cols].transpose(1, 0, 2).reshape(r, H, DH + DR)
    sum_wq = jnp.take(sum_wq, jnp.array(heads_back), axis=1).reshape(r, H * (DH + DR))
    sum_we = heads_all[..., head_cols:].reshape(n_ex, rl, kv_cols).transpose(1, 0, 2)
    sum_we = jnp.take(sum_we.reshape(rl, H, DH + DV), jnp.array(heads_back), axis=1)
    sum_we = sum_we.reshape(rl, H * (DH + DV))
    sum_wout = from_owner_order(sum_wout)
    sum_sgate, sum_sup, sum_sdown = (
        added(got.reshape(n_dp // inner, inner, r, ff_s)).transpose(1, 0, 2).reshape(r, -1)
        for got in shared_got
    )
    sum_egate, sum_eup, sum_edown = (
        added(back).reshape(-1, n_ex * r, ff_e) for back in (gate_back, up_back, down_back)
    )
    return (
        out_tokens,
        grad_tokens,
        pack_sum[:, lat + n_experts],
        sum_wq,
        pack_sum[:, :lat],
        pack_sum[:rl, lat + n_experts + 2],
        sum_we,
        sum_wout,
        pack_sum[:, lat + n_experts + 1],
        pack_sum[:, lat : lat + n_experts],
        sum_sgate,
        sum_sup,
        sum_sdown,
        sum_egate,
        sum_eup,
        sum_edown,
    )


def solution(mesh):
    both = ("dp", "expert")
    in_specs = (
        P(both, None),
        P(both, None),
        P("dp"),
        P(both, None),
        P(both, None),
        P(both),
        P(both, None),
        P(both, None),
        P(both),
        P(both, None),
        P(both, None),
        P(both),
        P(both, None),
        P(both, None),
        P(both, None),
        P(both, None),
        P("expert", "dp", None),
        P("expert", "dp", None),
        P("expert", "dp", None),
    )
    out_specs = (
        P(both, None),
        P(both, None),
        P(both),
        P(both, None),
        P(both, None),
        P(both),
        P(both, None),
        P(both, None),
        P(both),
        P(both, None),
        P(both, None),
        P(both, None),
        P(both, None),
        P("expert", "dp", None),
        P("expert", "dp", None),
        P("expert", "dp", None),
    )
    return jax.shard_map(shards, mesh=mesh, in_specs=in_specs, out_specs=out_specs, check_vma=False)
```

```python
import jax
import jax.numpy as jnp
from jax import lax
from jax.experimental import pallas as pl
from jax.experimental.pallas import tpu as pltpu
from jax.sharding import PartitionSpec as P

H = 16
DH = 128
DR = 64
DV = 128
KVR = 512

norm_eps = 1e-06
masked_score = -1e30
MESH = pl.DeviceIdType.MESH
ANY = pl.BlockSpec(memory_space=pl.ANY)
VMEM = pl.BlockSpec(memory_space=pltpu.VMEM)
BF = jnp.bfloat16
F32 = jnp.float32


def rms_norm(values, scale_gain):
    return (
        values
        * lax.rsqrt(jnp.mean(values * values, axis=-1, keepdims=True) + norm_eps)
        * scale_gain
    )


def rotate(values, cos_table, sine_table):
    half_dim = values.shape[-1] // 2
    first_half = values[..., :half_dim]
    second_half = values[..., half_dim:]
    return jnp.concatenate(
        [
            first_half * cos_table - second_half * sine_table,
            second_half * cos_table + first_half * sine_table,
        ],
        axis=-1,
    )


def rope_tables(positions):
    half_dim = DR // 2
    inv_freq = 10000.0 ** (-(jnp.arange(half_dim).astype(F32) * 2.0) / DR)
    angles = positions.astype(F32)[:, None] * inv_freq[None, :]
    return (jnp.cos(angles), jnp.sin(angles))


def swiglu(gate_in, up_in):
    return jax.nn.silu(gate_in) * up_in


def mm(left, right):
    return jnp.dot(left, right, preferred_element_type=F32)


def mm_rows(left, right):
    return lax.dot_general(left, right, (((0,), (0,)), ((), ())), preferred_element_type=F32)


def mm_cols(left, right):
    return lax.dot_general(left, right, (((1,), (1,)), ((), ())), preferred_element_type=F32)


def slot_places(route_rows, pair_order, capacity):
    pair_expert = route_rows.reshape(-1)
    earlier = pair_order[None, :] < pair_order[:, None]
    same_expert = pair_expert[None, :] == pair_expert[:, None]
    places = jnp.sum((earlier & same_expert).astype(jnp.int32), axis=1)
    slot_index = jnp.where(places < capacity, pair_expert * capacity + places, -1)
    return slot_index.reshape(route_rows.shape)


def turn(values, cos, sin, sign):
    half = DR // 2
    first = lax.rem(lax.broadcasted_iota(jnp.int32, values.shape, 1), DR) < half
    partner = jnp.where(
        first, -pltpu.roll(values, 2 * DR - half, 1), pltpu.roll(values, half, 1)
    )
    return values * cos + sign * (partner * sin)


def causal(i, tile, keep_ref):
    shape = (tile, (i + 1) * tile)
    query = lax.broadcasted_iota(jnp.int32, shape, 0) + i * tile
    key = lax.broadcasted_iota(jnp.int32, shape, 1)
    return (key <= query) & (keep_ref[:, : shape[1]] > 0.5)


def attend_forward(
    tok, gain, wq, wl, gain_lat, we, cos, sin, keep,
    hidden, latent, latent_low, qcat, kcat, value, lse, attended,
):
    per, rows, width = tok.shape
    seq = per * rows
    tile = 2 * rows
    scale = (DH + DR) ** (-0.5)

    def project(i, carry):
        at = pl.ds(pl.multiple_of(i * tile, tile), tile)
        x = tok[pl.ds(2 * i, 2)].reshape(tile, width).astype(F32)
        root = lax.rsqrt(jnp.mean(x * x, axis=-1, keepdims=True) + norm_eps)
        hid = (x * root * gain[...]).astype(BF)
        hidden[at, :] = hid
        c, s = cos[at, :], sin[at, :]
        query = mm(hid, wq[...])
        rope_q = turn(query[:, 2 * DH :], c, s, 1.0).astype(BF)
        lat = mm(hid, wl[...])
        latent[at, :] = lat
        plain = lat[:, :KVR]
        root = lax.rsqrt(jnp.mean(plain * plain, axis=-1, keepdims=True) + norm_eps)
        low = (plain * root * gain_lat[...]).astype(BF)
        latent_low[at, :] = low
        rope = lat[:, KVR : KVR + 2 * DR]
        lane = lax.broadcasted_iota(jnp.int32, rope.shape, 1)
        rope = jnp.where(lane < DR, rope, pltpu.roll(rope, DR, 1))
        rope = turn(rope, c, s, 1.0)
        expanded = mm(low, we[...]).astype(BF)
        for h in range(2):
            qcat[h, at, :DH] = query[:, h * DH : (h + 1) * DH].astype(BF)
            qcat[h, at, DH:] = rope_q
            mine = (lane < DR) if h == 0 else (lane >= DR)
            kcat[h, at, :DH] = expanded[:, h * (DH + DV) : h * (DH + DV) + DH]
            kcat[h, at, DH:] = jnp.where(mine, rope, 0.0).astype(BF)
            value[h, at, :] = expanded[:, h * (DH + DV) + DH : (h + 1) * (DH + DV)]
        return carry

    lax.fori_loop(0, seq // tile, project, 0)
    for h in range(2):
        for i in range(seq // tile):
            at, upto = slice(i * tile, (i + 1) * tile), slice(0, (i + 1) * tile)
            scores = mm_cols(qcat[h, at, :], kcat[h, upto, :]) * scale
            scores = jnp.where(causal(i, tile, keep), scores, masked_score)
            top = jnp.max(scores, axis=-1, keepdims=True)
            exp_scores = jnp.exp(scores - top)
            total = jnp.sum(exp_scores, axis=-1, keepdims=True)
            probs = (exp_scores / total).astype(BF)
            attended[at, h * DV : (h + 1) * DV] = mm(probs, value[h, upto, :]).astype(BF)
            lse[h, at, :] = jnp.broadcast_to(top + jnp.log(total), (tile, lse.shape[2]))


def attend_backward(
    grad, wo, wq, we, cos, sin, keep, qcat, kcat, value, lse, attended,
    gat, grad_wout, dk, dv, grad_query, grad_expanded, grad_rope,
):
    per, rows, width = grad.shape
    seq = per * rows
    tile = 2 * rows
    scale = (DH + DR) ** (-0.5)
    count = seq // tile
    grad_wout[...] = jnp.zeros_like(grad_wout)

    def project(i, carry):
        at = pl.ds(pl.multiple_of(i * tile, tile), tile)
        block = grad[pl.ds(2 * i, 2)].reshape(tile, width)
        gat[at, :] = mm_cols(block, wo[...]).astype(BF)
        grad_wout[...] += mm_rows(attended[at, :], block)
        return carry

    lax.fori_loop(0, count, project, 0)
    for h in range(2):
        dk[...] = jnp.zeros_like(dk)
        dv[...] = jnp.zeros_like(dv)
        for i in range(count):
            at, upto = slice(i * tile, (i + 1) * tile), slice(0, (i + 1) * tile)
            g = gat[at, h * DV : (h + 1) * DV]
            scores = mm_cols(qcat[h, at, :], kcat[h, upto, :]) * scale
            scores = jnp.where(causal(i, tile, keep), scores, masked_score)
            probs = jnp.exp(scores - lse[h, at, 0:1])
            grad_probs = mm_cols(g, value[h, upto, :])
            inner = jnp.sum(grad_probs * probs, axis=-1, keepdims=True)
            raw = (probs * (grad_probs - inner) * scale).astype(BF)
            grad_q = mm(raw, kcat[h, upto, :])
            grad_query[at, h * DH : (h + 1) * DH] = grad_q[:, :DH].astype(BF)
            rope = grad_q[:, DH:]
            lane = lax.broadcasted_iota(jnp.int32, rope.shape, 1)
            mine = (lane < DR) if h == 0 else (lane >= DR)
            rope = turn(rope, cos[at, :], sin[at, :], -1.0).astype(BF)
            if h == 0:
                grad_query[at, 2 * DH :] = rope
            else:
                grad_query[at, 2 * DH :] = jnp.where(mine, rope, grad_query[at, 2 * DH :])
            dk[upto, :] += mm_rows(raw, qcat[h, at, :])
            dv[upto, :] += mm_rows(probs.astype(BF), g)
        grad_expanded[:, h * (DH + DV) : h * (DH + DV) + DH] = dk[:, :DH].astype(BF)
        grad_expanded[:, h * (DH + DV) + DH : (h + 1) * (DH + DV)] = dv[...].astype(BF)
        rope = dk[:, DH:]
        if h == 0:
            grad_rope[...] = rope
        else:
            grad_rope[...] += pltpu.roll(rope, DR, 1)


def params(collective_id):
    return pltpu.CompilerParams(
        collective_id=collective_id, has_side_effects=True, vmem_limit_bytes=60 << 20
    )


def remote(src, dst, send_sem, recv_sem, device):
    return pltpu.make_async_remote_copy(
        src_ref=src,
        dst_ref=dst,
        send_sem=send_sem,
        recv_sem=recv_sem,
        device_id=device,
        device_id_type=MESH,
    )


def greet(devices):
    barrier = pltpu.get_barrier_semaphore()
    for device in devices:
        pl.semaphore_signal(barrier, inc=1, device_id=device, device_id_type=MESH)
    pl.semaphore_wait(barrier, len(devices))


def places(n_dp, n_ex):
    z = lax.axis_index("dp")
    e = lax.axis_index("expert")
    chips = n_ex // 2
    c, k = e // 2, lax.rem(e, 2)
    sibling = (z, e + 1 - 2 * k)
    same_core = [(z, lax.rem(c + i, chips) * 2 + k) for i in range(1, chips)]
    column = [(lax.rem(z + i, n_dp), e) for i in range(1, n_dp)]
    return z, e, c, k, sibling, same_core, column


def wait_recv(region, sem, device):
    remote(region, region, sem, sem, device).wait_recv()


def column_sum(array, n_dp, n_ex, inner, collective_id):
    shape = array.shape[1:]

    def kernel(x_ref, o_ref, buf, send, recv):
        z, e, c, k, sibling, same_core, _ = places(n_dp, n_ex)
        group = column_group(z, e, inner)
        greet(group[1:])
        copies = []
        for i in range(1, inner):
            to = lax.rem(z + i, inner)
            copy = remote(x_ref.at[to], buf.at[i], send.at[i], recv.at[i], group[i])
            copy.start()
            copies.append(copy)
        o_ref[...] = x_ref[lax.rem(z, inner)].astype(F32)
        for i in range(1, inner):
            copies[i - 1].wait_recv()
            o_ref[...] += buf[i].astype(F32)
        for copy in copies:
            copy.wait_send()

    return pl.pallas_call(
        kernel,
        out_shape=jax.ShapeDtypeStruct(shape, F32),
        in_specs=[VMEM],
        out_specs=VMEM,
        scratch_shapes=[pltpu.VMEM((inner,) + shape, BF)] + [pltpu.SemaphoreType.DMA((inner,))] * 2,
        compiler_params=params(collective_id),
    )(array)


def column_group(z, e, inner):
    start = z // inner * inner
    return [(start + lax.rem(z - start + i, inner), e) for i in range(inner)]


def first_exchange(tok, heads_w, pack, n_dp, n_ex, collective_id):
    chips = n_ex // 2

    def kernel(
        tok_ref, wa_ref, pk_ref, tok_out, wa_out, pk_out,
        t_send, t_recv, ts_send, ts_recv, a_send, a_recv, az_send, az_recv,
        p_send, p_recv, pf_send, pf_recv, ps_send, ps_recv, local,
    ):
        z, e, c, k, sibling, same_core, column = places(n_dp, n_ex)
        plane = [(z, lax.rem(e + i, n_ex)) for i in range(1, n_ex)]
        greet(plane + column)
        wa_far, pk_col, tok_far, near = [], [], [], []
        for i in range(1, n_ex):
            copy = remote(
                wa_ref.at[lax.rem(e + i, n_ex)], wa_out.at[z, e],
                a_send.at[i], a_recv.at[i], plane[i - 1],
            )
            copy.start()
            wa_far.append(copy)
        for i in range(1, n_dp):
            copy = remote(pk_ref, pk_out.at[z, e], p_send.at[i], p_recv.at[i], column[i - 1])
            copy.start()
            pk_col.append(copy)
        for i in range(1, chips):
            copy = remote(tok_ref, tok_out.at[e], t_send.at[i], t_recv.at[i], same_core[i - 1])
            copy.start()
            tok_far.append(copy)
        copy = remote(tok_ref, tok_out.at[e], ts_send.at[0], ts_recv.at[0], sibling)
        copy.start()
        near.append(copy)
        own = [
            pltpu.make_async_copy(wa_ref.at[e], wa_out.at[z, e], local.at[0]),
            pltpu.make_async_copy(pk_ref, pk_out.at[z, e], local.at[1]),
            pltpu.make_async_copy(tok_ref, tok_out.at[e], local.at[2]),
        ]
        for copy in own:
            copy.start()
        for copy in own:
            copy.wait()
        for copy in wa_far:
            copy.wait_recv()
        wa_col = []
        for i in range(1, n_dp):
            copy = remote(
                wa_out.at[z], wa_out.at[z], az_send.at[i], az_recv.at[i], column[i - 1]
            )
            copy.start()
            wa_col.append(copy)
        for copy in pk_col:
            copy.wait_recv()
        pk_far = []
        for i in range(1, chips):
            copy = remote(
                pk_out.at[:, e], pk_out.at[:, e], pf_send.at[i], pf_recv.at[i], same_core[i - 1]
            )
            copy.start()
            pk_far.append(copy)
        copy = remote(pk_out.at[:, e], pk_out.at[:, e], ps_send.at[0], ps_recv.at[0], sibling)
        copy.start()
        near.append(copy)
        for i in range(1, chips):
            source = lax.rem(c + chips - i, chips) * 2 + k
            tok_far[i - 1].wait_recv()
            copy = remote(
                tok_out.at[source], tok_out.at[source], ts_send.at[i], ts_recv.at[i], sibling
            )
            copy.start()
            near.append(copy)
            pk_far[i - 1].wait_recv()
            copy = remote(
                pk_out.at[:, source], pk_out.at[:, source], ps_send.at[i], ps_recv.at[i], sibling
            )
            copy.start()
            near.append(copy)
        for copy in near + wa_col:
            copy.wait()
        for copy in wa_far + pk_col + tok_far + pk_far:
            copy.wait_send()

    dma = pltpu.SemaphoreType.DMA
    return pl.pallas_call(
        kernel,
        out_shape=[
            jax.ShapeDtypeStruct((n_ex,) + tok.shape, tok.dtype),
            jax.ShapeDtypeStruct((n_dp,) + heads_w.shape, heads_w.dtype),
            jax.ShapeDtypeStruct((n_dp, n_ex) + pack.shape, pack.dtype),
        ],
        in_specs=[ANY] * 3,
        out_specs=[ANY] * 3,
        scratch_shapes=[dma((chips,))] * 4
        + [dma((n_ex,))] * 2
        + [dma((n_dp,))] * 4
        + [dma((chips,))] * 4
        + [dma((3,))],
        compiler_params=params(collective_id),
    )(tok, heads_w, pack)


class ExpertsIn:
    @staticmethod
    def scratch(n_dp):
        dma = pltpu.SemaphoreType.DMA
        return [dma((n_dp, 2)), dma((n_dp,)), dma((n_dp,)), dma((n_dp,))]

    @staticmethod
    def out(weight, n_dp, n_ex):
        return jax.ShapeDtypeStruct((n_ex, n_dp) + weight.shape[2:], BF)

    def __init__(self, weight, out, scratch, n_dp, n_ex, inner):
        self.weight, self.out, self.n_dp, self.inner = weight, out, n_dp, inner
        self.send, self.recv, self.sib_send, self.sib_recv = scratch
        self.z, self.e, self.c, self.k, self.sibling, _, _ = places(n_dp, n_ex)
        self.hh = n_ex // 2
        self.local = weight.shape[0]

    def sends(self, start):
        for i in list(range(1, self.n_dp)) + [0]:
            to = lax.rem(self.z + i, self.n_dp)
            expert = lax.rem(to, self.inner)

            def go(i=i, to=to, expert=expert):
                for h in range(2):
                    src = self.weight.at[lax.rem(expert, self.local), pl.ds(h * self.hh, self.hh)]
                    dst = self.out.at[pl.ds(h * self.hh, self.hh), self.z]
                    sem = self.recv.at[self.z]

                    def far(src=src, dst=dst, h=h):
                        copy = remote(src, dst, self.send.at[i, h], sem, (to, 2 * self.c + h))
                        if start:
                            copy.start()
                        else:
                            copy.wait_send()

                    if i:
                        far()
                    else:
                        pl.when(self.k != h)(far)
                        if start:

                            @pl.when(self.k == h)
                            def _(src=src, dst=dst):
                                pltpu.make_async_copy(src, dst, sem).start()

            pl.when(expert // self.local == self.k)(go)

    def begin(self):
        self.sends(True)

    def pass_on(self):
        mine = lax.rem(self.z, self.inner)
        for i in range(self.n_dp):
            d = lax.rem(self.z + self.n_dp - i, self.n_dp)
            region = self.out.at[pl.ds(self.k * self.hh, self.hh), d]
            if i:
                wait_recv(region, self.recv.at[d], self.sibling)
            else:
                from_here = mine // self.local == self.k

                @pl.when(from_here)
                def _(region=region, d=d):
                    src = self.weight.at[
                        lax.rem(mine, self.local), pl.ds(self.k * self.hh, self.hh)
                    ]
                    pltpu.make_async_copy(src, region, self.recv.at[d]).wait()

                @pl.when(jnp.logical_not(from_here))
                def _(region=region, d=d):
                    wait_recv(region, self.recv.at[d], self.sibling)

            remote(
                region, region, self.sib_send.at[i], self.sib_recv.at[i], self.sibling
            ).start()

    def end(self):
        self.sends(False)
        for i in range(self.n_dp):
            d = lax.rem(self.z + self.n_dp - i, self.n_dp)
            mine = self.out.at[pl.ds(self.k * self.hh, self.hh), d]
            remote(
                mine, mine, self.sib_send.at[i], self.sib_recv.at[i], self.sibling
            ).wait_send()
            region = self.out.at[pl.ds((1 - self.k) * self.hh, self.hh), d]
            wait_recv(region, self.sib_recv.at[i], self.sibling)


def forward_exchange(attend, w_out, tok, gain, experts, shared, n_dp, n_ex, inner, collective_id):
    chips = n_ex // 2
    rows, width = tok.shape
    count = len(experts)
    r = w_out.shape[0]
    parts = DV // r
    hp = n_dp // parts
    seq = n_ex * rows

    def kernel(*refs):
        att_in, refs = refs[:9], refs[9:]
        wo_in, tok_ref, gain_ref = refs[:3]
        e_in, s_in = refs[3 : 3 + count], refs[3 + count : 6 + count]
        refs = refs[6 + count :]
        att_out, refs = refs[:8], refs[8:]
        wo_out, res_ref, xcol_ref = refs[:3]
        w_out, s_out = refs[3 : 3 + count], refs[3 + count : 6 + count]
        refs = refs[6 + count :]
        x_ref, from_sib, out_buf, from_far, xbuf = refs[:5]
        (
            near_s, near_r, far_s, far_r, x_s, x_r,
            sh_s, sh_r, sp_s, sp_r, sf_s, sf_r, wo_s, wo_r, local,
        ) = refs[5:20]
        refs = refs[20:]
        z, e, c, k, sibling, same_core, column = places(n_dp, n_ex)
        group = column_group(z, e, inner)
        part = lax.rem(e, parts)
        members = [
            (lax.rem(z + i, n_dp), e - part + lax.rem(part + j, parts))
            for i in range(n_dp)
            for j in range(parts)
        ]
        greet(same_core + column + [(device[0], sibling[1]) for device in column] + members[1:])

        def wo_sends(start):
            for i in range(n_dp):
                target = (lax.rem(z + i, n_dp), e - part + z // hp)
                dst, sem = wo_out.at[lax.rem(z, hp), part], wo_r.at[lax.rem(z, hp), part]

                def far(i=i, target=target, dst=dst, sem=sem):
                    copy = remote(wo_in, dst, wo_s.at[i], sem, target)
                    if start:
                        copy.start()
                    else:
                        copy.wait_send()

                if i:
                    far()
                else:
                    pl.when(z // hp != part)(far)
                    if start:

                        @pl.when(z // hp == part)
                        def _(dst=dst, sem=sem):
                            pltpu.make_async_copy(wo_in, dst, sem).start()

        def wo_arrivals():
            for h in range(hp):
                for p in range(parts):
                    here = jnp.logical_and(part * hp + h == z, part == p)

                    @pl.when(here)
                    def _(h=h, p=p):
                        pltpu.make_async_copy(wo_in, wo_out.at[h, p], wo_r.at[h, p]).wait()

                    @pl.when(jnp.logical_not(here))
                    def _(h=h, p=p):
                        wait_recv(wo_out.at[h, p], wo_r.at[h, p], sibling)

        my_l = lax.rem(z, inner)
        matrices = [
            ExpertsIn(e_in[m], w_out[m], refs[4 * m : 4 * m + 4], n_dp, n_ex, inner)
            for m in range(count)
        ]
        wo_sends(True)
        shared_copies = []
        for i in range(1, n_dp):
            for m in range(3):
                copy = remote(
                    s_in[m].at[lax.rem(lax.rem(z + i, n_dp), inner)], s_out[m].at[e, z],
                    sh_s.at[m, i], sh_r.at[m, i], column[i - 1],
                )
                copy.start()
                shared_copies.append(copy)
        own = [
            pltpu.make_async_copy(s_in[m].at[my_l], s_out[m].at[e, z], local.at[m])
            for m in range(3)
        ]
        for copy in own:
            copy.start()
        matrices[0].begin()
        attend_forward(*att_in, *att_out)
        wo_arrivals()
        wo = wo_out[...].reshape(hp * DV, width)

        def project(i, carry):
            at = pl.ds(pl.multiple_of(i * 2 * rows, 2 * rows), 2 * rows)
            block = mm(att_out[7][at, :], wo).astype(BF)
            x_ref[pl.ds(2 * i, 2)] = block.reshape(2, rows, width)
            return carry

        lax.fori_loop(0, chips, project, 0)
        near = []
        for i in list(range(1, chips)) + [0]:
            chip = lax.rem(c + i, chips)
            copy = remote(
                x_ref.at[chip * 2 + 1 - k], from_sib.at[chip], near_s.at[i], near_r.at[i], sibling
            )
            copy.start()
            near.append(copy)
        far = []
        for i in range(1, chips):
            chip = lax.rem(c + i, chips)
            near[i - 1].wait_recv()
            out_buf[i] = (
                x_ref[chip * 2 + k].astype(F32) + from_sib[chip].astype(F32)
            ).astype(BF)
            copy = remote(out_buf.at[i], from_far.at[i], far_s.at[i], far_r.at[i], same_core[i - 1])
            copy.start()
            far.append(copy)
        near[chips - 1].wait_recv()
        res_ref[...] = x_ref[e].astype(F32) + from_sib[c].astype(F32) + tok_ref[...].astype(F32)
        for i in range(1, chips):
            far[i - 1].wait_recv()
            res_ref[...] += from_far[i].astype(F32)
        residual = res_ref[...]
        scale = lax.rsqrt(jnp.mean(residual * residual, axis=-1, keepdims=True) + norm_eps)
        xbuf[...] = (residual * scale * gain_ref[...]).astype(BF)
        x_copies = []
        for i in range(1, inner):
            copy = remote(xbuf, xcol_ref.at[my_l], x_s.at[i], x_r.at[i], group[i])
            copy.start()
            x_copies.append(copy)
        x_own = pltpu.make_async_copy(xbuf, xcol_ref.at[my_l], local.at[3])
        x_own.start()
        for matrix in matrices[1:]:
            matrix.begin()
        for copy in own:
            copy.wait()
        for copy in shared_copies:
            copy.wait_recv()
        plane, to_sib = [], []
        for m in range(3):
            block = s_out[m].at[e]
            for i in range(1, chips):
                copy = remote(block, block, sp_s.at[m, i], sp_r.at[m, i], same_core[i - 1])
                copy.start()
                plane.append(copy)
            copy = remote(block, block, sf_s.at[m, 0], sf_r.at[m, 0], sibling)
            copy.start()
            to_sib.append(copy)
        for m in range(3):
            for i in range(1, chips):
                plane[m * (chips - 1) + i - 1].wait_recv()
                block = s_out[m].at[lax.rem(c + chips - i, chips) * 2 + k]
                copy = remote(block, block, sf_s.at[m, i], sf_r.at[m, i], sibling)
                copy.start()
                to_sib.append(copy)
        for matrix in matrices:
            matrix.pass_on()
        for copy in x_copies + to_sib:
            copy.wait()
        x_own.wait()
        for copy in plane + shared_copies + near + far:
            copy.wait_send()
        wo_sends(False)
        for matrix in matrices:
            matrix.end()

    dma = pltpu.SemaphoreType.DMA
    ff_s = shared[0].shape[2]
    scratch = []
    for _ in experts:
        scratch += ExpertsIn.scratch(n_dp)
    sds = jax.ShapeDtypeStruct
    outs = pl.pallas_call(
        kernel,
        out_shape=[
            sds((seq, width), BF),
            sds((seq, attend[3].shape[1]), F32),
            sds((seq, KVR), BF),
            sds((2, seq, 2 * DH), BF),
            sds((2, seq, 2 * DH), BF),
            sds((2, seq, DV), BF),
            sds((2, seq, 128), F32),
            sds((seq, 2 * DV), BF),
            sds((hp, parts, r, width), BF),
            sds((rows, width), F32),
            sds((inner, rows, width), BF),
        ]
        + [ExpertsIn.out(w, n_dp, n_ex) for w in experts]
        + [sds((n_ex, n_dp, r, ff_s), BF)] * 3,
        in_specs=[VMEM] * 9 + [ANY] + [VMEM] * 2 + [ANY] * (3 + count),
        out_specs=[VMEM] * 10 + [ANY] * (4 + count),
        scratch_shapes=[pltpu.VMEM((n_ex, rows, width), BF)]
        + [pltpu.VMEM((chips, rows, width), BF)] * 3
        + [pltpu.VMEM((rows, width), BF)]
        + [dma((chips,))] * 4
        + [dma((inner,))] * 2
        + [dma((3, n_dp))] * 2
        + [dma((3, chips))] * 4
        + [dma((n_dp,)), dma((hp, parts)), dma((4,))]
        + scratch,
        compiler_params=params(collective_id),
    )(*attend, w_out, tok, gain, *experts, *shared)
    return outs[:8], outs[8], outs[9], outs[10], outs[11 : 11 + count], outs[11 + count :]


def between(blocks, way, weights, totals, n_dp, n_ex, inner, collective_id):
    chips = n_ex // 2
    n_in, n_back = len(weights), len(totals)

    def kernel(x_ref, *refs):
        w_in, t_in = refs[:n_in], refs[n_in : n_in + n_back]
        refs = refs[n_in + n_back :]
        o_ref, w_out, t_out = refs[0], refs[1 : 1 + n_in], refs[1 + n_in : 1 + n_in + n_back]
        refs = refs[1 + n_in + n_back :]
        send, recv, local = refs[:3]
        z, e, c, k, sibling, same_core, column = places(n_dp, n_ex)
        greet(same_core + [sibling] + column + [(device[0], sibling[1]) for device in column])
        refs = refs[3:]
        works = [
            ExpertsIn(w_in[m], w_out[m], refs[4 * m : 4 * m + 4], n_dp, n_ex, inner)
            for m in range(n_in)
        ]
        refs = refs[4 * n_in :]
        works += [
            ExpertsBack(t_in[m], t_out[m], refs[7 * m : 7 * m + 7], n_dp, n_ex, inner)
            for m in range(n_back)
        ]
        copies = []
        for i in range(1, chips):
            to = same_core[i - 1] if way > 0 else same_core[chips - i - 1]
            copy = remote(x_ref.at[i], o_ref.at[i], send.at[i], recv.at[i], to)
            copy.start()
            copies.append(copy)
        copy = pltpu.make_async_copy(x_ref.at[0], o_ref.at[0], local)
        copy.start()
        copies.append(copy)
        for work in works:
            work.begin()
        for work in works:
            work.pass_on()
        for copy in copies:
            copy.wait()
        for work in works:
            work.end()

    dma = pltpu.SemaphoreType.DMA
    scratch = [dma((chips,)), dma((chips,)), dma]
    for _ in weights:
        scratch += ExpertsIn.scratch(n_dp)
    for total in totals:
        scratch += ExpertsBack.scratch(total, n_dp, inner)
    outs = pl.pallas_call(
        kernel,
        out_shape=[jax.ShapeDtypeStruct(blocks.shape, BF)]
        + [ExpertsIn.out(w, n_dp, n_ex) for w in weights]
        + [ExpertsBack.out(total, n_dp, inner) for total in totals],
        in_specs=[ANY] * (1 + n_in + n_back),
        out_specs=[ANY] * (1 + n_in + n_back),
        scratch_shapes=scratch,
        compiler_params=params(collective_id),
    )(blocks, *weights, *totals)
    return outs[0], outs[1:]


class ExpertsBack:
    @staticmethod
    def scratch(total, n_dp, inner):
        n_ex, _, r, ff = total.shape
        dma = pltpu.SemaphoreType.DMA
        return [
            pltpu.VMEM((n_ex // 2, n_dp, r, ff), BF),
            pltpu.VMEM((n_ex // 2, n_dp, r, ff), BF),
            dma((n_dp,)),
            dma((n_dp,)),
            dma((n_dp,)),
            dma((n_dp,)),
            dma((n_dp // inner, 2, 2)),
        ]

    @staticmethod
    def out(total, n_dp, inner):
        n_ex, _, r, ff = total.shape
        return jax.ShapeDtypeStruct((n_dp // inner, 2, n_ex, r, ff), BF)

    def __init__(self, total, out, scratch, n_dp, n_ex, inner):
        self.total, self.out, self.n_dp, self.inner = total, out, n_dp, inner
        self.own, self.sib, self.near_s, self.near_r, self.load, self.send, self.recv = scratch
        self.z, self.e, self.c, self.k, self.sibling, _, _ = places(n_dp, n_ex)
        self.hh = n_ex // 2

    def near(self, i):
        d = lax.rem(self.z + i, self.n_dp)
        return remote(
            self.total.at[pl.ds((1 - self.k) * self.hh, self.hh), d],
            self.sib.at[:, d], self.near_s.at[i], self.near_r.at[i], self.sibling,
        )

    def loads(self, i):
        d = lax.rem(self.z + i, self.n_dp)
        return pltpu.make_async_copy(
            self.total.at[pl.ds(self.k * self.hh, self.hh), d], self.own.at[:, d], self.load.at[i]
        )

    def order(self):
        return list(range(1, self.n_dp)) + [0]

    def begin(self):
        for i in self.order():
            self.near(i).start()
            self.loads(i).start()

    def route(self, i):
        d = lax.rem(self.z + i, self.n_dp)
        expert = lax.rem(self.z, self.inner)
        dst = self.out.at[
            self.z // self.inner, lax.rem(expert, 2), pl.ds(self.k * self.hh, self.hh)
        ]
        sem = self.recv.at[self.z // self.inner, lax.rem(expert, 2), self.k]
        return self.own.at[:, d], dst, sem, d, expert // 2

    def stay(self):
        src, dst, sem, _, _ = self.route(0)
        return pltpu.make_async_copy(src, dst, sem)

    def go(self, i):
        src, dst, sem, d, core = self.route(i)
        return remote(src, dst, self.send.at[i], sem, (d, 2 * self.c + core))

    def here(self):
        return lax.rem(self.z, self.inner) // 2 == self.k

    def pass_on(self):
        for i in self.order():
            d = lax.rem(self.z + i, self.n_dp)
            self.near(i).wait_recv()
            self.loads(i).wait()
            for j in range(self.hh):
                self.own[j, d] = (
                    self.own[j, d].astype(F32) + self.sib[j, d].astype(F32)
                ).astype(BF)
            if i:
                self.go(i).start()
            else:
                pl.when(self.here())(lambda: self.stay().start())
                pl.when(jnp.logical_not(self.here()))(lambda: self.go(0).start())

    def end(self):
        for i in self.order():
            self.near(i).wait_send()
            if i:
                self.go(i).wait_send()
            else:
                pl.when(jnp.logical_not(self.here()))(lambda: self.go(0).wait_send())
        for o in range(self.n_dp // self.inner):
            for j in range(2):
                for h in range(2):
                    region = self.out.at[o, j, pl.ds(h * self.hh, self.hh)]
                    source = o * self.inner + 2 * self.k + j
                    here = jnp.logical_and(source == self.z, self.k == h)

                    @pl.when(here)
                    def _(region=region, o=o, j=j, h=h):
                        d = self.z
                        pltpu.make_async_copy(
                            self.own.at[:, d], region, self.recv.at[o, j, h]
                        ).wait()

                    @pl.when(jnp.logical_not(here))
                    def _(region=region, o=o, j=j, h=h):
                        wait_recv(region, self.recv.at[o, j, h], self.sibling)


def backward_exchange(grad, attend, hidden, latent_low, totals, n_dp, n_ex, inner, collective_id):
    chips = n_ex // 2
    rows, width = grad.shape
    seq = n_ex * rows
    extra = len(totals)
    wq, we = attend[1], attend[2]
    lat_cols = KVR + 2 * DR

    def kernel(*refs):
        grad_ref, att_in, refs = refs[0], refs[1:12], refs[12:]
        hidden_ref, low_ref, t_refs = refs[0], refs[1], refs[2 : 2 + extra]
        refs = refs[2 + extra :]
        sums, wout_ref, wq_ref, we_ref = refs[:2], refs[2], refs[3], refs[4]
        back_refs, refs = refs[5 : 5 + extra], refs[5 + extra :]
        gbuf, att_tmp, refs = refs[0], refs[1:8], refs[8:]
        x_refs, bufs, refs = refs[:2], refs[2:8], refs[8:]
        t_s, t_r, ts_s, ts_r, local = refs[:5]
        sems, rest = refs[5:13], refs[13:]
        z, e, c, k, sibling, same_core, column = places(n_dp, n_ex)
        greet(same_core + [sibling] + column + [(d[0], sibling[1]) for d in column])
        backs = [
            ExpertsBack(t_refs[m], back_refs[m], rest[7 * m : 7 * m + 7], n_dp, n_ex, inner)
            for m in range(extra)
        ]
        gather, to_sib = [], []
        for i in range(1, chips):
            copy = remote(grad_ref, gbuf.at[e], t_s.at[i], t_r.at[i], same_core[i - 1])
            copy.start()
            gather.append(copy)
        copy = remote(grad_ref, gbuf.at[e], ts_s.at[0], ts_r.at[0], sibling)
        copy.start()
        to_sib.append(copy)
        own = pltpu.make_async_copy(grad_ref, gbuf.at[e], local)
        own.start()
        for back in backs:
            back.begin()
        for i in range(1, chips):
            gather[i - 1].wait_recv()
            block = gbuf.at[lax.rem(c + chips - i, chips) * 2 + k]
            copy = remote(block, block, ts_s.at[i], ts_r.at[i], sibling)
            copy.start()
            to_sib.append(copy)
        for back in backs:
            back.pass_on()
        own.wait()
        for copy in to_sib:
            copy.wait_recv()
        for copy in gather + to_sib:
            copy.wait_send()
        gat, grad_wout, dk, dv, grad_query, grad_expanded, grad_rope = att_tmp
        attend_backward(gbuf, *att_in, *att_tmp)

        def spread(i, carry):
            at = pl.ds(pl.multiple_of(i * 2 * rows, 2 * rows), 2 * rows)
            block = mm_cols(grad_query[at, :], att_in[1][...]).astype(BF)
            x_refs[0][pl.ds(2 * i, 2)] = block.reshape(2, rows, width)
            block = mm_cols(grad_expanded[at, :], att_in[2][...]).astype(BF)
            x_refs[1][pl.ds(2 * i, 2), :, :KVR] = block.reshape(2, rows, KVR)
            block = grad_rope[at, :].astype(BF)
            x_refs[1][pl.ds(2 * i, 2), :, KVR:] = block.reshape(2, rows, 2 * DR)
            return carry

        lax.fori_loop(0, chips, spread, 0)
        near, far = {}, {}
        for i in list(range(1, chips)) + [0]:
            chip = lax.rem(c + i, chips)
            for j in range(2):
                near[i, j] = remote(
                    x_refs[j].at[chip * 2 + 1 - k],
                    bufs[3 * j].at[chip],
                    sems[4 * j].at[i],
                    sems[4 * j + 1].at[i],
                    sibling,
                )
                near[i, j].start()
        for i in range(1, chips):
            chip = lax.rem(c + i, chips)
            for j in range(2):
                from_sib, out_buf, from_far = bufs[3 * j : 3 * j + 3]
                near[i, j].wait_recv()
                out_buf[i] = (
                    x_refs[j][chip * 2 + k].astype(F32) + from_sib[chip].astype(F32)
                ).astype(BF)
                far[i, j] = remote(
                    out_buf.at[i],
                    from_far.at[i],
                    sems[4 * j + 2].at[i],
                    sems[4 * j + 3].at[i],
                    same_core[i - 1],
                )
                far[i, j].start()
        wout_ref[...] = grad_wout[...].astype(BF)
        we_ref[...] = mm_rows(low_ref[...], grad_expanded[...]).astype(BF)

        def wq_rows(i, carry):
            at = pl.ds(pl.multiple_of(i * 256, 256), 256)
            wq_ref[at, :] = mm_rows(hidden_ref[:, at], grad_query[...]).astype(BF)
            return carry

        lax.fori_loop(0, width // 256, wq_rows, 0)
        for j in range(2):
            near[0, j].wait_recv()
            sums[j][...] = x_refs[j][e].astype(F32) + bufs[3 * j][c].astype(F32)
        for i in range(1, chips):
            for j in range(2):
                far[i, j].wait_recv()
                sums[j][...] += bufs[3 * j + 2][i].astype(F32)
        for copy in list(near.values()) + list(far.values()):
            copy.wait_send()
        for back in backs:
            back.end()

    dma = pltpu.SemaphoreType.DMA
    sds = jax.ShapeDtypeStruct
    vmem = pltpu.VMEM
    scratch = [
        vmem((n_ex, rows, width), BF),
        vmem((seq, 2 * DV), BF),
        vmem((2 * DV, width), F32),
        vmem((seq, 2 * DH), F32),
        vmem((seq, DV), F32),
        vmem((seq, wq.shape[1]), BF),
        vmem((seq, we.shape[1]), BF),
        vmem((seq, 2 * DR), F32),
        vmem((n_ex, rows, width), BF),
        vmem((n_ex, rows, lat_cols), BF),
    ]
    scratch += [vmem((chips, rows, width), BF)] * 3 + [vmem((chips, rows, lat_cols), BF)] * 3
    scratch += [dma((chips,))] * 4 + [dma] + [dma((chips,))] * 8
    for total in totals:
        scratch += ExpertsBack.scratch(total, n_dp, inner)
    outs = pl.pallas_call(
        kernel,
        out_shape=[
            sds((rows, width), F32),
            sds((rows, lat_cols), F32),
            sds((2 * DV, width), BF),
            sds(wq.shape, BF),
            sds(we.shape, BF),
        ]
        + [ExpertsBack.out(total, n_dp, inner) for total in totals],
        in_specs=[ANY] + [VMEM] * 13 + [ANY] * extra,
        out_specs=[VMEM] * 5 + [ANY] * extra,
        scratch_shapes=scratch,
        compiler_params=params(collective_id),
    )(grad, *attend, hidden, latent_low, *totals)
    return outs[:5], outs[5:]


def last_exchange(heads, wout, pack, shared, totals, n_dp, n_ex, inner, collective_id):
    chips = n_ex // 2
    extra = len(totals)
    rows, cols = pack.shape[1:]
    r = rows // n_dp

    def kernel(heads_ref, wout_ref, pack_ref, *refs):
        sh_in, t_refs = refs[:3], refs[3 : 3 + extra]
        refs = refs[3 + extra :]
        heads_out, wout_out, pack_out = refs[:3]
        sh_out, back_refs = refs[3:6], refs[6 : 6 + extra]
        refs = refs[6 + extra :]
        hbuf, hsum, wbuf, psib, pout, pfar, psum, pbuf = refs[:8]
        (
            h_s, h_r, hp_s, hp_r, w_s, w_r, pn_s, pn_r, pf_s, pf_r, pc_s, pc_r, s_s, s_r, local,
        ) = refs[8:23]
        rest = refs[23:]
        z, e, c, k, sibling, same_core, column = places(n_dp, n_ex)
        plane = [(z, lax.rem(e + i, n_ex)) for i in range(1, n_ex)]
        greet(plane + column + [(d[0], sibling[1]) for d in column])
        backs = [
            ExpertsBack(t_refs[m], back_refs[m], rest[7 * m : 7 * m + 7], n_dp, n_ex, inner)
            for m in range(extra)
        ]
        near, far = [], []
        for i in list(range(1, chips)) + [0]:
            chip = lax.rem(c + i, chips)
            copy = remote(
                pack_ref.at[chip * 2 + 1 - k], psib.at[chip], pn_s.at[i], pn_r.at[i], sibling
            )
            copy.start()
            near.append(copy)
        heads_col, others = [], []
        for i in range(1, n_dp):
            to = lax.rem(z + i, n_dp)
            copy = remote(heads_ref.at[to], hbuf.at[i], h_s.at[i], h_r.at[i], column[i - 1])
            copy.start()
            heads_col.append(copy)
        for back in backs:
            back.begin()
        for i in range(1, chips):
            chip = lax.rem(c + i, chips)
            near[i - 1].wait_recv()
            pout[i] = (
                pack_ref[chip * 2 + k].astype(F32) + psib[chip].astype(F32)
            ).astype(BF)
            copy = remote(pout.at[i], pfar.at[i], pf_s.at[i], pf_r.at[i], same_core[i - 1])
            copy.start()
            far.append(copy)
        near[chips - 1].wait_recv()
        total = pack_ref[e].astype(F32) + psib[c].astype(F32)
        for i in range(1, chips):
            far[i - 1].wait_recv()
            total = total + pfar[i].astype(F32)
        psum[...] = total.astype(BF).reshape(n_dp, r, cols)
        pack_col, wout_col = [], []
        for i in range(1, n_dp):
            to = lax.rem(z + i, n_dp)
            copy = remote(psum.at[to], pbuf.at[i], pc_s.at[i], pc_r.at[i], column[i - 1])
            copy.start()
            pack_col.append(copy)
            copy = remote(wout_ref.at[to], wbuf.at[i], w_s.at[i], w_r.at[i], column[i - 1])
            copy.start()
            wout_col.append(copy)
            for m in range(3):
                copy = remote(
                    sh_in[m].at[to], sh_out[m].at[z], s_s.at[m, i], s_r.at[m, i], column[i - 1]
                )
                copy.start()
                others.append(copy)
        for m in range(3):
            copy = pltpu.make_async_copy(sh_in[m].at[z], sh_out[m].at[z], local.at[m])
            copy.start()
            others.append(copy)
        for copy in heads_col:
            copy.wait_recv()
        for j in range(n_ex):
            block = heads_ref[z, j].astype(F32)
            for i in range(1, n_dp):
                block = block + hbuf[i, j].astype(F32)
            hsum[j] = block.astype(BF)
        heads_plane = []
        for i in range(1, n_ex):
            copy = remote(
                hsum.at[lax.rem(e + i, n_ex)], heads_out.at[e], hp_s.at[i], hp_r.at[i],
                plane[i - 1],
            )
            copy.start()
            heads_plane.append(copy)
        keep = pltpu.make_async_copy(hsum.at[e], heads_out.at[e], local.at[3])
        keep.start()
        for back in backs:
            back.pass_on()
        for copy in wout_col + pack_col:
            copy.wait_recv()
        wout_sum = wout_ref[z].astype(F32)
        pack_sum = psum[z].astype(F32)
        for i in range(1, n_dp):
            wout_sum = wout_sum + wbuf[i].astype(F32)
            pack_sum = pack_sum + pbuf[i].astype(F32)
        wout_out[...] = wout_sum
        pack_out[...] = pack_sum
        for copy in near + far + heads_col + wout_col + pack_col:
            copy.wait_send()
        keep.wait()
        for copy in heads_plane + others:
            copy.wait()
        for back in backs:
            back.end()

    dma = pltpu.SemaphoreType.DMA
    scratch = [
        pltpu.VMEM(heads.shape, BF),
        pltpu.VMEM(heads.shape[1:], BF),
        pltpu.VMEM(wout.shape, BF),
        pltpu.VMEM((chips, rows, cols), BF),
        pltpu.VMEM((chips, rows, cols), BF),
        pltpu.VMEM((chips, rows, cols), BF),
        pltpu.VMEM((n_dp, r, cols), BF),
        pltpu.VMEM((n_dp, r, cols), BF),
        dma((n_dp,)), dma((n_dp,)), dma((n_ex,)), dma((n_ex,)), dma((n_dp,)), dma((n_dp,)),
        dma((chips,)), dma((chips,)), dma((chips,)), dma((chips,)), dma((n_dp,)), dma((n_dp,)),
        dma((3, n_dp)), dma((3, n_dp)), dma((4,)),
    ]
    for total in totals:
        scratch += ExpertsBack.scratch(total, n_dp, inner)
    outs = pl.pallas_call(
        kernel,
        out_shape=[
            jax.ShapeDtypeStruct(heads.shape[1:], BF),
            jax.ShapeDtypeStruct(wout.shape[1:], F32),
            jax.ShapeDtypeStruct((r, cols), F32),
        ]
        + [jax.ShapeDtypeStruct(array.shape, BF) for array in shared]
        + [ExpertsBack.out(total, n_dp, inner) for total in totals],
        in_specs=[VMEM] * 3 + [ANY] * (3 + extra),
        out_specs=[ANY, VMEM, VMEM] + [ANY] * (3 + extra),
        scratch_shapes=scratch,
        compiler_params=params(collective_id),
    )(heads, wout, pack, *shared, *totals)
    return outs[0], outs[1], outs[2], outs[3:6], outs[6:]


def shards(
    tokens,
    cotangent,
    lengths,
    routes,
    place_order,
    attn_gain,
    w_query,
    w_latent,
    latent_gain,
    w_expand,
    w_out,
    ffn_gain,
    w_router,
    shared_gate,
    shared_up,
    shared_down,
    expert_gate,
    expert_up,
    expert_down,
):
    rows, width = tokens.shape
    n_dp = lax.axis_size("dp")
    n_ex = lax.axis_size("expert")
    chips = n_ex // 2
    z = lax.axis_index("dp")
    e = lax.axis_index("expert")
    chip = e // 2
    n_experts = w_router.shape[1]
    top_k = routes.shape[1]
    capacity = (rows * top_k * 5 + 4 * n_experts - 1) // (4 * n_experts)
    cap = (capacity + 15) // 16 * 16
    seq = rows * n_ex
    r = w_query.shape[0]
    rl = w_expand.shape[0]
    hp = H // n_ex
    parts = DV // r
    heads = [
        (d * n_ex + (j // parts) * parts) * r // DV
        for j in range(n_ex)
        for d in range(j % parts * hp, j % parts * hp + hp)
    ]
    heads_back = [heads.index(h) for h in range(H)]
    inner = n_experts // chips
    my_local = lax.rem(z, inner)
    part_groups = [[i * parts + m for m in range(parts)] for i in range(n_ex // parts)]
    ff_e = expert_gate.shape[2]
    ff_s = shared_gate.shape[1] // inner
    lat = KVR + DR
    head_cols = hp * (DH + DR)
    kv_cols = hp * (DH + DV)

    def to_owner_order(values):
        cut = values.reshape(values.shape[0], n_dp, n_ex, r)
        return cut.transpose(0, 2, 1, 3).reshape(values.shape)

    def from_owner_order(values):
        cut = values.reshape(values.shape[0], n_ex, n_dp, r)
        return cut.transpose(0, 2, 1, 3).reshape(values.shape)

    def pick(values, index, axis=0):
        return lax.dynamic_index_in_dim(values, index, axis, keepdims=False)

    wq_send = jnp.take(w_query.reshape(r, H, DH + DR), jnp.array(heads), axis=1)
    wq_send = wq_send.reshape(r, n_ex, hp, DH + DR)
    wq_send = jnp.concatenate(
        [
            wq_send[..., :DH].reshape(r, n_ex, hp * DH),
            wq_send[..., DH:].reshape(r, n_ex, hp * DR),
        ],
        axis=-1,
    ).transpose(1, 0, 2)
    we_send = jnp.take(w_expand.reshape(rl, H, DH + DV), jnp.array(heads), axis=1)
    we_send = we_send.reshape(rl, n_ex, kv_cols).transpose(1, 0, 2)
    we_send = we_send.reshape(n_ex, r, rl * kv_cols // r)
    wa_send = jnp.concatenate([wq_send, we_send], axis=-1)
    slot_own = slot_places(routes, place_order[0], capacity)
    slot_place = jnp.where(slot_own >= 0, slot_own - routes * capacity, -1)
    slot_cols = 2 * rows * top_k // r
    slot_pack = jnp.stack([routes, slot_place]).astype(BF).reshape(2, r, slot_cols // 2)
    small_cols = lat + n_experts + 3
    pack_cols = (small_cols + slot_cols + 127) // 128 * 128
    pack = jnp.concatenate(
        [
            w_latent,
            w_router,
            attn_gain[:, None],
            ffn_gain[:, None],
            jnp.pad(latent_gain, (0, r - rl))[:, None],
            slot_pack[0],
            slot_pack[1],
            jnp.zeros((r, pack_cols - small_cols - slot_cols), BF),
        ],
        axis=1,
    )
    cot_owner = to_owner_order(cotangent)
    tok_all, wa_all, pk_all = first_exchange(tokens, wa_send, pack, n_dp, n_ex, 1)
    wq = wa_all[..., :head_cols].reshape(width, head_cols)
    wexp = wa_all[..., head_cols:].reshape(KVR, kv_cols)
    pk_flat = pk_all.reshape(width, pack_cols)
    w_lat = pk_flat[:, :lat]
    gain_one = pk_flat[:, lat + n_experts].astype(F32)
    gain_two = pk_all[..., lat + n_experts + 1].transpose(1, 0, 2).reshape(width).astype(F32)
    router = pk_all[..., lat : lat + n_experts].transpose(1, 0, 2, 3).reshape(width, n_experts)
    gain_lat = (
        pk_all[..., lat + n_experts + 2].reshape(n_dp * n_ex, r)[:, :rl].reshape(KVR).astype(F32)
    )
    col_groups = [[o * inner + i for i in range(inner)] for o in range(n_dp // inner)]
    cot_send, _ = lax.optimization_barrier((cot_owner, pk_all))
    cot_col = lax.all_gather(cot_send, "dp", axis=0, tiled=True, axis_index_groups=col_groups)
    slots_all = n_experts * capacity
    slot_col = pick(pk_all[..., small_cols : small_cols + slot_cols], e, 1)
    slot_col = lax.dynamic_slice_in_dim(slot_col, z - my_local, inner, 0).astype(jnp.int32)
    slot_col = slot_col.reshape(inner, r, 2, slot_cols // 2).transpose(2, 0, 1, 3)
    slot_col = slot_col.reshape(2, inner, rows, top_k)
    slot_ids = jnp.where(
        slot_col[1] >= 0,
        slot_col[0] * capacity + slot_col[1] + (jnp.arange(inner) * slots_all)[:, None, None],
        -1,
    ).reshape(inner * rows, top_k)
    place = jnp.arange(cap)
    far_experts = [lax.rem(chip + m, chips) * inner + my_local for m in range(chips)]
    wanted = (
        jnp.stack(far_experts)[:, None, None] * capacity
        + (jnp.arange(inner) * slots_all)[None, :, None]
        + place[None, None, :]
    )
    wanted = jnp.where(place[None, None, :] < capacity, wanted, -2).reshape(-1)
    n_slots = wanted.shape[0]
    per_far = n_slots // chips
    hot = sum((wanted[:, None] == slot_ids[None, :, j]).astype(BF) for j in range(top_k))
    hot_t = sum((slot_ids[:, j][:, None] == wanted[None, :]).astype(BF) for j in range(top_k))

    def through(values, way):
        cut = values.reshape(chips, per_far, -1)
        got = [cut[0]]
        for m in range(1, chips):
            perm = [(i, (i + 2 * m * way) % n_ex) for i in range(n_ex)]
            got.append(lax.ppermute(cut[m], "expert", perm))
        return jnp.concatenate(got, axis=0)

    positions = jnp.arange(seq)
    cos_table, sine_table = rope_tables(positions)
    cos_wide, sine_wide = jnp.tile(cos_table, (1, 4)), jnp.tile(sine_table, (1, 4))
    keep = (positions < lengths[0]).astype(F32)[None]
    attend_out, wo_rows, residual, x_col, (wg, wu), (sgate, sup, sdown) = forward_exchange(
        [tok_all, gain_one[None], wq, pk_flat, gain_lat[None], wexp, cos_wide, sine_wide, keep],
        to_owner_order(w_out),
        to_owner_order(tokens),
        gain_two[None],
        [w.reshape(-1, n_ex, r, ff_e) for w in (expert_gate, expert_up)],
        [w.reshape(r, inner, ff_s).transpose(1, 0, 2) for w in (shared_gate, shared_up, shared_down)],
        n_dp,
        n_ex,
        inner,
        2,
    )
    hidden_one, latent_raw, latent_low, qcat, kcat, value, lse, attended = attend_out
    wo_rows = wo_rows.reshape(hp * DV, width)
    sgate, sup, sdown = (w.reshape(width, ff_s) for w in (sgate, sup, sdown))
    hidden_two = pick(x_col, my_local)
    x_col = x_col.reshape(inner * rows, width)

    x_in, (wd,) = between(
        mm(hot, x_col).astype(BF).reshape(chips, per_far, width),
        1,
        [expert_down.reshape(-1, n_ex, r, ff_e)],
        [],
        n_dp,
        n_ex,
        inner,
        8,
    )
    x_in = x_in.reshape(n_slots, width)
    grad_in = through(mm(hot, cot_col).astype(BF), 1)
    wg, wu, wd = (w.reshape(width, ff_e) for w in (wg, wu, wd))

    def probs_of(logits):
        top = jnp.max(logits, axis=-1, keepdims=True)
        exp_logits = jnp.exp(logits - top)
        return exp_logits / jnp.sum(exp_logits, axis=-1, keepdims=True)

    shared_a = mm(x_col, sgate)
    shared_b = mm(x_col, sup)
    shared_hidden, shared_back = jax.vjp(swiglu, shared_a, shared_b)
    shared_hidden = shared_hidden.astype(BF)
    shared_out = mm_cols(shared_hidden, sdown)
    grad_sa, grad_sb = (v.astype(BF) for v in shared_back(mm(cot_col, sdown)))
    shared_grads = [
        mm_rows(x_col, grad_sa).astype(BF),
        mm_rows(x_col, grad_sb).astype(BF),
        mm_rows(cot_col, shared_hidden).astype(BF),
    ]
    shared_dx = mm_cols(grad_sa, sgate) + mm_cols(grad_sb, sup)

    slot_probs = probs_of(mm(x_in, router))
    slot_gate = jnp.sum(
        jnp.where(jnp.arange(n_experts)[None, :] == far_experts[0], slot_probs, 0.0),
        axis=1,
        keepdims=True,
    )
    expert_a = mm(x_in, wg)
    expert_b = mm(x_in, wu)
    expert_hidden, expert_back = jax.vjp(swiglu, expert_a, expert_b)
    expert_hidden = expert_hidden.astype(BF)
    rows_back = through(mm_cols(expert_hidden, wd).astype(BF), -1)
    slot_grad = (slot_gate * grad_in.astype(F32)).astype(BF)
    grad_ea, grad_eb = (v.astype(BF) for v in expert_back(mm(slot_grad, wd)))
    expert_totals = [
        mm_rows(left, right).astype(BF).reshape(n_ex, n_dp, r, ff_e)
        for left, right in ((x_in, grad_ea), (x_in, grad_eb), (slot_grad, expert_hidden))
    ]
    dx_back, (down_back,) = between(
        (mm_cols(grad_ea, wg) + mm_cols(grad_eb, wu)).astype(BF).reshape(chips, per_far, width),
        -1,
        [],
        expert_totals[2:],
        n_dp,
        n_ex,
        inner,
        9,
    )
    dx_back = dx_back.reshape(n_slots, width)

    col_probs = probs_of(mm(x_col, router))
    expert_axis = jnp.arange(n_experts)[None, :]
    gates = [
        jnp.sum(jnp.where(expert_axis == expert, col_probs, 0.0), axis=1, keepdims=True)
        for expert in far_experts
    ]
    gate_hot = jnp.concatenate(
        [hot_t[:, m * per_far : (m + 1) * per_far] * gates[m].astype(BF) for m in range(chips)],
        axis=1,
    )
    out_col = (mm(gate_hot, rows_back) + shared_out).astype(BF)
    dots = mm_cols(cot_col, rows_back) * hot_t.astype(F32)
    dots = jnp.sum(dots.reshape(inner * rows, chips, per_far), axis=-1)
    grad_probs_col = sum(
        jnp.where(expert_axis == far_experts[m], dots[:, m : m + 1], 0.0) for m in range(chips)
    )
    dx_col = mm(hot_t, dx_back) + shared_dx
    dx_send = jnp.concatenate(
        [dx_col, grad_probs_col, jnp.zeros((inner * rows, 128 - n_experts), F32)], axis=1
    ).astype(BF)
    dx_sum = column_sum(dx_send.reshape(inner, rows, width + 128), n_dp, n_ex, inner, 3)
    router_probs = lax.dynamic_slice_in_dim(col_probs, my_local * rows, rows, 0)
    grad_probs = dx_sum[:, width : width + n_experts]
    grad_logits = (
        router_probs * (grad_probs - jnp.sum(grad_probs * router_probs, axis=-1, keepdims=True))
    ).astype(BF)
    grad_router = mm_rows(hidden_two, grad_logits)
    grad_hidden_two = dx_sum[:, :width] + mm_cols(grad_logits, router)
    _, norm_two_back = jax.vjp(rms_norm, residual, gain_two)
    grad_resid_norm, grad_gain_two = norm_two_back(grad_hidden_two)
    grad_residual = cot_owner.astype(F32) + grad_resid_norm

    out_col, shared_grads, _ = lax.optimization_barrier((out_col, shared_grads, dx_sum))
    out_sum = lax.psum_scatter(
        out_col, "dp", scatter_dimension=0, tiled=True, axis_index_groups=col_groups
    )
    out_tokens = from_owner_order((residual + out_sum.astype(F32)).astype(BF))
    shared_sums = [
        lax.psum_scatter(
            grad.reshape(n_ex, n_dp, r, ff_s), "expert", scatter_dimension=0, tiled=True
        ).reshape(n_dp, r, ff_s)
        for grad in shared_grads
    ]
    attend_grads, (gate_back,) = backward_exchange(
        grad_residual.astype(BF),
        [wo_rows, wq, wexp, cos_wide, sine_wide, keep, qcat, kcat, value, lse, attended],
        hidden_one,
        latent_low,
        expert_totals[:1],
        n_dp,
        n_ex,
        inner,
        5,
    )
    grad_query_sum, grad_latent_sum, grad_wout, grad_wq, grad_we = attend_grads
    own_start = e * rows
    latent_own = lax.dynamic_slice_in_dim(latent_raw, own_start, rows, 0)[:, :lat]
    cos_own = lax.dynamic_slice_in_dim(cos_table, own_start, rows, 0)
    sine_own = lax.dynamic_slice_in_dim(sine_table, own_start, rows, 0)

    def make_latent(latent_in, gain_in):
        return (
            rms_norm(latent_in[:, :KVR], gain_in),
            rotate(latent_in[:, KVR:], cos_own, sine_own),
        )

    _, latent_back = jax.vjp(make_latent, latent_own, gain_lat)
    grad_latent_raw, grad_gain_lat = latent_back(
        (grad_latent_sum[:, :KVR], grad_latent_sum[:, KVR:lat])
    )
    grad_latent_low = grad_latent_raw.astype(BF)
    _, norm_one_back = jax.vjp(rms_norm, tokens.astype(F32), gain_one)
    grad_hidden_one = grad_query_sum + mm_cols(grad_latent_low, w_lat)
    grad_tokens_norm, grad_gain_one = norm_one_back(grad_hidden_one)
    grad_tokens = from_owner_order(grad_residual) + grad_tokens_norm

    wout_back = lax.all_to_all(
        grad_wout.reshape(hp, parts, r, width).transpose(1, 0, 2, 3),
        "expert",
        0,
        0,
        axis_index_groups=part_groups,
        tiled=True,
    ).reshape(n_dp, r, width)
    grad_wq = grad_wq.reshape(n_dp, n_ex, r, head_cols)
    grad_we = grad_we.reshape(n_dp, n_ex, r, rl * kv_cols // r)
    heads_grad = jnp.concatenate([grad_wq, grad_we], axis=-1)
    hidden_own = lax.dynamic_slice_in_dim(hidden_one, own_start, rows, 0)

    def by_owner(values):
        return values.reshape(n_ex, n_dp, r, -1).transpose(1, 0, 2, 3)

    pack_grad = jnp.concatenate(
        [
            mm_rows(hidden_own, grad_latent_low).reshape(n_dp, n_ex, r, lat),
            by_owner(grad_router),
            grad_gain_one.reshape(n_dp, n_ex, r, 1),
            by_owner(grad_gain_two),
            jnp.pad(grad_gain_lat.reshape(n_dp, n_ex, rl, 1), ((0, 0),) * 2 + ((0, r - rl), (0, 0))),
            jnp.zeros((n_dp, n_ex, r, -small_cols % 128), F32),
        ],
        axis=-1,
    ).astype(BF)
    pack_grad = pack_grad.transpose(1, 0, 2, 3).reshape(n_ex, n_dp * r, -1)
    heads_all, sum_wout, pack_sum, shared_got, (up_back,) = last_exchange(
        heads_grad, wout_back, pack_grad, shared_sums, expert_totals[1:2], n_dp, n_ex, inner, 7
    )

    def added(values):
        return jnp.sum(values.astype(F32), axis=0)

    heads_all = heads_all.astype(F32)
    sum_wq = heads_all[..., :head_cols].transpose(1, 0, 2)
    sum_wq = jnp.concatenate(
        [
            sum_wq[..., : hp * DH].reshape(r, n_ex, hp, DH),
            sum_wq[..., hp * DH :].reshape(r, n_ex, hp, DR),
        ],
        axis=-1,
    ).reshape(r, H, DH + DR)
    sum_wq = jnp.take(sum_wq, jnp.array(heads_back), axis=1).reshape(r, H * (DH + DR))
    sum_we = heads_all[..., head_cols:].reshape(n_ex, rl, kv_cols).transpose(1, 0, 2)
    sum_we = jnp.take(sum_we.reshape(rl, H, DH + DV), jnp.array(heads_back), axis=1)
    sum_we = sum_we.reshape(rl, H * (DH + DV))
    sum_wout = from_owner_order(sum_wout)
    sum_sgate, sum_sup, sum_sdown = (
        added(got.reshape(n_dp // inner, inner, r, ff_s)).transpose(1, 0, 2).reshape(r, -1)
        for got in shared_got
    )
    sum_egate, sum_eup, sum_edown = (
        added(back).reshape(-1, n_ex * r, ff_e) for back in (gate_back, up_back, down_back)
    )
    return (
        out_tokens,
        grad_tokens,
        pack_sum[:, lat + n_experts],
        sum_wq,
        pack_sum[:, :lat],
        pack_sum[:rl, lat + n_experts + 2],
        sum_we,
        sum_wout,
        pack_sum[:, lat + n_experts + 1],
        pack_sum[:, lat : lat + n_experts],
        sum_sgate,
        sum_sup,
        sum_sdown,
        sum_egate,
        sum_eup,
        sum_edown,
    )


def solution(mesh):
    both = ("dp", "expert")
    in_specs = (
        P(both, None),
        P(both, None),
        P("dp"),
        P(both, None),
        P(both, None),
        P(both),
        P(both, None),
        P(both, None),
        P(both),
        P(both, None),
        P(both, None),
        P(both),
        P(both, None),
        P(both, None),
        P(both, None),
        P(both, None),
        P("expert", "dp", None),
        P("expert", "dp", None),
        P("expert", "dp", None),
    )
    out_specs = (
        P(both, None),
        P(both, None),
        P(both),
        P(both, None),
        P(both, None),
        P(both),
        P(both, None),
        P(both, None),
        P(both),
        P(both, None),
        P(both, None),
        P(both, None),
        P(both, None),
        P("expert", "dp", None),
        P("expert", "dp", None),
        P("expert", "dp", None),
    )
    return jax.shard_map(shards, mesh=mesh, in_specs=in_specs, out_specs=out_specs, check_vma=False)
```

```python
import jax
import jax.numpy as jnp
from jax import lax
from jax.experimental import pallas as pl
from jax.experimental.pallas import tpu as pltpu
from jax.sharding import PartitionSpec as P

H = 16
DH = 128
DR = 64
DV = 128
KVR = 512

norm_eps = 1e-06
masked_score = -1e30
MESH = pl.DeviceIdType.MESH
ANY = pl.BlockSpec(memory_space=pl.ANY)
VMEM = pl.BlockSpec(memory_space=pltpu.VMEM)
BF = jnp.bfloat16
F32 = jnp.float32


def rms_norm(values, scale_gain):
    return (
        values
        * lax.rsqrt(jnp.mean(values * values, axis=-1, keepdims=True) + norm_eps)
        * scale_gain
    )


def rotate(values, cos_table, sine_table):
    half_dim = values.shape[-1] // 2
    first_half = values[..., :half_dim]
    second_half = values[..., half_dim:]
    return jnp.concatenate(
        [
            first_half * cos_table - second_half * sine_table,
            second_half * cos_table + first_half * sine_table,
        ],
        axis=-1,
    )


def rope_tables(positions):
    half_dim = DR // 2
    inv_freq = 10000.0 ** (-(jnp.arange(half_dim).astype(F32) * 2.0) / DR)
    angles = positions.astype(F32)[:, None] * inv_freq[None, :]
    return (jnp.cos(angles), jnp.sin(angles))


def swiglu(gate_in, up_in):
    return jax.nn.silu(gate_in) * up_in


def mm(left, right):
    return jnp.dot(left, right, preferred_element_type=F32)


def mm_rows(left, right):
    return lax.dot_general(left, right, (((0,), (0,)), ((), ())), preferred_element_type=F32)


def mm_cols(left, right):
    return lax.dot_general(left, right, (((1,), (1,)), ((), ())), preferred_element_type=F32)


def slot_places(route_rows, pair_order, capacity):
    pair_expert = route_rows.reshape(-1)
    earlier = pair_order[None, :] < pair_order[:, None]
    same_expert = pair_expert[None, :] == pair_expert[:, None]
    places = jnp.sum((earlier & same_expert).astype(jnp.int32), axis=1)
    slot_index = jnp.where(places < capacity, pair_expert * capacity + places, -1)
    return slot_index.reshape(route_rows.shape)


def turn(values, cos, sin, sign):
    half = DR // 2
    first = lax.rem(lax.broadcasted_iota(jnp.int32, values.shape, 1), DR) < half
    partner = jnp.where(
        first, -pltpu.roll(values, 2 * DR - half, 1), pltpu.roll(values, half, 1)
    )
    return values * cos + sign * (partner * sin)


def causal(i, tile, keep_ref):
    shape = (tile, (i + 1) * tile)
    query = lax.broadcasted_iota(jnp.int32, shape, 0) + i * tile
    key = lax.broadcasted_iota(jnp.int32, shape, 1)
    return (key <= query) & (keep_ref[:, : shape[1]] > 0.5)


def attend_forward(
    tok, gain, wq, wl, gain_lat, we, cos, sin, keep,
    hidden, latent, latent_low, qcat, kcat, value, lse, attended,
):
    per, rows, width = tok.shape
    seq = per * rows
    tile = 2 * rows
    scale = (DH + DR) ** (-0.5)

    def project(i, carry):
        at = pl.ds(pl.multiple_of(i * tile, tile), tile)
        x = tok[pl.ds(2 * i, 2)].reshape(tile, width).astype(F32)
        root = lax.rsqrt(jnp.mean(x * x, axis=-1, keepdims=True) + norm_eps)
        hid = (x * root * gain[...]).astype(BF)
        hidden[at, :] = hid
        c, s = cos[at, :], sin[at, :]
        query = mm(hid, wq[...])
        rope_q = turn(query[:, 2 * DH :], c, s, 1.0).astype(BF)
        lat = mm(hid, wl[...])
        latent[at, :] = lat
        plain = lat[:, :KVR]
        root = lax.rsqrt(jnp.mean(plain * plain, axis=-1, keepdims=True) + norm_eps)
        low = (plain * root * gain_lat[...]).astype(BF)
        latent_low[at, :] = low
        rope = lat[:, KVR : KVR + 2 * DR]
        lane = lax.broadcasted_iota(jnp.int32, rope.shape, 1)
        rope = jnp.where(lane < DR, rope, pltpu.roll(rope, DR, 1))
        rope = turn(rope, c, s, 1.0)
        expanded = mm(low, we[...]).astype(BF)
        for h in range(2):
            qcat[h, at, :DH] = query[:, h * DH : (h + 1) * DH].astype(BF)
            qcat[h, at, DH:] = rope_q
            mine = (lane < DR) if h == 0 else (lane >= DR)
            kcat[h, at, :DH] = expanded[:, h * (DH + DV) : h * (DH + DV) + DH]
            kcat[h, at, DH:] = jnp.where(mine, rope, 0.0).astype(BF)
            value[h, at, :] = expanded[:, h * (DH + DV) + DH : (h + 1) * (DH + DV)]
        return carry

    lax.fori_loop(0, seq // tile, project, 0)
    for h in range(2):
        for i in range(seq // tile):
            at, upto = slice(i * tile, (i + 1) * tile), slice(0, (i + 1) * tile)
            scores = mm_cols(qcat[h, at, :], kcat[h, upto, :]) * scale
            scores = jnp.where(causal(i, tile, keep), scores, masked_score)
            top = jnp.max(scores, axis=-1, keepdims=True)
            exp_scores = jnp.exp(scores - top)
            total = jnp.sum(exp_scores, axis=-1, keepdims=True)
            probs = (exp_scores / total).astype(BF)
            attended[at, h * DV : (h + 1) * DV] = mm(probs, value[h, upto, :]).astype(BF)
            lse[h, at, :] = jnp.broadcast_to(top + jnp.log(total), (tile, lse.shape[2]))


def attend_backward(
    grad, wo, wq, we, cos, sin, keep, qcat, kcat, value, lse, attended,
    gat, grad_wout, dk, dv, grad_query, grad_expanded, grad_rope,
):
    per, rows, width = grad.shape
    seq = per * rows
    tile = 2 * rows
    scale = (DH + DR) ** (-0.5)
    count = seq // tile
    grad_wout[...] = jnp.zeros_like(grad_wout)

    def project(i, carry):
        at = pl.ds(pl.multiple_of(i * tile, tile), tile)
        block = grad[pl.ds(2 * i, 2)].reshape(tile, width)
        gat[at, :] = mm_cols(block, wo[...]).astype(BF)
        grad_wout[...] += mm_rows(attended[at, :], block)
        return carry

    lax.fori_loop(0, count, project, 0)
    for h in range(2):
        dk[...] = jnp.zeros_like(dk)
        dv[...] = jnp.zeros_like(dv)
        for i in range(count):
            at, upto = slice(i * tile, (i + 1) * tile), slice(0, (i + 1) * tile)
            g = gat[at, h * DV : (h + 1) * DV]
            scores = mm_cols(qcat[h, at, :], kcat[h, upto, :]) * scale
            scores = jnp.where(causal(i, tile, keep), scores, masked_score)
            probs = jnp.exp(scores - lse[h, at, 0:1])
            grad_probs = mm_cols(g, value[h, upto, :])
            inner = jnp.sum(grad_probs * probs, axis=-1, keepdims=True)
            raw = (probs * (grad_probs - inner) * scale).astype(BF)
            grad_q = mm(raw, kcat[h, upto, :])
            grad_query[at, h * DH : (h + 1) * DH] = grad_q[:, :DH].astype(BF)
            rope = grad_q[:, DH:]
            lane = lax.broadcasted_iota(jnp.int32, rope.shape, 1)
            mine = (lane < DR) if h == 0 else (lane >= DR)
            rope = turn(rope, cos[at, :], sin[at, :], -1.0).astype(BF)
            if h == 0:
                grad_query[at, 2 * DH :] = rope
            else:
                grad_query[at, 2 * DH :] = jnp.where(mine, rope, grad_query[at, 2 * DH :])
            dk[upto, :] += mm_rows(raw, qcat[h, at, :])
            dv[upto, :] += mm_rows(probs.astype(BF), g)
        grad_expanded[:, h * (DH + DV) : h * (DH + DV) + DH] = dk[:, :DH].astype(BF)
        grad_expanded[:, h * (DH + DV) + DH : (h + 1) * (DH + DV)] = dv[...].astype(BF)
        rope = dk[:, DH:]
        if h == 0:
            grad_rope[...] = rope
        else:
            grad_rope[...] += pltpu.roll(rope, DR, 1)


def params(collective_id):
    return pltpu.CompilerParams(
        collective_id=collective_id, has_side_effects=True, vmem_limit_bytes=60 << 20
    )


def remote(src, dst, send_sem, recv_sem, device):
    return pltpu.make_async_remote_copy(
        src_ref=src,
        dst_ref=dst,
        send_sem=send_sem,
        recv_sem=recv_sem,
        device_id=device,
        device_id_type=MESH,
    )


def greet(devices):
    barrier = pltpu.get_barrier_semaphore()
    for device in devices:
        pl.semaphore_signal(barrier, inc=1, device_id=device, device_id_type=MESH)
    pl.semaphore_wait(barrier, len(devices))


def places(n_dp, n_ex):
    z = lax.axis_index("dp")
    e = lax.axis_index("expert")
    chips = n_ex // 2
    c, k = e // 2, lax.rem(e, 2)
    sibling = (z, e + 1 - 2 * k)
    same_core = [(z, lax.rem(c + i, chips) * 2 + k) for i in range(1, chips)]
    column = [(lax.rem(z + i, n_dp), e) for i in range(1, n_dp)]
    return z, e, c, k, sibling, same_core, column


def wait_recv(region, sem, device):
    remote(region, region, sem, sem, device).wait_recv()


def column_sum(array, shared, totals, n_dp, n_ex, inner, collective_id):
    chips = n_ex // 2
    shape = array.shape[1:]
    extra = len(totals)
    _, _, r, ff_s = shared[0].shape

    def kernel(x_ref, *refs):
        s_in, t_refs, refs = refs[:3], refs[3 : 3 + extra], refs[3 + extra :]
        o_ref, s_out, back_refs = refs[0], refs[1:4], refs[4 : 4 + extra]
        refs = refs[4 + extra :]
        buf, from_sib, out_buf, from_far = refs[:4]
        send, recv, near_s, near_r, far_s, far_r = refs[4:10]
        rest = refs[10:]
        z, e, c, k, sibling, same_core, column = places(n_dp, n_ex)
        group = column_group(z, e, inner)
        greet(same_core + [sibling] + column + [(d[0], sibling[1]) for d in column])
        backs = [
            ExpertsBack(t_refs[m], back_refs[m], rest[7 * m : 7 * m + 7], n_dp, n_ex, inner)
            for m in range(extra)
        ]
        copies = []
        for i in range(1, inner):
            to = lax.rem(z + i, inner)
            copy = remote(x_ref.at[to], buf.at[i], send.at[i], recv.at[i], group[i])
            copy.start()
            copies.append(copy)
        near, far = {}, {}
        for i in list(range(1, chips)) + [0]:
            chip = lax.rem(c + i, chips)
            for m in range(3):
                near[i, m] = remote(
                    s_in[m].at[chip * 2 + 1 - k], from_sib.at[m, i],
                    near_s.at[m, i], near_r.at[m, i], sibling,
                )
                near[i, m].start()
        for back in backs:
            back.begin()

        def pair(i, m):
            chip = lax.rem(c + i, chips)
            near[i, m].wait_recv()

            def row(d, carry):
                out_buf[m, i, d] = (
                    s_in[m][chip * 2 + k, d].astype(F32) + from_sib[m, i, d].astype(F32)
                ).astype(BF)
                return carry

            lax.fori_loop(0, n_dp, row, 0)

        for i in range(1, chips):
            for m in range(3):
                pair(i, m)
                far[i, m] = remote(
                    out_buf.at[m, i], from_far.at[m, i], far_s.at[m, i], far_r.at[m, i],
                    same_core[i - 1],
                )
                far[i, m].start()
        o_ref[...] = x_ref[lax.rem(z, inner)].astype(F32)
        for back in backs:
            back.pass_on()
        for m in range(3):
            pair(0, m)
        for i in range(1, inner):
            copies[i - 1].wait_recv()
            o_ref[...] += buf[i].astype(F32)
        for m in range(3):
            for i in range(1, chips):
                far[i, m].wait_recv()

            def row(d, carry, m=m):
                total = out_buf[m, 0, d].astype(F32)
                for i in range(1, chips):
                    total = total + from_far[m, i, d].astype(F32)
                s_out[m][d] = total.astype(BF)
                return carry

            lax.fori_loop(0, n_dp, row, 0)
        for copy in copies + list(near.values()) + list(far.values()):
            copy.wait_send()
        for back in backs:
            back.end()

    dma = pltpu.SemaphoreType.DMA
    scratch = [pltpu.VMEM((inner,) + shape, BF)]
    scratch += [pltpu.VMEM((3, chips, n_dp, r, ff_s), BF)] * 3
    scratch += [dma((inner,))] * 2 + [dma((3, chips))] * 4
    for total in totals:
        scratch += ExpertsBack.scratch(total, n_dp, inner)
    outs = pl.pallas_call(
        kernel,
        out_shape=[jax.ShapeDtypeStruct(shape, F32)]
        + [jax.ShapeDtypeStruct((n_dp, r, ff_s), BF)] * 3
        + [ExpertsBack.out(total, n_dp, inner) for total in totals],
        in_specs=[VMEM] * 4 + [ANY] * extra,
        out_specs=[VMEM] * 4 + [ANY] * extra,
        scratch_shapes=scratch,
        compiler_params=params(collective_id),
    )(array, *shared, *totals)
    return outs[0], outs[1:4], outs[4:]


def column_group(z, e, inner):
    start = z // inner * inner
    return [(start + lax.rem(z - start + i, inner), e) for i in range(inner)]


def first_exchange(tok, heads_w, pack, n_dp, n_ex, collective_id):
    chips = n_ex // 2

    def kernel(
        tok_ref, wa_ref, pk_ref, tok_out, wa_out, pk_out,
        t_send, t_recv, ts_send, ts_recv, a_send, a_recv, az_send, az_recv,
        p_send, p_recv, pf_send, pf_recv, ps_send, ps_recv, local,
    ):
        z, e, c, k, sibling, same_core, column = places(n_dp, n_ex)
        plane = [(z, lax.rem(e + i, n_ex)) for i in range(1, n_ex)]
        greet(plane + column)
        wa_far, pk_col, tok_far, near = [], [], [], []
        for i in range(1, n_ex):
            copy = remote(
                wa_ref.at[lax.rem(e + i, n_ex)], wa_out.at[z, e],
                a_send.at[i], a_recv.at[i], plane[i - 1],
            )
            copy.start()
            wa_far.append(copy)
        for i in range(1, n_dp):
            copy = remote(pk_ref, pk_out.at[z, e], p_send.at[i], p_recv.at[i], column[i - 1])
            copy.start()
            pk_col.append(copy)
        for i in range(1, chips):
            copy = remote(tok_ref, tok_out.at[e], t_send.at[i], t_recv.at[i], same_core[i - 1])
            copy.start()
            tok_far.append(copy)
        copy = remote(tok_ref, tok_out.at[e], ts_send.at[0], ts_recv.at[0], sibling)
        copy.start()
        near.append(copy)
        own = [
            pltpu.make_async_copy(wa_ref.at[e], wa_out.at[z, e], local.at[0]),
            pltpu.make_async_copy(pk_ref, pk_out.at[z, e], local.at[1]),
            pltpu.make_async_copy(tok_ref, tok_out.at[e], local.at[2]),
        ]
        for copy in own:
            copy.start()
        for copy in own:
            copy.wait()
        for copy in wa_far:
            copy.wait_recv()
        wa_col = []
        for i in range(1, n_dp):
            copy = remote(
                wa_out.at[z], wa_out.at[z], az_send.at[i], az_recv.at[i], column[i - 1]
            )
            copy.start()
            wa_col.append(copy)
        for copy in pk_col:
            copy.wait_recv()
        pk_far = []
        for i in range(1, chips):
            copy = remote(
                pk_out.at[:, e], pk_out.at[:, e], pf_send.at[i], pf_recv.at[i], same_core[i - 1]
            )
            copy.start()
            pk_far.append(copy)
        copy = remote(pk_out.at[:, e], pk_out.at[:, e], ps_send.at[0], ps_recv.at[0], sibling)
        copy.start()
        near.append(copy)
        for i in range(1, chips):
            source = lax.rem(c + chips - i, chips) * 2 + k
            tok_far[i - 1].wait_recv()
            copy = remote(
                tok_out.at[source], tok_out.at[source], ts_send.at[i], ts_recv.at[i], sibling
            )
            copy.start()
            near.append(copy)
            pk_far[i - 1].wait_recv()
            copy = remote(
                pk_out.at[:, source], pk_out.at[:, source], ps_send.at[i], ps_recv.at[i], sibling
            )
            copy.start()
            near.append(copy)
        for copy in near + wa_col:
            copy.wait()
        for copy in wa_far + pk_col + tok_far + pk_far:
            copy.wait_send()

    dma = pltpu.SemaphoreType.DMA
    return pl.pallas_call(
        kernel,
        out_shape=[
            jax.ShapeDtypeStruct((n_ex,) + tok.shape, tok.dtype),
            jax.ShapeDtypeStruct((n_dp,) + heads_w.shape, heads_w.dtype),
            jax.ShapeDtypeStruct((n_dp, n_ex) + pack.shape, pack.dtype),
        ],
        in_specs=[ANY] * 3,
        out_specs=[ANY] * 3,
        scratch_shapes=[dma((chips,))] * 4
        + [dma((n_ex,))] * 2
        + [dma((n_dp,))] * 4
        + [dma((chips,))] * 4
        + [dma((3,))],
        compiler_params=params(collective_id),
    )(tok, heads_w, pack)


class ExpertsIn:
    @staticmethod
    def scratch(n_dp):
        dma = pltpu.SemaphoreType.DMA
        return [dma((n_dp, 2)), dma((n_dp,)), dma((n_dp,)), dma((n_dp,))]

    @staticmethod
    def out(weight, n_dp, n_ex):
        return jax.ShapeDtypeStruct((n_ex, n_dp) + weight.shape[2:], BF)

    def __init__(self, weight, out, scratch, n_dp, n_ex, inner):
        self.weight, self.out, self.n_dp, self.inner = weight, out, n_dp, inner
        self.send, self.recv, self.sib_send, self.sib_recv = scratch
        self.z, self.e, self.c, self.k, self.sibling, _, _ = places(n_dp, n_ex)
        self.hh = n_ex // 2
        self.local = weight.shape[0]

    def sends(self, start):
        for i in list(range(1, self.n_dp)) + [0]:
            to = lax.rem(self.z + i, self.n_dp)
            expert = lax.rem(to, self.inner)

            def go(i=i, to=to, expert=expert):
                for h in range(2):
                    src = self.weight.at[lax.rem(expert, self.local), pl.ds(h * self.hh, self.hh)]
                    dst = self.out.at[pl.ds(h * self.hh, self.hh), self.z]
                    sem = self.recv.at[self.z]

                    def far(src=src, dst=dst, h=h):
                        copy = remote(src, dst, self.send.at[i, h], sem, (to, 2 * self.c + h))
                        if start:
                            copy.start()
                        else:
                            copy.wait_send()

                    if i:
                        far()
                    else:
                        pl.when(self.k != h)(far)
                        if start:

                            @pl.when(self.k == h)
                            def _(src=src, dst=dst):
                                pltpu.make_async_copy(src, dst, sem).start()

            pl.when(expert // self.local == self.k)(go)

    def begin(self):
        self.sends(True)

    def pass_on(self):
        mine = lax.rem(self.z, self.inner)
        for i in range(self.n_dp):
            d = lax.rem(self.z + self.n_dp - i, self.n_dp)
            region = self.out.at[pl.ds(self.k * self.hh, self.hh), d]
            if i:
                wait_recv(region, self.recv.at[d], self.sibling)
            else:
                from_here = mine // self.local == self.k

                @pl.when(from_here)
                def _(region=region, d=d):
                    src = self.weight.at[
                        lax.rem(mine, self.local), pl.ds(self.k * self.hh, self.hh)
                    ]
                    pltpu.make_async_copy(src, region, self.recv.at[d]).wait()

                @pl.when(jnp.logical_not(from_here))
                def _(region=region, d=d):
                    wait_recv(region, self.recv.at[d], self.sibling)

            remote(
                region, region, self.sib_send.at[i], self.sib_recv.at[i], self.sibling
            ).start()

    def end(self):
        self.sends(False)
        for i in range(self.n_dp):
            d = lax.rem(self.z + self.n_dp - i, self.n_dp)
            mine = self.out.at[pl.ds(self.k * self.hh, self.hh), d]
            remote(
                mine, mine, self.sib_send.at[i], self.sib_recv.at[i], self.sibling
            ).wait_send()
            region = self.out.at[pl.ds((1 - self.k) * self.hh, self.hh), d]
            wait_recv(region, self.sib_recv.at[i], self.sibling)


def forward_exchange(attend, w_out, tok, gain, experts, shared, n_dp, n_ex, inner, collective_id):
    chips = n_ex // 2
    rows, width = tok.shape
    count = len(experts)
    r = w_out.shape[0]
    parts = DV // r
    hp = n_dp // parts
    seq = n_ex * rows

    def kernel(*refs):
        att_in, refs = refs[:9], refs[9:]
        wo_in, tok_ref, gain_ref = refs[:3]
        e_in, s_in = refs[3 : 3 + count], refs[3 + count : 6 + count]
        refs = refs[6 + count :]
        att_out, refs = refs[:8], refs[8:]
        wo_out, res_ref, xcol_ref = refs[:3]
        w_out, s_out = refs[3 : 3 + count], refs[3 + count : 6 + count]
        refs = refs[6 + count :]
        x_ref, from_sib, out_buf, from_far, xbuf = refs[:5]
        (
            near_s, near_r, far_s, far_r, x_s, x_r,
            sh_s, sh_r, sp_s, sp_r, sf_s, sf_r, wo_s, wo_r, local,
        ) = refs[5:20]
        refs = refs[20:]
        z, e, c, k, sibling, same_core, column = places(n_dp, n_ex)
        group = column_group(z, e, inner)
        part = lax.rem(e, parts)
        members = [
            (lax.rem(z + i, n_dp), e - part + lax.rem(part + j, parts))
            for i in range(n_dp)
            for j in range(parts)
        ]
        greet(same_core + column + [(device[0], sibling[1]) for device in column] + members[1:])

        def wo_sends(start):
            for i in range(n_dp):
                target = (lax.rem(z + i, n_dp), e - part + z // hp)
                dst, sem = wo_out.at[lax.rem(z, hp), part], wo_r.at[lax.rem(z, hp), part]

                def far(i=i, target=target, dst=dst, sem=sem):
                    copy = remote(wo_in, dst, wo_s.at[i], sem, target)
                    if start:
                        copy.start()
                    else:
                        copy.wait_send()

                if i:
                    far()
                else:
                    pl.when(z // hp != part)(far)
                    if start:

                        @pl.when(z // hp == part)
                        def _(dst=dst, sem=sem):
                            pltpu.make_async_copy(wo_in, dst, sem).start()

        def wo_arrivals():
            for h in range(hp):
                for p in range(parts):
                    here = jnp.logical_and(part * hp + h == z, part == p)

                    @pl.when(here)
                    def _(h=h, p=p):
                        pltpu.make_async_copy(wo_in, wo_out.at[h, p], wo_r.at[h, p]).wait()

                    @pl.when(jnp.logical_not(here))
                    def _(h=h, p=p):
                        wait_recv(wo_out.at[h, p], wo_r.at[h, p], sibling)

        my_l = lax.rem(z, inner)
        matrices = [
            ExpertsIn(e_in[m], w_out[m], refs[4 * m : 4 * m + 4], n_dp, n_ex, inner)
            for m in range(count)
        ]
        wo_sends(True)
        shared_copies = []
        for i in range(1, n_dp):
            for m in range(3):
                copy = remote(
                    s_in[m].at[lax.rem(lax.rem(z + i, n_dp), inner)], s_out[m].at[e, z],
                    sh_s.at[m, i], sh_r.at[m, i], column[i - 1],
                )
                copy.start()
                shared_copies.append(copy)
        own = [
            pltpu.make_async_copy(s_in[m].at[my_l], s_out[m].at[e, z], local.at[m])
            for m in range(3)
        ]
        for copy in own:
            copy.start()
        matrices[0].begin()
        attend_forward(*att_in, *att_out)
        wo_arrivals()
        wo = wo_out[...].reshape(hp * DV, width)

        def project(i, carry):
            at = pl.ds(pl.multiple_of(i * 2 * rows, 2 * rows), 2 * rows)
            block = mm(att_out[7][at, :], wo).astype(BF)
            x_ref[pl.ds(2 * i, 2)] = block.reshape(2, rows, width)
            return carry

        lax.fori_loop(0, chips, project, 0)
        near = []
        for i in list(range(1, chips)) + [0]:
            chip = lax.rem(c + i, chips)
            copy = remote(
                x_ref.at[chip * 2 + 1 - k], from_sib.at[chip], near_s.at[i], near_r.at[i], sibling
            )
            copy.start()
            near.append(copy)
        far = []
        for i in range(1, chips):
            chip = lax.rem(c + i, chips)
            near[i - 1].wait_recv()
            out_buf[i] = (
                x_ref[chip * 2 + k].astype(F32) + from_sib[chip].astype(F32)
            ).astype(BF)
            copy = remote(out_buf.at[i], from_far.at[i], far_s.at[i], far_r.at[i], same_core[i - 1])
            copy.start()
            far.append(copy)
        near[chips - 1].wait_recv()
        res_ref[...] = x_ref[e].astype(F32) + from_sib[c].astype(F32) + tok_ref[...].astype(F32)
        for i in range(1, chips):
            far[i - 1].wait_recv()
            res_ref[...] += from_far[i].astype(F32)
        residual = res_ref[...]
        scale = lax.rsqrt(jnp.mean(residual * residual, axis=-1, keepdims=True) + norm_eps)
        xbuf[...] = (residual * scale * gain_ref[...]).astype(BF)
        x_copies = []
        for i in range(1, inner):
            copy = remote(xbuf, xcol_ref.at[my_l], x_s.at[i], x_r.at[i], group[i])
            copy.start()
            x_copies.append(copy)
        x_own = pltpu.make_async_copy(xbuf, xcol_ref.at[my_l], local.at[3])
        x_own.start()
        for matrix in matrices[1:]:
            matrix.begin()
        for copy in own:
            copy.wait()
        for copy in shared_copies:
            copy.wait_recv()
        plane, to_sib = [], []
        for m in range(3):
            block = s_out[m].at[e]
            for i in range(1, chips):
                copy = remote(block, block, sp_s.at[m, i], sp_r.at[m, i], same_core[i - 1])
                copy.start()
                plane.append(copy)
            copy = remote(block, block, sf_s.at[m, 0], sf_r.at[m, 0], sibling)
            copy.start()
            to_sib.append(copy)
        for m in range(3):
            for i in range(1, chips):
                plane[m * (chips - 1) + i - 1].wait_recv()
                block = s_out[m].at[lax.rem(c + chips - i, chips) * 2 + k]
                copy = remote(block, block, sf_s.at[m, i], sf_r.at[m, i], sibling)
                copy.start()
                to_sib.append(copy)
        for matrix in matrices:
            matrix.pass_on()
        for copy in x_copies + to_sib:
            copy.wait()
        x_own.wait()
        for copy in plane + shared_copies + near + far:
            copy.wait_send()
        wo_sends(False)
        for matrix in matrices:
            matrix.end()

    dma = pltpu.SemaphoreType.DMA
    ff_s = shared[0].shape[2]
    scratch = []
    for _ in experts:
        scratch += ExpertsIn.scratch(n_dp)
    sds = jax.ShapeDtypeStruct
    outs = pl.pallas_call(
        kernel,
        out_shape=[
            sds((seq, width), BF),
            sds((seq, attend[3].shape[1]), F32),
            sds((seq, KVR), BF),
            sds((2, seq, 2 * DH), BF),
            sds((2, seq, 2 * DH), BF),
            sds((2, seq, DV), BF),
            sds((2, seq, 128), F32),
            sds((seq, 2 * DV), BF),
            sds((hp, parts, r, width), BF),
            sds((rows, width), F32),
            sds((inner, rows, width), BF),
        ]
        + [ExpertsIn.out(w, n_dp, n_ex) for w in experts]
        + [sds((n_ex, n_dp, r, ff_s), BF)] * 3,
        in_specs=[VMEM] * 9 + [ANY] + [VMEM] * 2 + [ANY] * (3 + count),
        out_specs=[VMEM] * 10 + [ANY] * (4 + count),
        scratch_shapes=[pltpu.VMEM((n_ex, rows, width), BF)]
        + [pltpu.VMEM((chips, rows, width), BF)] * 3
        + [pltpu.VMEM((rows, width), BF)]
        + [dma((chips,))] * 4
        + [dma((inner,))] * 2
        + [dma((3, n_dp))] * 2
        + [dma((3, chips))] * 4
        + [dma((n_dp,)), dma((hp, parts)), dma((4,))]
        + scratch,
        compiler_params=params(collective_id),
    )(*attend, w_out, tok, gain, *experts, *shared)
    return outs[:8], outs[8], outs[9], outs[10], outs[11 : 11 + count], outs[11 + count :]


def between(blocks, way, weights, totals, n_dp, n_ex, inner, collective_id):
    chips = n_ex // 2
    n_in, n_back = len(weights), len(totals)

    def kernel(x_ref, *refs):
        w_in, t_in = refs[:n_in], refs[n_in : n_in + n_back]
        refs = refs[n_in + n_back :]
        o_ref, w_out, t_out = refs[0], refs[1 : 1 + n_in], refs[1 + n_in : 1 + n_in + n_back]
        refs = refs[1 + n_in + n_back :]
        send, recv, local = refs[:3]
        z, e, c, k, sibling, same_core, column = places(n_dp, n_ex)
        greet(same_core + [sibling] + column + [(device[0], sibling[1]) for device in column])
        refs = refs[3:]
        works = [
            ExpertsIn(w_in[m], w_out[m], refs[4 * m : 4 * m + 4], n_dp, n_ex, inner)
            for m in range(n_in)
        ]
        refs = refs[4 * n_in :]
        works += [
            ExpertsBack(t_in[m], t_out[m], refs[7 * m : 7 * m + 7], n_dp, n_ex, inner)
            for m in range(n_back)
        ]
        copies = []
        for i in range(1, chips):
            to = same_core[i - 1] if way > 0 else same_core[chips - i - 1]
            copy = remote(x_ref.at[i], o_ref.at[i], send.at[i], recv.at[i], to)
            copy.start()
            copies.append(copy)
        copy = pltpu.make_async_copy(x_ref.at[0], o_ref.at[0], local)
        copy.start()
        copies.append(copy)
        for work in works:
            work.begin()
        for work in works:
            work.pass_on()
        for copy in copies:
            copy.wait()
        for work in works:
            work.end()

    dma = pltpu.SemaphoreType.DMA
    scratch = [dma((chips,)), dma((chips,)), dma]
    for _ in weights:
        scratch += ExpertsIn.scratch(n_dp)
    for total in totals:
        scratch += ExpertsBack.scratch(total, n_dp, inner)
    outs = pl.pallas_call(
        kernel,
        out_shape=[jax.ShapeDtypeStruct(blocks.shape, BF)]
        + [ExpertsIn.out(w, n_dp, n_ex) for w in weights]
        + [ExpertsBack.out(total, n_dp, inner) for total in totals],
        in_specs=[ANY] * (1 + n_in + n_back),
        out_specs=[ANY] * (1 + n_in + n_back),
        scratch_shapes=scratch,
        compiler_params=params(collective_id),
    )(blocks, *weights, *totals)
    return outs[0], outs[1:]


class ExpertsBack:
    @staticmethod
    def scratch(total, n_dp, inner):
        n_ex, _, r, ff = total.shape
        dma = pltpu.SemaphoreType.DMA
        return [
            pltpu.VMEM((n_ex // 2, n_dp, r, ff), BF),
            pltpu.VMEM((n_ex // 2, n_dp, r, ff), BF),
            dma((n_dp,)),
            dma((n_dp,)),
            dma((n_dp,)),
            dma((n_dp,)),
            dma((n_dp // inner, 2, 2)),
        ]

    @staticmethod
    def out(total, n_dp, inner):
        n_ex, _, r, ff = total.shape
        return jax.ShapeDtypeStruct((n_dp // inner, 2, n_ex, r, ff), BF)

    def __init__(self, total, out, scratch, n_dp, n_ex, inner):
        self.total, self.out, self.n_dp, self.inner = total, out, n_dp, inner
        self.own, self.sib, self.near_s, self.near_r, self.load, self.send, self.recv = scratch
        self.z, self.e, self.c, self.k, self.sibling, _, _ = places(n_dp, n_ex)
        self.hh = n_ex // 2

    def near(self, i):
        d = lax.rem(self.z + i, self.n_dp)
        return remote(
            self.total.at[pl.ds((1 - self.k) * self.hh, self.hh), d],
            self.sib.at[:, d], self.near_s.at[i], self.near_r.at[i], self.sibling,
        )

    def loads(self, i):
        d = lax.rem(self.z + i, self.n_dp)
        return pltpu.make_async_copy(
            self.total.at[pl.ds(self.k * self.hh, self.hh), d], self.own.at[:, d], self.load.at[i]
        )

    def order(self):
        return list(range(1, self.n_dp)) + [0]

    def begin(self):
        for i in self.order():
            self.near(i).start()
            self.loads(i).start()

    def route(self, i):
        d = lax.rem(self.z + i, self.n_dp)
        expert = lax.rem(self.z, self.inner)
        dst = self.out.at[
            self.z // self.inner, lax.rem(expert, 2), pl.ds(self.k * self.hh, self.hh)
        ]
        sem = self.recv.at[self.z // self.inner, lax.rem(expert, 2), self.k]
        return self.own.at[:, d], dst, sem, d, expert // 2

    def stay(self):
        src, dst, sem, _, _ = self.route(0)
        return pltpu.make_async_copy(src, dst, sem)

    def go(self, i):
        src, dst, sem, d, core = self.route(i)
        return remote(src, dst, self.send.at[i], sem, (d, 2 * self.c + core))

    def here(self):
        return lax.rem(self.z, self.inner) // 2 == self.k

    def pass_on(self):
        for i in self.order():
            d = lax.rem(self.z + i, self.n_dp)
            self.near(i).wait_recv()
            self.loads(i).wait()
            for j in range(self.hh):
                self.own[j, d] = (
                    self.own[j, d].astype(F32) + self.sib[j, d].astype(F32)
                ).astype(BF)
            if i:
                self.go(i).start()
            else:
                pl.when(self.here())(lambda: self.stay().start())
                pl.when(jnp.logical_not(self.here()))(lambda: self.go(0).start())

    def end(self):
        for i in self.order():
            self.near(i).wait_send()
            if i:
                self.go(i).wait_send()
            else:
                pl.when(jnp.logical_not(self.here()))(lambda: self.go(0).wait_send())
        for o in range(self.n_dp // self.inner):
            for j in range(2):
                for h in range(2):
                    region = self.out.at[o, j, pl.ds(h * self.hh, self.hh)]
                    source = o * self.inner + 2 * self.k + j
                    here = jnp.logical_and(source == self.z, self.k == h)

                    @pl.when(here)
                    def _(region=region, o=o, j=j, h=h):
                        d = self.z
                        pltpu.make_async_copy(
                            self.own.at[:, d], region, self.recv.at[o, j, h]
                        ).wait()

                    @pl.when(jnp.logical_not(here))
                    def _(region=region, o=o, j=j, h=h):
                        wait_recv(region, self.recv.at[o, j, h], self.sibling)


def rms_back(x, gain, grad):
    root = lax.rsqrt(jnp.mean(x * x, axis=-1, keepdims=True) + norm_eps)
    scaled = grad * gain
    along = jnp.mean(x * scaled, axis=-1, keepdims=True)
    return root * scaled - x * (root * root * root) * along, grad * x * root


def backward_exchange(
    grad, attend, hidden, latent_low, own, shared, totals, n_dp, n_ex, inner, collective_id
):
    chips = n_ex // 2
    rows, width = grad.shape
    seq = n_ex * rows
    extra = len(totals)
    wq, we = attend[1], attend[2]
    lat_cols = KVR + 2 * DR
    r = width // (n_dp * n_ex)
    rl = KVR // (n_dp * n_ex)
    parts = DV // r
    hp = n_dp // parts
    n_dev = n_dp * n_ex
    wq_cols = wq.shape[1]
    we_cols = rl * we.shape[1] // r
    head_cols = wq_cols + we_cols

    def kernel(*refs):
        grad_ref, att_in, refs = refs[0], refs[1:12], refs[12:]
        hidden_ref, low_ref, refs = refs[0], refs[1], refs[2:]
        wl_ref, lat_ref, tok_ref, gain_ref, glat_ref, gnat_ref, router_ref, gtwo_ref = refs[:8]
        sh_in, t_refs, refs = refs[8:11], refs[11 : 11 + extra], refs[11 + extra :]
        tok_out, vec_out, pack_out, heads_mid, heads_out, wout_out = refs[:6]
        sh_out, back_refs, refs = refs[6:9], refs[9 : 9 + extra], refs[9 + extra :]
        gbuf, att_tmp, refs = refs[0], refs[1:8], refs[8:]
        part_l, bufs, sums, refs = refs[0], refs[1:7], refs[7:9], refs[9:]
        hsrc, wsrc, pack, psib, pout, pfar, psum, pbuf, vec, vbuf, vzbuf = refs[:11]
        refs = refs[11:]
        t_s, t_r, ts_s, ts_r, local = refs[:5]
        sems, refs = refs[5:13], refs[13:]
        (
            h_s, h_r, hz_s, hz_r, w_s, w_r, pn_s, pn_r, pf_s, pf_r, pc_s, pc_r, s_s, s_r,
            v_s, v_r, vz_s, vz_r,
        ) = refs[:18]
        rest = refs[18:]
        x_refs = (gbuf, part_l)
        z, e, c, k, sibling, same_core, column = places(n_dp, n_ex)
        plane = [(z, lax.rem(e + i, n_ex)) for i in range(1, n_ex)]
        part = lax.rem(e, parts)
        members = [
            (lax.rem(z + i, n_dp), e - part + lax.rem(part + j, parts))
            for i in range(n_dp)
            for j in range(parts)
        ]
        greet(plane + column + [(d[0], sibling[1]) for d in column] + members[1:])
        backs = [
            ExpertsBack(t_refs[m], back_refs[m], rest[7 * m : 7 * m + 7], n_dp, n_ex, inner)
            for m in range(extra)
        ]
        gather, to_sib, others = [], [], []
        for i in range(1, chips):
            copy = remote(grad_ref, gbuf.at[e], t_s.at[i], t_r.at[i], same_core[i - 1])
            copy.start()
            gather.append(copy)
        copy = remote(grad_ref, gbuf.at[e], ts_s.at[0], ts_r.at[0], sibling)
        copy.start()
        to_sib.append(copy)
        keep = pltpu.make_async_copy(grad_ref, gbuf.at[e], local.at[0])
        keep.start()
        for back in backs:
            back.begin()
        for m in range(3):
            for i in range(1, n_dp):
                copy = remote(
                    sh_in[m].at[lax.rem(z + i, n_dp)], sh_out[m].at[z],
                    s_s.at[m, i], s_r.at[m, i], column[i - 1],
                )
                copy.start()
                others.append(copy)
            copy = pltpu.make_async_copy(sh_in[m].at[z], sh_out[m].at[z], local.at[1 + m])
            copy.start()
            others.append(copy)
        for i in range(1, chips):
            gather[i - 1].wait_recv()
            block = gbuf.at[lax.rem(c + chips - i, chips) * 2 + k]
            copy = remote(block, block, ts_s.at[i], ts_r.at[i], sibling)
            copy.start()
            to_sib.append(copy)
        for back in backs:
            back.pass_on()
        keep.wait()
        for copy in to_sib:
            copy.wait_recv()
        for copy in gather + to_sib:
            copy.wait_send()
        gat, grad_wout, dk, dv, grad_query, grad_expanded, grad_rope = att_tmp
        attend_backward(gbuf, *att_in, *att_tmp)

        wsrc[...] = grad_wout[...].astype(BF).reshape(hp, parts, r, width)

        def wout_sends(start):
            for h in range(hp):
                for p in range(parts):
                    target = (part * hp + h, e - part + p)
                    here = jnp.logical_and(part * hp + h == z, p == part)

                    def far(h=h, p=p, target=target):
                        copy = remote(
                            wsrc.at[h, p], wout_out.at[z], w_s.at[h, p], w_r.at[z], target
                        )
                        if start:
                            copy.start()
                        else:
                            copy.wait_send()

                    pl.when(jnp.logical_not(here))(far)
                    if start:

                        @pl.when(here)
                        def _(h=h, p=p):
                            pltpu.make_async_copy(
                                wsrc.at[h, p], wout_out.at[z], w_r.at[z]
                            ).start()

        wout_sends(True)

        def spread(i, carry):
            at = pl.ds(pl.multiple_of(i * 2 * rows, 2 * rows), 2 * rows)
            block = mm_cols(grad_query[at, :], att_in[1][...]).astype(BF)
            gbuf[pl.ds(2 * i, 2)] = block.reshape(2, rows, width)
            block = mm_cols(grad_expanded[at, :], att_in[2][...]).astype(BF)
            part_l[pl.ds(2 * i, 2), :, :KVR] = block.reshape(2, rows, KVR)
            block = grad_rope[at, :].astype(BF)
            part_l[pl.ds(2 * i, 2), :, KVR:] = block.reshape(2, rows, 2 * DR)
            return carry

        lax.fori_loop(0, chips, spread, 0)
        near, far = {}, {}
        for i in list(range(1, chips)) + [0]:
            chip = lax.rem(c + i, chips)
            for j in range(2):
                near[i, j] = remote(
                    x_refs[j].at[chip * 2 + 1 - k],
                    bufs[3 * j].at[chip],
                    sems[4 * j].at[i],
                    sems[4 * j + 1].at[i],
                    sibling,
                )
                near[i, j].start()
        for i in range(1, chips):
            chip = lax.rem(c + i, chips)
            for j in range(2):
                from_sib, out_buf, from_far = bufs[3 * j : 3 * j + 3]
                near[i, j].wait_recv()
                out_buf[i] = (
                    x_refs[j][chip * 2 + k].astype(F32) + from_sib[chip].astype(F32)
                ).astype(BF)
                far[i, j] = remote(
                    out_buf.at[i],
                    from_far.at[i],
                    sems[4 * j + 2].at[i],
                    sems[4 * j + 3].at[i],
                    same_core[i - 1],
                )
                far[i, j].start()

        per_tile = 256 // r

        def wq_rows(i, carry):
            at = pl.ds(pl.multiple_of(i * 256, 256), 256)
            block = mm_rows(hidden_ref[:, at], grad_query[...]).astype(BF)
            hsrc[pl.ds(i * per_tile, per_tile), :, :wq_cols] = block.reshape(
                per_tile, r, wq_cols
            )
            return carry

        lax.fori_loop(0, width // 256, wq_rows, 0)
        grad_we = mm_rows(low_ref[...], grad_expanded[...]).astype(BF)
        for j in range(r // rl):
            block = grad_we[:, j * we_cols : (j + 1) * we_cols]
            hsrc[:, j * rl : (j + 1) * rl, wq_cols:] = block.reshape(n_dev, rl, we_cols)
        heads_far = []
        for i in range(1, n_ex):
            for d in range(n_dp):
                copy = remote(
                    hsrc.at[d * n_ex + lax.rem(e + i, n_ex)], heads_mid.at[d, e],
                    h_s.at[i, d], h_r.at[i, d], plane[i - 1],
                )
                copy.start()
                heads_far.append(copy)
        for d in range(n_dp):
            copy = pltpu.make_async_copy(
                hsrc.at[d * n_ex + e], heads_mid.at[d, e], h_r.at[0, d]
            )
            copy.start()
            copy.wait()
        for j in range(2):
            near[0, j].wait_recv()
            sums[j][...] = x_refs[j][e].astype(F32) + bufs[3 * j][c].astype(F32)
        for i in range(1, chips):
            for j in range(2):
                far[i, j].wait_recv()
                sums[j][...] += bufs[3 * j + 2][i].astype(F32)

        at = pl.ds(pl.multiple_of(e * rows, rows), rows)
        cos, sin = att_in[3][at, :], att_in[4][at, :]
        lat_grad, lat_gain = rms_back(lat_ref[:, :KVR], glat_ref[...], sums[1][:, :KVR])
        rope = turn(sums[1][:, KVR:], cos, sin, -1.0)
        lane = lax.broadcasted_iota(jnp.int32, rope.shape, 1)
        rope = jnp.where(lane < DR, rope, 0.0)
        low = jnp.concatenate([lat_grad, rope], axis=1).astype(BF)
        total = sums[0][...] + mm_cols(low, wl_ref[:, :lat_cols])
        tok_grad, tok_gain = rms_back(tok_ref[...].astype(F32), gain_ref[...], total)
        tok_out[...] = gnat_ref[...] + tok_grad
        vec[...] = jnp.zeros_like(vec)
        vec[0:1, :] = jnp.sum(tok_gain, axis=0, keepdims=True)
        vec[1:2, :] = gtwo_ref[...]
        vec[2:3, :KVR] = jnp.sum(lat_gain, axis=0, keepdims=True)
        vec_far = []
        for i in range(1, n_ex):
            copy = remote(vec, vbuf.at[i], v_s.at[i], v_r.at[i], plane[i - 1])
            copy.start()
            vec_far.append(copy)
        for d in range(n_dp):
            block = hidden_ref[at, d * n_ex * r : (d + 1) * n_ex * r]
            block = mm_rows(block, low).reshape(n_ex, r, lat_cols)
            pack[:, d * r : (d + 1) * r, :KVR] = block[:, :, :KVR].astype(BF)
            block = block[:, :, KVR:] + router_ref[:, d * r : (d + 1) * r].astype(F32)
            pack[:, d * r : (d + 1) * r, KVR:] = block.astype(BF)
        pack_near, pack_far = [], []
        for i in list(range(1, chips)) + [0]:
            chip = lax.rem(c + i, chips)
            copy = remote(pack.at[chip * 2 + 1 - k], psib.at[chip], pn_s.at[i], pn_r.at[i], sibling)
            copy.start()
            pack_near.append(copy)
        for copy in heads_far:
            copy.wait_recv()
        heads_col = []
        for i in range(1, n_dp):
            d = lax.rem(z + i, n_dp)
            copy = remote(
                heads_mid.at[d], heads_out.at[z], hz_s.at[i], hz_r.at[i], column[i - 1]
            )
            copy.start()
            heads_col.append(copy)
        copy = pltpu.make_async_copy(heads_mid.at[z], heads_out.at[z], local.at[4])
        copy.start()
        heads_col.append(copy)
        for i in range(1, chips):
            chip = lax.rem(c + i, chips)
            pack_near[i - 1].wait_recv()
            pout[i] = (pack[chip * 2 + k].astype(F32) + psib[chip].astype(F32)).astype(BF)
            copy = remote(pout.at[i], pfar.at[i], pf_s.at[i], pf_r.at[i], same_core[i - 1])
            copy.start()
            pack_far.append(copy)
        for copy in vec_far:
            copy.wait_recv()
            copy.wait_send()
        for i in range(1, n_ex):
            vec[...] += vbuf[i]
        vec_col = []
        for i in range(1, n_dp):
            copy = remote(vec, vzbuf.at[i], vz_s.at[i], vz_r.at[i], column[i - 1])
            copy.start()
            vec_col.append(copy)
        pack_near[chips - 1].wait_recv()
        total = pack[e].astype(F32) + psib[c].astype(F32)
        for i in range(1, chips):
            pack_far[i - 1].wait_recv()
            total = total + pfar[i].astype(F32)
        psum[...] = total.astype(BF).reshape(n_dp, r, lat_cols)
        pack_col = []
        for i in range(1, n_dp):
            copy = remote(
                psum.at[lax.rem(z + i, n_dp)], pbuf.at[i], pc_s.at[i], pc_r.at[i], column[i - 1]
            )
            copy.start()
            pack_col.append(copy)
        result = vec[...]
        for i in range(1, n_dp):
            vec_col[i - 1].wait_recv()
            result = result + vzbuf[i]
        vec_out[...] = result
        result = psum[z].astype(F32)
        for i in range(1, n_dp):
            pack_col[i - 1].wait_recv()
            result = result + pbuf[i].astype(F32)
        pack_out[...] = result

        for i in range(n_dp):
            here = jnp.logical_and(z // hp == part, z == i)

            @pl.when(here)
            def _(i=i):
                pltpu.make_async_copy(
                    wsrc.at[lax.rem(z, hp), part], wout_out.at[i], w_r.at[i]
                ).wait()

            @pl.when(jnp.logical_not(here))
            def _(i=i):
                wait_recv(wout_out.at[i], w_r.at[i], sibling)

        wout_sends(False)
        for copy in list(near.values()) + list(far.values()) + heads_far:
            copy.wait_send()
        for copy in pack_near + pack_far + vec_col + pack_col:
            copy.wait_send()
        for copy in heads_col + others:
            copy.wait()
        for back in backs:
            back.end()

    dma = pltpu.SemaphoreType.DMA
    sds = jax.ShapeDtypeStruct
    vmem = pltpu.VMEM
    scratch = [
        vmem((n_ex, rows, width), BF),
        vmem((seq, 2 * DV), BF),
        vmem((2 * DV, width), F32),
        vmem((seq, 2 * DH), F32),
        vmem((seq, DV), F32),
        vmem((seq, wq.shape[1]), BF),
        vmem((seq, we.shape[1]), BF),
        vmem((seq, 2 * DR), F32),
        vmem((n_ex, rows, lat_cols), BF),
    ]
    scratch += [vmem((chips, rows, width), BF)] * 3 + [vmem((chips, rows, lat_cols), BF)] * 3
    scratch += [
        vmem((rows, width), F32),
        vmem((rows, lat_cols), F32),
        vmem((n_dev, r, head_cols), BF),
        vmem((hp, parts, r, width), BF),
        vmem((n_ex, n_dp * r, lat_cols), BF),
        vmem((chips, n_dp * r, lat_cols), BF),
        vmem((chips, n_dp * r, lat_cols), BF),
        vmem((chips, n_dp * r, lat_cols), BF),
        vmem((n_dp, r, lat_cols), BF),
        vmem((n_dp, r, lat_cols), BF),
        vmem((8, width), F32),
        vmem((n_ex, 8, width), F32),
        vmem((n_dp, 8, width), F32),
    ]
    scratch += [dma((chips,))] * 4 + [dma((5,))] + [dma((chips,))] * 8
    scratch += [dma((n_ex, n_dp))] * 2 + [dma((n_dp,))] * 2 + [dma((hp, parts)), dma((n_dp,))]
    scratch += [dma((chips,))] * 4 + [dma((n_dp,))] * 2 + [dma((3, n_dp))] * 2
    scratch += [dma((n_ex,))] * 2 + [dma((n_dp,))] * 2
    for total in totals:
        scratch += ExpertsBack.scratch(total, n_dp, inner)
    outs = pl.pallas_call(
        kernel,
        out_shape=[
            sds((rows, width), F32),
            sds((8, width), F32),
            sds((r, lat_cols), F32),
            sds((n_dp, n_ex, r, head_cols), BF),
            sds((n_dp, n_ex, r, head_cols), BF),
            sds((n_dp, r, width), BF),
        ]
        + [sds(array.shape, BF) for array in shared]
        + [ExpertsBack.out(total, n_dp, inner) for total in totals],
        in_specs=[ANY] + [VMEM] * 21 + [ANY] * (3 + extra),
        out_specs=[VMEM] * 3 + [ANY] * (6 + extra),
        scratch_shapes=scratch,
        compiler_params=params(collective_id),
    )(grad, *attend, hidden, latent_low, *own, *shared, *totals)
    return outs[:3], outs[4], outs[5], outs[6:9], outs[9:]


def shards(
    tokens,
    cotangent,
    lengths,
    routes,
    place_order,
    attn_gain,
    w_query,
    w_latent,
    latent_gain,
    w_expand,
    w_out,
    ffn_gain,
    w_router,
    shared_gate,
    shared_up,
    shared_down,
    expert_gate,
    expert_up,
    expert_down,
):
    rows, width = tokens.shape
    n_dp = lax.axis_size("dp")
    n_ex = lax.axis_size("expert")
    chips = n_ex // 2
    z = lax.axis_index("dp")
    e = lax.axis_index("expert")
    chip = e // 2
    n_experts = w_router.shape[1]
    top_k = routes.shape[1]
    capacity = (rows * top_k * 5 + 4 * n_experts - 1) // (4 * n_experts)
    cap = (capacity + 15) // 16 * 16
    seq = rows * n_ex
    r = w_query.shape[0]
    rl = w_expand.shape[0]
    hp = H // n_ex
    parts = DV // r
    heads = [
        (d * n_ex + (j // parts) * parts) * r // DV
        for j in range(n_ex)
        for d in range(j % parts * hp, j % parts * hp + hp)
    ]
    heads_back = [heads.index(h) for h in range(H)]
    inner = n_experts // chips
    my_local = lax.rem(z, inner)
    ff_e = expert_gate.shape[2]
    ff_s = shared_gate.shape[1] // inner
    lat = KVR + DR
    head_cols = hp * (DH + DR)
    kv_cols = hp * (DH + DV)

    def to_owner_order(values):
        cut = values.reshape(values.shape[0], n_dp, n_ex, r)
        return cut.transpose(0, 2, 1, 3).reshape(values.shape)

    def from_owner_order(values):
        cut = values.reshape(values.shape[0], n_ex, n_dp, r)
        return cut.transpose(0, 2, 1, 3).reshape(values.shape)

    def pick(values, index, axis=0):
        return lax.dynamic_index_in_dim(values, index, axis, keepdims=False)

    wq_send = jnp.take(w_query.reshape(r, H, DH + DR), jnp.array(heads), axis=1)
    wq_send = wq_send.reshape(r, n_ex, hp, DH + DR)
    wq_send = jnp.concatenate(
        [
            wq_send[..., :DH].reshape(r, n_ex, hp * DH),
            wq_send[..., DH:].reshape(r, n_ex, hp * DR),
        ],
        axis=-1,
    ).transpose(1, 0, 2)
    we_send = jnp.take(w_expand.reshape(rl, H, DH + DV), jnp.array(heads), axis=1)
    we_cols = rl * kv_cols // r
    we_send = we_send.reshape(rl, n_ex, r // rl, we_cols).transpose(1, 2, 0, 3)
    we_send = we_send.reshape(n_ex, r, we_cols)
    wa_send = jnp.concatenate([wq_send, we_send], axis=-1)
    slot_own = slot_places(routes, place_order[0], capacity)
    slot_place = jnp.where(slot_own >= 0, slot_own - routes * capacity, -1)
    slot_cols = 2 * rows * top_k // r
    slot_pack = jnp.stack([routes, slot_place]).astype(BF).reshape(2, r, slot_cols // 2)
    small_cols = lat + n_experts + 3
    pack_cols = (small_cols + slot_cols + 127) // 128 * 128
    pack = jnp.concatenate(
        [
            w_latent,
            w_router,
            attn_gain[:, None],
            ffn_gain[:, None],
            jnp.pad(latent_gain, (0, r - rl))[:, None],
            slot_pack[0],
            slot_pack[1],
            jnp.zeros((r, pack_cols - small_cols - slot_cols), BF),
        ],
        axis=1,
    )
    cot_owner = to_owner_order(cotangent)
    tok_all, wa_all, pk_all = first_exchange(tokens, wa_send, pack, n_dp, n_ex, 1)
    wq = wa_all[..., :head_cols].reshape(width, head_cols)
    wexp = wa_all[..., head_cols:].reshape(n_dp * n_ex, r // rl, rl, we_cols)
    wexp = wexp.transpose(0, 2, 1, 3).reshape(KVR, kv_cols)
    pk_flat = pk_all.reshape(width, pack_cols)
    w_lat = pk_flat[:, :lat]
    gain_one = pk_flat[:, lat + n_experts].astype(F32)
    gain_two = pk_all[..., lat + n_experts + 1].transpose(1, 0, 2).reshape(width).astype(F32)
    router = pk_all[..., lat : lat + n_experts].transpose(1, 0, 2, 3).reshape(width, n_experts)
    gain_lat = (
        pk_all[..., lat + n_experts + 2].reshape(n_dp * n_ex, r)[:, :rl].reshape(KVR).astype(F32)
    )
    col_groups = [[o * inner + i for i in range(inner)] for o in range(n_dp // inner)]
    cot_send, _ = lax.optimization_barrier((cot_owner, pk_all))
    cot_col = lax.all_gather(cot_send, "dp", axis=0, tiled=True, axis_index_groups=col_groups)
    slots_all = n_experts * capacity
    slot_col = pick(pk_all[..., small_cols : small_cols + slot_cols], e, 1)
    slot_col = lax.dynamic_slice_in_dim(slot_col, z - my_local, inner, 0).astype(jnp.int32)
    slot_col = slot_col.reshape(inner, r, 2, slot_cols // 2).transpose(2, 0, 1, 3)
    slot_col = slot_col.reshape(2, inner, rows, top_k)
    slot_ids = jnp.where(
        slot_col[1] >= 0,
        slot_col[0] * capacity + slot_col[1] + (jnp.arange(inner) * slots_all)[:, None, None],
        -1,
    ).reshape(inner * rows, top_k)
    place = jnp.arange(cap)
    far_experts = [lax.rem(chip + m, chips) * inner + my_local for m in range(chips)]
    wanted = (
        jnp.stack(far_experts)[:, None, None] * capacity
        + (jnp.arange(inner) * slots_all)[None, :, None]
        + place[None, None, :]
    )
    wanted = jnp.where(place[None, None, :] < capacity, wanted, -2).reshape(-1)
    n_slots = wanted.shape[0]
    per_far = n_slots // chips
    hot = sum((wanted[:, None] == slot_ids[None, :, j]).astype(BF) for j in range(top_k))
    hot_t = sum((slot_ids[:, j][:, None] == wanted[None, :]).astype(BF) for j in range(top_k))

    def through(values, way):
        cut = values.reshape(chips, per_far, -1)
        got = [cut[0]]
        for m in range(1, chips):
            perm = [(i, (i + 2 * m * way) % n_ex) for i in range(n_ex)]
            got.append(lax.ppermute(cut[m], "expert", perm))
        return jnp.concatenate(got, axis=0)

    positions = jnp.arange(seq)
    cos_table, sine_table = rope_tables(positions)
    cos_wide, sine_wide = jnp.tile(cos_table, (1, 4)), jnp.tile(sine_table, (1, 4))
    keep = (positions < lengths[0]).astype(F32)[None]
    attend_out, wo_rows, residual, x_col, (wg, wu), (sgate, sup, sdown) = forward_exchange(
        [tok_all, gain_one[None], wq, pk_flat, gain_lat[None], wexp, cos_wide, sine_wide, keep],
        to_owner_order(w_out),
        to_owner_order(tokens),
        gain_two[None],
        [w.reshape(-1, n_ex, r, ff_e) for w in (expert_gate, expert_up)],
        [w.reshape(r, inner, ff_s).transpose(1, 0, 2) for w in (shared_gate, shared_up, shared_down)],
        n_dp,
        n_ex,
        inner,
        2,
    )
    hidden_one, latent_raw, latent_low, qcat, kcat, value, lse, attended = attend_out
    wo_rows = wo_rows.reshape(hp * DV, width)
    sgate, sup, sdown = (w.reshape(width, ff_s) for w in (sgate, sup, sdown))
    hidden_two = pick(x_col, my_local)
    x_col = x_col.reshape(inner * rows, width)

    x_in, (wd,) = between(
        mm(hot, x_col).astype(BF).reshape(chips, per_far, width),
        1,
        [expert_down.reshape(-1, n_ex, r, ff_e)],
        [],
        n_dp,
        n_ex,
        inner,
        8,
    )
    x_in = x_in.reshape(n_slots, width)
    grad_in = through(mm(hot, cot_col).astype(BF), 1)
    wg, wu, wd = (w.reshape(width, ff_e) for w in (wg, wu, wd))

    def probs_of(logits):
        top = jnp.max(logits, axis=-1, keepdims=True)
        exp_logits = jnp.exp(logits - top)
        return exp_logits / jnp.sum(exp_logits, axis=-1, keepdims=True)

    shared_a = mm(x_col, sgate)
    shared_b = mm(x_col, sup)
    shared_hidden, shared_back = jax.vjp(swiglu, shared_a, shared_b)
    shared_hidden = shared_hidden.astype(BF)
    shared_out = mm_cols(shared_hidden, sdown)
    grad_sa, grad_sb = (v.astype(BF) for v in shared_back(mm(cot_col, sdown)))
    shared_grads = [
        mm_rows(x_col, grad_sa).astype(BF),
        mm_rows(x_col, grad_sb).astype(BF),
        mm_rows(cot_col, shared_hidden).astype(BF),
    ]
    shared_dx = mm_cols(grad_sa, sgate) + mm_cols(grad_sb, sup)

    slot_probs = probs_of(mm(x_in, router))
    slot_gate = jnp.sum(
        jnp.where(jnp.arange(n_experts)[None, :] == far_experts[0], slot_probs, 0.0),
        axis=1,
        keepdims=True,
    )
    expert_a = mm(x_in, wg)
    expert_b = mm(x_in, wu)
    expert_hidden, expert_back = jax.vjp(swiglu, expert_a, expert_b)
    expert_hidden = expert_hidden.astype(BF)
    rows_back = through(mm_cols(expert_hidden, wd).astype(BF), -1)
    slot_grad = (slot_gate * grad_in.astype(F32)).astype(BF)
    grad_ea, grad_eb = (v.astype(BF) for v in expert_back(mm(slot_grad, wd)))
    expert_totals = [
        mm_rows(left, right).astype(BF).reshape(n_ex, n_dp, r, ff_e)
        for left, right in ((x_in, grad_ea), (x_in, grad_eb), (slot_grad, expert_hidden))
    ]
    dx_back, (down_back,) = between(
        (mm_cols(grad_ea, wg) + mm_cols(grad_eb, wu)).astype(BF).reshape(chips, per_far, width),
        -1,
        [],
        expert_totals[2:],
        n_dp,
        n_ex,
        inner,
        9,
    )
    dx_back = dx_back.reshape(n_slots, width)

    col_probs = probs_of(mm(x_col, router))
    expert_axis = jnp.arange(n_experts)[None, :]
    gates = [
        jnp.sum(jnp.where(expert_axis == expert, col_probs, 0.0), axis=1, keepdims=True)
        for expert in far_experts
    ]
    gate_hot = jnp.concatenate(
        [hot_t[:, m * per_far : (m + 1) * per_far] * gates[m].astype(BF) for m in range(chips)],
        axis=1,
    )
    out_col = (mm(gate_hot, rows_back) + shared_out).astype(BF)
    dots = mm_cols(cot_col, rows_back) * hot_t.astype(F32)
    dots = jnp.sum(dots.reshape(inner * rows, chips, per_far), axis=-1)
    grad_probs_col = sum(
        jnp.where(expert_axis == far_experts[m], dots[:, m : m + 1], 0.0) for m in range(chips)
    )
    dx_col = mm(hot_t, dx_back) + shared_dx
    dx_send = jnp.concatenate(
        [dx_col, grad_probs_col, jnp.zeros((inner * rows, 128 - n_experts), F32)], axis=1
    ).astype(BF)
    dx_sum, shared_sums, (gate_back,) = column_sum(
        dx_send.reshape(inner, rows, width + 128),
        [grad.reshape(n_ex, n_dp, r, ff_s) for grad in shared_grads],
        expert_totals[:1],
        n_dp,
        n_ex,
        inner,
        3,
    )
    router_probs = lax.dynamic_slice_in_dim(col_probs, my_local * rows, rows, 0)
    grad_probs = dx_sum[:, width : width + n_experts]
    grad_logits = (
        router_probs * (grad_probs - jnp.sum(grad_probs * router_probs, axis=-1, keepdims=True))
    ).astype(BF)
    grad_router = mm_rows(hidden_two, grad_logits)
    grad_hidden_two = dx_sum[:, :width] + mm_cols(grad_logits, router)
    _, norm_two_back = jax.vjp(rms_norm, residual, gain_two)
    grad_resid_norm, grad_gain_two = norm_two_back(grad_hidden_two)
    grad_residual = cot_owner.astype(F32) + grad_resid_norm

    out_col, _ = lax.optimization_barrier((out_col, dx_sum))
    out_sum = lax.psum_scatter(
        out_col, "dp", scatter_dimension=0, tiled=True, axis_index_groups=col_groups
    )
    out_tokens = from_owner_order((residual + out_sum.astype(F32)).astype(BF))
    latent_own = lax.dynamic_slice_in_dim(latent_raw, e * rows, rows, 0)
    router_back = jnp.pad(
        grad_router.reshape(n_ex, n_dp * r, n_experts),
        ((0, 0), (0, 0), (DR, DR - n_experts)),
    ).astype(BF)
    (grad_tokens, vec_sum, pack_sum), heads_got, wout_got, shared_got, (up_back,) = (
        backward_exchange(
            grad_residual.astype(BF),
            [wo_rows, wq, wexp, cos_wide, sine_wide, keep, qcat, kcat, value, lse, attended],
            hidden_one,
            latent_low,
            [
                pk_flat,
                latent_own,
                tokens,
                gain_one[None],
                gain_lat[None],
                from_owner_order(grad_residual),
                router_back,
                grad_gain_two[None],
            ],
            shared_sums,
            expert_totals[1:2],
            n_dp,
            n_ex,
            inner,
            5,
        )
    )

    def added(values):
        return jnp.sum(values.astype(F32), axis=0)

    heads_all = added(heads_got)
    sum_wq = heads_all[..., :head_cols].transpose(1, 0, 2)
    sum_wq = jnp.concatenate(
        [
            sum_wq[..., : hp * DH].reshape(r, n_ex, hp, DH),
            sum_wq[..., hp * DH :].reshape(r, n_ex, hp, DR),
        ],
        axis=-1,
    ).reshape(r, H, DH + DR)
    sum_wq = jnp.take(sum_wq, jnp.array(heads_back), axis=1).reshape(r, H * (DH + DR))
    sum_we = heads_all[..., head_cols:].reshape(n_ex, r // rl, rl, we_cols).transpose(2, 0, 1, 3)
    sum_we = jnp.take(sum_we.reshape(rl, H, DH + DV), jnp.array(heads_back), axis=1)
    sum_we = sum_we.reshape(rl, H * (DH + DV))
    sum_wout = from_owner_order(added(wout_got))
    device = z * n_ex + e
    sum_gain_one = lax.dynamic_slice_in_dim(vec_sum[0], device * r, r, 0)
    sum_gain_two = lax.dynamic_slice_in_dim(vec_sum[1], (e * n_dp + z) * r, r, 0)
    sum_gain_lat = lax.dynamic_slice_in_dim(vec_sum[2], device * rl, rl, 0)
    sum_sgate, sum_sup, sum_sdown = (
        added(got.reshape(n_dp // inner, inner, r, ff_s)).transpose(1, 0, 2).reshape(r, -1)
        for got in shared_got
    )
    sum_egate, sum_eup, sum_edown = (
        added(back).reshape(-1, n_ex * r, ff_e) for back in (gate_back, up_back, down_back)
    )
    return (
        out_tokens,
        grad_tokens,
        sum_gain_one,
        sum_wq,
        pack_sum[:, :lat],
        sum_gain_lat,
        sum_we,
        sum_wout,
        sum_gain_two,
        pack_sum[:, lat : lat + n_experts],
        sum_sgate,
        sum_sup,
        sum_sdown,
        sum_egate,
        sum_eup,
        sum_edown,
    )


def solution(mesh):
    both = ("dp", "expert")
    in_specs = (
        P(both, None),
        P(both, None),
        P("dp"),
        P(both, None),
        P(both, None),
        P(both),
        P(both, None),
        P(both, None),
        P(both),
        P(both, None),
        P(both, None),
        P(both),
        P(both, None),
        P(both, None),
        P(both, None),
        P(both, None),
        P("expert", "dp", None),
        P("expert", "dp", None),
        P("expert", "dp", None),
    )
    out_specs = (
        P(both, None),
        P(both, None),
        P(both),
        P(both, None),
        P(both, None),
        P(both),
        P(both, None),
        P(both, None),
        P(both),
        P(both, None),
        P(both, None),
        P(both, None),
        P(both, None),
        P("expert", "dp", None),
        P("expert", "dp", None),
        P("expert", "dp", None),
    )
    return jax.shard_map(shards, mesh=mesh, in_specs=in_specs, out_specs=out_specs, check_vma=False)
```

```python
import jax
import jax.numpy as jnp
from jax import lax
from jax.experimental import pallas as pl
from jax.experimental.pallas import tpu as pltpu
from jax.sharding import PartitionSpec as P

H = 16
DH = 128
DR = 64
DV = 128
KVR = 512

norm_eps = 1e-06
masked_score = -1e30
MESH = pl.DeviceIdType.MESH
ANY = pl.BlockSpec(memory_space=pl.ANY)
VMEM = pl.BlockSpec(memory_space=pltpu.VMEM)
BF = jnp.bfloat16
F32 = jnp.float32


def rms_norm(values, scale_gain):
    return (
        values
        * lax.rsqrt(jnp.mean(values * values, axis=-1, keepdims=True) + norm_eps)
        * scale_gain
    )


def rotate(values, cos_table, sine_table):
    half_dim = values.shape[-1] // 2
    first_half = values[..., :half_dim]
    second_half = values[..., half_dim:]
    return jnp.concatenate(
        [
            first_half * cos_table - second_half * sine_table,
            second_half * cos_table + first_half * sine_table,
        ],
        axis=-1,
    )


def rope_tables(positions):
    half_dim = DR // 2
    inv_freq = 10000.0 ** (-(jnp.arange(half_dim).astype(F32) * 2.0) / DR)
    angles = positions.astype(F32)[:, None] * inv_freq[None, :]
    return (jnp.cos(angles), jnp.sin(angles))


def swiglu(gate_in, up_in):
    return jax.nn.silu(gate_in) * up_in


def mm(left, right):
    return jnp.dot(left, right, preferred_element_type=F32)


def mm_rows(left, right):
    return lax.dot_general(left, right, (((0,), (0,)), ((), ())), preferred_element_type=F32)


def mm_cols(left, right):
    return lax.dot_general(left, right, (((1,), (1,)), ((), ())), preferred_element_type=F32)


def slot_places(route_rows, pair_order, capacity):
    pair_expert = route_rows.reshape(-1)
    earlier = pair_order[None, :] < pair_order[:, None]
    same_expert = pair_expert[None, :] == pair_expert[:, None]
    places = jnp.sum((earlier & same_expert).astype(jnp.int32), axis=1)
    slot_index = jnp.where(places < capacity, pair_expert * capacity + places, -1)
    return slot_index.reshape(route_rows.shape)


def turn(values, cos, sin, sign):
    half = DR // 2
    first = lax.rem(lax.broadcasted_iota(jnp.int32, values.shape, 1), DR) < half
    partner = jnp.where(
        first, -pltpu.roll(values, 2 * DR - half, 1), pltpu.roll(values, half, 1)
    )
    return values * cos + sign * (partner * sin)


def causal(i, tile, keep_ref):
    shape = (tile, (i + 1) * tile)
    query = lax.broadcasted_iota(jnp.int32, shape, 0) + i * tile
    key = lax.broadcasted_iota(jnp.int32, shape, 1)
    return (key <= query) & (keep_ref[:, : shape[1]] > 0.5)


def attend_forward(
    tok, gain, wq, wl, gain_lat, we, cos, sin, keep,
    hidden, latent, latent_low, qcat, kcat, value, lse, attended,
):
    per, rows, width = tok.shape
    seq = per * rows
    tile = 2 * rows
    scale = (DH + DR) ** (-0.5)

    def project(i, carry):
        at = pl.ds(pl.multiple_of(i * tile, tile), tile)
        x = tok[pl.ds(2 * i, 2)].reshape(tile, width).astype(F32)
        root = lax.rsqrt(jnp.mean(x * x, axis=-1, keepdims=True) + norm_eps)
        hid = (x * root * gain[...]).astype(BF)
        hidden[at, :] = hid
        c, s = cos[at, :], sin[at, :]
        query = mm(hid, wq[...])
        rope_q = turn(query[:, 2 * DH :], c, s, 1.0).astype(BF)
        lat = mm(hid, wl[...])
        latent[at, :] = lat
        plain = lat[:, :KVR]
        root = lax.rsqrt(jnp.mean(plain * plain, axis=-1, keepdims=True) + norm_eps)
        low = (plain * root * gain_lat[...]).astype(BF)
        latent_low[at, :] = low
        rope = lat[:, KVR : KVR + 2 * DR]
        lane = lax.broadcasted_iota(jnp.int32, rope.shape, 1)
        rope = jnp.where(lane < DR, rope, pltpu.roll(rope, DR, 1))
        rope = turn(rope, c, s, 1.0)
        expanded = mm(low, we[...]).astype(BF)
        for h in range(2):
            qcat[h, at, :DH] = query[:, h * DH : (h + 1) * DH].astype(BF)
            qcat[h, at, DH:] = rope_q
            mine = (lane < DR) if h == 0 else (lane >= DR)
            kcat[h, at, :DH] = expanded[:, h * (DH + DV) : h * (DH + DV) + DH]
            kcat[h, at, DH:] = jnp.where(mine, rope, 0.0).astype(BF)
            value[h, at, :] = expanded[:, h * (DH + DV) + DH : (h + 1) * (DH + DV)]
        return carry

    lax.fori_loop(0, seq // tile, project, 0)
    for h in range(2):
        for i in range(seq // tile):
            at, upto = slice(i * tile, (i + 1) * tile), slice(0, (i + 1) * tile)
            scores = mm_cols(qcat[h, at, :], kcat[h, upto, :]) * scale
            scores = jnp.where(causal(i, tile, keep), scores, masked_score)
            top = jnp.max(scores, axis=-1, keepdims=True)
            exp_scores = jnp.exp(scores - top)
            total = jnp.sum(exp_scores, axis=-1, keepdims=True)
            probs = (exp_scores / total).astype(BF)
            attended[at, h * DV : (h + 1) * DV] = mm(probs, value[h, upto, :]).astype(BF)
            lse[h, at, :] = jnp.broadcast_to(top + jnp.log(total), (tile, lse.shape[2]))


def attend_backward(
    grad, wo, wq, we, cos, sin, keep, qcat, kcat, value, lse, attended,
    gat, grad_wout, dk, dv, grad_query, grad_expanded, grad_rope,
):
    per, rows, width = grad.shape
    seq = per * rows
    tile = 2 * rows
    scale = (DH + DR) ** (-0.5)
    count = seq // tile
    grad_wout[...] = jnp.zeros_like(grad_wout)

    def project(i, carry):
        at = pl.ds(pl.multiple_of(i * tile, tile), tile)
        block = grad[pl.ds(2 * i, 2)].reshape(tile, width)
        gat[at, :] = mm_cols(block, wo[...]).astype(BF)
        grad_wout[...] += mm_rows(attended[at, :], block)
        return carry

    lax.fori_loop(0, count, project, 0)
    for h in range(2):
        dk[...] = jnp.zeros_like(dk)
        dv[...] = jnp.zeros_like(dv)
        for i in range(count):
            at, upto = slice(i * tile, (i + 1) * tile), slice(0, (i + 1) * tile)
            g = gat[at, h * DV : (h + 1) * DV]
            scores = mm_cols(qcat[h, at, :], kcat[h, upto, :]) * scale
            scores = jnp.where(causal(i, tile, keep), scores, masked_score)
            probs = jnp.exp(scores - lse[h, at, 0:1])
            grad_probs = mm_cols(g, value[h, upto, :])
            inner = jnp.sum(grad_probs * probs, axis=-1, keepdims=True)
            raw = (probs * (grad_probs - inner) * scale).astype(BF)
            grad_q = mm(raw, kcat[h, upto, :])
            grad_query[at, h * DH : (h + 1) * DH] = grad_q[:, :DH].astype(BF)
            rope = grad_q[:, DH:]
            lane = lax.broadcasted_iota(jnp.int32, rope.shape, 1)
            mine = (lane < DR) if h == 0 else (lane >= DR)
            rope = turn(rope, cos[at, :], sin[at, :], -1.0).astype(BF)
            if h == 0:
                grad_query[at, 2 * DH :] = rope
            else:
                grad_query[at, 2 * DH :] = jnp.where(mine, rope, grad_query[at, 2 * DH :])
            dk[upto, :] += mm_rows(raw, qcat[h, at, :])
            dv[upto, :] += mm_rows(probs.astype(BF), g)
        grad_expanded[:, h * (DH + DV) : h * (DH + DV) + DH] = dk[:, :DH].astype(BF)
        grad_expanded[:, h * (DH + DV) + DH : (h + 1) * (DH + DV)] = dv[...].astype(BF)
        rope = dk[:, DH:]
        if h == 0:
            grad_rope[...] = rope
        else:
            grad_rope[...] += pltpu.roll(rope, DR, 1)


def params(collective_id):
    return pltpu.CompilerParams(
        collective_id=collective_id, has_side_effects=True, vmem_limit_bytes=60 << 20
    )


def remote(src, dst, send_sem, recv_sem, device):
    return pltpu.make_async_remote_copy(
        src_ref=src,
        dst_ref=dst,
        send_sem=send_sem,
        recv_sem=recv_sem,
        device_id=device,
        device_id_type=MESH,
    )


def greet(devices):
    barrier = pltpu.get_barrier_semaphore()
    for device in devices:
        pl.semaphore_signal(barrier, inc=1, device_id=device, device_id_type=MESH)
    pl.semaphore_wait(barrier, len(devices))


def places(n_dp, n_ex):
    z = lax.axis_index("dp")
    e = lax.axis_index("expert")
    chips = n_ex // 2
    c, k = e // 2, lax.rem(e, 2)
    sibling = (z, e + 1 - 2 * k)
    same_core = [(z, lax.rem(c + i, chips) * 2 + k) for i in range(1, chips)]
    column = [(lax.rem(z + i, n_dp), e) for i in range(1, n_dp)]
    return z, e, c, k, sibling, same_core, column


def wait_recv(region, sem, device):
    remote(region, region, sem, sem, device).wait_recv()


def column_sum(array, rows_out, shared, totals, n_dp, n_ex, inner, collective_id):
    chips = n_ex // 2
    shape = array.shape[1:]
    extra = len(totals)
    _, _, r, ff_s = shared[0].shape

    def kernel(x_ref, *refs):
        s_in, r_ref, t_refs, refs = refs[:3], refs[3], refs[4 : 4 + extra], refs[4 + extra :]
        o_ref, s_out, r_out, back_refs = refs[0], refs[1:4], refs[4], refs[5 : 5 + extra]
        refs = refs[5 + extra :]
        buf, from_sib, out_buf, from_far = refs[:4]
        send, recv, near_s, near_r, far_s, far_r, r_s, r_r, local = refs[4:13]
        rest = refs[13:]
        z, e, c, k, sibling, same_core, column = places(n_dp, n_ex)
        group = column_group(z, e, inner)
        greet(same_core + [sibling] + column + [(d[0], sibling[1]) for d in column])
        backs = [
            ExpertsBack(t_refs[m], back_refs[m], rest[7 * m : 7 * m + 7], n_dp, n_ex, inner)
            for m in range(extra)
        ]
        copies, rows_back = [], []
        for i in range(1, inner):
            to = lax.rem(z + i, inner)
            copy = remote(x_ref.at[to], buf.at[i], send.at[i], recv.at[i], group[i])
            copy.start()
            copies.append(copy)
        near, far = {}, {}
        for i in list(range(1, chips)) + [0]:
            chip = lax.rem(c + i, chips)
            for m in range(3):
                near[i, m] = remote(
                    s_in[m].at[chip * 2 + 1 - k], from_sib.at[m, i],
                    near_s.at[m, i], near_r.at[m, i], sibling,
                )
                near[i, m].start()
        for back in backs:
            back.begin()
        for i in range(1, chips):
            copy = remote(
                r_ref.at[i], r_out.at[i], r_s.at[i], r_r.at[i], same_core[chips - i - 1]
            )
            copy.start()
            rows_back.append(copy)
        copy = pltpu.make_async_copy(r_ref.at[0], r_out.at[0], local)
        copy.start()
        rows_back.append(copy)

        def pair(i, m):
            chip = lax.rem(c + i, chips)
            near[i, m].wait_recv()

            def row(d, carry):
                out_buf[m, i, d] = (
                    s_in[m][chip * 2 + k, d].astype(F32) + from_sib[m, i, d].astype(F32)
                ).astype(BF)
                return carry

            lax.fori_loop(0, n_dp, row, 0)

        for i in range(1, chips):
            for m in range(3):
                pair(i, m)
                far[i, m] = remote(
                    out_buf.at[m, i], from_far.at[m, i], far_s.at[m, i], far_r.at[m, i],
                    same_core[i - 1],
                )
                far[i, m].start()
        o_ref[...] = x_ref[lax.rem(z, inner)].astype(F32)
        for back in backs:
            back.pass_on()
        for m in range(3):
            pair(0, m)
        for i in range(1, inner):
            copies[i - 1].wait_recv()
            o_ref[...] += buf[i].astype(F32)
        for m in range(3):
            for i in range(1, chips):
                far[i, m].wait_recv()

            def row(d, carry, m=m):
                total = out_buf[m, 0, d].astype(F32)
                for i in range(1, chips):
                    total = total + from_far[m, i, d].astype(F32)
                s_out[m][d] = total.astype(BF)
                return carry

            lax.fori_loop(0, n_dp, row, 0)
        for copy in copies + list(near.values()) + list(far.values()):
            copy.wait_send()
        for copy in rows_back:
            copy.wait()
        for back in backs:
            back.end()

    dma = pltpu.SemaphoreType.DMA
    scratch = [pltpu.VMEM((inner,) + shape, BF)]
    scratch += [pltpu.VMEM((3, chips, n_dp, r, ff_s), BF)] * 3
    scratch += [dma((inner,))] * 2 + [dma((3, chips))] * 4 + [dma((chips,))] * 2 + [dma]
    for total in totals:
        scratch += ExpertsBack.scratch(total, n_dp, inner)
    outs = pl.pallas_call(
        kernel,
        out_shape=[jax.ShapeDtypeStruct(shape, F32)]
        + [jax.ShapeDtypeStruct((n_dp, r, ff_s), BF)] * 3
        + [jax.ShapeDtypeStruct(rows_out.shape, BF)]
        + [ExpertsBack.out(total, n_dp, inner) for total in totals],
        in_specs=[VMEM] * 4 + [ANY] * (1 + extra),
        out_specs=[VMEM] * 4 + [ANY] * (1 + extra),
        scratch_shapes=scratch,
        compiler_params=params(collective_id),
    )(array, *shared, rows_out, *totals)
    return outs[0], outs[1:4], outs[4], outs[5:]


def column_group(z, e, inner):
    start = z // inner * inner
    return [(start + lax.rem(z - start + i, inner), e) for i in range(inner)]


def first_exchange(tok, heads_w, pack, n_dp, n_ex, collective_id):
    chips = n_ex // 2

    def kernel(
        tok_ref, wa_ref, pk_ref, tok_out, wa_out, pk_out,
        t_send, t_recv, ts_send, ts_recv, a_send, a_recv, az_send, az_recv,
        p_send, p_recv, pf_send, pf_recv, ps_send, ps_recv, local,
    ):
        z, e, c, k, sibling, same_core, column = places(n_dp, n_ex)
        plane = [(z, lax.rem(e + i, n_ex)) for i in range(1, n_ex)]
        greet(plane + column)
        wa_far, pk_col, tok_far, near = [], [], [], []
        for i in range(1, n_ex):
            copy = remote(
                wa_ref.at[lax.rem(e + i, n_ex)], wa_out.at[z, e],
                a_send.at[i], a_recv.at[i], plane[i - 1],
            )
            copy.start()
            wa_far.append(copy)
        for i in range(1, n_dp):
            copy = remote(pk_ref, pk_out.at[z, e], p_send.at[i], p_recv.at[i], column[i - 1])
            copy.start()
            pk_col.append(copy)
        for i in range(1, chips):
            copy = remote(tok_ref, tok_out.at[e], t_send.at[i], t_recv.at[i], same_core[i - 1])
            copy.start()
            tok_far.append(copy)
        copy = remote(tok_ref, tok_out.at[e], ts_send.at[0], ts_recv.at[0], sibling)
        copy.start()
        near.append(copy)
        own = [
            pltpu.make_async_copy(wa_ref.at[e], wa_out.at[z, e], local.at[0]),
            pltpu.make_async_copy(pk_ref, pk_out.at[z, e], local.at[1]),
            pltpu.make_async_copy(tok_ref, tok_out.at[e], local.at[2]),
        ]
        for copy in own:
            copy.start()
        for copy in own:
            copy.wait()
        for copy in wa_far:
            copy.wait_recv()
        wa_col = []
        for i in range(1, n_dp):
            copy = remote(
                wa_out.at[z], wa_out.at[z], az_send.at[i], az_recv.at[i], column[i - 1]
            )
            copy.start()
            wa_col.append(copy)
        for copy in pk_col:
            copy.wait_recv()
        pk_far = []
        for i in range(1, chips):
            copy = remote(
                pk_out.at[:, e], pk_out.at[:, e], pf_send.at[i], pf_recv.at[i], same_core[i - 1]
            )
            copy.start()
            pk_far.append(copy)
        copy = remote(pk_out.at[:, e], pk_out.at[:, e], ps_send.at[0], ps_recv.at[0], sibling)
        copy.start()
        near.append(copy)
        for i in range(1, chips):
            source = lax.rem(c + chips - i, chips) * 2 + k
            tok_far[i - 1].wait_recv()
            copy = remote(
                tok_out.at[source], tok_out.at[source], ts_send.at[i], ts_recv.at[i], sibling
            )
            copy.start()
            near.append(copy)
            pk_far[i - 1].wait_recv()
            copy = remote(
                pk_out.at[:, source], pk_out.at[:, source], ps_send.at[i], ps_recv.at[i], sibling
            )
            copy.start()
            near.append(copy)
        for copy in near + wa_col:
            copy.wait()
        for copy in wa_far + pk_col + tok_far + pk_far:
            copy.wait_send()

    dma = pltpu.SemaphoreType.DMA
    return pl.pallas_call(
        kernel,
        out_shape=[
            jax.ShapeDtypeStruct((n_ex,) + tok.shape, tok.dtype),
            jax.ShapeDtypeStruct((n_dp,) + heads_w.shape, heads_w.dtype),
            jax.ShapeDtypeStruct((n_dp, n_ex) + pack.shape, pack.dtype),
        ],
        in_specs=[ANY] * 3,
        out_specs=[ANY] * 3,
        scratch_shapes=[dma((chips,))] * 4
        + [dma((n_ex,))] * 2
        + [dma((n_dp,))] * 4
        + [dma((chips,))] * 4
        + [dma((3,))],
        compiler_params=params(collective_id),
    )(tok, heads_w, pack)


class ExpertsIn:
    @staticmethod
    def scratch(n_dp):
        dma = pltpu.SemaphoreType.DMA
        return [dma((n_dp, 2)), dma((n_dp,)), dma((n_dp,)), dma((n_dp,))]

    @staticmethod
    def out(weight, n_dp, n_ex):
        return jax.ShapeDtypeStruct((n_ex, n_dp) + weight.shape[2:], BF)

    def __init__(self, weight, out, scratch, n_dp, n_ex, inner):
        self.weight, self.out, self.n_dp, self.inner = weight, out, n_dp, inner
        self.send, self.recv, self.sib_send, self.sib_recv = scratch
        self.z, self.e, self.c, self.k, self.sibling, _, _ = places(n_dp, n_ex)
        self.hh = n_ex // 2
        self.local = weight.shape[0]

    def sends(self, start):
        for i in list(range(1, self.n_dp)) + [0]:
            to = lax.rem(self.z + i, self.n_dp)
            expert = lax.rem(to, self.inner)

            def go(i=i, to=to, expert=expert):
                for h in range(2):
                    src = self.weight.at[lax.rem(expert, self.local), pl.ds(h * self.hh, self.hh)]
                    dst = self.out.at[pl.ds(h * self.hh, self.hh), self.z]
                    sem = self.recv.at[self.z]

                    def far(src=src, dst=dst, h=h):
                        copy = remote(src, dst, self.send.at[i, h], sem, (to, 2 * self.c + h))
                        if start:
                            copy.start()
                        else:
                            copy.wait_send()

                    if i:
                        far()
                    else:
                        pl.when(self.k != h)(far)
                        if start:

                            @pl.when(self.k == h)
                            def _(src=src, dst=dst):
                                pltpu.make_async_copy(src, dst, sem).start()

            pl.when(expert // self.local == self.k)(go)

    def begin(self):
        self.sends(True)

    def pass_on(self):
        mine = lax.rem(self.z, self.inner)
        for i in range(self.n_dp):
            d = lax.rem(self.z + self.n_dp - i, self.n_dp)
            region = self.out.at[pl.ds(self.k * self.hh, self.hh), d]
            if i:
                wait_recv(region, self.recv.at[d], self.sibling)
            else:
                from_here = mine // self.local == self.k

                @pl.when(from_here)
                def _(region=region, d=d):
                    src = self.weight.at[
                        lax.rem(mine, self.local), pl.ds(self.k * self.hh, self.hh)
                    ]
                    pltpu.make_async_copy(src, region, self.recv.at[d]).wait()

                @pl.when(jnp.logical_not(from_here))
                def _(region=region, d=d):
                    wait_recv(region, self.recv.at[d], self.sibling)

            remote(
                region, region, self.sib_send.at[i], self.sib_recv.at[i], self.sibling
            ).start()

    def end(self):
        self.sends(False)
        for i in range(self.n_dp):
            d = lax.rem(self.z + self.n_dp - i, self.n_dp)
            mine = self.out.at[pl.ds(self.k * self.hh, self.hh), d]
            remote(
                mine, mine, self.sib_send.at[i], self.sib_recv.at[i], self.sibling
            ).wait_send()
            region = self.out.at[pl.ds((1 - self.k) * self.hh, self.hh), d]
            wait_recv(region, self.sib_recv.at[i], self.sibling)


def forward_exchange(attend, w_out, tok, gain, experts, shared, n_dp, n_ex, inner, collective_id):
    chips = n_ex // 2
    rows, width = tok.shape
    count = len(experts)
    r = w_out.shape[0]
    parts = DV // r
    hp = n_dp // parts
    seq = n_ex * rows

    def kernel(*refs):
        att_in, refs = refs[:9], refs[9:]
        wo_in, tok_ref, gain_ref = refs[:3]
        e_in, s_in = refs[3 : 3 + count], refs[3 + count : 6 + count]
        refs = refs[6 + count :]
        att_out, refs = refs[:8], refs[8:]
        wo_out, res_ref, xcol_ref = refs[:3]
        w_out, s_out = refs[3 : 3 + count], refs[3 + count : 6 + count]
        refs = refs[6 + count :]
        x_ref, from_sib, out_buf, from_far, xbuf = refs[:5]
        (
            near_s, near_r, far_s, far_r, x_s, x_r,
            sh_s, sh_r, sp_s, sp_r, sf_s, sf_r, wo_s, wo_r, local,
        ) = refs[5:20]
        refs = refs[20:]
        z, e, c, k, sibling, same_core, column = places(n_dp, n_ex)
        group = column_group(z, e, inner)
        part = lax.rem(e, parts)
        members = [
            (lax.rem(z + i, n_dp), e - part + lax.rem(part + j, parts))
            for i in range(n_dp)
            for j in range(parts)
        ]
        greet(same_core + column + [(device[0], sibling[1]) for device in column] + members[1:])

        def wo_sends(start):
            for i in range(n_dp):
                target = (lax.rem(z + i, n_dp), e - part + z // hp)
                dst, sem = wo_out.at[lax.rem(z, hp), part], wo_r.at[lax.rem(z, hp), part]

                def far(i=i, target=target, dst=dst, sem=sem):
                    copy = remote(wo_in, dst, wo_s.at[i], sem, target)
                    if start:
                        copy.start()
                    else:
                        copy.wait_send()

                if i:
                    far()
                else:
                    pl.when(z // hp != part)(far)
                    if start:

                        @pl.when(z // hp == part)
                        def _(dst=dst, sem=sem):
                            pltpu.make_async_copy(wo_in, dst, sem).start()

        def wo_arrivals():
            for h in range(hp):
                for p in range(parts):
                    here = jnp.logical_and(part * hp + h == z, part == p)

                    @pl.when(here)
                    def _(h=h, p=p):
                        pltpu.make_async_copy(wo_in, wo_out.at[h, p], wo_r.at[h, p]).wait()

                    @pl.when(jnp.logical_not(here))
                    def _(h=h, p=p):
                        wait_recv(wo_out.at[h, p], wo_r.at[h, p], sibling)

        my_l = lax.rem(z, inner)
        matrices = [
            ExpertsIn(e_in[m], w_out[m], refs[4 * m : 4 * m + 4], n_dp, n_ex, inner)
            for m in range(count)
        ]
        wo_sends(True)
        shared_copies = []
        for i in range(1, n_dp):
            for m in range(3):
                copy = remote(
                    s_in[m].at[lax.rem(lax.rem(z + i, n_dp), inner)], s_out[m].at[e, z],
                    sh_s.at[m, i], sh_r.at[m, i], column[i - 1],
                )
                copy.start()
                shared_copies.append(copy)
        own = [
            pltpu.make_async_copy(s_in[m].at[my_l], s_out[m].at[e, z], local.at[m])
            for m in range(3)
        ]
        for copy in own:
            copy.start()
        matrices[0].begin()
        attend_forward(*att_in, *att_out)
        wo_arrivals()
        wo = wo_out[...].reshape(hp * DV, width)

        def project(i, carry):
            at = pl.ds(pl.multiple_of(i * 2 * rows, 2 * rows), 2 * rows)
            block = mm(att_out[7][at, :], wo).astype(BF)
            x_ref[pl.ds(2 * i, 2)] = block.reshape(2, rows, width)
            return carry

        lax.fori_loop(0, chips, project, 0)
        near = []
        for i in list(range(1, chips)) + [0]:
            chip = lax.rem(c + i, chips)
            copy = remote(
                x_ref.at[chip * 2 + 1 - k], from_sib.at[chip], near_s.at[i], near_r.at[i], sibling
            )
            copy.start()
            near.append(copy)
        far = []
        for i in range(1, chips):
            chip = lax.rem(c + i, chips)
            near[i - 1].wait_recv()
            out_buf[i] = (
                x_ref[chip * 2 + k].astype(F32) + from_sib[chip].astype(F32)
            ).astype(BF)
            copy = remote(out_buf.at[i], from_far.at[i], far_s.at[i], far_r.at[i], same_core[i - 1])
            copy.start()
            far.append(copy)
        near[chips - 1].wait_recv()
        res_ref[...] = x_ref[e].astype(F32) + from_sib[c].astype(F32) + tok_ref[...].astype(F32)
        for i in range(1, chips):
            far[i - 1].wait_recv()
            res_ref[...] += from_far[i].astype(F32)
        residual = res_ref[...]
        scale = lax.rsqrt(jnp.mean(residual * residual, axis=-1, keepdims=True) + norm_eps)
        xbuf[...] = (residual * scale * gain_ref[...]).astype(BF)
        x_copies = []
        for i in range(1, inner):
            copy = remote(xbuf, xcol_ref.at[my_l], x_s.at[i], x_r.at[i], group[i])
            copy.start()
            x_copies.append(copy)
        x_own = pltpu.make_async_copy(xbuf, xcol_ref.at[my_l], local.at[3])
        x_own.start()
        for matrix in matrices[1:]:
            matrix.begin()
        for copy in own:
            copy.wait()
        for copy in shared_copies:
            copy.wait_recv()
        plane, to_sib = [], []
        for m in range(3):
            block = s_out[m].at[e]
            for i in range(1, chips):
                copy = remote(block, block, sp_s.at[m, i], sp_r.at[m, i], same_core[i - 1])
                copy.start()
                plane.append(copy)
            copy = remote(block, block, sf_s.at[m, 0], sf_r.at[m, 0], sibling)
            copy.start()
            to_sib.append(copy)
        for m in range(3):
            for i in range(1, chips):
                plane[m * (chips - 1) + i - 1].wait_recv()
                block = s_out[m].at[lax.rem(c + chips - i, chips) * 2 + k]
                copy = remote(block, block, sf_s.at[m, i], sf_r.at[m, i], sibling)
                copy.start()
                to_sib.append(copy)
        for matrix in matrices:
            matrix.pass_on()
        for copy in x_copies + to_sib:
            copy.wait()
        x_own.wait()
        for copy in plane + shared_copies + near + far:
            copy.wait_send()
        wo_sends(False)
        for matrix in matrices:
            matrix.end()

    dma = pltpu.SemaphoreType.DMA
    ff_s = shared[0].shape[2]
    scratch = []
    for _ in experts:
        scratch += ExpertsIn.scratch(n_dp)
    sds = jax.ShapeDtypeStruct
    outs = pl.pallas_call(
        kernel,
        out_shape=[
            sds((seq, width), BF),
            sds((seq, attend[3].shape[1]), F32),
            sds((seq, KVR), BF),
            sds((2, seq, 2 * DH), BF),
            sds((2, seq, 2 * DH), BF),
            sds((2, seq, DV), BF),
            sds((2, seq, 128), F32),
            sds((seq, 2 * DV), BF),
            sds((hp, parts, r, width), BF),
            sds((rows, width), F32),
            sds((inner, rows, width), BF),
        ]
        + [ExpertsIn.out(w, n_dp, n_ex) for w in experts]
        + [sds((n_ex, n_dp, r, ff_s), BF)] * 3,
        in_specs=[VMEM] * 9 + [ANY] + [VMEM] * 2 + [ANY] * (3 + count),
        out_specs=[VMEM] * 10 + [ANY] * (4 + count),
        scratch_shapes=[pltpu.VMEM((n_ex, rows, width), BF)]
        + [pltpu.VMEM((chips, rows, width), BF)] * 3
        + [pltpu.VMEM((rows, width), BF)]
        + [dma((chips,))] * 4
        + [dma((inner,))] * 2
        + [dma((3, n_dp))] * 2
        + [dma((3, chips))] * 4
        + [dma((n_dp,)), dma((hp, parts)), dma((4,))]
        + scratch,
        compiler_params=params(collective_id),
    )(*attend, w_out, tok, gain, *experts, *shared)
    return outs[:8], outs[8], outs[9], outs[10], outs[11 : 11 + count], outs[11 + count :]


def silu_parts(a):
    sig = 1.0 / (1.0 + jnp.exp(-a))
    return a * sig, sig * (1.0 + a * (1.0 - sig))


def dispatch(blocks, x, cot, shared, weight, n_dp, n_ex, inner, collective_id):
    chips = n_ex // 2
    rows, width = x.shape
    ff = shared[0].shape[1]
    tile = 256

    def kernel(
        b_ref, x_hbm, c_hbm, g_hbm, u_hbm, d_hbm, w_ref,
        o_ref, w_out, out_ref, dx_ref, gg_ref, gu_ref, gd_ref,
        x_v, c_v, g_v, u_v, d_v, hid, ga, gb, send, recv, loads, *rest,
    ):
        z, e, c, k, sibling, same_core, column = places(n_dp, n_ex)
        greet(same_core + [sibling] + column + [(device[0], sibling[1]) for device in column])
        matrix = ExpertsIn(w_ref, w_out, rest, n_dp, n_ex, inner)
        copies = []
        for i in range(1, chips):
            copy = remote(b_ref.at[i], o_ref.at[i], send.at[i], recv.at[i], same_core[i - 1])
            copy.start()
            copies.append(copy)
        copy = pltpu.make_async_copy(b_ref.at[0], o_ref.at[0], loads.at[0])
        copy.start()
        copies.append(copy)
        matrix.begin()
        moves = [
            pltpu.make_async_copy(src, dst, loads.at[1 + j])
            for j, (src, dst) in enumerate(
                [(x_hbm, x_v), (g_hbm, g_v), (u_hbm, u_v), (c_hbm, c_v), (d_hbm, d_v)]
            )
        ]
        for copy in moves:
            copy.start()
        for copy in moves:
            copy.wait()

        def rows_of(i, carry):
            at = pl.ds(pl.multiple_of(i * tile, tile), tile)
            first = mm(x_v[at, :], g_v[...])
            second = mm(x_v[at, :], u_v[...])
            silu, slope = silu_parts(first)
            low = (silu * second).astype(BF)
            hid[at, :] = low
            out_ref[at, :] = mm_cols(low, d_v[...])
            back = mm(c_v[at, :], d_v[...])
            low_a = (back * second * slope).astype(BF)
            low_b = (back * silu).astype(BF)
            ga[at, :] = low_a
            gb[at, :] = low_b
            dx_ref[at, :] = mm_cols(low_a, g_v[...]) + mm_cols(low_b, u_v[...])
            return carry

        lax.fori_loop(0, rows // tile, rows_of, 0)

        def columns_of(j, carry):
            at = pl.ds(pl.multiple_of(j * tile, tile), tile)
            gg_ref[at, :] = mm_rows(x_v[:, at], ga[...]).astype(BF)
            gu_ref[at, :] = mm_rows(x_v[:, at], gb[...]).astype(BF)
            gd_ref[at, :] = mm_rows(c_v[:, at], hid[...]).astype(BF)
            return carry

        lax.fori_loop(0, width // tile, columns_of, 0)
        matrix.pass_on()
        for copy in copies:
            copy.wait()
        matrix.end()

    dma = pltpu.SemaphoreType.DMA
    sds = jax.ShapeDtypeStruct
    vmem = pltpu.VMEM
    outs = pl.pallas_call(
        kernel,
        out_shape=[sds(blocks.shape, BF), ExpertsIn.out(weight, n_dp, n_ex)]
        + [sds((rows, width), F32)] * 2
        + [sds((width, ff), BF)] * 3,
        in_specs=[ANY] * 7,
        out_specs=[ANY] * 2 + [VMEM] * 5,
        scratch_shapes=[vmem((rows, width), BF)] * 2
        + [vmem((width, ff), BF)] * 3
        + [vmem((rows, ff), BF)] * 3
        + [dma((chips,)), dma((chips,)), dma((6,))]
        + ExpertsIn.scratch(n_dp),
        compiler_params=params(collective_id),
    )(blocks, x, cot, *shared, weight)
    return outs[0], outs[1], outs[2], outs[3], outs[4:]


def experts_back(values, weights, dots, n_dp, n_ex, inner, collective_id):
    chips = n_ex // 2
    n_slots, width = values[0].shape
    ff = values[2].shape[1]
    per_far = n_slots // chips
    r = width // (n_dp * n_ex)
    tile = 256
    span = n_dp * r

    def kernel(*refs):
        v_hbm, w_hbm, dots_ref, refs = refs[:5], refs[5:8], refs[8], refs[9:]
        dx_out, dots_out, back_out, g_out, refs = refs[0], refs[1], refs[2], refs[3:5], refs[5:]
        x_v, s_v, a_v, b_v, h_v, wg, wu, wd, dx_v, total, stage = refs[:11]
        loads, send, recv, d_send, d_recv, local, out_sem = refs[11:18]
        z, e, c, k, sibling, same_core, column = places(n_dp, n_ex)
        moves = [
            pltpu.make_async_copy(src, dst, loads.at[j])
            for j, (src, dst) in enumerate(
                zip((*v_hbm, *w_hbm), (x_v, s_v, a_v, b_v, h_v, wg, wu, wd))
            )
        ]
        for j in (1, 4, 7, 2, 3, 5, 6, 0):
            moves[j].start()
        greet(same_core + [sibling] + column + [(device[0], sibling[1]) for device in column])
        back = ExpertsBack(total, back_out, refs[18:], n_dp, n_ex, inner)
        dot_copies = []
        for i in range(1, chips):
            copy = remote(
                dots_ref.at[i], dots_out.at[i], d_send.at[i], d_recv.at[i],
                same_core[chips - i - 1],
            )
            copy.start()
            dot_copies.append(copy)
        copy = pltpu.make_async_copy(dots_ref.at[0], dots_out.at[0], local.at[0])
        copy.start()
        dot_copies.append(copy)
        moves[1].wait()
        moves[4].wait()

        def down_rows(t, carry):
            j = lax.rem(t + (1 - k) * (n_ex // 2), n_ex)
            at = pl.ds(pl.multiple_of(j * span, span), span)
            block = mm_rows(s_v[:, at], h_v[...]).astype(BF)
            total[j] = block.reshape(n_dp, r, ff)
            return carry

        lax.fori_loop(0, n_ex, down_rows, 0)
        back.begin()
        for j in (7, 2, 3):
            moves[j].wait()

        def hidden_rows(i, carry):
            at = pl.ds(pl.multiple_of(i * tile, tile), tile)
            grad = mm(s_v[at, :], wd[...])
            silu, slope = silu_parts(a_v[at, :].astype(F32))
            second = b_v[at, :].astype(F32)
            a_v[at, :] = (grad * second * slope).astype(BF)
            b_v[at, :] = (grad * silu).astype(BF)
            return carry

        lax.fori_loop(0, n_slots // tile, hidden_rows, 0)
        moves[5].wait()
        moves[6].wait()
        copies = []
        for i in list(range(1, chips)) + [0]:
            at = slice(i * per_far, (i + 1) * per_far)
            block = mm_cols(a_v[at, :], wg[...]) + mm_cols(b_v[at, :], wu[...])
            dx_v[i] = block.astype(BF)
            if i:
                copy = remote(
                    dx_v.at[i], dx_out.at[i], send.at[i], recv.at[i], same_core[chips - i - 1]
                )
            else:
                copy = pltpu.make_async_copy(dx_v.at[0], dx_out.at[0], local.at[1])
            copy.start()
            copies.append(copy)
            if i == 1:
                back.pass_on()
        moves[0].wait()

        def other_rows(j, carry):
            at = pl.ds(pl.multiple_of(j * span, span), span)
            for m, side in enumerate((a_v, b_v)):

                @pl.when(j > 0)
                def _(m=m):
                    pltpu.make_async_copy(stage.at[m], g_out[m].at[j - 1], out_sem.at[m]).wait()

                block = mm_rows(x_v[:, at], side[...]).astype(BF)
                stage[m] = block.reshape(n_dp, r, ff)
                pltpu.make_async_copy(stage.at[m], g_out[m].at[j], out_sem.at[m]).start()
            return carry

        lax.fori_loop(0, n_ex, other_rows, 0)
        for m in range(2):
            pltpu.make_async_copy(stage.at[m], g_out[m].at[n_ex - 1], out_sem.at[m]).wait()
        for copy in copies + dot_copies:
            copy.wait()
        back.end()

    dma = pltpu.SemaphoreType.DMA
    sds = jax.ShapeDtypeStruct
    vmem = pltpu.VMEM
    total = sds((n_ex, n_dp, r, ff), BF)
    outs = pl.pallas_call(
        kernel,
        out_shape=[
            sds((chips, per_far, width), BF),
            sds(dots.shape, BF),
            ExpertsBack.out(total, n_dp, inner),
            total,
            total,
        ],
        in_specs=[ANY] * 9,
        out_specs=[ANY] * 5,
        scratch_shapes=[vmem((n_slots, width), BF)] * 2
        + [vmem((n_slots, ff), BF)] * 3
        + [vmem((width, ff), BF)] * 3
        + [
            vmem((chips, per_far, width), BF),
            vmem(total.shape, BF),
            vmem((2, n_dp, r, ff), BF),
            dma((8,)),
        ]
        + [dma((chips,))] * 4
        + [dma((2,))] * 2
        + ExpertsBack.scratch(total, n_dp, inner),
        compiler_params=params(collective_id),
    )(*values, *weights, dots)
    return outs[0], outs[1], outs[2], outs[3:]


class ExpertsBack:
    @staticmethod
    def scratch(total, n_dp, inner):
        n_ex, _, r, ff = total.shape
        dma = pltpu.SemaphoreType.DMA
        return [
            pltpu.VMEM((n_ex // 2, n_dp, r, ff), BF),
            pltpu.VMEM((n_ex // 2, n_dp, r, ff), BF),
            dma((n_dp,)),
            dma((n_dp,)),
            dma((n_dp,)),
            dma((n_dp,)),
            dma((n_dp // inner, 2, 2)),
        ]

    @staticmethod
    def out(total, n_dp, inner):
        n_ex, _, r, ff = total.shape
        return jax.ShapeDtypeStruct((n_dp // inner, 2, n_ex, r, ff), BF)

    def __init__(self, total, out, scratch, n_dp, n_ex, inner):
        self.total, self.out, self.n_dp, self.inner = total, out, n_dp, inner
        self.own, self.sib, self.near_s, self.near_r, self.load, self.send, self.recv = scratch
        self.z, self.e, self.c, self.k, self.sibling, _, _ = places(n_dp, n_ex)
        self.hh = n_ex // 2

    def near(self, i):
        d = lax.rem(self.z + i, self.n_dp)
        return remote(
            self.total.at[pl.ds((1 - self.k) * self.hh, self.hh), d],
            self.sib.at[:, d], self.near_s.at[i], self.near_r.at[i], self.sibling,
        )

    def loads(self, i):
        d = lax.rem(self.z + i, self.n_dp)
        return pltpu.make_async_copy(
            self.total.at[pl.ds(self.k * self.hh, self.hh), d], self.own.at[:, d], self.load.at[i]
        )

    def order(self):
        return list(range(1, self.n_dp)) + [0]

    def begin(self):
        for i in self.order():
            self.near(i).start()
            self.loads(i).start()

    def route(self, i):
        d = lax.rem(self.z + i, self.n_dp)
        expert = lax.rem(self.z, self.inner)
        dst = self.out.at[
            self.z // self.inner, lax.rem(expert, 2), pl.ds(self.k * self.hh, self.hh)
        ]
        sem = self.recv.at[self.z // self.inner, lax.rem(expert, 2), self.k]
        return self.own.at[:, d], dst, sem, d, expert // 2

    def stay(self):
        src, dst, sem, _, _ = self.route(0)
        return pltpu.make_async_copy(src, dst, sem)

    def go(self, i):
        src, dst, sem, d, core = self.route(i)
        return remote(src, dst, self.send.at[i], sem, (d, 2 * self.c + core))

    def here(self):
        return lax.rem(self.z, self.inner) // 2 == self.k

    def pass_on(self):
        for i in self.order():
            d = lax.rem(self.z + i, self.n_dp)
            self.near(i).wait_recv()
            self.loads(i).wait()
            for j in range(self.hh):
                self.own[j, d] = (
                    self.own[j, d].astype(F32) + self.sib[j, d].astype(F32)
                ).astype(BF)
            if i:
                self.go(i).start()
            else:
                pl.when(self.here())(lambda: self.stay().start())
                pl.when(jnp.logical_not(self.here()))(lambda: self.go(0).start())

    def end(self):
        for i in self.order():
            self.near(i).wait_send()
            if i:
                self.go(i).wait_send()
            else:
                pl.when(jnp.logical_not(self.here()))(lambda: self.go(0).wait_send())
        for o in range(self.n_dp // self.inner):
            for j in range(2):
                for h in range(2):
                    region = self.out.at[o, j, pl.ds(h * self.hh, self.hh)]
                    source = o * self.inner + 2 * self.k + j
                    here = jnp.logical_and(source == self.z, self.k == h)

                    @pl.when(here)
                    def _(region=region, o=o, j=j, h=h):
                        d = self.z
                        pltpu.make_async_copy(
                            self.own.at[:, d], region, self.recv.at[o, j, h]
                        ).wait()

                    @pl.when(jnp.logical_not(here))
                    def _(region=region, o=o, j=j, h=h):
                        wait_recv(region, self.recv.at[o, j, h], self.sibling)


def rms_back(x, gain, grad):
    root = lax.rsqrt(jnp.mean(x * x, axis=-1, keepdims=True) + norm_eps)
    scaled = grad * gain
    along = jnp.mean(x * scaled, axis=-1, keepdims=True)
    return root * scaled - x * (root * root * root) * along, grad * x * root


def backward_exchange(
    grad, attend, hidden, latent_low, own, out, shared, totals, n_dp, n_ex, inner, collective_id
):
    chips = n_ex // 2
    rows, width = grad.shape
    seq = n_ex * rows
    extra = len(totals)
    wq, we = attend[1], attend[2]
    lat_cols = KVR + 2 * DR
    r = width // (n_dp * n_ex)
    rl = KVR // (n_dp * n_ex)
    parts = DV // r
    hp = n_dp // parts
    n_dev = n_dp * n_ex
    wq_cols = wq.shape[1]
    we_cols = rl * we.shape[1] // r
    head_cols = wq_cols + we_cols

    def kernel(*refs):
        grad_ref, att_in, refs = refs[0], refs[1:12], refs[12:]
        hidden_ref, low_ref, refs = refs[0], refs[1], refs[2:]
        wl_ref, lat_ref, tok_ref, gain_ref, glat_ref, gnat_ref, router_ref, gtwo_ref = refs[:8]
        out_ref, sh_in, refs = refs[8], refs[9:12], refs[12:]
        t_refs, refs = refs[:extra], refs[extra:]
        tok_out, vec_out, pack_out, heads_mid, heads_out, wout_out, out_got = refs[:7]
        sh_out, back_refs, refs = refs[7:10], refs[10 : 10 + extra], refs[10 + extra :]
        gbuf, att_tmp, refs = refs[0], refs[1:8], refs[8:]
        part_l, bufs, sums, refs = refs[0], refs[1:7], refs[7:9], refs[9:]
        hsrc, wsrc, pack, psib, pout, pfar, psum, pbuf, vec, vbuf, vzbuf = refs[:11]
        refs = refs[11:]
        t_s, t_r, ts_s, ts_r, local = refs[:5]
        sems, refs = refs[5:13], refs[13:]
        (
            h_s, h_r, hz_s, hz_r, w_s, w_r, pn_s, pn_r, pf_s, pf_r, pc_s, pc_r, s_s, s_r,
            v_s, v_r, vz_s, vz_r, o_s, o_r,
        ) = refs[:20]
        rest = refs[20:]
        x_refs = (gbuf, part_l)
        group = column_group(lax.axis_index("dp"), lax.axis_index("expert"), inner)
        z, e, c, k, sibling, same_core, column = places(n_dp, n_ex)
        plane = [(z, lax.rem(e + i, n_ex)) for i in range(1, n_ex)]
        part = lax.rem(e, parts)
        members = [
            (lax.rem(z + i, n_dp), e - part + lax.rem(part + j, parts))
            for i in range(n_dp)
            for j in range(parts)
        ]
        greet(plane + column + [(d[0], sibling[1]) for d in column] + members[1:])
        backs = [
            ExpertsBack(t_refs[m], back_refs[m], rest[7 * m : 7 * m + 7], n_dp, n_ex, inner)
            for m in range(extra)
        ]
        gather, to_sib, others = [], [], []
        for i in range(1, chips):
            copy = remote(grad_ref, gbuf.at[e], t_s.at[i], t_r.at[i], same_core[i - 1])
            copy.start()
            gather.append(copy)
        copy = remote(grad_ref, gbuf.at[e], ts_s.at[0], ts_r.at[0], sibling)
        copy.start()
        to_sib.append(copy)
        keep = pltpu.make_async_copy(grad_ref, gbuf.at[e], local.at[0])
        keep.start()
        for back in backs:
            back.begin()
        for m in range(3):
            for i in range(1, n_dp):
                copy = remote(
                    sh_in[m].at[lax.rem(z + i, n_dp)], sh_out[m].at[z],
                    s_s.at[m, i], s_r.at[m, i], column[i - 1],
                )
                copy.start()
                others.append(copy)
            copy = pltpu.make_async_copy(sh_in[m].at[z], sh_out[m].at[z], local.at[1 + m])
            copy.start()
            others.append(copy)
        mine = lax.rem(z, inner)
        for i in range(1, inner):
            copy = remote(
                out_ref.at[lax.rem(mine + i, inner)], out_got.at[mine], o_s.at[i], o_r.at[i],
                group[i],
            )
            copy.start()
            others.append(copy)
        copy = pltpu.make_async_copy(out_ref.at[mine], out_got.at[mine], local.at[5])
        copy.start()
        others.append(copy)
        for i in range(1, chips):
            gather[i - 1].wait_recv()
            block = gbuf.at[lax.rem(c + chips - i, chips) * 2 + k]
            copy = remote(block, block, ts_s.at[i], ts_r.at[i], sibling)
            copy.start()
            to_sib.append(copy)
        for back in backs:
            back.pass_on()
        keep.wait()
        for copy in to_sib:
            copy.wait_recv()
        for copy in gather + to_sib:
            copy.wait_send()
        gat, grad_wout, dk, dv, grad_query, grad_expanded, grad_rope = att_tmp
        attend_backward(gbuf, *att_in, *att_tmp)

        wsrc[...] = grad_wout[...].astype(BF).reshape(hp, parts, r, width)

        def wout_sends(start):
            for h in range(hp):
                for p in range(parts):
                    target = (part * hp + h, e - part + p)
                    here = jnp.logical_and(part * hp + h == z, p == part)

                    def far(h=h, p=p, target=target):
                        copy = remote(
                            wsrc.at[h, p], wout_out.at[z], w_s.at[h, p], w_r.at[z], target
                        )
                        if start:
                            copy.start()
                        else:
                            copy.wait_send()

                    pl.when(jnp.logical_not(here))(far)
                    if start:

                        @pl.when(here)
                        def _(h=h, p=p):
                            pltpu.make_async_copy(
                                wsrc.at[h, p], wout_out.at[z], w_r.at[z]
                            ).start()

        wout_sends(True)

        def spread(i, carry):
            at = pl.ds(pl.multiple_of(i * 2 * rows, 2 * rows), 2 * rows)
            block = mm_cols(grad_query[at, :], att_in[1][...]).astype(BF)
            gbuf[pl.ds(2 * i, 2)] = block.reshape(2, rows, width)
            block = mm_cols(grad_expanded[at, :], att_in[2][...]).astype(BF)
            part_l[pl.ds(2 * i, 2), :, :KVR] = block.reshape(2, rows, KVR)
            block = grad_rope[at, :].astype(BF)
            part_l[pl.ds(2 * i, 2), :, KVR:] = block.reshape(2, rows, 2 * DR)
            return carry

        lax.fori_loop(0, chips, spread, 0)
        near, far = {}, {}
        for i in list(range(1, chips)) + [0]:
            chip = lax.rem(c + i, chips)
            for j in range(2):
                near[i, j] = remote(
                    x_refs[j].at[chip * 2 + 1 - k],
                    bufs[3 * j].at[chip],
                    sems[4 * j].at[i],
                    sems[4 * j + 1].at[i],
                    sibling,
                )
                near[i, j].start()
        for i in range(1, chips):
            chip = lax.rem(c + i, chips)
            for j in range(2):
                from_sib, out_buf, from_far = bufs[3 * j : 3 * j + 3]
                near[i, j].wait_recv()
                out_buf[i] = (
                    x_refs[j][chip * 2 + k].astype(F32) + from_sib[chip].astype(F32)
                ).astype(BF)
                far[i, j] = remote(
                    out_buf.at[i],
                    from_far.at[i],
                    sems[4 * j + 2].at[i],
                    sems[4 * j + 3].at[i],
                    same_core[i - 1],
                )
                far[i, j].start()

        per_tile = 256 // r

        def wq_rows(i, carry):
            at = pl.ds(pl.multiple_of(i * 256, 256), 256)
            block = mm_rows(hidden_ref[:, at], grad_query[...]).astype(BF)
            hsrc[pl.ds(i * per_tile, per_tile), :, :wq_cols] = block.reshape(
                per_tile, r, wq_cols
            )
            return carry

        lax.fori_loop(0, width // 256, wq_rows, 0)
        grad_we = mm_rows(low_ref[...], grad_expanded[...]).astype(BF)
        for j in range(r // rl):
            block = grad_we[:, j * we_cols : (j + 1) * we_cols]
            hsrc[:, j * rl : (j + 1) * rl, wq_cols:] = block.reshape(n_dev, rl, we_cols)
        heads_far = []
        for i in range(1, n_ex):
            for d in range(n_dp):
                copy = remote(
                    hsrc.at[d * n_ex + lax.rem(e + i, n_ex)], heads_mid.at[d, e],
                    h_s.at[i, d], h_r.at[i, d], plane[i - 1],
                )
                copy.start()
                heads_far.append(copy)
        for d in range(n_dp):
            copy = pltpu.make_async_copy(
                hsrc.at[d * n_ex + e], heads_mid.at[d, e], h_r.at[0, d]
            )
            copy.start()
            copy.wait()
        for j in range(2):
            near[0, j].wait_recv()
            sums[j][...] = x_refs[j][e].astype(F32) + bufs[3 * j][c].astype(F32)
        for i in range(1, chips):
            for j in range(2):
                far[i, j].wait_recv()
                sums[j][...] += bufs[3 * j + 2][i].astype(F32)

        at = pl.ds(pl.multiple_of(e * rows, rows), rows)
        cos, sin = att_in[3][at, :], att_in[4][at, :]
        lat_grad, lat_gain = rms_back(lat_ref[:, :KVR], glat_ref[...], sums[1][:, :KVR])
        rope = turn(sums[1][:, KVR:], cos, sin, -1.0)
        lane = lax.broadcasted_iota(jnp.int32, rope.shape, 1)
        rope = jnp.where(lane < DR, rope, 0.0)
        low = jnp.concatenate([lat_grad, rope], axis=1).astype(BF)
        total = sums[0][...] + mm_cols(low, wl_ref[:, :lat_cols])
        tok_grad, tok_gain = rms_back(tok_ref[...].astype(F32), gain_ref[...], total)
        tok_out[...] = gnat_ref[...] + tok_grad
        vec[...] = jnp.zeros_like(vec)
        vec[0:1, :] = jnp.sum(tok_gain, axis=0, keepdims=True)
        vec[1:2, :] = gtwo_ref[...]
        vec[2:3, :KVR] = jnp.sum(lat_gain, axis=0, keepdims=True)
        vec_far = []
        for i in range(1, n_ex):
            copy = remote(vec, vbuf.at[i], v_s.at[i], v_r.at[i], plane[i - 1])
            copy.start()
            vec_far.append(copy)
        for d in range(n_dp):
            block = hidden_ref[at, d * n_ex * r : (d + 1) * n_ex * r]
            block = mm_rows(block, low).reshape(n_ex, r, lat_cols)
            pack[:, d * r : (d + 1) * r, :KVR] = block[:, :, :KVR].astype(BF)
            block = block[:, :, KVR:] + router_ref[:, d * r : (d + 1) * r].astype(F32)
            pack[:, d * r : (d + 1) * r, KVR:] = block.astype(BF)
        pack_near, pack_far = [], []
        for i in list(range(1, chips)) + [0]:
            chip = lax.rem(c + i, chips)
            copy = remote(pack.at[chip * 2 + 1 - k], psib.at[chip], pn_s.at[i], pn_r.at[i], sibling)
            copy.start()
            pack_near.append(copy)
        for copy in heads_far:
            copy.wait_recv()
        heads_col = []
        for i in range(1, n_dp):
            d = lax.rem(z + i, n_dp)
            copy = remote(
                heads_mid.at[d], heads_out.at[z], hz_s.at[i], hz_r.at[i], column[i - 1]
            )
            copy.start()
            heads_col.append(copy)
        copy = pltpu.make_async_copy(heads_mid.at[z], heads_out.at[z], local.at[4])
        copy.start()
        heads_col.append(copy)
        for i in range(1, chips):
            chip = lax.rem(c + i, chips)
            pack_near[i - 1].wait_recv()
            pout[i] = (pack[chip * 2 + k].astype(F32) + psib[chip].astype(F32)).astype(BF)
            copy = remote(pout.at[i], pfar.at[i], pf_s.at[i], pf_r.at[i], same_core[i - 1])
            copy.start()
            pack_far.append(copy)
        for copy in vec_far:
            copy.wait_recv()
            copy.wait_send()
        for i in range(1, n_ex):
            vec[...] += vbuf[i]
        vec_col = []
        for i in range(1, n_dp):
            copy = remote(vec, vzbuf.at[i], vz_s.at[i], vz_r.at[i], column[i - 1])
            copy.start()
            vec_col.append(copy)
        pack_near[chips - 1].wait_recv()
        total = pack[e].astype(F32) + psib[c].astype(F32)
        for i in range(1, chips):
            pack_far[i - 1].wait_recv()
            total = total + pfar[i].astype(F32)
        psum[...] = total.astype(BF).reshape(n_dp, r, lat_cols)
        pack_col = []
        for i in range(1, n_dp):
            copy = remote(
                psum.at[lax.rem(z + i, n_dp)], pbuf.at[i], pc_s.at[i], pc_r.at[i], column[i - 1]
            )
            copy.start()
            pack_col.append(copy)
        result = vec[...]
        for i in range(1, n_dp):
            vec_col[i - 1].wait_recv()
            result = result + vzbuf[i]
        vec_out[...] = result
        result = psum[z].astype(F32)
        for i in range(1, n_dp):
            pack_col[i - 1].wait_recv()
            result = result + pbuf[i].astype(F32)
        pack_out[...] = result

        for i in range(n_dp):
            here = jnp.logical_and(z // hp == part, z == i)

            @pl.when(here)
            def _(i=i):
                pltpu.make_async_copy(
                    wsrc.at[lax.rem(z, hp), part], wout_out.at[i], w_r.at[i]
                ).wait()

            @pl.when(jnp.logical_not(here))
            def _(i=i):
                wait_recv(wout_out.at[i], w_r.at[i], sibling)

        wout_sends(False)
        for copy in list(near.values()) + list(far.values()) + heads_far:
            copy.wait_send()
        for copy in pack_near + pack_far + vec_col + pack_col:
            copy.wait_send()
        for copy in heads_col + others:
            copy.wait()
        for back in backs:
            back.end()

    dma = pltpu.SemaphoreType.DMA
    sds = jax.ShapeDtypeStruct
    vmem = pltpu.VMEM
    scratch = [
        vmem((n_ex, rows, width), BF),
        vmem((seq, 2 * DV), BF),
        vmem((2 * DV, width), F32),
        vmem((seq, 2 * DH), F32),
        vmem((seq, DV), F32),
        vmem((seq, wq.shape[1]), BF),
        vmem((seq, we.shape[1]), BF),
        vmem((seq, 2 * DR), F32),
        vmem((n_ex, rows, lat_cols), BF),
    ]
    scratch += [vmem((chips, rows, width), BF)] * 3 + [vmem((chips, rows, lat_cols), BF)] * 3
    scratch += [
        vmem((rows, width), F32),
        vmem((rows, lat_cols), F32),
        vmem((n_dev, r, head_cols), BF),
        vmem((hp, parts, r, width), BF),
        vmem((n_ex, n_dp * r, lat_cols), BF),
        vmem((chips, n_dp * r, lat_cols), BF),
        vmem((chips, n_dp * r, lat_cols), BF),
        vmem((chips, n_dp * r, lat_cols), BF),
        vmem((n_dp, r, lat_cols), BF),
        vmem((n_dp, r, lat_cols), BF),
        vmem((8, width), F32),
        vmem((n_ex, 8, width), F32),
        vmem((n_dp, 8, width), F32),
    ]
    scratch += [dma((chips,))] * 4 + [dma((6,))] + [dma((chips,))] * 8
    scratch += [dma((n_ex, n_dp))] * 2 + [dma((n_dp,))] * 2 + [dma((hp, parts)), dma((n_dp,))]
    scratch += [dma((chips,))] * 4 + [dma((n_dp,))] * 2 + [dma((3, n_dp))] * 2
    scratch += [dma((n_ex,))] * 2 + [dma((n_dp,))] * 2 + [dma((inner,))] * 2
    for total in totals:
        scratch += ExpertsBack.scratch(total, n_dp, inner)
    outs = pl.pallas_call(
        kernel,
        out_shape=[
            sds((rows, width), F32),
            sds((8, width), F32),
            sds((r, lat_cols), F32),
            sds((n_dp, n_ex, r, head_cols), BF),
            sds((n_dp, n_ex, r, head_cols), BF),
            sds((n_dp, r, width), BF),
            sds(out.shape, BF),
        ]
        + [sds(array.shape, BF) for array in shared]
        + [ExpertsBack.out(total, n_dp, inner) for total in totals],
        in_specs=[ANY] + [VMEM] * 21 + [ANY] * (4 + extra),
        out_specs=[VMEM] * 3 + [ANY] * (7 + extra),
        scratch_shapes=scratch,
        compiler_params=params(collective_id),
    )(grad, *attend, hidden, latent_low, *own, out, *shared, *totals)
    return outs[:3], outs[4], outs[5], outs[6], outs[7:10], outs[10:]


def shards(
    tokens,
    cotangent,
    lengths,
    routes,
    place_order,
    attn_gain,
    w_query,
    w_latent,
    latent_gain,
    w_expand,
    w_out,
    ffn_gain,
    w_router,
    shared_gate,
    shared_up,
    shared_down,
    expert_gate,
    expert_up,
    expert_down,
):
    rows, width = tokens.shape
    n_dp = lax.axis_size("dp")
    n_ex = lax.axis_size("expert")
    chips = n_ex // 2
    z = lax.axis_index("dp")
    e = lax.axis_index("expert")
    chip = e // 2
    n_experts = w_router.shape[1]
    top_k = routes.shape[1]
    capacity = (rows * top_k * 5 + 4 * n_experts - 1) // (4 * n_experts)
    cap = (capacity + 15) // 16 * 16
    seq = rows * n_ex
    r = w_query.shape[0]
    rl = w_expand.shape[0]
    hp = H // n_ex
    parts = DV // r
    heads = [
        (d * n_ex + (j // parts) * parts) * r // DV
        for j in range(n_ex)
        for d in range(j % parts * hp, j % parts * hp + hp)
    ]
    heads_back = [heads.index(h) for h in range(H)]
    inner = n_experts // chips
    my_local = lax.rem(z, inner)
    ff_e = expert_gate.shape[2]
    ff_s = shared_gate.shape[1] // inner
    lat = KVR + DR
    head_cols = hp * (DH + DR)
    kv_cols = hp * (DH + DV)

    def to_owner_order(values):
        cut = values.reshape(values.shape[0], n_dp, n_ex, r)
        return cut.transpose(0, 2, 1, 3).reshape(values.shape)

    def from_owner_order(values):
        cut = values.reshape(values.shape[0], n_ex, n_dp, r)
        return cut.transpose(0, 2, 1, 3).reshape(values.shape)

    def pick(values, index, axis=0):
        return lax.dynamic_index_in_dim(values, index, axis, keepdims=False)

    wq_send = jnp.take(w_query.reshape(r, H, DH + DR), jnp.array(heads), axis=1)
    wq_send = wq_send.reshape(r, n_ex, hp, DH + DR)
    wq_send = jnp.concatenate(
        [
            wq_send[..., :DH].reshape(r, n_ex, hp * DH),
            wq_send[..., DH:].reshape(r, n_ex, hp * DR),
        ],
        axis=-1,
    ).transpose(1, 0, 2)
    we_send = jnp.take(w_expand.reshape(rl, H, DH + DV), jnp.array(heads), axis=1)
    we_cols = rl * kv_cols // r
    we_send = we_send.reshape(rl, n_ex, r // rl, we_cols).transpose(1, 2, 0, 3)
    we_send = we_send.reshape(n_ex, r, we_cols)
    wa_send = jnp.concatenate([wq_send, we_send], axis=-1)
    slot_own = slot_places(routes, place_order[0], capacity)
    slot_place = jnp.where(slot_own >= 0, slot_own - routes * capacity, -1)
    slot_cols = 2 * rows * top_k // r
    slot_pack = jnp.stack([routes, slot_place]).astype(BF).reshape(2, r, slot_cols // 2)
    small_cols = lat + n_experts + 3
    pack_cols = (small_cols + slot_cols + 127) // 128 * 128
    pack = jnp.concatenate(
        [
            w_latent,
            w_router,
            attn_gain[:, None],
            ffn_gain[:, None],
            jnp.pad(latent_gain, (0, r - rl))[:, None],
            slot_pack[0],
            slot_pack[1],
            jnp.zeros((r, pack_cols - small_cols - slot_cols), BF),
        ],
        axis=1,
    )
    cot_owner = to_owner_order(cotangent)
    tok_all, wa_all, pk_all = first_exchange(tokens, wa_send, pack, n_dp, n_ex, 1)
    wq = wa_all[..., :head_cols].reshape(width, head_cols)
    wexp = wa_all[..., head_cols:].reshape(n_dp * n_ex, r // rl, rl, we_cols)
    wexp = wexp.transpose(0, 2, 1, 3).reshape(KVR, kv_cols)
    pk_flat = pk_all.reshape(width, pack_cols)
    w_lat = pk_flat[:, :lat]
    gain_one = pk_flat[:, lat + n_experts].astype(F32)
    gain_two = pk_all[..., lat + n_experts + 1].transpose(1, 0, 2).reshape(width).astype(F32)
    router = pk_all[..., lat : lat + n_experts].transpose(1, 0, 2, 3).reshape(width, n_experts)
    gain_lat = (
        pk_all[..., lat + n_experts + 2].reshape(n_dp * n_ex, r)[:, :rl].reshape(KVR).astype(F32)
    )
    col_groups = [[o * inner + i for i in range(inner)] for o in range(n_dp // inner)]
    cot_send, _ = lax.optimization_barrier((cot_owner, pk_all))
    cot_col = lax.all_gather(cot_send, "dp", axis=0, tiled=True, axis_index_groups=col_groups)
    slots_all = n_experts * capacity
    slot_col = pick(pk_all[..., small_cols : small_cols + slot_cols], e, 1)
    slot_col = lax.dynamic_slice_in_dim(slot_col, z - my_local, inner, 0).astype(jnp.int32)
    slot_col = slot_col.reshape(inner, r, 2, slot_cols // 2).transpose(2, 0, 1, 3)
    slot_col = slot_col.reshape(2, inner, rows, top_k)
    slot_ids = jnp.where(
        slot_col[1] >= 0,
        slot_col[0] * capacity + slot_col[1] + (jnp.arange(inner) * slots_all)[:, None, None],
        -1,
    ).reshape(inner * rows, top_k)
    place = jnp.arange(cap)
    far_experts = [lax.rem(chip + m, chips) * inner + my_local for m in range(chips)]
    wanted = (
        jnp.stack(far_experts)[:, None, None] * capacity
        + (jnp.arange(inner) * slots_all)[None, :, None]
        + place[None, None, :]
    )
    wanted = jnp.where(place[None, None, :] < capacity, wanted, -2).reshape(-1)
    n_slots = wanted.shape[0]
    per_far = n_slots // chips
    hot = sum((wanted[:, None] == slot_ids[None, :, j]).astype(BF) for j in range(top_k))
    hot_t = sum((slot_ids[:, j][:, None] == wanted[None, :]).astype(BF) for j in range(top_k))

    def through(values, way):
        cut = values.reshape(chips, per_far, -1)
        got = [cut[0]]
        for m in range(1, chips):
            perm = [(i, (i + 2 * m * way) % n_ex) for i in range(n_ex)]
            got.append(lax.ppermute(cut[m], "expert", perm))
        return jnp.concatenate(got, axis=0)

    positions = jnp.arange(seq)
    cos_table, sine_table = rope_tables(positions)
    cos_wide, sine_wide = jnp.tile(cos_table, (1, 4)), jnp.tile(sine_table, (1, 4))
    keep = (positions < lengths[0]).astype(F32)[None]
    attend_out, wo_rows, residual, x_col, (wg, wu), (sgate, sup, sdown) = forward_exchange(
        [tok_all, gain_one[None], wq, pk_flat, gain_lat[None], wexp, cos_wide, sine_wide, keep],
        to_owner_order(w_out),
        to_owner_order(tokens),
        gain_two[None],
        [w.reshape(-1, n_ex, r, ff_e) for w in (expert_gate, expert_up)],
        [w.reshape(r, inner, ff_s).transpose(1, 0, 2) for w in (shared_gate, shared_up, shared_down)],
        n_dp,
        n_ex,
        inner,
        2,
    )
    hidden_one, latent_raw, latent_low, qcat, kcat, value, lse, attended = attend_out
    wo_rows = wo_rows.reshape(hp * DV, width)
    sgate, sup, sdown = (w.reshape(width, ff_s) for w in (sgate, sup, sdown))
    hidden_two = pick(x_col, my_local)
    x_col = x_col.reshape(inner * rows, width)

    x_in, wd, shared_out, shared_dx, shared_grads = dispatch(
        mm(hot, x_col).astype(BF).reshape(chips, per_far, width),
        x_col,
        cot_col,
        (sgate, sup, sdown),
        expert_down.reshape(-1, n_ex, r, ff_e),
        n_dp,
        n_ex,
        inner,
        8,
    )
    x_in = x_in.reshape(n_slots, width)
    grad_in = through(mm(hot, cot_col).astype(BF), 1)
    wg, wu, wd = (w.reshape(width, ff_e) for w in (wg, wu, wd))

    def probs_of(logits):
        top = jnp.max(logits, axis=-1, keepdims=True)
        exp_logits = jnp.exp(logits - top)
        return exp_logits / jnp.sum(exp_logits, axis=-1, keepdims=True)

    slot_probs = probs_of(mm(x_in, router))
    slot_gate = jnp.sum(
        jnp.where(jnp.arange(n_experts)[None, :] == far_experts[0], slot_probs, 0.0),
        axis=1,
        keepdims=True,
    )
    expert_a = mm(x_in, wg)
    expert_b = mm(x_in, wu)
    expert_hidden = swiglu(expert_a, expert_b).astype(BF)
    expert_rows = mm_cols(expert_hidden, wd).astype(BF)
    slot_dots = jnp.sum(grad_in.astype(F32) * expert_rows.astype(F32), axis=-1, keepdims=True)
    slot_dots = jnp.broadcast_to(slot_dots, (n_slots, 128)).astype(BF)
    slot_grad = (slot_gate * grad_in.astype(F32)).astype(BF)
    dx_back, dots_back, down_back, expert_totals = experts_back(
        [x_in, slot_grad, expert_a.astype(BF), expert_b.astype(BF), expert_hidden],
        [wg, wu, wd],
        slot_dots.reshape(chips, per_far, 128),
        n_dp,
        n_ex,
        inner,
        9,
    )
    dx_back = dx_back.reshape(n_slots, width)

    col_probs = probs_of(mm(x_col, router))
    expert_axis = jnp.arange(n_experts)[None, :]
    gates = [
        jnp.sum(jnp.where(expert_axis == expert, col_probs, 0.0), axis=1, keepdims=True)
        for expert in far_experts
    ]
    gate_hot = jnp.concatenate(
        [hot_t[:, m * per_far : (m + 1) * per_far] * gates[m].astype(BF) for m in range(chips)],
        axis=1,
    )
    dots = dots_back.reshape(n_slots, 128)[:, 0].astype(F32)[None] * hot_t.astype(F32)
    dots = jnp.sum(dots.reshape(inner * rows, chips, per_far), axis=-1)
    grad_probs_col = sum(
        jnp.where(expert_axis == far_experts[m], dots[:, m : m + 1], 0.0) for m in range(chips)
    )
    dx_col = mm(hot_t, dx_back) + shared_dx
    dx_send = jnp.concatenate(
        [dx_col, grad_probs_col, jnp.zeros((inner * rows, 128 - n_experts), F32)], axis=1
    ).astype(BF)
    dx_sum, shared_sums, rows_back, (gate_back,) = column_sum(
        dx_send.reshape(inner, rows, width + 128),
        expert_rows.reshape(chips, per_far, width),
        [grad.reshape(n_ex, n_dp, r, ff_s) for grad in shared_grads],
        expert_totals[:1],
        n_dp,
        n_ex,
        inner,
        3,
    )
    router_probs = lax.dynamic_slice_in_dim(col_probs, my_local * rows, rows, 0)
    grad_probs = dx_sum[:, width : width + n_experts]
    grad_logits = (
        router_probs * (grad_probs - jnp.sum(grad_probs * router_probs, axis=-1, keepdims=True))
    ).astype(BF)
    grad_router = mm_rows(hidden_two, grad_logits)
    grad_hidden_two = dx_sum[:, :width] + mm_cols(grad_logits, router)
    _, norm_two_back = jax.vjp(rms_norm, residual, gain_two)
    grad_resid_norm, grad_gain_two = norm_two_back(grad_hidden_two)
    grad_residual = cot_owner.astype(F32) + grad_resid_norm

    out_col = mm(gate_hot, rows_back.reshape(n_slots, width)) + shared_out
    latent_own = lax.dynamic_slice_in_dim(latent_raw, e * rows, rows, 0)
    router_back = jnp.pad(
        grad_router.reshape(n_ex, n_dp * r, n_experts),
        ((0, 0), (0, 0), (DR, DR - n_experts)),
    ).astype(BF)
    (grad_tokens, vec_sum, pack_sum), heads_got, wout_got, out_got, shared_got, (up_back,) = (
        backward_exchange(
            grad_residual.astype(BF),
            [wo_rows, wq, wexp, cos_wide, sine_wide, keep, qcat, kcat, value, lse, attended],
            hidden_one,
            latent_low,
            [
                pk_flat,
                latent_own,
                tokens,
                gain_one[None],
                gain_lat[None],
                from_owner_order(grad_residual),
                router_back,
                grad_gain_two[None],
            ],
            out_col.astype(BF).reshape(inner, rows, width),
            shared_sums,
            expert_totals[1:2],
            n_dp,
            n_ex,
            inner,
            5,
        )
    )

    def added(values):
        return jnp.sum(values.astype(F32), axis=0)

    out_tokens = from_owner_order((residual + added(out_got)).astype(BF))
    heads_all = added(heads_got)
    sum_wq = heads_all[..., :head_cols].transpose(1, 0, 2)
    sum_wq = jnp.concatenate(
        [
            sum_wq[..., : hp * DH].reshape(r, n_ex, hp, DH),
            sum_wq[..., hp * DH :].reshape(r, n_ex, hp, DR),
        ],
        axis=-1,
    ).reshape(r, H, DH + DR)
    sum_wq = jnp.take(sum_wq, jnp.array(heads_back), axis=1).reshape(r, H * (DH + DR))
    sum_we = heads_all[..., head_cols:].reshape(n_ex, r // rl, rl, we_cols).transpose(2, 0, 1, 3)
    sum_we = jnp.take(sum_we.reshape(rl, H, DH + DV), jnp.array(heads_back), axis=1)
    sum_we = sum_we.reshape(rl, H * (DH + DV))
    sum_wout = from_owner_order(added(wout_got))
    device = z * n_ex + e
    sum_gain_one = lax.dynamic_slice_in_dim(vec_sum[0], device * r, r, 0)
    sum_gain_two = lax.dynamic_slice_in_dim(vec_sum[1], (e * n_dp + z) * r, r, 0)
    sum_gain_lat = lax.dynamic_slice_in_dim(vec_sum[2], device * rl, rl, 0)
    sum_sgate, sum_sup, sum_sdown = (
        added(got.reshape(n_dp // inner, inner, r, ff_s)).transpose(1, 0, 2).reshape(r, -1)
        for got in shared_got
    )
    sum_egate, sum_eup, sum_edown = (
        added(back).reshape(-1, n_ex * r, ff_e) for back in (gate_back, up_back, down_back)
    )
    return (
        out_tokens,
        grad_tokens,
        sum_gain_one,
        sum_wq,
        pack_sum[:, :lat],
        sum_gain_lat,
        sum_we,
        sum_wout,
        sum_gain_two,
        pack_sum[:, lat : lat + n_experts],
        sum_sgate,
        sum_sup,
        sum_sdown,
        sum_egate,
        sum_eup,
        sum_edown,
    )


def solution(mesh):
    both = ("dp", "expert")
    in_specs = (
        P(both, None),
        P(both, None),
        P("dp"),
        P(both, None),
        P(both, None),
        P(both),
        P(both, None),
        P(both, None),
        P(both),
        P(both, None),
        P(both, None),
        P(both),
        P(both, None),
        P(both, None),
        P(both, None),
        P(both, None),
        P("expert", "dp", None),
        P("expert", "dp", None),
        P("expert", "dp", None),
    )
    out_specs = (
        P(both, None),
        P(both, None),
        P(both),
        P(both, None),
        P(both, None),
        P(both),
        P(both, None),
        P(both, None),
        P(both),
        P(both, None),
        P(both, None),
        P(both, None),
        P(both, None),
        P("expert", "dp", None),
        P("expert", "dp", None),
        P("expert", "dp", None),
    )
    return jax.shard_map(shards, mesh=mesh, in_specs=in_specs, out_specs=out_specs, check_vma=False)
```

```python
import jax
import jax.numpy as jnp
from jax import lax
from jax.experimental import pallas as pl
from jax.experimental.pallas import tpu as pltpu
from jax.sharding import PartitionSpec as P

H = 16
DH = 128
DR = 64
DV = 128
KVR = 512

norm_eps = 1e-06
masked_score = -1e30
MESH = pl.DeviceIdType.MESH
ANY = pl.BlockSpec(memory_space=pl.ANY)
VMEM = pl.BlockSpec(memory_space=pltpu.VMEM)
BF = jnp.bfloat16
F32 = jnp.float32


def rms_norm(values, scale_gain):
    return (
        values
        * lax.rsqrt(jnp.mean(values * values, axis=-1, keepdims=True) + norm_eps)
        * scale_gain
    )


def swiglu(gate_in, up_in):
    return jax.nn.silu(gate_in) * up_in


def mm(left, right):
    return jnp.dot(left, right, preferred_element_type=F32)


def mm_rows(left, right):
    return lax.dot_general(left, right, (((0,), (0,)), ((), ())), preferred_element_type=F32)


def mm_cols(left, right):
    return lax.dot_general(left, right, (((1,), (1,)), ((), ())), preferred_element_type=F32)


def slot_places(route_rows, pair_order, capacity):
    pair_expert = route_rows.reshape(-1)
    earlier = pair_order[None, :] < pair_order[:, None]
    same_expert = pair_expert[None, :] == pair_expert[:, None]
    places = jnp.sum((earlier & same_expert).astype(jnp.int32), axis=1)
    slot_index = jnp.where(places < capacity, pair_expert * capacity + places, -1)
    return slot_index.reshape(route_rows.shape)


def turn(values, cos, sin, sign):
    half = DR // 2
    first = lax.rem(lax.broadcasted_iota(jnp.int32, values.shape, 1), DR) < half
    partner = jnp.where(
        first, -pltpu.roll(values, 2 * DR - half, 1), pltpu.roll(values, half, 1)
    )
    return values * cos + sign * (partner * sin)


def causal(i, tile, keep_ref):
    shape = (tile, (i + 1) * tile)
    query = lax.broadcasted_iota(jnp.int32, shape, 0) + i * tile
    key = lax.broadcasted_iota(jnp.int32, shape, 1)
    return (key <= query) & (keep_ref[:, : shape[1]] > 0.5)


def attend_forward(
    tok, gain, wq, wl, gain_lat, we, cos, sin, keep,
    hidden, latent, latent_low, qcat, kcat, value, lse, attended,
):
    per, rows, width = tok.shape
    seq = per * rows
    tile = 2 * rows
    scale = (DH + DR) ** (-0.5)

    def project(i, carry):
        at = pl.ds(pl.multiple_of(i * tile, tile), tile)
        x = tok[pl.ds(2 * i, 2)].reshape(tile, width).astype(F32)
        root = lax.rsqrt(jnp.mean(x * x, axis=-1, keepdims=True) + norm_eps)
        hid = (x * root * gain[...]).astype(BF)
        hidden[at, :] = hid
        c, s = cos[at, :], sin[at, :]
        query = mm(hid, wq[...])
        rope_q = turn(query[:, 2 * DH :], c, s, 1.0).astype(BF)
        lat = mm(hid, wl[...])
        latent[at, :] = lat
        plain = lat[:, :KVR]
        root = lax.rsqrt(jnp.mean(plain * plain, axis=-1, keepdims=True) + norm_eps)
        low = (plain * root * gain_lat[...]).astype(BF)
        latent_low[at, :] = low
        rope = lat[:, KVR : KVR + 2 * DR]
        lane = lax.broadcasted_iota(jnp.int32, rope.shape, 1)
        rope = jnp.where(lane < DR, rope, pltpu.roll(rope, DR, 1))
        rope = turn(rope, c, s, 1.0)
        expanded = mm(low, we[...]).astype(BF)
        for h in range(2):
            qcat[h, at, :DH] = query[:, h * DH : (h + 1) * DH].astype(BF)
            qcat[h, at, DH:] = rope_q
            mine = (lane < DR) if h == 0 else (lane >= DR)
            kcat[h, at, :DH] = expanded[:, h * (DH + DV) : h * (DH + DV) + DH]
            kcat[h, at, DH:] = jnp.where(mine, rope, 0.0).astype(BF)
            value[h, at, :] = expanded[:, h * (DH + DV) + DH : (h + 1) * (DH + DV)]
        return carry

    lax.fori_loop(0, seq // tile, project, 0)
    for h in range(2):
        for i in range(seq // tile):
            at, upto = slice(i * tile, (i + 1) * tile), slice(0, (i + 1) * tile)
            scores = mm_cols(qcat[h, at, :], kcat[h, upto, :]) * scale
            scores = jnp.where(causal(i, tile, keep), scores, masked_score)
            top = jnp.max(scores, axis=-1, keepdims=True)
            exp_scores = jnp.exp(scores - top)
            total = jnp.sum(exp_scores, axis=-1, keepdims=True)
            probs = (exp_scores / total).astype(BF)
            attended[at, h * DV : (h + 1) * DV] = mm(probs, value[h, upto, :]).astype(BF)
            lse[h, at, :] = jnp.broadcast_to(top + jnp.log(total), (tile, lse.shape[2]))


def attend_backward(
    grad, wo, wq, we, cos, sin, keep, qcat, kcat, value, lse, attended,
    gat, grad_wout, dk, dv, grad_query, grad_expanded, grad_rope,
):
    per, rows, width = grad.shape
    seq = per * rows
    tile = 2 * rows
    scale = (DH + DR) ** (-0.5)
    count = seq // tile
    grad_wout[...] = jnp.zeros_like(grad_wout)

    def project(i, carry):
        at = pl.ds(pl.multiple_of(i * tile, tile), tile)
        block = grad[pl.ds(2 * i, 2)].reshape(tile, width)
        gat[at, :] = mm_cols(block, wo[...]).astype(BF)
        grad_wout[...] += mm_rows(attended[at, :], block)
        return carry

    lax.fori_loop(0, count, project, 0)
    for h in range(2):
        dk[...] = jnp.zeros_like(dk)
        dv[...] = jnp.zeros_like(dv)
        for i in range(count):
            at, upto = slice(i * tile, (i + 1) * tile), slice(0, (i + 1) * tile)
            g = gat[at, h * DV : (h + 1) * DV]
            scores = mm_cols(qcat[h, at, :], kcat[h, upto, :]) * scale
            scores = jnp.where(causal(i, tile, keep), scores, masked_score)
            probs = jnp.exp(scores - lse[h, at, 0:1])
            grad_probs = mm_cols(g, value[h, upto, :])
            inner = jnp.sum(grad_probs * probs, axis=-1, keepdims=True)
            raw = (probs * (grad_probs - inner) * scale).astype(BF)
            grad_q = mm(raw, kcat[h, upto, :])
            grad_query[at, h * DH : (h + 1) * DH] = grad_q[:, :DH].astype(BF)
            rope = grad_q[:, DH:]
            lane = lax.broadcasted_iota(jnp.int32, rope.shape, 1)
            mine = (lane < DR) if h == 0 else (lane >= DR)
            rope = turn(rope, cos[at, :], sin[at, :], -1.0).astype(BF)
            if h == 0:
                grad_query[at, 2 * DH :] = rope
            else:
                grad_query[at, 2 * DH :] = jnp.where(mine, rope, grad_query[at, 2 * DH :])
            dk[upto, :] += mm_rows(raw, qcat[h, at, :])
            dv[upto, :] += mm_rows(probs.astype(BF), g)
        grad_expanded[:, h * (DH + DV) : h * (DH + DV) + DH] = dk[:, :DH].astype(BF)
        grad_expanded[:, h * (DH + DV) + DH : (h + 1) * (DH + DV)] = dv[...].astype(BF)
        rope = dk[:, DH:]
        if h == 0:
            grad_rope[...] = rope
        else:
            grad_rope[...] += pltpu.roll(rope, DR, 1)


def params(collective_id):
    return pltpu.CompilerParams(
        collective_id=collective_id, has_side_effects=True, vmem_limit_bytes=60 << 20
    )


def remote(src, dst, send_sem, recv_sem, device):
    return pltpu.make_async_remote_copy(
        src_ref=src,
        dst_ref=dst,
        send_sem=send_sem,
        recv_sem=recv_sem,
        device_id=device,
        device_id_type=MESH,
    )


def greet(devices):
    barrier = pltpu.get_barrier_semaphore()
    for device in devices:
        pl.semaphore_signal(barrier, inc=1, device_id=device, device_id_type=MESH)
    pl.semaphore_wait(barrier, len(devices))


def places(n_dp, n_ex):
    z = lax.axis_index("dp")
    e = lax.axis_index("expert")
    chips = n_ex // 2
    c, k = e // 2, lax.rem(e, 2)
    sibling = (z, e + 1 - 2 * k)
    same_core = [(z, lax.rem(c + i, chips) * 2 + k) for i in range(1, chips)]
    column = [(lax.rem(z + i, n_dp), e) for i in range(1, n_dp)]
    return z, e, c, k, sibling, same_core, column


def wait_recv(region, sem, device):
    remote(region, region, sem, sem, device).wait_recv()


def column_sum(array, rows_out, shared, totals, n_dp, n_ex, inner, collective_id):
    chips = n_ex // 2
    shape = array.shape[1:]
    extra = len(totals)
    _, _, r, ff_s = shared[0].shape

    def kernel(x_ref, *refs):
        s_in, r_ref, t_refs, refs = refs[:3], refs[3], refs[4 : 4 + extra], refs[4 + extra :]
        o_ref, s_out, r_out, back_refs = refs[0], refs[1:4], refs[4], refs[5 : 5 + extra]
        refs = refs[5 + extra :]
        buf, from_sib, out_buf, from_far = refs[:4]
        send, recv, near_s, near_r, far_s, far_r, r_s, r_r, local = refs[4:13]
        rest = refs[13:]
        z, e, c, k, sibling, same_core, column = places(n_dp, n_ex)
        group = column_group(z, e, inner)
        greet(same_core + [sibling] + column + [(d[0], sibling[1]) for d in column])
        backs = [
            ExpertsBack(t_refs[m], back_refs[m], rest[7 * m : 7 * m + 7], n_dp, n_ex, inner)
            for m in range(extra)
        ]
        copies, rows_back = [], []
        for i in range(1, inner):
            to = lax.rem(z + i, inner)
            copy = remote(x_ref.at[to], buf.at[i], send.at[i], recv.at[i], group[i])
            copy.start()
            copies.append(copy)
        near, far = {}, {}
        for i in list(range(1, chips)) + [0]:
            chip = lax.rem(c + i, chips)
            for m in range(3):
                near[i, m] = remote(
                    s_in[m].at[chip * 2 + 1 - k], from_sib.at[m, i],
                    near_s.at[m, i], near_r.at[m, i], sibling,
                )
                near[i, m].start()
        for back in backs:
            back.begin()
        for i in range(1, chips):
            copy = remote(
                r_ref.at[i], r_out.at[i], r_s.at[i], r_r.at[i], same_core[chips - i - 1]
            )
            copy.start()
            rows_back.append(copy)
        copy = pltpu.make_async_copy(r_ref.at[0], r_out.at[0], local)
        copy.start()
        rows_back.append(copy)

        def pair(i, m):
            chip = lax.rem(c + i, chips)
            near[i, m].wait_recv()

            def row(d, carry):
                out_buf[m, i, d] = (
                    s_in[m][chip * 2 + k, d].astype(F32) + from_sib[m, i, d].astype(F32)
                ).astype(BF)
                return carry

            lax.fori_loop(0, n_dp, row, 0)

        for i in range(1, chips):
            for m in range(3):
                pair(i, m)
                far[i, m] = remote(
                    out_buf.at[m, i], from_far.at[m, i], far_s.at[m, i], far_r.at[m, i],
                    same_core[i - 1],
                )
                far[i, m].start()
        o_ref[...] = x_ref[lax.rem(z, inner)].astype(F32)
        for back in backs:
            back.pass_on()
        for m in range(3):
            pair(0, m)
        for i in range(1, inner):
            copies[i - 1].wait_recv()
            o_ref[...] += buf[i].astype(F32)
        for m in range(3):
            for i in range(1, chips):
                far[i, m].wait_recv()

            def row(d, carry, m=m):
                total = out_buf[m, 0, d].astype(F32)
                for i in range(1, chips):
                    total = total + from_far[m, i, d].astype(F32)
                s_out[m][d] = total.astype(BF)
                return carry

            lax.fori_loop(0, n_dp, row, 0)
        for copy in copies + list(near.values()) + list(far.values()):
            copy.wait_send()
        for copy in rows_back:
            copy.wait()
        for back in backs:
            back.end()

    dma = pltpu.SemaphoreType.DMA
    scratch = [pltpu.VMEM((inner,) + shape, BF)]
    scratch += [pltpu.VMEM((3, chips, n_dp, r, ff_s), BF)] * 3
    scratch += [dma((inner,))] * 2 + [dma((3, chips))] * 4 + [dma((chips,))] * 2 + [dma]
    for total in totals:
        scratch += ExpertsBack.scratch(total, n_dp, inner)
    outs = pl.pallas_call(
        kernel,
        out_shape=[jax.ShapeDtypeStruct(shape, F32)]
        + [jax.ShapeDtypeStruct((n_dp, r, ff_s), BF)] * 3
        + [jax.ShapeDtypeStruct(rows_out.shape, BF)]
        + [ExpertsBack.out(total, n_dp, inner) for total in totals],
        in_specs=[VMEM] * 4 + [ANY] * (1 + extra),
        out_specs=[VMEM] * 4 + [ANY] * (1 + extra),
        scratch_shapes=scratch,
        compiler_params=params(collective_id),
    )(array, *shared, rows_out, *totals)
    return outs[0], outs[1:4], outs[4], outs[5:]


def column_group(z, e, inner):
    start = z // inner * inner
    return [(start + lax.rem(z - start + i, inner), e) for i in range(inner)]


def first_exchange(tok, heads_w, pack, n_dp, n_ex, collective_id):
    chips = n_ex // 2

    def kernel(
        tok_ref, wa_ref, pk_ref, tok_out, wa_out, pk_out,
        t_send, t_recv, ts_send, ts_recv, a_send, a_recv, az_send, az_recv,
        p_send, p_recv, pf_send, pf_recv, ps_send, ps_recv, local,
    ):
        z, e, c, k, sibling, same_core, column = places(n_dp, n_ex)
        plane = [(z, lax.rem(e + i, n_ex)) for i in range(1, n_ex)]
        greet(plane + column)
        wa_far, pk_col, tok_far, near = [], [], [], []
        for i in range(1, n_ex):
            copy = remote(
                wa_ref.at[lax.rem(e + i, n_ex)], wa_out.at[z, e],
                a_send.at[i], a_recv.at[i], plane[i - 1],
            )
            copy.start()
            wa_far.append(copy)
        for i in range(1, n_dp):
            copy = remote(pk_ref, pk_out.at[z, e], p_send.at[i], p_recv.at[i], column[i - 1])
            copy.start()
            pk_col.append(copy)
        for i in range(1, chips):
            copy = remote(tok_ref, tok_out.at[e], t_send.at[i], t_recv.at[i], same_core[i - 1])
            copy.start()
            tok_far.append(copy)
        copy = remote(tok_ref, tok_out.at[e], ts_send.at[0], ts_recv.at[0], sibling)
        copy.start()
        near.append(copy)
        own = [
            pltpu.make_async_copy(wa_ref.at[e], wa_out.at[z, e], local.at[0]),
            pltpu.make_async_copy(pk_ref, pk_out.at[z, e], local.at[1]),
            pltpu.make_async_copy(tok_ref, tok_out.at[e], local.at[2]),
        ]
        for copy in own:
            copy.start()
        for copy in own:
            copy.wait()
        for copy in wa_far:
            copy.wait_recv()
        wa_col = []
        for i in range(1, n_dp):
            copy = remote(
                wa_out.at[z], wa_out.at[z], az_send.at[i], az_recv.at[i], column[i - 1]
            )
            copy.start()
            wa_col.append(copy)
        for copy in pk_col:
            copy.wait_recv()
        pk_far = []
        for i in range(1, chips):
            copy = remote(
                pk_out.at[:, e], pk_out.at[:, e], pf_send.at[i], pf_recv.at[i], same_core[i - 1]
            )
            copy.start()
            pk_far.append(copy)
        copy = remote(pk_out.at[:, e], pk_out.at[:, e], ps_send.at[0], ps_recv.at[0], sibling)
        copy.start()
        near.append(copy)
        for i in range(1, chips):
            source = lax.rem(c + chips - i, chips) * 2 + k
            tok_far[i - 1].wait_recv()
            copy = remote(
                tok_out.at[source], tok_out.at[source], ts_send.at[i], ts_recv.at[i], sibling
            )
            copy.start()
            near.append(copy)
            pk_far[i - 1].wait_recv()
            copy = remote(
                pk_out.at[:, source], pk_out.at[:, source], ps_send.at[i], ps_recv.at[i], sibling
            )
            copy.start()
            near.append(copy)
        for copy in near + wa_col:
            copy.wait()
        for copy in wa_far + pk_col + tok_far + pk_far:
            copy.wait_send()

    dma = pltpu.SemaphoreType.DMA
    return pl.pallas_call(
        kernel,
        out_shape=[
            jax.ShapeDtypeStruct((n_ex,) + tok.shape, tok.dtype),
            jax.ShapeDtypeStruct((n_dp,) + heads_w.shape, heads_w.dtype),
            jax.ShapeDtypeStruct((n_dp, n_ex) + pack.shape, pack.dtype),
        ],
        in_specs=[ANY] * 3,
        out_specs=[ANY] * 3,
        scratch_shapes=[dma((chips,))] * 4
        + [dma((n_ex,))] * 2
        + [dma((n_dp,))] * 4
        + [dma((chips,))] * 4
        + [dma((3,))],
        compiler_params=params(collective_id),
    )(tok, heads_w, pack)


class ExpertsIn:
    @staticmethod
    def scratch(n_dp):
        dma = pltpu.SemaphoreType.DMA
        return [dma((n_dp, 2)), dma((n_dp,)), dma((n_dp,)), dma((n_dp,))]

    @staticmethod
    def out(weight, n_dp, n_ex):
        return jax.ShapeDtypeStruct((n_ex, n_dp) + weight.shape[2:], BF)

    def __init__(self, weight, out, scratch, n_dp, n_ex, inner):
        self.weight, self.out, self.n_dp, self.inner = weight, out, n_dp, inner
        self.send, self.recv, self.sib_send, self.sib_recv = scratch
        self.z, self.e, self.c, self.k, self.sibling, _, _ = places(n_dp, n_ex)
        self.hh = n_ex // 2
        self.local = weight.shape[0]

    def sends(self, start):
        for i in list(range(1, self.n_dp)) + [0]:
            to = lax.rem(self.z + i, self.n_dp)
            expert = lax.rem(to, self.inner)

            def go(i=i, to=to, expert=expert):
                for h in range(2):
                    src = self.weight.at[lax.rem(expert, self.local), pl.ds(h * self.hh, self.hh)]
                    dst = self.out.at[pl.ds(h * self.hh, self.hh), self.z]
                    sem = self.recv.at[self.z]

                    def far(src=src, dst=dst, h=h):
                        copy = remote(src, dst, self.send.at[i, h], sem, (to, 2 * self.c + h))
                        if start:
                            copy.start()
                        else:
                            copy.wait_send()

                    if i:
                        far()
                    else:
                        pl.when(self.k != h)(far)
                        if start:

                            @pl.when(self.k == h)
                            def _(src=src, dst=dst):
                                pltpu.make_async_copy(src, dst, sem).start()

            pl.when(expert // self.local == self.k)(go)

    def begin(self):
        self.sends(True)

    def pass_on(self):
        mine = lax.rem(self.z, self.inner)
        for i in range(self.n_dp):
            d = lax.rem(self.z + self.n_dp - i, self.n_dp)
            region = self.out.at[pl.ds(self.k * self.hh, self.hh), d]
            if i:
                wait_recv(region, self.recv.at[d], self.sibling)
            else:
                from_here = mine // self.local == self.k

                @pl.when(from_here)
                def _(region=region, d=d):
                    src = self.weight.at[
                        lax.rem(mine, self.local), pl.ds(self.k * self.hh, self.hh)
                    ]
                    pltpu.make_async_copy(src, region, self.recv.at[d]).wait()

                @pl.when(jnp.logical_not(from_here))
                def _(region=region, d=d):
                    wait_recv(region, self.recv.at[d], self.sibling)

            remote(
                region, region, self.sib_send.at[i], self.sib_recv.at[i], self.sibling
            ).start()

    def end(self):
        self.sends(False)
        for i in range(self.n_dp):
            d = lax.rem(self.z + self.n_dp - i, self.n_dp)
            mine = self.out.at[pl.ds(self.k * self.hh, self.hh), d]
            remote(
                mine, mine, self.sib_send.at[i], self.sib_recv.at[i], self.sibling
            ).wait_send()
            region = self.out.at[pl.ds((1 - self.k) * self.hh, self.hh), d]
            wait_recv(region, self.sib_recv.at[i], self.sibling)


def forward_exchange(attend, w_out, tok, gain, cot, experts, shared, n_dp, n_ex, inner, collective_id):
    chips = n_ex // 2
    rows, width = tok.shape
    count = len(experts)
    r = w_out.shape[0]
    parts = DV // r
    hp = n_dp // parts
    seq = n_ex * rows
    rl = KVR // (n_dp * n_ex)
    we_cols = rl * hp * (DH + DV) // r
    wq_cols = hp * (DH + DR)

    def kernel(*refs):
        att_in, refs = refs[:8], refs[8:]
        wo_in, tok_ref, gain_ref, cot_in = refs[:4]
        e_in, s_in = refs[4 : 4 + count], refs[4 + count : 7 + count]
        refs = refs[7 + count :]
        att_out, refs = refs[:8], refs[8:]
        wq_ref, we_ref, wo_out, res_ref, xcol_ref, cot_out = refs[:6]
        w_out, s_out = refs[6 : 6 + count], refs[6 + count : 9 + count]
        refs = refs[9 + count :]
        x_ref, from_sib, out_buf, from_far, xbuf = refs[:5]
        (
            near_s, near_r, far_s, far_r, x_s, x_r,
            sh_s, sh_r, sp_s, sp_r, sf_s, sf_r, wo_s, wo_r, co_s, co_r, local,
        ) = refs[5:22]
        refs = refs[22:]
        z, e, c, k, sibling, same_core, column = places(n_dp, n_ex)
        group = column_group(z, e, inner)
        part = lax.rem(e, parts)
        members = [
            (lax.rem(z + i, n_dp), e - part + lax.rem(part + j, parts))
            for i in range(n_dp)
            for j in range(parts)
        ]
        greet(same_core + column + [(device[0], sibling[1]) for device in column] + members[1:])

        def wo_sends(start):
            for i in range(n_dp):
                target = (lax.rem(z + i, n_dp), e - part + z // hp)
                dst, sem = wo_out.at[lax.rem(z, hp), part], wo_r.at[lax.rem(z, hp), part]

                def far(i=i, target=target, dst=dst, sem=sem):
                    copy = remote(wo_in, dst, wo_s.at[i], sem, target)
                    if start:
                        copy.start()
                    else:
                        copy.wait_send()

                if i:
                    far()
                else:
                    pl.when(z // hp != part)(far)
                    if start:

                        @pl.when(z // hp == part)
                        def _(dst=dst, sem=sem):
                            pltpu.make_async_copy(wo_in, dst, sem).start()

        def wo_arrivals():
            for h in range(hp):
                for p in range(parts):
                    here = jnp.logical_and(part * hp + h == z, part == p)

                    @pl.when(here)
                    def _(h=h, p=p):
                        pltpu.make_async_copy(wo_in, wo_out.at[h, p], wo_r.at[h, p]).wait()

                    @pl.when(jnp.logical_not(here))
                    def _(h=h, p=p):
                        wait_recv(wo_out.at[h, p], wo_r.at[h, p], sibling)

        my_l = lax.rem(z, inner)
        matrices = [
            ExpertsIn(e_in[m], w_out[m], refs[4 * m : 4 * m + 4], n_dp, n_ex, inner)
            for m in range(count)
        ]
        wo_sends(True)
        shared_copies = []
        for i in range(1, n_dp):
            for m in range(3):
                copy = remote(
                    s_in[m].at[lax.rem(lax.rem(z + i, n_dp), inner)], s_out[m].at[e, z],
                    sh_s.at[m, i], sh_r.at[m, i], column[i - 1],
                )
                copy.start()
                shared_copies.append(copy)
        own = [
            pltpu.make_async_copy(s_in[m].at[my_l], s_out[m].at[e, z], local.at[m])
            for m in range(3)
        ]
        for copy in own:
            copy.start()
        matrices[0].begin()
        cot_copies = []
        for i in range(1, inner):
            copy = remote(cot_in, cot_out.at[my_l], co_s.at[i], co_r.at[i], group[i])
            copy.start()
            cot_copies.append(copy)
        copy = pltpu.make_async_copy(cot_in, cot_out.at[my_l], local.at[4])
        copy.start()
        cot_copies.append(copy)
        tok_all, gain_one, wa_ref, wl_ref, gain_lat, cos, sin, keep = att_in
        wq_ref[...] = wa_ref[:, :, :, :wq_cols].reshape(width, wq_cols)
        for j in range(r // rl):
            block = wa_ref[:, :, j * rl : (j + 1) * rl, wq_cols:].reshape(KVR, we_cols)
            we_ref[:, j * we_cols : (j + 1) * we_cols] = block
        attend_forward(
            tok_all, gain_one, wq_ref, wl_ref, gain_lat, we_ref, cos, sin, keep, *att_out
        )
        wo_arrivals()
        wo = wo_out[...].reshape(hp * DV, width)

        def project(i, carry):
            at = pl.ds(pl.multiple_of(i * 2 * rows, 2 * rows), 2 * rows)
            block = mm(att_out[7][at, :], wo).astype(BF)
            x_ref[pl.ds(2 * i, 2)] = block.reshape(2, rows, width)
            return carry

        lax.fori_loop(0, chips, project, 0)
        near = []
        for i in list(range(1, chips)) + [0]:
            chip = lax.rem(c + i, chips)
            copy = remote(
                x_ref.at[chip * 2 + 1 - k], from_sib.at[chip], near_s.at[i], near_r.at[i], sibling
            )
            copy.start()
            near.append(copy)
        far = []
        for i in range(1, chips):
            chip = lax.rem(c + i, chips)
            near[i - 1].wait_recv()
            out_buf[i] = (
                x_ref[chip * 2 + k].astype(F32) + from_sib[chip].astype(F32)
            ).astype(BF)
            copy = remote(out_buf.at[i], from_far.at[i], far_s.at[i], far_r.at[i], same_core[i - 1])
            copy.start()
            far.append(copy)
        near[chips - 1].wait_recv()
        res_ref[...] = x_ref[e].astype(F32) + from_sib[c].astype(F32) + tok_ref[...].astype(F32)
        for i in range(1, chips):
            far[i - 1].wait_recv()
            res_ref[...] += from_far[i].astype(F32)
        residual = res_ref[...]
        scale = lax.rsqrt(jnp.mean(residual * residual, axis=-1, keepdims=True) + norm_eps)
        xbuf[...] = (residual * scale * gain_ref[...]).astype(BF)
        x_copies = []
        for i in range(1, inner):
            copy = remote(xbuf, xcol_ref.at[my_l], x_s.at[i], x_r.at[i], group[i])
            copy.start()
            x_copies.append(copy)
        x_own = pltpu.make_async_copy(xbuf, xcol_ref.at[my_l], local.at[3])
        x_own.start()
        for matrix in matrices[1:]:
            matrix.begin()
        for copy in own:
            copy.wait()
        for copy in shared_copies:
            copy.wait_recv()
        plane, to_sib = [], []
        for m in range(3):
            block = s_out[m].at[e]
            for i in range(1, chips):
                copy = remote(block, block, sp_s.at[m, i], sp_r.at[m, i], same_core[i - 1])
                copy.start()
                plane.append(copy)
            copy = remote(block, block, sf_s.at[m, 0], sf_r.at[m, 0], sibling)
            copy.start()
            to_sib.append(copy)
        for m in range(3):
            for i in range(1, chips):
                plane[m * (chips - 1) + i - 1].wait_recv()
                block = s_out[m].at[lax.rem(c + chips - i, chips) * 2 + k]
                copy = remote(block, block, sf_s.at[m, i], sf_r.at[m, i], sibling)
                copy.start()
                to_sib.append(copy)
        for matrix in matrices:
            matrix.pass_on()
        for copy in x_copies + cot_copies + to_sib:
            copy.wait()
        x_own.wait()
        for copy in plane + shared_copies + near + far:
            copy.wait_send()
        wo_sends(False)
        for matrix in matrices:
            matrix.end()

    dma = pltpu.SemaphoreType.DMA
    ff_s = shared[0].shape[2]
    scratch = []
    for _ in experts:
        scratch += ExpertsIn.scratch(n_dp)
    sds = jax.ShapeDtypeStruct
    outs = pl.pallas_call(
        kernel,
        out_shape=[
            sds((seq, width), BF),
            sds((seq, attend[3].shape[1]), F32),
            sds((seq, KVR), BF),
            sds((2, seq, 2 * DH), BF),
            sds((2, seq, 2 * DH), BF),
            sds((2, seq, DV), BF),
            sds((2, seq, 128), F32),
            sds((seq, 2 * DV), BF),
            sds((width, wq_cols), BF),
            sds((KVR, hp * (DH + DV)), BF),
            sds((hp, parts, r, width), BF),
            sds((rows, width), F32),
            sds((inner, rows, width), BF),
            sds((inner, rows, width), BF),
        ]
        + [ExpertsIn.out(w, n_dp, n_ex) for w in experts]
        + [sds((n_ex, n_dp, r, ff_s), BF)] * 3,
        in_specs=[VMEM] * 8 + [ANY] + [VMEM] * 2 + [ANY] * (4 + count),
        out_specs=[VMEM] * 12 + [ANY] * (5 + count),
        scratch_shapes=[pltpu.VMEM((n_ex, rows, width), BF)]
        + [pltpu.VMEM((chips, rows, width), BF)] * 3
        + [pltpu.VMEM((rows, width), BF)]
        + [dma((chips,))] * 4
        + [dma((inner,))] * 2
        + [dma((3, n_dp))] * 2
        + [dma((3, chips))] * 4
        + [dma((n_dp,)), dma((hp, parts))]
        + [dma((inner,))] * 2
        + [dma((5,))]
        + scratch,
        compiler_params=params(collective_id),
    )(*attend, w_out, tok, gain, cot, *experts, *shared)
    return outs[:8], outs[8:11], outs[11], outs[12], outs[13], outs[14 : 14 + count], outs[14 + count :]


def silu_parts(a):
    sig = 1.0 / (1.0 + jnp.exp(-a))
    return a * sig, sig * (1.0 + a * (1.0 - sig))


def dispatch(hot, x, cot, shared, weights, n_dp, n_ex, inner, collective_id):
    chips = n_ex // 2
    rows, width = x.shape
    ff = shared[0].shape[1]
    tile = 256

    per_far = hot.shape[0] // chips
    count = len(weights)

    def kernel(hot_ref, x_hbm, c_hbm, g_hbm, u_hbm, d_hbm, *refs):
        w_in, refs = refs[:count], refs[count:]
        o_ref, go_ref, w_out, refs = refs[0], refs[1], refs[2 : 2 + count], refs[2 + count :]
        out_ref, dx_ref, gg_ref, gu_ref, gd_ref = refs[:5]
        hot_v, x_v, c_v, g_v, u_v, d_v, hid, ga, gb, b_v, send, recv, loads, keep = refs[5:19]
        rest = refs[19:]
        z, e, c, k, sibling, same_core, column = places(n_dp, n_ex)
        moves = [
            pltpu.make_async_copy(src, dst, loads.at[j])
            for j, (src, dst) in enumerate(
                [
                    (hot_ref, hot_v), (x_hbm, x_v), (c_hbm, c_v),
                    (g_hbm, g_v), (u_hbm, u_v), (d_hbm, d_v),
                ]
            )
        ]
        for copy in moves:
            copy.start()
        greet(same_core + [sibling] + column + [(device[0], sibling[1]) for device in column])
        matrices = [
            ExpertsIn(w_in[m], w_out[m], rest[4 * m : 4 * m + 4], n_dp, n_ex, inner)
            for m in range(count)
        ]
        for matrix in matrices:
            matrix.begin()
        copies = []
        for j, (source, target) in enumerate(((x_v, o_ref), (c_v, go_ref))):
            if not j:
                moves[0].wait()
            moves[1 + j].wait()
            for i in list(range(1, chips)) + [0]:
                block = mm(hot_v[i * per_far : (i + 1) * per_far, :], source[...])
                b_v[j, i] = block.astype(BF)
                if i:
                    copy = remote(
                        b_v.at[j, i], target.at[i], send.at[j, i], recv.at[j, i],
                        same_core[i - 1],
                    )
                else:
                    copy = pltpu.make_async_copy(b_v.at[j, 0], target.at[0], keep.at[j])
                copy.start()
                copies.append(copy)
        for copy in moves[3:]:
            copy.wait()

        def rows_of(i, carry):
            at = pl.ds(pl.multiple_of(i * tile, tile), tile)
            first = mm(x_v[at, :], g_v[...])
            second = mm(x_v[at, :], u_v[...])
            silu, slope = silu_parts(first)
            low = (silu * second).astype(BF)
            hid[at, :] = low
            out_ref[at, :] = mm_cols(low, d_v[...])
            back = mm(c_v[at, :], d_v[...])
            low_a = (back * second * slope).astype(BF)
            low_b = (back * silu).astype(BF)
            ga[at, :] = low_a
            gb[at, :] = low_b
            dx_ref[at, :] = mm_cols(low_a, g_v[...]) + mm_cols(low_b, u_v[...])
            return carry

        lax.fori_loop(0, rows // tile, rows_of, 0)

        def columns_of(j, carry):
            at = pl.ds(pl.multiple_of(j * tile, tile), tile)
            gg_ref[at, :] = mm_rows(x_v[:, at], ga[...]).astype(BF)
            gu_ref[at, :] = mm_rows(x_v[:, at], gb[...]).astype(BF)
            gd_ref[at, :] = mm_rows(c_v[:, at], hid[...]).astype(BF)
            return carry

        lax.fori_loop(0, width // tile, columns_of, 0)
        for matrix in matrices:
            matrix.pass_on()
        for copy in copies:
            copy.wait()
        for matrix in matrices:
            matrix.end()

    dma = pltpu.SemaphoreType.DMA
    sds = jax.ShapeDtypeStruct
    vmem = pltpu.VMEM
    scratch = []
    for _ in weights:
        scratch += ExpertsIn.scratch(n_dp)
    outs = pl.pallas_call(
        kernel,
        out_shape=[sds((chips, per_far, width), BF)] * 2
        + [ExpertsIn.out(weight, n_dp, n_ex) for weight in weights]
        + [sds((rows, width), F32)] * 2
        + [sds((width, ff), BF)] * 3,
        in_specs=[ANY] * (6 + count),
        out_specs=[ANY] * (2 + count) + [VMEM] * 5,
        scratch_shapes=[vmem(hot.shape, BF)]
        + [vmem((rows, width), BF)] * 2
        + [vmem((width, ff), BF)] * 3
        + [vmem((rows, ff), BF)] * 3
        + [vmem((2, chips, per_far, width), BF)]
        + [dma((2, chips)), dma((2, chips)), dma((6,)), dma((2,))]
        + scratch,
        compiler_params=params(collective_id),
    )(hot, x, cot, *shared, *weights)
    return outs[:2], outs[2 : 2 + count], outs[2 + count], outs[3 + count], outs[4 + count :]


def experts_back(values, weights, dots, n_dp, n_ex, inner, collective_id):
    chips = n_ex // 2
    n_slots, width = values[0].shape
    ff = values[2].shape[1]
    per_far = n_slots // chips
    r = width // (n_dp * n_ex)
    tile = 256
    span = n_dp * r

    def kernel(*refs):
        v_hbm, w_hbm, dots_ref, refs = refs[:5], refs[5:8], refs[8], refs[9:]
        dx_out, dots_out, back_out, g_out, refs = refs[0], refs[1], refs[2], refs[3:5], refs[5:]
        x_v, s_v, a_v, b_v, h_v, wg, wu, wd, dx_v, total, stage = refs[:11]
        loads, send, recv, d_send, d_recv, local, out_sem = refs[11:18]
        z, e, c, k, sibling, same_core, column = places(n_dp, n_ex)
        moves = [
            pltpu.make_async_copy(src, dst, loads.at[j])
            for j, (src, dst) in enumerate(
                zip((*v_hbm, *w_hbm), (x_v, s_v, a_v, b_v, h_v, wg, wu, wd))
            )
        ]
        for j in (1, 4, 7, 2, 3, 5, 6, 0):
            moves[j].start()
        greet(same_core + [sibling] + column + [(device[0], sibling[1]) for device in column])
        back = ExpertsBack(total, back_out, refs[18:], n_dp, n_ex, inner)
        dot_copies = []
        for i in range(1, chips):
            copy = remote(
                dots_ref.at[i], dots_out.at[i], d_send.at[i], d_recv.at[i],
                same_core[chips - i - 1],
            )
            copy.start()
            dot_copies.append(copy)
        copy = pltpu.make_async_copy(dots_ref.at[0], dots_out.at[0], local.at[0])
        copy.start()
        dot_copies.append(copy)
        moves[1].wait()
        moves[4].wait()

        def down_rows(t, carry):
            j = lax.rem(t + (1 - k) * (n_ex // 2), n_ex)
            at = pl.ds(pl.multiple_of(j * span, span), span)
            block = mm_rows(s_v[:, at], h_v[...]).astype(BF)
            total[j] = block.reshape(n_dp, r, ff)
            return carry

        lax.fori_loop(0, n_ex, down_rows, 0)
        back.begin()
        for j in (7, 2, 3):
            moves[j].wait()

        def hidden_rows(i, carry):
            at = pl.ds(pl.multiple_of(i * tile, tile), tile)
            grad = mm(s_v[at, :], wd[...])
            silu, slope = silu_parts(a_v[at, :].astype(F32))
            second = b_v[at, :].astype(F32)
            a_v[at, :] = (grad * second * slope).astype(BF)
            b_v[at, :] = (grad * silu).astype(BF)
            return carry

        lax.fori_loop(0, n_slots // tile, hidden_rows, 0)
        moves[5].wait()
        moves[6].wait()
        copies = []
        for i in list(range(1, chips)) + [0]:
            at = slice(i * per_far, (i + 1) * per_far)
            block = mm_cols(a_v[at, :], wg[...]) + mm_cols(b_v[at, :], wu[...])
            dx_v[i] = block.astype(BF)
            if i:
                copy = remote(
                    dx_v.at[i], dx_out.at[i], send.at[i], recv.at[i], same_core[chips - i - 1]
                )
            else:
                copy = pltpu.make_async_copy(dx_v.at[0], dx_out.at[0], local.at[1])
            copy.start()
            copies.append(copy)
            if i == 1:
                back.pass_on()
        moves[0].wait()

        def other_rows(j, carry):
            at = pl.ds(pl.multiple_of(j * span, span), span)
            for m, side in enumerate((a_v, b_v)):

                @pl.when(j > 0)
                def _(m=m):
                    pltpu.make_async_copy(stage.at[m], g_out[m].at[j - 1], out_sem.at[m]).wait()

                block = mm_rows(x_v[:, at], side[...]).astype(BF)
                stage[m] = block.reshape(n_dp, r, ff)
                pltpu.make_async_copy(stage.at[m], g_out[m].at[j], out_sem.at[m]).start()
            return carry

        lax.fori_loop(0, n_ex, other_rows, 0)
        for m in range(2):
            pltpu.make_async_copy(stage.at[m], g_out[m].at[n_ex - 1], out_sem.at[m]).wait()
        for copy in copies + dot_copies:
            copy.wait()
        back.end()

    dma = pltpu.SemaphoreType.DMA
    sds = jax.ShapeDtypeStruct
    vmem = pltpu.VMEM
    total = sds((n_ex, n_dp, r, ff), BF)
    outs = pl.pallas_call(
        kernel,
        out_shape=[
            sds((chips, per_far, width), BF),
            sds(dots.shape, BF),
            ExpertsBack.out(total, n_dp, inner),
            total,
            total,
        ],
        in_specs=[ANY] * 9,
        out_specs=[ANY] * 5,
        scratch_shapes=[vmem((n_slots, width), BF)] * 2
        + [vmem((n_slots, ff), BF)] * 3
        + [vmem((width, ff), BF)] * 3
        + [
            vmem((chips, per_far, width), BF),
            vmem(total.shape, BF),
            vmem((2, n_dp, r, ff), BF),
            dma((8,)),
        ]
        + [dma((chips,))] * 4
        + [dma((2,))] * 2
        + ExpertsBack.scratch(total, n_dp, inner),
        compiler_params=params(collective_id),
    )(*values, *weights, dots)
    return outs[0], outs[1], outs[2], outs[3:]


class ExpertsBack:
    @staticmethod
    def scratch(total, n_dp, inner):
        n_ex, _, r, ff = total.shape
        dma = pltpu.SemaphoreType.DMA
        hh = n_ex // 2
        return [
            pltpu.VMEM((hh, n_dp, r, ff), BF),
            pltpu.VMEM((hh, n_dp, r, ff), BF),
            dma((hh,)),
            dma((hh,)),
            dma((hh,)),
            dma((hh, n_dp)),
            dma((n_dp // inner, 2, 2, hh)),
        ]

    @staticmethod
    def out(total, n_dp, inner):
        n_ex, _, r, ff = total.shape
        return jax.ShapeDtypeStruct((n_dp // inner, 2, n_ex, r, ff), BF)

    def __init__(self, total, out, scratch, n_dp, n_ex, inner):
        self.total, self.out, self.n_dp, self.inner = total, out, n_dp, inner
        self.own, self.sib, self.near_s, self.near_r, self.load, self.send, self.recv = scratch
        self.z, self.e, self.c, self.k, self.sibling, _, _ = places(n_dp, n_ex)
        self.hh = n_ex // 2

    def near(self, j):
        return remote(
            self.total.at[(1 - self.k) * self.hh + j], self.sib.at[j],
            self.near_s.at[j], self.near_r.at[j], self.sibling,
        )

    def loads(self, j):
        return pltpu.make_async_copy(
            self.total.at[self.k * self.hh + j], self.own.at[j], self.load.at[j]
        )

    def begin(self):
        for j in range(self.hh):
            self.near(j).start()
            self.loads(j).start()

    def route(self, j, i):
        d = lax.rem(self.z + i, self.n_dp)
        expert = lax.rem(self.z, self.inner)
        o = self.z // self.inner
        dst = self.out.at[o, lax.rem(expert, 2), self.k * self.hh + j]
        sem = self.recv.at[o, lax.rem(expert, 2), self.k, j]
        return self.own.at[j, d], dst, sem, (d, 2 * self.c + expert // 2)

    def stay(self, j):
        src, dst, sem, _ = self.route(j, 0)
        return pltpu.make_async_copy(src, dst, sem)

    def go(self, j, i):
        src, dst, sem, device = self.route(j, i)
        return remote(src, dst, self.send.at[j, i], sem, device)

    def here(self):
        return lax.rem(self.z, self.inner) // 2 == self.k

    def pass_on(self):
        for j in range(self.hh):
            self.near(j).wait_recv()
            self.loads(j).wait()
            for d in range(self.n_dp):
                self.own[j, d] = (
                    self.own[j, d].astype(F32) + self.sib[j, d].astype(F32)
                ).astype(BF)
            for i in range(1, self.n_dp):
                self.go(j, i).start()
            pl.when(self.here())(lambda j=j: self.stay(j).start())
            pl.when(jnp.logical_not(self.here()))(lambda j=j: self.go(j, 0).start())

    def end(self):
        for j in range(self.hh):
            self.near(j).wait_send()
            for i in range(1, self.n_dp):
                self.go(j, i).wait_send()
            pl.when(jnp.logical_not(self.here()))(lambda j=j: self.go(j, 0).wait_send())
        for o in range(self.n_dp // self.inner):
            for i in range(2):
                for h in range(2):
                    source = o * self.inner + 2 * self.k + i
                    here = jnp.logical_and(source == self.z, self.k == h)
                    for j in range(self.hh):
                        region = self.out.at[o, i, h * self.hh + j]
                        sem = self.recv.at[o, i, h, j]

                        @pl.when(here)
                        def _(region=region, sem=sem, j=j):
                            pltpu.make_async_copy(self.own.at[j, self.z], region, sem).wait()

                        @pl.when(jnp.logical_not(here))
                        def _(region=region, sem=sem):
                            wait_recv(region, sem, self.sibling)


def rms_back(x, gain, grad):
    root = lax.rsqrt(jnp.mean(x * x, axis=-1, keepdims=True) + norm_eps)
    scaled = grad * gain
    along = jnp.mean(x * scaled, axis=-1, keepdims=True)
    return root * scaled - x * (root * root * root) * along, grad * x * root


def backward_exchange(
    grad, attend, hidden, latent_low, own, out, shared, totals, n_dp, n_ex, inner, collective_id
):
    chips = n_ex // 2
    rows, width = grad.shape
    seq = n_ex * rows
    extra = len(totals)
    wq, we = attend[1], attend[2]
    lat_cols = KVR + 2 * DR
    r = width // (n_dp * n_ex)
    rl = KVR // (n_dp * n_ex)
    parts = DV // r
    hp = n_dp // parts
    n_dev = n_dp * n_ex
    wq_cols = wq.shape[1]
    we_cols = rl * we.shape[1] // r
    head_cols = wq_cols + we_cols

    def kernel(*refs):
        grad_ref, att_in, refs = refs[0], refs[1:12], refs[12:]
        hidden_ref, low_ref, refs = refs[0], refs[1], refs[2:]
        wl_ref, lat_ref, tok_ref, gain_ref, glat_ref, gnat_ref, router_ref, gtwo_ref = refs[:8]
        out_ref, sh_in, refs = refs[8], refs[9:12], refs[12:]
        t_refs, refs = refs[:extra], refs[extra:]
        tok_out, vec_out, pack_out, heads_mid, heads_out, wout_out, out_got = refs[:7]
        sh_out, back_refs, refs = refs[7:10], refs[10 : 10 + extra], refs[10 + extra :]
        gbuf, att_tmp, refs = refs[0], refs[1:8], refs[8:]
        part_l, bufs, sums, refs = refs[0], refs[1:7], refs[7:9], refs[9:]
        hsrc, wsrc, pack, psib, pout, pfar, psum, pbuf, vec, vbuf, vzbuf = refs[:11]
        refs = refs[11:]
        t_s, t_r, ts_s, ts_r, local = refs[:5]
        sems, refs = refs[5:13], refs[13:]
        (
            h_s, h_r, hz_s, hz_r, w_s, w_r, pn_s, pn_r, pf_s, pf_r, pc_s, pc_r, s_s, s_r,
            v_s, v_r, vz_s, vz_r, o_s, o_r,
        ) = refs[:20]
        rest = refs[20:]
        x_refs = (gbuf, part_l)
        group = column_group(lax.axis_index("dp"), lax.axis_index("expert"), inner)
        z, e, c, k, sibling, same_core, column = places(n_dp, n_ex)
        plane = [(z, lax.rem(e + i, n_ex)) for i in range(1, n_ex)]
        part = lax.rem(e, parts)
        members = [
            (lax.rem(z + i, n_dp), e - part + lax.rem(part + j, parts))
            for i in range(n_dp)
            for j in range(parts)
        ]
        greet(plane + column + [(d[0], sibling[1]) for d in column] + members[1:])
        backs = [
            ExpertsBack(t_refs[m], back_refs[m], rest[7 * m : 7 * m + 7], n_dp, n_ex, inner)
            for m in range(extra)
        ]
        gather, to_sib, others = [], [], []
        for i in range(1, chips):
            copy = remote(grad_ref, gbuf.at[e], t_s.at[i], t_r.at[i], same_core[i - 1])
            copy.start()
            gather.append(copy)
        copy = remote(grad_ref, gbuf.at[e], ts_s.at[0], ts_r.at[0], sibling)
        copy.start()
        to_sib.append(copy)
        keep = pltpu.make_async_copy(grad_ref, gbuf.at[e], local.at[0])
        keep.start()
        for back in backs:
            back.begin()
        for m in range(3):
            for i in range(1, n_dp):
                copy = remote(
                    sh_in[m].at[lax.rem(z + i, n_dp)], sh_out[m].at[z],
                    s_s.at[m, i], s_r.at[m, i], column[i - 1],
                )
                copy.start()
                others.append(copy)
            copy = pltpu.make_async_copy(sh_in[m].at[z], sh_out[m].at[z], local.at[1 + m])
            copy.start()
            others.append(copy)
        mine = lax.rem(z, inner)
        for i in range(1, inner):
            copy = remote(
                out_ref.at[lax.rem(mine + i, inner)], out_got.at[mine], o_s.at[i], o_r.at[i],
                group[i],
            )
            copy.start()
            others.append(copy)
        copy = pltpu.make_async_copy(out_ref.at[mine], out_got.at[mine], local.at[5])
        copy.start()
        others.append(copy)
        for i in range(1, chips):
            gather[i - 1].wait_recv()
            block = gbuf.at[lax.rem(c + chips - i, chips) * 2 + k]
            copy = remote(block, block, ts_s.at[i], ts_r.at[i], sibling)
            copy.start()
            to_sib.append(copy)
        for back in backs:
            back.pass_on()
        keep.wait()
        for copy in to_sib:
            copy.wait_recv()
        for copy in gather + to_sib:
            copy.wait_send()
        gat, grad_wout, dk, dv, grad_query, grad_expanded, grad_rope = att_tmp
        attend_backward(gbuf, *att_in, *att_tmp)

        wsrc[...] = grad_wout[...].astype(BF).reshape(hp, parts, r, width)

        def wout_sends(start):
            for h in range(hp):
                for p in range(parts):
                    target = (part * hp + h, e - part + p)
                    here = jnp.logical_and(part * hp + h == z, p == part)

                    def far(h=h, p=p, target=target):
                        copy = remote(
                            wsrc.at[h, p], wout_out.at[z], w_s.at[h, p], w_r.at[z], target
                        )
                        if start:
                            copy.start()
                        else:
                            copy.wait_send()

                    pl.when(jnp.logical_not(here))(far)
                    if start:

                        @pl.when(here)
                        def _(h=h, p=p):
                            pltpu.make_async_copy(
                                wsrc.at[h, p], wout_out.at[z], w_r.at[z]
                            ).start()

        wout_sends(True)

        def spread(i, carry):
            at = pl.ds(pl.multiple_of(i * 2 * rows, 2 * rows), 2 * rows)
            block = mm_cols(grad_query[at, :], att_in[1][...]).astype(BF)
            gbuf[pl.ds(2 * i, 2)] = block.reshape(2, rows, width)
            block = mm_cols(grad_expanded[at, :], att_in[2][...]).astype(BF)
            part_l[pl.ds(2 * i, 2), :, :KVR] = block.reshape(2, rows, KVR)
            block = grad_rope[at, :].astype(BF)
            part_l[pl.ds(2 * i, 2), :, KVR:] = block.reshape(2, rows, 2 * DR)
            return carry

        lax.fori_loop(0, chips, spread, 0)
        near, far = {}, {}
        for i in list(range(1, chips)) + [0]:
            chip = lax.rem(c + i, chips)
            for j in range(2):
                near[i, j] = remote(
                    x_refs[j].at[chip * 2 + 1 - k],
                    bufs[3 * j].at[chip],
                    sems[4 * j].at[i],
                    sems[4 * j + 1].at[i],
                    sibling,
                )
                near[i, j].start()
        for i in range(1, chips):
            chip = lax.rem(c + i, chips)
            for j in range(2):
                from_sib, out_buf, from_far = bufs[3 * j : 3 * j + 3]
                near[i, j].wait_recv()
                out_buf[i] = (
                    x_refs[j][chip * 2 + k].astype(F32) + from_sib[chip].astype(F32)
                ).astype(BF)
                far[i, j] = remote(
                    out_buf.at[i],
                    from_far.at[i],
                    sems[4 * j + 2].at[i],
                    sems[4 * j + 3].at[i],
                    same_core[i - 1],
                )
                far[i, j].start()

        per_tile = 256 // r

        def wq_rows(i, carry):
            at = pl.ds(pl.multiple_of(i * 256, 256), 256)
            block = mm_rows(hidden_ref[:, at], grad_query[...]).astype(BF)
            hsrc[pl.ds(i * per_tile, per_tile), :, :wq_cols] = block.reshape(
                per_tile, r, wq_cols
            )
            return carry

        lax.fori_loop(0, width // 256, wq_rows, 0)
        grad_we = mm_rows(low_ref[...], grad_expanded[...]).astype(BF)
        for j in range(r // rl):
            block = grad_we[:, j * we_cols : (j + 1) * we_cols]
            hsrc[:, j * rl : (j + 1) * rl, wq_cols:] = block.reshape(n_dev, rl, we_cols)
        heads_far = []
        for i in range(1, n_ex):
            for d in range(n_dp):
                copy = remote(
                    hsrc.at[d * n_ex + lax.rem(e + i, n_ex)], heads_mid.at[d, e],
                    h_s.at[i, d], h_r.at[i, d], plane[i - 1],
                )
                copy.start()
                heads_far.append(copy)
        for d in range(n_dp):
            copy = pltpu.make_async_copy(
                hsrc.at[d * n_ex + e], heads_mid.at[d, e], h_r.at[0, d]
            )
            copy.start()
            copy.wait()
        for j in range(2):
            near[0, j].wait_recv()
            sums[j][...] = x_refs[j][e].astype(F32) + bufs[3 * j][c].astype(F32)
        for i in range(1, chips):
            for j in range(2):
                far[i, j].wait_recv()
                sums[j][...] += bufs[3 * j + 2][i].astype(F32)

        at = pl.ds(pl.multiple_of(e * rows, rows), rows)
        cos, sin = att_in[3][at, :], att_in[4][at, :]
        lat_grad, lat_gain = rms_back(lat_ref[:, :KVR], glat_ref[...], sums[1][:, :KVR])
        rope = turn(sums[1][:, KVR:], cos, sin, -1.0)
        lane = lax.broadcasted_iota(jnp.int32, rope.shape, 1)
        rope = jnp.where(lane < DR, rope, 0.0)
        low = jnp.concatenate([lat_grad, rope], axis=1).astype(BF)
        total = sums[0][...] + mm_cols(low, wl_ref[:, :lat_cols])
        tok_grad, tok_gain = rms_back(tok_ref[...].astype(F32), gain_ref[...], total)
        tok_out[...] = gnat_ref[...] + tok_grad
        vec[...] = jnp.zeros_like(vec)
        vec[0:1, :] = jnp.sum(tok_gain, axis=0, keepdims=True)
        vec[1:2, :] = gtwo_ref[...]
        vec[2:3, :KVR] = jnp.sum(lat_gain, axis=0, keepdims=True)
        vec_far = []
        for i in range(1, n_ex):
            copy = remote(vec, vbuf.at[i], v_s.at[i], v_r.at[i], plane[i - 1])
            copy.start()
            vec_far.append(copy)
        for d in range(n_dp):
            block = hidden_ref[at, d * n_ex * r : (d + 1) * n_ex * r]
            block = mm_rows(block, low).reshape(n_ex, r, lat_cols)
            pack[:, d * r : (d + 1) * r, :KVR] = block[:, :, :KVR].astype(BF)
            block = block[:, :, KVR:] + router_ref[:, d * r : (d + 1) * r].astype(F32)
            pack[:, d * r : (d + 1) * r, KVR:] = block.astype(BF)
        pack_near, pack_far = [], []
        for i in list(range(1, chips)) + [0]:
            chip = lax.rem(c + i, chips)
            copy = remote(pack.at[chip * 2 + 1 - k], psib.at[chip], pn_s.at[i], pn_r.at[i], sibling)
            copy.start()
            pack_near.append(copy)
        for copy in heads_far:
            copy.wait_recv()
        heads_col = []
        for i in range(1, n_dp):
            d = lax.rem(z + i, n_dp)
            copy = remote(
                heads_mid.at[d], heads_out.at[z], hz_s.at[i], hz_r.at[i], column[i - 1]
            )
            copy.start()
            heads_col.append(copy)
        copy = pltpu.make_async_copy(heads_mid.at[z], heads_out.at[z], local.at[4])
        copy.start()
        heads_col.append(copy)
        for i in range(1, chips):
            chip = lax.rem(c + i, chips)
            pack_near[i - 1].wait_recv()
            pout[i] = (pack[chip * 2 + k].astype(F32) + psib[chip].astype(F32)).astype(BF)
            copy = remote(pout.at[i], pfar.at[i], pf_s.at[i], pf_r.at[i], same_core[i - 1])
            copy.start()
            pack_far.append(copy)
        for copy in vec_far:
            copy.wait_recv()
            copy.wait_send()
        for i in range(1, n_ex):
            vec[...] += vbuf[i]
        vec_col = []
        for i in range(1, n_dp):
            copy = remote(vec, vzbuf.at[i], vz_s.at[i], vz_r.at[i], column[i - 1])
            copy.start()
            vec_col.append(copy)
        pack_near[chips - 1].wait_recv()
        total = pack[e].astype(F32) + psib[c].astype(F32)
        for i in range(1, chips):
            pack_far[i - 1].wait_recv()
            total = total + pfar[i].astype(F32)
        psum[...] = total.astype(BF).reshape(n_dp, r, lat_cols)
        pack_col = []
        for i in range(1, n_dp):
            copy = remote(
                psum.at[lax.rem(z + i, n_dp)], pbuf.at[i], pc_s.at[i], pc_r.at[i], column[i - 1]
            )
            copy.start()
            pack_col.append(copy)
        result = vec[...]
        for i in range(1, n_dp):
            vec_col[i - 1].wait_recv()
            result = result + vzbuf[i]
        vec_out[...] = result
        result = psum[z].astype(F32)
        for i in range(1, n_dp):
            pack_col[i - 1].wait_recv()
            result = result + pbuf[i].astype(F32)
        pack_out[...] = result

        for i in range(n_dp):
            here = jnp.logical_and(z // hp == part, z == i)

            @pl.when(here)
            def _(i=i):
                pltpu.make_async_copy(
                    wsrc.at[lax.rem(z, hp), part], wout_out.at[i], w_r.at[i]
                ).wait()

            @pl.when(jnp.logical_not(here))
            def _(i=i):
                wait_recv(wout_out.at[i], w_r.at[i], sibling)

        wout_sends(False)
        for copy in list(near.values()) + list(far.values()) + heads_far:
            copy.wait_send()
        for copy in pack_near + pack_far + vec_col + pack_col:
            copy.wait_send()
        for copy in heads_col + others:
            copy.wait()
        for back in backs:
            back.end()

    dma = pltpu.SemaphoreType.DMA
    sds = jax.ShapeDtypeStruct
    vmem = pltpu.VMEM
    scratch = [
        vmem((n_ex, rows, width), BF),
        vmem((seq, 2 * DV), BF),
        vmem((2 * DV, width), F32),
        vmem((seq, 2 * DH), F32),
        vmem((seq, DV), F32),
        vmem((seq, wq.shape[1]), BF),
        vmem((seq, we.shape[1]), BF),
        vmem((seq, 2 * DR), F32),
        vmem((n_ex, rows, lat_cols), BF),
    ]
    scratch += [vmem((chips, rows, width), BF)] * 3 + [vmem((chips, rows, lat_cols), BF)] * 3
    scratch += [
        vmem((rows, width), F32),
        vmem((rows, lat_cols), F32),
        vmem((n_dev, r, head_cols), BF),
        vmem((hp, parts, r, width), BF),
        vmem((n_ex, n_dp * r, lat_cols), BF),
        vmem((chips, n_dp * r, lat_cols), BF),
        vmem((chips, n_dp * r, lat_cols), BF),
        vmem((chips, n_dp * r, lat_cols), BF),
        vmem((n_dp, r, lat_cols), BF),
        vmem((n_dp, r, lat_cols), BF),
        vmem((8, width), F32),
        vmem((n_ex, 8, width), F32),
        vmem((n_dp, 8, width), F32),
    ]
    scratch += [dma((chips,))] * 4 + [dma((6,))] + [dma((chips,))] * 8
    scratch += [dma((n_ex, n_dp))] * 2 + [dma((n_dp,))] * 2 + [dma((hp, parts)), dma((n_dp,))]
    scratch += [dma((chips,))] * 4 + [dma((n_dp,))] * 2 + [dma((3, n_dp))] * 2
    scratch += [dma((n_ex,))] * 2 + [dma((n_dp,))] * 2 + [dma((inner,))] * 2
    for total in totals:
        scratch += ExpertsBack.scratch(total, n_dp, inner)
    outs = pl.pallas_call(
        kernel,
        out_shape=[
            sds((rows, width), F32),
            sds((8, width), F32),
            sds((r, lat_cols), F32),
            sds((n_dp, n_ex, r, head_cols), BF),
            sds((n_dp, n_ex, r, head_cols), BF),
            sds((n_dp, r, width), BF),
            sds(out.shape, BF),
        ]
        + [sds(array.shape, BF) for array in shared]
        + [ExpertsBack.out(total, n_dp, inner) for total in totals],
        in_specs=[ANY] + [VMEM] * 21 + [ANY] * (4 + extra),
        out_specs=[VMEM] * 3 + [ANY] * (7 + extra),
        scratch_shapes=scratch,
        compiler_params=params(collective_id),
    )(grad, *attend, hidden, latent_low, *own, out, *shared, *totals)
    return outs[:3], outs[4], outs[5], outs[6], outs[7:10], outs[10:]


def shards(
    tokens,
    cotangent,
    lengths,
    routes,
    place_order,
    attn_gain,
    w_query,
    w_latent,
    latent_gain,
    w_expand,
    w_out,
    ffn_gain,
    w_router,
    shared_gate,
    shared_up,
    shared_down,
    expert_gate,
    expert_up,
    expert_down,
):
    rows, width = tokens.shape
    n_dp = lax.axis_size("dp")
    n_ex = lax.axis_size("expert")
    chips = n_ex // 2
    z = lax.axis_index("dp")
    e = lax.axis_index("expert")
    chip = e // 2
    n_experts = w_router.shape[1]
    top_k = routes.shape[1]
    capacity = (rows * top_k * 5 + 4 * n_experts - 1) // (4 * n_experts)
    cap = (capacity + 15) // 16 * 16
    seq = rows * n_ex
    r = w_query.shape[0]
    rl = w_expand.shape[0]
    hp = H // n_ex
    parts = DV // r
    heads = [
        (d * n_ex + (j // parts) * parts) * r // DV
        for j in range(n_ex)
        for d in range(j % parts * hp, j % parts * hp + hp)
    ]
    heads_back = [heads.index(h) for h in range(H)]
    inner = n_experts // chips
    my_local = lax.rem(z, inner)
    ff_e = expert_gate.shape[2]
    ff_s = shared_gate.shape[1] // inner
    lat = KVR + DR
    head_cols = hp * (DH + DR)
    kv_cols = hp * (DH + DV)

    def to_owner_order(values):
        cut = values.reshape(values.shape[0], n_dp, n_ex, r)
        return cut.transpose(0, 2, 1, 3).reshape(values.shape)

    def from_owner_order(values):
        cut = values.reshape(values.shape[0], n_ex, n_dp, r)
        return cut.transpose(0, 2, 1, 3).reshape(values.shape)

    def pick(values, index, axis=0):
        return lax.dynamic_index_in_dim(values, index, axis, keepdims=False)

    wq_send = jnp.take(w_query.reshape(r, H, DH + DR), jnp.array(heads), axis=1)
    wq_send = wq_send.reshape(r, n_ex, hp, DH + DR)
    wq_send = jnp.concatenate(
        [
            wq_send[..., :DH].reshape(r, n_ex, hp * DH),
            wq_send[..., DH:].reshape(r, n_ex, hp * DR),
        ],
        axis=-1,
    ).transpose(1, 0, 2)
    we_send = jnp.take(w_expand.reshape(rl, H, DH + DV), jnp.array(heads), axis=1)
    we_cols = rl * kv_cols // r
    we_send = we_send.reshape(rl, n_ex, r // rl, we_cols).transpose(1, 2, 0, 3)
    we_send = we_send.reshape(n_ex, r, we_cols)
    wa_send = jnp.concatenate([wq_send, we_send], axis=-1)
    slot_own = slot_places(routes, place_order[0], capacity)
    slot_place = jnp.where(slot_own >= 0, slot_own - routes * capacity, -1)
    slot_cols = 2 * rows * top_k // r
    slot_pack = jnp.stack([routes, slot_place]).astype(BF).reshape(2, r, slot_cols // 2)
    small_cols = lat + n_experts + 3
    pack_cols = (small_cols + slot_cols + 127) // 128 * 128
    pack = jnp.concatenate(
        [
            w_latent,
            w_router,
            attn_gain[:, None],
            ffn_gain[:, None],
            jnp.pad(latent_gain, (0, r - rl))[:, None],
            slot_pack[0],
            slot_pack[1],
            jnp.zeros((r, pack_cols - small_cols - slot_cols), BF),
        ],
        axis=1,
    )
    cot_owner = to_owner_order(cotangent)
    tok_all, wa_all, pk_all = first_exchange(tokens, wa_send, pack, n_dp, n_ex, 1)
    pk_flat = pk_all.reshape(width, pack_cols)
    w_lat = pk_flat[:, :lat]
    gain_one = pk_flat[:, lat + n_experts].astype(F32)
    gain_two = pk_all[..., lat + n_experts + 1].transpose(1, 0, 2).reshape(width).astype(F32)
    router = pk_all[..., lat : lat + n_experts].transpose(1, 0, 2, 3).reshape(width, n_experts)
    gain_lat = (
        pk_all[..., lat + n_experts + 2].reshape(n_dp * n_ex, r)[:, :rl].reshape(KVR).astype(F32)
    )
    slots_all = n_experts * capacity
    slot_col = pick(pk_all[..., small_cols : small_cols + slot_cols], e, 1)
    slot_col = lax.dynamic_slice_in_dim(slot_col, z - my_local, inner, 0).astype(jnp.int32)
    slot_col = slot_col.reshape(inner, r, 2, slot_cols // 2).transpose(2, 0, 1, 3)
    slot_col = slot_col.reshape(2, inner, rows, top_k)
    slot_ids = jnp.where(
        slot_col[1] >= 0,
        slot_col[0] * capacity + slot_col[1] + (jnp.arange(inner) * slots_all)[:, None, None],
        -1,
    ).reshape(inner * rows, top_k)
    place = jnp.arange(cap)
    far_experts = [lax.rem(chip + m, chips) * inner + my_local for m in range(chips)]
    wanted = (
        jnp.stack(far_experts)[:, None, None] * capacity
        + (jnp.arange(inner) * slots_all)[None, :, None]
        + place[None, None, :]
    )
    wanted = jnp.where(place[None, None, :] < capacity, wanted, -2).reshape(-1)
    n_slots = wanted.shape[0]
    per_far = n_slots // chips
    hot = sum((wanted[:, None] == slot_ids[None, :, j]).astype(BF) for j in range(top_k))
    hot_t = sum((slot_ids[:, j][:, None] == wanted[None, :]).astype(BF) for j in range(top_k))

    positions = jnp.arange(seq)
    lane = jnp.arange(2 * DR) % (DR // 2)
    angles = positions.astype(F32)[:, None] * (10000.0 ** (-(lane.astype(F32) * 2.0) / DR))[None, :]
    cos_wide, sine_wide = jnp.cos(angles), jnp.sin(angles)
    keep = (positions < lengths[0]).astype(F32)[None]
    attend_out, (wq, wexp, wo_rows), residual, x_col, cot_col, (wg,), shared_w = forward_exchange(
        [tok_all, gain_one[None], wa_all, pk_flat, gain_lat[None], cos_wide, sine_wide, keep],
        to_owner_order(w_out),
        to_owner_order(tokens),
        gain_two[None],
        cot_owner,
        [expert_gate.reshape(-1, n_ex, r, ff_e)],
        [w.reshape(r, inner, ff_s).transpose(1, 0, 2) for w in (shared_gate, shared_up, shared_down)],
        n_dp,
        n_ex,
        inner,
        2,
    )
    hidden_one, latent_raw, latent_low, qcat, kcat, value, lse, attended = attend_out
    wo_rows = wo_rows.reshape(hp * DV, width)
    cot_col = cot_col.reshape(inner * rows, width)
    hidden_two = pick(x_col, my_local)
    x_col = x_col.reshape(inner * rows, width)

    (x_in, grad_in), (wu, wd), shared_out, shared_dx, shared_grads = dispatch(
        hot,
        x_col,
        cot_col,
        [w.reshape(width, ff_s) for w in shared_w],
        [w.reshape(-1, n_ex, r, ff_e) for w in (expert_up, expert_down)],
        n_dp,
        n_ex,
        inner,
        8,
    )
    x_in = x_in.reshape(n_slots, width)
    grad_in = grad_in.reshape(n_slots, width)
    wg, wu, wd = (w.reshape(width, ff_e) for w in (wg, wu, wd))

    def probs_of(logits):
        top = jnp.max(logits, axis=-1, keepdims=True)
        exp_logits = jnp.exp(logits - top)
        return exp_logits / jnp.sum(exp_logits, axis=-1, keepdims=True)

    slot_probs = probs_of(mm(x_in, router))
    slot_gate = jnp.sum(
        jnp.where(jnp.arange(n_experts)[None, :] == far_experts[0], slot_probs, 0.0),
        axis=1,
        keepdims=True,
    )
    expert_a = mm(x_in, wg)
    expert_b = mm(x_in, wu)
    expert_hidden = swiglu(expert_a, expert_b).astype(BF)
    expert_rows = mm_cols(expert_hidden, wd).astype(BF)
    slot_dots = jnp.sum(grad_in.astype(F32) * expert_rows.astype(F32), axis=-1, keepdims=True)
    slot_dots = jnp.broadcast_to(slot_dots, (n_slots, 128)).astype(BF)
    slot_grad = (slot_gate * grad_in.astype(F32)).astype(BF)
    dx_back, dots_back, down_back, expert_totals = experts_back(
        [x_in, slot_grad, expert_a.astype(BF), expert_b.astype(BF), expert_hidden],
        [wg, wu, wd],
        slot_dots.reshape(chips, per_far, 128),
        n_dp,
        n_ex,
        inner,
        9,
    )
    dx_back = dx_back.reshape(n_slots, width)

    col_probs = probs_of(mm(x_col, router))
    expert_axis = jnp.arange(n_experts)[None, :]
    gates = [
        jnp.sum(jnp.where(expert_axis == expert, col_probs, 0.0), axis=1, keepdims=True)
        for expert in far_experts
    ]
    gate_hot = jnp.concatenate(
        [hot_t[:, m * per_far : (m + 1) * per_far] * gates[m].astype(BF) for m in range(chips)],
        axis=1,
    )
    dots = dots_back.reshape(n_slots, 128)[:, 0].astype(F32)[None] * hot_t.astype(F32)
    dots = jnp.sum(dots.reshape(inner * rows, chips, per_far), axis=-1)
    grad_probs_col = sum(
        jnp.where(expert_axis == far_experts[m], dots[:, m : m + 1], 0.0) for m in range(chips)
    )
    dx_col = mm(hot_t, dx_back) + shared_dx
    dx_send = jnp.concatenate(
        [dx_col, grad_probs_col, jnp.zeros((inner * rows, 128 - n_experts), F32)], axis=1
    ).astype(BF)
    dx_sum, shared_sums, rows_back, (gate_back,) = column_sum(
        dx_send.reshape(inner, rows, width + 128),
        expert_rows.reshape(chips, per_far, width),
        [grad.reshape(n_ex, n_dp, r, ff_s) for grad in shared_grads],
        expert_totals[:1],
        n_dp,
        n_ex,
        inner,
        3,
    )
    router_probs = lax.dynamic_slice_in_dim(col_probs, my_local * rows, rows, 0)
    grad_probs = dx_sum[:, width : width + n_experts]
    grad_logits = (
        router_probs * (grad_probs - jnp.sum(grad_probs * router_probs, axis=-1, keepdims=True))
    ).astype(BF)
    grad_router = mm_rows(hidden_two, grad_logits)
    grad_hidden_two = dx_sum[:, :width] + mm_cols(grad_logits, router)
    _, norm_two_back = jax.vjp(rms_norm, residual, gain_two)
    grad_resid_norm, grad_gain_two = norm_two_back(grad_hidden_two)
    grad_residual = cot_owner.astype(F32) + grad_resid_norm

    out_col = mm(gate_hot, rows_back.reshape(n_slots, width)) + shared_out
    latent_own = lax.dynamic_slice_in_dim(latent_raw, e * rows, rows, 0)
    router_back = jnp.pad(
        grad_router.reshape(n_ex, n_dp * r, n_experts),
        ((0, 0), (0, 0), (DR, DR - n_experts)),
    ).astype(BF)
    (grad_tokens, vec_sum, pack_sum), heads_got, wout_got, out_got, shared_got, (up_back,) = (
        backward_exchange(
            grad_residual.astype(BF),
            [wo_rows, wq, wexp, cos_wide, sine_wide, keep, qcat, kcat, value, lse, attended],
            hidden_one,
            latent_low,
            [
                pk_flat,
                latent_own,
                tokens,
                gain_one[None],
                gain_lat[None],
                from_owner_order(grad_residual),
                router_back,
                grad_gain_two[None],
            ],
            out_col.astype(BF).reshape(inner, rows, width),
            shared_sums,
            expert_totals[1:2],
            n_dp,
            n_ex,
            inner,
            5,
        )
    )

    def added(values):
        return jnp.sum(values.astype(F32), axis=0)

    out_tokens = from_owner_order((residual + added(out_got)).astype(BF))
    heads_all = added(heads_got)
    sum_wq = heads_all[..., :head_cols].transpose(1, 0, 2)
    sum_wq = jnp.concatenate(
        [
            sum_wq[..., : hp * DH].reshape(r, n_ex, hp, DH),
            sum_wq[..., hp * DH :].reshape(r, n_ex, hp, DR),
        ],
        axis=-1,
    ).reshape(r, H, DH + DR)
    sum_wq = jnp.take(sum_wq, jnp.array(heads_back), axis=1).reshape(r, H * (DH + DR))
    sum_we = heads_all[..., head_cols:].reshape(n_ex, r // rl, rl, we_cols).transpose(2, 0, 1, 3)
    sum_we = jnp.take(sum_we.reshape(rl, H, DH + DV), jnp.array(heads_back), axis=1)
    sum_we = sum_we.reshape(rl, H * (DH + DV))
    sum_wout = from_owner_order(added(wout_got))
    device = z * n_ex + e
    sum_gain_one = lax.dynamic_slice_in_dim(vec_sum[0], device * r, r, 0)
    sum_gain_two = lax.dynamic_slice_in_dim(vec_sum[1], (e * n_dp + z) * r, r, 0)
    sum_gain_lat = lax.dynamic_slice_in_dim(vec_sum[2], device * rl, rl, 0)
    sum_sgate, sum_sup, sum_sdown = (
        added(got.reshape(n_dp // inner, inner, r, ff_s)).transpose(1, 0, 2).reshape(r, -1)
        for got in shared_got
    )
    sum_egate, sum_eup, sum_edown = (
        added(back).reshape(-1, n_ex * r, ff_e) for back in (gate_back, up_back, down_back)
    )
    return (
        out_tokens,
        grad_tokens,
        sum_gain_one,
        sum_wq,
        pack_sum[:, :lat],
        sum_gain_lat,
        sum_we,
        sum_wout,
        sum_gain_two,
        pack_sum[:, lat : lat + n_experts],
        sum_sgate,
        sum_sup,
        sum_sdown,
        sum_egate,
        sum_eup,
        sum_edown,
    )


def solution(mesh):
    both = ("dp", "expert")
    in_specs = (
        P(both, None),
        P(both, None),
        P("dp"),
        P(both, None),
        P(both, None),
        P(both),
        P(both, None),
        P(both, None),
        P(both),
        P(both, None),
        P(both, None),
        P(both),
        P(both, None),
        P(both, None),
        P(both, None),
        P(both, None),
        P("expert", "dp", None),
        P("expert", "dp", None),
        P("expert", "dp", None),
    )
    out_specs = (
        P(both, None),
        P(both, None),
        P(both),
        P(both, None),
        P(both, None),
        P(both),
        P(both, None),
        P(both, None),
        P(both),
        P(both, None),
        P(both, None),
        P(both, None),
        P(both, None),
        P("expert", "dp", None),
        P("expert", "dp", None),
        P("expert", "dp", None),
    )
    return jax.shard_map(shards, mesh=mesh, in_specs=in_specs, out_specs=out_specs, check_vma=False)
```

```python
import jax
import jax.numpy as jnp
from jax import lax
from jax.experimental import pallas as pl
from jax.experimental.pallas import tpu as pltpu
from jax.sharding import PartitionSpec as P

H = 16
DH = 128
DR = 64
DV = 128
KVR = 512

norm_eps = 1e-06
masked_score = -1e30
MESH = pl.DeviceIdType.MESH
ANY = pl.BlockSpec(memory_space=pl.ANY)
VMEM = pl.BlockSpec(memory_space=pltpu.VMEM)
BF = jnp.bfloat16
F32 = jnp.float32


def rms_norm(values, scale_gain):
    return (
        values
        * lax.rsqrt(jnp.mean(values * values, axis=-1, keepdims=True) + norm_eps)
        * scale_gain
    )


def mm(left, right):
    return jnp.dot(left, right, preferred_element_type=F32)


def mm_rows(left, right):
    return lax.dot_general(left, right, (((0,), (0,)), ((), ())), preferred_element_type=F32)


def mm_cols(left, right):
    return lax.dot_general(left, right, (((1,), (1,)), ((), ())), preferred_element_type=F32)


def slot_places(route_rows, pair_order, capacity):
    pair_expert = route_rows.reshape(-1)
    earlier = pair_order[None, :] < pair_order[:, None]
    same_expert = pair_expert[None, :] == pair_expert[:, None]
    places = jnp.sum((earlier & same_expert).astype(jnp.int32), axis=1)
    slot_index = jnp.where(places < capacity, pair_expert * capacity + places, -1)
    return slot_index.reshape(route_rows.shape)


def turn(values, cos, sin, sign):
    half = DR // 2
    first = lax.rem(lax.broadcasted_iota(jnp.int32, values.shape, 1), DR) < half
    partner = jnp.where(
        first, -pltpu.roll(values, 2 * DR - half, 1), pltpu.roll(values, half, 1)
    )
    return values * cos + sign * (partner * sin)


def causal(i, tile, keep_ref):
    shape = (tile, (i + 1) * tile)
    query = lax.broadcasted_iota(jnp.int32, shape, 0) + i * tile
    key = lax.broadcasted_iota(jnp.int32, shape, 1)
    return (key <= query) & (keep_ref[:, : shape[1]] > 0.5)


def attend_forward(
    tok, gain, wq, wl, gain_lat, we, cos, sin, keep,
    hidden, latent, latent_low, qcat, kcat, value, lse, attended,
):
    per, rows, width = tok.shape
    seq = per * rows
    tile = 2 * rows
    scale = (DH + DR) ** (-0.5)

    def project(i, carry):
        at = pl.ds(pl.multiple_of(i * tile, tile), tile)
        x = tok[pl.ds(2 * i, 2)].reshape(tile, width).astype(F32)
        root = lax.rsqrt(jnp.mean(x * x, axis=-1, keepdims=True) + norm_eps)
        hid = (x * root * gain[...]).astype(BF)
        hidden[at, :] = hid
        c, s = cos[at, :], sin[at, :]
        query = mm(hid, wq[...])
        rope_q = turn(query[:, 2 * DH :], c, s, 1.0).astype(BF)
        lat = mm(hid, wl[...])
        latent[at, :] = lat
        plain = lat[:, :KVR]
        root = lax.rsqrt(jnp.mean(plain * plain, axis=-1, keepdims=True) + norm_eps)
        low = (plain * root * gain_lat[...]).astype(BF)
        latent_low[at, :] = low
        rope = lat[:, KVR : KVR + 2 * DR]
        lane = lax.broadcasted_iota(jnp.int32, rope.shape, 1)
        rope = jnp.where(lane < DR, rope, pltpu.roll(rope, DR, 1))
        rope = turn(rope, c, s, 1.0)
        expanded = mm(low, we[...]).astype(BF)
        for h in range(2):
            qcat[h, at, :DH] = query[:, h * DH : (h + 1) * DH].astype(BF)
            qcat[h, at, DH:] = rope_q
            mine = (lane < DR) if h == 0 else (lane >= DR)
            kcat[h, at, :DH] = expanded[:, h * (DH + DV) : h * (DH + DV) + DH]
            kcat[h, at, DH:] = jnp.where(mine, rope, 0.0).astype(BF)
            value[h, at, :] = expanded[:, h * (DH + DV) + DH : (h + 1) * (DH + DV)]
        return carry

    lax.fori_loop(0, seq // tile, project, 0)
    for h in range(2):
        for i in range(seq // tile):
            at, upto = slice(i * tile, (i + 1) * tile), slice(0, (i + 1) * tile)
            scores = mm_cols(qcat[h, at, :], kcat[h, upto, :]) * scale
            scores = jnp.where(causal(i, tile, keep), scores, masked_score)
            top = jnp.max(scores, axis=-1, keepdims=True)
            exp_scores = jnp.exp(scores - top)
            total = jnp.sum(exp_scores, axis=-1, keepdims=True)
            probs = (exp_scores / total).astype(BF)
            attended[at, h * DV : (h + 1) * DV] = mm(probs, value[h, upto, :]).astype(BF)
            lse[h, at, :] = jnp.broadcast_to(top + jnp.log(total), (tile, lse.shape[2]))


def attend_backward(
    grad, wo, wq, we, cos, sin, keep, qcat, kcat, value, lse, attended,
    gat, grad_wout, dk, dv, grad_query, grad_expanded, grad_rope,
):
    per, rows, width = grad.shape
    seq = per * rows
    tile = 2 * rows
    scale = (DH + DR) ** (-0.5)
    count = seq // tile
    grad_wout[...] = jnp.zeros_like(grad_wout)

    def project(i, carry):
        at = pl.ds(pl.multiple_of(i * tile, tile), tile)
        block = grad[pl.ds(2 * i, 2)].reshape(tile, width)
        gat[at, :] = mm_cols(block, wo[...]).astype(BF)
        grad_wout[...] += mm_rows(attended[at, :], block)
        return carry

    lax.fori_loop(0, count, project, 0)
    for h in range(2):
        dk[...] = jnp.zeros_like(dk)
        dv[...] = jnp.zeros_like(dv)
        for i in range(count):
            at, upto = slice(i * tile, (i + 1) * tile), slice(0, (i + 1) * tile)
            g = gat[at, h * DV : (h + 1) * DV]
            scores = mm_cols(qcat[h, at, :], kcat[h, upto, :]) * scale
            scores = jnp.where(causal(i, tile, keep), scores, masked_score)
            probs = jnp.exp(scores - lse[h, at, 0:1])
            grad_probs = mm_cols(g, value[h, upto, :])
            inner = jnp.sum(grad_probs * probs, axis=-1, keepdims=True)
            raw = (probs * (grad_probs - inner) * scale).astype(BF)
            grad_q = mm(raw, kcat[h, upto, :])
            grad_query[at, h * DH : (h + 1) * DH] = grad_q[:, :DH].astype(BF)
            rope = grad_q[:, DH:]
            lane = lax.broadcasted_iota(jnp.int32, rope.shape, 1)
            mine = (lane < DR) if h == 0 else (lane >= DR)
            rope = turn(rope, cos[at, :], sin[at, :], -1.0).astype(BF)
            if h == 0:
                grad_query[at, 2 * DH :] = rope
            else:
                grad_query[at, 2 * DH :] = jnp.where(mine, rope, grad_query[at, 2 * DH :])
            dk[upto, :] += mm_rows(raw, qcat[h, at, :])
            dv[upto, :] += mm_rows(probs.astype(BF), g)
        grad_expanded[:, h * (DH + DV) : h * (DH + DV) + DH] = dk[:, :DH].astype(BF)
        grad_expanded[:, h * (DH + DV) + DH : (h + 1) * (DH + DV)] = dv[...].astype(BF)
        rope = dk[:, DH:]
        if h == 0:
            grad_rope[...] = rope
        else:
            grad_rope[...] += pltpu.roll(rope, DR, 1)


def params(collective_id):
    return pltpu.CompilerParams(
        collective_id=collective_id, has_side_effects=True, vmem_limit_bytes=60 << 20
    )


def remote(src, dst, send_sem, recv_sem, device):
    return pltpu.make_async_remote_copy(
        src_ref=src,
        dst_ref=dst,
        send_sem=send_sem,
        recv_sem=recv_sem,
        device_id=device,
        device_id_type=MESH,
    )


def greet(devices):
    barrier = pltpu.get_barrier_semaphore()
    for device in devices:
        pl.semaphore_signal(barrier, inc=1, device_id=device, device_id_type=MESH)
    pl.semaphore_wait(barrier, len(devices))


def places(n_dp, n_ex):
    z = lax.axis_index("dp")
    e = lax.axis_index("expert")
    chips = n_ex // 2
    c, k = e // 2, lax.rem(e, 2)
    sibling = (z, e + 1 - 2 * k)
    same_core = [(z, lax.rem(c + i, chips) * 2 + k) for i in range(1, chips)]
    column = [(lax.rem(z + i, n_dp), e) for i in range(1, n_dp)]
    return z, e, c, k, sibling, same_core, column


def wait_recv(region, sem, device):
    remote(region, region, sem, sem, device).wait_recv()


def column_sum(array, rows_out, shared, totals, n_dp, n_ex, inner, collective_id):
    chips = n_ex // 2
    shape = array.shape[1:]
    extra = len(totals)
    _, _, r, ff_s = shared[0].shape

    def kernel(x_ref, *refs):
        s_in, r_ref, t_refs, refs = refs[:3], refs[3], refs[4 : 4 + extra], refs[4 + extra :]
        o_ref, s_out, r_out, back_refs = refs[0], refs[1:4], refs[4], refs[5 : 5 + extra]
        refs = refs[5 + extra :]
        buf, from_sib, out_buf, from_far = refs[:4]
        send, recv, near_s, near_r, far_s, far_r, r_s, r_r, local = refs[4:13]
        rest = refs[13:]
        z, e, c, k, sibling, same_core, column = places(n_dp, n_ex)
        group = column_group(z, e, inner)
        greet(same_core + [sibling] + column + [(d[0], sibling[1]) for d in column])
        backs = [
            ExpertsBack(t_refs[m], back_refs[m], rest[7 * m : 7 * m + 7], n_dp, n_ex, inner)
            for m in range(extra)
        ]
        copies, rows_back = [], []
        for i in range(1, inner):
            to = lax.rem(z + i, inner)
            copy = remote(x_ref.at[to], buf.at[i], send.at[i], recv.at[i], group[i])
            copy.start()
            copies.append(copy)
        near, far = {}, {}
        for i in list(range(1, chips)) + [0]:
            chip = lax.rem(c + i, chips)
            for m in range(3):
                near[i, m] = remote(
                    s_in[m].at[chip * 2 + 1 - k], from_sib.at[m, i],
                    near_s.at[m, i], near_r.at[m, i], sibling,
                )
                near[i, m].start()
        for back in backs:
            back.begin()
        for i in range(1, chips):
            copy = remote(
                r_ref.at[i], r_out.at[i], r_s.at[i], r_r.at[i], same_core[chips - i - 1]
            )
            copy.start()
            rows_back.append(copy)
        copy = pltpu.make_async_copy(r_ref.at[0], r_out.at[0], local)
        copy.start()
        rows_back.append(copy)

        def pair(i, m):
            chip = lax.rem(c + i, chips)
            near[i, m].wait_recv()

            def row(d, carry):
                out_buf[m, i, d] = (
                    s_in[m][chip * 2 + k, d].astype(F32) + from_sib[m, i, d].astype(F32)
                ).astype(BF)
                return carry

            lax.fori_loop(0, n_dp, row, 0)

        for i in range(1, chips):
            for m in range(3):
                pair(i, m)
                far[i, m] = remote(
                    out_buf.at[m, i], from_far.at[m, i], far_s.at[m, i], far_r.at[m, i],
                    same_core[i - 1],
                )
                far[i, m].start()
        o_ref[...] = x_ref[lax.rem(z, inner)].astype(F32)
        for back in backs:
            back.pass_on()
        for m in range(3):
            pair(0, m)
        for i in range(1, inner):
            copies[i - 1].wait_recv()
            o_ref[...] += buf[i].astype(F32)
        for m in range(3):
            for i in range(1, chips):
                far[i, m].wait_recv()

            def row(d, carry, m=m):
                total = out_buf[m, 0, d].astype(F32)
                for i in range(1, chips):
                    total = total + from_far[m, i, d].astype(F32)
                s_out[m][d] = total.astype(BF)
                return carry

            lax.fori_loop(0, n_dp, row, 0)
        for copy in copies + list(near.values()) + list(far.values()):
            copy.wait_send()
        for copy in rows_back:
            copy.wait()
        for back in backs:
            back.end()

    dma = pltpu.SemaphoreType.DMA
    scratch = [pltpu.VMEM((inner,) + shape, BF)]
    scratch += [pltpu.VMEM((3, chips, n_dp, r, ff_s), BF)] * 3
    scratch += [dma((inner,))] * 2 + [dma((3, chips))] * 4 + [dma((chips,))] * 2 + [dma]
    for total in totals:
        scratch += ExpertsBack.scratch(total, n_dp, inner)
    outs = pl.pallas_call(
        kernel,
        out_shape=[jax.ShapeDtypeStruct(shape, F32)]
        + [jax.ShapeDtypeStruct((n_dp, r, ff_s), BF)] * 3
        + [jax.ShapeDtypeStruct(rows_out.shape, BF)]
        + [ExpertsBack.out(total, n_dp, inner) for total in totals],
        in_specs=[VMEM] * 4 + [ANY] * (1 + extra),
        out_specs=[VMEM] * 4 + [ANY] * (1 + extra),
        scratch_shapes=scratch,
        compiler_params=params(collective_id),
    )(array, *shared, rows_out, *totals)
    return outs[0], outs[1:4], outs[4], outs[5:]


class Relay:
    @staticmethod
    def scratch(inner):
        dma = pltpu.SemaphoreType.DMA
        return [dma((inner,)), dma((inner,)), dma((inner,)), dma]

    def __init__(self, block, out, scratch, n_dp, n_ex, inner):
        self.block, self.out, self.inner = block, out, inner
        self.up_s, self.down_s, self.recv, self.local = scratch
        self.z, self.e, *_ = places(n_dp, n_ex)
        self.mine = lax.rem(self.z, inner)

    def copy(self, source, src, step):
        sem = self.up_s if step > 0 else self.down_s
        return remote(
            src, self.out.at[source], sem.at[source], self.recv.at[source], (self.z + step, self.e)
        )

    def keep(self):
        return pltpu.make_async_copy(self.block, self.out.at[self.mine], self.local)

    def begin(self):
        pl.when(self.mine < self.inner - 1)(lambda: self.copy(self.mine, self.block, 1).start())
        pl.when(self.mine > 0)(lambda: self.copy(self.mine, self.block, -1).start())
        self.keep().start()

    def pass_on(self):
        for t in range(1, self.inner):
            for step in (1, -1):
                source = self.mine - step * t
                exists = source >= 0 if step > 0 else source < self.inner
                more = self.mine < self.inner - 1 if step > 0 else self.mine > 0

                @pl.when(exists)
                def _(source=source, step=step):
                    self.copy(source, self.out.at[source], step).wait_recv()

                @pl.when(jnp.logical_and(exists, more))
                def _(source=source, step=step):
                    self.copy(source, self.out.at[source], step).start()

    def end(self):
        self.keep().wait()
        pl.when(self.mine < self.inner - 1)(
            lambda: self.copy(self.mine, self.block, 1).wait_send()
        )
        pl.when(self.mine > 0)(lambda: self.copy(self.mine, self.block, -1).wait_send())
        for t in range(1, self.inner):
            for step in (1, -1):
                source = self.mine - step * t
                exists = source >= 0 if step > 0 else source < self.inner
                more = self.mine < self.inner - 1 if step > 0 else self.mine > 0

                @pl.when(jnp.logical_and(exists, more))
                def _(source=source, step=step):
                    self.copy(source, self.out.at[source], step).wait_send()


def column_group(z, e, inner):
    start = z // inner * inner
    return [(start + lax.rem(z - start + i, inner), e) for i in range(inner)]


def first_exchange(tok, heads_w, pack, n_dp, n_ex, collective_id):
    chips = n_ex // 2

    def kernel(
        tok_ref, wa_ref, pk_ref, tok_out, wa_out, pk_out,
        t_send, t_recv, ts_send, ts_recv, a_send, a_recv, az_send, az_recv,
        p_send, p_recv, pf_send, pf_recv, ps_send, ps_recv, local,
    ):
        z, e, c, k, sibling, same_core, column = places(n_dp, n_ex)
        plane = [(z, lax.rem(e + i, n_ex)) for i in range(1, n_ex)]
        greet(plane + column)
        wa_far, pk_col, tok_far, near = [], [], [], []
        for i in range(1, n_ex):
            copy = remote(
                wa_ref.at[lax.rem(e + i, n_ex)], wa_out.at[z, e],
                a_send.at[i], a_recv.at[i], plane[i - 1],
            )
            copy.start()
            wa_far.append(copy)
        for i in range(1, n_dp):
            copy = remote(pk_ref, pk_out.at[z, e], p_send.at[i], p_recv.at[i], column[i - 1])
            copy.start()
            pk_col.append(copy)
        for i in range(1, chips):
            copy = remote(tok_ref, tok_out.at[e], t_send.at[i], t_recv.at[i], same_core[i - 1])
            copy.start()
            tok_far.append(copy)
        copy = remote(tok_ref, tok_out.at[e], ts_send.at[0], ts_recv.at[0], sibling)
        copy.start()
        near.append(copy)
        own = [
            pltpu.make_async_copy(wa_ref.at[e], wa_out.at[z, e], local.at[0]),
            pltpu.make_async_copy(pk_ref, pk_out.at[z, e], local.at[1]),
            pltpu.make_async_copy(tok_ref, tok_out.at[e], local.at[2]),
        ]
        for copy in own:
            copy.start()
        for copy in own:
            copy.wait()
        for copy in wa_far:
            copy.wait_recv()
        wa_col = []
        for i in range(1, n_dp):
            copy = remote(
                wa_out.at[z], wa_out.at[z], az_send.at[i], az_recv.at[i], column[i - 1]
            )
            copy.start()
            wa_col.append(copy)
        for copy in pk_col:
            copy.wait_recv()
        pk_far = []
        for i in range(1, chips):
            copy = remote(
                pk_out.at[:, e], pk_out.at[:, e], pf_send.at[i], pf_recv.at[i], same_core[i - 1]
            )
            copy.start()
            pk_far.append(copy)
        copy = remote(pk_out.at[:, e], pk_out.at[:, e], ps_send.at[0], ps_recv.at[0], sibling)
        copy.start()
        near.append(copy)
        for i in range(1, chips):
            source = lax.rem(c + chips - i, chips) * 2 + k
            tok_far[i - 1].wait_recv()
            copy = remote(
                tok_out.at[source], tok_out.at[source], ts_send.at[i], ts_recv.at[i], sibling
            )
            copy.start()
            near.append(copy)
            pk_far[i - 1].wait_recv()
            copy = remote(
                pk_out.at[:, source], pk_out.at[:, source], ps_send.at[i], ps_recv.at[i], sibling
            )
            copy.start()
            near.append(copy)
        for copy in near + wa_col:
            copy.wait()
        for copy in wa_far + pk_col + tok_far + pk_far:
            copy.wait_send()

    dma = pltpu.SemaphoreType.DMA
    return pl.pallas_call(
        kernel,
        out_shape=[
            jax.ShapeDtypeStruct((n_ex,) + tok.shape, tok.dtype),
            jax.ShapeDtypeStruct((n_dp,) + heads_w.shape, heads_w.dtype),
            jax.ShapeDtypeStruct((n_dp, n_ex) + pack.shape, pack.dtype),
        ],
        in_specs=[ANY] * 3,
        out_specs=[ANY] * 3,
        scratch_shapes=[dma((chips,))] * 4
        + [dma((n_ex,))] * 2
        + [dma((n_dp,))] * 4
        + [dma((chips,))] * 4
        + [dma((3,))],
        compiler_params=params(collective_id),
    )(tok, heads_w, pack)


class ExpertsIn:
    @staticmethod
    def scratch(n_dp):
        dma = pltpu.SemaphoreType.DMA
        return [dma((n_dp, 2)), dma((n_dp,)), dma((n_dp,)), dma((n_dp,))]

    @staticmethod
    def out(weight, n_dp, n_ex):
        return jax.ShapeDtypeStruct((n_ex, n_dp) + weight.shape[2:], BF)

    def __init__(self, weight, out, scratch, n_dp, n_ex, inner):
        self.weight, self.out, self.n_dp, self.inner = weight, out, n_dp, inner
        self.send, self.recv, self.sib_send, self.sib_recv = scratch
        self.z, self.e, self.c, self.k, self.sibling, _, _ = places(n_dp, n_ex)
        self.hh = n_ex // 2
        self.local = weight.shape[0]

    def sends(self, start):
        for i in list(range(1, self.n_dp)) + [0]:
            to = lax.rem(self.z + i, self.n_dp)
            expert = lax.rem(to, self.inner)

            def go(i=i, to=to, expert=expert):
                for h in range(2):
                    src = self.weight.at[lax.rem(expert, self.local), pl.ds(h * self.hh, self.hh)]
                    dst = self.out.at[pl.ds(h * self.hh, self.hh), self.z]
                    sem = self.recv.at[self.z]

                    def far(src=src, dst=dst, h=h):
                        copy = remote(src, dst, self.send.at[i, h], sem, (to, 2 * self.c + h))
                        if start:
                            copy.start()
                        else:
                            copy.wait_send()

                    if i:
                        far()
                    else:
                        pl.when(self.k != h)(far)
                        if start:

                            @pl.when(self.k == h)
                            def _(src=src, dst=dst):
                                pltpu.make_async_copy(src, dst, sem).start()

            pl.when(expert // self.local == self.k)(go)

    def begin(self):
        self.sends(True)

    def pass_on(self):
        mine = lax.rem(self.z, self.inner)
        for i in range(self.n_dp):
            d = lax.rem(self.z + self.n_dp - i, self.n_dp)
            region = self.out.at[pl.ds(self.k * self.hh, self.hh), d]
            if i:
                wait_recv(region, self.recv.at[d], self.sibling)
            else:
                from_here = mine // self.local == self.k

                @pl.when(from_here)
                def _(region=region, d=d):
                    src = self.weight.at[
                        lax.rem(mine, self.local), pl.ds(self.k * self.hh, self.hh)
                    ]
                    pltpu.make_async_copy(src, region, self.recv.at[d]).wait()

                @pl.when(jnp.logical_not(from_here))
                def _(region=region, d=d):
                    wait_recv(region, self.recv.at[d], self.sibling)

            remote(
                region, region, self.sib_send.at[i], self.sib_recv.at[i], self.sibling
            ).start()

    def end(self):
        self.sends(False)
        for i in range(self.n_dp):
            d = lax.rem(self.z + self.n_dp - i, self.n_dp)
            mine = self.out.at[pl.ds(self.k * self.hh, self.hh), d]
            remote(
                mine, mine, self.sib_send.at[i], self.sib_recv.at[i], self.sibling
            ).wait_send()
            region = self.out.at[pl.ds((1 - self.k) * self.hh, self.hh), d]
            wait_recv(region, self.sib_recv.at[i], self.sibling)


def forward_exchange(attend, w_out, tok, gain, cot, experts, shared, n_dp, n_ex, inner, collective_id):
    chips = n_ex // 2
    rows, width = tok.shape
    count = len(experts)
    r = w_out.shape[0]
    parts = DV // r
    hp = n_dp // parts
    seq = n_ex * rows
    rl = KVR // (n_dp * n_ex)
    we_cols = rl * hp * (DH + DV) // r
    wq_cols = hp * (DH + DR)

    def kernel(*refs):
        att_in, refs = refs[:8], refs[8:]
        wo_in, tok_ref, gain_ref, cot_in = refs[:4]
        e_in, s_in = refs[4 : 4 + count], refs[4 + count : 7 + count]
        refs = refs[7 + count :]
        att_out, refs = refs[:8], refs[8:]
        wq_ref, we_ref, wo_out, res_ref, xcol_ref, cot_out = refs[:6]
        w_out, s_out = refs[6 : 6 + count], refs[6 + count : 9 + count]
        refs = refs[9 + count :]
        x_ref, from_sib, out_buf, from_far, xbuf = refs[:5]
        (
            near_s, near_r, far_s, far_r,
            sh_s, sh_r, sp_s, sp_r, sf_s, sf_r, wo_s, wo_r, local,
        ) = refs[5:18]
        x_sems, co_sems, refs = refs[18:22], refs[22:26], refs[26:]
        z, e, c, k, sibling, same_core, column = places(n_dp, n_ex)
        part = lax.rem(e, parts)
        members = [
            (lax.rem(z + i, n_dp), e - part + lax.rem(part + j, parts))
            for i in range(n_dp)
            for j in range(parts)
        ]
        greet(same_core + column + [(device[0], sibling[1]) for device in column] + members[1:])

        def wo_sends(start):
            for i in range(n_dp):
                target = (lax.rem(z + i, n_dp), e - part + z // hp)
                dst, sem = wo_out.at[lax.rem(z, hp), part], wo_r.at[lax.rem(z, hp), part]

                def far(i=i, target=target, dst=dst, sem=sem):
                    copy = remote(wo_in, dst, wo_s.at[i], sem, target)
                    if start:
                        copy.start()
                    else:
                        copy.wait_send()

                if i:
                    far()
                else:
                    pl.when(z // hp != part)(far)
                    if start:

                        @pl.when(z // hp == part)
                        def _(dst=dst, sem=sem):
                            pltpu.make_async_copy(wo_in, dst, sem).start()

        def wo_arrivals():
            for h in range(hp):
                for p in range(parts):
                    here = jnp.logical_and(part * hp + h == z, part == p)

                    @pl.when(here)
                    def _(h=h, p=p):
                        pltpu.make_async_copy(wo_in, wo_out.at[h, p], wo_r.at[h, p]).wait()

                    @pl.when(jnp.logical_not(here))
                    def _(h=h, p=p):
                        wait_recv(wo_out.at[h, p], wo_r.at[h, p], sibling)

        my_l = lax.rem(z, inner)
        matrices = [
            ExpertsIn(e_in[m], w_out[m], refs[4 * m : 4 * m + 4], n_dp, n_ex, inner)
            for m in range(count)
        ]
        wo_sends(True)
        shared_copies = []
        for i in range(1, n_dp):
            for m in range(3):
                copy = remote(
                    s_in[m].at[lax.rem(lax.rem(z + i, n_dp), inner)], s_out[m].at[e, z],
                    sh_s.at[m, i], sh_r.at[m, i], column[i - 1],
                )
                copy.start()
                shared_copies.append(copy)
        own = [
            pltpu.make_async_copy(s_in[m].at[my_l], s_out[m].at[e, z], local.at[m])
            for m in range(3)
        ]
        for copy in own:
            copy.start()
        matrices[0].begin()
        tok_all, gain_one, wa_ref, wl_ref, gain_lat, cos, sin, keep = att_in
        wq_ref[...] = wa_ref[:, :, :, :wq_cols].reshape(width, wq_cols)
        for j in range(r // rl):
            block = wa_ref[:, :, j * rl : (j + 1) * rl, wq_cols:].reshape(KVR, we_cols)
            we_ref[:, j * we_cols : (j + 1) * we_cols] = block
        attend_forward(
            tok_all, gain_one, wq_ref, wl_ref, gain_lat, we_ref, cos, sin, keep, *att_out
        )
        wo_arrivals()
        wo = wo_out[...].reshape(hp * DV, width)

        def project(i, carry):
            at = pl.ds(pl.multiple_of(i * 2 * rows, 2 * rows), 2 * rows)
            block = mm(att_out[7][at, :], wo).astype(BF)
            x_ref[pl.ds(2 * i, 2)] = block.reshape(2, rows, width)
            return carry

        lax.fori_loop(0, chips, project, 0)
        near = []
        for i in list(range(1, chips)) + [0]:
            chip = lax.rem(c + i, chips)
            copy = remote(
                x_ref.at[chip * 2 + 1 - k], from_sib.at[chip], near_s.at[i], near_r.at[i], sibling
            )
            copy.start()
            near.append(copy)
        far = []
        for i in range(1, chips):
            chip = lax.rem(c + i, chips)
            near[i - 1].wait_recv()
            out_buf[i] = (
                x_ref[chip * 2 + k].astype(F32) + from_sib[chip].astype(F32)
            ).astype(BF)
            copy = remote(out_buf.at[i], from_far.at[i], far_s.at[i], far_r.at[i], same_core[i - 1])
            copy.start()
            far.append(copy)
        near[chips - 1].wait_recv()
        res_ref[...] = x_ref[e].astype(F32) + from_sib[c].astype(F32) + tok_ref[...].astype(F32)
        for i in range(1, chips):
            far[i - 1].wait_recv()
            res_ref[...] += from_far[i].astype(F32)
        residual = res_ref[...]
        scale = lax.rsqrt(jnp.mean(residual * residual, axis=-1, keepdims=True) + norm_eps)
        xbuf[...] = (residual * scale * gain_ref[...]).astype(BF)
        relays = [
            Relay(xbuf, xcol_ref, x_sems, n_dp, n_ex, inner),
            Relay(cot_in, cot_out, co_sems, n_dp, n_ex, inner),
        ]
        relays[0].begin()
        relays[0].pass_on()
        relays[1].begin()
        for matrix in matrices[1:]:
            matrix.begin()
        for copy in own:
            copy.wait()
        for copy in shared_copies:
            copy.wait_recv()
        plane, to_sib = [], []
        for m in range(3):
            block = s_out[m].at[e]
            for i in range(1, chips):
                copy = remote(block, block, sp_s.at[m, i], sp_r.at[m, i], same_core[i - 1])
                copy.start()
                plane.append(copy)
            copy = remote(block, block, sf_s.at[m, 0], sf_r.at[m, 0], sibling)
            copy.start()
            to_sib.append(copy)
        for m in range(3):
            for i in range(1, chips):
                plane[m * (chips - 1) + i - 1].wait_recv()
                block = s_out[m].at[lax.rem(c + chips - i, chips) * 2 + k]
                copy = remote(block, block, sf_s.at[m, i], sf_r.at[m, i], sibling)
                copy.start()
                to_sib.append(copy)
        relays[1].pass_on()
        for matrix in matrices:
            matrix.pass_on()
        for copy in to_sib:
            copy.wait()
        for relay in relays:
            relay.end()
        for copy in plane + shared_copies + near + far:
            copy.wait_send()
        wo_sends(False)
        for matrix in matrices:
            matrix.end()

    dma = pltpu.SemaphoreType.DMA
    ff_s = shared[0].shape[2]
    scratch = []
    for _ in experts:
        scratch += ExpertsIn.scratch(n_dp)
    sds = jax.ShapeDtypeStruct
    outs = pl.pallas_call(
        kernel,
        out_shape=[
            sds((seq, width), BF),
            sds((seq, attend[3].shape[1]), F32),
            sds((seq, KVR), BF),
            sds((2, seq, 2 * DH), BF),
            sds((2, seq, 2 * DH), BF),
            sds((2, seq, DV), BF),
            sds((2, seq, 128), F32),
            sds((seq, 2 * DV), BF),
            sds((width, wq_cols), BF),
            sds((KVR, hp * (DH + DV)), BF),
            sds((hp, parts, r, width), BF),
            sds((rows, width), F32),
            sds((inner, rows, width), BF),
            sds((inner, rows, width), BF),
        ]
        + [ExpertsIn.out(w, n_dp, n_ex) for w in experts]
        + [sds((n_ex, n_dp, r, ff_s), BF)] * 3,
        in_specs=[VMEM] * 8 + [ANY] + [VMEM] * 2 + [ANY] * (4 + count),
        out_specs=[VMEM] * 12 + [ANY] * (5 + count),
        scratch_shapes=[pltpu.VMEM((n_ex, rows, width), BF)]
        + [pltpu.VMEM((chips, rows, width), BF)] * 3
        + [pltpu.VMEM((rows, width), BF)]
        + [dma((chips,))] * 4
        + [dma((3, n_dp))] * 2
        + [dma((3, chips))] * 4
        + [dma((n_dp,)), dma((hp, parts)), dma((3,))]
        + Relay.scratch(inner) * 2
        + scratch,
        compiler_params=params(collective_id),
    )(*attend, w_out, tok, gain, cot, *experts, *shared)
    return outs[:8], outs[8:11], outs[11], outs[12], outs[13], outs[14 : 14 + count], outs[14 + count :]


def silu_parts(a):
    sig = 1.0 / (1.0 + jnp.exp(-a))
    return a * sig, sig * (1.0 + a * (1.0 - sig))


def dispatch(hot, x, cot, shared, weights, n_dp, n_ex, inner, collective_id):
    chips = n_ex // 2
    rows, width = x.shape
    ff = shared[0].shape[1]
    tile = 256

    per_far = hot.shape[0] // chips
    count = len(weights)

    def kernel(hot_ref, x_hbm, c_hbm, g_hbm, u_hbm, d_hbm, *refs):
        w_in, refs = refs[:count], refs[count:]
        o_ref, go_ref, w_out, refs = refs[0], refs[1], refs[2 : 2 + count], refs[2 + count :]
        out_ref, dx_ref, gg_ref, gu_ref, gd_ref = refs[:5]
        hot_v, x_v, c_v, g_v, u_v, d_v, hid, ga, gb, b_v, send, recv, loads, keep = refs[5:19]
        rest = refs[19:]
        z, e, c, k, sibling, same_core, column = places(n_dp, n_ex)
        moves = [
            pltpu.make_async_copy(src, dst, loads.at[j])
            for j, (src, dst) in enumerate(
                [
                    (hot_ref, hot_v), (x_hbm, x_v), (c_hbm, c_v),
                    (g_hbm, g_v), (u_hbm, u_v), (d_hbm, d_v),
                ]
            )
        ]
        for copy in moves:
            copy.start()
        greet(same_core + [sibling] + column + [(device[0], sibling[1]) for device in column])
        matrices = [
            ExpertsIn(w_in[m], w_out[m], rest[4 * m : 4 * m + 4], n_dp, n_ex, inner)
            for m in range(count)
        ]
        for matrix in matrices:
            matrix.begin()
        copies = []
        for j, (source, target) in enumerate(((x_v, o_ref), (c_v, go_ref))):
            if not j:
                moves[0].wait()
            moves[1 + j].wait()
            for i in list(range(1, chips)) + [0]:
                block = mm(hot_v[i * per_far : (i + 1) * per_far, :], source[...])
                b_v[j, i] = block.astype(BF)
                if i:
                    copy = remote(
                        b_v.at[j, i], target.at[i], send.at[j, i], recv.at[j, i],
                        same_core[i - 1],
                    )
                else:
                    copy = pltpu.make_async_copy(b_v.at[j, 0], target.at[0], keep.at[j])
                copy.start()
                copies.append(copy)
        for copy in moves[3:]:
            copy.wait()

        def rows_of(i, carry):
            at = pl.ds(pl.multiple_of(i * tile, tile), tile)
            first = mm(x_v[at, :], g_v[...])
            second = mm(x_v[at, :], u_v[...])
            silu, slope = silu_parts(first)
            low = (silu * second).astype(BF)
            hid[at, :] = low
            out_ref[at, :] = mm_cols(low, d_v[...])
            back = mm(c_v[at, :], d_v[...])
            low_a = (back * second * slope).astype(BF)
            low_b = (back * silu).astype(BF)
            ga[at, :] = low_a
            gb[at, :] = low_b
            dx_ref[at, :] = mm_cols(low_a, g_v[...]) + mm_cols(low_b, u_v[...])
            return carry

        lax.fori_loop(0, rows // tile, rows_of, 0)

        def columns_of(j, carry):
            at = pl.ds(pl.multiple_of(j * tile, tile), tile)
            gg_ref[at, :] = mm_rows(x_v[:, at], ga[...]).astype(BF)
            gu_ref[at, :] = mm_rows(x_v[:, at], gb[...]).astype(BF)
            gd_ref[at, :] = mm_rows(c_v[:, at], hid[...]).astype(BF)
            return carry

        lax.fori_loop(0, width // tile, columns_of, 0)
        for matrix in matrices:
            matrix.pass_on()
        for copy in copies:
            copy.wait()
        for matrix in matrices:
            matrix.end()

    dma = pltpu.SemaphoreType.DMA
    sds = jax.ShapeDtypeStruct
    vmem = pltpu.VMEM
    scratch = []
    for _ in weights:
        scratch += ExpertsIn.scratch(n_dp)
    outs = pl.pallas_call(
        kernel,
        out_shape=[sds((chips, per_far, width), BF)] * 2
        + [ExpertsIn.out(weight, n_dp, n_ex) for weight in weights]
        + [sds((rows, width), F32)] * 2
        + [sds((width, ff), BF)] * 3,
        in_specs=[ANY] * (6 + count),
        out_specs=[ANY] * (2 + count) + [VMEM] * 5,
        scratch_shapes=[vmem(hot.shape, BF)]
        + [vmem((rows, width), BF)] * 2
        + [vmem((width, ff), BF)] * 3
        + [vmem((rows, ff), BF)] * 3
        + [vmem((2, chips, per_far, width), BF)]
        + [dma((2, chips)), dma((2, chips)), dma((6,)), dma((2,))]
        + scratch,
        compiler_params=params(collective_id),
    )(hot, x, cot, *shared, *weights)
    return outs[:2], outs[2 : 2 + count], outs[2 + count], outs[3 + count], outs[4 + count :]


def experts_run(x_in, grad_in, weights, router, n_dp, n_ex, inner, collective_id):
    chips = n_ex // 2
    n_slots, width = x_in.shape
    ff = weights[0].shape[1]
    per_far = n_slots // chips
    r = width // (n_dp * n_ex)
    tile = per_far
    span = n_dp * r
    n_experts = inner * chips

    def kernel(*refs):
        in_hbm, refs = refs[:6], refs[6:]
        dx_out, dots_out, rows_out, back_out, g_out, refs = *refs[:4], refs[4:6], refs[6:]
        x_v, s_v, wg, wu, wd, route, a_v, b_v, h_v, dx_v, total, stage, dots_v = refs[:13]
        loads, send, recv, d_send, d_recv, local, rows_sem, out_sem = refs[13:21]
        z, e, c, k, sibling, same_core, column = places(n_dp, n_ex)
        moves = [
            pltpu.make_async_copy(src, dst, loads.at[j])
            for j, (src, dst) in enumerate(zip(in_hbm, (x_v, s_v, wg, wu, wd, route)))
        ]
        for j in (5, 0, 2, 3, 4, 1):
            moves[j].start()
        greet(same_core + [sibling] + column + [(device[0], sibling[1]) for device in column])
        back = ExpertsBack(total, back_out, refs[21:], n_dp, n_ex, inner)
        expert = c * inner + lax.rem(z, inner)
        for j in (5, 0, 2, 3, 4, 1):
            moves[j].wait()

        def forward(i, carry):
            at = pl.ds(pl.multiple_of(i * tile, tile), tile)
            x = x_v[at, :]
            logits = mm(x, route[...])
            lane = lax.broadcasted_iota(jnp.int32, logits.shape, 1)
            logits = jnp.where(lane < n_experts, logits, masked_score)
            chances = jnp.exp(logits - jnp.max(logits, axis=-1, keepdims=True))
            gate = jnp.sum(jnp.where(lane == expert, chances, 0.0), axis=-1, keepdims=True)
            gate = gate / jnp.sum(chances, axis=-1, keepdims=True)
            first = mm(x, wg[...])
            second = mm(x, wu[...])
            a_v[at, :] = first.astype(BF)
            b_v[at, :] = second.astype(BF)
            hid = (silu_parts(first)[0] * second).astype(BF)
            h_v[at, :] = hid
            rows = mm_cols(hid, wd[...]).astype(BF)
            dx_v[i] = rows
            grad = s_v[at, :].astype(F32)
            dots = jnp.sum(grad * rows.astype(F32), axis=-1, keepdims=True)
            dots_v[i] = jnp.broadcast_to(dots, (tile, 128)).astype(BF)
            s_v[at, :] = (gate * grad).astype(BF)
            pltpu.make_async_copy(dx_v.at[i], rows_out.at[i], rows_sem.at[i]).start()
            return carry

        lax.fori_loop(0, chips, forward, 0)
        dot_copies = []
        for i in range(1, chips):
            copy = remote(
                dots_v.at[i], dots_out.at[i], d_send.at[i], d_recv.at[i], same_core[chips - i - 1]
            )
            copy.start()
            dot_copies.append(copy)
        copy = pltpu.make_async_copy(dots_v.at[0], dots_out.at[0], local.at[0])
        copy.start()
        dot_copies.append(copy)

        def down_rows(t, carry):
            j = lax.rem(t + (1 - k) * (n_ex // 2), n_ex)
            at = pl.ds(pl.multiple_of(j * span, span), span)
            block = mm_rows(s_v[:, at], h_v[...]).astype(BF)
            total[j] = block.reshape(n_dp, r, ff)
            return carry

        lax.fori_loop(0, n_ex, down_rows, 0)
        back.begin()

        def hidden_rows(i, carry):
            at = pl.ds(pl.multiple_of(i * tile, tile), tile)
            grad = mm(s_v[at, :], wd[...])
            silu, slope = silu_parts(a_v[at, :].astype(F32))
            second = b_v[at, :].astype(F32)
            a_v[at, :] = (grad * second * slope).astype(BF)
            b_v[at, :] = (grad * silu).astype(BF)
            return carry

        lax.fori_loop(0, chips, hidden_rows, 0)
        back.pass_on()
        copies = []
        for i in list(range(1, chips)) + [0]:
            at = slice(i * per_far, (i + 1) * per_far)
            block = mm_cols(a_v[at, :], wg[...]) + mm_cols(b_v[at, :], wu[...])
            pltpu.make_async_copy(dx_v.at[i], rows_out.at[i], rows_sem.at[i]).wait()
            dx_v[i] = block.astype(BF)
            if i:
                copy = remote(
                    dx_v.at[i], dx_out.at[i], send.at[i], recv.at[i], same_core[chips - i - 1]
                )
            else:
                copy = pltpu.make_async_copy(dx_v.at[0], dx_out.at[0], local.at[1])
            copy.start()
            copies.append(copy)

        def other_rows(j, carry):
            at = pl.ds(pl.multiple_of(j * span, span), span)
            for m, side in enumerate((a_v, b_v)):

                @pl.when(j > 0)
                def _(m=m):
                    pltpu.make_async_copy(stage.at[m], g_out[m].at[j - 1], out_sem.at[m]).wait()

                block = mm_rows(x_v[:, at], side[...]).astype(BF)
                stage[m] = block.reshape(n_dp, r, ff)
                pltpu.make_async_copy(stage.at[m], g_out[m].at[j], out_sem.at[m]).start()
            return carry

        lax.fori_loop(0, n_ex, other_rows, 0)
        for m in range(2):
            pltpu.make_async_copy(stage.at[m], g_out[m].at[n_ex - 1], out_sem.at[m]).wait()
        for copy in copies + dot_copies:
            copy.wait()
        back.end()

    dma = pltpu.SemaphoreType.DMA
    sds = jax.ShapeDtypeStruct
    vmem = pltpu.VMEM
    total = sds((n_ex, n_dp, r, ff), BF)
    blocks = sds((chips, per_far, width), BF)
    dots = sds((chips, per_far, 128), BF)
    outs = pl.pallas_call(
        kernel,
        out_shape=[blocks, dots, blocks, ExpertsBack.out(total, n_dp, inner), total, total],
        in_specs=[ANY] * 6,
        out_specs=[ANY] * 6,
        scratch_shapes=[vmem((n_slots, width), BF)] * 2
        + [vmem((width, ff), BF)] * 3
        + [vmem((width, 128), BF)]
        + [vmem((n_slots, ff), BF)] * 3
        + [
            vmem(blocks.shape, BF),
            vmem(total.shape, BF),
            vmem((2, n_dp, r, ff), BF),
            vmem(dots.shape, BF),
            dma((6,)),
        ]
        + [dma((chips,))] * 4
        + [dma((2,)), dma((chips,)), dma((2,))]
        + ExpertsBack.scratch(total, n_dp, inner),
        compiler_params=params(collective_id),
    )(x_in, grad_in, *weights, router)
    return outs[0], outs[1], outs[2], outs[3], outs[4:]


class ExpertsBack:
    @staticmethod
    def scratch(total, n_dp, inner):
        n_ex, _, r, ff = total.shape
        dma = pltpu.SemaphoreType.DMA
        hh = n_ex // 2
        return [
            pltpu.VMEM((hh, n_dp, r, ff), BF),
            pltpu.VMEM((hh, n_dp, r, ff), BF),
            dma((hh,)),
            dma((hh,)),
            dma((hh,)),
            dma((hh, n_dp)),
            dma((n_dp // inner, 2, 2, hh)),
        ]

    @staticmethod
    def out(total, n_dp, inner):
        n_ex, _, r, ff = total.shape
        return jax.ShapeDtypeStruct((n_dp // inner, 2, n_ex, r, ff), BF)

    def __init__(self, total, out, scratch, n_dp, n_ex, inner):
        self.total, self.out, self.n_dp, self.inner = total, out, n_dp, inner
        self.own, self.sib, self.near_s, self.near_r, self.load, self.send, self.recv = scratch
        self.z, self.e, self.c, self.k, self.sibling, _, _ = places(n_dp, n_ex)
        self.hh = n_ex // 2

    def near(self, j):
        return remote(
            self.total.at[(1 - self.k) * self.hh + j], self.sib.at[j],
            self.near_s.at[j], self.near_r.at[j], self.sibling,
        )

    def loads(self, j):
        return pltpu.make_async_copy(
            self.total.at[self.k * self.hh + j], self.own.at[j], self.load.at[j]
        )

    def begin(self):
        for j in range(self.hh):
            self.near(j).start()
            self.loads(j).start()

    def route(self, j, i):
        d = lax.rem(self.z + i, self.n_dp)
        expert = lax.rem(self.z, self.inner)
        o = self.z // self.inner
        dst = self.out.at[o, lax.rem(expert, 2), self.k * self.hh + j]
        sem = self.recv.at[o, lax.rem(expert, 2), self.k, j]
        return self.own.at[j, d], dst, sem, (d, 2 * self.c + expert // 2)

    def stay(self, j):
        src, dst, sem, _ = self.route(j, 0)
        return pltpu.make_async_copy(src, dst, sem)

    def go(self, j, i):
        src, dst, sem, device = self.route(j, i)
        return remote(src, dst, self.send.at[j, i], sem, device)

    def here(self):
        return lax.rem(self.z, self.inner) // 2 == self.k

    def pass_on(self):
        for j in range(self.hh):
            self.near(j).wait_recv()
            self.loads(j).wait()
            for d in range(self.n_dp):
                self.own[j, d] = (
                    self.own[j, d].astype(F32) + self.sib[j, d].astype(F32)
                ).astype(BF)
            for i in range(1, self.n_dp):
                self.go(j, i).start()
            pl.when(self.here())(lambda j=j: self.stay(j).start())
            pl.when(jnp.logical_not(self.here()))(lambda j=j: self.go(j, 0).start())

    def end(self):
        for j in range(self.hh):
            self.near(j).wait_send()
            for i in range(1, self.n_dp):
                self.go(j, i).wait_send()
            pl.when(jnp.logical_not(self.here()))(lambda j=j: self.go(j, 0).wait_send())
        for o in range(self.n_dp // self.inner):
            for i in range(2):
                for h in range(2):
                    source = o * self.inner + 2 * self.k + i
                    here = jnp.logical_and(source == self.z, self.k == h)
                    for j in range(self.hh):
                        region = self.out.at[o, i, h * self.hh + j]
                        sem = self.recv.at[o, i, h, j]

                        @pl.when(here)
                        def _(region=region, sem=sem, j=j):
                            pltpu.make_async_copy(self.own.at[j, self.z], region, sem).wait()

                        @pl.when(jnp.logical_not(here))
                        def _(region=region, sem=sem):
                            wait_recv(region, sem, self.sibling)


def rms_back(x, gain, grad):
    root = lax.rsqrt(jnp.mean(x * x, axis=-1, keepdims=True) + norm_eps)
    scaled = grad * gain
    along = jnp.mean(x * scaled, axis=-1, keepdims=True)
    return root * scaled - x * (root * root * root) * along, grad * x * root


def backward_exchange(
    grad, attend, hidden, latent_low, own, out, shared, totals, n_dp, n_ex, inner, collective_id
):
    chips = n_ex // 2
    rows, width = grad.shape
    seq = n_ex * rows
    extra = len(totals)
    wq, we = attend[1], attend[2]
    lat_cols = KVR + 2 * DR
    r = width // (n_dp * n_ex)
    rl = KVR // (n_dp * n_ex)
    parts = DV // r
    hp = n_dp // parts
    n_dev = n_dp * n_ex
    wq_cols = wq.shape[1]
    we_cols = rl * we.shape[1] // r
    head_cols = wq_cols + we_cols

    def kernel(*refs):
        grad_ref, att_in, refs = refs[0], refs[1:12], refs[12:]
        hidden_ref, low_ref, refs = refs[0], refs[1], refs[2:]
        wl_ref, lat_ref, tok_ref, gain_ref, glat_ref, gnat_ref, router_ref, gtwo_ref = refs[:8]
        out_ref, sh_in, refs = refs[8], refs[9:12], refs[12:]
        t_refs, refs = refs[:extra], refs[extra:]
        tok_out, vec_out, pack_out, heads_mid, heads_out, wout_out, out_got = refs[:7]
        sh_out, back_refs, refs = refs[7:10], refs[10 : 10 + extra], refs[10 + extra :]
        gbuf, att_tmp, refs = refs[0], refs[1:8], refs[8:]
        part_l, bufs, sums, refs = refs[0], refs[1:7], refs[7:9], refs[9:]
        hsrc, wsrc, pack, psib, pout, pfar, psum, pbuf, vec, vbuf, vzbuf = refs[:11]
        refs = refs[11:]
        t_s, t_r, ts_s, ts_r, local = refs[:5]
        sems, refs = refs[5:13], refs[13:]
        (
            h_s, h_r, hz_s, hz_r, w_s, w_r, pn_s, pn_r, pf_s, pf_r, pc_s, pc_r, s_s, s_r,
            v_s, v_r, vz_s, vz_r, o_s, o_r,
        ) = refs[:20]
        rest = refs[20:]
        x_refs = (gbuf, part_l)
        group = column_group(lax.axis_index("dp"), lax.axis_index("expert"), inner)
        z, e, c, k, sibling, same_core, column = places(n_dp, n_ex)
        plane = [(z, lax.rem(e + i, n_ex)) for i in range(1, n_ex)]
        part = lax.rem(e, parts)
        members = [
            (lax.rem(z + i, n_dp), e - part + lax.rem(part + j, parts))
            for i in range(n_dp)
            for j in range(parts)
        ]
        greet(plane + column + [(d[0], sibling[1]) for d in column] + members[1:])
        backs = [
            ExpertsBack(t_refs[m], back_refs[m], rest[7 * m : 7 * m + 7], n_dp, n_ex, inner)
            for m in range(extra)
        ]
        gather, to_sib, others = [], [], []
        for i in range(1, chips):
            copy = remote(grad_ref, gbuf.at[e], t_s.at[i], t_r.at[i], same_core[i - 1])
            copy.start()
            gather.append(copy)
        copy = remote(grad_ref, gbuf.at[e], ts_s.at[0], ts_r.at[0], sibling)
        copy.start()
        to_sib.append(copy)
        keep = pltpu.make_async_copy(grad_ref, gbuf.at[e], local.at[0])
        keep.start()
        for back in backs:
            back.begin()
        for m in range(3):
            for i in range(1, n_dp):
                copy = remote(
                    sh_in[m].at[lax.rem(z + i, n_dp)], sh_out[m].at[z],
                    s_s.at[m, i], s_r.at[m, i], column[i - 1],
                )
                copy.start()
                others.append(copy)
            copy = pltpu.make_async_copy(sh_in[m].at[z], sh_out[m].at[z], local.at[1 + m])
            copy.start()
            others.append(copy)
        mine = lax.rem(z, inner)
        for i in range(1, inner):
            copy = remote(
                out_ref.at[lax.rem(mine + i, inner)], out_got.at[mine], o_s.at[i], o_r.at[i],
                group[i],
            )
            copy.start()
            others.append(copy)
        copy = pltpu.make_async_copy(out_ref.at[mine], out_got.at[mine], local.at[5])
        copy.start()
        others.append(copy)
        for i in range(1, chips):
            gather[i - 1].wait_recv()
            block = gbuf.at[lax.rem(c + chips - i, chips) * 2 + k]
            copy = remote(block, block, ts_s.at[i], ts_r.at[i], sibling)
            copy.start()
            to_sib.append(copy)
        for back in backs:
            back.pass_on()
        keep.wait()
        for copy in to_sib:
            copy.wait_recv()
        for copy in gather + to_sib:
            copy.wait_send()
        gat, grad_wout, dk, dv, grad_query, grad_expanded, grad_rope = att_tmp
        attend_backward(gbuf, *att_in, *att_tmp)

        wsrc[...] = grad_wout[...].astype(BF).reshape(hp, parts, r, width)

        def wout_sends(start):
            for h in range(hp):
                for p in range(parts):
                    target = (part * hp + h, e - part + p)
                    here = jnp.logical_and(part * hp + h == z, p == part)

                    def far(h=h, p=p, target=target):
                        copy = remote(
                            wsrc.at[h, p], wout_out.at[z], w_s.at[h, p], w_r.at[z], target
                        )
                        if start:
                            copy.start()
                        else:
                            copy.wait_send()

                    pl.when(jnp.logical_not(here))(far)
                    if start:

                        @pl.when(here)
                        def _(h=h, p=p):
                            pltpu.make_async_copy(
                                wsrc.at[h, p], wout_out.at[z], w_r.at[z]
                            ).start()

        wout_sends(True)

        def spread(i, carry):
            at = pl.ds(pl.multiple_of(i * 2 * rows, 2 * rows), 2 * rows)
            block = mm_cols(grad_query[at, :], att_in[1][...]).astype(BF)
            gbuf[pl.ds(2 * i, 2)] = block.reshape(2, rows, width)
            block = mm_cols(grad_expanded[at, :], att_in[2][...]).astype(BF)
            part_l[pl.ds(2 * i, 2), :, :KVR] = block.reshape(2, rows, KVR)
            block = grad_rope[at, :].astype(BF)
            part_l[pl.ds(2 * i, 2), :, KVR:] = block.reshape(2, rows, 2 * DR)
            return carry

        lax.fori_loop(0, chips, spread, 0)
        near, far = {}, {}
        for i in list(range(1, chips)) + [0]:
            chip = lax.rem(c + i, chips)
            for j in range(2):
                near[i, j] = remote(
                    x_refs[j].at[chip * 2 + 1 - k],
                    bufs[3 * j].at[chip],
                    sems[4 * j].at[i],
                    sems[4 * j + 1].at[i],
                    sibling,
                )
                near[i, j].start()
        for i in range(1, chips):
            chip = lax.rem(c + i, chips)
            for j in range(2):
                from_sib, out_buf, from_far = bufs[3 * j : 3 * j + 3]
                near[i, j].wait_recv()
                out_buf[i] = (
                    x_refs[j][chip * 2 + k].astype(F32) + from_sib[chip].astype(F32)
                ).astype(BF)
                far[i, j] = remote(
                    out_buf.at[i],
                    from_far.at[i],
                    sems[4 * j + 2].at[i],
                    sems[4 * j + 3].at[i],
                    same_core[i - 1],
                )
                far[i, j].start()

        per_tile = 256 // r

        def wq_rows(i, carry):
            at = pl.ds(pl.multiple_of(i * 256, 256), 256)
            block = mm_rows(hidden_ref[:, at], grad_query[...]).astype(BF)
            hsrc[pl.ds(i * per_tile, per_tile), :, :wq_cols] = block.reshape(
                per_tile, r, wq_cols
            )
            return carry

        lax.fori_loop(0, width // 256, wq_rows, 0)
        grad_we = mm_rows(low_ref[...], grad_expanded[...]).astype(BF)
        for j in range(r // rl):
            block = grad_we[:, j * we_cols : (j + 1) * we_cols]
            hsrc[:, j * rl : (j + 1) * rl, wq_cols:] = block.reshape(n_dev, rl, we_cols)
        heads_far = []
        for i in range(1, n_ex):
            for d in range(n_dp):
                copy = remote(
                    hsrc.at[d * n_ex + lax.rem(e + i, n_ex)], heads_mid.at[d, e],
                    h_s.at[i, d], h_r.at[i, d], plane[i - 1],
                )
                copy.start()
                heads_far.append(copy)
        for d in range(n_dp):
            copy = pltpu.make_async_copy(
                hsrc.at[d * n_ex + e], heads_mid.at[d, e], h_r.at[0, d]
            )
            copy.start()
            copy.wait()
        for j in range(2):
            near[0, j].wait_recv()
            sums[j][...] = x_refs[j][e].astype(F32) + bufs[3 * j][c].astype(F32)
        for i in range(1, chips):
            for j in range(2):
                far[i, j].wait_recv()
                sums[j][...] += bufs[3 * j + 2][i].astype(F32)

        at = pl.ds(pl.multiple_of(e * rows, rows), rows)
        cos, sin = att_in[3][at, :], att_in[4][at, :]
        lat_grad, lat_gain = rms_back(lat_ref[:, :KVR], glat_ref[...], sums[1][:, :KVR])
        rope = turn(sums[1][:, KVR:], cos, sin, -1.0)
        lane = lax.broadcasted_iota(jnp.int32, rope.shape, 1)
        rope = jnp.where(lane < DR, rope, 0.0)
        low = jnp.concatenate([lat_grad, rope], axis=1).astype(BF)
        total = sums[0][...] + mm_cols(low, wl_ref[:, :lat_cols])
        tok_grad, tok_gain = rms_back(tok_ref[...].astype(F32), gain_ref[...], total)
        tok_out[...] = gnat_ref[...] + tok_grad
        vec[...] = jnp.zeros_like(vec)
        vec[0:1, :] = jnp.sum(tok_gain, axis=0, keepdims=True)
        vec[1:2, :] = gtwo_ref[...]
        vec[2:3, :KVR] = jnp.sum(lat_gain, axis=0, keepdims=True)
        vec_far = []
        for i in range(1, n_ex):
            copy = remote(vec, vbuf.at[i], v_s.at[i], v_r.at[i], plane[i - 1])
            copy.start()
            vec_far.append(copy)
        for d in range(n_dp):
            block = hidden_ref[at, d * n_ex * r : (d + 1) * n_ex * r]
            block = mm_rows(block, low).reshape(n_ex, r, lat_cols)
            pack[:, d * r : (d + 1) * r, :KVR] = block[:, :, :KVR].astype(BF)
            block = block[:, :, KVR:] + router_ref[:, d * r : (d + 1) * r].astype(F32)
            pack[:, d * r : (d + 1) * r, KVR:] = block.astype(BF)
        pack_near, pack_far = [], []
        for i in list(range(1, chips)) + [0]:
            chip = lax.rem(c + i, chips)
            copy = remote(pack.at[chip * 2 + 1 - k], psib.at[chip], pn_s.at[i], pn_r.at[i], sibling)
            copy.start()
            pack_near.append(copy)
        for copy in heads_far:
            copy.wait_recv()
        heads_col = []
        for i in range(1, n_dp):
            d = lax.rem(z + i, n_dp)
            copy = remote(
                heads_mid.at[d], heads_out.at[z], hz_s.at[i], hz_r.at[i], column[i - 1]
            )
            copy.start()
            heads_col.append(copy)
        copy = pltpu.make_async_copy(heads_mid.at[z], heads_out.at[z], local.at[4])
        copy.start()
        heads_col.append(copy)
        for i in range(1, chips):
            chip = lax.rem(c + i, chips)
            pack_near[i - 1].wait_recv()
            pout[i] = (pack[chip * 2 + k].astype(F32) + psib[chip].astype(F32)).astype(BF)
            copy = remote(pout.at[i], pfar.at[i], pf_s.at[i], pf_r.at[i], same_core[i - 1])
            copy.start()
            pack_far.append(copy)
        for copy in vec_far:
            copy.wait_recv()
            copy.wait_send()
        for i in range(1, n_ex):
            vec[...] += vbuf[i]
        vec_col = []
        for i in range(1, n_dp):
            copy = remote(vec, vzbuf.at[i], vz_s.at[i], vz_r.at[i], column[i - 1])
            copy.start()
            vec_col.append(copy)
        pack_near[chips - 1].wait_recv()
        total = pack[e].astype(F32) + psib[c].astype(F32)
        for i in range(1, chips):
            pack_far[i - 1].wait_recv()
            total = total + pfar[i].astype(F32)
        psum[...] = total.astype(BF).reshape(n_dp, r, lat_cols)
        pack_col = []
        for i in range(1, n_dp):
            copy = remote(
                psum.at[lax.rem(z + i, n_dp)], pbuf.at[i], pc_s.at[i], pc_r.at[i], column[i - 1]
            )
            copy.start()
            pack_col.append(copy)
        result = vec[...]
        for i in range(1, n_dp):
            vec_col[i - 1].wait_recv()
            result = result + vzbuf[i]
        vec_out[...] = result
        result = psum[z].astype(F32)
        for i in range(1, n_dp):
            pack_col[i - 1].wait_recv()
            result = result + pbuf[i].astype(F32)
        pack_out[...] = result

        for i in range(n_dp):
            here = jnp.logical_and(z // hp == part, z == i)

            @pl.when(here)
            def _(i=i):
                pltpu.make_async_copy(
                    wsrc.at[lax.rem(z, hp), part], wout_out.at[i], w_r.at[i]
                ).wait()

            @pl.when(jnp.logical_not(here))
            def _(i=i):
                wait_recv(wout_out.at[i], w_r.at[i], sibling)

        wout_sends(False)
        for copy in list(near.values()) + list(far.values()) + heads_far:
            copy.wait_send()
        for copy in pack_near + pack_far + vec_col + pack_col:
            copy.wait_send()
        for copy in heads_col + others:
            copy.wait()
        for back in backs:
            back.end()

    dma = pltpu.SemaphoreType.DMA
    sds = jax.ShapeDtypeStruct
    vmem = pltpu.VMEM
    scratch = [
        vmem((n_ex, rows, width), BF),
        vmem((seq, 2 * DV), BF),
        vmem((2 * DV, width), F32),
        vmem((seq, 2 * DH), F32),
        vmem((seq, DV), F32),
        vmem((seq, wq.shape[1]), BF),
        vmem((seq, we.shape[1]), BF),
        vmem((seq, 2 * DR), F32),
        vmem((n_ex, rows, lat_cols), BF),
    ]
    scratch += [vmem((chips, rows, width), BF)] * 3 + [vmem((chips, rows, lat_cols), BF)] * 3
    scratch += [
        vmem((rows, width), F32),
        vmem((rows, lat_cols), F32),
        vmem((n_dev, r, head_cols), BF),
        vmem((hp, parts, r, width), BF),
        vmem((n_ex, n_dp * r, lat_cols), BF),
        vmem((chips, n_dp * r, lat_cols), BF),
        vmem((chips, n_dp * r, lat_cols), BF),
        vmem((chips, n_dp * r, lat_cols), BF),
        vmem((n_dp, r, lat_cols), BF),
        vmem((n_dp, r, lat_cols), BF),
        vmem((8, width), F32),
        vmem((n_ex, 8, width), F32),
        vmem((n_dp, 8, width), F32),
    ]
    scratch += [dma((chips,))] * 4 + [dma((6,))] + [dma((chips,))] * 8
    scratch += [dma((n_ex, n_dp))] * 2 + [dma((n_dp,))] * 2 + [dma((hp, parts)), dma((n_dp,))]
    scratch += [dma((chips,))] * 4 + [dma((n_dp,))] * 2 + [dma((3, n_dp))] * 2
    scratch += [dma((n_ex,))] * 2 + [dma((n_dp,))] * 2 + [dma((inner,))] * 2
    for total in totals:
        scratch += ExpertsBack.scratch(total, n_dp, inner)
    outs = pl.pallas_call(
        kernel,
        out_shape=[
            sds((rows, width), F32),
            sds((8, width), F32),
            sds((r, lat_cols), F32),
            sds((n_dp, n_ex, r, head_cols), BF),
            sds((n_dp, n_ex, r, head_cols), BF),
            sds((n_dp, r, width), BF),
            sds(out.shape, BF),
        ]
        + [sds(array.shape, BF) for array in shared]
        + [ExpertsBack.out(total, n_dp, inner) for total in totals],
        in_specs=[ANY] + [VMEM] * 21 + [ANY] * (4 + extra),
        out_specs=[VMEM] * 3 + [ANY] * (7 + extra),
        scratch_shapes=scratch,
        compiler_params=params(collective_id),
    )(grad, *attend, hidden, latent_low, *own, out, *shared, *totals)
    return outs[:3], outs[4], outs[5], outs[6], outs[7:10], outs[10:]


def shards(
    tokens,
    cotangent,
    lengths,
    routes,
    place_order,
    attn_gain,
    w_query,
    w_latent,
    latent_gain,
    w_expand,
    w_out,
    ffn_gain,
    w_router,
    shared_gate,
    shared_up,
    shared_down,
    expert_gate,
    expert_up,
    expert_down,
):
    rows, width = tokens.shape
    n_dp = lax.axis_size("dp")
    n_ex = lax.axis_size("expert")
    chips = n_ex // 2
    z = lax.axis_index("dp")
    e = lax.axis_index("expert")
    chip = e // 2
    n_experts = w_router.shape[1]
    top_k = routes.shape[1]
    capacity = (rows * top_k * 5 + 4 * n_experts - 1) // (4 * n_experts)
    cap = (capacity + 15) // 16 * 16
    seq = rows * n_ex
    r = w_query.shape[0]
    rl = w_expand.shape[0]
    hp = H // n_ex
    parts = DV // r
    heads = [
        (d * n_ex + (j // parts) * parts) * r // DV
        for j in range(n_ex)
        for d in range(j % parts * hp, j % parts * hp + hp)
    ]
    heads_back = [heads.index(h) for h in range(H)]
    inner = n_experts // chips
    my_local = lax.rem(z, inner)
    ff_e = expert_gate.shape[2]
    ff_s = shared_gate.shape[1] // inner
    lat = KVR + DR
    head_cols = hp * (DH + DR)
    kv_cols = hp * (DH + DV)

    def to_owner_order(values):
        cut = values.reshape(values.shape[0], n_dp, n_ex, r)
        return cut.transpose(0, 2, 1, 3).reshape(values.shape)

    def from_owner_order(values):
        cut = values.reshape(values.shape[0], n_ex, n_dp, r)
        return cut.transpose(0, 2, 1, 3).reshape(values.shape)

    def pick(values, index, axis=0):
        return lax.dynamic_index_in_dim(values, index, axis, keepdims=False)

    wq_send = jnp.take(w_query.reshape(r, H, DH + DR), jnp.array(heads), axis=1)
    wq_send = wq_send.reshape(r, n_ex, hp, DH + DR)
    wq_send = jnp.concatenate(
        [
            wq_send[..., :DH].reshape(r, n_ex, hp * DH),
            wq_send[..., DH:].reshape(r, n_ex, hp * DR),
        ],
        axis=-1,
    ).transpose(1, 0, 2)
    we_send = jnp.take(w_expand.reshape(rl, H, DH + DV), jnp.array(heads), axis=1)
    we_cols = rl * kv_cols // r
    we_send = we_send.reshape(rl, n_ex, r // rl, we_cols).transpose(1, 2, 0, 3)
    we_send = we_send.reshape(n_ex, r, we_cols)
    wa_send = jnp.concatenate([wq_send, we_send], axis=-1)
    slot_own = slot_places(routes, place_order[0], capacity)
    slot_place = jnp.where(slot_own >= 0, slot_own - routes * capacity, -1)
    slot_cols = 2 * rows * top_k // r
    slot_pack = jnp.stack([routes, slot_place]).astype(BF).reshape(2, r, slot_cols // 2)
    small_cols = lat + n_experts + 3
    pack_cols = (small_cols + slot_cols + 127) // 128 * 128
    pack = jnp.concatenate(
        [
            w_latent,
            w_router,
            attn_gain[:, None],
            ffn_gain[:, None],
            jnp.pad(latent_gain, (0, r - rl))[:, None],
            slot_pack[0],
            slot_pack[1],
            jnp.zeros((r, pack_cols - small_cols - slot_cols), BF),
        ],
        axis=1,
    )
    cot_owner = to_owner_order(cotangent)
    tok_all, wa_all, pk_all = first_exchange(tokens, wa_send, pack, n_dp, n_ex, 1)
    pk_flat = pk_all.reshape(width, pack_cols)
    w_lat = pk_flat[:, :lat]
    gain_one = pk_flat[:, lat + n_experts].astype(F32)
    gain_two = pk_all[..., lat + n_experts + 1].transpose(1, 0, 2).reshape(width).astype(F32)
    router = pk_all[..., lat : lat + n_experts].transpose(1, 0, 2, 3).reshape(width, n_experts)
    gain_lat = (
        pk_all[..., lat + n_experts + 2].reshape(n_dp * n_ex, r)[:, :rl].reshape(KVR).astype(F32)
    )
    slots_all = n_experts * capacity
    slot_col = pick(pk_all[..., small_cols : small_cols + slot_cols], e, 1)
    slot_col = lax.dynamic_slice_in_dim(slot_col, z - my_local, inner, 0).astype(jnp.int32)
    slot_col = slot_col.reshape(inner, r, 2, slot_cols // 2).transpose(2, 0, 1, 3)
    slot_col = slot_col.reshape(2, inner, rows, top_k)
    slot_ids = jnp.where(
        slot_col[1] >= 0,
        slot_col[0] * capacity + slot_col[1] + (jnp.arange(inner) * slots_all)[:, None, None],
        -1,
    ).reshape(inner * rows, top_k)
    place = jnp.arange(cap)
    far_experts = [lax.rem(chip + m, chips) * inner + my_local for m in range(chips)]
    wanted = (
        jnp.stack(far_experts)[:, None, None] * capacity
        + (jnp.arange(inner) * slots_all)[None, :, None]
        + place[None, None, :]
    )
    wanted = jnp.where(place[None, None, :] < capacity, wanted, -2).reshape(-1)
    n_slots = wanted.shape[0]
    per_far = n_slots // chips
    hot = sum((wanted[:, None] == slot_ids[None, :, j]).astype(BF) for j in range(top_k))
    hot_t = sum((slot_ids[:, j][:, None] == wanted[None, :]).astype(BF) for j in range(top_k))

    positions = jnp.arange(seq)
    lane = jnp.arange(2 * DR) % (DR // 2)
    angles = positions.astype(F32)[:, None] * (10000.0 ** (-(lane.astype(F32) * 2.0) / DR))[None, :]
    cos_wide, sine_wide = jnp.cos(angles), jnp.sin(angles)
    keep = (positions < lengths[0]).astype(F32)[None]
    attend_out, (wq, wexp, wo_rows), residual, x_col, cot_col, (wg,), shared_w = forward_exchange(
        [tok_all, gain_one[None], wa_all, pk_flat, gain_lat[None], cos_wide, sine_wide, keep],
        to_owner_order(w_out),
        to_owner_order(tokens),
        gain_two[None],
        cot_owner,
        [expert_gate.reshape(-1, n_ex, r, ff_e)],
        [w.reshape(r, inner, ff_s).transpose(1, 0, 2) for w in (shared_gate, shared_up, shared_down)],
        n_dp,
        n_ex,
        inner,
        2,
    )
    hidden_one, latent_raw, latent_low, qcat, kcat, value, lse, attended = attend_out
    wo_rows = wo_rows.reshape(hp * DV, width)
    cot_col = cot_col.reshape(inner * rows, width)
    hidden_two = pick(x_col, my_local)
    x_col = x_col.reshape(inner * rows, width)

    (x_in, grad_in), (wu, wd), shared_out, shared_dx, shared_grads = dispatch(
        hot,
        x_col,
        cot_col,
        [w.reshape(width, ff_s) for w in shared_w],
        [w.reshape(-1, n_ex, r, ff_e) for w in (expert_up, expert_down)],
        n_dp,
        n_ex,
        inner,
        8,
    )
    x_in = x_in.reshape(n_slots, width)
    grad_in = grad_in.reshape(n_slots, width)
    wg, wu, wd = (w.reshape(width, ff_e) for w in (wg, wu, wd))

    def probs_of(logits):
        top = jnp.max(logits, axis=-1, keepdims=True)
        exp_logits = jnp.exp(logits - top)
        return exp_logits / jnp.sum(exp_logits, axis=-1, keepdims=True)

    dx_back, dots_back, expert_rows, down_back, expert_totals = experts_run(
        x_in,
        grad_in,
        [wg, wu, wd],
        jnp.pad(router, ((0, 0), (0, 128 - n_experts))),
        n_dp,
        n_ex,
        inner,
        9,
    )
    dx_back = dx_back.reshape(n_slots, width)

    col_probs = probs_of(mm(x_col, router))
    expert_axis = jnp.arange(n_experts)[None, :]
    gates = [
        jnp.sum(jnp.where(expert_axis == expert, col_probs, 0.0), axis=1, keepdims=True)
        for expert in far_experts
    ]
    gate_hot = jnp.concatenate(
        [hot_t[:, m * per_far : (m + 1) * per_far] * gates[m].astype(BF) for m in range(chips)],
        axis=1,
    )
    dots = dots_back.reshape(n_slots, 128)[:, 0].astype(F32)[None] * hot_t.astype(F32)
    dots = jnp.sum(dots.reshape(inner * rows, chips, per_far), axis=-1)
    grad_probs_col = sum(
        jnp.where(expert_axis == far_experts[m], dots[:, m : m + 1], 0.0) for m in range(chips)
    )
    dx_col = mm(hot_t, dx_back) + shared_dx
    dx_send = jnp.concatenate(
        [dx_col, grad_probs_col, jnp.zeros((inner * rows, 128 - n_experts), F32)], axis=1
    ).astype(BF)
    dx_sum, shared_sums, rows_back, (gate_back,) = column_sum(
        dx_send.reshape(inner, rows, width + 128),
        expert_rows,
        [grad.reshape(n_ex, n_dp, r, ff_s) for grad in shared_grads],
        expert_totals[:1],
        n_dp,
        n_ex,
        inner,
        3,
    )
    router_probs = lax.dynamic_slice_in_dim(col_probs, my_local * rows, rows, 0)
    grad_probs = dx_sum[:, width : width + n_experts]
    grad_logits = (
        router_probs * (grad_probs - jnp.sum(grad_probs * router_probs, axis=-1, keepdims=True))
    ).astype(BF)
    grad_router = mm_rows(hidden_two, grad_logits)
    grad_hidden_two = dx_sum[:, :width] + mm_cols(grad_logits, router)
    _, norm_two_back = jax.vjp(rms_norm, residual, gain_two)
    grad_resid_norm, grad_gain_two = norm_two_back(grad_hidden_two)
    grad_residual = cot_owner.astype(F32) + grad_resid_norm

    out_col = mm(gate_hot, rows_back.reshape(n_slots, width)) + shared_out
    latent_own = lax.dynamic_slice_in_dim(latent_raw, e * rows, rows, 0)
    router_back = jnp.pad(
        grad_router.reshape(n_ex, n_dp * r, n_experts),
        ((0, 0), (0, 0), (DR, DR - n_experts)),
    ).astype(BF)
    (grad_tokens, vec_sum, pack_sum), heads_got, wout_got, out_got, shared_got, (up_back,) = (
        backward_exchange(
            grad_residual.astype(BF),
            [wo_rows, wq, wexp, cos_wide, sine_wide, keep, qcat, kcat, value, lse, attended],
            hidden_one,
            latent_low,
            [
                pk_flat,
                latent_own,
                tokens,
                gain_one[None],
                gain_lat[None],
                from_owner_order(grad_residual),
                router_back,
                grad_gain_two[None],
            ],
            out_col.astype(BF).reshape(inner, rows, width),
            shared_sums,
            expert_totals[1:2],
            n_dp,
            n_ex,
            inner,
            5,
        )
    )

    def added(values):
        return jnp.sum(values.astype(F32), axis=0)

    out_tokens = from_owner_order((residual + added(out_got)).astype(BF))
    heads_all = added(heads_got)
    sum_wq = heads_all[..., :head_cols].transpose(1, 0, 2)
    sum_wq = jnp.concatenate(
        [
            sum_wq[..., : hp * DH].reshape(r, n_ex, hp, DH),
            sum_wq[..., hp * DH :].reshape(r, n_ex, hp, DR),
        ],
        axis=-1,
    ).reshape(r, H, DH + DR)
    sum_wq = jnp.take(sum_wq, jnp.array(heads_back), axis=1).reshape(r, H * (DH + DR))
    sum_we = heads_all[..., head_cols:].reshape(n_ex, r // rl, rl, we_cols).transpose(2, 0, 1, 3)
    sum_we = jnp.take(sum_we.reshape(rl, H, DH + DV), jnp.array(heads_back), axis=1)
    sum_we = sum_we.reshape(rl, H * (DH + DV))
    sum_wout = from_owner_order(added(wout_got))
    device = z * n_ex + e
    sum_gain_one = lax.dynamic_slice_in_dim(vec_sum[0], device * r, r, 0)
    sum_gain_two = lax.dynamic_slice_in_dim(vec_sum[1], (e * n_dp + z) * r, r, 0)
    sum_gain_lat = lax.dynamic_slice_in_dim(vec_sum[2], device * rl, rl, 0)
    sum_sgate, sum_sup, sum_sdown = (
        added(got.reshape(n_dp // inner, inner, r, ff_s)).transpose(1, 0, 2).reshape(r, -1)
        for got in shared_got
    )
    sum_egate, sum_eup, sum_edown = (
        added(back).reshape(-1, n_ex * r, ff_e) for back in (gate_back, up_back, down_back)
    )
    return (
        out_tokens,
        grad_tokens,
        sum_gain_one,
        sum_wq,
        pack_sum[:, :lat],
        sum_gain_lat,
        sum_we,
        sum_wout,
        sum_gain_two,
        pack_sum[:, lat : lat + n_experts],
        sum_sgate,
        sum_sup,
        sum_sdown,
        sum_egate,
        sum_eup,
        sum_edown,
    )


def solution(mesh):
    both = ("dp", "expert")
    in_specs = (
        P(both, None),
        P(both, None),
        P("dp"),
        P(both, None),
        P(both, None),
        P(both),
        P(both, None),
        P(both, None),
        P(both),
        P(both, None),
        P(both, None),
        P(both),
        P(both, None),
        P(both, None),
        P(both, None),
        P(both, None),
        P("expert", "dp", None),
        P("expert", "dp", None),
        P("expert", "dp", None),
    )
    out_specs = (
        P(both, None),
        P(both, None),
        P(both),
        P(both, None),
        P(both, None),
        P(both),
        P(both, None),
        P(both, None),
        P(both),
        P(both, None),
        P(both, None),
        P(both, None),
        P(both, None),
        P("expert", "dp", None),
        P("expert", "dp", None),
        P("expert", "dp", None),
    )
    return jax.shard_map(shards, mesh=mesh, in_specs=in_specs, out_specs=out_specs, check_vma=False)
```

```python
import jax
import jax.numpy as jnp
from jax import lax
from jax.experimental import pallas as pl
from jax.experimental.pallas import tpu as pltpu
from jax.sharding import PartitionSpec as P

H = 16
DH = 128
DR = 64
DV = 128
KVR = 512

norm_eps = 1e-06
masked_score = -1e30
MESH = pl.DeviceIdType.MESH
ANY = pl.BlockSpec(memory_space=pl.ANY)
VMEM = pl.BlockSpec(memory_space=pltpu.VMEM)
BF = jnp.bfloat16
F32 = jnp.float32


def rms_norm(values, scale_gain):
    return (
        values
        * lax.rsqrt(jnp.mean(values * values, axis=-1, keepdims=True) + norm_eps)
        * scale_gain
    )


def mm(left, right):
    return jnp.dot(left, right, preferred_element_type=F32)


def mm_rows(left, right):
    return lax.dot_general(left, right, (((0,), (0,)), ((), ())), preferred_element_type=F32)


def mm_cols(left, right):
    return lax.dot_general(left, right, (((1,), (1,)), ((), ())), preferred_element_type=F32)


def slot_places(route_rows, pair_order, capacity):
    pair_expert = route_rows.reshape(-1)
    earlier = pair_order[None, :] < pair_order[:, None]
    same_expert = pair_expert[None, :] == pair_expert[:, None]
    places = jnp.sum((earlier & same_expert).astype(jnp.int32), axis=1)
    slot_index = jnp.where(places < capacity, pair_expert * capacity + places, -1)
    return slot_index.reshape(route_rows.shape)


def turn(values, cos, sin, sign):
    half = DR // 2
    first = lax.rem(lax.broadcasted_iota(jnp.int32, values.shape, 1), DR) < half
    partner = jnp.where(
        first, -pltpu.roll(values, 2 * DR - half, 1), pltpu.roll(values, half, 1)
    )
    return values * cos + sign * (partner * sin)


def causal(i, tile, keep_ref):
    shape = (tile, (i + 1) * tile)
    query = lax.broadcasted_iota(jnp.int32, shape, 0) + i * tile
    key = lax.broadcasted_iota(jnp.int32, shape, 1)
    return (key <= query) & (keep_ref[:, : shape[1]] > 0.5)


def attend_forward(
    tok, gain, wq, wl, gain_lat, we, cos, sin, keep,
    hidden, latent, latent_low, qcat, kcat, value, lse, attended,
):
    per, rows, width = tok.shape
    seq = per * rows
    tile = 2 * rows
    scale = (DH + DR) ** (-0.5)

    def project(i, carry):
        at = pl.ds(pl.multiple_of(i * tile, tile), tile)
        x = tok[pl.ds(2 * i, 2)].reshape(tile, width).astype(F32)
        root = lax.rsqrt(jnp.mean(x * x, axis=-1, keepdims=True) + norm_eps)
        hid = (x * root * gain[...]).astype(BF)
        hidden[at, :] = hid
        c, s = cos[at, :], sin[at, :]
        query = mm(hid, wq[...])
        rope_q = turn(query[:, 2 * DH :], c, s, 1.0).astype(BF)
        lat = mm(hid, wl[...])
        latent[at, :] = lat
        plain = lat[:, :KVR]
        root = lax.rsqrt(jnp.mean(plain * plain, axis=-1, keepdims=True) + norm_eps)
        low = (plain * root * gain_lat[...]).astype(BF)
        latent_low[at, :] = low
        rope = lat[:, KVR : KVR + 2 * DR]
        lane = lax.broadcasted_iota(jnp.int32, rope.shape, 1)
        rope = jnp.where(lane < DR, rope, pltpu.roll(rope, DR, 1))
        rope = turn(rope, c, s, 1.0)
        expanded = mm(low, we[...]).astype(BF)
        for h in range(2):
            qcat[h, at, :DH] = query[:, h * DH : (h + 1) * DH].astype(BF)
            qcat[h, at, DH:] = rope_q
            mine = (lane < DR) if h == 0 else (lane >= DR)
            kcat[h, at, :DH] = expanded[:, h * (DH + DV) : h * (DH + DV) + DH]
            kcat[h, at, DH:] = jnp.where(mine, rope, 0.0).astype(BF)
            value[h, at, :] = expanded[:, h * (DH + DV) + DH : (h + 1) * (DH + DV)]
        return carry

    lax.fori_loop(0, seq // tile, project, 0)
    for h in range(2):
        for i in range(seq // tile):
            at, upto = slice(i * tile, (i + 1) * tile), slice(0, (i + 1) * tile)
            scores = mm_cols(qcat[h, at, :], kcat[h, upto, :]) * scale
            scores = jnp.where(causal(i, tile, keep), scores, masked_score)
            top = jnp.max(scores, axis=-1, keepdims=True)
            exp_scores = jnp.exp(scores - top)
            total = jnp.sum(exp_scores, axis=-1, keepdims=True)
            probs = (exp_scores / total).astype(BF)
            attended[at, h * DV : (h + 1) * DV] = mm(probs, value[h, upto, :]).astype(BF)
            lse[h, at, :] = jnp.broadcast_to(top + jnp.log(total), (tile, lse.shape[2]))


def attend_backward(
    grad, wo, wq, we, cos, sin, keep, qcat, kcat, value, lse, attended,
    gat, grad_wout, dk, dv, grad_query, grad_expanded, grad_rope,
):
    per, rows, width = grad.shape
    seq = per * rows
    tile = 2 * rows
    scale = (DH + DR) ** (-0.5)
    count = seq // tile
    grad_wout[...] = jnp.zeros_like(grad_wout)

    def project(i, carry):
        at = pl.ds(pl.multiple_of(i * tile, tile), tile)
        block = grad[pl.ds(2 * i, 2)].reshape(tile, width)
        gat[at, :] = mm_cols(block, wo[...]).astype(BF)
        grad_wout[...] += mm_rows(attended[at, :], block)
        return carry

    lax.fori_loop(0, count, project, 0)
    for h in range(2):
        dk[...] = jnp.zeros_like(dk)
        dv[...] = jnp.zeros_like(dv)
        for i in range(count):
            at, upto = slice(i * tile, (i + 1) * tile), slice(0, (i + 1) * tile)
            g = gat[at, h * DV : (h + 1) * DV]
            scores = mm_cols(qcat[h, at, :], kcat[h, upto, :]) * scale
            scores = jnp.where(causal(i, tile, keep), scores, masked_score)
            probs = jnp.exp(scores - lse[h, at, 0:1])
            grad_probs = mm_cols(g, value[h, upto, :])
            inner = jnp.sum(grad_probs * probs, axis=-1, keepdims=True)
            raw = (probs * (grad_probs - inner) * scale).astype(BF)
            grad_q = mm(raw, kcat[h, upto, :])
            grad_query[at, h * DH : (h + 1) * DH] = grad_q[:, :DH].astype(BF)
            rope = grad_q[:, DH:]
            lane = lax.broadcasted_iota(jnp.int32, rope.shape, 1)
            mine = (lane < DR) if h == 0 else (lane >= DR)
            rope = turn(rope, cos[at, :], sin[at, :], -1.0).astype(BF)
            if h == 0:
                grad_query[at, 2 * DH :] = rope
            else:
                grad_query[at, 2 * DH :] = jnp.where(mine, rope, grad_query[at, 2 * DH :])
            dk[upto, :] += mm_rows(raw, qcat[h, at, :])
            dv[upto, :] += mm_rows(probs.astype(BF), g)
        grad_expanded[:, h * (DH + DV) : h * (DH + DV) + DH] = dk[:, :DH].astype(BF)
        grad_expanded[:, h * (DH + DV) + DH : (h + 1) * (DH + DV)] = dv[...].astype(BF)
        rope = dk[:, DH:]
        if h == 0:
            grad_rope[...] = rope
        else:
            grad_rope[...] += pltpu.roll(rope, DR, 1)


def params(collective_id):
    return pltpu.CompilerParams(
        collective_id=collective_id, has_side_effects=True, vmem_limit_bytes=60 << 20
    )


def remote(src, dst, send_sem, recv_sem, device):
    return pltpu.make_async_remote_copy(
        src_ref=src,
        dst_ref=dst,
        send_sem=send_sem,
        recv_sem=recv_sem,
        device_id=device,
        device_id_type=MESH,
    )


def greet(devices):
    barrier = pltpu.get_barrier_semaphore()
    for device in devices:
        pl.semaphore_signal(barrier, inc=1, device_id=device, device_id_type=MESH)
    pl.semaphore_wait(barrier, len(devices))


def places(n_dp, n_ex):
    z = lax.axis_index("dp")
    e = lax.axis_index("expert")
    chips = n_ex // 2
    c, k = e // 2, lax.rem(e, 2)
    sibling = (z, e + 1 - 2 * k)
    same_core = [(z, lax.rem(c + i, chips) * 2 + k) for i in range(1, chips)]
    column = [(lax.rem(z + i, n_dp), e) for i in range(1, n_dp)]
    return z, e, c, k, sibling, same_core, column


def wait_recv(region, sem, device):
    remote(region, region, sem, sem, device).wait_recv()


def column_sum(array, rows_out, shared, totals, n_dp, n_ex, inner, collective_id):
    chips = n_ex // 2
    shape = array.shape[1:]
    extra = len(totals)
    _, _, r, ff_s = shared[0].shape

    def kernel(x_hbm, *refs):
        s_in, r_ref, t_refs, refs = refs[:3], refs[3], refs[4 : 4 + extra], refs[4 + extra :]
        o_ref, s_out, r_out, back_refs = refs[0], refs[1:4], refs[4], refs[5 : 5 + extra]
        refs = refs[5 + extra :]
        x_ref, s_v, from_sib, out_buf, from_far = refs[0], refs[1:4], *refs[4:7]
        loads, near_s, near_r, far_s, far_r, r_s, r_r, local = refs[7:15]
        relay_refs, rest = refs[15:18], refs[18:]
        moves = stage([x_hbm, *s_in], [x_ref, *s_v], loads)
        z, e, c, k, sibling, same_core, column = places(n_dp, n_ex)
        greet(same_core + [sibling] + column + [(d[0], sibling[1]) for d in column])
        backs = [
            ExpertsBack(t_refs[m], back_refs[m], rest[7 * m : 7 * m + 7], n_dp, n_ex, inner)
            for m in range(extra)
        ]
        relay = RelaySum(x_ref, relay_refs, n_dp, n_ex, inner)
        near, far, rows_back = {}, {}, []
        for i in list(range(1, chips)) + [0]:
            chip = lax.rem(c + i, chips)
            for m in range(3):
                near[i, m] = remote(
                    s_in[m].at[chip * 2 + 1 - k], from_sib.at[m, i],
                    near_s.at[m, i], near_r.at[m, i], sibling,
                )
                near[i, m].start()
        for back in backs:
            back.begin()
        for i in range(1, chips):
            copy = remote(
                r_ref.at[i], r_out.at[i], r_s.at[i], r_r.at[i], same_core[chips - i - 1]
            )
            copy.start()
            rows_back.append(copy)
        copy = pltpu.make_async_copy(r_ref.at[0], r_out.at[0], local)
        copy.start()
        rows_back.append(copy)
        moves[0].wait()
        relay.run()

        def pair(i, m):
            chip = lax.rem(c + i, chips)
            near[i, m].wait_recv()

            def row(d, carry):
                out_buf[m, i, d] = (
                    s_v[m][chip * 2 + k, d].astype(F32) + from_sib[m, i, d].astype(F32)
                ).astype(BF)
                return carry

            lax.fori_loop(0, n_dp, row, 0)

        for back in backs:
            back.pass_on()
        for move in moves[1:]:
            move.wait()
        for i in range(1, chips):
            for m in range(3):
                pair(i, m)
                far[i, m] = remote(
                    out_buf.at[m, i], from_far.at[m, i], far_s.at[m, i], far_r.at[m, i],
                    same_core[i - 1],
                )
                far[i, m].start()
        for m in range(3):
            pair(0, m)
        relay.finish(o_ref)
        for m in range(3):
            for i in range(1, chips):
                far[i, m].wait_recv()

            def row(d, carry, m=m):
                total = out_buf[m, 0, d].astype(F32)
                for i in range(1, chips):
                    total = total + from_far[m, i, d].astype(F32)
                s_out[m][d] = total.astype(BF)
                return carry

            lax.fori_loop(0, n_dp, row, 0)
        for copy in list(near.values()) + list(far.values()):
            copy.wait_send()
        for copy in rows_back:
            copy.wait()
        relay.end()
        for back in backs:
            back.end()

    dma = pltpu.SemaphoreType.DMA
    scratch = like([array, *shared])
    scratch += [pltpu.VMEM((3, chips, n_dp, r, ff_s), BF)] * 3
    scratch += [dma((4,))] + [dma((3, chips))] * 4 + [dma((chips,))] * 2 + [dma]
    scratch += RelaySum.scratch(shape, inner)
    for total in totals:
        scratch += ExpertsBack.scratch(total, n_dp, inner)
    outs = pl.pallas_call(
        kernel,
        out_shape=[jax.ShapeDtypeStruct(shape, F32)]
        + [jax.ShapeDtypeStruct((n_dp, r, ff_s), BF)] * 3
        + [jax.ShapeDtypeStruct(rows_out.shape, BF)]
        + [ExpertsBack.out(total, n_dp, inner) for total in totals],
        in_specs=[ANY] * (5 + extra),
        out_specs=[VMEM] * 4 + [ANY] * (1 + extra),
        scratch_shapes=scratch,
        compiler_params=params(collective_id),
    )(array, *shared, rows_out, *totals)
    return outs[0], outs[1:4], outs[4], outs[5:]


class Relay:
    @staticmethod
    def scratch(inner):
        dma = pltpu.SemaphoreType.DMA
        return [dma((inner,)), dma((inner,)), dma((inner,)), dma]

    def __init__(self, block, out, scratch, n_dp, n_ex, inner):
        self.block, self.out, self.inner = block, out, inner
        self.up_s, self.down_s, self.recv, self.local = scratch
        self.z, self.e, *_ = places(n_dp, n_ex)
        self.mine = lax.rem(self.z, inner)

    def copy(self, source, src, step):
        sem = self.up_s if step > 0 else self.down_s
        return remote(
            src, self.out.at[source], sem.at[source], self.recv.at[source], (self.z + step, self.e)
        )

    def keep(self):
        return pltpu.make_async_copy(self.block, self.out.at[self.mine], self.local)

    def begin(self):
        pl.when(self.mine < self.inner - 1)(lambda: self.copy(self.mine, self.block, 1).start())
        pl.when(self.mine > 0)(lambda: self.copy(self.mine, self.block, -1).start())
        self.keep().start()

    def pass_on(self):
        for t in range(1, self.inner):
            for step in (1, -1):
                source = self.mine - step * t
                exists = source >= 0 if step > 0 else source < self.inner
                more = self.mine < self.inner - 1 if step > 0 else self.mine > 0

                @pl.when(exists)
                def _(source=source, step=step):
                    self.copy(source, self.out.at[source], step).wait_recv()

                @pl.when(jnp.logical_and(exists, more))
                def _(source=source, step=step):
                    self.copy(source, self.out.at[source], step).start()

    def end(self):
        self.keep().wait()
        pl.when(self.mine < self.inner - 1)(
            lambda: self.copy(self.mine, self.block, 1).wait_send()
        )
        pl.when(self.mine > 0)(lambda: self.copy(self.mine, self.block, -1).wait_send())
        for t in range(1, self.inner):
            for step in (1, -1):
                source = self.mine - step * t
                exists = source >= 0 if step > 0 else source < self.inner
                more = self.mine < self.inner - 1 if step > 0 else self.mine > 0

                @pl.when(jnp.logical_and(exists, more))
                def _(source=source, step=step):
                    self.copy(source, self.out.at[source], step).wait_send()


class RelaySum:
    @staticmethod
    def scratch(shape, inner):
        dma = pltpu.SemaphoreType.DMA
        return [pltpu.VMEM((inner + 1,) + shape, BF), dma((inner,)), dma((inner + 1,))]

    def __init__(self, blocks, scratch, n_dp, n_ex, inner):
        self.blocks, self.inner = blocks, inner
        self.buf, self.send, self.recv = scratch
        self.z, self.e, *_ = places(n_dp, n_ex)
        self.mine = lax.rem(self.z, inner)

    def copy(self, t, src, slot, step):
        return remote(
            src, self.buf.at[slot], self.send.at[t], self.recv.at[slot], (self.z + step, self.e)
        )

    def routes(self, t, step):
        inner, mine = self.inner, self.mine
        if step > 0:
            return [(mine < t, mine == 0, t)]
        last = mine == inner - 1
        return [
            (jnp.logical_and(mine > t, mine - 1 != t), last, t),
            (mine - 1 == t, last, inner),
        ]

    def hop(self, t, step, start):
        for active, first, slot in self.routes(t, step):

            @pl.when(jnp.logical_and(active, first))
            def _(slot=slot):
                copy = self.copy(t, self.blocks.at[t], slot, step)
                if start:
                    copy.start()
                else:
                    copy.wait_send()

            @pl.when(jnp.logical_and(active, jnp.logical_not(first)))
            def _(slot=slot):
                copy = self.copy(t, self.buf.at[t], slot, step)
                if start:
                    self.copy(t, self.buf.at[t], t, step).wait_recv()
                    total = self.buf[t].astype(F32) + self.blocks[t].astype(F32)
                    self.buf[t] = total.astype(BF)
                    copy.start()
                else:
                    copy.wait_send()

    def run(self):
        inner = self.inner

        def up():
            for t in range(inner - 1, 0, -1):
                self.hop(t, 1, True)

        def down():
            for t in range(inner - 1):
                self.hop(t, -1, True)

        @pl.when(self.mine < inner // 2)
        def _():
            up()
            down()

        @pl.when(self.mine >= inner // 2)
        def _():
            down()
            up()

    def finish(self, out):
        out[...] = self.blocks[self.mine].astype(F32)

        @pl.when(self.mine > 0)
        def _():
            self.copy(0, self.buf.at[self.mine], self.mine, 1).wait_recv()
            out[...] += self.buf[self.mine].astype(F32)

        @pl.when(self.mine < self.inner - 1)
        def _():
            self.copy(0, self.buf.at[self.inner], self.inner, 1).wait_recv()
            out[...] += self.buf[self.inner].astype(F32)

    def end(self):
        for t in range(self.inner):
            if t:
                self.hop(t, 1, False)
            if t < self.inner - 1:
                self.hop(t, -1, False)


def stage(sources, targets, sems):
    copies = [
        pltpu.make_async_copy(source, target, sems.at[j])
        for j, (source, target) in enumerate(zip(sources, targets))
    ]
    for copy in copies:
        copy.start()
    return copies


def like(arrays):
    return [pltpu.VMEM(array.shape, array.dtype) for array in arrays]


def column_group(z, e, inner):
    start = z // inner * inner
    return [(start + lax.rem(z - start + i, inner), e) for i in range(inner)]


def first_exchange(tok, heads_w, pack, n_dp, n_ex, collective_id):
    chips = n_ex // 2

    def kernel(
        tok_ref, wa_ref, pk_ref, tok_out, wa_out, pk_out,
        t_send, t_recv, ts_send, ts_recv, a_send, a_recv, az_send, az_recv,
        p_send, p_recv, pf_send, pf_recv, ps_send, ps_recv, local,
    ):
        z, e, c, k, sibling, same_core, column = places(n_dp, n_ex)
        plane = [(z, lax.rem(e + i, n_ex)) for i in range(1, n_ex)]
        greet(plane + column)
        wa_far, pk_col, tok_far, near = [], [], [], []
        for i in range(1, n_ex):
            copy = remote(
                wa_ref.at[lax.rem(e + i, n_ex)], wa_out.at[z, e],
                a_send.at[i], a_recv.at[i], plane[i - 1],
            )
            copy.start()
            wa_far.append(copy)
        for i in range(1, n_dp):
            copy = remote(pk_ref, pk_out.at[z, e], p_send.at[i], p_recv.at[i], column[i - 1])
            copy.start()
            pk_col.append(copy)
        for i in range(1, chips):
            copy = remote(tok_ref, tok_out.at[e], t_send.at[i], t_recv.at[i], same_core[i - 1])
            copy.start()
            tok_far.append(copy)
        copy = remote(tok_ref, tok_out.at[e], ts_send.at[0], ts_recv.at[0], sibling)
        copy.start()
        near.append(copy)
        own = [
            pltpu.make_async_copy(wa_ref.at[e], wa_out.at[z, e], local.at[0]),
            pltpu.make_async_copy(pk_ref, pk_out.at[z, e], local.at[1]),
            pltpu.make_async_copy(tok_ref, tok_out.at[e], local.at[2]),
        ]
        for copy in own:
            copy.start()
        for copy in own:
            copy.wait()
        for copy in wa_far:
            copy.wait_recv()
        wa_col = []
        for i in range(1, n_dp):
            copy = remote(
                wa_out.at[z], wa_out.at[z], az_send.at[i], az_recv.at[i], column[i - 1]
            )
            copy.start()
            wa_col.append(copy)
        for copy in pk_col:
            copy.wait_recv()
        pk_far = []
        for i in range(1, chips):
            copy = remote(
                pk_out.at[:, e], pk_out.at[:, e], pf_send.at[i], pf_recv.at[i], same_core[i - 1]
            )
            copy.start()
            pk_far.append(copy)
        copy = remote(pk_out.at[:, e], pk_out.at[:, e], ps_send.at[0], ps_recv.at[0], sibling)
        copy.start()
        near.append(copy)
        for i in range(1, chips):
            source = lax.rem(c + chips - i, chips) * 2 + k
            tok_far[i - 1].wait_recv()
            copy = remote(
                tok_out.at[source], tok_out.at[source], ts_send.at[i], ts_recv.at[i], sibling
            )
            copy.start()
            near.append(copy)
            pk_far[i - 1].wait_recv()
            copy = remote(
                pk_out.at[:, source], pk_out.at[:, source], ps_send.at[i], ps_recv.at[i], sibling
            )
            copy.start()
            near.append(copy)
        for copy in near + wa_col:
            copy.wait()
        for copy in wa_far + pk_col + tok_far + pk_far:
            copy.wait_send()

    dma = pltpu.SemaphoreType.DMA
    return pl.pallas_call(
        kernel,
        out_shape=[
            jax.ShapeDtypeStruct((n_ex,) + tok.shape, tok.dtype),
            jax.ShapeDtypeStruct((n_dp,) + heads_w.shape, heads_w.dtype),
            jax.ShapeDtypeStruct((n_dp, n_ex) + pack.shape, pack.dtype),
        ],
        in_specs=[ANY] * 3,
        out_specs=[ANY] * 3,
        scratch_shapes=[dma((chips,))] * 4
        + [dma((n_ex,))] * 2
        + [dma((n_dp,))] * 4
        + [dma((chips,))] * 4
        + [dma((3,))],
        compiler_params=params(collective_id),
    )(tok, heads_w, pack)


class ExpertsIn:
    @staticmethod
    def scratch(n_dp):
        dma = pltpu.SemaphoreType.DMA
        return [dma((n_dp, 2)), dma((n_dp,)), dma((n_dp,)), dma((n_dp,))]

    @staticmethod
    def out(weight, n_dp, n_ex):
        return jax.ShapeDtypeStruct((n_ex, n_dp) + weight.shape[2:], BF)

    def __init__(self, weight, out, scratch, n_dp, n_ex, inner):
        self.weight, self.out, self.n_dp, self.inner = weight, out, n_dp, inner
        self.send, self.recv, self.sib_send, self.sib_recv = scratch
        self.z, self.e, self.c, self.k, self.sibling, _, _ = places(n_dp, n_ex)
        self.hh = n_ex // 2
        self.local = weight.shape[0]

    def sends(self, start):
        for i in list(range(1, self.n_dp)) + [0]:
            to = lax.rem(self.z + i, self.n_dp)
            expert = lax.rem(to, self.inner)

            def go(i=i, to=to, expert=expert):
                for h in range(2):
                    src = self.weight.at[lax.rem(expert, self.local), pl.ds(h * self.hh, self.hh)]
                    dst = self.out.at[pl.ds(h * self.hh, self.hh), self.z]
                    sem = self.recv.at[self.z]

                    def far(src=src, dst=dst, h=h):
                        copy = remote(src, dst, self.send.at[i, h], sem, (to, 2 * self.c + h))
                        if start:
                            copy.start()
                        else:
                            copy.wait_send()

                    if i:
                        far()
                    else:
                        pl.when(self.k != h)(far)
                        if start:

                            @pl.when(self.k == h)
                            def _(src=src, dst=dst):
                                pltpu.make_async_copy(src, dst, sem).start()

            pl.when(expert // self.local == self.k)(go)

    def begin(self):
        self.sends(True)

    def pass_on(self):
        mine = lax.rem(self.z, self.inner)
        for i in range(self.n_dp):
            d = lax.rem(self.z + self.n_dp - i, self.n_dp)
            region = self.out.at[pl.ds(self.k * self.hh, self.hh), d]
            if i:
                wait_recv(region, self.recv.at[d], self.sibling)
            else:
                from_here = mine // self.local == self.k

                @pl.when(from_here)
                def _(region=region, d=d):
                    src = self.weight.at[
                        lax.rem(mine, self.local), pl.ds(self.k * self.hh, self.hh)
                    ]
                    pltpu.make_async_copy(src, region, self.recv.at[d]).wait()

                @pl.when(jnp.logical_not(from_here))
                def _(region=region, d=d):
                    wait_recv(region, self.recv.at[d], self.sibling)

            remote(
                region, region, self.sib_send.at[i], self.sib_recv.at[i], self.sibling
            ).start()

    def end(self):
        self.sends(False)
        for i in range(self.n_dp):
            d = lax.rem(self.z + self.n_dp - i, self.n_dp)
            mine = self.out.at[pl.ds(self.k * self.hh, self.hh), d]
            remote(
                mine, mine, self.sib_send.at[i], self.sib_recv.at[i], self.sibling
            ).wait_send()
            region = self.out.at[pl.ds((1 - self.k) * self.hh, self.hh), d]
            wait_recv(region, self.sib_recv.at[i], self.sibling)


def forward_exchange(attend, w_out, tok, gain, cot, experts, shared, n_dp, n_ex, inner, collective_id):
    chips = n_ex // 2
    rows, width = tok.shape
    count = len(experts)
    r = w_out.shape[0]
    parts = DV // r
    hp = n_dp // parts
    seq = n_ex * rows
    rl = KVR // (n_dp * n_ex)
    we_cols = rl * hp * (DH + DV) // r
    wq_cols = hp * (DH + DR)

    def kernel(*refs):
        att_hbm, refs = refs[:8], refs[8:]
        wo_in, tok_ref, gain_ref, cot_in = refs[:4]
        e_in, s_in = refs[4 : 4 + count], refs[4 + count : 7 + count]
        refs = refs[7 + count :]
        kept_hbm, refs = refs[:11], refs[11:]
        res_ref, xcol_ref, cot_out = refs[:3]
        refs = refs[3:]
        w_out, s_out = refs[:count], refs[count : 3 + count]
        refs = refs[3 + count :]
        staged, kept, refs = refs[:5], refs[5:16], refs[16:]
        stage_sem, kept_sem, refs = refs[0], refs[1], refs[2:]
        att_out, (wq_ref, we_ref, wo_out) = kept[:8], kept[8:]
        big = (0, 2, 3, 5, 6)
        moves = stage([att_hbm[j] for j in big], staged, stage_sem)
        att_in = list(att_hbm)
        for j, ref in zip(big, staged):
            att_in[j] = ref
        x_ref, from_sib, out_buf, from_far, xbuf = refs[:5]
        (
            near_s, near_r, far_s, far_r,
            sh_s, sh_r, sp_s, sp_r, sf_s, sf_r, wo_s, wo_r, local,
        ) = refs[5:18]
        x_sems, co_sems, refs = refs[18:22], refs[22:26], refs[26:]
        z, e, c, k, sibling, same_core, column = places(n_dp, n_ex)
        part = lax.rem(e, parts)
        members = [
            (lax.rem(z + i, n_dp), e - part + lax.rem(part + j, parts))
            for i in range(n_dp)
            for j in range(parts)
        ]
        greet(same_core + column + [(device[0], sibling[1]) for device in column] + members[1:])

        def wo_sends(start):
            for i in range(n_dp):
                target = (lax.rem(z + i, n_dp), e - part + z // hp)
                dst, sem = wo_out.at[lax.rem(z, hp), part], wo_r.at[lax.rem(z, hp), part]

                def far(i=i, target=target, dst=dst, sem=sem):
                    copy = remote(wo_in, dst, wo_s.at[i], sem, target)
                    if start:
                        copy.start()
                    else:
                        copy.wait_send()

                if i:
                    far()
                else:
                    pl.when(z // hp != part)(far)
                    if start:

                        @pl.when(z // hp == part)
                        def _(dst=dst, sem=sem):
                            pltpu.make_async_copy(wo_in, dst, sem).start()

        def wo_arrivals():
            for h in range(hp):
                for p in range(parts):
                    here = jnp.logical_and(part * hp + h == z, part == p)

                    @pl.when(here)
                    def _(h=h, p=p):
                        pltpu.make_async_copy(wo_in, wo_out.at[h, p], wo_r.at[h, p]).wait()

                    @pl.when(jnp.logical_not(here))
                    def _(h=h, p=p):
                        wait_recv(wo_out.at[h, p], wo_r.at[h, p], sibling)

        my_l = lax.rem(z, inner)
        matrices = [
            ExpertsIn(e_in[m], w_out[m], refs[4 * m : 4 * m + 4], n_dp, n_ex, inner)
            for m in range(count)
        ]
        wo_sends(True)
        shared_copies = []
        for i in range(1, n_dp):
            for m in range(3):
                copy = remote(
                    s_in[m].at[lax.rem(lax.rem(z + i, n_dp), inner)], s_out[m].at[e, z],
                    sh_s.at[m, i], sh_r.at[m, i], column[i - 1],
                )
                copy.start()
                shared_copies.append(copy)
        own = [
            pltpu.make_async_copy(s_in[m].at[my_l], s_out[m].at[e, z], local.at[m])
            for m in range(3)
        ]
        for copy in own:
            copy.start()
        matrices[0].begin()
        tok_all, gain_one, wa_ref, wl_ref, gain_lat, cos, sin, keep = att_in
        for move in moves:
            move.wait()
        wq_ref[...] = wa_ref[:, :, :, :wq_cols].reshape(width, wq_cols)
        for j in range(r // rl):
            block = wa_ref[:, :, j * rl : (j + 1) * rl, wq_cols:].reshape(KVR, we_cols)
            we_ref[:, j * we_cols : (j + 1) * we_cols] = block
        attend_forward(
            tok_all, gain_one, wq_ref, wl_ref, gain_lat, we_ref, cos, sin, keep, *att_out
        )
        wo_arrivals()
        kept_moves = stage(kept, kept_hbm, kept_sem)
        wo = wo_out[...].reshape(hp * DV, width)

        def project(i, carry):
            at = pl.ds(pl.multiple_of(i * 2 * rows, 2 * rows), 2 * rows)
            block = mm(att_out[7][at, :], wo).astype(BF)
            x_ref[pl.ds(2 * i, 2)] = block.reshape(2, rows, width)
            return carry

        lax.fori_loop(0, chips, project, 0)
        near = []
        for i in list(range(1, chips)) + [0]:
            chip = lax.rem(c + i, chips)
            copy = remote(
                x_ref.at[chip * 2 + 1 - k], from_sib.at[chip], near_s.at[i], near_r.at[i], sibling
            )
            copy.start()
            near.append(copy)
        far = []
        for i in range(1, chips):
            chip = lax.rem(c + i, chips)
            near[i - 1].wait_recv()
            out_buf[i] = (
                x_ref[chip * 2 + k].astype(F32) + from_sib[chip].astype(F32)
            ).astype(BF)
            copy = remote(out_buf.at[i], from_far.at[i], far_s.at[i], far_r.at[i], same_core[i - 1])
            copy.start()
            far.append(copy)
        near[chips - 1].wait_recv()
        res_ref[...] = x_ref[e].astype(F32) + from_sib[c].astype(F32) + tok_ref[...].astype(F32)
        for i in range(1, chips):
            far[i - 1].wait_recv()
            res_ref[...] += from_far[i].astype(F32)
        residual = res_ref[...]
        scale = lax.rsqrt(jnp.mean(residual * residual, axis=-1, keepdims=True) + norm_eps)
        xbuf[...] = (residual * scale * gain_ref[...]).astype(BF)
        relays = [
            Relay(xbuf, xcol_ref, x_sems, n_dp, n_ex, inner),
            Relay(cot_in, cot_out, co_sems, n_dp, n_ex, inner),
        ]
        relays[0].begin()
        relays[0].pass_on()
        relays[1].begin()
        for matrix in matrices[1:]:
            matrix.begin()
        for copy in own:
            copy.wait()
        for copy in shared_copies:
            copy.wait_recv()
        plane, to_sib = [], []
        for m in range(3):
            block = s_out[m].at[e]
            for i in range(1, chips):
                copy = remote(block, block, sp_s.at[m, i], sp_r.at[m, i], same_core[i - 1])
                copy.start()
                plane.append(copy)
            copy = remote(block, block, sf_s.at[m, 0], sf_r.at[m, 0], sibling)
            copy.start()
            to_sib.append(copy)
        for m in range(3):
            for i in range(1, chips):
                plane[m * (chips - 1) + i - 1].wait_recv()
                block = s_out[m].at[lax.rem(c + chips - i, chips) * 2 + k]
                copy = remote(block, block, sf_s.at[m, i], sf_r.at[m, i], sibling)
                copy.start()
                to_sib.append(copy)
        relays[1].pass_on()
        for matrix in matrices:
            matrix.pass_on()
        for copy in to_sib:
            copy.wait()
        for relay in relays:
            relay.end()
        for copy in plane + shared_copies + near + far:
            copy.wait_send()
        wo_sends(False)
        for move in kept_moves:
            move.wait()
        for matrix in matrices:
            matrix.end()

    dma = pltpu.SemaphoreType.DMA
    ff_s = shared[0].shape[2]
    scratch = []
    for _ in experts:
        scratch += ExpertsIn.scratch(n_dp)
    sds = jax.ShapeDtypeStruct
    kept = [
        sds((seq, width), BF),
        sds((seq, attend[3].shape[1]), F32),
        sds((seq, KVR), BF),
        sds((2, seq, 2 * DH), BF),
        sds((2, seq, 2 * DH), BF),
        sds((2, seq, DV), BF),
        sds((2, seq, 128), F32),
        sds((seq, 2 * DV), BF),
        sds((width, wq_cols), BF),
        sds((KVR, hp * (DH + DV)), BF),
        sds((hp, parts, r, width), BF),
    ]
    big = (0, 2, 3, 5, 6)
    outs = pl.pallas_call(
        kernel,
        out_shape=kept
        + [
            sds((rows, width), F32),
            sds((inner, rows, width), BF),
            sds((inner, rows, width), BF),
        ]
        + [ExpertsIn.out(w, n_dp, n_ex) for w in experts]
        + [sds((n_ex, n_dp, r, ff_s), BF)] * 3,
        in_specs=[ANY if j in big else VMEM for j in range(8)]
        + [ANY]
        + [VMEM] * 2
        + [ANY] * (4 + count),
        out_specs=[ANY] * 11 + [VMEM] + [ANY] * (5 + count),
        scratch_shapes=like([attend[j] for j in big])
        + like(kept)
        + [dma((5,)), dma((11,))]
        + [pltpu.VMEM((n_ex, rows, width), BF)]
        + [pltpu.VMEM((chips, rows, width), BF)] * 3
        + [pltpu.VMEM((rows, width), BF)]
        + [dma((chips,))] * 4
        + [dma((3, n_dp))] * 2
        + [dma((3, chips))] * 4
        + [dma((n_dp,)), dma((hp, parts)), dma((3,))]
        + Relay.scratch(inner) * 2
        + scratch,
        compiler_params=params(collective_id),
    )(*attend, w_out, tok, gain, cot, *experts, *shared)
    return outs[:8], outs[8:11], outs[11], outs[12], outs[13], outs[14 : 14 + count], outs[14 + count :]


def silu_parts(a):
    sig = 1.0 / (1.0 + jnp.exp(-a))
    return a * sig, sig * (1.0 + a * (1.0 - sig))


def dispatch(hot, x, cot, shared, weights, n_dp, n_ex, inner, collective_id):
    chips = n_ex // 2
    rows, width = x.shape
    ff = shared[0].shape[1]
    tile = 256

    per_far = hot.shape[0] // chips
    count = len(weights)

    def kernel(hot_ref, x_hbm, c_hbm, g_hbm, u_hbm, d_hbm, *refs):
        w_in, refs = refs[:count], refs[count:]
        o_ref, go_ref, w_out, refs = refs[0], refs[1], refs[2 : 2 + count], refs[2 + count :]
        results, refs = refs[:5], refs[5:]
        hot_v, x_v, c_v, g_v, u_v, d_v, hid, ga, gb, b_v, send, recv, loads, keep = refs[:14]
        out_ref, dx_ref, gg_ref, gu_ref, gd_ref = refs[14:19]
        results_sem, rest = refs[19], refs[20:]
        z, e, c, k, sibling, same_core, column = places(n_dp, n_ex)
        moves = [
            pltpu.make_async_copy(src, dst, loads.at[j])
            for j, (src, dst) in enumerate(
                [
                    (hot_ref, hot_v), (x_hbm, x_v), (c_hbm, c_v),
                    (g_hbm, g_v), (u_hbm, u_v), (d_hbm, d_v),
                ]
            )
        ]
        for copy in moves:
            copy.start()
        greet(same_core + [sibling] + column + [(device[0], sibling[1]) for device in column])
        matrices = [
            ExpertsIn(w_in[m], w_out[m], rest[4 * m : 4 * m + 4], n_dp, n_ex, inner)
            for m in range(count)
        ]
        for matrix in matrices:
            matrix.begin()
        copies = []
        for j, (source, target) in enumerate(((x_v, o_ref), (c_v, go_ref))):
            if not j:
                moves[0].wait()
            moves[1 + j].wait()
            for i in list(range(1, chips)) + [0]:
                block = mm(hot_v[i * per_far : (i + 1) * per_far, :], source[...])
                b_v[j, i] = block.astype(BF)
                if i:
                    copy = remote(
                        b_v.at[j, i], target.at[i], send.at[j, i], recv.at[j, i],
                        same_core[i - 1],
                    )
                else:
                    copy = pltpu.make_async_copy(b_v.at[j, 0], target.at[0], keep.at[j])
                copy.start()
                copies.append(copy)
        for copy in moves[3:]:
            copy.wait()

        def rows_of(i, carry):
            at = pl.ds(pl.multiple_of(i * tile, tile), tile)
            first = mm(x_v[at, :], g_v[...])
            second = mm(x_v[at, :], u_v[...])
            silu, slope = silu_parts(first)
            low = (silu * second).astype(BF)
            hid[at, :] = low
            out_ref[at, :] = mm_cols(low, d_v[...])
            back = mm(c_v[at, :], d_v[...])
            low_a = (back * second * slope).astype(BF)
            low_b = (back * silu).astype(BF)
            ga[at, :] = low_a
            gb[at, :] = low_b
            dx_ref[at, :] = mm_cols(low_a, g_v[...]) + mm_cols(low_b, u_v[...])
            return carry

        lax.fori_loop(0, rows // tile, rows_of, 0)

        def columns_of(j, carry):
            at = pl.ds(pl.multiple_of(j * tile, tile), tile)
            gg_ref[at, :] = mm_rows(x_v[:, at], ga[...]).astype(BF)
            gu_ref[at, :] = mm_rows(x_v[:, at], gb[...]).astype(BF)
            gd_ref[at, :] = mm_rows(c_v[:, at], hid[...]).astype(BF)
            return carry

        lax.fori_loop(0, width // tile, columns_of, 0)
        result_moves = stage([out_ref, dx_ref, gg_ref, gu_ref, gd_ref], results, results_sem)
        for matrix in matrices:
            matrix.pass_on()
        for copy in copies + result_moves:
            copy.wait()
        for matrix in matrices:
            matrix.end()

    dma = pltpu.SemaphoreType.DMA
    sds = jax.ShapeDtypeStruct
    vmem = pltpu.VMEM
    scratch = []
    for _ in weights:
        scratch += ExpertsIn.scratch(n_dp)
    results = [sds((rows, width), F32)] * 2 + [sds((width, ff), BF)] * 3
    outs = pl.pallas_call(
        kernel,
        out_shape=[sds((chips, per_far, width), BF)] * 2
        + [ExpertsIn.out(weight, n_dp, n_ex) for weight in weights]
        + results,
        in_specs=[ANY] * (6 + count),
        out_specs=[ANY] * (7 + count),
        scratch_shapes=[vmem(hot.shape, BF)]
        + [vmem((rows, width), BF)] * 2
        + [vmem((width, ff), BF)] * 3
        + [vmem((rows, ff), BF)] * 3
        + [vmem((2, chips, per_far, width), BF)]
        + [dma((2, chips)), dma((2, chips)), dma((6,)), dma((2,))]
        + like(results)
        + [dma((5,))]
        + scratch,
        compiler_params=params(collective_id),
    )(hot, x, cot, *shared, *weights)
    return outs[:2], outs[2 : 2 + count], outs[2 + count], outs[3 + count], outs[4 + count :]


def experts_run(x_in, grad_in, weights, router, n_dp, n_ex, inner, collective_id):
    chips = n_ex // 2
    n_slots, width = x_in.shape
    ff = weights[0].shape[1]
    per_far = n_slots // chips
    r = width // (n_dp * n_ex)
    tile = per_far
    span = n_dp * r
    n_experts = inner * chips

    def kernel(*refs):
        in_hbm, refs = refs[:6], refs[6:]
        dx_out, dots_out, rows_out, back_out, g_out, refs = *refs[:4], refs[4:6], refs[6:]
        x_v, s_v, wg, wu, wd, route, a_v, b_v, h_v, dx_v, total, stage, dots_v = refs[:13]
        loads, send, recv, d_send, d_recv, local, rows_sem, out_sem = refs[13:21]
        z, e, c, k, sibling, same_core, column = places(n_dp, n_ex)
        moves = [
            pltpu.make_async_copy(src, dst, loads.at[j])
            for j, (src, dst) in enumerate(zip(in_hbm, (x_v, s_v, wg, wu, wd, route)))
        ]
        for j in (5, 0, 2, 3, 4, 1):
            moves[j].start()
        greet(same_core + [sibling] + column + [(device[0], sibling[1]) for device in column])
        back = ExpertsBack(total, back_out, refs[21:], n_dp, n_ex, inner)
        expert = c * inner + lax.rem(z, inner)
        for j in (5, 0, 2, 3, 4, 1):
            moves[j].wait()

        def forward(i, carry):
            at = pl.ds(pl.multiple_of(i * tile, tile), tile)
            x = x_v[at, :]
            logits = mm(x, route[...])
            lane = lax.broadcasted_iota(jnp.int32, logits.shape, 1)
            logits = jnp.where(lane < n_experts, logits, masked_score)
            chances = jnp.exp(logits - jnp.max(logits, axis=-1, keepdims=True))
            gate = jnp.sum(jnp.where(lane == expert, chances, 0.0), axis=-1, keepdims=True)
            gate = gate / jnp.sum(chances, axis=-1, keepdims=True)
            first = mm(x, wg[...])
            second = mm(x, wu[...])
            a_v[at, :] = first.astype(BF)
            b_v[at, :] = second.astype(BF)
            hid = (silu_parts(first)[0] * second).astype(BF)
            h_v[at, :] = hid
            rows = mm_cols(hid, wd[...]).astype(BF)
            dx_v[i] = rows
            grad = s_v[at, :].astype(F32)
            dots = jnp.sum(grad * rows.astype(F32), axis=-1, keepdims=True)
            dots_v[i] = jnp.broadcast_to(dots, (tile, 128)).astype(BF)
            s_v[at, :] = (gate * grad).astype(BF)
            pltpu.make_async_copy(dx_v.at[i], rows_out.at[i], rows_sem.at[i]).start()
            return carry

        lax.fori_loop(0, chips, forward, 0)
        dot_copies = []
        for i in range(1, chips):
            copy = remote(
                dots_v.at[i], dots_out.at[i], d_send.at[i], d_recv.at[i], same_core[chips - i - 1]
            )
            copy.start()
            dot_copies.append(copy)
        copy = pltpu.make_async_copy(dots_v.at[0], dots_out.at[0], local.at[0])
        copy.start()
        dot_copies.append(copy)

        def down_rows(t, carry):
            j = lax.rem(t + (1 - k) * (n_ex // 2), n_ex)
            at = pl.ds(pl.multiple_of(j * span, span), span)
            block = mm_rows(s_v[:, at], h_v[...]).astype(BF)
            total[j] = block.reshape(n_dp, r, ff)
            return carry

        lax.fori_loop(0, n_ex, down_rows, 0)
        back.begin()

        def hidden_rows(i, carry):
            at = pl.ds(pl.multiple_of(i * tile, tile), tile)
            grad = mm(s_v[at, :], wd[...])
            silu, slope = silu_parts(a_v[at, :].astype(F32))
            second = b_v[at, :].astype(F32)
            a_v[at, :] = (grad * second * slope).astype(BF)
            b_v[at, :] = (grad * silu).astype(BF)
            return carry

        lax.fori_loop(0, chips, hidden_rows, 0)
        back.pass_on()
        copies = []
        for i in list(range(1, chips)) + [0]:
            at = slice(i * per_far, (i + 1) * per_far)
            block = mm_cols(a_v[at, :], wg[...]) + mm_cols(b_v[at, :], wu[...])
            pltpu.make_async_copy(dx_v.at[i], rows_out.at[i], rows_sem.at[i]).wait()
            dx_v[i] = block.astype(BF)
            if i:
                copy = remote(
                    dx_v.at[i], dx_out.at[i], send.at[i], recv.at[i], same_core[chips - i - 1]
                )
            else:
                copy = pltpu.make_async_copy(dx_v.at[0], dx_out.at[0], local.at[1])
            copy.start()
            copies.append(copy)

        def other_rows(j, carry):
            at = pl.ds(pl.multiple_of(j * span, span), span)
            for m, side in enumerate((a_v, b_v)):

                @pl.when(j > 0)
                def _(m=m):
                    pltpu.make_async_copy(stage.at[m], g_out[m].at[j - 1], out_sem.at[m]).wait()

                block = mm_rows(x_v[:, at], side[...]).astype(BF)
                stage[m] = block.reshape(n_dp, r, ff)
                pltpu.make_async_copy(stage.at[m], g_out[m].at[j], out_sem.at[m]).start()
            return carry

        lax.fori_loop(0, n_ex, other_rows, 0)
        for m in range(2):
            pltpu.make_async_copy(stage.at[m], g_out[m].at[n_ex - 1], out_sem.at[m]).wait()
        for copy in copies + dot_copies:
            copy.wait()
        back.end()

    dma = pltpu.SemaphoreType.DMA
    sds = jax.ShapeDtypeStruct
    vmem = pltpu.VMEM
    total = sds((n_ex, n_dp, r, ff), BF)
    blocks = sds((chips, per_far, width), BF)
    dots = sds((chips, per_far, 128), BF)
    outs = pl.pallas_call(
        kernel,
        out_shape=[blocks, dots, blocks, ExpertsBack.out(total, n_dp, inner), total, total],
        in_specs=[ANY] * 6,
        out_specs=[ANY] * 6,
        scratch_shapes=[vmem((n_slots, width), BF)] * 2
        + [vmem((width, ff), BF)] * 3
        + [vmem((width, 128), BF)]
        + [vmem((n_slots, ff), BF)] * 3
        + [
            vmem(blocks.shape, BF),
            vmem(total.shape, BF),
            vmem((2, n_dp, r, ff), BF),
            vmem(dots.shape, BF),
            dma((6,)),
        ]
        + [dma((chips,))] * 4
        + [dma((2,)), dma((chips,)), dma((2,))]
        + ExpertsBack.scratch(total, n_dp, inner),
        compiler_params=params(collective_id),
    )(x_in, grad_in, *weights, router)
    return outs[0], outs[1], outs[2], outs[3], outs[4:]


class ExpertsBack:
    @staticmethod
    def scratch(total, n_dp, inner):
        n_ex, _, r, ff = total.shape
        dma = pltpu.SemaphoreType.DMA
        hh = n_ex // 2
        return [
            pltpu.VMEM((hh, n_dp, r, ff), BF),
            pltpu.VMEM((hh, n_dp, r, ff), BF),
            dma((hh,)),
            dma((hh,)),
            dma((hh,)),
            dma((hh, n_dp)),
            dma((n_dp // inner, 2, 2, hh)),
        ]

    @staticmethod
    def out(total, n_dp, inner):
        n_ex, _, r, ff = total.shape
        return jax.ShapeDtypeStruct((n_dp // inner, 2, n_ex, r, ff), BF)

    def __init__(self, total, out, scratch, n_dp, n_ex, inner):
        self.total, self.out, self.n_dp, self.inner = total, out, n_dp, inner
        self.own, self.sib, self.near_s, self.near_r, self.load, self.send, self.recv = scratch
        self.z, self.e, self.c, self.k, self.sibling, _, _ = places(n_dp, n_ex)
        self.hh = n_ex // 2

    def near(self, j):
        return remote(
            self.total.at[(1 - self.k) * self.hh + j], self.sib.at[j],
            self.near_s.at[j], self.near_r.at[j], self.sibling,
        )

    def loads(self, j):
        return pltpu.make_async_copy(
            self.total.at[self.k * self.hh + j], self.own.at[j], self.load.at[j]
        )

    def begin(self):
        for j in range(self.hh):
            self.near(j).start()
            self.loads(j).start()

    def route(self, j, i):
        d = lax.rem(self.z + i, self.n_dp)
        expert = lax.rem(self.z, self.inner)
        o = self.z // self.inner
        dst = self.out.at[o, lax.rem(expert, 2), self.k * self.hh + j]
        sem = self.recv.at[o, lax.rem(expert, 2), self.k, j]
        return self.own.at[j, d], dst, sem, (d, 2 * self.c + expert // 2)

    def stay(self, j):
        src, dst, sem, _ = self.route(j, 0)
        return pltpu.make_async_copy(src, dst, sem)

    def go(self, j, i):
        src, dst, sem, device = self.route(j, i)
        return remote(src, dst, self.send.at[j, i], sem, device)

    def here(self):
        return lax.rem(self.z, self.inner) // 2 == self.k

    def pass_on(self):
        for j in range(self.hh):
            self.near(j).wait_recv()
            self.loads(j).wait()
            for d in range(self.n_dp):
                self.own[j, d] = (
                    self.own[j, d].astype(F32) + self.sib[j, d].astype(F32)
                ).astype(BF)
            for i in range(1, self.n_dp):
                self.go(j, i).start()
            pl.when(self.here())(lambda j=j: self.stay(j).start())
            pl.when(jnp.logical_not(self.here()))(lambda j=j: self.go(j, 0).start())

    def end(self):
        for j in range(self.hh):
            self.near(j).wait_send()
            for i in range(1, self.n_dp):
                self.go(j, i).wait_send()
            pl.when(jnp.logical_not(self.here()))(lambda j=j: self.go(j, 0).wait_send())
        for o in range(self.n_dp // self.inner):
            for i in range(2):
                for h in range(2):
                    source = o * self.inner + 2 * self.k + i
                    here = jnp.logical_and(source == self.z, self.k == h)
                    for j in range(self.hh):
                        region = self.out.at[o, i, h * self.hh + j]
                        sem = self.recv.at[o, i, h, j]

                        @pl.when(here)
                        def _(region=region, sem=sem, j=j):
                            pltpu.make_async_copy(self.own.at[j, self.z], region, sem).wait()

                        @pl.when(jnp.logical_not(here))
                        def _(region=region, sem=sem):
                            wait_recv(region, sem, self.sibling)


def rms_back(x, gain, grad):
    root = lax.rsqrt(jnp.mean(x * x, axis=-1, keepdims=True) + norm_eps)
    scaled = grad * gain
    along = jnp.mean(x * scaled, axis=-1, keepdims=True)
    return root * scaled - x * (root * root * root) * along, grad * x * root


def backward_exchange(
    grad, attend, hidden, latent_low, own, out, shared, totals, n_dp, n_ex, inner, collective_id
):
    chips = n_ex // 2
    rows, width = grad.shape
    seq = n_ex * rows
    extra = len(totals)
    wq, we = attend[1], attend[2]
    lat_cols = KVR + 2 * DR
    r = width // (n_dp * n_ex)
    rl = KVR // (n_dp * n_ex)
    parts = DV // r
    hp = n_dp // parts
    n_dev = n_dp * n_ex
    wq_cols = wq.shape[1]
    we_cols = rl * we.shape[1] // r
    head_cols = wq_cols + we_cols
    given_arrays = [*attend, hidden, latent_low, *own]
    big = [j for j, array in enumerate(given_arrays) if array.shape[0] > 1]

    def kernel(*refs):
        grad_ref, given, refs = refs[0], list(refs[1:22]), refs[22:]
        out_ref, sh_in, refs = refs[0], refs[1:4], refs[4:]
        t_refs, refs = refs[:extra], refs[extra:]
        tok_out, vec_out, pack_out, heads_mid, heads_out, wout_out, out_got = refs[:7]
        sh_out, back_refs, refs = refs[7:10], refs[10 : 10 + extra], refs[10 + extra :]
        gbuf, att_tmp, refs = refs[0], refs[1:8], refs[8:]
        part_l, bufs, sums, refs = refs[0], refs[1:7], refs[7:9], refs[9:]
        hsrc, wsrc, pack, psib, pout, pfar, psum, pbuf, vec, vbuf, vzbuf = refs[:11]
        refs = refs[11:]
        t_s, t_r, ts_s, ts_r, local = refs[:5]
        sems, refs = refs[5:13], refs[13:]
        (
            h_s, h_r, hz_s, hz_r, w_s, w_r, pn_s, pn_r, pf_s, pf_r, pc_s, pc_r, s_s, s_r,
            v_s, v_r, vz_s, vz_r, o_s, o_r,
        ) = refs[:20]
        staged, stage_sem, rest = refs[20 : 20 + len(big)], refs[20 + len(big)], refs[21 + len(big) :]
        moves = stage([given[j] for j in big], staged, stage_sem)
        for j, ref in zip(big, staged):
            given[j] = ref
        att_in, hidden_ref, low_ref = given[:11], given[11], given[12]
        wl_ref, lat_ref, tok_ref, gain_ref, glat_ref, gnat_ref, router_ref, gtwo_ref = given[13:]
        x_refs = (gbuf, part_l)
        group = column_group(lax.axis_index("dp"), lax.axis_index("expert"), inner)
        z, e, c, k, sibling, same_core, column = places(n_dp, n_ex)
        plane = [(z, lax.rem(e + i, n_ex)) for i in range(1, n_ex)]
        part = lax.rem(e, parts)
        members = [
            (lax.rem(z + i, n_dp), e - part + lax.rem(part + j, parts))
            for i in range(n_dp)
            for j in range(parts)
        ]
        greet(plane + column + [(d[0], sibling[1]) for d in column] + members[1:])
        backs = [
            ExpertsBack(t_refs[m], back_refs[m], rest[7 * m : 7 * m + 7], n_dp, n_ex, inner)
            for m in range(extra)
        ]
        gather, to_sib, others = [], [], []
        for i in range(1, chips):
            copy = remote(grad_ref, gbuf.at[e], t_s.at[i], t_r.at[i], same_core[i - 1])
            copy.start()
            gather.append(copy)
        copy = remote(grad_ref, gbuf.at[e], ts_s.at[0], ts_r.at[0], sibling)
        copy.start()
        to_sib.append(copy)
        keep = pltpu.make_async_copy(grad_ref, gbuf.at[e], local.at[0])
        keep.start()
        for back in backs:
            back.begin()
        for m in range(3):
            for i in range(1, n_dp):
                copy = remote(
                    sh_in[m].at[lax.rem(z + i, n_dp)], sh_out[m].at[z],
                    s_s.at[m, i], s_r.at[m, i], column[i - 1],
                )
                copy.start()
                others.append(copy)
            copy = pltpu.make_async_copy(sh_in[m].at[z], sh_out[m].at[z], local.at[1 + m])
            copy.start()
            others.append(copy)
        mine = lax.rem(z, inner)
        for i in range(1, inner):
            copy = remote(
                out_ref.at[lax.rem(mine + i, inner)], out_got.at[mine], o_s.at[i], o_r.at[i],
                group[i],
            )
            copy.start()
            others.append(copy)
        copy = pltpu.make_async_copy(out_ref.at[mine], out_got.at[mine], local.at[5])
        copy.start()
        others.append(copy)
        for i in range(1, chips):
            gather[i - 1].wait_recv()
            block = gbuf.at[lax.rem(c + chips - i, chips) * 2 + k]
            copy = remote(block, block, ts_s.at[i], ts_r.at[i], sibling)
            copy.start()
            to_sib.append(copy)
        for back in backs:
            back.pass_on()
        keep.wait()
        for copy in to_sib:
            copy.wait_recv()
        for copy in gather + to_sib:
            copy.wait_send()
        gat, grad_wout, dk, dv, grad_query, grad_expanded, grad_rope = att_tmp
        for move in moves:
            move.wait()
        attend_backward(gbuf, *att_in, *att_tmp)

        wsrc[...] = grad_wout[...].astype(BF).reshape(hp, parts, r, width)

        def wout_sends(start):
            for h in range(hp):
                for p in range(parts):
                    target = (part * hp + h, e - part + p)
                    here = jnp.logical_and(part * hp + h == z, p == part)

                    def far(h=h, p=p, target=target):
                        copy = remote(
                            wsrc.at[h, p], wout_out.at[z], w_s.at[h, p], w_r.at[z], target
                        )
                        if start:
                            copy.start()
                        else:
                            copy.wait_send()

                    pl.when(jnp.logical_not(here))(far)
                    if start:

                        @pl.when(here)
                        def _(h=h, p=p):
                            pltpu.make_async_copy(
                                wsrc.at[h, p], wout_out.at[z], w_r.at[z]
                            ).start()

        wout_sends(True)

        def spread(i, carry):
            at = pl.ds(pl.multiple_of(i * 2 * rows, 2 * rows), 2 * rows)
            block = mm_cols(grad_query[at, :], att_in[1][...]).astype(BF)
            gbuf[pl.ds(2 * i, 2)] = block.reshape(2, rows, width)
            block = mm_cols(grad_expanded[at, :], att_in[2][...]).astype(BF)
            part_l[pl.ds(2 * i, 2), :, :KVR] = block.reshape(2, rows, KVR)
            block = grad_rope[at, :].astype(BF)
            part_l[pl.ds(2 * i, 2), :, KVR:] = block.reshape(2, rows, 2 * DR)
            return carry

        lax.fori_loop(0, chips, spread, 0)
        near, far = {}, {}
        for i in list(range(1, chips)) + [0]:
            chip = lax.rem(c + i, chips)
            for j in range(2):
                near[i, j] = remote(
                    x_refs[j].at[chip * 2 + 1 - k],
                    bufs[3 * j].at[chip],
                    sems[4 * j].at[i],
                    sems[4 * j + 1].at[i],
                    sibling,
                )
                near[i, j].start()
        for i in range(1, chips):
            chip = lax.rem(c + i, chips)
            for j in range(2):
                from_sib, out_buf, from_far = bufs[3 * j : 3 * j + 3]
                near[i, j].wait_recv()
                out_buf[i] = (
                    x_refs[j][chip * 2 + k].astype(F32) + from_sib[chip].astype(F32)
                ).astype(BF)
                far[i, j] = remote(
                    out_buf.at[i],
                    from_far.at[i],
                    sems[4 * j + 2].at[i],
                    sems[4 * j + 3].at[i],
                    same_core[i - 1],
                )
                far[i, j].start()

        per_tile = 256 // r

        def wq_rows(i, carry):
            at = pl.ds(pl.multiple_of(i * 256, 256), 256)
            block = mm_rows(hidden_ref[:, at], grad_query[...]).astype(BF)
            hsrc[pl.ds(i * per_tile, per_tile), :, :wq_cols] = block.reshape(
                per_tile, r, wq_cols
            )
            return carry

        lax.fori_loop(0, width // 256, wq_rows, 0)
        grad_we = mm_rows(low_ref[...], grad_expanded[...]).astype(BF)
        for j in range(r // rl):
            block = grad_we[:, j * we_cols : (j + 1) * we_cols]
            hsrc[:, j * rl : (j + 1) * rl, wq_cols:] = block.reshape(n_dev, rl, we_cols)
        heads_far = []
        for i in range(1, n_ex):
            for d in range(n_dp):
                copy = remote(
                    hsrc.at[d * n_ex + lax.rem(e + i, n_ex)], heads_mid.at[d, e],
                    h_s.at[i, d], h_r.at[i, d], plane[i - 1],
                )
                copy.start()
                heads_far.append(copy)
        for d in range(n_dp):
            copy = pltpu.make_async_copy(
                hsrc.at[d * n_ex + e], heads_mid.at[d, e], h_r.at[0, d]
            )
            copy.start()
            copy.wait()
        for j in range(2):
            near[0, j].wait_recv()
            sums[j][...] = x_refs[j][e].astype(F32) + bufs[3 * j][c].astype(F32)
        for i in range(1, chips):
            for j in range(2):
                far[i, j].wait_recv()
                sums[j][...] += bufs[3 * j + 2][i].astype(F32)

        at = pl.ds(pl.multiple_of(e * rows, rows), rows)
        cos, sin = att_in[3][at, :], att_in[4][at, :]
        lat_grad, lat_gain = rms_back(lat_ref[:, :KVR], glat_ref[...], sums[1][:, :KVR])
        rope = turn(sums[1][:, KVR:], cos, sin, -1.0)
        lane = lax.broadcasted_iota(jnp.int32, rope.shape, 1)
        rope = jnp.where(lane < DR, rope, 0.0)
        low = jnp.concatenate([lat_grad, rope], axis=1).astype(BF)
        total = sums[0][...] + mm_cols(low, wl_ref[:, :lat_cols])
        tok_grad, tok_gain = rms_back(tok_ref[...].astype(F32), gain_ref[...], total)
        tok_out[...] = gnat_ref[...] + tok_grad
        vec[...] = jnp.zeros_like(vec)
        vec[0:1, :] = jnp.sum(tok_gain, axis=0, keepdims=True)
        vec[1:2, :] = gtwo_ref[...]
        vec[2:3, :KVR] = jnp.sum(lat_gain, axis=0, keepdims=True)
        vec_far = []
        for i in range(1, n_ex):
            copy = remote(vec, vbuf.at[i], v_s.at[i], v_r.at[i], plane[i - 1])
            copy.start()
            vec_far.append(copy)
        for d in range(n_dp):
            block = hidden_ref[at, d * n_ex * r : (d + 1) * n_ex * r]
            block = mm_rows(block, low).reshape(n_ex, r, lat_cols)
            pack[:, d * r : (d + 1) * r, :KVR] = block[:, :, :KVR].astype(BF)
            block = block[:, :, KVR:] + router_ref[:, d * r : (d + 1) * r].astype(F32)
            pack[:, d * r : (d + 1) * r, KVR:] = block.astype(BF)
        pack_near, pack_far = [], []
        for i in list(range(1, chips)) + [0]:
            chip = lax.rem(c + i, chips)
            copy = remote(pack.at[chip * 2 + 1 - k], psib.at[chip], pn_s.at[i], pn_r.at[i], sibling)
            copy.start()
            pack_near.append(copy)
        for copy in heads_far:
            copy.wait_recv()
        heads_col = []
        for i in range(1, n_dp):
            d = lax.rem(z + i, n_dp)
            copy = remote(
                heads_mid.at[d], heads_out.at[z], hz_s.at[i], hz_r.at[i], column[i - 1]
            )
            copy.start()
            heads_col.append(copy)
        copy = pltpu.make_async_copy(heads_mid.at[z], heads_out.at[z], local.at[4])
        copy.start()
        heads_col.append(copy)
        for i in range(1, chips):
            chip = lax.rem(c + i, chips)
            pack_near[i - 1].wait_recv()
            pout[i] = (pack[chip * 2 + k].astype(F32) + psib[chip].astype(F32)).astype(BF)
            copy = remote(pout.at[i], pfar.at[i], pf_s.at[i], pf_r.at[i], same_core[i - 1])
            copy.start()
            pack_far.append(copy)
        for copy in vec_far:
            copy.wait_recv()
            copy.wait_send()
        for i in range(1, n_ex):
            vec[...] += vbuf[i]
        vec_col = []
        for i in range(1, n_dp):
            copy = remote(vec, vzbuf.at[i], vz_s.at[i], vz_r.at[i], column[i - 1])
            copy.start()
            vec_col.append(copy)
        pack_near[chips - 1].wait_recv()
        total = pack[e].astype(F32) + psib[c].astype(F32)
        for i in range(1, chips):
            pack_far[i - 1].wait_recv()
            total = total + pfar[i].astype(F32)
        psum[...] = total.astype(BF).reshape(n_dp, r, lat_cols)
        pack_col = []
        for i in range(1, n_dp):
            copy = remote(
                psum.at[lax.rem(z + i, n_dp)], pbuf.at[i], pc_s.at[i], pc_r.at[i], column[i - 1]
            )
            copy.start()
            pack_col.append(copy)
        result = vec[...]
        for i in range(1, n_dp):
            vec_col[i - 1].wait_recv()
            result = result + vzbuf[i]
        vec_out[...] = result
        result = psum[z].astype(F32)
        for i in range(1, n_dp):
            pack_col[i - 1].wait_recv()
            result = result + pbuf[i].astype(F32)
        pack_out[...] = result

        for i in range(n_dp):
            here = jnp.logical_and(z // hp == part, z == i)

            @pl.when(here)
            def _(i=i):
                pltpu.make_async_copy(
                    wsrc.at[lax.rem(z, hp), part], wout_out.at[i], w_r.at[i]
                ).wait()

            @pl.when(jnp.logical_not(here))
            def _(i=i):
                wait_recv(wout_out.at[i], w_r.at[i], sibling)

        wout_sends(False)
        for copy in list(near.values()) + list(far.values()) + heads_far:
            copy.wait_send()
        for copy in pack_near + pack_far + vec_col + pack_col:
            copy.wait_send()
        for copy in heads_col + others:
            copy.wait()
        for back in backs:
            back.end()

    dma = pltpu.SemaphoreType.DMA
    sds = jax.ShapeDtypeStruct
    vmem = pltpu.VMEM
    scratch = [
        vmem((n_ex, rows, width), BF),
        vmem((seq, 2 * DV), BF),
        vmem((2 * DV, width), F32),
        vmem((seq, 2 * DH), F32),
        vmem((seq, DV), F32),
        vmem((seq, wq.shape[1]), BF),
        vmem((seq, we.shape[1]), BF),
        vmem((seq, 2 * DR), F32),
        vmem((n_ex, rows, lat_cols), BF),
    ]
    scratch += [vmem((chips, rows, width), BF)] * 3 + [vmem((chips, rows, lat_cols), BF)] * 3
    scratch += [
        vmem((rows, width), F32),
        vmem((rows, lat_cols), F32),
        vmem((n_dev, r, head_cols), BF),
        vmem((hp, parts, r, width), BF),
        vmem((n_ex, n_dp * r, lat_cols), BF),
        vmem((chips, n_dp * r, lat_cols), BF),
        vmem((chips, n_dp * r, lat_cols), BF),
        vmem((chips, n_dp * r, lat_cols), BF),
        vmem((n_dp, r, lat_cols), BF),
        vmem((n_dp, r, lat_cols), BF),
        vmem((8, width), F32),
        vmem((n_ex, 8, width), F32),
        vmem((n_dp, 8, width), F32),
    ]
    scratch += [dma((chips,))] * 4 + [dma((6,))] + [dma((chips,))] * 8
    scratch += [dma((n_ex, n_dp))] * 2 + [dma((n_dp,))] * 2 + [dma((hp, parts)), dma((n_dp,))]
    scratch += [dma((chips,))] * 4 + [dma((n_dp,))] * 2 + [dma((3, n_dp))] * 2
    scratch += [dma((n_ex,))] * 2 + [dma((n_dp,))] * 2 + [dma((inner,))] * 2
    scratch += like([given_arrays[j] for j in big]) + [dma((len(big),))]
    for total in totals:
        scratch += ExpertsBack.scratch(total, n_dp, inner)
    outs = pl.pallas_call(
        kernel,
        out_shape=[
            sds((rows, width), F32),
            sds((8, width), F32),
            sds((r, lat_cols), F32),
            sds((n_dp, n_ex, r, head_cols), BF),
            sds((n_dp, n_ex, r, head_cols), BF),
            sds((n_dp, r, width), BF),
            sds(out.shape, BF),
        ]
        + [sds(array.shape, BF) for array in shared]
        + [ExpertsBack.out(total, n_dp, inner) for total in totals],
        in_specs=[ANY]
        + [ANY if j in big else VMEM for j in range(21)]
        + [ANY] * (4 + extra),
        out_specs=[VMEM] * 3 + [ANY] * (7 + extra),
        scratch_shapes=scratch,
        compiler_params=params(collective_id),
    )(grad, *attend, hidden, latent_low, *own, out, *shared, *totals)
    return outs[:3], outs[4], outs[5], outs[6], outs[7:10], outs[10:]


def shards(
    tokens,
    cotangent,
    lengths,
    routes,
    place_order,
    attn_gain,
    w_query,
    w_latent,
    latent_gain,
    w_expand,
    w_out,
    ffn_gain,
    w_router,
    shared_gate,
    shared_up,
    shared_down,
    expert_gate,
    expert_up,
    expert_down,
):
    rows, width = tokens.shape
    n_dp = lax.axis_size("dp")
    n_ex = lax.axis_size("expert")
    chips = n_ex // 2
    z = lax.axis_index("dp")
    e = lax.axis_index("expert")
    chip = e // 2
    n_experts = w_router.shape[1]
    top_k = routes.shape[1]
    capacity = (rows * top_k * 5 + 4 * n_experts - 1) // (4 * n_experts)
    cap = (capacity + 15) // 16 * 16
    seq = rows * n_ex
    r = w_query.shape[0]
    rl = w_expand.shape[0]
    hp = H // n_ex
    parts = DV // r
    heads = [
        (d * n_ex + (j // parts) * parts) * r // DV
        for j in range(n_ex)
        for d in range(j % parts * hp, j % parts * hp + hp)
    ]
    heads_back = [heads.index(h) for h in range(H)]
    inner = n_experts // chips
    my_local = lax.rem(z, inner)
    ff_e = expert_gate.shape[2]
    ff_s = shared_gate.shape[1] // inner
    lat = KVR + DR
    head_cols = hp * (DH + DR)
    kv_cols = hp * (DH + DV)

    def to_owner_order(values):
        cut = values.reshape(values.shape[0], n_dp, n_ex, r)
        return cut.transpose(0, 2, 1, 3).reshape(values.shape)

    def from_owner_order(values):
        cut = values.reshape(values.shape[0], n_ex, n_dp, r)
        return cut.transpose(0, 2, 1, 3).reshape(values.shape)

    def pick(values, index, axis=0):
        return lax.dynamic_index_in_dim(values, index, axis, keepdims=False)

    wq_send = jnp.take(w_query.reshape(r, H, DH + DR), jnp.array(heads), axis=1)
    wq_send = wq_send.reshape(r, n_ex, hp, DH + DR)
    wq_send = jnp.concatenate(
        [
            wq_send[..., :DH].reshape(r, n_ex, hp * DH),
            wq_send[..., DH:].reshape(r, n_ex, hp * DR),
        ],
        axis=-1,
    ).transpose(1, 0, 2)
    we_send = jnp.take(w_expand.reshape(rl, H, DH + DV), jnp.array(heads), axis=1)
    we_cols = rl * kv_cols // r
    we_send = we_send.reshape(rl, n_ex, r // rl, we_cols).transpose(1, 2, 0, 3)
    we_send = we_send.reshape(n_ex, r, we_cols)
    wa_send = jnp.concatenate([wq_send, we_send], axis=-1)
    slot_own = slot_places(routes, place_order[0], capacity)
    slot_place = jnp.where(slot_own >= 0, slot_own - routes * capacity, -1)
    slot_cols = 2 * rows * top_k // r
    slot_pack = jnp.stack([routes, slot_place]).astype(BF).reshape(2, r, slot_cols // 2)
    small_cols = lat + n_experts + 3
    pack_cols = (small_cols + slot_cols + 127) // 128 * 128
    pack = jnp.concatenate(
        [
            w_latent,
            w_router,
            attn_gain[:, None],
            ffn_gain[:, None],
            jnp.pad(latent_gain, (0, r - rl))[:, None],
            slot_pack[0],
            slot_pack[1],
            jnp.zeros((r, pack_cols - small_cols - slot_cols), BF),
        ],
        axis=1,
    )
    cot_owner = to_owner_order(cotangent)
    tok_all, wa_all, pk_all = first_exchange(tokens, wa_send, pack, n_dp, n_ex, 1)
    pk_flat = pk_all.reshape(width, pack_cols)
    w_lat = pk_flat[:, :lat]
    gain_one = pk_flat[:, lat + n_experts].astype(F32)
    gain_two = pk_all[..., lat + n_experts + 1].transpose(1, 0, 2).reshape(width).astype(F32)
    router = pk_all[..., lat : lat + n_experts].transpose(1, 0, 2, 3).reshape(width, n_experts)
    gain_lat = (
        pk_all[..., lat + n_experts + 2].reshape(n_dp * n_ex, r)[:, :rl].reshape(KVR).astype(F32)
    )
    slots_all = n_experts * capacity
    slot_col = pick(pk_all[..., small_cols : small_cols + slot_cols], e, 1)
    slot_col = lax.dynamic_slice_in_dim(slot_col, z - my_local, inner, 0).astype(jnp.int32)
    slot_col = slot_col.reshape(inner, r, 2, slot_cols // 2).transpose(2, 0, 1, 3)
    slot_col = slot_col.reshape(2, inner, rows, top_k)
    slot_ids = jnp.where(
        slot_col[1] >= 0,
        slot_col[0] * capacity + slot_col[1] + (jnp.arange(inner) * slots_all)[:, None, None],
        -1,
    ).reshape(inner * rows, top_k)
    place = jnp.arange(cap)
    far_experts = [lax.rem(chip + m, chips) * inner + my_local for m in range(chips)]
    wanted = (
        jnp.stack(far_experts)[:, None, None] * capacity
        + (jnp.arange(inner) * slots_all)[None, :, None]
        + place[None, None, :]
    )
    wanted = jnp.where(place[None, None, :] < capacity, wanted, -2).reshape(-1)
    n_slots = wanted.shape[0]
    per_far = n_slots // chips
    hot = sum((wanted[:, None] == slot_ids[None, :, j]).astype(BF) for j in range(top_k))
    hot_t = sum((slot_ids[:, j][:, None] == wanted[None, :]).astype(BF) for j in range(top_k))

    positions = jnp.arange(seq)
    lane = jnp.arange(2 * DR) % (DR // 2)
    angles = positions.astype(F32)[:, None] * (10000.0 ** (-(lane.astype(F32) * 2.0) / DR))[None, :]
    cos_wide, sine_wide = jnp.cos(angles), jnp.sin(angles)
    keep = (positions < lengths[0]).astype(F32)[None]
    attend_out, (wq, wexp, wo_rows), residual, x_col, cot_col, (wg,), shared_w = forward_exchange(
        [tok_all, gain_one[None], wa_all, pk_flat, gain_lat[None], cos_wide, sine_wide, keep],
        to_owner_order(w_out),
        to_owner_order(tokens),
        gain_two[None],
        cot_owner,
        [expert_gate.reshape(-1, n_ex, r, ff_e)],
        [w.reshape(r, inner, ff_s).transpose(1, 0, 2) for w in (shared_gate, shared_up, shared_down)],
        n_dp,
        n_ex,
        inner,
        2,
    )
    hidden_one, latent_raw, latent_low, qcat, kcat, value, lse, attended = attend_out
    wo_rows = wo_rows.reshape(hp * DV, width)
    cot_col = cot_col.reshape(inner * rows, width)
    hidden_two = pick(x_col, my_local)
    x_col = x_col.reshape(inner * rows, width)

    (x_in, grad_in), (wu, wd), shared_out, shared_dx, shared_grads = dispatch(
        hot,
        x_col,
        cot_col,
        [w.reshape(width, ff_s) for w in shared_w],
        [w.reshape(-1, n_ex, r, ff_e) for w in (expert_up, expert_down)],
        n_dp,
        n_ex,
        inner,
        8,
    )
    x_in = x_in.reshape(n_slots, width)
    grad_in = grad_in.reshape(n_slots, width)
    wg, wu, wd = (w.reshape(width, ff_e) for w in (wg, wu, wd))

    def probs_of(logits):
        top = jnp.max(logits, axis=-1, keepdims=True)
        exp_logits = jnp.exp(logits - top)
        return exp_logits / jnp.sum(exp_logits, axis=-1, keepdims=True)

    dx_back, dots_back, expert_rows, down_back, expert_totals = experts_run(
        x_in,
        grad_in,
        [wg, wu, wd],
        jnp.pad(router, ((0, 0), (0, 128 - n_experts))),
        n_dp,
        n_ex,
        inner,
        9,
    )
    dx_back = dx_back.reshape(n_slots, width)

    col_probs = probs_of(mm(x_col, router))
    expert_axis = jnp.arange(n_experts)[None, :]
    gates = [
        jnp.sum(jnp.where(expert_axis == expert, col_probs, 0.0), axis=1, keepdims=True)
        for expert in far_experts
    ]
    gate_hot = jnp.concatenate(
        [hot_t[:, m * per_far : (m + 1) * per_far] * gates[m].astype(BF) for m in range(chips)],
        axis=1,
    )
    dots = dots_back.reshape(n_slots, 128)[:, 0].astype(F32)[None] * hot_t.astype(F32)
    dots = jnp.sum(dots.reshape(inner * rows, chips, per_far), axis=-1)
    grad_probs_col = sum(
        jnp.where(expert_axis == far_experts[m], dots[:, m : m + 1], 0.0) for m in range(chips)
    )
    dx_col = mm(hot_t, dx_back) + shared_dx
    dx_send = jnp.concatenate(
        [dx_col, grad_probs_col, jnp.zeros((inner * rows, 128 - n_experts), F32)], axis=1
    ).astype(BF)
    dx_sum, shared_sums, rows_back, (gate_back,) = column_sum(
        dx_send.reshape(inner, rows, width + 128),
        expert_rows,
        [grad.reshape(n_ex, n_dp, r, ff_s) for grad in shared_grads],
        expert_totals[:1],
        n_dp,
        n_ex,
        inner,
        3,
    )
    router_probs = lax.dynamic_slice_in_dim(col_probs, my_local * rows, rows, 0)
    grad_probs = dx_sum[:, width : width + n_experts]
    grad_logits = (
        router_probs * (grad_probs - jnp.sum(grad_probs * router_probs, axis=-1, keepdims=True))
    ).astype(BF)
    grad_router = mm_rows(hidden_two, grad_logits)
    grad_hidden_two = dx_sum[:, :width] + mm_cols(grad_logits, router)
    _, norm_two_back = jax.vjp(rms_norm, residual, gain_two)
    grad_resid_norm, grad_gain_two = norm_two_back(grad_hidden_two)
    grad_residual = cot_owner.astype(F32) + grad_resid_norm

    out_col = mm(gate_hot, rows_back.reshape(n_slots, width)) + shared_out
    latent_own = lax.dynamic_slice_in_dim(latent_raw, e * rows, rows, 0)
    router_back = jnp.pad(
        grad_router.reshape(n_ex, n_dp * r, n_experts),
        ((0, 0), (0, 0), (DR, DR - n_experts)),
    ).astype(BF)
    (grad_tokens, vec_sum, pack_sum), heads_got, wout_got, out_got, shared_got, (up_back,) = (
        backward_exchange(
            grad_residual.astype(BF),
            [wo_rows, wq, wexp, cos_wide, sine_wide, keep, qcat, kcat, value, lse, attended],
            hidden_one,
            latent_low,
            [
                pk_flat,
                latent_own,
                tokens,
                gain_one[None],
                gain_lat[None],
                from_owner_order(grad_residual),
                router_back,
                grad_gain_two[None],
            ],
            out_col.astype(BF).reshape(inner, rows, width),
            shared_sums,
            expert_totals[1:2],
            n_dp,
            n_ex,
            inner,
            5,
        )
    )

    def added(values):
        return jnp.sum(values.astype(F32), axis=0)

    out_tokens = from_owner_order((residual + added(out_got)).astype(BF))
    heads_all = added(heads_got)
    wq_parts, we_parts = [], []
    for h in heads_back:
        block, i = heads_all[h // hp], h % hp
        wq_parts.append(block[:, i * DH : (i + 1) * DH])
        wq_parts.append(block[:, hp * DH + i * DR : hp * DH + (i + 1) * DR])
        per = (DH + DV) // we_cols
        for j in range(i * per, (i + 1) * per):
            we_parts.append(block[j * rl : (j + 1) * rl, head_cols:])
    sum_wq = jnp.concatenate(wq_parts, axis=1)
    sum_we = jnp.concatenate(we_parts, axis=1)
    sum_wout = from_owner_order(added(wout_got))
    device = z * n_ex + e
    sum_gain_one = lax.dynamic_slice_in_dim(vec_sum[0], device * r, r, 0)
    sum_gain_two = lax.dynamic_slice_in_dim(vec_sum[1], (e * n_dp + z) * r, r, 0)
    sum_gain_lat = lax.dynamic_slice_in_dim(vec_sum[2], device * rl, rl, 0)
    sum_sgate, sum_sup, sum_sdown = (
        added(got.reshape(n_dp // inner, inner, r, ff_s)).transpose(1, 0, 2).reshape(r, -1)
        for got in shared_got
    )
    sum_egate, sum_eup, sum_edown = (
        added(back).reshape(-1, n_ex * r, ff_e) for back in (gate_back, up_back, down_back)
    )
    return (
        out_tokens,
        grad_tokens,
        sum_gain_one,
        sum_wq,
        pack_sum[:, :lat],
        sum_gain_lat,
        sum_we,
        sum_wout,
        sum_gain_two,
        pack_sum[:, lat : lat + n_experts],
        sum_sgate,
        sum_sup,
        sum_sdown,
        sum_egate,
        sum_eup,
        sum_edown,
    )


def solution(mesh):
    both = ("dp", "expert")
    in_specs = (
        P(both, None),
        P(both, None),
        P("dp"),
        P(both, None),
        P(both, None),
        P(both),
        P(both, None),
        P(both, None),
        P(both),
        P(both, None),
        P(both, None),
        P(both),
        P(both, None),
        P(both, None),
        P(both, None),
        P(both, None),
        P("expert", "dp", None),
        P("expert", "dp", None),
        P("expert", "dp", None),
    )
    out_specs = (
        P(both, None),
        P(both, None),
        P(both),
        P(both, None),
        P(both, None),
        P(both),
        P(both, None),
        P(both, None),
        P(both),
        P(both, None),
        P(both, None),
        P(both, None),
        P(both, None),
        P("expert", "dp", None),
        P("expert", "dp", None),
        P("expert", "dp", None),
    )
    return jax.shard_map(shards, mesh=mesh, in_specs=in_specs, out_specs=out_specs, check_vma=False)
```

```python
import jax
import jax.numpy as jnp
from jax import lax
from jax.experimental import pallas as pl
from jax.experimental.pallas import tpu as pltpu
from jax.sharding import PartitionSpec as P

H = 16
DH = 128
DR = 64
DV = 128
KVR = 512

norm_eps = 1e-06
masked_score = -1e30
MESH = pl.DeviceIdType.MESH
ANY = pl.BlockSpec(memory_space=pl.ANY)
VMEM = pl.BlockSpec(memory_space=pltpu.VMEM)
BF = jnp.bfloat16
F32 = jnp.float32


def rms_norm(values, scale_gain):
    return (
        values
        * lax.rsqrt(jnp.mean(values * values, axis=-1, keepdims=True) + norm_eps)
        * scale_gain
    )


def mm(left, right):
    return jnp.dot(left, right, preferred_element_type=F32)


def mm_rows(left, right):
    return lax.dot_general(left, right, (((0,), (0,)), ((), ())), preferred_element_type=F32)


def mm_cols(left, right):
    return lax.dot_general(left, right, (((1,), (1,)), ((), ())), preferred_element_type=F32)


def slot_places(route_rows, pair_order, capacity):
    pair_expert = route_rows.reshape(-1)
    earlier = pair_order[None, :] < pair_order[:, None]
    same_expert = pair_expert[None, :] == pair_expert[:, None]
    places = jnp.sum((earlier & same_expert).astype(jnp.int32), axis=1)
    slot_index = jnp.where(places < capacity, pair_expert * capacity + places, -1)
    return slot_index.reshape(route_rows.shape)


def turn(values, cos, sin, sign):
    half = DR // 2
    first = lax.rem(lax.broadcasted_iota(jnp.int32, values.shape, 1), DR) < half
    partner = jnp.where(
        first, -pltpu.roll(values, 2 * DR - half, 1), pltpu.roll(values, half, 1)
    )
    return values * cos + sign * (partner * sin)


def causal(i, tile, keep_ref):
    shape = (tile, (i + 1) * tile)
    query = lax.broadcasted_iota(jnp.int32, shape, 0) + i * tile
    key = lax.broadcasted_iota(jnp.int32, shape, 1)
    return (key <= query) & (keep_ref[:, : shape[1]] > 0.5)


def attend_forward(
    tok, gain, wq, wl, gain_lat, we, cos, sin, keep,
    hidden, latent, latent_low, qcat, kcat, value, lse, attended,
):
    per, rows, width = tok.shape
    seq = per * rows
    tile = 2 * rows
    scale = (DH + DR) ** (-0.5)

    def project(i, carry):
        at = pl.ds(pl.multiple_of(i * tile, tile), tile)
        x = tok[pl.ds(2 * i, 2)].reshape(tile, width).astype(F32)
        root = lax.rsqrt(jnp.mean(x * x, axis=-1, keepdims=True) + norm_eps)
        hid = (x * root * gain[...]).astype(BF)
        hidden[at, :] = hid
        c, s = cos[at, :], sin[at, :]
        query = mm(hid, wq[...])
        rope_q = turn(query[:, 2 * DH :], c, s, 1.0).astype(BF)
        lat = mm(hid, wl[...])
        latent[at, :] = lat
        plain = lat[:, :KVR]
        root = lax.rsqrt(jnp.mean(plain * plain, axis=-1, keepdims=True) + norm_eps)
        low = (plain * root * gain_lat[...]).astype(BF)
        latent_low[at, :] = low
        rope = lat[:, KVR : KVR + 2 * DR]
        lane = lax.broadcasted_iota(jnp.int32, rope.shape, 1)
        rope = jnp.where(lane < DR, rope, pltpu.roll(rope, DR, 1))
        rope = turn(rope, c, s, 1.0)
        expanded = mm(low, we[...]).astype(BF)
        for h in range(2):
            qcat[h, at, :DH] = query[:, h * DH : (h + 1) * DH].astype(BF)
            qcat[h, at, DH:] = rope_q
            mine = (lane < DR) if h == 0 else (lane >= DR)
            kcat[h, at, :DH] = expanded[:, h * (DH + DV) : h * (DH + DV) + DH]
            kcat[h, at, DH:] = jnp.where(mine, rope, 0.0).astype(BF)
            value[h, at, :] = expanded[:, h * (DH + DV) + DH : (h + 1) * (DH + DV)]
        return carry

    lax.fori_loop(0, seq // tile, project, 0)
    for h in range(2):
        for i in range(seq // tile):
            at, upto = slice(i * tile, (i + 1) * tile), slice(0, (i + 1) * tile)
            scores = mm_cols(qcat[h, at, :], kcat[h, upto, :]) * scale
            scores = jnp.where(causal(i, tile, keep), scores, masked_score)
            top = jnp.max(scores, axis=-1, keepdims=True)
            exp_scores = jnp.exp(scores - top)
            total = jnp.sum(exp_scores, axis=-1, keepdims=True)
            probs = (exp_scores / total).astype(BF)
            attended[at, h * DV : (h + 1) * DV] = mm(probs, value[h, upto, :]).astype(BF)
            lse[h, at, :] = jnp.broadcast_to(top + jnp.log(total), (tile, lse.shape[2]))


def attend_backward(
    grad, wo, wq, we, cos, sin, keep, qcat, kcat, value, lse, attended,
    gat, grad_wout, dk, dv, grad_query, grad_expanded, grad_rope,
):
    per, rows, width = grad.shape
    seq = per * rows
    tile = 2 * rows
    scale = (DH + DR) ** (-0.5)
    count = seq // tile
    grad_wout[...] = jnp.zeros_like(grad_wout)

    def project(i, carry):
        at = pl.ds(pl.multiple_of(i * tile, tile), tile)
        block = grad[pl.ds(2 * i, 2)].reshape(tile, width)
        gat[at, :] = mm_cols(block, wo[...]).astype(BF)
        grad_wout[...] += mm_rows(attended[at, :], block)
        return carry

    lax.fori_loop(0, count, project, 0)
    for h in range(2):
        dk[...] = jnp.zeros_like(dk)
        dv[...] = jnp.zeros_like(dv)
        for i in range(count):
            at, upto = slice(i * tile, (i + 1) * tile), slice(0, (i + 1) * tile)
            g = gat[at, h * DV : (h + 1) * DV]
            scores = mm_cols(qcat[h, at, :], kcat[h, upto, :]) * scale
            scores = jnp.where(causal(i, tile, keep), scores, masked_score)
            probs = jnp.exp(scores - lse[h, at, 0:1])
            grad_probs = mm_cols(g, value[h, upto, :])
            inner = jnp.sum(grad_probs * probs, axis=-1, keepdims=True)
            raw = (probs * (grad_probs - inner) * scale).astype(BF)
            grad_q = mm(raw, kcat[h, upto, :])
            grad_query[at, h * DH : (h + 1) * DH] = grad_q[:, :DH].astype(BF)
            rope = grad_q[:, DH:]
            lane = lax.broadcasted_iota(jnp.int32, rope.shape, 1)
            mine = (lane < DR) if h == 0 else (lane >= DR)
            rope = turn(rope, cos[at, :], sin[at, :], -1.0).astype(BF)
            if h == 0:
                grad_query[at, 2 * DH :] = rope
            else:
                grad_query[at, 2 * DH :] = jnp.where(mine, rope, grad_query[at, 2 * DH :])
            dk[upto, :] += mm_rows(raw, qcat[h, at, :])
            dv[upto, :] += mm_rows(probs.astype(BF), g)
        grad_expanded[:, h * (DH + DV) : h * (DH + DV) + DH] = dk[:, :DH].astype(BF)
        grad_expanded[:, h * (DH + DV) + DH : (h + 1) * (DH + DV)] = dv[...].astype(BF)
        rope = dk[:, DH:]
        if h == 0:
            grad_rope[...] = rope
        else:
            grad_rope[...] += pltpu.roll(rope, DR, 1)


def params(collective_id):
    return pltpu.CompilerParams(
        collective_id=collective_id, has_side_effects=True, vmem_limit_bytes=60 << 20
    )


def remote(src, dst, send_sem, recv_sem, device):
    return pltpu.make_async_remote_copy(
        src_ref=src,
        dst_ref=dst,
        send_sem=send_sem,
        recv_sem=recv_sem,
        device_id=device,
        device_id_type=MESH,
    )


def greet(devices):
    barrier = pltpu.get_barrier_semaphore()
    for device in devices:
        pl.semaphore_signal(barrier, inc=1, device_id=device, device_id_type=MESH)
    pl.semaphore_wait(barrier, len(devices))


def places(n_dp, n_ex):
    z = lax.axis_index("dp")
    e = lax.axis_index("expert")
    chips = n_ex // 2
    c, k = e // 2, lax.rem(e, 2)
    sibling = (z, e + 1 - 2 * k)
    same_core = [(z, lax.rem(c + i, chips) * 2 + k) for i in range(1, chips)]
    column = [(lax.rem(z + i, n_dp), e) for i in range(1, n_dp)]
    return z, e, c, k, sibling, same_core, column


def wait_recv(region, sem, device):
    remote(region, region, sem, sem, device).wait_recv()


def column_sum(array, rows_out, shared, totals, n_dp, n_ex, inner, collective_id):
    chips = n_ex // 2
    shape = array.shape[1:]
    extra = len(totals)
    _, _, r, ff_s = shared[0].shape

    def kernel(x_hbm, *refs):
        s_in, r_ref, t_refs, refs = refs[:3], refs[3], refs[4 : 4 + extra], refs[4 + extra :]
        o_ref, s_out, r_out, back_refs = refs[0], refs[1:4], refs[4], refs[5 : 5 + extra]
        refs = refs[5 + extra :]
        x_ref, s_v, from_sib, out_buf, from_far = refs[0], refs[1:4], *refs[4:7]
        loads, near_s, near_r, far_s, far_r, r_s, r_r, local = refs[7:15]
        relay_refs, rest = refs[15:18], refs[18:]
        moves = stage([x_hbm, *s_in], [x_ref, *s_v], loads)
        z, e, c, k, sibling, same_core, column = places(n_dp, n_ex)
        greet(same_core + [sibling] + column + [(d[0], sibling[1]) for d in column])
        backs = [
            ExpertsBack(t_refs[m], back_refs[m], rest[7 * m : 7 * m + 7], n_dp, n_ex, inner)
            for m in range(extra)
        ]
        relay = RelaySum(x_ref, relay_refs, n_dp, n_ex, inner)
        near, far, rows_back = {}, {}, []
        for i in list(range(1, chips)) + [0]:
            chip = lax.rem(c + i, chips)
            for m in range(3):
                near[i, m] = remote(
                    s_in[m].at[chip * 2 + 1 - k], from_sib.at[m, i],
                    near_s.at[m, i], near_r.at[m, i], sibling,
                )
                near[i, m].start()
        for back in backs:
            back.begin()
        for i in range(1, chips):
            copy = remote(
                r_ref.at[i], r_out.at[i], r_s.at[i], r_r.at[i], same_core[chips - i - 1]
            )
            copy.start()
            rows_back.append(copy)
        copy = pltpu.make_async_copy(r_ref.at[0], r_out.at[0], local)
        copy.start()
        rows_back.append(copy)
        moves[0].wait()
        relay.run()

        def pair(i, m):
            chip = lax.rem(c + i, chips)
            near[i, m].wait_recv()

            def row(d, carry):
                out_buf[m, i, d] = (
                    s_v[m][chip * 2 + k, d].astype(F32) + from_sib[m, i, d].astype(F32)
                ).astype(BF)
                return carry

            lax.fori_loop(0, n_dp, row, 0)

        for back in backs:
            back.pass_on()
        for move in moves[1:]:
            move.wait()
        for i in range(1, chips):
            for m in range(3):
                pair(i, m)
                far[i, m] = remote(
                    out_buf.at[m, i], from_far.at[m, i], far_s.at[m, i], far_r.at[m, i],
                    same_core[i - 1],
                )
                far[i, m].start()
        for m in range(3):
            pair(0, m)
        relay.finish(o_ref)
        for m in range(3):
            for i in range(1, chips):
                far[i, m].wait_recv()

            def row(d, carry, m=m):
                total = out_buf[m, 0, d].astype(F32)
                for i in range(1, chips):
                    total = total + from_far[m, i, d].astype(F32)
                s_out[m][d] = total.astype(BF)
                return carry

            lax.fori_loop(0, n_dp, row, 0)
        for copy in list(near.values()) + list(far.values()):
            copy.wait_send()
        for copy in rows_back:
            copy.wait()
        relay.end()
        for back in backs:
            back.end()

    dma = pltpu.SemaphoreType.DMA
    scratch = like([array, *shared])
    scratch += [pltpu.VMEM((3, chips, n_dp, r, ff_s), BF)] * 3
    scratch += [dma((4,))] + [dma((3, chips))] * 4 + [dma((chips,))] * 2 + [dma]
    scratch += RelaySum.scratch(shape, inner)
    for total in totals:
        scratch += ExpertsBack.scratch(total, n_dp, inner)
    outs = pl.pallas_call(
        kernel,
        out_shape=[jax.ShapeDtypeStruct(shape, F32)]
        + [jax.ShapeDtypeStruct((n_dp, r, ff_s), BF)] * 3
        + [jax.ShapeDtypeStruct(rows_out.shape, BF)]
        + [ExpertsBack.out(total, n_dp, inner) for total in totals],
        in_specs=[ANY] * (5 + extra),
        out_specs=[VMEM] * 4 + [ANY] * (1 + extra),
        scratch_shapes=scratch,
        compiler_params=params(collective_id),
    )(array, *shared, rows_out, *totals)
    return outs[0], outs[1:4], outs[4], outs[5:]


class Relay:
    @staticmethod
    def scratch(inner):
        dma = pltpu.SemaphoreType.DMA
        return [dma((inner,)), dma((inner,)), dma((inner,)), dma]

    def __init__(self, block, out, scratch, n_dp, n_ex, inner):
        self.block, self.out, self.inner = block, out, inner
        self.up_s, self.down_s, self.recv, self.local = scratch
        self.z, self.e, *_ = places(n_dp, n_ex)
        self.mine = lax.rem(self.z, inner)

    def copy(self, source, src, step):
        sem = self.up_s if step > 0 else self.down_s
        return remote(
            src, self.out.at[source], sem.at[source], self.recv.at[source], (self.z + step, self.e)
        )

    def keep(self):
        return pltpu.make_async_copy(self.block, self.out.at[self.mine], self.local)

    def begin(self):
        pl.when(self.mine < self.inner - 1)(lambda: self.copy(self.mine, self.block, 1).start())
        pl.when(self.mine > 0)(lambda: self.copy(self.mine, self.block, -1).start())
        self.keep().start()

    def pass_on(self):
        for t in range(1, self.inner):
            for step in (1, -1):
                source = self.mine - step * t
                exists = source >= 0 if step > 0 else source < self.inner
                more = self.mine < self.inner - 1 if step > 0 else self.mine > 0

                @pl.when(exists)
                def _(source=source, step=step):
                    self.copy(source, self.out.at[source], step).wait_recv()

                @pl.when(jnp.logical_and(exists, more))
                def _(source=source, step=step):
                    self.copy(source, self.out.at[source], step).start()

    def end(self):
        self.keep().wait()
        pl.when(self.mine < self.inner - 1)(
            lambda: self.copy(self.mine, self.block, 1).wait_send()
        )
        pl.when(self.mine > 0)(lambda: self.copy(self.mine, self.block, -1).wait_send())
        for t in range(1, self.inner):
            for step in (1, -1):
                source = self.mine - step * t
                exists = source >= 0 if step > 0 else source < self.inner
                more = self.mine < self.inner - 1 if step > 0 else self.mine > 0

                @pl.when(jnp.logical_and(exists, more))
                def _(source=source, step=step):
                    self.copy(source, self.out.at[source], step).wait_send()


class RelaySum:
    @staticmethod
    def scratch(shape, inner):
        dma = pltpu.SemaphoreType.DMA
        return [pltpu.VMEM((inner + 1,) + shape, BF), dma((inner,)), dma((inner + 1,))]

    def __init__(self, blocks, scratch, n_dp, n_ex, inner):
        self.blocks, self.inner = blocks, inner
        self.buf, self.send, self.recv = scratch
        self.z, self.e, *_ = places(n_dp, n_ex)
        self.mine = lax.rem(self.z, inner)

    def copy(self, t, src, slot, step):
        return remote(
            src, self.buf.at[slot], self.send.at[t], self.recv.at[slot], (self.z + step, self.e)
        )

    def routes(self, t, step):
        inner, mine = self.inner, self.mine
        if step > 0:
            return [(mine < t, mine == 0, t)]
        last = mine == inner - 1
        return [
            (jnp.logical_and(mine > t, mine - 1 != t), last, t),
            (mine - 1 == t, last, inner),
        ]

    def hop(self, t, step, start):
        for active, first, slot in self.routes(t, step):

            @pl.when(jnp.logical_and(active, first))
            def _(slot=slot):
                copy = self.copy(t, self.blocks.at[t], slot, step)
                if start:
                    copy.start()
                else:
                    copy.wait_send()

            @pl.when(jnp.logical_and(active, jnp.logical_not(first)))
            def _(slot=slot):
                copy = self.copy(t, self.buf.at[t], slot, step)
                if start:
                    self.copy(t, self.buf.at[t], t, step).wait_recv()
                    total = self.buf[t].astype(F32) + self.blocks[t].astype(F32)
                    self.buf[t] = total.astype(BF)
                    copy.start()
                else:
                    copy.wait_send()

    def run(self):
        inner = self.inner

        def up():
            for t in range(inner - 1, 0, -1):
                self.hop(t, 1, True)

        def down():
            for t in range(inner - 1):
                self.hop(t, -1, True)

        @pl.when(self.mine < inner // 2)
        def _():
            up()
            down()

        @pl.when(self.mine >= inner // 2)
        def _():
            down()
            up()

    def finish(self, out):
        out[...] = self.blocks[self.mine].astype(F32)

        @pl.when(self.mine > 0)
        def _():
            self.copy(0, self.buf.at[self.mine], self.mine, 1).wait_recv()
            out[...] += self.buf[self.mine].astype(F32)

        @pl.when(self.mine < self.inner - 1)
        def _():
            self.copy(0, self.buf.at[self.inner], self.inner, 1).wait_recv()
            out[...] += self.buf[self.inner].astype(F32)

    def end(self):
        for t in range(self.inner):
            if t:
                self.hop(t, 1, False)
            if t < self.inner - 1:
                self.hop(t, -1, False)


def stage(sources, targets, sems):
    copies = [
        pltpu.make_async_copy(source, target, sems.at[j])
        for j, (source, target) in enumerate(zip(sources, targets))
    ]
    for copy in copies:
        copy.start()
    return copies


def like(arrays):
    return [pltpu.VMEM(array.shape, array.dtype) for array in arrays]


def column_group(z, e, inner):
    start = z // inner * inner
    return [(start + lax.rem(z - start + i, inner), e) for i in range(inner)]


class ExpertsIn:
    @staticmethod
    def scratch(n_dp):
        dma = pltpu.SemaphoreType.DMA
        return [dma((n_dp, 2)), dma((n_dp,)), dma((n_dp,)), dma((n_dp,))]

    @staticmethod
    def out(weight, n_dp, n_ex):
        return jax.ShapeDtypeStruct((n_ex, n_dp) + weight.shape[2:], BF)

    def __init__(self, weight, out, scratch, n_dp, n_ex, inner):
        self.weight, self.out, self.n_dp, self.inner = weight, out, n_dp, inner
        self.send, self.recv, self.sib_send, self.sib_recv = scratch
        self.z, self.e, self.c, self.k, self.sibling, _, _ = places(n_dp, n_ex)
        self.hh = n_ex // 2
        self.local = weight.shape[0]

    def sends(self, start):
        for i in list(range(1, self.n_dp)) + [0]:
            to = lax.rem(self.z + i, self.n_dp)
            expert = lax.rem(to, self.inner)

            def go(i=i, to=to, expert=expert):
                for h in range(2):
                    src = self.weight.at[lax.rem(expert, self.local), pl.ds(h * self.hh, self.hh)]
                    dst = self.out.at[pl.ds(h * self.hh, self.hh), self.z]
                    sem = self.recv.at[self.z]

                    def far(src=src, dst=dst, h=h):
                        copy = remote(src, dst, self.send.at[i, h], sem, (to, 2 * self.c + h))
                        if start:
                            copy.start()
                        else:
                            copy.wait_send()

                    if i:
                        far()
                    else:
                        pl.when(self.k != h)(far)
                        if start:

                            @pl.when(self.k == h)
                            def _(src=src, dst=dst):
                                pltpu.make_async_copy(src, dst, sem).start()

            pl.when(expert // self.local == self.k)(go)

    def begin(self):
        self.sends(True)

    def pass_on(self):
        mine = lax.rem(self.z, self.inner)
        for i in range(self.n_dp):
            d = lax.rem(self.z + self.n_dp - i, self.n_dp)
            region = self.out.at[pl.ds(self.k * self.hh, self.hh), d]
            if i:
                wait_recv(region, self.recv.at[d], self.sibling)
            else:
                from_here = mine // self.local == self.k

                @pl.when(from_here)
                def _(region=region, d=d):
                    src = self.weight.at[
                        lax.rem(mine, self.local), pl.ds(self.k * self.hh, self.hh)
                    ]
                    pltpu.make_async_copy(src, region, self.recv.at[d]).wait()

                @pl.when(jnp.logical_not(from_here))
                def _(region=region, d=d):
                    wait_recv(region, self.recv.at[d], self.sibling)

            remote(
                region, region, self.sib_send.at[i], self.sib_recv.at[i], self.sibling
            ).start()

    def end(self):
        self.sends(False)
        for i in range(self.n_dp):
            d = lax.rem(self.z + self.n_dp - i, self.n_dp)
            mine = self.out.at[pl.ds(self.k * self.hh, self.hh), d]
            remote(
                mine, mine, self.sib_send.at[i], self.sib_recv.at[i], self.sibling
            ).wait_send()
            region = self.out.at[pl.ds((1 - self.k) * self.hh, self.hh), d]
            wait_recv(region, self.sib_recv.at[i], self.sibling)


def gain_rows(gains, target, width, order):
    per = 128 // width
    for t in range(len(order) // per):
        tile = jnp.zeros((8, 128), F32)
        for q in range(per):
            d, e = order[t * per + q]
            piece = gains[d, e, 0:8].astype(F32)
            lane = lax.broadcasted_iota(jnp.int32, piece.shape, 1)
            if q:
                piece = pltpu.roll(piece, q * width, 1)
            tile = jnp.where(lane // width == q, piece, tile)
        target[:, t * 128 : (t + 1) * 128] = tile


def forward_exchange(
    first, tables, w_out, tok, cot, experts, shared, n_dp, n_ex, inner, collective_id
):
    chips = n_ex // 2
    rows, width = tok.shape
    count = len(experts)
    r = w_out.shape[0]
    parts = DV // r
    hp = n_dp // parts
    seq = n_ex * rows
    rl = KVR // (n_dp * n_ex)
    we_cols = rl * hp * (DH + DV) // r
    wq_cols = hp * (DH + DR)

    natural = [(d, j) for d in range(n_dp) for j in range(n_ex)]
    by_owner = [(d, j) for j in range(n_ex) for d in range(n_dp)]

    def kernel(*refs):
        first_in, tables_hbm, keep, refs = refs[:4], refs[4:6], refs[6], refs[7:]
        wo_in, tok_ref, cot_in = refs[:3]
        e_in, s_in = refs[3 : 3 + count], refs[3 + count : 6 + count]
        refs = refs[6 + count :]
        kept_hbm, refs = refs[:12], refs[12:]
        gain_one, gain_ref, gain_lat, res_ref, xcol_ref, cot_out = refs[:6]
        refs = refs[6:]
        w_out, s_out = refs[:count], refs[count : 3 + count]
        refs = refs[3 + count :]
        (cos, sin), (tok_all, wa_ref, gr_ref), refs = refs[:2], refs[2:5], refs[5:]
        kept, refs = refs[:12], refs[12:]
        stage_sem, kept_sem, refs = refs[0], refs[1], refs[2:]
        first_sems, own_sem, refs = refs[:14], refs[14], refs[15:]
        att_out, (wq_ref, we_ref, wo_out, pk_ref) = kept[:8], kept[8:]
        moves = stage(tables_hbm, (cos, sin), stage_sem)
        x_ref, from_sib, out_buf, from_far, xbuf = refs[:5]
        (
            near_s, near_r, far_s, far_r,
            sh_s, sh_r, sp_s, sp_r, sf_s, sf_r, wo_s, wo_r, local,
        ) = refs[5:18]
        x_sems, co_sems, refs = refs[18:22], refs[22:26], refs[26:]
        z, e, c, k, sibling, same_core, column = places(n_dp, n_ex)
        part = lax.rem(e, parts)
        members = [
            (lax.rem(z + i, n_dp), e - part + lax.rem(part + j, parts))
            for i in range(n_dp)
            for j in range(parts)
        ]
        plane = [(z, lax.rem(e + i, n_ex)) for i in range(1, n_ex)]
        greet(plane + column + [(device[0], sibling[1]) for device in column] + members[1:])

        def wo_sends(start):
            for i in range(n_dp):
                target = (lax.rem(z + i, n_dp), e - part + z // hp)
                dst, sem = wo_out.at[lax.rem(z, hp), part], wo_r.at[lax.rem(z, hp), part]

                def far(i=i, target=target, dst=dst, sem=sem):
                    copy = remote(wo_in, dst, wo_s.at[i], sem, target)
                    if start:
                        copy.start()
                    else:
                        copy.wait_send()

                if i:
                    far()
                else:
                    pl.when(z // hp != part)(far)
                    if start:

                        @pl.when(z // hp == part)
                        def _(dst=dst, sem=sem):
                            pltpu.make_async_copy(wo_in, dst, sem).start()

        def wo_arrivals():
            for h in range(hp):
                for p in range(parts):
                    here = jnp.logical_and(part * hp + h == z, part == p)

                    @pl.when(here)
                    def _(h=h, p=p):
                        pltpu.make_async_copy(wo_in, wo_out.at[h, p], wo_r.at[h, p]).wait()

                    @pl.when(jnp.logical_not(here))
                    def _(h=h, p=p):
                        wait_recv(wo_out.at[h, p], wo_r.at[h, p], sibling)

        my_l = lax.rem(z, inner)
        matrices = [
            ExpertsIn(e_in[m], w_out[m], refs[4 * m : 4 * m + 4], n_dp, n_ex, inner)
            for m in range(count)
        ]
        tok_in, wa_in, *packs_in = first_in
        packs = (pk_ref, gr_ref)
        (
            t_send, t_recv, ts_send, ts_recv, a_send, a_recv, az_send, az_recv,
            p_send, p_recv, pf_send, pf_recv, ps_send, ps_recv,
        ) = first_sems
        wa_far, pk_col, tok_far, first_near = [], [], [], []
        for i in range(1, n_ex):
            copy = remote(
                wa_in.at[lax.rem(e + i, n_ex)], wa_ref.at[z, e],
                a_send.at[i], a_recv.at[i], plane[i - 1],
            )
            copy.start()
            wa_far.append(copy)
        for i in range(1, n_dp):
            for m in range(2):
                copy = remote(
                    packs_in[m], packs[m].at[z, e], p_send.at[m, i], p_recv.at[m, i],
                    column[i - 1],
                )
                copy.start()
                pk_col.append(copy)
        for i in range(1, chips):
            copy = remote(tok_in, tok_all.at[e], t_send.at[i], t_recv.at[i], same_core[i - 1])
            copy.start()
            tok_far.append(copy)
        copy = remote(tok_in, tok_all.at[e], ts_send.at[0], ts_recv.at[0], sibling)
        copy.start()
        first_near.append(copy)
        first_own = stage(
            [wa_in.at[e], packs_in[0], packs_in[1], tok_in],
            [wa_ref.at[z, e], pk_ref.at[z, e], gr_ref.at[z, e], tok_all.at[e]],
            own_sem,
        )
        for copy in first_own:
            copy.wait()
        for copy in wa_far:
            copy.wait_recv()
        wa_col = []
        for i in range(1, n_dp):
            copy = remote(
                wa_ref.at[z], wa_ref.at[z], az_send.at[i], az_recv.at[i], column[i - 1]
            )
            copy.start()
            wa_col.append(copy)
        wo_sends(True)
        shared_copies = []
        for i in range(1, n_dp):
            for m in range(3):
                copy = remote(
                    s_in[m].at[lax.rem(lax.rem(z + i, n_dp), inner)], s_out[m].at[e, z],
                    sh_s.at[m, i], sh_r.at[m, i], column[i - 1],
                )
                copy.start()
                shared_copies.append(copy)
        own = [
            pltpu.make_async_copy(s_in[m].at[my_l], s_out[m].at[e, z], local.at[m])
            for m in range(3)
        ]
        for copy in own:
            copy.start()
        matrices[0].begin()
        for copy in pk_col:
            copy.wait_recv()
        pk_far = []
        for m in range(2):
            block = packs[m].at[:, e]
            for i in range(1, chips):
                copy = remote(block, block, pf_send.at[m, i], pf_recv.at[m, i], same_core[i - 1])
                copy.start()
                pk_far.append((i, m, copy))
            copy = remote(block, block, ps_send.at[m, 0], ps_recv.at[m, 0], sibling)
            copy.start()
            first_near.append(copy)
        for i in range(1, chips):
            source = lax.rem(c + chips - i, chips) * 2 + k
            tok_far[i - 1].wait_recv()
            copy = remote(
                tok_all.at[source], tok_all.at[source], ts_send.at[i], ts_recv.at[i], sibling
            )
            copy.start()
            first_near.append(copy)
        for i, m, copy in pk_far:
            copy.wait_recv()
            block = packs[m].at[:, lax.rem(c + chips - i, chips) * 2 + k]
            copy = remote(block, block, ps_send.at[m, i], ps_recv.at[m, i], sibling)
            copy.start()
            first_near.append(copy)
        for copy in first_near + wa_col:
            copy.wait()
        for copy in wa_far + pk_col + tok_far + [copy for _, _, copy in pk_far]:
            copy.wait_send()
        for move in moves:
            move.wait()
        gain_rows(gr_ref, gain_one, r, natural)
        gain_rows(gr_ref, gain_ref, r, by_owner)
        gain_rows(gr_ref, gain_lat, rl, natural)
        wl_ref = pk_ref.reshape(width, pk_ref.shape[3])
        wq_ref[...] = wa_ref[:, :, :, :wq_cols].reshape(width, wq_cols)
        for j in range(r // rl):
            block = wa_ref[:, :, j * rl : (j + 1) * rl, wq_cols:].reshape(KVR, we_cols)
            we_ref[:, j * we_cols : (j + 1) * we_cols] = block
        attend_forward(
            tok_all, gain_one.at[0:1], wq_ref, wl_ref, gain_lat.at[2:3], we_ref, cos, sin, keep,
            *att_out,
        )
        wo_arrivals()
        kept_moves = stage(kept, kept_hbm, kept_sem)
        wo = wo_out[...].reshape(hp * DV, width)

        def project(i, carry):
            at = pl.ds(pl.multiple_of(i * 2 * rows, 2 * rows), 2 * rows)
            block = mm(att_out[7][at, :], wo).astype(BF)
            x_ref[pl.ds(2 * i, 2)] = block.reshape(2, rows, width)
            return carry

        lax.fori_loop(0, chips, project, 0)
        near = []
        for i in list(range(1, chips)) + [0]:
            chip = lax.rem(c + i, chips)
            copy = remote(
                x_ref.at[chip * 2 + 1 - k], from_sib.at[chip], near_s.at[i], near_r.at[i], sibling
            )
            copy.start()
            near.append(copy)
        far = []
        for i in range(1, chips):
            chip = lax.rem(c + i, chips)
            near[i - 1].wait_recv()
            out_buf[i] = (
                x_ref[chip * 2 + k].astype(F32) + from_sib[chip].astype(F32)
            ).astype(BF)
            copy = remote(out_buf.at[i], from_far.at[i], far_s.at[i], far_r.at[i], same_core[i - 1])
            copy.start()
            far.append(copy)
        near[chips - 1].wait_recv()
        res_ref[...] = x_ref[e].astype(F32) + from_sib[c].astype(F32) + tok_ref[...].astype(F32)
        for i in range(1, chips):
            far[i - 1].wait_recv()
            res_ref[...] += from_far[i].astype(F32)
        residual = res_ref[...]
        scale = lax.rsqrt(jnp.mean(residual * residual, axis=-1, keepdims=True) + norm_eps)
        xbuf[...] = (residual * scale * gain_ref[1:2, :]).astype(BF)
        relays = [
            Relay(xbuf, xcol_ref, x_sems, n_dp, n_ex, inner),
            Relay(cot_in, cot_out, co_sems, n_dp, n_ex, inner),
        ]
        relays[0].begin()
        relays[0].pass_on()
        relays[1].begin()
        for matrix in matrices[1:]:
            matrix.begin()
        for copy in own:
            copy.wait()
        for copy in shared_copies:
            copy.wait_recv()
        plane, to_sib = [], []
        for m in range(3):
            block = s_out[m].at[e]
            for i in range(1, chips):
                copy = remote(block, block, sp_s.at[m, i], sp_r.at[m, i], same_core[i - 1])
                copy.start()
                plane.append(copy)
            copy = remote(block, block, sf_s.at[m, 0], sf_r.at[m, 0], sibling)
            copy.start()
            to_sib.append(copy)
        for m in range(3):
            for i in range(1, chips):
                plane[m * (chips - 1) + i - 1].wait_recv()
                block = s_out[m].at[lax.rem(c + chips - i, chips) * 2 + k]
                copy = remote(block, block, sf_s.at[m, i], sf_r.at[m, i], sibling)
                copy.start()
                to_sib.append(copy)
        relays[1].pass_on()
        for matrix in matrices:
            matrix.pass_on()
        for copy in to_sib:
            copy.wait()
        for relay in relays:
            relay.end()
        for copy in plane + shared_copies + near + far:
            copy.wait_send()
        wo_sends(False)
        for move in kept_moves:
            move.wait()
        for matrix in matrices:
            matrix.end()

    dma = pltpu.SemaphoreType.DMA
    ff_s = shared[0].shape[2]
    scratch = []
    for _ in experts:
        scratch += ExpertsIn.scratch(n_dp)
    sds = jax.ShapeDtypeStruct
    kept = [
        sds((seq, width), BF),
        sds((seq, first[2].shape[1]), F32),
        sds((seq, KVR), BF),
        sds((2, seq, 2 * DH), BF),
        sds((2, seq, 2 * DH), BF),
        sds((2, seq, DV), BF),
        sds((2, seq, 128), F32),
        sds((seq, 2 * DV), BF),
        sds((width, wq_cols), BF),
        sds((KVR, hp * (DH + DV)), BF),
        sds((hp, parts, r, width), BF),
        sds((n_dp, n_ex) + first[2].shape, BF),
    ]
    outs = pl.pallas_call(
        kernel,
        out_shape=kept
        + [
            sds((8, width), F32),
            sds((8, width), F32),
            sds((8, KVR), F32),
            sds((rows, width), F32),
            sds((inner, rows, width), BF),
            sds((inner, rows, width), BF),
        ]
        + [ExpertsIn.out(w, n_dp, n_ex) for w in experts]
        + [sds((n_ex, n_dp, r, ff_s), BF)] * 3,
        in_specs=[ANY] * 6 + [VMEM, ANY, VMEM] + [ANY] * (4 + count),
        out_specs=[ANY] * 12 + [VMEM] * 4 + [ANY] * (5 + count),
        scratch_shapes=like(tables[:2])
        + [
            pltpu.VMEM((n_ex, rows, width), BF),
            pltpu.VMEM((n_dp,) + first[1].shape, BF),
            pltpu.VMEM((n_dp, n_ex) + first[3].shape, BF),
        ]
        + like(kept)
        + [dma((2,)), dma((12,))]
        + [dma((chips,))] * 4
        + [dma((n_ex,))] * 2
        + [dma((n_dp,))] * 2
        + [dma((2, n_dp))] * 2
        + [dma((2, chips))] * 4
        + [dma((4,))]
        + [pltpu.VMEM((n_ex, rows, width), BF)]
        + [pltpu.VMEM((chips, rows, width), BF)] * 3
        + [pltpu.VMEM((rows, width), BF)]
        + [dma((chips,))] * 4
        + [dma((3, n_dp))] * 2
        + [dma((3, chips))] * 4
        + [dma((n_dp,)), dma((hp, parts)), dma((3,))]
        + Relay.scratch(inner) * 2
        + scratch,
        compiler_params=params(collective_id),
    )(*first, *tables, w_out, tok, cot, *experts, *shared)
    return outs[:8], outs[8:12], outs[12:15], outs[15:18], outs[18 : 18 + count], outs[18 + count :]


def silu_parts(a):
    sig = 1.0 / (1.0 + jnp.exp(-a))
    return a * sig, sig * (1.0 + a * (1.0 - sig))


def dispatch(hot, x, cot, shared, weights, n_dp, n_ex, inner, collective_id):
    chips = n_ex // 2
    rows, width = x.shape
    ff = shared[0].shape[1]
    tile = 256

    per_far = hot.shape[0] // chips
    count = len(weights)

    def kernel(hot_ref, x_hbm, c_hbm, g_hbm, u_hbm, d_hbm, *refs):
        w_in, refs = refs[:count], refs[count:]
        o_ref, go_ref, w_out, refs = refs[0], refs[1], refs[2 : 2 + count], refs[2 + count :]
        results, refs = refs[:5], refs[5:]
        hot_v, x_v, c_v, g_v, u_v, d_v, hid, ga, gb, b_v, send, recv, loads, keep = refs[:14]
        out_ref, dx_ref, gg_ref, gu_ref, gd_ref = refs[14:19]
        results_sem, rest = refs[19], refs[20:]
        z, e, c, k, sibling, same_core, column = places(n_dp, n_ex)
        moves = [
            pltpu.make_async_copy(src, dst, loads.at[j])
            for j, (src, dst) in enumerate(
                [
                    (hot_ref, hot_v), (x_hbm, x_v), (c_hbm, c_v),
                    (g_hbm, g_v), (u_hbm, u_v), (d_hbm, d_v),
                ]
            )
        ]
        for copy in moves:
            copy.start()
        greet(same_core + [sibling] + column + [(device[0], sibling[1]) for device in column])
        matrices = [
            ExpertsIn(w_in[m], w_out[m], rest[4 * m : 4 * m + 4], n_dp, n_ex, inner)
            for m in range(count)
        ]
        for matrix in matrices:
            matrix.begin()
        copies = []
        for j, (source, target) in enumerate(((x_v, o_ref), (c_v, go_ref))):
            if not j:
                moves[0].wait()
            moves[1 + j].wait()
            for i in list(range(1, chips)) + [0]:
                block = mm(hot_v[i * per_far : (i + 1) * per_far, :], source[...])
                b_v[j, i] = block.astype(BF)
                if i:
                    copy = remote(
                        b_v.at[j, i], target.at[i], send.at[j, i], recv.at[j, i],
                        same_core[i - 1],
                    )
                else:
                    copy = pltpu.make_async_copy(b_v.at[j, 0], target.at[0], keep.at[j])
                copy.start()
                copies.append(copy)
        for copy in moves[3:]:
            copy.wait()

        def rows_of(i, carry):
            at = pl.ds(pl.multiple_of(i * tile, tile), tile)
            first = mm(x_v[at, :], g_v[...])
            second = mm(x_v[at, :], u_v[...])
            silu, slope = silu_parts(first)
            low = (silu * second).astype(BF)
            hid[at, :] = low
            out_ref[at, :] = mm_cols(low, d_v[...])
            back = mm(c_v[at, :], d_v[...])
            low_a = (back * second * slope).astype(BF)
            low_b = (back * silu).astype(BF)
            ga[at, :] = low_a
            gb[at, :] = low_b
            dx_ref[at, :] = mm_cols(low_a, g_v[...]) + mm_cols(low_b, u_v[...])
            return carry

        lax.fori_loop(0, rows // tile, rows_of, 0)

        def columns_of(j, carry):
            at = pl.ds(pl.multiple_of(j * tile, tile), tile)
            gg_ref[at, :] = mm_rows(x_v[:, at], ga[...]).astype(BF)
            gu_ref[at, :] = mm_rows(x_v[:, at], gb[...]).astype(BF)
            gd_ref[at, :] = mm_rows(c_v[:, at], hid[...]).astype(BF)
            return carry

        lax.fori_loop(0, width // tile, columns_of, 0)
        result_moves = stage([out_ref, dx_ref, gg_ref, gu_ref, gd_ref], results, results_sem)
        for matrix in matrices:
            matrix.pass_on()
        for copy in copies + result_moves:
            copy.wait()
        for matrix in matrices:
            matrix.end()

    dma = pltpu.SemaphoreType.DMA
    sds = jax.ShapeDtypeStruct
    vmem = pltpu.VMEM
    scratch = []
    for _ in weights:
        scratch += ExpertsIn.scratch(n_dp)
    results = [sds((rows, width), F32)] * 2 + [sds((width, ff), BF)] * 3
    outs = pl.pallas_call(
        kernel,
        out_shape=[sds((chips, per_far, width), BF)] * 2
        + [ExpertsIn.out(weight, n_dp, n_ex) for weight in weights]
        + results,
        in_specs=[ANY] * (6 + count),
        out_specs=[ANY] * (7 + count),
        scratch_shapes=[vmem(hot.shape, BF)]
        + [vmem((rows, width), BF)] * 2
        + [vmem((width, ff), BF)] * 3
        + [vmem((rows, ff), BF)] * 3
        + [vmem((2, chips, per_far, width), BF)]
        + [dma((2, chips)), dma((2, chips)), dma((6,)), dma((2,))]
        + like(results)
        + [dma((5,))]
        + scratch,
        compiler_params=params(collective_id),
    )(hot, x, cot, *shared, *weights)
    return outs[:2], outs[2 : 2 + count], outs[2 + count], outs[3 + count], outs[4 + count :]


def experts_run(x_in, grad_in, weights, router, n_dp, n_ex, inner, collective_id):
    chips = n_ex // 2
    n_slots, width = x_in.shape
    ff = weights[0].shape[1]
    per_far = n_slots // chips
    r = width // (n_dp * n_ex)
    tile = per_far
    span = n_dp * r
    n_experts = inner * chips

    def kernel(*refs):
        in_hbm, refs = refs[:6], refs[6:]
        dx_out, dots_out, rows_out, back_out, g_out, refs = *refs[:4], refs[4:6], refs[6:]
        x_v, s_v, wg, wu, wd, route, a_v, b_v, h_v, dx_v, total, stage, dots_v = refs[:13]
        loads, send, recv, d_send, d_recv, local, rows_sem, out_sem = refs[13:21]
        z, e, c, k, sibling, same_core, column = places(n_dp, n_ex)
        moves = [
            pltpu.make_async_copy(src, dst, loads.at[j])
            for j, (src, dst) in enumerate(zip(in_hbm, (x_v, s_v, wg, wu, wd, route)))
        ]
        for j in (5, 0, 2, 3, 4, 1):
            moves[j].start()
        greet(same_core + [sibling] + column + [(device[0], sibling[1]) for device in column])
        back = ExpertsBack(total, back_out, refs[21:], n_dp, n_ex, inner)
        expert = c * inner + lax.rem(z, inner)
        for j in (5, 0, 2, 3, 4, 1):
            moves[j].wait()

        def forward(i, carry):
            at = pl.ds(pl.multiple_of(i * tile, tile), tile)
            x = x_v[at, :]
            logits = mm(x, route[...])
            lane = lax.broadcasted_iota(jnp.int32, logits.shape, 1)
            logits = jnp.where(lane < n_experts, logits, masked_score)
            chances = jnp.exp(logits - jnp.max(logits, axis=-1, keepdims=True))
            gate = jnp.sum(jnp.where(lane == expert, chances, 0.0), axis=-1, keepdims=True)
            gate = gate / jnp.sum(chances, axis=-1, keepdims=True)
            first = mm(x, wg[...])
            second = mm(x, wu[...])
            a_v[at, :] = first.astype(BF)
            b_v[at, :] = second.astype(BF)
            hid = (silu_parts(first)[0] * second).astype(BF)
            h_v[at, :] = hid
            rows = mm_cols(hid, wd[...]).astype(BF)
            dx_v[i] = rows
            grad = s_v[at, :].astype(F32)
            dots = jnp.sum(grad * rows.astype(F32), axis=-1, keepdims=True)
            dots_v[i] = jnp.broadcast_to(dots, (tile, 128)).astype(BF)
            s_v[at, :] = (gate * grad).astype(BF)
            pltpu.make_async_copy(dx_v.at[i], rows_out.at[i], rows_sem.at[i]).start()
            return carry

        lax.fori_loop(0, chips, forward, 0)
        dot_copies = []
        for i in range(1, chips):
            copy = remote(
                dots_v.at[i], dots_out.at[i], d_send.at[i], d_recv.at[i], same_core[chips - i - 1]
            )
            copy.start()
            dot_copies.append(copy)
        copy = pltpu.make_async_copy(dots_v.at[0], dots_out.at[0], local.at[0])
        copy.start()
        dot_copies.append(copy)

        def down_rows(t, carry):
            j = lax.rem(t + (1 - k) * (n_ex // 2), n_ex)
            at = pl.ds(pl.multiple_of(j * span, span), span)
            block = mm_rows(s_v[:, at], h_v[...]).astype(BF)
            total[j] = block.reshape(n_dp, r, ff)
            return carry

        lax.fori_loop(0, n_ex, down_rows, 0)
        back.begin()

        def hidden_rows(i, carry):
            at = pl.ds(pl.multiple_of(i * tile, tile), tile)
            grad = mm(s_v[at, :], wd[...])
            silu, slope = silu_parts(a_v[at, :].astype(F32))
            second = b_v[at, :].astype(F32)
            a_v[at, :] = (grad * second * slope).astype(BF)
            b_v[at, :] = (grad * silu).astype(BF)
            return carry

        lax.fori_loop(0, chips, hidden_rows, 0)
        back.pass_on()
        copies = []
        for i in list(range(1, chips)) + [0]:
            at = slice(i * per_far, (i + 1) * per_far)
            block = mm_cols(a_v[at, :], wg[...]) + mm_cols(b_v[at, :], wu[...])
            pltpu.make_async_copy(dx_v.at[i], rows_out.at[i], rows_sem.at[i]).wait()
            dx_v[i] = block.astype(BF)
            if i:
                copy = remote(
                    dx_v.at[i], dx_out.at[i], send.at[i], recv.at[i], same_core[chips - i - 1]
                )
            else:
                copy = pltpu.make_async_copy(dx_v.at[0], dx_out.at[0], local.at[1])
            copy.start()
            copies.append(copy)

        def other_rows(j, carry):
            at = pl.ds(pl.multiple_of(j * span, span), span)
            for m, side in enumerate((a_v, b_v)):

                @pl.when(j > 0)
                def _(m=m):
                    pltpu.make_async_copy(stage.at[m], g_out[m].at[j - 1], out_sem.at[m]).wait()

                block = mm_rows(x_v[:, at], side[...]).astype(BF)
                stage[m] = block.reshape(n_dp, r, ff)
                pltpu.make_async_copy(stage.at[m], g_out[m].at[j], out_sem.at[m]).start()
            return carry

        lax.fori_loop(0, n_ex, other_rows, 0)
        for m in range(2):
            pltpu.make_async_copy(stage.at[m], g_out[m].at[n_ex - 1], out_sem.at[m]).wait()
        for copy in copies + dot_copies:
            copy.wait()
        back.end()

    dma = pltpu.SemaphoreType.DMA
    sds = jax.ShapeDtypeStruct
    vmem = pltpu.VMEM
    total = sds((n_ex, n_dp, r, ff), BF)
    blocks = sds((chips, per_far, width), BF)
    dots = sds((chips, per_far, 128), BF)
    outs = pl.pallas_call(
        kernel,
        out_shape=[blocks, dots, blocks, ExpertsBack.out(total, n_dp, inner), total, total],
        in_specs=[ANY] * 6,
        out_specs=[ANY] * 6,
        scratch_shapes=[vmem((n_slots, width), BF)] * 2
        + [vmem((width, ff), BF)] * 3
        + [vmem((width, 128), BF)]
        + [vmem((n_slots, ff), BF)] * 3
        + [
            vmem(blocks.shape, BF),
            vmem(total.shape, BF),
            vmem((2, n_dp, r, ff), BF),
            vmem(dots.shape, BF),
            dma((6,)),
        ]
        + [dma((chips,))] * 4
        + [dma((2,)), dma((chips,)), dma((2,))]
        + ExpertsBack.scratch(total, n_dp, inner),
        compiler_params=params(collective_id),
    )(x_in, grad_in, *weights, router)
    return outs[0], outs[1], outs[2], outs[3], outs[4:]


class ExpertsBack:
    @staticmethod
    def scratch(total, n_dp, inner):
        n_ex, _, r, ff = total.shape
        dma = pltpu.SemaphoreType.DMA
        hh = n_ex // 2
        return [
            pltpu.VMEM((hh, n_dp, r, ff), BF),
            pltpu.VMEM((hh, n_dp, r, ff), BF),
            dma((hh,)),
            dma((hh,)),
            dma((hh,)),
            dma((hh, n_dp)),
            dma((n_dp // inner, 2, 2, hh)),
        ]

    @staticmethod
    def out(total, n_dp, inner):
        n_ex, _, r, ff = total.shape
        return jax.ShapeDtypeStruct((n_dp // inner, 2, n_ex, r, ff), BF)

    def __init__(self, total, out, scratch, n_dp, n_ex, inner):
        self.total, self.out, self.n_dp, self.inner = total, out, n_dp, inner
        self.own, self.sib, self.near_s, self.near_r, self.load, self.send, self.recv = scratch
        self.z, self.e, self.c, self.k, self.sibling, _, _ = places(n_dp, n_ex)
        self.hh = n_ex // 2

    def near(self, j):
        return remote(
            self.total.at[(1 - self.k) * self.hh + j], self.sib.at[j],
            self.near_s.at[j], self.near_r.at[j], self.sibling,
        )

    def loads(self, j):
        return pltpu.make_async_copy(
            self.total.at[self.k * self.hh + j], self.own.at[j], self.load.at[j]
        )

    def begin(self):
        for j in range(self.hh):
            self.near(j).start()
            self.loads(j).start()

    def route(self, j, i):
        d = lax.rem(self.z + i, self.n_dp)
        expert = lax.rem(self.z, self.inner)
        o = self.z // self.inner
        dst = self.out.at[o, lax.rem(expert, 2), self.k * self.hh + j]
        sem = self.recv.at[o, lax.rem(expert, 2), self.k, j]
        return self.own.at[j, d], dst, sem, (d, 2 * self.c + expert // 2)

    def stay(self, j):
        src, dst, sem, _ = self.route(j, 0)
        return pltpu.make_async_copy(src, dst, sem)

    def go(self, j, i):
        src, dst, sem, device = self.route(j, i)
        return remote(src, dst, self.send.at[j, i], sem, device)

    def here(self):
        return lax.rem(self.z, self.inner) // 2 == self.k

    def pass_on(self):
        for j in range(self.hh):
            self.near(j).wait_recv()
            self.loads(j).wait()
            for d in range(self.n_dp):
                self.own[j, d] = (
                    self.own[j, d].astype(F32) + self.sib[j, d].astype(F32)
                ).astype(BF)
            for i in range(1, self.n_dp):
                self.go(j, i).start()
            pl.when(self.here())(lambda j=j: self.stay(j).start())
            pl.when(jnp.logical_not(self.here()))(lambda j=j: self.go(j, 0).start())

    def end(self):
        for j in range(self.hh):
            self.near(j).wait_send()
            for i in range(1, self.n_dp):
                self.go(j, i).wait_send()
            pl.when(jnp.logical_not(self.here()))(lambda j=j: self.go(j, 0).wait_send())
        for o in range(self.n_dp // self.inner):
            for i in range(2):
                for h in range(2):
                    source = o * self.inner + 2 * self.k + i
                    here = jnp.logical_and(source == self.z, self.k == h)
                    for j in range(self.hh):
                        region = self.out.at[o, i, h * self.hh + j]
                        sem = self.recv.at[o, i, h, j]

                        @pl.when(here)
                        def _(region=region, sem=sem, j=j):
                            pltpu.make_async_copy(self.own.at[j, self.z], region, sem).wait()

                        @pl.when(jnp.logical_not(here))
                        def _(region=region, sem=sem):
                            wait_recv(region, sem, self.sibling)


def rms_back(x, gain, grad):
    root = lax.rsqrt(jnp.mean(x * x, axis=-1, keepdims=True) + norm_eps)
    scaled = grad * gain
    along = jnp.mean(x * scaled, axis=-1, keepdims=True)
    return root * scaled - x * (root * root * root) * along, grad * x * root


def backward_exchange(
    grad, attend, hidden, latent_low, own, out, shared, totals, n_dp, n_ex, inner, collective_id
):
    chips = n_ex // 2
    rows, width = grad.shape
    seq = n_ex * rows
    extra = len(totals)
    wq, we = attend[1], attend[2]
    lat_cols = KVR + 2 * DR
    r = width // (n_dp * n_ex)
    rl = KVR // (n_dp * n_ex)
    parts = DV // r
    hp = n_dp // parts
    n_dev = n_dp * n_ex
    wq_cols = wq.shape[1]
    we_cols = rl * we.shape[1] // r
    head_cols = wq_cols + we_cols
    given_arrays = [*attend, hidden, latent_low, *own]
    big = [j for j, array in enumerate(given_arrays) if array.shape[0] > 1]

    def kernel(*refs):
        grad_ref, given, refs = refs[0], list(refs[1:22]), refs[22:]
        out_ref, sh_in, refs = refs[0], refs[1:4], refs[4:]
        t_refs, refs = refs[:extra], refs[extra:]
        tok_out, vec_out, pack_out, heads_mid, heads_out, wout_out, out_got = refs[:7]
        sh_out, back_refs, refs = refs[7:10], refs[10 : 10 + extra], refs[10 + extra :]
        gbuf, att_tmp, refs = refs[0], refs[1:8], refs[8:]
        part_l, bufs, sums, refs = refs[0], refs[1:7], refs[7:9], refs[9:]
        hsrc, wsrc, pack, psib, pout, pfar, psum, pbuf, vec, vbuf, vzbuf = refs[:11]
        refs = refs[11:]
        t_s, t_r, ts_s, ts_r, local = refs[:5]
        sems, refs = refs[5:13], refs[13:]
        (
            h_s, h_r, hz_s, hz_r, w_s, w_r, pn_s, pn_r, pf_s, pf_r, pc_s, pc_r, s_s, s_r,
            v_s, v_r, vz_s, vz_r, o_s, o_r,
        ) = refs[:20]
        staged, stage_sem, rest = refs[20 : 20 + len(big)], refs[20 + len(big)], refs[21 + len(big) :]
        moves = stage([given[j] for j in big], staged, stage_sem)
        for j, ref in zip(big, staged):
            given[j] = ref
        att_in, hidden_ref, low_ref = given[:11], given[11], given[12]
        wl_ref, lat_ref, tok_ref, gain_ref, glat_ref, gnat_ref, router_ref, gtwo_ref = given[13:]
        x_refs = (gbuf, part_l)
        group = column_group(lax.axis_index("dp"), lax.axis_index("expert"), inner)
        z, e, c, k, sibling, same_core, column = places(n_dp, n_ex)
        plane = [(z, lax.rem(e + i, n_ex)) for i in range(1, n_ex)]
        part = lax.rem(e, parts)
        members = [
            (lax.rem(z + i, n_dp), e - part + lax.rem(part + j, parts))
            for i in range(n_dp)
            for j in range(parts)
        ]
        greet(plane + column + [(d[0], sibling[1]) for d in column] + members[1:])
        backs = [
            ExpertsBack(t_refs[m], back_refs[m], rest[7 * m : 7 * m + 7], n_dp, n_ex, inner)
            for m in range(extra)
        ]
        gather, to_sib, others = [], [], []
        for i in range(1, chips):
            copy = remote(grad_ref, gbuf.at[e], t_s.at[i], t_r.at[i], same_core[i - 1])
            copy.start()
            gather.append(copy)
        copy = remote(grad_ref, gbuf.at[e], ts_s.at[0], ts_r.at[0], sibling)
        copy.start()
        to_sib.append(copy)
        keep = pltpu.make_async_copy(grad_ref, gbuf.at[e], local.at[0])
        keep.start()
        for back in backs:
            back.begin()
        for m in range(3):
            for i in range(1, n_dp):
                copy = remote(
                    sh_in[m].at[lax.rem(z + i, n_dp)], sh_out[m].at[z],
                    s_s.at[m, i], s_r.at[m, i], column[i - 1],
                )
                copy.start()
                others.append(copy)
            copy = pltpu.make_async_copy(sh_in[m].at[z], sh_out[m].at[z], local.at[1 + m])
            copy.start()
            others.append(copy)
        mine = lax.rem(z, inner)
        for i in range(1, inner):
            copy = remote(
                out_ref.at[lax.rem(mine + i, inner)], out_got.at[mine], o_s.at[i], o_r.at[i],
                group[i],
            )
            copy.start()
            others.append(copy)
        copy = pltpu.make_async_copy(out_ref.at[mine], out_got.at[mine], local.at[5])
        copy.start()
        others.append(copy)
        for i in range(1, chips):
            gather[i - 1].wait_recv()
            block = gbuf.at[lax.rem(c + chips - i, chips) * 2 + k]
            copy = remote(block, block, ts_s.at[i], ts_r.at[i], sibling)
            copy.start()
            to_sib.append(copy)
        for back in backs:
            back.pass_on()
        keep.wait()
        for copy in to_sib:
            copy.wait_recv()
        for copy in gather + to_sib:
            copy.wait_send()
        gat, grad_wout, dk, dv, grad_query, grad_expanded, grad_rope = att_tmp
        for move in moves:
            move.wait()
        attend_backward(gbuf, *att_in, *att_tmp)

        wsrc[...] = grad_wout[...].astype(BF).reshape(hp, parts, r, width)

        def wout_sends(start):
            for h in range(hp):
                for p in range(parts):
                    target = (part * hp + h, e - part + p)
                    here = jnp.logical_and(part * hp + h == z, p == part)

                    def far(h=h, p=p, target=target):
                        copy = remote(
                            wsrc.at[h, p], wout_out.at[z], w_s.at[h, p], w_r.at[z], target
                        )
                        if start:
                            copy.start()
                        else:
                            copy.wait_send()

                    pl.when(jnp.logical_not(here))(far)
                    if start:

                        @pl.when(here)
                        def _(h=h, p=p):
                            pltpu.make_async_copy(
                                wsrc.at[h, p], wout_out.at[z], w_r.at[z]
                            ).start()

        wout_sends(True)

        def spread(i, carry):
            at = pl.ds(pl.multiple_of(i * 2 * rows, 2 * rows), 2 * rows)
            block = mm_cols(grad_query[at, :], att_in[1][...]).astype(BF)
            gbuf[pl.ds(2 * i, 2)] = block.reshape(2, rows, width)
            block = mm_cols(grad_expanded[at, :], att_in[2][...]).astype(BF)
            part_l[pl.ds(2 * i, 2), :, :KVR] = block.reshape(2, rows, KVR)
            block = grad_rope[at, :].astype(BF)
            part_l[pl.ds(2 * i, 2), :, KVR:] = block.reshape(2, rows, 2 * DR)
            return carry

        lax.fori_loop(0, chips, spread, 0)
        near, far = {}, {}
        for i in list(range(1, chips)) + [0]:
            chip = lax.rem(c + i, chips)
            for j in range(2):
                near[i, j] = remote(
                    x_refs[j].at[chip * 2 + 1 - k],
                    bufs[3 * j].at[chip],
                    sems[4 * j].at[i],
                    sems[4 * j + 1].at[i],
                    sibling,
                )
                near[i, j].start()
        for i in range(1, chips):
            chip = lax.rem(c + i, chips)
            for j in range(2):
                from_sib, out_buf, from_far = bufs[3 * j : 3 * j + 3]
                near[i, j].wait_recv()
                out_buf[i] = (
                    x_refs[j][chip * 2 + k].astype(F32) + from_sib[chip].astype(F32)
                ).astype(BF)
                far[i, j] = remote(
                    out_buf.at[i],
                    from_far.at[i],
                    sems[4 * j + 2].at[i],
                    sems[4 * j + 3].at[i],
                    same_core[i - 1],
                )
                far[i, j].start()

        per_tile = 256 // r

        def wq_rows(i, carry):
            at = pl.ds(pl.multiple_of(i * 256, 256), 256)
            block = mm_rows(hidden_ref[:, at], grad_query[...]).astype(BF)
            hsrc[pl.ds(i * per_tile, per_tile), :, :wq_cols] = block.reshape(
                per_tile, r, wq_cols
            )
            return carry

        lax.fori_loop(0, width // 256, wq_rows, 0)
        grad_we = mm_rows(low_ref[...], grad_expanded[...]).astype(BF)
        for j in range(r // rl):
            block = grad_we[:, j * we_cols : (j + 1) * we_cols]
            hsrc[:, j * rl : (j + 1) * rl, wq_cols:] = block.reshape(n_dev, rl, we_cols)
        heads_far = []
        for i in range(1, n_ex):
            for d in range(n_dp):
                copy = remote(
                    hsrc.at[d * n_ex + lax.rem(e + i, n_ex)], heads_mid.at[d, e],
                    h_s.at[i, d], h_r.at[i, d], plane[i - 1],
                )
                copy.start()
                heads_far.append(copy)
        for d in range(n_dp):
            copy = pltpu.make_async_copy(
                hsrc.at[d * n_ex + e], heads_mid.at[d, e], h_r.at[0, d]
            )
            copy.start()
            copy.wait()
        for j in range(2):
            near[0, j].wait_recv()
            sums[j][...] = x_refs[j][e].astype(F32) + bufs[3 * j][c].astype(F32)
        for i in range(1, chips):
            for j in range(2):
                far[i, j].wait_recv()
                sums[j][...] += bufs[3 * j + 2][i].astype(F32)

        at = pl.ds(pl.multiple_of(e * rows, rows), rows)
        cos, sin = att_in[3][at, :], att_in[4][at, :]
        lat_grad, lat_gain = rms_back(lat_ref[:, :KVR], glat_ref[...], sums[1][:, :KVR])
        rope = turn(sums[1][:, KVR:], cos, sin, -1.0)
        lane = lax.broadcasted_iota(jnp.int32, rope.shape, 1)
        rope = jnp.where(lane < DR, rope, 0.0)
        low = jnp.concatenate([lat_grad, rope], axis=1).astype(BF)
        total = sums[0][...] + mm_cols(low, wl_ref[:, :lat_cols])
        tok_grad, tok_gain = rms_back(tok_ref[...].astype(F32), gain_ref[...], total)
        tok_out[...] = gnat_ref[...] + tok_grad
        vec[...] = jnp.zeros_like(vec)
        vec[0:1, :] = jnp.sum(tok_gain, axis=0, keepdims=True)
        vec[1:2, :] = gtwo_ref[...]
        vec[2:3, :KVR] = jnp.sum(lat_gain, axis=0, keepdims=True)
        vec_far = []
        for i in range(1, n_ex):
            copy = remote(vec, vbuf.at[i], v_s.at[i], v_r.at[i], plane[i - 1])
            copy.start()
            vec_far.append(copy)
        for d in range(n_dp):
            block = hidden_ref[at, d * n_ex * r : (d + 1) * n_ex * r]
            block = mm_rows(block, low).reshape(n_ex, r, lat_cols)
            pack[:, d * r : (d + 1) * r, :KVR] = block[:, :, :KVR].astype(BF)
            block = block[:, :, KVR:] + router_ref[:, d * r : (d + 1) * r].astype(F32)
            pack[:, d * r : (d + 1) * r, KVR:] = block.astype(BF)
        pack_near, pack_far = [], []
        for i in list(range(1, chips)) + [0]:
            chip = lax.rem(c + i, chips)
            copy = remote(pack.at[chip * 2 + 1 - k], psib.at[chip], pn_s.at[i], pn_r.at[i], sibling)
            copy.start()
            pack_near.append(copy)
        for copy in heads_far:
            copy.wait_recv()
        heads_col = []
        for i in range(1, n_dp):
            d = lax.rem(z + i, n_dp)
            copy = remote(
                heads_mid.at[d], heads_out.at[z], hz_s.at[i], hz_r.at[i], column[i - 1]
            )
            copy.start()
            heads_col.append(copy)
        copy = pltpu.make_async_copy(heads_mid.at[z], heads_out.at[z], local.at[4])
        copy.start()
        heads_col.append(copy)
        for i in range(1, chips):
            chip = lax.rem(c + i, chips)
            pack_near[i - 1].wait_recv()
            pout[i] = (pack[chip * 2 + k].astype(F32) + psib[chip].astype(F32)).astype(BF)
            copy = remote(pout.at[i], pfar.at[i], pf_s.at[i], pf_r.at[i], same_core[i - 1])
            copy.start()
            pack_far.append(copy)
        for copy in vec_far:
            copy.wait_recv()
            copy.wait_send()
        for i in range(1, n_ex):
            vec[...] += vbuf[i]
        vec_col = []
        for i in range(1, n_dp):
            copy = remote(vec, vzbuf.at[i], vz_s.at[i], vz_r.at[i], column[i - 1])
            copy.start()
            vec_col.append(copy)
        pack_near[chips - 1].wait_recv()
        total = pack[e].astype(F32) + psib[c].astype(F32)
        for i in range(1, chips):
            pack_far[i - 1].wait_recv()
            total = total + pfar[i].astype(F32)
        psum[...] = total.astype(BF).reshape(n_dp, r, lat_cols)
        pack_col = []
        for i in range(1, n_dp):
            copy = remote(
                psum.at[lax.rem(z + i, n_dp)], pbuf.at[i], pc_s.at[i], pc_r.at[i], column[i - 1]
            )
            copy.start()
            pack_col.append(copy)
        result = vec[...]
        for i in range(1, n_dp):
            vec_col[i - 1].wait_recv()
            result = result + vzbuf[i]
        vec_out[...] = result
        result = psum[z].astype(F32)
        for i in range(1, n_dp):
            pack_col[i - 1].wait_recv()
            result = result + pbuf[i].astype(F32)
        pack_out[...] = result

        for i in range(n_dp):
            here = jnp.logical_and(z // hp == part, z == i)

            @pl.when(here)
            def _(i=i):
                pltpu.make_async_copy(
                    wsrc.at[lax.rem(z, hp), part], wout_out.at[i], w_r.at[i]
                ).wait()

            @pl.when(jnp.logical_not(here))
            def _(i=i):
                wait_recv(wout_out.at[i], w_r.at[i], sibling)

        wout_sends(False)
        for copy in list(near.values()) + list(far.values()) + heads_far:
            copy.wait_send()
        for copy in pack_near + pack_far + vec_col + pack_col:
            copy.wait_send()
        for copy in heads_col + others:
            copy.wait()
        for back in backs:
            back.end()

    dma = pltpu.SemaphoreType.DMA
    sds = jax.ShapeDtypeStruct
    vmem = pltpu.VMEM
    scratch = [
        vmem((n_ex, rows, width), BF),
        vmem((seq, 2 * DV), BF),
        vmem((2 * DV, width), F32),
        vmem((seq, 2 * DH), F32),
        vmem((seq, DV), F32),
        vmem((seq, wq.shape[1]), BF),
        vmem((seq, we.shape[1]), BF),
        vmem((seq, 2 * DR), F32),
        vmem((n_ex, rows, lat_cols), BF),
    ]
    scratch += [vmem((chips, rows, width), BF)] * 3 + [vmem((chips, rows, lat_cols), BF)] * 3
    scratch += [
        vmem((rows, width), F32),
        vmem((rows, lat_cols), F32),
        vmem((n_dev, r, head_cols), BF),
        vmem((hp, parts, r, width), BF),
        vmem((n_ex, n_dp * r, lat_cols), BF),
        vmem((chips, n_dp * r, lat_cols), BF),
        vmem((chips, n_dp * r, lat_cols), BF),
        vmem((chips, n_dp * r, lat_cols), BF),
        vmem((n_dp, r, lat_cols), BF),
        vmem((n_dp, r, lat_cols), BF),
        vmem((8, width), F32),
        vmem((n_ex, 8, width), F32),
        vmem((n_dp, 8, width), F32),
    ]
    scratch += [dma((chips,))] * 4 + [dma((6,))] + [dma((chips,))] * 8
    scratch += [dma((n_ex, n_dp))] * 2 + [dma((n_dp,))] * 2 + [dma((hp, parts)), dma((n_dp,))]
    scratch += [dma((chips,))] * 4 + [dma((n_dp,))] * 2 + [dma((3, n_dp))] * 2
    scratch += [dma((n_ex,))] * 2 + [dma((n_dp,))] * 2 + [dma((inner,))] * 2
    scratch += like([given_arrays[j] for j in big]) + [dma((len(big),))]
    for total in totals:
        scratch += ExpertsBack.scratch(total, n_dp, inner)
    outs = pl.pallas_call(
        kernel,
        out_shape=[
            sds((rows, width), F32),
            sds((8, width), F32),
            sds((r, lat_cols), F32),
            sds((n_dp, n_ex, r, head_cols), BF),
            sds((n_dp, n_ex, r, head_cols), BF),
            sds((n_dp, r, width), BF),
            sds(out.shape, BF),
        ]
        + [sds(array.shape, BF) for array in shared]
        + [ExpertsBack.out(total, n_dp, inner) for total in totals],
        in_specs=[ANY]
        + [ANY if j in big else VMEM for j in range(21)]
        + [ANY] * (4 + extra),
        out_specs=[VMEM] * 3 + [ANY] * (7 + extra),
        scratch_shapes=scratch,
        compiler_params=params(collective_id),
    )(grad, *attend, hidden, latent_low, *own, out, *shared, *totals)
    return outs[:3], outs[4], outs[5], outs[6], outs[7:10], outs[10:]


def shards(
    tokens,
    cotangent,
    lengths,
    routes,
    place_order,
    attn_gain,
    w_query,
    w_latent,
    latent_gain,
    w_expand,
    w_out,
    ffn_gain,
    w_router,
    shared_gate,
    shared_up,
    shared_down,
    expert_gate,
    expert_up,
    expert_down,
):
    rows, width = tokens.shape
    n_dp = lax.axis_size("dp")
    n_ex = lax.axis_size("expert")
    chips = n_ex // 2
    z = lax.axis_index("dp")
    e = lax.axis_index("expert")
    chip = e // 2
    n_experts = w_router.shape[1]
    top_k = routes.shape[1]
    capacity = (rows * top_k * 5 + 4 * n_experts - 1) // (4 * n_experts)
    cap = (capacity + 15) // 16 * 16
    seq = rows * n_ex
    r = w_query.shape[0]
    rl = w_expand.shape[0]
    hp = H // n_ex
    parts = DV // r
    heads = [
        (d * n_ex + (j // parts) * parts) * r // DV
        for j in range(n_ex)
        for d in range(j % parts * hp, j % parts * hp + hp)
    ]
    heads_back = [heads.index(h) for h in range(H)]
    inner = n_experts // chips
    my_local = lax.rem(z, inner)
    ff_e = expert_gate.shape[2]
    ff_s = shared_gate.shape[1] // inner
    lat = KVR + DR
    head_cols = hp * (DH + DR)
    kv_cols = hp * (DH + DV)

    def to_owner_order(values):
        cut = values.reshape(values.shape[0], n_dp, n_ex, r)
        return cut.transpose(0, 2, 1, 3).reshape(values.shape)

    def from_owner_order(values):
        cut = values.reshape(values.shape[0], n_ex, n_dp, r)
        return cut.transpose(0, 2, 1, 3).reshape(values.shape)

    def pick(values, index, axis=0):
        return lax.dynamic_index_in_dim(values, index, axis, keepdims=False)

    wq_send = jnp.take(w_query.reshape(r, H, DH + DR), jnp.array(heads), axis=1)
    wq_send = wq_send.reshape(r, n_ex, hp, DH + DR)
    wq_send = jnp.concatenate(
        [
            wq_send[..., :DH].reshape(r, n_ex, hp * DH),
            wq_send[..., DH:].reshape(r, n_ex, hp * DR),
        ],
        axis=-1,
    ).transpose(1, 0, 2)
    we_send = jnp.take(w_expand.reshape(rl, H, DH + DV), jnp.array(heads), axis=1)
    we_cols = rl * kv_cols // r
    we_send = we_send.reshape(rl, n_ex, r // rl, we_cols).transpose(1, 2, 0, 3)
    we_send = we_send.reshape(n_ex, r, we_cols)
    wa_send = jnp.concatenate([wq_send, we_send], axis=-1)
    slot_own = slot_places(routes, place_order[0], capacity)
    slot_place = jnp.where(slot_own >= 0, slot_own - routes * capacity, -1)
    slot_cols = 2 * rows * top_k // r
    slot_pack = jnp.stack([routes, slot_place]).astype(BF).reshape(2, r, slot_cols // 2)
    small_cols = lat + n_experts
    pack_cols = (small_cols + slot_cols + 127) // 128 * 128
    pack = jnp.concatenate(
        [
            w_latent,
            w_router,
            slot_pack[0],
            slot_pack[1],
            jnp.zeros((r, pack_cols - small_cols - slot_cols), BF),
        ],
        axis=1,
    )
    cot_owner = to_owner_order(cotangent)
    gains = jnp.stack(
        [jnp.pad(gain, (0, 128 - gain.shape[0])) for gain in (attn_gain, ffn_gain, latent_gain)]
    )
    gains = jnp.pad(gains, ((0, 13), (0, 0)))

    positions = jnp.arange(seq)
    lane = jnp.arange(2 * DR) % (DR // 2)
    angles = positions.astype(F32)[:, None] * (10000.0 ** (-(lane.astype(F32) * 2.0) / DR))[None, :]
    cos_wide, sine_wide = jnp.cos(angles), jnp.sin(angles)
    keep = (positions < lengths[0]).astype(F32)[None]
    attend_out, (wq, wexp, wo_rows, pk_all), gain_outs, rows_outs, (wg,), shared_w = (
        forward_exchange(
            [tokens, wa_send, pack, gains],
            [cos_wide, sine_wide, keep],
            to_owner_order(w_out),
            to_owner_order(tokens),
            cot_owner,
            [expert_gate.reshape(-1, n_ex, r, ff_e)],
            [
                w.reshape(r, inner, ff_s).transpose(1, 0, 2)
                for w in (shared_gate, shared_up, shared_down)
            ],
            n_dp,
            n_ex,
            inner,
            2,
        )
    )
    residual, x_col, cot_col = rows_outs
    gain_one, gain_two, gain_lat = (out[j] for j, out in enumerate(gain_outs))
    hidden_one, latent_raw, latent_low, qcat, kcat, value, lse, attended = attend_out
    wo_rows = wo_rows.reshape(hp * DV, width)
    cot_col = cot_col.reshape(inner * rows, width)
    hidden_two = pick(x_col, my_local)
    x_col = x_col.reshape(inner * rows, width)

    router = pk_all[..., lat : lat + n_experts].transpose(1, 0, 2, 3).reshape(width, n_experts)
    pk_flat = pk_all.reshape(width, pack_cols)

    slots_all = n_experts * capacity
    slot_col = pick(pk_all[..., small_cols : small_cols + slot_cols], e, 1)
    slot_col = lax.dynamic_slice_in_dim(slot_col, z - my_local, inner, 0).astype(jnp.int32)
    slot_col = slot_col.reshape(inner, r, 2, slot_cols // 2).transpose(2, 0, 1, 3)
    slot_col = slot_col.reshape(2, inner, rows, top_k)
    slot_ids = jnp.where(
        slot_col[1] >= 0,
        slot_col[0] * capacity + slot_col[1] + (jnp.arange(inner) * slots_all)[:, None, None],
        -1,
    ).reshape(inner * rows, top_k)
    place = jnp.arange(cap)
    far_experts = [lax.rem(chip + m, chips) * inner + my_local for m in range(chips)]
    wanted = (
        jnp.stack(far_experts)[:, None, None] * capacity
        + (jnp.arange(inner) * slots_all)[None, :, None]
        + place[None, None, :]
    )
    wanted = jnp.where(place[None, None, :] < capacity, wanted, -2).reshape(-1)
    n_slots = wanted.shape[0]
    per_far = n_slots // chips
    hot = sum((wanted[:, None] == slot_ids[None, :, j]).astype(BF) for j in range(top_k))
    hot_t = sum((slot_ids[:, j][:, None] == wanted[None, :]).astype(BF) for j in range(top_k))

    (x_in, grad_in), (wu, wd), shared_out, shared_dx, shared_grads = dispatch(
        hot,
        x_col,
        cot_col,
        [w.reshape(width, ff_s) for w in shared_w],
        [w.reshape(-1, n_ex, r, ff_e) for w in (expert_up, expert_down)],
        n_dp,
        n_ex,
        inner,
        8,
    )
    x_in = x_in.reshape(n_slots, width)
    grad_in = grad_in.reshape(n_slots, width)
    wg, wu, wd = (w.reshape(width, ff_e) for w in (wg, wu, wd))

    def probs_of(logits):
        top = jnp.max(logits, axis=-1, keepdims=True)
        exp_logits = jnp.exp(logits - top)
        return exp_logits / jnp.sum(exp_logits, axis=-1, keepdims=True)

    dx_back, dots_back, expert_rows, down_back, expert_totals = experts_run(
        x_in,
        grad_in,
        [wg, wu, wd],
        jnp.pad(router, ((0, 0), (0, 128 - n_experts))),
        n_dp,
        n_ex,
        inner,
        9,
    )
    dx_back = dx_back.reshape(n_slots, width)

    col_probs = probs_of(mm(x_col, router))
    expert_axis = jnp.arange(n_experts)[None, :]
    gates = [
        jnp.sum(jnp.where(expert_axis == expert, col_probs, 0.0), axis=1, keepdims=True)
        for expert in far_experts
    ]
    gate_hot = jnp.concatenate(
        [hot_t[:, m * per_far : (m + 1) * per_far] * gates[m].astype(BF) for m in range(chips)],
        axis=1,
    )
    dots = dots_back.reshape(n_slots, 128)[:, 0].astype(F32)[None] * hot_t.astype(F32)
    dots = jnp.sum(dots.reshape(inner * rows, chips, per_far), axis=-1)
    grad_probs_col = sum(
        jnp.where(expert_axis == far_experts[m], dots[:, m : m + 1], 0.0) for m in range(chips)
    )
    dx_col = mm(hot_t, dx_back) + shared_dx
    dx_send = jnp.concatenate(
        [dx_col, grad_probs_col, jnp.zeros((inner * rows, 128 - n_experts), F32)], axis=1
    ).astype(BF)
    dx_sum, shared_sums, rows_back, (gate_back,) = column_sum(
        dx_send.reshape(inner, rows, width + 128),
        expert_rows,
        [grad.reshape(n_ex, n_dp, r, ff_s) for grad in shared_grads],
        expert_totals[:1],
        n_dp,
        n_ex,
        inner,
        3,
    )
    router_probs = lax.dynamic_slice_in_dim(col_probs, my_local * rows, rows, 0)
    grad_probs = dx_sum[:, width : width + n_experts]
    grad_logits = (
        router_probs * (grad_probs - jnp.sum(grad_probs * router_probs, axis=-1, keepdims=True))
    ).astype(BF)
    grad_router = mm_rows(hidden_two, grad_logits)
    grad_hidden_two = dx_sum[:, :width] + mm_cols(grad_logits, router)
    _, norm_two_back = jax.vjp(rms_norm, residual, gain_two)
    grad_resid_norm, grad_gain_two = norm_two_back(grad_hidden_two)
    grad_residual = cot_owner.astype(F32) + grad_resid_norm

    out_col = mm(gate_hot, rows_back.reshape(n_slots, width)) + shared_out
    latent_own = lax.dynamic_slice_in_dim(latent_raw, e * rows, rows, 0)
    router_back = jnp.pad(
        grad_router.reshape(n_ex, n_dp * r, n_experts),
        ((0, 0), (0, 0), (DR, DR - n_experts)),
    ).astype(BF)
    (grad_tokens, vec_sum, pack_sum), heads_got, wout_got, out_got, shared_got, (up_back,) = (
        backward_exchange(
            grad_residual.astype(BF),
            [wo_rows, wq, wexp, cos_wide, sine_wide, keep, qcat, kcat, value, lse, attended],
            hidden_one,
            latent_low,
            [
                pk_flat,
                latent_own,
                tokens,
                gain_one[None],
                gain_lat[None],
                from_owner_order(grad_residual),
                router_back,
                grad_gain_two[None],
            ],
            out_col.astype(BF).reshape(inner, rows, width),
            shared_sums,
            expert_totals[1:2],
            n_dp,
            n_ex,
            inner,
            5,
        )
    )

    def added(values):
        return jnp.sum(values.astype(F32), axis=0)

    out_tokens = from_owner_order((residual + added(out_got)).astype(BF))
    heads_all = added(heads_got)
    wq_parts, we_parts = [], []
    for h in heads_back:
        block, i = heads_all[h // hp], h % hp
        wq_parts.append(block[:, i * DH : (i + 1) * DH])
        wq_parts.append(block[:, hp * DH + i * DR : hp * DH + (i + 1) * DR])
        per = (DH + DV) // we_cols
        for j in range(i * per, (i + 1) * per):
            we_parts.append(block[j * rl : (j + 1) * rl, head_cols:])
    sum_wq = jnp.concatenate(wq_parts, axis=1)
    sum_we = jnp.concatenate(we_parts, axis=1)
    sum_wout = from_owner_order(added(wout_got))
    device = z * n_ex + e
    sum_gain_one = lax.dynamic_slice_in_dim(vec_sum[0], device * r, r, 0)
    sum_gain_two = lax.dynamic_slice_in_dim(vec_sum[1], (e * n_dp + z) * r, r, 0)
    sum_gain_lat = lax.dynamic_slice_in_dim(vec_sum[2], device * rl, rl, 0)
    sum_sgate, sum_sup, sum_sdown = (
        added(got.reshape(n_dp // inner, inner, r, ff_s)).transpose(1, 0, 2).reshape(r, -1)
        for got in shared_got
    )
    sum_egate, sum_eup, sum_edown = (
        added(back).reshape(-1, n_ex * r, ff_e) for back in (gate_back, up_back, down_back)
    )
    return (
        out_tokens,
        grad_tokens,
        sum_gain_one,
        sum_wq,
        pack_sum[:, :lat],
        sum_gain_lat,
        sum_we,
        sum_wout,
        sum_gain_two,
        pack_sum[:, lat : lat + n_experts],
        sum_sgate,
        sum_sup,
        sum_sdown,
        sum_egate,
        sum_eup,
        sum_edown,
    )


def solution(mesh):
    both = ("dp", "expert")
    in_specs = (
        P(both, None),
        P(both, None),
        P("dp"),
        P(both, None),
        P(both, None),
        P(both),
        P(both, None),
        P(both, None),
        P(both),
        P(both, None),
        P(both, None),
        P(both),
        P(both, None),
        P(both, None),
        P(both, None),
        P(both, None),
        P("expert", "dp", None),
        P("expert", "dp", None),
        P("expert", "dp", None),
    )
    out_specs = (
        P(both, None),
        P(both, None),
        P(both),
        P(both, None),
        P(both, None),
        P(both),
        P(both, None),
        P(both, None),
        P(both),
        P(both, None),
        P(both, None),
        P(both, None),
        P(both, None),
        P("expert", "dp", None),
        P("expert", "dp", None),
        P("expert", "dp", None),
    )
    return jax.shard_map(shards, mesh=mesh, in_specs=in_specs, out_specs=out_specs, check_vma=False)
```

```python
import jax
import jax.numpy as jnp
import numpy as np
from jax import lax
from jax.experimental import pallas as pl
from jax.experimental.pallas import tpu as pltpu
from jax.sharding import PartitionSpec as P

H = 16
DH = 128
DR = 64
DV = 128
KVR = 512

norm_eps = 1e-06
masked_score = -1e30
MESH = pl.DeviceIdType.MESH
ANY = pl.BlockSpec(memory_space=pl.ANY)
VMEM = pl.BlockSpec(memory_space=pltpu.VMEM)
BF = jnp.bfloat16
F32 = jnp.float32


def rms_norm(values, scale_gain):
    return (
        values
        * lax.rsqrt(jnp.mean(values * values, axis=-1, keepdims=True) + norm_eps)
        * scale_gain
    )


def mm(left, right):
    return jnp.dot(left, right, preferred_element_type=F32)


def mm_rows(left, right):
    return lax.dot_general(left, right, (((0,), (0,)), ((), ())), preferred_element_type=F32)


def mm_cols(left, right):
    return lax.dot_general(left, right, (((1,), (1,)), ((), ())), preferred_element_type=F32)


def slot_places(route_rows, pair_order, capacity):
    pair_expert = route_rows.reshape(-1)
    earlier = pair_order[None, :] < pair_order[:, None]
    same_expert = pair_expert[None, :] == pair_expert[:, None]
    places = jnp.sum((earlier & same_expert).astype(jnp.int32), axis=1)
    slot_index = jnp.where(places < capacity, pair_expert * capacity + places, -1)
    return slot_index.reshape(route_rows.shape)


def turn(values, cos, sin, sign):
    half = DR // 2
    first = lax.rem(lax.broadcasted_iota(jnp.int32, values.shape, 1), DR) < half
    partner = jnp.where(
        first, -pltpu.roll(values, 2 * DR - half, 1), pltpu.roll(values, half, 1)
    )
    return values * cos + sign * (partner * sin)


def causal(i, tile, keep_ref):
    shape = (tile, (i + 1) * tile)
    query = lax.broadcasted_iota(jnp.int32, shape, 0) + i * tile
    key = lax.broadcasted_iota(jnp.int32, shape, 1)
    return (key <= query) & (keep_ref[:, : shape[1]] > 0.5)


def attend_forward(
    tok, gain, wq, wl, gain_lat, we, cos, sin, keep,
    hidden, latent, latent_low, qcat, kcat, value, lse, attended,
):
    per, rows, width = tok.shape
    seq = per * rows
    tile = 2 * rows
    scale = (DH + DR) ** (-0.5)

    def project(i, carry):
        at = pl.ds(pl.multiple_of(i * tile, tile), tile)
        x = tok[pl.ds(2 * i, 2)].reshape(tile, width).astype(F32)
        root = lax.rsqrt(jnp.mean(x * x, axis=-1, keepdims=True) + norm_eps)
        hid = (x * root * gain[...]).astype(BF)
        hidden[at, :] = hid
        c, s = cos[at, :], sin[at, :]
        query = mm(hid, wq[...])
        rope_q = turn(query[:, 2 * DH :], c, s, 1.0).astype(BF)
        lat = mm(hid, wl[...])
        latent[at, :] = lat
        plain = lat[:, :KVR]
        root = lax.rsqrt(jnp.mean(plain * plain, axis=-1, keepdims=True) + norm_eps)
        low = (plain * root * gain_lat[...]).astype(BF)
        latent_low[at, :] = low
        rope = lat[:, KVR : KVR + 2 * DR]
        lane = lax.broadcasted_iota(jnp.int32, rope.shape, 1)
        rope = jnp.where(lane < DR, rope, pltpu.roll(rope, DR, 1))
        rope = turn(rope, c, s, 1.0)
        expanded = mm(low, we[...]).astype(BF)
        for h in range(2):
            qcat[h, at, :DH] = query[:, h * DH : (h + 1) * DH].astype(BF)
            qcat[h, at, DH:] = rope_q
            mine = (lane < DR) if h == 0 else (lane >= DR)
            kcat[h, at, :DH] = expanded[:, h * (DH + DV) : h * (DH + DV) + DH]
            kcat[h, at, DH:] = jnp.where(mine, rope, 0.0).astype(BF)
            value[h, at, :] = expanded[:, h * (DH + DV) + DH : (h + 1) * (DH + DV)]
        return carry

    lax.fori_loop(0, seq // tile, project, 0)
    for h in range(2):
        for i in range(seq // tile):
            at, upto = slice(i * tile, (i + 1) * tile), slice(0, (i + 1) * tile)
            scores = mm_cols(qcat[h, at, :], kcat[h, upto, :]) * scale
            scores = jnp.where(causal(i, tile, keep), scores, masked_score)
            top = jnp.max(scores, axis=-1, keepdims=True)
            exp_scores = jnp.exp(scores - top)
            total = jnp.sum(exp_scores, axis=-1, keepdims=True)
            probs = (exp_scores / total).astype(BF)
            attended[at, h * DV : (h + 1) * DV] = mm(probs, value[h, upto, :]).astype(BF)
            lse[h, at, :] = jnp.broadcast_to(top + jnp.log(total), (tile, lse.shape[2]))


def attend_backward(
    grad, wo, wq, we, cos, sin, keep, qcat, kcat, value, lse, attended,
    gat, grad_wout, dk, dv, grad_query, grad_expanded, grad_rope,
):
    per, rows, width = grad.shape
    seq = per * rows
    tile = 2 * rows
    scale = (DH + DR) ** (-0.5)
    count = seq // tile
    grad_wout[...] = jnp.zeros_like(grad_wout)

    def project(i, carry):
        at = pl.ds(pl.multiple_of(i * tile, tile), tile)
        block = grad[pl.ds(2 * i, 2)].reshape(tile, width)
        gat[at, :] = mm_cols(block, wo[...]).astype(BF)
        grad_wout[...] += mm_rows(attended[at, :], block)
        return carry

    lax.fori_loop(0, count, project, 0)
    for h in range(2):
        dk[...] = jnp.zeros_like(dk)
        dv[...] = jnp.zeros_like(dv)
        for i in range(count):
            at, upto = slice(i * tile, (i + 1) * tile), slice(0, (i + 1) * tile)
            g = gat[at, h * DV : (h + 1) * DV]
            scores = mm_cols(qcat[h, at, :], kcat[h, upto, :]) * scale
            scores = jnp.where(causal(i, tile, keep), scores, masked_score)
            probs = jnp.exp(scores - lse[h, at, 0:1])
            grad_probs = mm_cols(g, value[h, upto, :])
            inner = jnp.sum(grad_probs * probs, axis=-1, keepdims=True)
            raw = (probs * (grad_probs - inner) * scale).astype(BF)
            grad_q = mm(raw, kcat[h, upto, :])
            grad_query[at, h * DH : (h + 1) * DH] = grad_q[:, :DH].astype(BF)
            rope = grad_q[:, DH:]
            lane = lax.broadcasted_iota(jnp.int32, rope.shape, 1)
            mine = (lane < DR) if h == 0 else (lane >= DR)
            rope = turn(rope, cos[at, :], sin[at, :], -1.0).astype(BF)
            if h == 0:
                grad_query[at, 2 * DH :] = rope
            else:
                grad_query[at, 2 * DH :] = jnp.where(mine, rope, grad_query[at, 2 * DH :])
            dk[upto, :] += mm_rows(raw, qcat[h, at, :])
            dv[upto, :] += mm_rows(probs.astype(BF), g)
        grad_expanded[:, h * (DH + DV) : h * (DH + DV) + DH] = dk[:, :DH].astype(BF)
        grad_expanded[:, h * (DH + DV) + DH : (h + 1) * (DH + DV)] = dv[...].astype(BF)
        rope = dk[:, DH:]
        if h == 0:
            grad_rope[...] = rope
        else:
            grad_rope[...] += pltpu.roll(rope, DR, 1)


def params(collective_id):
    return pltpu.CompilerParams(
        collective_id=collective_id, has_side_effects=True, vmem_limit_bytes=60 << 20
    )


def remote(src, dst, send_sem, recv_sem, device):
    return pltpu.make_async_remote_copy(
        src_ref=src,
        dst_ref=dst,
        send_sem=send_sem,
        recv_sem=recv_sem,
        device_id=device,
        device_id_type=MESH,
    )


def greet(devices):
    barrier = pltpu.get_barrier_semaphore()
    for device in devices:
        pl.semaphore_signal(barrier, inc=1, device_id=device, device_id_type=MESH)
    pl.semaphore_wait(barrier, len(devices))


def places(n_dp, n_ex):
    z = lax.axis_index("dp")
    e = lax.axis_index("expert")
    chips = n_ex // 2
    c, k = e // 2, lax.rem(e, 2)
    sibling = (z, e + 1 - 2 * k)
    same_core = [(z, lax.rem(c + i, chips) * 2 + k) for i in range(1, chips)]
    column = [(lax.rem(z + i, n_dp), e) for i in range(1, n_dp)]
    return z, e, c, k, sibling, same_core, column


def wait_recv(region, sem, device):
    remote(region, region, sem, sem, device).wait_recv()


def column_sum(array, rows_out, shared, totals, n_dp, n_ex, inner, collective_id):
    chips = n_ex // 2
    shape = array.shape[1:]
    extra = len(totals)
    _, _, r, ff_s = shared[0].shape

    def kernel(x_hbm, *refs):
        s_in, r_ref, t_refs, refs = refs[:3], refs[3], refs[4 : 4 + extra], refs[4 + extra :]
        o_ref, s_out, r_out, back_refs = refs[0], refs[1:4], refs[4], refs[5 : 5 + extra]
        refs = refs[5 + extra :]
        x_ref, s_v, from_sib, out_buf, from_far = refs[0], refs[1:4], *refs[4:7]
        loads, near_s, near_r, far_s, far_r, r_s, r_r, local = refs[7:15]
        relay_refs, rest = refs[15:18], refs[18:]
        moves = stage([x_hbm, *s_in], [x_ref, *s_v], loads)
        z, e, c, k, sibling, same_core, column = places(n_dp, n_ex)
        greet(same_core + [sibling] + column + [(d[0], sibling[1]) for d in column])
        backs = [
            ExpertsBack(t_refs[m], back_refs[m], rest[7 * m : 7 * m + 7], n_dp, n_ex, inner)
            for m in range(extra)
        ]
        relay = RelaySum(x_ref, relay_refs, n_dp, n_ex, inner)
        near, far, rows_back = {}, {}, []
        for i in list(range(1, chips)) + [0]:
            chip = lax.rem(c + i, chips)
            for m in range(3):
                near[i, m] = remote(
                    s_in[m].at[chip * 2 + 1 - k], from_sib.at[m, i],
                    near_s.at[m, i], near_r.at[m, i], sibling,
                )
                near[i, m].start()
        for back in backs:
            back.begin()
        moves[0].wait()
        relay.begin()
        for back in backs:
            back.pass_on()
        relay.run()
        for i in range(1, chips):
            copy = remote(
                r_ref.at[i], r_out.at[i], r_s.at[i], r_r.at[i], same_core[chips - i - 1]
            )
            copy.start()
            rows_back.append(copy)
        copy = pltpu.make_async_copy(r_ref.at[0], r_out.at[0], local)
        copy.start()
        rows_back.append(copy)

        def pair(i, m):
            chip = lax.rem(c + i, chips)
            near[i, m].wait_recv()

            def row(d, carry):
                out_buf[m, i, d] = (
                    s_v[m][chip * 2 + k, d].astype(F32) + from_sib[m, i, d].astype(F32)
                ).astype(BF)
                return carry

            lax.fori_loop(0, n_dp, row, 0)

        for move in moves[1:]:
            move.wait()
        for i in range(1, chips):
            for m in range(3):
                pair(i, m)
                far[i, m] = remote(
                    out_buf.at[m, i], from_far.at[m, i], far_s.at[m, i], far_r.at[m, i],
                    same_core[i - 1],
                )
                far[i, m].start()
        for m in range(3):
            pair(0, m)
        relay.finish(o_ref)
        for m in range(3):
            for i in range(1, chips):
                far[i, m].wait_recv()

            def row(d, carry, m=m):
                total = out_buf[m, 0, d].astype(F32)
                for i in range(1, chips):
                    total = total + from_far[m, i, d].astype(F32)
                s_out[m][d] = total.astype(BF)
                return carry

            lax.fori_loop(0, n_dp, row, 0)
        for copy in list(near.values()) + list(far.values()):
            copy.wait_send()
        for copy in rows_back:
            copy.wait()
        relay.end()
        for back in backs:
            back.end()

    dma = pltpu.SemaphoreType.DMA
    scratch = like([array, *shared])
    scratch += [pltpu.VMEM((3, chips, n_dp, r, ff_s), BF)] * 3
    scratch += [dma((4,))] + [dma((3, chips))] * 4 + [dma((chips,))] * 2 + [dma]
    scratch += RelaySum.scratch(shape, inner)
    for total in totals:
        scratch += ExpertsBack.scratch(total, n_dp, inner)
    outs = pl.pallas_call(
        kernel,
        out_shape=[jax.ShapeDtypeStruct(shape, F32)]
        + [jax.ShapeDtypeStruct((n_dp, r, ff_s), BF)] * 3
        + [jax.ShapeDtypeStruct(rows_out.shape, BF)]
        + [ExpertsBack.out(total, n_dp, inner) for total in totals],
        in_specs=[ANY] * (5 + extra),
        out_specs=[VMEM] * 4 + [ANY] * (1 + extra),
        scratch_shapes=scratch,
        compiler_params=params(collective_id),
    )(array, *shared, rows_out, *totals)
    return outs[0], outs[1:4], outs[4], outs[5:]


class Relay:
    @staticmethod
    def scratch(inner):
        dma = pltpu.SemaphoreType.DMA
        return [dma((inner,)), dma((inner,)), dma((inner,)), dma]

    def __init__(self, block, out, scratch, n_dp, n_ex, inner):
        self.block, self.out, self.inner = block, out, inner
        self.up_s, self.down_s, self.recv, self.local = scratch
        self.z, self.e, *_ = places(n_dp, n_ex)
        self.mine = lax.rem(self.z, inner)

    def copy(self, source, src, step):
        sem = self.up_s if step > 0 else self.down_s
        return remote(
            src, self.out.at[source], sem.at[source], self.recv.at[source], (self.z + step, self.e)
        )

    def keep(self):
        return pltpu.make_async_copy(self.block, self.out.at[self.mine], self.local)

    def begin(self):
        pl.when(self.mine < self.inner - 1)(lambda: self.copy(self.mine, self.block, 1).start())
        pl.when(self.mine > 0)(lambda: self.copy(self.mine, self.block, -1).start())
        self.keep().start()

    def pass_on(self):
        for t in range(1, self.inner):
            for step in (1, -1):
                source = self.mine - step * t
                exists = source >= 0 if step > 0 else source < self.inner
                more = self.mine < self.inner - 1 if step > 0 else self.mine > 0

                @pl.when(exists)
                def _(source=source, step=step):
                    self.copy(source, self.out.at[source], step).wait_recv()

                @pl.when(jnp.logical_and(exists, more))
                def _(source=source, step=step):
                    self.copy(source, self.out.at[source], step).start()

    def end(self):
        self.keep().wait()
        pl.when(self.mine < self.inner - 1)(
            lambda: self.copy(self.mine, self.block, 1).wait_send()
        )
        pl.when(self.mine > 0)(lambda: self.copy(self.mine, self.block, -1).wait_send())
        for t in range(1, self.inner):
            for step in (1, -1):
                source = self.mine - step * t
                exists = source >= 0 if step > 0 else source < self.inner
                more = self.mine < self.inner - 1 if step > 0 else self.mine > 0

                @pl.when(jnp.logical_and(exists, more))
                def _(source=source, step=step):
                    self.copy(source, self.out.at[source], step).wait_send()


class RelaySum:
    @staticmethod
    def scratch(shape, inner):
        dma = pltpu.SemaphoreType.DMA
        return [pltpu.VMEM((inner + 1,) + shape, BF), dma((inner,)), dma((inner + 1,))]

    def __init__(self, blocks, scratch, n_dp, n_ex, inner):
        self.blocks, self.inner = blocks, inner
        self.buf, self.send, self.recv = scratch
        self.z, self.e, *_ = places(n_dp, n_ex)
        self.mine = lax.rem(self.z, inner)

    def copy(self, t, src, slot, step):
        return remote(
            src, self.buf.at[slot], self.send.at[t], self.recv.at[slot], (self.z + step, self.e)
        )

    def routes(self, t, step):
        inner, mine = self.inner, self.mine
        if step > 0:
            return [(mine < t, mine == 0, t)]
        last = mine == inner - 1
        return [
            (jnp.logical_and(mine > t, mine - 1 != t), last, t),
            (mine - 1 == t, last, inner),
        ]

    def hop(self, t, step, start, edge):
        for active, first, slot in self.routes(t, step):
            if edge:
                pl.when(jnp.logical_and(active, first))(
                    lambda slot=slot: self.copy(t, self.blocks.at[t], slot, step).start()
                )
                continue

            @pl.when(jnp.logical_and(active, first))
            def _(slot=slot):
                if not start:
                    self.copy(t, self.blocks.at[t], slot, step).wait_send()

            @pl.when(jnp.logical_and(active, jnp.logical_not(first)))
            def _(slot=slot):
                copy = self.copy(t, self.buf.at[t], slot, step)
                if start:
                    self.copy(t, self.buf.at[t], t, step).wait_recv()
                    total = self.buf[t].astype(F32) + self.blocks[t].astype(F32)
                    self.buf[t] = total.astype(BF)
                    copy.start()
                else:
                    copy.wait_send()

    def begin(self):
        for t in range(self.inner - 1, 0, -1):
            self.hop(t, 1, True, True)
        for t in range(self.inner - 1):
            self.hop(t, -1, True, True)

    def run(self):
        inner = self.inner

        def up():
            for t in range(inner - 1, 0, -1):
                self.hop(t, 1, True, False)

        def down():
            for t in range(inner - 1):
                self.hop(t, -1, True, False)

        @pl.when(self.mine < inner // 2)
        def _():
            up()
            down()

        @pl.when(self.mine >= inner // 2)
        def _():
            down()
            up()

    def finish(self, out):
        out[...] = self.blocks[self.mine].astype(F32)

        @pl.when(self.mine > 0)
        def _():
            self.copy(0, self.buf.at[self.mine], self.mine, 1).wait_recv()
            out[...] += self.buf[self.mine].astype(F32)

        @pl.when(self.mine < self.inner - 1)
        def _():
            self.copy(0, self.buf.at[self.inner], self.inner, 1).wait_recv()
            out[...] += self.buf[self.inner].astype(F32)

    def end(self):
        for t in range(self.inner):
            if t:
                self.hop(t, 1, False, False)
            if t < self.inner - 1:
                self.hop(t, -1, False, False)


def stage(sources, targets, sems):
    copies = [
        pltpu.make_async_copy(source, target, sems.at[j])
        for j, (source, target) in enumerate(zip(sources, targets))
    ]
    for copy in copies:
        copy.start()
    return copies


def like(arrays):
    return [pltpu.VMEM(array.shape, array.dtype) for array in arrays]


def column_group(z, e, inner):
    start = z // inner * inner
    return [(start + lax.rem(z - start + i, inner), e) for i in range(inner)]


class ExpertsIn:
    @staticmethod
    def scratch(n_dp):
        dma = pltpu.SemaphoreType.DMA
        return [dma((n_dp, 2)), dma((n_dp,)), dma((n_dp,)), dma((n_dp,))]

    @staticmethod
    def out(weight, n_dp, n_ex):
        return jax.ShapeDtypeStruct((n_ex, n_dp) + weight.shape[2:], BF)

    def __init__(self, weight, out, scratch, n_dp, n_ex, inner):
        self.weight, self.out, self.n_dp, self.inner = weight, out, n_dp, inner
        self.send, self.recv, self.sib_send, self.sib_recv = scratch
        self.z, self.e, self.c, self.k, self.sibling, _, _ = places(n_dp, n_ex)
        self.hh = n_ex // 2
        self.local = weight.shape[0]

    def sends(self, start):
        for i in list(range(1, self.n_dp)) + [0]:
            to = lax.rem(self.z + i, self.n_dp)
            expert = lax.rem(to, self.inner)

            def go(i=i, to=to, expert=expert):
                for h in range(2):
                    src = self.weight.at[lax.rem(expert, self.local), pl.ds(h * self.hh, self.hh)]
                    dst = self.out.at[pl.ds(h * self.hh, self.hh), self.z]
                    sem = self.recv.at[self.z]

                    def far(src=src, dst=dst, h=h):
                        copy = remote(src, dst, self.send.at[i, h], sem, (to, 2 * self.c + h))
                        if start:
                            copy.start()
                        else:
                            copy.wait_send()

                    if i:
                        far()
                    else:
                        pl.when(self.k != h)(far)
                        if start:

                            @pl.when(self.k == h)
                            def _(src=src, dst=dst):
                                pltpu.make_async_copy(src, dst, sem).start()

            pl.when(expert // self.local == self.k)(go)

    def begin(self):
        self.sends(True)

    def pass_on(self):
        mine = lax.rem(self.z, self.inner)
        for i in range(self.n_dp):
            d = lax.rem(self.z + self.n_dp - i, self.n_dp)
            region = self.out.at[pl.ds(self.k * self.hh, self.hh), d]
            if i:
                wait_recv(region, self.recv.at[d], self.sibling)
            else:
                from_here = mine // self.local == self.k

                @pl.when(from_here)
                def _(region=region, d=d):
                    src = self.weight.at[
                        lax.rem(mine, self.local), pl.ds(self.k * self.hh, self.hh)
                    ]
                    pltpu.make_async_copy(src, region, self.recv.at[d]).wait()

                @pl.when(jnp.logical_not(from_here))
                def _(region=region, d=d):
                    wait_recv(region, self.recv.at[d], self.sibling)

            remote(
                region, region, self.sib_send.at[i], self.sib_recv.at[i], self.sibling
            ).start()

    def end(self):
        self.sends(False)
        for i in range(self.n_dp):
            d = lax.rem(self.z + self.n_dp - i, self.n_dp)
            mine = self.out.at[pl.ds(self.k * self.hh, self.hh), d]
            remote(
                mine, mine, self.sib_send.at[i], self.sib_recv.at[i], self.sibling
            ).wait_send()
            region = self.out.at[pl.ds((1 - self.k) * self.hh, self.hh), d]
            wait_recv(region, self.sib_recv.at[i], self.sibling)


def gain_rows(gains, target, width, order):
    per = 128 // width
    for t in range(len(order) // per):
        tile = jnp.zeros((8, 128), F32)
        for q in range(per):
            d, e = order[t * per + q]
            piece = gains[d, e, 0:8].astype(F32)
            lane = lax.broadcasted_iota(jnp.int32, piece.shape, 1)
            if q:
                piece = pltpu.roll(piece, q * width, 1)
            tile = jnp.where(lane // width == q, piece, tile)
        target[:, t * 128 : (t + 1) * 128] = tile


def forward_exchange(
    first, tables, w_out, tok, cot, experts, shared, n_dp, n_ex, inner, collective_id
):
    chips = n_ex // 2
    rows, width = tok.shape
    count = len(experts)
    r = w_out.shape[0]
    parts = DV // r
    hp = n_dp // parts
    seq = n_ex * rows
    rl = KVR // (n_dp * n_ex)
    we_cols = rl * hp * (DH + DV) // r
    wq_cols = hp * (DH + DR)

    natural = [(d, j) for d in range(n_dp) for j in range(n_ex)]
    by_owner = [(d, j) for j in range(n_ex) for d in range(n_dp)]

    def kernel(*refs):
        first_in, tables_hbm, keep, refs = refs[:4], refs[4:6], refs[6], refs[7:]
        wo_in, tok_ref, cot_in = refs[:3]
        e_in, s_in = refs[3 : 3 + count], refs[3 + count : 6 + count]
        refs = refs[6 + count :]
        kept_hbm, refs = refs[:12], refs[12:]
        gain_one, gain_ref, gain_lat, res_ref, xcol_ref, cot_out = refs[:6]
        refs = refs[6:]
        w_out, s_out = refs[:count], refs[count : 3 + count]
        refs = refs[3 + count :]
        (cos, sin), (tok_all, wa_ref, gr_ref), refs = refs[:2], refs[2:5], refs[5:]
        kept, refs = refs[:12], refs[12:]
        stage_sem, kept_sem, refs = refs[0], refs[1], refs[2:]
        first_sems, own_sem, refs = refs[:14], refs[14], refs[15:]
        att_out, (wq_ref, we_ref, wo_out, pk_ref) = kept[:8], kept[8:]
        moves = stage(tables_hbm, (cos, sin), stage_sem)
        x_ref, from_sib, out_buf, from_far, xbuf = refs[:5]
        (
            near_s, near_r, far_s, far_r,
            sh_s, sh_r, sp_s, sp_r, sf_s, sf_r, wo_s, wo_r, local,
        ) = refs[5:18]
        x_sems, co_sems, refs = refs[18:22], refs[22:26], refs[26:]
        z, e, c, k, sibling, same_core, column = places(n_dp, n_ex)
        part = lax.rem(e, parts)
        members = [
            (lax.rem(z + i, n_dp), e - part + lax.rem(part + j, parts))
            for i in range(n_dp)
            for j in range(parts)
        ]
        plane = [(z, lax.rem(e + i, n_ex)) for i in range(1, n_ex)]
        greet(plane + column + [(device[0], sibling[1]) for device in column] + members[1:])

        def wo_sends(start):
            for i in range(n_dp):
                target = (lax.rem(z + i, n_dp), e - part + z // hp)
                dst, sem = wo_out.at[lax.rem(z, hp), part], wo_r.at[lax.rem(z, hp), part]

                def far(i=i, target=target, dst=dst, sem=sem):
                    copy = remote(wo_in, dst, wo_s.at[i], sem, target)
                    if start:
                        copy.start()
                    else:
                        copy.wait_send()

                if i:
                    far()
                else:
                    pl.when(z // hp != part)(far)
                    if start:

                        @pl.when(z // hp == part)
                        def _(dst=dst, sem=sem):
                            pltpu.make_async_copy(wo_in, dst, sem).start()

        def wo_arrivals():
            for h in range(hp):
                for p in range(parts):
                    here = jnp.logical_and(part * hp + h == z, part == p)

                    @pl.when(here)
                    def _(h=h, p=p):
                        pltpu.make_async_copy(wo_in, wo_out.at[h, p], wo_r.at[h, p]).wait()

                    @pl.when(jnp.logical_not(here))
                    def _(h=h, p=p):
                        wait_recv(wo_out.at[h, p], wo_r.at[h, p], sibling)

        my_l = lax.rem(z, inner)
        matrices = [
            ExpertsIn(e_in[m], w_out[m], refs[4 * m : 4 * m + 4], n_dp, n_ex, inner)
            for m in range(count)
        ]
        tok_in, wa_in, *packs_in = first_in
        packs = (pk_ref, gr_ref)
        (
            t_send, t_recv, ts_send, ts_recv, a_send, a_recv, az_send, az_recv,
            p_send, p_recv, pf_send, pf_recv, ps_send, ps_recv,
        ) = first_sems
        wa_far, pk_col, tok_far, first_near = [], [], [], []
        for i in range(1, n_ex):
            copy = remote(
                wa_in.at[lax.rem(e + i, n_ex)], wa_ref.at[z, e],
                a_send.at[i], a_recv.at[i], plane[i - 1],
            )
            copy.start()
            wa_far.append(copy)
        for i in range(1, n_dp):
            for m in range(2):
                copy = remote(
                    packs_in[m], packs[m].at[z, e], p_send.at[m, i], p_recv.at[m, i],
                    column[i - 1],
                )
                copy.start()
                pk_col.append(copy)
        for i in range(1, chips):
            copy = remote(tok_in, tok_all.at[e], t_send.at[i], t_recv.at[i], same_core[i - 1])
            copy.start()
            tok_far.append(copy)
        copy = remote(tok_in, tok_all.at[e], ts_send.at[0], ts_recv.at[0], sibling)
        copy.start()
        first_near.append(copy)
        first_own = stage(
            [wa_in.at[e], packs_in[0], packs_in[1], tok_in],
            [wa_ref.at[z, e], pk_ref.at[z, e], gr_ref.at[z, e], tok_all.at[e]],
            own_sem,
        )
        for copy in first_own:
            copy.wait()
        for copy in wa_far:
            copy.wait_recv()
        wa_col = []
        for i in range(1, n_dp):
            copy = remote(
                wa_ref.at[z], wa_ref.at[z], az_send.at[i], az_recv.at[i], column[i - 1]
            )
            copy.start()
            wa_col.append(copy)
        wo_sends(True)
        shared_copies = []
        for i in range(1, n_dp):
            for m in range(3):
                copy = remote(
                    s_in[m].at[lax.rem(lax.rem(z + i, n_dp), inner)], s_out[m].at[e, z],
                    sh_s.at[m, i], sh_r.at[m, i], column[i - 1],
                )
                copy.start()
                shared_copies.append(copy)
        own = [
            pltpu.make_async_copy(s_in[m].at[my_l], s_out[m].at[e, z], local.at[m])
            for m in range(3)
        ]
        for copy in own:
            copy.start()
        matrices[0].begin()
        for copy in pk_col:
            copy.wait_recv()
        pk_far = []
        for m in range(2):
            block = packs[m].at[:, e]
            for i in range(1, chips):
                copy = remote(block, block, pf_send.at[m, i], pf_recv.at[m, i], same_core[i - 1])
                copy.start()
                pk_far.append((i, m, copy))
            copy = remote(block, block, ps_send.at[m, 0], ps_recv.at[m, 0], sibling)
            copy.start()
            first_near.append(copy)
        for i in range(1, chips):
            source = lax.rem(c + chips - i, chips) * 2 + k
            tok_far[i - 1].wait_recv()
            copy = remote(
                tok_all.at[source], tok_all.at[source], ts_send.at[i], ts_recv.at[i], sibling
            )
            copy.start()
            first_near.append(copy)
        for i, m, copy in pk_far:
            copy.wait_recv()
            block = packs[m].at[:, lax.rem(c + chips - i, chips) * 2 + k]
            copy = remote(block, block, ps_send.at[m, i], ps_recv.at[m, i], sibling)
            copy.start()
            first_near.append(copy)
        for copy in first_near + wa_col:
            copy.wait()
        for copy in wa_far + pk_col + tok_far + [copy for _, _, copy in pk_far]:
            copy.wait_send()
        for move in moves:
            move.wait()
        gain_rows(gr_ref, gain_one, r, natural)
        gain_rows(gr_ref, gain_ref, r, by_owner)
        gain_rows(gr_ref, gain_lat, rl, natural)
        wl_ref = pk_ref.reshape(width, pk_ref.shape[3])
        wq_ref[...] = wa_ref[:, :, :, :wq_cols].reshape(width, wq_cols)
        for j in range(r // rl):
            block = wa_ref[:, :, j * rl : (j + 1) * rl, wq_cols:].reshape(KVR, we_cols)
            we_ref[:, j * we_cols : (j + 1) * we_cols] = block
        attend_forward(
            tok_all, gain_one.at[0:1], wq_ref, wl_ref, gain_lat.at[2:3], we_ref, cos, sin, keep,
            *att_out,
        )
        wo_arrivals()
        kept_moves = stage(kept, kept_hbm, kept_sem)
        wo = wo_out[...].reshape(hp * DV, width)

        def project(i, carry):
            at = pl.ds(pl.multiple_of(i * 2 * rows, 2 * rows), 2 * rows)
            block = mm(att_out[7][at, :], wo).astype(BF)
            x_ref[pl.ds(2 * i, 2)] = block.reshape(2, rows, width)
            return carry

        lax.fori_loop(0, chips, project, 0)
        near = []
        for i in list(range(1, chips)) + [0]:
            chip = lax.rem(c + i, chips)
            copy = remote(
                x_ref.at[chip * 2 + 1 - k], from_sib.at[chip], near_s.at[i], near_r.at[i], sibling
            )
            copy.start()
            near.append(copy)
        far = []
        for i in range(1, chips):
            chip = lax.rem(c + i, chips)
            near[i - 1].wait_recv()
            out_buf[i] = (
                x_ref[chip * 2 + k].astype(F32) + from_sib[chip].astype(F32)
            ).astype(BF)
            copy = remote(out_buf.at[i], from_far.at[i], far_s.at[i], far_r.at[i], same_core[i - 1])
            copy.start()
            far.append(copy)
        near[chips - 1].wait_recv()
        res_ref[...] = x_ref[e].astype(F32) + from_sib[c].astype(F32) + tok_ref[...].astype(F32)
        for i in range(1, chips):
            far[i - 1].wait_recv()
            res_ref[...] += from_far[i].astype(F32)
        residual = res_ref[...]
        scale = lax.rsqrt(jnp.mean(residual * residual, axis=-1, keepdims=True) + norm_eps)
        xbuf[...] = (residual * scale * gain_ref[1:2, :]).astype(BF)
        relays = [
            Relay(xbuf, xcol_ref, x_sems, n_dp, n_ex, inner),
            Relay(cot_in, cot_out, co_sems, n_dp, n_ex, inner),
        ]
        relays[0].begin()
        relays[0].pass_on()
        relays[1].begin()
        for matrix in matrices[1:]:
            matrix.begin()
        for copy in own:
            copy.wait()
        for copy in shared_copies:
            copy.wait_recv()
        plane, to_sib = [], []
        for m in range(3):
            block = s_out[m].at[e]
            for i in range(1, chips):
                copy = remote(block, block, sp_s.at[m, i], sp_r.at[m, i], same_core[i - 1])
                copy.start()
                plane.append(copy)
            copy = remote(block, block, sf_s.at[m, 0], sf_r.at[m, 0], sibling)
            copy.start()
            to_sib.append(copy)
        for m in range(3):
            for i in range(1, chips):
                plane[m * (chips - 1) + i - 1].wait_recv()
                block = s_out[m].at[lax.rem(c + chips - i, chips) * 2 + k]
                copy = remote(block, block, sf_s.at[m, i], sf_r.at[m, i], sibling)
                copy.start()
                to_sib.append(copy)
        relays[1].pass_on()
        for matrix in matrices:
            matrix.pass_on()
        for copy in to_sib:
            copy.wait()
        for relay in relays:
            relay.end()
        for copy in plane + shared_copies + near + far:
            copy.wait_send()
        wo_sends(False)
        for move in kept_moves:
            move.wait()
        for matrix in matrices:
            matrix.end()

    dma = pltpu.SemaphoreType.DMA
    ff_s = shared[0].shape[2]
    scratch = []
    for _ in experts:
        scratch += ExpertsIn.scratch(n_dp)
    sds = jax.ShapeDtypeStruct
    kept = [
        sds((seq, width), BF),
        sds((seq, first[2].shape[1]), F32),
        sds((seq, KVR), BF),
        sds((2, seq, 2 * DH), BF),
        sds((2, seq, 2 * DH), BF),
        sds((2, seq, DV), BF),
        sds((2, seq, 128), F32),
        sds((seq, 2 * DV), BF),
        sds((width, wq_cols), BF),
        sds((KVR, hp * (DH + DV)), BF),
        sds((hp, parts, r, width), BF),
        sds((n_dp, n_ex) + first[2].shape, BF),
    ]
    outs = pl.pallas_call(
        kernel,
        out_shape=kept
        + [
            sds((8, width), F32),
            sds((8, width), F32),
            sds((8, KVR), F32),
            sds((rows, width), F32),
            sds((inner, rows, width), BF),
            sds((inner, rows, width), BF),
        ]
        + [ExpertsIn.out(w, n_dp, n_ex) for w in experts]
        + [sds((n_ex, n_dp, r, ff_s), BF)] * 3,
        in_specs=[ANY] * 6 + [VMEM, ANY, VMEM] + [ANY] * (4 + count),
        out_specs=[ANY] * 12 + [VMEM] * 4 + [ANY] * (5 + count),
        scratch_shapes=like(tables[:2])
        + [
            pltpu.VMEM((n_ex, rows, width), BF),
            pltpu.VMEM((n_dp,) + first[1].shape, BF),
            pltpu.VMEM((n_dp, n_ex) + first[3].shape, BF),
        ]
        + like(kept)
        + [dma((2,)), dma((12,))]
        + [dma((chips,))] * 4
        + [dma((n_ex,))] * 2
        + [dma((n_dp,))] * 2
        + [dma((2, n_dp))] * 2
        + [dma((2, chips))] * 4
        + [dma((4,))]
        + [pltpu.VMEM((n_ex, rows, width), BF)]
        + [pltpu.VMEM((chips, rows, width), BF)] * 3
        + [pltpu.VMEM((rows, width), BF)]
        + [dma((chips,))] * 4
        + [dma((3, n_dp))] * 2
        + [dma((3, chips))] * 4
        + [dma((n_dp,)), dma((hp, parts)), dma((3,))]
        + Relay.scratch(inner) * 2
        + scratch,
        compiler_params=params(collective_id),
    )(*first, *tables, w_out, tok, cot, *experts, *shared)
    return outs[:8], outs[8:12], outs[12:15], outs[15:18], outs[18 : 18 + count], outs[18 + count :]


def silu_parts(a):
    sig = 1.0 / (1.0 + jnp.exp(-a))
    return a * sig, sig * (1.0 + a * (1.0 - sig))


def dispatch(hot, x, cot, shared, weights, n_dp, n_ex, inner, collective_id):
    chips = n_ex // 2
    rows, width = x.shape
    ff = shared[0].shape[1]
    tile = 256

    per_far = hot.shape[0] // chips
    count = len(weights)

    def kernel(hot_ref, x_hbm, c_hbm, g_hbm, u_hbm, d_hbm, *refs):
        w_in, refs = refs[:count], refs[count:]
        o_ref, go_ref, w_out, refs = refs[0], refs[1], refs[2 : 2 + count], refs[2 + count :]
        results, refs = refs[:5], refs[5:]
        hot_v, x_v, c_v, g_v, u_v, d_v, hid, ga, gb, b_v, send, recv, loads, keep = refs[:14]
        out_ref, dx_ref, gg_ref, gu_ref, gd_ref = refs[14:19]
        results_sem, rest = refs[19], refs[20:]
        z, e, c, k, sibling, same_core, column = places(n_dp, n_ex)
        moves = [
            pltpu.make_async_copy(src, dst, loads.at[j])
            for j, (src, dst) in enumerate(
                [
                    (hot_ref, hot_v), (x_hbm, x_v), (c_hbm, c_v),
                    (g_hbm, g_v), (u_hbm, u_v), (d_hbm, d_v),
                ]
            )
        ]
        for copy in moves:
            copy.start()
        greet(same_core + [sibling] + column + [(device[0], sibling[1]) for device in column])
        matrices = [
            ExpertsIn(w_in[m], w_out[m], rest[4 * m : 4 * m + 4], n_dp, n_ex, inner)
            for m in range(count)
        ]
        for matrix in matrices:
            matrix.begin()
        copies = []
        for j, (source, target) in enumerate(((x_v, o_ref), (c_v, go_ref))):
            if not j:
                moves[0].wait()
            moves[1 + j].wait()
            for i in list(range(1, chips)) + [0]:
                block = mm(hot_v[i * per_far : (i + 1) * per_far, :], source[...])
                b_v[j, i] = block.astype(BF)
                if i:
                    copy = remote(
                        b_v.at[j, i], target.at[i], send.at[j, i], recv.at[j, i],
                        same_core[i - 1],
                    )
                else:
                    copy = pltpu.make_async_copy(b_v.at[j, 0], target.at[0], keep.at[j])
                copy.start()
                copies.append(copy)
        for copy in moves[3:]:
            copy.wait()

        def rows_of(i, carry):
            at = pl.ds(pl.multiple_of(i * tile, tile), tile)
            first = mm(x_v[at, :], g_v[...])
            second = mm(x_v[at, :], u_v[...])
            silu, slope = silu_parts(first)
            low = (silu * second).astype(BF)
            hid[at, :] = low
            out_ref[at, :] = mm_cols(low, d_v[...])
            back = mm(c_v[at, :], d_v[...])
            low_a = (back * second * slope).astype(BF)
            low_b = (back * silu).astype(BF)
            ga[at, :] = low_a
            gb[at, :] = low_b
            dx_ref[at, :] = mm_cols(low_a, g_v[...]) + mm_cols(low_b, u_v[...])
            return carry

        lax.fori_loop(0, rows // tile, rows_of, 0)

        def columns_of(j, carry):
            at = pl.ds(pl.multiple_of(j * tile, tile), tile)
            gg_ref[at, :] = mm_rows(x_v[:, at], ga[...]).astype(BF)
            gu_ref[at, :] = mm_rows(x_v[:, at], gb[...]).astype(BF)
            gd_ref[at, :] = mm_rows(c_v[:, at], hid[...]).astype(BF)
            return carry

        lax.fori_loop(0, width // tile, columns_of, 0)
        result_moves = stage([out_ref, dx_ref, gg_ref, gu_ref, gd_ref], results, results_sem)
        for matrix in matrices:
            matrix.pass_on()
        for copy in copies + result_moves:
            copy.wait()
        for matrix in matrices:
            matrix.end()

    dma = pltpu.SemaphoreType.DMA
    sds = jax.ShapeDtypeStruct
    vmem = pltpu.VMEM
    scratch = []
    for _ in weights:
        scratch += ExpertsIn.scratch(n_dp)
    results = [sds((rows, width), F32)] * 2 + [sds((width, ff), BF)] * 3
    outs = pl.pallas_call(
        kernel,
        out_shape=[sds((chips, per_far, width), BF)] * 2
        + [ExpertsIn.out(weight, n_dp, n_ex) for weight in weights]
        + results,
        in_specs=[ANY] * (6 + count),
        out_specs=[ANY] * (7 + count),
        scratch_shapes=[vmem(hot.shape, BF)]
        + [vmem((rows, width), BF)] * 2
        + [vmem((width, ff), BF)] * 3
        + [vmem((rows, ff), BF)] * 3
        + [vmem((2, chips, per_far, width), BF)]
        + [dma((2, chips)), dma((2, chips)), dma((6,)), dma((2,))]
        + like(results)
        + [dma((5,))]
        + scratch,
        compiler_params=params(collective_id),
    )(hot, x, cot, *shared, *weights)
    return outs[:2], outs[2 : 2 + count], outs[2 + count], outs[3 + count], outs[4 + count :]


def experts_run(x_in, grad_in, weights, router, n_dp, n_ex, inner, collective_id):
    chips = n_ex // 2
    n_slots, width = x_in.shape
    ff = weights[0].shape[1]
    per_far = n_slots // chips
    r = width // (n_dp * n_ex)
    tile = per_far
    span = n_dp * r
    n_experts = inner * chips

    def kernel(*refs):
        in_hbm, refs = refs[:6], refs[6:]
        dx_out, dots_out, rows_out, back_out, g_out, refs = *refs[:4], refs[4:6], refs[6:]
        x_v, s_v, wg, wu, wd, route, a_v, b_v, h_v, dx_v, total, stage, dots_v, g_v = refs[:14]
        loads, send, recv, d_send, d_recv, local, rows_sem, out_sem = refs[14:22]
        z, e, c, k, sibling, same_core, column = places(n_dp, n_ex)
        moves = [
            pltpu.make_async_copy(src, dst, loads.at[j])
            for j, (src, dst) in enumerate(zip(in_hbm, (x_v, s_v, wg, wu, wd, route)))
        ]
        for j in (5, 0, 2, 3, 4, 1):
            moves[j].start()
        greet(same_core + [sibling] + column + [(device[0], sibling[1]) for device in column])
        back = ExpertsBack(total, back_out, refs[22:], n_dp, n_ex, inner, True)
        expert = c * inner + lax.rem(z, inner)
        for j in (5, 0, 2, 3, 4, 1):
            moves[j].wait()

        def forward(i, carry):
            at = pl.ds(pl.multiple_of(i * tile, tile), tile)
            x = x_v[at, :]
            logits = mm(x, route[...])
            lane = lax.broadcasted_iota(jnp.int32, logits.shape, 1)
            logits = jnp.where(lane < n_experts, logits, masked_score)
            chances = jnp.exp(logits - jnp.max(logits, axis=-1, keepdims=True))
            gate = jnp.sum(jnp.where(lane == expert, chances, 0.0), axis=-1, keepdims=True)
            gate = gate / jnp.sum(chances, axis=-1, keepdims=True)
            first = mm(x, wg[...])
            second = mm(x, wu[...])
            a_v[at, :] = first.astype(BF)
            b_v[at, :] = second.astype(BF)
            hid = (silu_parts(first)[0] * second).astype(BF)
            h_v[at, :] = hid
            g_v[at, :] = s_v[at, :]
            s_v[at, :] = (gate * s_v[at, :].astype(F32)).astype(BF)
            return carry

        lax.fori_loop(0, chips, forward, 0)

        for j in range(n_ex // 2):
            at = pl.ds(pl.multiple_of(((1 - k) * (n_ex // 2) + j) * span, span), span)
            block = mm_rows(s_v[:, at], h_v[...]).astype(BF)
            total[j] = block.reshape(n_dp, r, ff)
            back.near(j).start()
        for j in range(n_ex // 2):
            at = pl.ds(pl.multiple_of((k * (n_ex // 2) + j) * span, span), span)
            block = mm_rows(s_v[:, at], h_v[...]).astype(BF)
            back.own[j] = block.reshape(n_dp, r, ff)
        back.pass_on()

        def rows_of(i, carry):
            at = pl.ds(pl.multiple_of(i * tile, tile), tile)
            rows = mm_cols(h_v[at, :], wd[...]).astype(BF)
            dx_v[i] = rows
            dots = jnp.sum(
                g_v[at, :].astype(F32) * rows.astype(F32), axis=-1, keepdims=True
            )
            dots_v[i] = jnp.broadcast_to(dots, (tile, 128)).astype(BF)
            pltpu.make_async_copy(dx_v.at[i], rows_out.at[i], rows_sem.at[i]).start()
            return carry

        lax.fori_loop(0, chips, rows_of, 0)
        dot_copies = []
        for i in range(1, chips):
            copy = remote(
                dots_v.at[i], dots_out.at[i], d_send.at[i], d_recv.at[i], same_core[chips - i - 1]
            )
            copy.start()
            dot_copies.append(copy)
        copy = pltpu.make_async_copy(dots_v.at[0], dots_out.at[0], local.at[0])
        copy.start()
        dot_copies.append(copy)

        def hidden_rows(i, carry):
            at = pl.ds(pl.multiple_of(i * tile, tile), tile)
            grad = mm(s_v[at, :], wd[...])
            silu, slope = silu_parts(a_v[at, :].astype(F32))
            second = b_v[at, :].astype(F32)
            a_v[at, :] = (grad * second * slope).astype(BF)
            b_v[at, :] = (grad * silu).astype(BF)
            return carry

        lax.fori_loop(0, chips, hidden_rows, 0)
        copies = []
        for i in list(range(1, chips)) + [0]:
            at = slice(i * per_far, (i + 1) * per_far)
            block = mm_cols(a_v[at, :], wg[...]) + mm_cols(b_v[at, :], wu[...])
            pltpu.make_async_copy(dx_v.at[i], rows_out.at[i], rows_sem.at[i]).wait()
            dx_v[i] = block.astype(BF)
            if i:
                copy = remote(
                    dx_v.at[i], dx_out.at[i], send.at[i], recv.at[i], same_core[chips - i - 1]
                )
            else:
                copy = pltpu.make_async_copy(dx_v.at[0], dx_out.at[0], local.at[1])
            copy.start()
            copies.append(copy)

        def other_rows(j, carry):
            at = pl.ds(pl.multiple_of(j * span, span), span)
            for m, side in enumerate((a_v, b_v)):

                @pl.when(j > 0)
                def _(m=m):
                    pltpu.make_async_copy(stage.at[m], g_out[m].at[j - 1], out_sem.at[m]).wait()

                block = mm_rows(x_v[:, at], side[...]).astype(BF)
                stage[m] = block.reshape(n_dp, r, ff)
                pltpu.make_async_copy(stage.at[m], g_out[m].at[j], out_sem.at[m]).start()
            return carry

        lax.fori_loop(0, n_ex, other_rows, 0)
        for m in range(2):
            pltpu.make_async_copy(stage.at[m], g_out[m].at[n_ex - 1], out_sem.at[m]).wait()
        for copy in copies + dot_copies:
            copy.wait()
        back.end()

    dma = pltpu.SemaphoreType.DMA
    sds = jax.ShapeDtypeStruct
    vmem = pltpu.VMEM
    total = sds((n_ex, n_dp, r, ff), BF)
    blocks = sds((chips, per_far, width), BF)
    dots = sds((chips, per_far, 128), BF)
    outs = pl.pallas_call(
        kernel,
        out_shape=[blocks, dots, blocks, ExpertsBack.out(total, n_dp, inner), total, total],
        in_specs=[ANY] * 6,
        out_specs=[ANY] * 6,
        scratch_shapes=[vmem((n_slots, width), BF)] * 2
        + [vmem((width, ff), BF)] * 3
        + [vmem((width, 128), BF)]
        + [vmem((n_slots, ff), BF)] * 3
        + [
            vmem(blocks.shape, BF),
            vmem((n_ex // 2,) + total.shape[1:], BF),
            vmem((2, n_dp, r, ff), BF),
            vmem(dots.shape, BF),
            vmem((n_slots, width), BF),
            dma((6,)),
        ]
        + [dma((chips,))] * 4
        + [dma((2,)), dma((chips,)), dma((2,))]
        + ExpertsBack.scratch(total, n_dp, inner),
        compiler_params=params(collective_id),
    )(x_in, grad_in, *weights, router)
    return outs[0], outs[1], outs[2], outs[3], outs[4:]


class ExpertsBack:
    @staticmethod
    def scratch(total, n_dp, inner):
        n_ex, _, r, ff = total.shape
        dma = pltpu.SemaphoreType.DMA
        hh = n_ex // 2
        return [
            pltpu.VMEM((hh, n_dp, r, ff), BF),
            pltpu.VMEM((hh, n_dp, r, ff), BF),
            dma((hh,)),
            dma((hh,)),
            dma((hh,)),
            dma((hh, n_dp)),
            dma((n_dp // inner, 2, 2, hh)),
        ]

    @staticmethod
    def out(total, n_dp, inner):
        n_ex, _, r, ff = total.shape
        return jax.ShapeDtypeStruct((n_dp // inner, 2, n_ex, r, ff), BF)

    def __init__(self, total, out, scratch, n_dp, n_ex, inner, halved=False):
        self.total, self.out, self.n_dp, self.inner, self.halved = total, out, n_dp, inner, halved
        self.own, self.sib, self.near_s, self.near_r, self.load, self.send, self.recv = scratch
        self.z, self.e, self.c, self.k, self.sibling, _, _ = places(n_dp, n_ex)
        self.hh = n_ex // 2

    def near(self, j):
        return remote(
            self.total.at[j if self.halved else (1 - self.k) * self.hh + j], self.sib.at[j],
            self.near_s.at[j], self.near_r.at[j], self.sibling,
        )

    def loads(self, j):
        return pltpu.make_async_copy(
            self.total.at[self.k * self.hh + j], self.own.at[j], self.load.at[j]
        )

    def begin(self):
        for j in range(self.hh):
            self.near(j).start()
            self.loads(j).start()

    def route(self, j, i):
        d = lax.rem(self.z + i, self.n_dp)
        expert = lax.rem(self.z, self.inner)
        o = self.z // self.inner
        dst = self.out.at[o, lax.rem(expert, 2), self.k * self.hh + j]
        sem = self.recv.at[o, lax.rem(expert, 2), self.k, j]
        return self.own.at[j, d], dst, sem, (d, 2 * self.c + expert // 2)

    def stay(self, j):
        src, dst, sem, _ = self.route(j, 0)
        return pltpu.make_async_copy(src, dst, sem)

    def go(self, j, i):
        src, dst, sem, device = self.route(j, i)
        return remote(src, dst, self.send.at[j, i], sem, device)

    def here(self):
        return lax.rem(self.z, self.inner) // 2 == self.k

    def pass_on(self):
        for j in range(self.hh):
            self.near(j).wait_recv()
            if not self.halved:
                self.loads(j).wait()
            for d in range(self.n_dp):
                self.own[j, d] = (
                    self.own[j, d].astype(F32) + self.sib[j, d].astype(F32)
                ).astype(BF)
            for i in range(1, self.n_dp):
                self.go(j, i).start()
            pl.when(self.here())(lambda j=j: self.stay(j).start())
            pl.when(jnp.logical_not(self.here()))(lambda j=j: self.go(j, 0).start())

    def end(self):
        for j in range(self.hh):
            self.near(j).wait_send()
            for i in range(1, self.n_dp):
                self.go(j, i).wait_send()
            pl.when(jnp.logical_not(self.here()))(lambda j=j: self.go(j, 0).wait_send())
        for o in range(self.n_dp // self.inner):
            for i in range(2):
                for h in range(2):
                    source = o * self.inner + 2 * self.k + i
                    here = jnp.logical_and(source == self.z, self.k == h)
                    for j in range(self.hh):
                        region = self.out.at[o, i, h * self.hh + j]
                        sem = self.recv.at[o, i, h, j]

                        @pl.when(here)
                        def _(region=region, sem=sem, j=j):
                            pltpu.make_async_copy(self.own.at[j, self.z], region, sem).wait()

                        @pl.when(jnp.logical_not(here))
                        def _(region=region, sem=sem):
                            wait_recv(region, sem, self.sibling)


def rms_back(x, gain, grad):
    root = lax.rsqrt(jnp.mean(x * x, axis=-1, keepdims=True) + norm_eps)
    scaled = grad * gain
    along = jnp.mean(x * scaled, axis=-1, keepdims=True)
    return root * scaled - x * (root * root * root) * along, grad * x * root


def backward_exchange(
    grad, attend, hidden, latent_low, own, out, shared, totals, n_dp, n_ex, inner, collective_id
):
    chips = n_ex // 2
    rows, width = grad.shape
    seq = n_ex * rows
    extra = len(totals)
    wq, we = attend[1], attend[2]
    lat_cols = KVR + 2 * DR
    r = width // (n_dp * n_ex)
    rl = KVR // (n_dp * n_ex)
    parts = DV // r
    hp = n_dp // parts
    n_dev = n_dp * n_ex
    wq_cols = wq.shape[1]
    we_cols = rl * we.shape[1] // r
    head_cols = wq_cols + we_cols
    given_arrays = [*attend, hidden, latent_low, *own]
    big = [j for j, array in enumerate(given_arrays) if array.shape[0] > 8 or array.ndim > 2]

    def kernel(*refs):
        grad_ref, given, refs = refs[0], list(refs[1:22]), refs[22:]
        out_ref, sh_in, refs = refs[0], refs[1:4], refs[4:]
        t_refs, refs = refs[:extra], refs[extra:]
        tok_out, vec_out, pack_out, heads_mid, heads_out, wout_out, out_got = refs[:7]
        sh_out, back_refs, refs = refs[7:10], refs[10 : 10 + extra], refs[10 + extra :]
        gbuf, att_tmp, refs = refs[0], refs[1:8], refs[8:]
        part_l, bufs, sums, refs = refs[0], refs[1:7], refs[7:9], refs[9:]
        hsrc, wsrc, pack, psib, pout, pfar, psum, pbuf, vec, vbuf, vzbuf = refs[:11]
        refs = refs[11:]
        t_s, t_r, ts_s, ts_r, local = refs[:5]
        sems, refs = refs[5:13], refs[13:]
        (
            h_s, h_r, hz_s, hz_r, w_s, w_r, pn_s, pn_r, pf_s, pf_r, pc_s, pc_r, s_s, s_r,
            v_s, v_r, vz_s, vz_r, o_s, o_r,
        ) = refs[:20]
        staged, stage_sem, rest = refs[20 : 20 + len(big)], refs[20 + len(big)], refs[21 + len(big) :]
        moves = stage([given[j] for j in big], staged, stage_sem)
        for j, ref in zip(big, staged):
            given[j] = ref
        att_in, hidden_ref, low_ref = given[:11], given[11], given[12]
        wl_ref, lat_ref, tok_ref, gain_ref, glat_ref, gnat_ref, router_ref, gtwo_ref = given[13:]
        gain_ref, glat_ref = gain_ref.at[0:1], glat_ref.at[2:3]
        x_refs = (gbuf, part_l)
        group = column_group(lax.axis_index("dp"), lax.axis_index("expert"), inner)
        z, e, c, k, sibling, same_core, column = places(n_dp, n_ex)
        plane = [(z, lax.rem(e + i, n_ex)) for i in range(1, n_ex)]
        part = lax.rem(e, parts)
        members = [
            (lax.rem(z + i, n_dp), e - part + lax.rem(part + j, parts))
            for i in range(n_dp)
            for j in range(parts)
        ]
        greet(plane + column + [(d[0], sibling[1]) for d in column] + members[1:])
        backs = [
            ExpertsBack(t_refs[m], back_refs[m], rest[7 * m : 7 * m + 7], n_dp, n_ex, inner)
            for m in range(extra)
        ]
        gather, to_sib, others = [], [], []
        for i in range(1, chips):
            copy = remote(grad_ref, gbuf.at[e], t_s.at[i], t_r.at[i], same_core[i - 1])
            copy.start()
            gather.append(copy)
        copy = remote(grad_ref, gbuf.at[e], ts_s.at[0], ts_r.at[0], sibling)
        copy.start()
        to_sib.append(copy)
        keep = pltpu.make_async_copy(grad_ref, gbuf.at[e], local.at[0])
        keep.start()
        for back in backs:
            back.begin()
        for m in range(3):
            for i in range(1, n_dp):
                copy = remote(
                    sh_in[m].at[lax.rem(z + i, n_dp)], sh_out[m].at[z],
                    s_s.at[m, i], s_r.at[m, i], column[i - 1],
                )
                copy.start()
                others.append(copy)
            copy = pltpu.make_async_copy(sh_in[m].at[z], sh_out[m].at[z], local.at[1 + m])
            copy.start()
            others.append(copy)
        mine = lax.rem(z, inner)
        for i in range(1, inner):
            copy = remote(
                out_ref.at[lax.rem(mine + i, inner)], out_got.at[mine], o_s.at[i], o_r.at[i],
                group[i],
            )
            copy.start()
            others.append(copy)
        copy = pltpu.make_async_copy(out_ref.at[mine], out_got.at[mine], local.at[5])
        copy.start()
        others.append(copy)
        for i in range(1, chips):
            gather[i - 1].wait_recv()
            block = gbuf.at[lax.rem(c + chips - i, chips) * 2 + k]
            copy = remote(block, block, ts_s.at[i], ts_r.at[i], sibling)
            copy.start()
            to_sib.append(copy)
        for back in backs:
            back.pass_on()
        keep.wait()
        for copy in to_sib:
            copy.wait_recv()
        for copy in gather + to_sib:
            copy.wait_send()
        gat, grad_wout, dk, dv, grad_query, grad_expanded, grad_rope = att_tmp
        for move in moves:
            move.wait()
        attend_backward(gbuf, *att_in, *att_tmp)

        wsrc[...] = grad_wout[...].astype(BF).reshape(hp, parts, r, width)

        def wout_sends(start):
            for h in range(hp):
                for p in range(parts):
                    target = (part * hp + h, e - part + p)
                    here = jnp.logical_and(part * hp + h == z, p == part)

                    def far(h=h, p=p, target=target):
                        copy = remote(
                            wsrc.at[h, p], wout_out.at[z], w_s.at[h, p], w_r.at[z], target
                        )
                        if start:
                            copy.start()
                        else:
                            copy.wait_send()

                    pl.when(jnp.logical_not(here))(far)
                    if start:

                        @pl.when(here)
                        def _(h=h, p=p):
                            pltpu.make_async_copy(
                                wsrc.at[h, p], wout_out.at[z], w_r.at[z]
                            ).start()

        wout_sends(True)

        def spread(i, carry):
            at = pl.ds(pl.multiple_of(i * 2 * rows, 2 * rows), 2 * rows)
            block = mm_cols(grad_query[at, :], att_in[1][...]).astype(BF)
            gbuf[pl.ds(2 * i, 2)] = block.reshape(2, rows, width)
            block = mm_cols(grad_expanded[at, :], att_in[2][...]).astype(BF)
            part_l[pl.ds(2 * i, 2), :, :KVR] = block.reshape(2, rows, KVR)
            block = grad_rope[at, :].astype(BF)
            part_l[pl.ds(2 * i, 2), :, KVR:] = block.reshape(2, rows, 2 * DR)
            return carry

        lax.fori_loop(0, chips, spread, 0)
        near, far = {}, {}
        for i in list(range(1, chips)) + [0]:
            chip = lax.rem(c + i, chips)
            for j in range(2):
                near[i, j] = remote(
                    x_refs[j].at[chip * 2 + 1 - k],
                    bufs[3 * j].at[chip],
                    sems[4 * j].at[i],
                    sems[4 * j + 1].at[i],
                    sibling,
                )
                near[i, j].start()
        for i in range(1, chips):
            chip = lax.rem(c + i, chips)
            for j in range(2):
                from_sib, out_buf, from_far = bufs[3 * j : 3 * j + 3]
                near[i, j].wait_recv()
                out_buf[i] = (
                    x_refs[j][chip * 2 + k].astype(F32) + from_sib[chip].astype(F32)
                ).astype(BF)
                far[i, j] = remote(
                    out_buf.at[i],
                    from_far.at[i],
                    sems[4 * j + 2].at[i],
                    sems[4 * j + 3].at[i],
                    same_core[i - 1],
                )
                far[i, j].start()

        per_tile = 256 // r

        def wq_rows(i, carry):
            at = pl.ds(pl.multiple_of(i * 256, 256), 256)
            block = mm_rows(hidden_ref[:, at], grad_query[...]).astype(BF)
            hsrc[pl.ds(i * per_tile, per_tile), :, :wq_cols] = block.reshape(
                per_tile, r, wq_cols
            )
            return carry

        lax.fori_loop(0, width // 256, wq_rows, 0)
        grad_we = mm_rows(low_ref[...], grad_expanded[...]).astype(BF)
        for j in range(r // rl):
            block = grad_we[:, j * we_cols : (j + 1) * we_cols]
            hsrc[:, j * rl : (j + 1) * rl, wq_cols:] = block.reshape(n_dev, rl, we_cols)
        heads_far = []
        for i in range(1, n_ex):
            for d in range(n_dp):
                copy = remote(
                    hsrc.at[d * n_ex + lax.rem(e + i, n_ex)], heads_mid.at[d, e],
                    h_s.at[i, d], h_r.at[i, d], plane[i - 1],
                )
                copy.start()
                heads_far.append(copy)
        for d in range(n_dp):
            copy = pltpu.make_async_copy(
                hsrc.at[d * n_ex + e], heads_mid.at[d, e], h_r.at[0, d]
            )
            copy.start()
            copy.wait()
        for j in range(2):
            near[0, j].wait_recv()
            sums[j][...] = x_refs[j][e].astype(F32) + bufs[3 * j][c].astype(F32)
        for i in range(1, chips):
            for j in range(2):
                far[i, j].wait_recv()
                sums[j][...] += bufs[3 * j + 2][i].astype(F32)

        at = pl.ds(pl.multiple_of(e * rows, rows), rows)
        cos, sin = att_in[3][at, :], att_in[4][at, :]
        lat_grad, lat_gain = rms_back(lat_ref[:, :KVR], glat_ref[...], sums[1][:, :KVR])
        rope = turn(sums[1][:, KVR:], cos, sin, -1.0)
        lane = lax.broadcasted_iota(jnp.int32, rope.shape, 1)
        rope = jnp.where(lane < DR, rope, 0.0)
        low = jnp.concatenate([lat_grad, rope], axis=1).astype(BF)
        total = sums[0][...] + mm_cols(low, wl_ref[:, :lat_cols])
        tok_grad, tok_gain = rms_back(tok_ref[...].astype(F32), gain_ref[...], total)
        tok_out[...] = gnat_ref[...] + tok_grad
        vec[...] = jnp.zeros_like(vec)
        vec[0:1, :] = jnp.sum(tok_gain, axis=0, keepdims=True)
        vec[1:2, :] = gtwo_ref[...]
        vec[2:3, :KVR] = jnp.sum(lat_gain, axis=0, keepdims=True)
        vec_far = []
        for i in range(1, n_ex):
            copy = remote(vec, vbuf.at[i], v_s.at[i], v_r.at[i], plane[i - 1])
            copy.start()
            vec_far.append(copy)
        for d in range(n_dp):
            block = hidden_ref[at, d * n_ex * r : (d + 1) * n_ex * r]
            block = mm_rows(block, low).reshape(n_ex, r, lat_cols)
            pack[:, d * r : (d + 1) * r, :KVR] = block[:, :, :KVR].astype(BF)
            block = block[:, :, KVR:] + router_ref[:, d * r : (d + 1) * r].astype(F32)
            pack[:, d * r : (d + 1) * r, KVR:] = block.astype(BF)
        pack_near, pack_far = [], []
        for i in list(range(1, chips)) + [0]:
            chip = lax.rem(c + i, chips)
            copy = remote(pack.at[chip * 2 + 1 - k], psib.at[chip], pn_s.at[i], pn_r.at[i], sibling)
            copy.start()
            pack_near.append(copy)
        for copy in heads_far:
            copy.wait_recv()
        heads_col = []
        for i in range(1, n_dp):
            d = lax.rem(z + i, n_dp)
            copy = remote(
                heads_mid.at[d], heads_out.at[z], hz_s.at[i], hz_r.at[i], column[i - 1]
            )
            copy.start()
            heads_col.append(copy)
        copy = pltpu.make_async_copy(heads_mid.at[z], heads_out.at[z], local.at[4])
        copy.start()
        heads_col.append(copy)
        for i in range(1, chips):
            chip = lax.rem(c + i, chips)
            pack_near[i - 1].wait_recv()
            pout[i] = (pack[chip * 2 + k].astype(F32) + psib[chip].astype(F32)).astype(BF)
            copy = remote(pout.at[i], pfar.at[i], pf_s.at[i], pf_r.at[i], same_core[i - 1])
            copy.start()
            pack_far.append(copy)
        for copy in vec_far:
            copy.wait_recv()
            copy.wait_send()
        for i in range(1, n_ex):
            vec[...] += vbuf[i]
        vec_col = []
        for i in range(1, n_dp):
            copy = remote(vec, vzbuf.at[i], vz_s.at[i], vz_r.at[i], column[i - 1])
            copy.start()
            vec_col.append(copy)
        pack_near[chips - 1].wait_recv()
        total = pack[e].astype(F32) + psib[c].astype(F32)
        for i in range(1, chips):
            pack_far[i - 1].wait_recv()
            total = total + pfar[i].astype(F32)
        psum[...] = total.astype(BF).reshape(n_dp, r, lat_cols)
        pack_col = []
        for i in range(1, n_dp):
            copy = remote(
                psum.at[lax.rem(z + i, n_dp)], pbuf.at[i], pc_s.at[i], pc_r.at[i], column[i - 1]
            )
            copy.start()
            pack_col.append(copy)
        result = vec[...]
        for i in range(1, n_dp):
            vec_col[i - 1].wait_recv()
            result = result + vzbuf[i]
        vec_out[...] = result
        result = psum[z].astype(F32)
        for i in range(1, n_dp):
            pack_col[i - 1].wait_recv()
            result = result + pbuf[i].astype(F32)
        pack_out[...] = result

        for i in range(n_dp):
            here = jnp.logical_and(z // hp == part, z == i)

            @pl.when(here)
            def _(i=i):
                pltpu.make_async_copy(
                    wsrc.at[lax.rem(z, hp), part], wout_out.at[i], w_r.at[i]
                ).wait()

            @pl.when(jnp.logical_not(here))
            def _(i=i):
                wait_recv(wout_out.at[i], w_r.at[i], sibling)

        wout_sends(False)
        for copy in list(near.values()) + list(far.values()) + heads_far:
            copy.wait_send()
        for copy in pack_near + pack_far + vec_col + pack_col:
            copy.wait_send()
        for copy in heads_col + others:
            copy.wait()
        for back in backs:
            back.end()

    dma = pltpu.SemaphoreType.DMA
    sds = jax.ShapeDtypeStruct
    vmem = pltpu.VMEM
    scratch = [
        vmem((n_ex, rows, width), BF),
        vmem((seq, 2 * DV), BF),
        vmem((2 * DV, width), F32),
        vmem((seq, 2 * DH), F32),
        vmem((seq, DV), F32),
        vmem((seq, wq.shape[1]), BF),
        vmem((seq, we.shape[1]), BF),
        vmem((seq, 2 * DR), F32),
        vmem((n_ex, rows, lat_cols), BF),
    ]
    scratch += [vmem((chips, rows, width), BF)] * 3 + [vmem((chips, rows, lat_cols), BF)] * 3
    scratch += [
        vmem((rows, width), F32),
        vmem((rows, lat_cols), F32),
        vmem((n_dev, r, head_cols), BF),
        vmem((hp, parts, r, width), BF),
        vmem((n_ex, n_dp * r, lat_cols), BF),
        vmem((chips, n_dp * r, lat_cols), BF),
        vmem((chips, n_dp * r, lat_cols), BF),
        vmem((chips, n_dp * r, lat_cols), BF),
        vmem((n_dp, r, lat_cols), BF),
        vmem((n_dp, r, lat_cols), BF),
        vmem((8, width), F32),
        vmem((n_ex, 8, width), F32),
        vmem((n_dp, 8, width), F32),
    ]
    scratch += [dma((chips,))] * 4 + [dma((6,))] + [dma((chips,))] * 8
    scratch += [dma((n_ex, n_dp))] * 2 + [dma((n_dp,))] * 2 + [dma((hp, parts)), dma((n_dp,))]
    scratch += [dma((chips,))] * 4 + [dma((n_dp,))] * 2 + [dma((3, n_dp))] * 2
    scratch += [dma((n_ex,))] * 2 + [dma((n_dp,))] * 2 + [dma((inner,))] * 2
    scratch += like([given_arrays[j] for j in big]) + [dma((len(big),))]
    for total in totals:
        scratch += ExpertsBack.scratch(total, n_dp, inner)
    outs = pl.pallas_call(
        kernel,
        out_shape=[
            sds((rows, width), F32),
            sds((8, width), F32),
            sds((r, lat_cols), F32),
            sds((n_dp, n_ex, r, head_cols), BF),
            sds((n_dp, n_ex, r, head_cols), BF),
            sds((n_dp, r, width), BF),
            sds(out.shape, BF),
        ]
        + [sds(array.shape, BF) for array in shared]
        + [ExpertsBack.out(total, n_dp, inner) for total in totals],
        in_specs=[ANY]
        + [ANY if j in big else VMEM for j in range(21)]
        + [ANY] * (4 + extra),
        out_specs=[VMEM] * 3 + [ANY] * (7 + extra),
        scratch_shapes=scratch,
        compiler_params=params(collective_id),
    )(grad, *attend, hidden, latent_low, *own, out, *shared, *totals)
    return outs[:3], outs[4], outs[5], outs[6], outs[7:10], outs[10:]


def heads_together(got, order, hp, rl, wq_cols):
    n_dp, n_ex, r, cols = got.shape
    we_cols = cols - wq_cols
    count = len(order)
    per = (DH + DV) // we_cols

    def kernel(x_ref, q_ref, e_ref):
        for pair in range(count // 2):
            pieces = []
            for h in (2 * pair, 2 * pair + 1):
                device, i = order[h] // hp, order[h] % hp
                total = x_ref[0, device].astype(F32)
                for d in range(1, n_dp):
                    total = total + x_ref[d, device].astype(F32)
                rope = total[:, hp * DH : hp * DH + 2 * DR]
                pieces.append((total[:, i * DH : (i + 1) * DH], rope, i))
                for j in range(per):
                    at = (h * per + j) * we_cols
                    e_ref[:, at : at + we_cols] = total[
                        (i * per + j) * rl : (i * per + j + 1) * rl, wq_cols:
                    ]
            (plain, rope, i), (plain_b, rope_b, i_b) = pieces
            lane = lax.broadcasted_iota(jnp.int32, plain.shape, 1)
            rope = pltpu.roll(rope, DR, 1) if i else rope
            rope_b = rope_b if i_b else pltpu.roll(rope_b, DR, 1)
            turned = pltpu.roll(plain_b, DR, 1)
            at = pair * 2 * (DH + DR)
            q_ref[:, at : at + DH] = plain
            q_ref[:, at + DH : at + 2 * DH] = jnp.where(lane < DR, rope, turned)
            q_ref[:, at + 2 * DH : at + 3 * DH] = jnp.where(lane < DR, turned, rope_b)

    return pl.pallas_call(
        kernel,
        out_shape=[
            jax.ShapeDtypeStruct((r, count * (DH + DR)), F32),
            jax.ShapeDtypeStruct((rl, count * (DH + DV)), F32),
        ],
        in_specs=[VMEM],
        out_specs=[VMEM] * 2,
        compiler_params=pltpu.CompilerParams(vmem_limit_bytes=40 << 20),
    )(got)


def shards(
    tokens,
    cotangent,
    lengths,
    routes,
    place_order,
    attn_gain,
    w_query,
    w_latent,
    latent_gain,
    w_expand,
    w_out,
    ffn_gain,
    w_router,
    shared_gate,
    shared_up,
    shared_down,
    expert_gate,
    expert_up,
    expert_down,
):
    rows, width = tokens.shape
    n_dp = lax.axis_size("dp")
    n_ex = lax.axis_size("expert")
    chips = n_ex // 2
    z = lax.axis_index("dp")
    e = lax.axis_index("expert")
    chip = e // 2
    n_experts = w_router.shape[1]
    top_k = routes.shape[1]
    capacity = (rows * top_k * 5 + 4 * n_experts - 1) // (4 * n_experts)
    cap = (capacity + 15) // 16 * 16
    seq = rows * n_ex
    r = w_query.shape[0]
    rl = w_expand.shape[0]
    hp = H // n_ex
    parts = DV // r
    heads = [
        (d * n_ex + (j // parts) * parts) * r // DV
        for j in range(n_ex)
        for d in range(j % parts * hp, j % parts * hp + hp)
    ]
    heads_back = [heads.index(h) for h in range(H)]
    inner = n_experts // chips
    my_local = lax.rem(z, inner)
    ff_e = expert_gate.shape[2]
    ff_s = shared_gate.shape[1] // inner
    lat = KVR + DR
    head_cols = hp * (DH + DR)
    kv_cols = hp * (DH + DV)

    def to_owner_order(values):
        cut = values.reshape(values.shape[0], n_dp, n_ex, r)
        return cut.transpose(0, 2, 1, 3).reshape(values.shape)

    def from_owner_order(values):
        cut = values.reshape(values.shape[0], n_ex, n_dp, r)
        return cut.transpose(0, 2, 1, 3).reshape(values.shape)

    def pick(values, index, axis=0):
        return lax.dynamic_index_in_dim(values, index, axis, keepdims=False)

    wq_send = jnp.take(w_query.reshape(r, H, DH + DR), jnp.array(heads), axis=1)
    wq_send = wq_send.reshape(r, n_ex, hp, DH + DR)
    wq_send = jnp.concatenate(
        [
            wq_send[..., :DH].reshape(r, n_ex, hp * DH),
            wq_send[..., DH:].reshape(r, n_ex, hp * DR),
        ],
        axis=-1,
    ).transpose(1, 0, 2)
    we_send = jnp.take(w_expand.reshape(rl, H, DH + DV), jnp.array(heads), axis=1)
    we_cols = rl * kv_cols // r
    we_send = we_send.reshape(rl, n_ex, r // rl, we_cols).transpose(1, 2, 0, 3)
    we_send = we_send.reshape(n_ex, r, we_cols)
    wa_send = jnp.concatenate([wq_send, we_send], axis=-1)
    slot_own = slot_places(routes, place_order[0], capacity)
    slot_place = jnp.where(slot_own >= 0, slot_own - routes * capacity, -1)
    slot_cols = 2 * rows * top_k // r
    slot_pack = jnp.stack([routes, slot_place]).astype(BF).reshape(2, r, slot_cols // 2)
    small_cols = lat + n_experts
    pack_cols = (small_cols + slot_cols + 127) // 128 * 128
    pack = jnp.concatenate(
        [
            w_latent,
            w_router,
            slot_pack[0],
            slot_pack[1],
            jnp.zeros((r, pack_cols - small_cols - slot_cols), BF),
        ],
        axis=1,
    )
    cot_owner = to_owner_order(cotangent)
    gains = jnp.stack(
        [jnp.pad(gain, (0, 128 - gain.shape[0])) for gain in (attn_gain, ffn_gain, latent_gain)]
    )
    gains = jnp.pad(gains, ((0, 13), (0, 0)))

    positions = jnp.arange(seq)
    lane = np.arange(2 * DR) % (DR // 2)
    angles = np.arange(seq)[:, None] * (10000.0 ** (-2.0 * lane / DR))[None, :]
    cos_wide, sine_wide = (jnp.asarray(f(angles), F32) for f in (np.cos, np.sin))
    keep = (positions < lengths[0]).astype(F32)[None]
    attend_out, (wq, wexp, wo_rows, pk_all), gain_outs, rows_outs, (wg,), shared_w = (
        forward_exchange(
            [tokens, wa_send, pack, gains],
            [cos_wide, sine_wide, keep],
            to_owner_order(w_out),
            to_owner_order(tokens),
            cot_owner,
            [expert_gate.reshape(-1, n_ex, r, ff_e)],
            [
                w.reshape(r, inner, ff_s).transpose(1, 0, 2)
                for w in (shared_gate, shared_up, shared_down)
            ],
            n_dp,
            n_ex,
            inner,
            2,
        )
    )
    residual, x_col, cot_col = rows_outs
    gain_two = gain_outs[1][1]
    hidden_one, latent_raw, latent_low, qcat, kcat, value, lse, attended = attend_out
    wo_rows = wo_rows.reshape(hp * DV, width)
    cot_col = cot_col.reshape(inner * rows, width)
    hidden_two = pick(x_col, my_local)
    x_col = x_col.reshape(inner * rows, width)

    router = pk_all[..., lat : lat + n_experts].transpose(1, 0, 2, 3).reshape(width, n_experts)
    pk_flat = pk_all.reshape(width, pack_cols)

    slots_all = n_experts * capacity
    slot_col = pick(pk_all[..., small_cols : small_cols + slot_cols], e, 1)
    slot_col = lax.dynamic_slice_in_dim(slot_col, z - my_local, inner, 0).astype(jnp.int32)
    slot_col = slot_col.reshape(inner, r, 2, slot_cols // 2).transpose(2, 0, 1, 3)
    slot_col = slot_col.reshape(2, inner, rows, top_k)
    slot_ids = jnp.where(
        slot_col[1] >= 0,
        slot_col[0] * capacity + slot_col[1] + (jnp.arange(inner) * slots_all)[:, None, None],
        -1,
    ).reshape(inner * rows, top_k)
    place = jnp.arange(cap)
    far_experts = [lax.rem(chip + m, chips) * inner + my_local for m in range(chips)]
    wanted = (
        jnp.stack(far_experts)[:, None, None] * capacity
        + (jnp.arange(inner) * slots_all)[None, :, None]
        + place[None, None, :]
    )
    wanted = jnp.where(place[None, None, :] < capacity, wanted, -2).reshape(-1)
    n_slots = wanted.shape[0]
    per_far = n_slots // chips
    hot = sum((wanted[:, None] == slot_ids[None, :, j]).astype(BF) for j in range(top_k))
    hot_t = sum((slot_ids[:, j][:, None] == wanted[None, :]).astype(BF) for j in range(top_k))

    (x_in, grad_in), (wu, wd), shared_out, shared_dx, shared_grads = dispatch(
        hot,
        x_col,
        cot_col,
        [w.reshape(width, ff_s) for w in shared_w],
        [w.reshape(-1, n_ex, r, ff_e) for w in (expert_up, expert_down)],
        n_dp,
        n_ex,
        inner,
        8,
    )
    x_in = x_in.reshape(n_slots, width)
    grad_in = grad_in.reshape(n_slots, width)
    wg, wu, wd = (w.reshape(width, ff_e) for w in (wg, wu, wd))

    def probs_of(logits):
        top = jnp.max(logits, axis=-1, keepdims=True)
        exp_logits = jnp.exp(logits - top)
        return exp_logits / jnp.sum(exp_logits, axis=-1, keepdims=True)

    dx_back, dots_back, expert_rows, down_back, expert_totals = experts_run(
        x_in,
        grad_in,
        [wg, wu, wd],
        jnp.pad(router, ((0, 0), (0, 128 - n_experts))),
        n_dp,
        n_ex,
        inner,
        9,
    )
    dx_back = dx_back.reshape(n_slots, width)

    col_probs = probs_of(mm(x_col, router))
    expert_axis = jnp.arange(n_experts)[None, :]
    gates = [
        jnp.sum(jnp.where(expert_axis == expert, col_probs, 0.0), axis=1, keepdims=True)
        for expert in far_experts
    ]
    gate_hot = jnp.concatenate(
        [hot_t[:, m * per_far : (m + 1) * per_far] * gates[m].astype(BF) for m in range(chips)],
        axis=1,
    )
    dots = dots_back.reshape(n_slots, 128)[:, 0].astype(F32)[None] * hot_t.astype(F32)
    dots = jnp.sum(dots.reshape(inner * rows, chips, per_far), axis=-1)
    grad_probs_col = sum(
        jnp.where(expert_axis == far_experts[m], dots[:, m : m + 1], 0.0) for m in range(chips)
    )
    dx_col = mm(hot_t, dx_back) + shared_dx
    dx_send = jnp.concatenate(
        [dx_col, grad_probs_col, jnp.zeros((inner * rows, 128 - n_experts), F32)], axis=1
    ).astype(BF)
    dx_sum, shared_sums, rows_back, (gate_back,) = column_sum(
        dx_send.reshape(inner, rows, width + 128),
        expert_rows,
        [grad.reshape(n_ex, n_dp, r, ff_s) for grad in shared_grads],
        expert_totals[:1],
        n_dp,
        n_ex,
        inner,
        3,
    )
    router_probs = lax.dynamic_slice_in_dim(col_probs, my_local * rows, rows, 0)
    grad_probs = dx_sum[:, width : width + n_experts]
    grad_logits = (
        router_probs * (grad_probs - jnp.sum(grad_probs * router_probs, axis=-1, keepdims=True))
    ).astype(BF)
    grad_router = mm_rows(hidden_two, grad_logits)
    grad_hidden_two = dx_sum[:, :width] + mm_cols(grad_logits, router)
    _, norm_two_back = jax.vjp(rms_norm, residual, gain_two)
    grad_resid_norm, grad_gain_two = norm_two_back(grad_hidden_two)
    grad_residual = cot_owner.astype(F32) + grad_resid_norm

    out_col = mm(gate_hot, rows_back.reshape(n_slots, width)) + shared_out
    latent_own = lax.dynamic_slice_in_dim(latent_raw, e * rows, rows, 0)
    router_back = jnp.pad(
        grad_router.reshape(n_ex, n_dp * r, n_experts),
        ((0, 0), (0, 0), (DR, DR - n_experts)),
    ).astype(BF)
    (grad_tokens, vec_sum, pack_sum), heads_got, wout_got, out_got, shared_got, (up_back,) = (
        backward_exchange(
            grad_residual.astype(BF),
            [wo_rows, wq, wexp, cos_wide, sine_wide, keep, qcat, kcat, value, lse, attended],
            hidden_one,
            latent_low,
            [
                pk_flat,
                latent_own,
                tokens,
                gain_outs[0],
                gain_outs[2],
                from_owner_order(grad_residual),
                router_back,
                grad_gain_two[None],
            ],
            out_col.astype(BF).reshape(inner, rows, width),
            shared_sums,
            expert_totals[1:2],
            n_dp,
            n_ex,
            inner,
            5,
        )
    )

    def added(values):
        return jnp.sum(values.astype(F32), axis=0)

    out_tokens = from_owner_order((residual + added(out_got)).astype(BF))
    sum_wq, sum_we = heads_together(heads_got, heads_back, hp, rl, head_cols)
    sum_wout = from_owner_order(added(wout_got))
    device = z * n_ex + e
    sum_gain_one = lax.dynamic_slice_in_dim(vec_sum[0], device * r, r, 0)
    sum_gain_two = lax.dynamic_slice_in_dim(vec_sum[1], (e * n_dp + z) * r, r, 0)
    sum_gain_lat = lax.dynamic_slice_in_dim(vec_sum[2], device * rl, rl, 0)
    sum_sgate, sum_sup, sum_sdown = (
        added(got.reshape(n_dp // inner, inner, r, ff_s)).transpose(1, 0, 2).reshape(r, -1)
        for got in shared_got
    )
    sum_egate, sum_eup, sum_edown = (
        added(back).reshape(-1, n_ex * r, ff_e) for back in (gate_back, up_back, down_back)
    )
    return (
        out_tokens,
        grad_tokens,
        sum_gain_one,
        sum_wq,
        pack_sum[:, :lat],
        sum_gain_lat,
        sum_we,
        sum_wout,
        sum_gain_two,
        pack_sum[:, lat : lat + n_experts],
        sum_sgate,
        sum_sup,
        sum_sdown,
        sum_egate,
        sum_eup,
        sum_edown,
    )


def solution(mesh):
    both = ("dp", "expert")
    in_specs = (
        P(both, None),
        P(both, None),
        P("dp"),
        P(both, None),
        P(both, None),
        P(both),
        P(both, None),
        P(both, None),
        P(both),
        P(both, None),
        P(both, None),
        P(both),
        P(both, None),
        P(both, None),
        P(both, None),
        P(both, None),
        P("expert", "dp", None),
        P("expert", "dp", None),
        P("expert", "dp", None),
    )
    out_specs = (
        P(both, None),
        P(both, None),
        P(both),
        P(both, None),
        P(both, None),
        P(both),
        P(both, None),
        P(both, None),
        P(both),
        P(both, None),
        P(both, None),
        P(both, None),
        P(both, None),
        P("expert", "dp", None),
        P("expert", "dp", None),
        P("expert", "dp", None),
    )
    return jax.shard_map(shards, mesh=mesh, in_specs=in_specs, out_specs=out_specs, check_vma=False)
```

```python
import jax
import jax.numpy as jnp
import numpy as np
from jax import lax
from jax.experimental import pallas as pl
from jax.experimental.pallas import tpu as pltpu
from jax.sharding import PartitionSpec as P

H = 16
DH = 128
DR = 64
DV = 128
KVR = 512

norm_eps = 1e-06
masked_score = -1e30
MESH = pl.DeviceIdType.MESH
ANY = pl.BlockSpec(memory_space=pl.ANY)
VMEM = pl.BlockSpec(memory_space=pltpu.VMEM)
BF = jnp.bfloat16
F32 = jnp.float32


def rms_norm(values, scale_gain):
    return (
        values
        * lax.rsqrt(jnp.mean(values * values, axis=-1, keepdims=True) + norm_eps)
        * scale_gain
    )


def mm(left, right):
    return jnp.dot(left, right, preferred_element_type=F32)


def mm_rows(left, right):
    return lax.dot_general(left, right, (((0,), (0,)), ((), ())), preferred_element_type=F32)


def mm_cols(left, right):
    return lax.dot_general(left, right, (((1,), (1,)), ((), ())), preferred_element_type=F32)


def slot_places(route_rows, pair_order, capacity):
    pair_expert = route_rows.reshape(-1)
    earlier = pair_order[None, :] < pair_order[:, None]
    same_expert = pair_expert[None, :] == pair_expert[:, None]
    places = jnp.sum((earlier & same_expert).astype(jnp.int32), axis=1)
    slot_index = jnp.where(places < capacity, pair_expert * capacity + places, -1)
    return slot_index.reshape(route_rows.shape)


def turn(values, cos, sin, sign):
    half = DR // 2
    first = lax.rem(lax.broadcasted_iota(jnp.int32, values.shape, 1), DR) < half
    partner = jnp.where(
        first, -pltpu.roll(values, 2 * DR - half, 1), pltpu.roll(values, half, 1)
    )
    return values * cos + sign * (partner * sin)


def causal(i, tile, keep_ref):
    shape = (tile, (i + 1) * tile)
    query = lax.broadcasted_iota(jnp.int32, shape, 0) + i * tile
    key = lax.broadcasted_iota(jnp.int32, shape, 1)
    return (key <= query) & (keep_ref[:, : shape[1]] > 0.5)


def attend_forward(
    tok, gain, wq, wl, gain_lat, we, cos, sin, keep,
    hidden, latent, latent_low, qcat, kcat, value, lse, attended,
):
    per, rows, width = tok.shape
    seq = per * rows
    tile = 2 * rows
    scale = (DH + DR) ** (-0.5)

    def project(i, carry):
        at = pl.ds(pl.multiple_of(i * tile, tile), tile)
        x = tok[pl.ds(2 * i, 2)].reshape(tile, width).astype(F32)
        root = lax.rsqrt(jnp.mean(x * x, axis=-1, keepdims=True) + norm_eps)
        hid = (x * root * gain[...]).astype(BF)
        hidden[at, :] = hid
        c, s = cos[at, :], sin[at, :]
        query = mm(hid, wq[...])
        rope_q = turn(query[:, 2 * DH :], c, s, 1.0).astype(BF)
        lat = mm(hid, wl[...])
        latent[at, :] = lat
        plain = lat[:, :KVR]
        root = lax.rsqrt(jnp.mean(plain * plain, axis=-1, keepdims=True) + norm_eps)
        low = (plain * root * gain_lat[...]).astype(BF)
        latent_low[at, :] = low
        rope = lat[:, KVR : KVR + 2 * DR]
        lane = lax.broadcasted_iota(jnp.int32, rope.shape, 1)
        rope = jnp.where(lane < DR, rope, pltpu.roll(rope, DR, 1))
        rope = turn(rope, c, s, 1.0)
        expanded = mm(low, we[...]).astype(BF)
        for h in range(2):
            qcat[h, at, :DH] = query[:, h * DH : (h + 1) * DH].astype(BF)
            qcat[h, at, DH:] = rope_q
            mine = (lane < DR) if h == 0 else (lane >= DR)
            kcat[h, at, :DH] = expanded[:, h * (DH + DV) : h * (DH + DV) + DH]
            kcat[h, at, DH:] = jnp.where(mine, rope, 0.0).astype(BF)
            value[h, at, :] = expanded[:, h * (DH + DV) + DH : (h + 1) * (DH + DV)]
        return carry

    lax.fori_loop(0, seq // tile, project, 0)
    for h in range(2):
        for i in range(seq // tile):
            at, upto = slice(i * tile, (i + 1) * tile), slice(0, (i + 1) * tile)
            scores = mm_cols(qcat[h, at, :], kcat[h, upto, :]) * scale
            scores = jnp.where(causal(i, tile, keep), scores, masked_score)
            top = jnp.max(scores, axis=-1, keepdims=True)
            exp_scores = jnp.exp(scores - top)
            total = jnp.sum(exp_scores, axis=-1, keepdims=True)
            probs = (exp_scores / total).astype(BF)
            attended[at, h * DV : (h + 1) * DV] = mm(probs, value[h, upto, :]).astype(BF)
            lse[h, at, :] = jnp.broadcast_to(top + jnp.log(total), (tile, lse.shape[2]))


def attend_backward(
    grad, wo, wq, we, cos, sin, keep, qcat, kcat, value, lse, attended,
    gat, grad_wout, dk, dv, grad_query, grad_expanded, grad_rope,
):
    per, rows, width = grad.shape
    seq = per * rows
    tile = 2 * rows
    scale = (DH + DR) ** (-0.5)
    count = seq // tile
    grad_wout[...] = jnp.zeros_like(grad_wout)

    def project(i, carry):
        at = pl.ds(pl.multiple_of(i * tile, tile), tile)
        block = grad[pl.ds(2 * i, 2)].reshape(tile, width)
        gat[at, :] = mm_cols(block, wo[...]).astype(BF)
        grad_wout[...] += mm_rows(attended[at, :], block)
        return carry

    lax.fori_loop(0, count, project, 0)
    for h in range(2):
        dk[...] = jnp.zeros_like(dk)
        dv[...] = jnp.zeros_like(dv)
        for i in range(count):
            at, upto = slice(i * tile, (i + 1) * tile), slice(0, (i + 1) * tile)
            g = gat[at, h * DV : (h + 1) * DV]
            scores = mm_cols(qcat[h, at, :], kcat[h, upto, :]) * scale
            scores = jnp.where(causal(i, tile, keep), scores, masked_score)
            probs = jnp.exp(scores - lse[h, at, 0:1])
            grad_probs = mm_cols(g, value[h, upto, :])
            inner = jnp.sum(grad_probs * probs, axis=-1, keepdims=True)
            raw = (probs * (grad_probs - inner) * scale).astype(BF)
            grad_q = mm(raw, kcat[h, upto, :])
            grad_query[at, h * DH : (h + 1) * DH] = grad_q[:, :DH].astype(BF)
            rope = grad_q[:, DH:]
            lane = lax.broadcasted_iota(jnp.int32, rope.shape, 1)
            mine = (lane < DR) if h == 0 else (lane >= DR)
            rope = turn(rope, cos[at, :], sin[at, :], -1.0).astype(BF)
            if h == 0:
                grad_query[at, 2 * DH :] = rope
            else:
                grad_query[at, 2 * DH :] = jnp.where(mine, rope, grad_query[at, 2 * DH :])
            dk[upto, :] += mm_rows(raw, qcat[h, at, :])
            dv[upto, :] += mm_rows(probs.astype(BF), g)
        grad_expanded[:, h * (DH + DV) : h * (DH + DV) + DH] = dk[:, :DH].astype(BF)
        grad_expanded[:, h * (DH + DV) + DH : (h + 1) * (DH + DV)] = dv[...].astype(BF)
        rope = dk[:, DH:]
        if h == 0:
            grad_rope[...] = rope
        else:
            grad_rope[...] += pltpu.roll(rope, DR, 1)


def params(collective_id):
    return pltpu.CompilerParams(
        collective_id=collective_id, has_side_effects=True, vmem_limit_bytes=60 << 20
    )


def remote(src, dst, send_sem, recv_sem, device):
    return pltpu.make_async_remote_copy(
        src_ref=src,
        dst_ref=dst,
        send_sem=send_sem,
        recv_sem=recv_sem,
        device_id=device,
        device_id_type=MESH,
    )


def greet(devices):
    barrier = pltpu.get_barrier_semaphore()
    for device in devices:
        pl.semaphore_signal(barrier, inc=1, device_id=device, device_id_type=MESH)
    pl.semaphore_wait(barrier, len(devices))


def places(n_dp, n_ex):
    z = lax.axis_index("dp")
    e = lax.axis_index("expert")
    chips = n_ex // 2
    c, k = e // 2, lax.rem(e, 2)
    sibling = (z, e + 1 - 2 * k)
    same_core = [(z, lax.rem(c + i, chips) * 2 + k) for i in range(1, chips)]
    column = [(lax.rem(z + i, n_dp), e) for i in range(1, n_dp)]
    return z, e, c, k, sibling, same_core, column


def wait_recv(region, sem, device):
    remote(region, region, sem, sem, device).wait_recv()


def column_sum(array, rows_out, shared, totals, n_dp, n_ex, inner, collective_id):
    chips = n_ex // 2
    shape = array.shape[1:]
    extra = len(totals)
    _, _, r, ff_s = shared[0].shape

    def kernel(x_hbm, *refs):
        s_in, r_ref, t_refs, refs = refs[:3], refs[3], refs[4 : 4 + extra], refs[4 + extra :]
        o_ref, s_out, r_out, back_refs = refs[0], refs[1:4], refs[4], refs[5 : 5 + extra]
        refs = refs[5 + extra :]
        x_ref, s_v, from_sib, out_buf, from_far = refs[0], refs[1:4], *refs[4:7]
        loads, near_s, near_r, far_s, far_r, r_s, r_r, local = refs[7:15]
        relay_refs, rest = refs[15:18], refs[18:]
        moves = stage([x_hbm, *s_in], [x_ref, *s_v], loads)
        z, e, c, k, sibling, same_core, column = places(n_dp, n_ex)
        greet(same_core + [sibling] + column + [(d[0], sibling[1]) for d in column])
        backs = [
            ExpertsBack(t_refs[m], back_refs[m], rest[7 * m : 7 * m + 7], n_dp, n_ex, inner)
            for m in range(extra)
        ]
        relay = RelaySum(x_ref, relay_refs, n_dp, n_ex, inner)
        near, far, rows_back = {}, {}, []
        for i in list(range(1, chips)) + [0]:
            chip = lax.rem(c + i, chips)
            for m in range(3):
                near[i, m] = remote(
                    s_in[m].at[chip * 2 + 1 - k], from_sib.at[m, i],
                    near_s.at[m, i], near_r.at[m, i], sibling,
                )
                near[i, m].start()
        for back in backs:
            back.begin()
        moves[0].wait()
        relay.begin()
        relay.run()
        for back in backs:
            back.pass_on()
        for i in range(1, chips):
            copy = remote(
                r_ref.at[i], r_out.at[i], r_s.at[i], r_r.at[i], same_core[chips - i - 1]
            )
            copy.start()
            rows_back.append(copy)
        copy = pltpu.make_async_copy(r_ref.at[0], r_out.at[0], local)
        copy.start()
        rows_back.append(copy)

        def pair(i, m):
            chip = lax.rem(c + i, chips)
            near[i, m].wait_recv()

            def row(d, carry):
                out_buf[m, i, d] = (
                    s_v[m][chip * 2 + k, d].astype(F32) + from_sib[m, i, d].astype(F32)
                ).astype(BF)
                return carry

            lax.fori_loop(0, n_dp, row, 0)

        for move in moves[1:]:
            move.wait()
        for i in range(1, chips):
            for m in range(3):
                pair(i, m)
                far[i, m] = remote(
                    out_buf.at[m, i], from_far.at[m, i], far_s.at[m, i], far_r.at[m, i],
                    same_core[i - 1],
                )
                far[i, m].start()
        for m in range(3):
            pair(0, m)
        relay.finish(o_ref)
        for m in range(3):
            for i in range(1, chips):
                far[i, m].wait_recv()

            def row(d, carry, m=m):
                total = out_buf[m, 0, d].astype(F32)
                for i in range(1, chips):
                    total = total + from_far[m, i, d].astype(F32)
                s_out[m][d] = total.astype(BF)
                return carry

            lax.fori_loop(0, n_dp, row, 0)
        for copy in list(near.values()) + list(far.values()):
            copy.wait_send()
        for copy in rows_back:
            copy.wait()
        relay.end()
        for back in backs:
            back.end()

    dma = pltpu.SemaphoreType.DMA
    scratch = like([array, *shared])
    scratch += [pltpu.VMEM((3, chips, n_dp, r, ff_s), BF)] * 3
    scratch += [dma((4,))] + [dma((3, chips))] * 4 + [dma((chips,))] * 2 + [dma]
    scratch += RelaySum.scratch(shape, inner)
    for total in totals:
        scratch += ExpertsBack.scratch(total, n_dp, inner)
    outs = pl.pallas_call(
        kernel,
        out_shape=[jax.ShapeDtypeStruct(shape, F32)]
        + [jax.ShapeDtypeStruct((n_dp, r, ff_s), BF)] * 3
        + [jax.ShapeDtypeStruct(rows_out.shape, BF)]
        + [ExpertsBack.out(total, n_dp, inner) for total in totals],
        in_specs=[ANY] * (5 + extra),
        out_specs=[VMEM] * 4 + [ANY] * (1 + extra),
        scratch_shapes=scratch,
        compiler_params=params(collective_id),
    )(array, *shared, rows_out, *totals)
    return outs[0], outs[1:4], outs[4], outs[5:]


class Relay:
    @staticmethod
    def scratch(inner):
        dma = pltpu.SemaphoreType.DMA
        return [dma((inner,)), dma((inner,)), dma((inner,)), dma]

    def __init__(self, block, out, scratch, n_dp, n_ex, inner):
        self.block, self.out, self.inner = block, out, inner
        self.up_s, self.down_s, self.recv, self.local = scratch
        self.z, self.e, *_ = places(n_dp, n_ex)
        self.mine = lax.rem(self.z, inner)

    def copy(self, source, src, step):
        sem = self.up_s if step > 0 else self.down_s
        return remote(
            src, self.out.at[source], sem.at[source], self.recv.at[source], (self.z + step, self.e)
        )

    def keep(self):
        return pltpu.make_async_copy(self.block, self.out.at[self.mine], self.local)

    def begin(self):
        pl.when(self.mine < self.inner - 1)(lambda: self.copy(self.mine, self.block, 1).start())
        pl.when(self.mine > 0)(lambda: self.copy(self.mine, self.block, -1).start())
        self.keep().start()

    def pass_on(self):
        for t in range(1, self.inner):
            for step in (1, -1):
                source = self.mine - step * t
                exists = source >= 0 if step > 0 else source < self.inner
                more = self.mine < self.inner - 1 if step > 0 else self.mine > 0

                @pl.when(exists)
                def _(source=source, step=step):
                    self.copy(source, self.out.at[source], step).wait_recv()

                @pl.when(jnp.logical_and(exists, more))
                def _(source=source, step=step):
                    self.copy(source, self.out.at[source], step).start()

    def end(self):
        self.keep().wait()
        pl.when(self.mine < self.inner - 1)(
            lambda: self.copy(self.mine, self.block, 1).wait_send()
        )
        pl.when(self.mine > 0)(lambda: self.copy(self.mine, self.block, -1).wait_send())
        for t in range(1, self.inner):
            for step in (1, -1):
                source = self.mine - step * t
                exists = source >= 0 if step > 0 else source < self.inner
                more = self.mine < self.inner - 1 if step > 0 else self.mine > 0

                @pl.when(jnp.logical_and(exists, more))
                def _(source=source, step=step):
                    self.copy(source, self.out.at[source], step).wait_send()


class RelaySum:
    @staticmethod
    def scratch(shape, inner):
        dma = pltpu.SemaphoreType.DMA
        return [pltpu.VMEM((inner + 1,) + shape, BF), dma((inner,)), dma((inner + 1,))]

    def __init__(self, blocks, scratch, n_dp, n_ex, inner):
        self.blocks, self.inner = blocks, inner
        self.buf, self.send, self.recv = scratch
        self.z, self.e, *_ = places(n_dp, n_ex)
        self.mine = lax.rem(self.z, inner)

    def copy(self, t, src, slot, step):
        return remote(
            src, self.buf.at[slot], self.send.at[t], self.recv.at[slot], (self.z + step, self.e)
        )

    def routes(self, t, step):
        inner, mine = self.inner, self.mine
        if step > 0:
            return [(mine < t, mine == 0, t)]
        last = mine == inner - 1
        return [
            (jnp.logical_and(mine > t, mine - 1 != t), last, t),
            (mine - 1 == t, last, inner),
        ]

    def hop(self, t, step, start, edge):
        for active, first, slot in self.routes(t, step):
            if edge:
                pl.when(jnp.logical_and(active, first))(
                    lambda slot=slot: self.copy(t, self.blocks.at[t], slot, step).start()
                )
                continue

            @pl.when(jnp.logical_and(active, first))
            def _(slot=slot):
                if not start:
                    self.copy(t, self.blocks.at[t], slot, step).wait_send()

            @pl.when(jnp.logical_and(active, jnp.logical_not(first)))
            def _(slot=slot):
                copy = self.copy(t, self.buf.at[t], slot, step)
                if start:
                    self.copy(t, self.buf.at[t], t, step).wait_recv()
                    total = self.buf[t].astype(F32) + self.blocks[t].astype(F32)
                    self.buf[t] = total.astype(BF)
                    copy.start()
                else:
                    copy.wait_send()

    def begin(self):
        for t in range(self.inner - 1, 0, -1):
            self.hop(t, 1, True, True)
        for t in range(self.inner - 1):
            self.hop(t, -1, True, True)

    def run(self):
        inner = self.inner

        def up():
            for t in range(inner - 1, 0, -1):
                self.hop(t, 1, True, False)

        def down():
            for t in range(inner - 1):
                self.hop(t, -1, True, False)

        @pl.when(self.mine < inner // 2)
        def _():
            up()
            down()

        @pl.when(self.mine >= inner // 2)
        def _():
            down()
            up()

    def finish(self, out):
        out[...] = self.blocks[self.mine].astype(F32)

        @pl.when(self.mine > 0)
        def _():
            self.copy(0, self.buf.at[self.mine], self.mine, 1).wait_recv()
            out[...] += self.buf[self.mine].astype(F32)

        @pl.when(self.mine < self.inner - 1)
        def _():
            self.copy(0, self.buf.at[self.inner], self.inner, 1).wait_recv()
            out[...] += self.buf[self.inner].astype(F32)

    def end(self):
        for t in range(self.inner):
            if t:
                self.hop(t, 1, False, False)
            if t < self.inner - 1:
                self.hop(t, -1, False, False)


def stage(sources, targets, sems):
    copies = [
        pltpu.make_async_copy(source, target, sems.at[j])
        for j, (source, target) in enumerate(zip(sources, targets))
    ]
    for copy in copies:
        copy.start()
    return copies


def like(arrays):
    return [pltpu.VMEM(array.shape, array.dtype) for array in arrays]


def column_group(z, e, inner):
    start = z // inner * inner
    return [(start + lax.rem(z - start + i, inner), e) for i in range(inner)]


class ExpertsIn:
    @staticmethod
    def scratch(n_dp):
        dma = pltpu.SemaphoreType.DMA
        return [dma((n_dp, 2)), dma((n_dp,)), dma((n_dp,)), dma((n_dp,))]

    @staticmethod
    def out(weight, n_dp, n_ex):
        return jax.ShapeDtypeStruct((n_ex, n_dp) + weight.shape[2:], BF)

    def __init__(self, weight, out, scratch, n_dp, n_ex, inner):
        self.weight, self.out, self.n_dp, self.inner = weight, out, n_dp, inner
        self.send, self.recv, self.sib_send, self.sib_recv = scratch
        self.z, self.e, self.c, self.k, self.sibling, _, _ = places(n_dp, n_ex)
        self.hh = n_ex // 2
        self.local = weight.shape[0]

    def sends(self, start):
        for i in list(range(1, self.n_dp)) + [0]:
            to = lax.rem(self.z + i, self.n_dp)
            expert = lax.rem(to, self.inner)

            def go(i=i, to=to, expert=expert):
                for h in range(2):
                    src = self.weight.at[lax.rem(expert, self.local), pl.ds(h * self.hh, self.hh)]
                    dst = self.out.at[pl.ds(h * self.hh, self.hh), self.z]
                    sem = self.recv.at[self.z]

                    def far(src=src, dst=dst, h=h):
                        copy = remote(src, dst, self.send.at[i, h], sem, (to, 2 * self.c + h))
                        if start:
                            copy.start()
                        else:
                            copy.wait_send()

                    if i:
                        far()
                    else:
                        pl.when(self.k != h)(far)
                        if start:

                            @pl.when(self.k == h)
                            def _(src=src, dst=dst):
                                pltpu.make_async_copy(src, dst, sem).start()

            pl.when(expert // self.local == self.k)(go)

    def begin(self):
        self.sends(True)

    def pass_on(self):
        mine = lax.rem(self.z, self.inner)
        for i in range(self.n_dp):
            d = lax.rem(self.z + self.n_dp - i, self.n_dp)
            region = self.out.at[pl.ds(self.k * self.hh, self.hh), d]
            if i:
                wait_recv(region, self.recv.at[d], self.sibling)
            else:
                from_here = mine // self.local == self.k

                @pl.when(from_here)
                def _(region=region, d=d):
                    src = self.weight.at[
                        lax.rem(mine, self.local), pl.ds(self.k * self.hh, self.hh)
                    ]
                    pltpu.make_async_copy(src, region, self.recv.at[d]).wait()

                @pl.when(jnp.logical_not(from_here))
                def _(region=region, d=d):
                    wait_recv(region, self.recv.at[d], self.sibling)

            remote(
                region, region, self.sib_send.at[i], self.sib_recv.at[i], self.sibling
            ).start()

    def end(self):
        self.sends(False)
        for i in range(self.n_dp):
            d = lax.rem(self.z + self.n_dp - i, self.n_dp)
            mine = self.out.at[pl.ds(self.k * self.hh, self.hh), d]
            remote(
                mine, mine, self.sib_send.at[i], self.sib_recv.at[i], self.sibling
            ).wait_send()
            region = self.out.at[pl.ds((1 - self.k) * self.hh, self.hh), d]
            wait_recv(region, self.sib_recv.at[i], self.sibling)


def gain_rows(gains, target, width, order):
    per = 128 // width
    for t in range(len(order) // per):
        tile = jnp.zeros((8, 128), F32)
        for q in range(per):
            d, e = order[t * per + q]
            piece = gains[d, e, 0:8].astype(F32)
            lane = lax.broadcasted_iota(jnp.int32, piece.shape, 1)
            if q:
                piece = pltpu.roll(piece, q * width, 1)
            tile = jnp.where(lane // width == q, piece, tile)
        target[:, t * 128 : (t + 1) * 128] = tile


def forward_exchange(
    first, tables, w_out, tok, cot, experts, shared, n_dp, n_ex, inner, collective_id
):
    chips = n_ex // 2
    rows, width = tok.shape
    count = len(experts)
    r = w_out.shape[0]
    parts = DV // r
    hp = n_dp // parts
    seq = n_ex * rows
    rl = KVR // (n_dp * n_ex)
    we_cols = rl * hp * (DH + DV) // r
    wq_cols = hp * (DH + DR)

    natural = [(d, j) for d in range(n_dp) for j in range(n_ex)]
    by_owner = [(d, j) for j in range(n_ex) for d in range(n_dp)]

    def kernel(*refs):
        first_in, tables_hbm, keep, refs = refs[:4], refs[4:6], refs[6], refs[7:]
        wo_in, tok_ref, cot_in = refs[:3]
        e_in, s_in = refs[3 : 3 + count], refs[3 + count : 6 + count]
        refs = refs[6 + count :]
        kept_hbm, refs = refs[:12], refs[12:]
        gain_one, gain_ref, gain_lat, res_ref, xcol_ref, cot_out = refs[:6]
        refs = refs[6:]
        w_out, s_out = refs[:count], refs[count : 3 + count]
        refs = refs[3 + count :]
        (cos, sin), (tok_all, wa_ref, gr_ref), refs = refs[:2], refs[2:5], refs[5:]
        kept, refs = refs[:12], refs[12:]
        stage_sem, kept_sem, refs = refs[0], refs[1], refs[2:]
        first_sems, own_sem, refs = refs[:14], refs[14], refs[15:]
        att_out, (wq_ref, we_ref, wo_out, pk_ref) = kept[:8], kept[8:]
        moves = stage(tables_hbm, (cos, sin), stage_sem)
        x_ref, from_sib, out_buf, from_far, xbuf = refs[:5]
        (
            near_s, near_r, far_s, far_r,
            sh_s, sh_r, sp_s, sp_r, sf_s, sf_r, wo_s, wo_r, local,
        ) = refs[5:18]
        x_sems, co_sems, refs = refs[18:22], refs[22:26], refs[26:]
        z, e, c, k, sibling, same_core, column = places(n_dp, n_ex)
        part = lax.rem(e, parts)
        members = [
            (lax.rem(z + i, n_dp), e - part + lax.rem(part + j, parts))
            for i in range(n_dp)
            for j in range(parts)
        ]
        plane = [(z, lax.rem(e + i, n_ex)) for i in range(1, n_ex)]
        greet(plane + column + [(device[0], sibling[1]) for device in column] + members[1:])

        def wo_sends(start):
            for i in range(n_dp):
                target = (lax.rem(z + i, n_dp), e - part + z // hp)
                dst, sem = wo_out.at[lax.rem(z, hp), part], wo_r.at[lax.rem(z, hp), part]

                def far(i=i, target=target, dst=dst, sem=sem):
                    copy = remote(wo_in, dst, wo_s.at[i], sem, target)
                    if start:
                        copy.start()
                    else:
                        copy.wait_send()

                if i:
                    far()
                else:
                    pl.when(z // hp != part)(far)
                    if start:

                        @pl.when(z // hp == part)
                        def _(dst=dst, sem=sem):
                            pltpu.make_async_copy(wo_in, dst, sem).start()

        def wo_arrivals():
            for h in range(hp):
                for p in range(parts):
                    here = jnp.logical_and(part * hp + h == z, part == p)

                    @pl.when(here)
                    def _(h=h, p=p):
                        pltpu.make_async_copy(wo_in, wo_out.at[h, p], wo_r.at[h, p]).wait()

                    @pl.when(jnp.logical_not(here))
                    def _(h=h, p=p):
                        wait_recv(wo_out.at[h, p], wo_r.at[h, p], sibling)

        my_l = lax.rem(z, inner)
        matrices = [
            ExpertsIn(e_in[m], w_out[m], refs[4 * m : 4 * m + 4], n_dp, n_ex, inner)
            for m in range(count)
        ]
        tok_in, wa_in, *packs_in = first_in
        packs = (pk_ref, gr_ref)
        (
            t_send, t_recv, ts_send, ts_recv, a_send, a_recv, az_send, az_recv,
            p_send, p_recv, pf_send, pf_recv, ps_send, ps_recv,
        ) = first_sems
        wa_far, pk_col, tok_far, first_near = [], [], [], []
        for i in range(1, n_ex):
            copy = remote(
                wa_in.at[lax.rem(e + i, n_ex)], wa_ref.at[z, e],
                a_send.at[i], a_recv.at[i], plane[i - 1],
            )
            copy.start()
            wa_far.append(copy)
        for i in range(1, n_dp):
            for m in range(2):
                copy = remote(
                    packs_in[m], packs[m].at[z, e], p_send.at[m, i], p_recv.at[m, i],
                    column[i - 1],
                )
                copy.start()
                pk_col.append(copy)
        for i in range(1, chips):
            copy = remote(tok_in, tok_all.at[e], t_send.at[i], t_recv.at[i], same_core[i - 1])
            copy.start()
            tok_far.append(copy)
        copy = remote(tok_in, tok_all.at[e], ts_send.at[0], ts_recv.at[0], sibling)
        copy.start()
        first_near.append(copy)
        first_own = stage(
            [wa_in.at[e], packs_in[0], packs_in[1], tok_in],
            [wa_ref.at[z, e], pk_ref.at[z, e], gr_ref.at[z, e], tok_all.at[e]],
            own_sem,
        )
        for copy in first_own:
            copy.wait()
        for copy in wa_far:
            copy.wait_recv()
        wa_col = []
        for i in range(1, n_dp):
            copy = remote(
                wa_ref.at[z], wa_ref.at[z], az_send.at[i], az_recv.at[i], column[i - 1]
            )
            copy.start()
            wa_col.append(copy)
        wo_sends(True)
        shared_copies = []
        for i in range(1, n_dp):
            for m in range(3):
                copy = remote(
                    s_in[m].at[lax.rem(lax.rem(z + i, n_dp), inner)], s_out[m].at[e, z],
                    sh_s.at[m, i], sh_r.at[m, i], column[i - 1],
                )
                copy.start()
                shared_copies.append(copy)
        own = [
            pltpu.make_async_copy(s_in[m].at[my_l], s_out[m].at[e, z], local.at[m])
            for m in range(3)
        ]
        for copy in own:
            copy.start()
        matrices[0].begin()
        for copy in pk_col:
            copy.wait_recv()
        pk_far = []
        for m in range(2):
            block = packs[m].at[:, e]
            for i in range(1, chips):
                copy = remote(block, block, pf_send.at[m, i], pf_recv.at[m, i], same_core[i - 1])
                copy.start()
                pk_far.append((i, m, copy))
            copy = remote(block, block, ps_send.at[m, 0], ps_recv.at[m, 0], sibling)
            copy.start()
            first_near.append(copy)
        for i in range(1, chips):
            source = lax.rem(c + chips - i, chips) * 2 + k
            tok_far[i - 1].wait_recv()
            copy = remote(
                tok_all.at[source], tok_all.at[source], ts_send.at[i], ts_recv.at[i], sibling
            )
            copy.start()
            first_near.append(copy)
        for i, m, copy in pk_far:
            copy.wait_recv()
            block = packs[m].at[:, lax.rem(c + chips - i, chips) * 2 + k]
            copy = remote(block, block, ps_send.at[m, i], ps_recv.at[m, i], sibling)
            copy.start()
            first_near.append(copy)
        for copy in first_near + wa_col:
            copy.wait()
        for copy in wa_far + pk_col + tok_far + [copy for _, _, copy in pk_far]:
            copy.wait_send()
        for move in moves:
            move.wait()
        gain_rows(gr_ref, gain_one, r, natural)
        gain_rows(gr_ref, gain_ref, r, by_owner)
        gain_rows(gr_ref, gain_lat, rl, natural)
        wl_ref = pk_ref.reshape(width, pk_ref.shape[3])
        wq_ref[...] = wa_ref[:, :, :, :wq_cols].reshape(width, wq_cols)
        for j in range(r // rl):
            block = wa_ref[:, :, j * rl : (j + 1) * rl, wq_cols:].reshape(KVR, we_cols)
            we_ref[:, j * we_cols : (j + 1) * we_cols] = block
        attend_forward(
            tok_all, gain_one.at[0:1], wq_ref, wl_ref, gain_lat.at[2:3], we_ref, cos, sin, keep,
            *att_out,
        )
        wo_arrivals()
        kept_moves = stage(kept, kept_hbm, kept_sem)
        wo = wo_out[...].reshape(hp * DV, width)

        def project(i, carry):
            at = pl.ds(pl.multiple_of(i * 2 * rows, 2 * rows), 2 * rows)
            block = mm(att_out[7][at, :], wo).astype(BF)
            x_ref[pl.ds(2 * i, 2)] = block.reshape(2, rows, width)
            return carry

        lax.fori_loop(0, chips, project, 0)
        near = []
        for i in list(range(1, chips)) + [0]:
            chip = lax.rem(c + i, chips)
            copy = remote(
                x_ref.at[chip * 2 + 1 - k], from_sib.at[chip], near_s.at[i], near_r.at[i], sibling
            )
            copy.start()
            near.append(copy)
        far = []
        for i in range(1, chips):
            chip = lax.rem(c + i, chips)
            near[i - 1].wait_recv()
            out_buf[i] = (
                x_ref[chip * 2 + k].astype(F32) + from_sib[chip].astype(F32)
            ).astype(BF)
            copy = remote(out_buf.at[i], from_far.at[i], far_s.at[i], far_r.at[i], same_core[i - 1])
            copy.start()
            far.append(copy)
        near[chips - 1].wait_recv()
        res_ref[...] = x_ref[e].astype(F32) + from_sib[c].astype(F32) + tok_ref[...].astype(F32)
        for i in range(1, chips):
            far[i - 1].wait_recv()
            res_ref[...] += from_far[i].astype(F32)
        residual = res_ref[...]
        scale = lax.rsqrt(jnp.mean(residual * residual, axis=-1, keepdims=True) + norm_eps)
        xbuf[...] = (residual * scale * gain_ref[1:2, :]).astype(BF)
        relays = [
            Relay(xbuf, xcol_ref, x_sems, n_dp, n_ex, inner),
            Relay(cot_in, cot_out, co_sems, n_dp, n_ex, inner),
        ]
        relays[0].begin()
        relays[0].pass_on()
        relays[1].begin()
        for matrix in matrices[1:]:
            matrix.begin()
        for copy in own:
            copy.wait()
        for copy in shared_copies:
            copy.wait_recv()
        plane, to_sib = [], []
        for m in range(3):
            block = s_out[m].at[e]
            for i in range(1, chips):
                copy = remote(block, block, sp_s.at[m, i], sp_r.at[m, i], same_core[i - 1])
                copy.start()
                plane.append(copy)
            copy = remote(block, block, sf_s.at[m, 0], sf_r.at[m, 0], sibling)
            copy.start()
            to_sib.append(copy)
        for m in range(3):
            for i in range(1, chips):
                plane[m * (chips - 1) + i - 1].wait_recv()
                block = s_out[m].at[lax.rem(c + chips - i, chips) * 2 + k]
                copy = remote(block, block, sf_s.at[m, i], sf_r.at[m, i], sibling)
                copy.start()
                to_sib.append(copy)
        relays[1].pass_on()
        for matrix in matrices:
            matrix.pass_on()
        for copy in to_sib:
            copy.wait()
        for relay in relays:
            relay.end()
        for copy in plane + shared_copies + near + far:
            copy.wait_send()
        wo_sends(False)
        for move in kept_moves:
            move.wait()
        for matrix in matrices:
            matrix.end()

    dma = pltpu.SemaphoreType.DMA
    ff_s = shared[0].shape[2]
    scratch = []
    for _ in experts:
        scratch += ExpertsIn.scratch(n_dp)
    sds = jax.ShapeDtypeStruct
    kept = [
        sds((seq, width), BF),
        sds((seq, first[2].shape[1]), F32),
        sds((seq, KVR), BF),
        sds((2, seq, 2 * DH), BF),
        sds((2, seq, 2 * DH), BF),
        sds((2, seq, DV), BF),
        sds((2, seq, 128), F32),
        sds((seq, 2 * DV), BF),
        sds((width, wq_cols), BF),
        sds((KVR, hp * (DH + DV)), BF),
        sds((hp, parts, r, width), BF),
        sds((n_dp, n_ex) + first[2].shape, BF),
    ]
    outs = pl.pallas_call(
        kernel,
        out_shape=kept
        + [
            sds((8, width), F32),
            sds((8, width), F32),
            sds((8, KVR), F32),
            sds((rows, width), F32),
            sds((inner, rows, width), BF),
            sds((inner, rows, width), BF),
        ]
        + [ExpertsIn.out(w, n_dp, n_ex) for w in experts]
        + [sds((n_ex, n_dp, r, ff_s), BF)] * 3,
        in_specs=[ANY] * 6 + [VMEM, ANY, VMEM] + [ANY] * (4 + count),
        out_specs=[ANY] * 12 + [VMEM] * 4 + [ANY] * (5 + count),
        scratch_shapes=like(tables[:2])
        + [
            pltpu.VMEM((n_ex, rows, width), BF),
            pltpu.VMEM((n_dp,) + first[1].shape, BF),
            pltpu.VMEM((n_dp, n_ex) + first[3].shape, BF),
        ]
        + like(kept)
        + [dma((2,)), dma((12,))]
        + [dma((chips,))] * 4
        + [dma((n_ex,))] * 2
        + [dma((n_dp,))] * 2
        + [dma((2, n_dp))] * 2
        + [dma((2, chips))] * 4
        + [dma((4,))]
        + [pltpu.VMEM((n_ex, rows, width), BF)]
        + [pltpu.VMEM((chips, rows, width), BF)] * 3
        + [pltpu.VMEM((rows, width), BF)]
        + [dma((chips,))] * 4
        + [dma((3, n_dp))] * 2
        + [dma((3, chips))] * 4
        + [dma((n_dp,)), dma((hp, parts)), dma((3,))]
        + Relay.scratch(inner) * 2
        + scratch,
        compiler_params=params(collective_id),
    )(*first, *tables, w_out, tok, cot, *experts, *shared)
    return outs[:8], outs[8:12], outs[12:15], outs[15:18], outs[18 : 18 + count], outs[18 + count :]


def silu_parts(a):
    sig = 1.0 / (1.0 + jnp.exp(-a))
    return a * sig, sig * (1.0 + a * (1.0 - sig))


def dispatch(hot, x, cot, shared, weights, n_dp, n_ex, inner, collective_id):
    chips = n_ex // 2
    rows, width = x.shape
    ff = shared[0].shape[1]
    tile = 256

    per_far = hot.shape[0] // chips
    count = len(weights)

    def kernel(hot_ref, x_hbm, c_hbm, g_hbm, u_hbm, d_hbm, *refs):
        w_in, refs = refs[:count], refs[count:]
        o_ref, go_ref, w_out, refs = refs[0], refs[1], refs[2 : 2 + count], refs[2 + count :]
        results, refs = refs[:5], refs[5:]
        hot_v, x_v, c_v, g_v, u_v, d_v, hid, ga, gb, b_v, send, recv, loads, keep = refs[:14]
        out_ref, dx_ref, gg_ref, gu_ref, gd_ref = refs[14:19]
        results_sem, rest = refs[19], refs[20:]
        z, e, c, k, sibling, same_core, column = places(n_dp, n_ex)
        moves = [
            pltpu.make_async_copy(src, dst, loads.at[j])
            for j, (src, dst) in enumerate(
                [
                    (hot_ref, hot_v), (x_hbm, x_v), (c_hbm, c_v),
                    (g_hbm, g_v), (u_hbm, u_v), (d_hbm, d_v),
                ]
            )
        ]
        for copy in moves:
            copy.start()
        greet(same_core + [sibling] + column + [(device[0], sibling[1]) for device in column])
        matrices = [
            ExpertsIn(w_in[m], w_out[m], rest[4 * m : 4 * m + 4], n_dp, n_ex, inner)
            for m in range(count)
        ]
        for matrix in matrices:
            matrix.begin()
        copies = []
        for j, (source, target) in enumerate(((x_v, o_ref), (c_v, go_ref))):
            if not j:
                moves[0].wait()
            moves[1 + j].wait()
            for i in list(range(1, chips)) + [0]:
                block = mm(hot_v[i * per_far : (i + 1) * per_far, :], source[...])
                b_v[j, i] = block.astype(BF)
                if i:
                    copy = remote(
                        b_v.at[j, i], target.at[i], send.at[j, i], recv.at[j, i],
                        same_core[i - 1],
                    )
                else:
                    copy = pltpu.make_async_copy(b_v.at[j, 0], target.at[0], keep.at[j])
                copy.start()
                copies.append(copy)
        for copy in moves[3:]:
            copy.wait()

        def rows_of(i, carry):
            at = pl.ds(pl.multiple_of(i * tile, tile), tile)
            first = mm(x_v[at, :], g_v[...])
            second = mm(x_v[at, :], u_v[...])
            silu, slope = silu_parts(first)
            low = (silu * second).astype(BF)
            hid[at, :] = low
            out_ref[at, :] = mm_cols(low, d_v[...])
            back = mm(c_v[at, :], d_v[...])
            low_a = (back * second * slope).astype(BF)
            low_b = (back * silu).astype(BF)
            ga[at, :] = low_a
            gb[at, :] = low_b
            dx_ref[at, :] = mm_cols(low_a, g_v[...]) + mm_cols(low_b, u_v[...])
            return carry

        lax.fori_loop(0, rows // tile, rows_of, 0)

        def columns_of(j, carry):
            at = pl.ds(pl.multiple_of(j * tile, tile), tile)
            gg_ref[at, :] = mm_rows(x_v[:, at], ga[...]).astype(BF)
            gu_ref[at, :] = mm_rows(x_v[:, at], gb[...]).astype(BF)
            gd_ref[at, :] = mm_rows(c_v[:, at], hid[...]).astype(BF)
            return carry

        lax.fori_loop(0, width // tile, columns_of, 0)
        result_moves = stage([out_ref, dx_ref, gg_ref, gu_ref, gd_ref], results, results_sem)
        for matrix in matrices:
            matrix.pass_on()
        for copy in copies + result_moves:
            copy.wait()
        for matrix in matrices:
            matrix.end()

    dma = pltpu.SemaphoreType.DMA
    sds = jax.ShapeDtypeStruct
    vmem = pltpu.VMEM
    scratch = []
    for _ in weights:
        scratch += ExpertsIn.scratch(n_dp)
    results = [sds((rows, width), F32)] * 2 + [sds((width, ff), BF)] * 3
    outs = pl.pallas_call(
        kernel,
        out_shape=[sds((chips, per_far, width), BF)] * 2
        + [ExpertsIn.out(weight, n_dp, n_ex) for weight in weights]
        + results,
        in_specs=[ANY] * (6 + count),
        out_specs=[ANY] * (7 + count),
        scratch_shapes=[vmem(hot.shape, BF)]
        + [vmem((rows, width), BF)] * 2
        + [vmem((width, ff), BF)] * 3
        + [vmem((rows, ff), BF)] * 3
        + [vmem((2, chips, per_far, width), BF)]
        + [dma((2, chips)), dma((2, chips)), dma((6,)), dma((2,))]
        + like(results)
        + [dma((5,))]
        + scratch,
        compiler_params=params(collective_id),
    )(hot, x, cot, *shared, *weights)
    return outs[:2], outs[2 : 2 + count], outs[2 + count], outs[3 + count], outs[4 + count :]


def experts_run(x_in, grad_in, weights, router, n_dp, n_ex, inner, collective_id):
    chips = n_ex // 2
    n_slots, width = x_in.shape
    ff = weights[0].shape[1]
    per_far = n_slots // chips
    r = width // (n_dp * n_ex)
    tile = per_far
    span = n_dp * r
    n_experts = inner * chips

    def kernel(*refs):
        in_hbm, refs = refs[:6], refs[6:]
        dx_out, dots_out, rows_out, back_out, g_out, refs = *refs[:4], refs[4:6], refs[6:]
        x_v, s_v, wg, wu, wd, route, a_v, b_v, h_v, dx_v, total, stage, dots_v, g_v = refs[:14]
        loads, send, recv, d_send, d_recv, local, rows_sem, out_sem = refs[14:22]
        z, e, c, k, sibling, same_core, column = places(n_dp, n_ex)
        moves = [
            pltpu.make_async_copy(src, dst, loads.at[j])
            for j, (src, dst) in enumerate(zip(in_hbm, (x_v, s_v, wg, wu, wd, route)))
        ]
        for j in (5, 0, 2, 3, 4, 1):
            moves[j].start()
        greet(same_core + [sibling] + column + [(device[0], sibling[1]) for device in column])
        back = ExpertsBack(total, back_out, refs[22:], n_dp, n_ex, inner, True)
        expert = c * inner + lax.rem(z, inner)
        for j in (5, 0, 2, 3, 4, 1):
            moves[j].wait()

        def forward(i, carry):
            at = pl.ds(pl.multiple_of(i * tile, tile), tile)
            x = x_v[at, :]
            logits = mm(x, route[...])
            lane = lax.broadcasted_iota(jnp.int32, logits.shape, 1)
            logits = jnp.where(lane < n_experts, logits, masked_score)
            chances = jnp.exp(logits - jnp.max(logits, axis=-1, keepdims=True))
            gate = jnp.sum(jnp.where(lane == expert, chances, 0.0), axis=-1, keepdims=True)
            gate = gate / jnp.sum(chances, axis=-1, keepdims=True)
            first = mm(x, wg[...])
            second = mm(x, wu[...])
            a_v[at, :] = first.astype(BF)
            b_v[at, :] = second.astype(BF)
            hid = (silu_parts(first)[0] * second).astype(BF)
            h_v[at, :] = hid
            g_v[at, :] = s_v[at, :]
            s_v[at, :] = (gate * s_v[at, :].astype(F32)).astype(BF)
            return carry

        lax.fori_loop(0, chips, forward, 0)

        for j in range(n_ex // 2):
            at = pl.ds(pl.multiple_of(((1 - k) * (n_ex // 2) + j) * span, span), span)
            block = mm_rows(s_v[:, at], h_v[...]).astype(BF)
            total[j] = block.reshape(n_dp, r, ff)
            back.near(j).start()
        for j in range(n_ex // 2):
            at = pl.ds(pl.multiple_of((k * (n_ex // 2) + j) * span, span), span)
            block = mm_rows(s_v[:, at], h_v[...]).astype(BF)
            back.own[j] = block.reshape(n_dp, r, ff)
        back.pass_on()

        def rows_of(i, carry):
            at = pl.ds(pl.multiple_of(i * tile, tile), tile)
            rows = mm_cols(h_v[at, :], wd[...]).astype(BF)
            dx_v[i] = rows
            dots = jnp.sum(
                g_v[at, :].astype(F32) * rows.astype(F32), axis=-1, keepdims=True
            )
            dots_v[i] = jnp.broadcast_to(dots, (tile, 128)).astype(BF)
            pltpu.make_async_copy(dx_v.at[i], rows_out.at[i], rows_sem.at[i]).start()
            return carry

        lax.fori_loop(0, chips, rows_of, 0)
        dot_copies = []
        for i in range(1, chips):
            copy = remote(
                dots_v.at[i], dots_out.at[i], d_send.at[i], d_recv.at[i], same_core[chips - i - 1]
            )
            copy.start()
            dot_copies.append(copy)
        copy = pltpu.make_async_copy(dots_v.at[0], dots_out.at[0], local.at[0])
        copy.start()
        dot_copies.append(copy)

        def hidden_rows(i, carry):
            at = pl.ds(pl.multiple_of(i * tile, tile), tile)
            grad = mm(s_v[at, :], wd[...])
            silu, slope = silu_parts(a_v[at, :].astype(F32))
            second = b_v[at, :].astype(F32)
            a_v[at, :] = (grad * second * slope).astype(BF)
            b_v[at, :] = (grad * silu).astype(BF)
            return carry

        lax.fori_loop(0, chips, hidden_rows, 0)
        copies = []
        for i in list(range(1, chips)) + [0]:
            at = slice(i * per_far, (i + 1) * per_far)
            block = mm_cols(a_v[at, :], wg[...]) + mm_cols(b_v[at, :], wu[...])
            pltpu.make_async_copy(dx_v.at[i], rows_out.at[i], rows_sem.at[i]).wait()
            dx_v[i] = block.astype(BF)
            if i:
                copy = remote(
                    dx_v.at[i], dx_out.at[i], send.at[i], recv.at[i], same_core[chips - i - 1]
                )
            else:
                copy = pltpu.make_async_copy(dx_v.at[0], dx_out.at[0], local.at[1])
            copy.start()
            copies.append(copy)

        def other_rows(j, carry):
            at = pl.ds(pl.multiple_of(j * span, span), span)
            for m, side in enumerate((a_v, b_v)):

                @pl.when(j > 0)
                def _(m=m):
                    pltpu.make_async_copy(stage.at[m], g_out[m].at[j - 1], out_sem.at[m]).wait()

                block = mm_rows(x_v[:, at], side[...]).astype(BF)
                stage[m] = block.reshape(n_dp, r, ff)
                pltpu.make_async_copy(stage.at[m], g_out[m].at[j], out_sem.at[m]).start()
            return carry

        lax.fori_loop(0, n_ex, other_rows, 0)
        for m in range(2):
            pltpu.make_async_copy(stage.at[m], g_out[m].at[n_ex - 1], out_sem.at[m]).wait()
        for copy in copies + dot_copies:
            copy.wait()
        back.end()

    dma = pltpu.SemaphoreType.DMA
    sds = jax.ShapeDtypeStruct
    vmem = pltpu.VMEM
    total = sds((n_ex, n_dp, r, ff), BF)
    blocks = sds((chips, per_far, width), BF)
    dots = sds((chips, per_far, 128), BF)
    outs = pl.pallas_call(
        kernel,
        out_shape=[blocks, dots, blocks, ExpertsBack.out(total, n_dp, inner), total, total],
        in_specs=[ANY] * 6,
        out_specs=[ANY] * 6,
        scratch_shapes=[vmem((n_slots, width), BF)] * 2
        + [vmem((width, ff), BF)] * 3
        + [vmem((width, 128), BF)]
        + [vmem((n_slots, ff), BF)] * 3
        + [
            vmem(blocks.shape, BF),
            vmem((n_ex // 2,) + total.shape[1:], BF),
            vmem((2, n_dp, r, ff), BF),
            vmem(dots.shape, BF),
            vmem((n_slots, width), BF),
            dma((6,)),
        ]
        + [dma((chips,))] * 4
        + [dma((2,)), dma((chips,)), dma((2,))]
        + ExpertsBack.scratch(total, n_dp, inner),
        compiler_params=params(collective_id),
    )(x_in, grad_in, *weights, router)
    return outs[0], outs[1], outs[2], outs[3], outs[4:]


class ExpertsBack:
    @staticmethod
    def scratch(total, n_dp, inner):
        n_ex, _, r, ff = total.shape
        dma = pltpu.SemaphoreType.DMA
        hh = n_ex // 2
        return [
            pltpu.VMEM((hh, n_dp, r, ff), BF),
            pltpu.VMEM((hh, n_dp, r, ff), BF),
            dma((hh,)),
            dma((hh,)),
            dma((hh,)),
            dma((hh, n_dp)),
            dma((n_dp // inner, 2, 2, hh)),
        ]

    @staticmethod
    def out(total, n_dp, inner):
        n_ex, _, r, ff = total.shape
        return jax.ShapeDtypeStruct((n_dp // inner, 2, n_ex, r, ff), BF)

    def __init__(self, total, out, scratch, n_dp, n_ex, inner, halved=False):
        self.total, self.out, self.n_dp, self.inner, self.halved = total, out, n_dp, inner, halved
        self.own, self.sib, self.near_s, self.near_r, self.load, self.send, self.recv = scratch
        self.z, self.e, self.c, self.k, self.sibling, _, _ = places(n_dp, n_ex)
        self.hh = n_ex // 2

    def near(self, j):
        return remote(
            self.total.at[j if self.halved else (1 - self.k) * self.hh + j], self.sib.at[j],
            self.near_s.at[j], self.near_r.at[j], self.sibling,
        )

    def loads(self, j):
        return pltpu.make_async_copy(
            self.total.at[self.k * self.hh + j], self.own.at[j], self.load.at[j]
        )

    def begin(self):
        for j in range(self.hh):
            self.near(j).start()
            self.loads(j).start()

    def route(self, j, i):
        d = lax.rem(self.z + i, self.n_dp)
        expert = lax.rem(self.z, self.inner)
        o = self.z // self.inner
        dst = self.out.at[o, lax.rem(expert, 2), self.k * self.hh + j]
        sem = self.recv.at[o, lax.rem(expert, 2), self.k, j]
        return self.own.at[j, d], dst, sem, (d, 2 * self.c + expert // 2)

    def stay(self, j):
        src, dst, sem, _ = self.route(j, 0)
        return pltpu.make_async_copy(src, dst, sem)

    def go(self, j, i):
        src, dst, sem, device = self.route(j, i)
        return remote(src, dst, self.send.at[j, i], sem, device)

    def here(self):
        return lax.rem(self.z, self.inner) // 2 == self.k

    def pass_on(self):
        for j in range(self.hh):
            self.near(j).wait_recv()
            if not self.halved:
                self.loads(j).wait()
            for d in range(self.n_dp):
                self.own[j, d] = (
                    self.own[j, d].astype(F32) + self.sib[j, d].astype(F32)
                ).astype(BF)
            for i in range(1, self.n_dp):
                self.go(j, i).start()
            pl.when(self.here())(lambda j=j: self.stay(j).start())
            pl.when(jnp.logical_not(self.here()))(lambda j=j: self.go(j, 0).start())

    def end(self):
        for j in range(self.hh):
            self.near(j).wait_send()
            for i in range(1, self.n_dp):
                self.go(j, i).wait_send()
            pl.when(jnp.logical_not(self.here()))(lambda j=j: self.go(j, 0).wait_send())
        for o in range(self.n_dp // self.inner):
            for i in range(2):
                for h in range(2):
                    source = o * self.inner + 2 * self.k + i
                    here = jnp.logical_and(source == self.z, self.k == h)
                    for j in range(self.hh):
                        region = self.out.at[o, i, h * self.hh + j]
                        sem = self.recv.at[o, i, h, j]

                        @pl.when(here)
                        def _(region=region, sem=sem, j=j):
                            pltpu.make_async_copy(self.own.at[j, self.z], region, sem).wait()

                        @pl.when(jnp.logical_not(here))
                        def _(region=region, sem=sem):
                            wait_recv(region, sem, self.sibling)


def rms_back(x, gain, grad):
    root = lax.rsqrt(jnp.mean(x * x, axis=-1, keepdims=True) + norm_eps)
    scaled = grad * gain
    along = jnp.mean(x * scaled, axis=-1, keepdims=True)
    return root * scaled - x * (root * root * root) * along, grad * x * root


def backward_exchange(
    grad, attend, hidden, latent_low, own, out, shared, totals, n_dp, n_ex, inner, collective_id
):
    chips = n_ex // 2
    rows, width = grad.shape
    seq = n_ex * rows
    extra = len(totals)
    wq, we = attend[1], attend[2]
    lat_cols = KVR + 2 * DR
    r = width // (n_dp * n_ex)
    rl = KVR // (n_dp * n_ex)
    parts = DV // r
    hp = n_dp // parts
    n_dev = n_dp * n_ex
    wq_cols = wq.shape[1]
    we_cols = rl * we.shape[1] // r
    head_cols = wq_cols + we_cols
    given_arrays = [*attend, hidden, latent_low, *own]
    big = [j for j, array in enumerate(given_arrays) if array.shape[0] > 8 or array.ndim > 2]

    def kernel(*refs):
        grad_ref, given, refs = refs[0], list(refs[1:22]), refs[22:]
        out_ref, sh_in, refs = refs[0], refs[1:4], refs[4:]
        t_refs, refs = refs[:extra], refs[extra:]
        tok_out, vec_out, pack_out, heads_mid, heads_out, wout_out, out_got = refs[:7]
        sh_out, back_refs, refs = refs[7:10], refs[10 : 10 + extra], refs[10 + extra :]
        gbuf, att_tmp, refs = refs[0], refs[1:8], refs[8:]
        part_l, bufs, sums, refs = refs[0], refs[1:7], refs[7:9], refs[9:]
        hsrc, wsrc, pack, psib, pout, pfar, psum, pbuf, vec, vbuf, vzbuf = refs[:11]
        refs = refs[11:]
        t_s, t_r, ts_s, ts_r, local = refs[:5]
        sems, refs = refs[5:13], refs[13:]
        (
            h_s, h_r, hz_s, hz_r, w_s, w_r, pn_s, pn_r, pf_s, pf_r, pc_s, pc_r, s_s, s_r,
            v_s, v_r, vz_s, vz_r, o_s, o_r,
        ) = refs[:20]
        staged, stage_sem, rest = refs[20 : 20 + len(big)], refs[20 + len(big)], refs[21 + len(big) :]
        moves = stage([given[j] for j in big], staged, stage_sem)
        for j, ref in zip(big, staged):
            given[j] = ref
        att_in, hidden_ref, low_ref = given[:11], given[11], given[12]
        wl_ref, lat_ref, tok_ref, gain_ref, glat_ref, gnat_ref, router_ref, gtwo_ref = given[13:]
        gain_ref, glat_ref = gain_ref.at[0:1], glat_ref.at[2:3]
        x_refs = (gbuf, part_l)
        group = column_group(lax.axis_index("dp"), lax.axis_index("expert"), inner)
        z, e, c, k, sibling, same_core, column = places(n_dp, n_ex)
        plane = [(z, lax.rem(e + i, n_ex)) for i in range(1, n_ex)]
        part = lax.rem(e, parts)
        members = [
            (lax.rem(z + i, n_dp), e - part + lax.rem(part + j, parts))
            for i in range(n_dp)
            for j in range(parts)
        ]
        greet(plane + column + [(d[0], sibling[1]) for d in column] + members[1:])
        backs = [
            ExpertsBack(t_refs[m], back_refs[m], rest[7 * m : 7 * m + 7], n_dp, n_ex, inner)
            for m in range(extra)
        ]
        gather, to_sib, others = [], [], []
        for i in range(1, chips):
            copy = remote(grad_ref, gbuf.at[e], t_s.at[i], t_r.at[i], same_core[i - 1])
            copy.start()
            gather.append(copy)
        copy = remote(grad_ref, gbuf.at[e], ts_s.at[0], ts_r.at[0], sibling)
        copy.start()
        to_sib.append(copy)
        keep = pltpu.make_async_copy(grad_ref, gbuf.at[e], local.at[0])
        keep.start()
        for back in backs:
            back.begin()
        for m in range(3):
            for i in range(1, n_dp):
                copy = remote(
                    sh_in[m].at[lax.rem(z + i, n_dp)], sh_out[m].at[z],
                    s_s.at[m, i], s_r.at[m, i], column[i - 1],
                )
                copy.start()
                others.append(copy)
            copy = pltpu.make_async_copy(sh_in[m].at[z], sh_out[m].at[z], local.at[1 + m])
            copy.start()
            others.append(copy)
        mine = lax.rem(z, inner)
        for i in range(1, inner):
            copy = remote(
                out_ref.at[lax.rem(mine + i, inner)], out_got.at[mine], o_s.at[i], o_r.at[i],
                group[i],
            )
            copy.start()
            others.append(copy)
        copy = pltpu.make_async_copy(out_ref.at[mine], out_got.at[mine], local.at[5])
        copy.start()
        others.append(copy)
        for i in range(1, chips):
            gather[i - 1].wait_recv()
            block = gbuf.at[lax.rem(c + chips - i, chips) * 2 + k]
            copy = remote(block, block, ts_s.at[i], ts_r.at[i], sibling)
            copy.start()
            to_sib.append(copy)
        for back in backs:
            back.pass_on()
        keep.wait()
        for copy in to_sib:
            copy.wait_recv()
        for copy in gather + to_sib:
            copy.wait_send()
        gat, grad_wout, dk, dv, grad_query, grad_expanded, grad_rope = att_tmp
        for move in moves:
            move.wait()
        attend_backward(gbuf, *att_in, *att_tmp)

        wsrc[...] = grad_wout[...].astype(BF).reshape(hp, parts, r, width)

        def wout_sends(start):
            for h in range(hp):
                for p in range(parts):
                    target = (part * hp + h, e - part + p)
                    here = jnp.logical_and(part * hp + h == z, p == part)

                    def far(h=h, p=p, target=target):
                        copy = remote(
                            wsrc.at[h, p], wout_out.at[z], w_s.at[h, p], w_r.at[z], target
                        )
                        if start:
                            copy.start()
                        else:
                            copy.wait_send()

                    pl.when(jnp.logical_not(here))(far)
                    if start:

                        @pl.when(here)
                        def _(h=h, p=p):
                            pltpu.make_async_copy(
                                wsrc.at[h, p], wout_out.at[z], w_r.at[z]
                            ).start()

        wout_sends(True)

        def spread(i, carry):
            at = pl.ds(pl.multiple_of(i * 2 * rows, 2 * rows), 2 * rows)
            block = mm_cols(grad_query[at, :], att_in[1][...]).astype(BF)
            gbuf[pl.ds(2 * i, 2)] = block.reshape(2, rows, width)
            block = mm_cols(grad_expanded[at, :], att_in[2][...]).astype(BF)
            part_l[pl.ds(2 * i, 2), :, :KVR] = block.reshape(2, rows, KVR)
            block = grad_rope[at, :].astype(BF)
            part_l[pl.ds(2 * i, 2), :, KVR:] = block.reshape(2, rows, 2 * DR)
            return carry

        lax.fori_loop(0, chips, spread, 0)
        near, far = {}, {}
        for i in list(range(1, chips)) + [0]:
            chip = lax.rem(c + i, chips)
            for j in range(2):
                near[i, j] = remote(
                    x_refs[j].at[chip * 2 + 1 - k],
                    bufs[3 * j].at[chip],
                    sems[4 * j].at[i],
                    sems[4 * j + 1].at[i],
                    sibling,
                )
                near[i, j].start()
        for i in range(1, chips):
            chip = lax.rem(c + i, chips)
            for j in range(2):
                from_sib, out_buf, from_far = bufs[3 * j : 3 * j + 3]
                near[i, j].wait_recv()
                out_buf[i] = (
                    x_refs[j][chip * 2 + k].astype(F32) + from_sib[chip].astype(F32)
                ).astype(BF)
                far[i, j] = remote(
                    out_buf.at[i],
                    from_far.at[i],
                    sems[4 * j + 2].at[i],
                    sems[4 * j + 3].at[i],
                    same_core[i - 1],
                )
                far[i, j].start()

        per_tile = 256 // r

        def wq_rows(i, carry):
            at = pl.ds(pl.multiple_of(i * 256, 256), 256)
            block = mm_rows(hidden_ref[:, at], grad_query[...]).astype(BF)
            hsrc[pl.ds(i * per_tile, per_tile), :, :wq_cols] = block.reshape(
                per_tile, r, wq_cols
            )
            return carry

        lax.fori_loop(0, width // 256, wq_rows, 0)
        grad_we = mm_rows(low_ref[...], grad_expanded[...]).astype(BF)
        for j in range(r // rl):
            block = grad_we[:, j * we_cols : (j + 1) * we_cols]
            hsrc[:, j * rl : (j + 1) * rl, wq_cols:] = block.reshape(n_dev, rl, we_cols)
        heads_far = []
        for i in range(1, n_ex):
            for d in range(n_dp):
                copy = remote(
                    hsrc.at[d * n_ex + lax.rem(e + i, n_ex)], heads_mid.at[d, e],
                    h_s.at[i, d], h_r.at[i, d], plane[i - 1],
                )
                copy.start()
                heads_far.append(copy)
        for d in range(n_dp):
            copy = pltpu.make_async_copy(
                hsrc.at[d * n_ex + e], heads_mid.at[d, e], h_r.at[0, d]
            )
            copy.start()
            copy.wait()
        for j in range(2):
            near[0, j].wait_recv()
            sums[j][...] = x_refs[j][e].astype(F32) + bufs[3 * j][c].astype(F32)
        for i in range(1, chips):
            for j in range(2):
                far[i, j].wait_recv()
                sums[j][...] += bufs[3 * j + 2][i].astype(F32)

        at = pl.ds(pl.multiple_of(e * rows, rows), rows)
        cos, sin = att_in[3][at, :], att_in[4][at, :]
        lat_grad, lat_gain = rms_back(lat_ref[:, :KVR], glat_ref[...], sums[1][:, :KVR])
        rope = turn(sums[1][:, KVR:], cos, sin, -1.0)
        lane = lax.broadcasted_iota(jnp.int32, rope.shape, 1)
        rope = jnp.where(lane < DR, rope, 0.0)
        low = jnp.concatenate([lat_grad, rope], axis=1).astype(BF)
        total = sums[0][...] + mm_cols(low, wl_ref[:, :lat_cols])
        tok_grad, tok_gain = rms_back(tok_ref[...].astype(F32), gain_ref[...], total)
        tok_out[...] = gnat_ref[...] + tok_grad
        vec[...] = jnp.zeros_like(vec)
        vec[0:1, :] = jnp.sum(tok_gain, axis=0, keepdims=True)
        vec[1:2, :] = gtwo_ref[...]
        vec[2:3, :KVR] = jnp.sum(lat_gain, axis=0, keepdims=True)
        vec_far = []
        for i in range(1, n_ex):
            copy = remote(vec, vbuf.at[i], v_s.at[i], v_r.at[i], plane[i - 1])
            copy.start()
            vec_far.append(copy)
        for d in range(n_dp):
            block = hidden_ref[at, d * n_ex * r : (d + 1) * n_ex * r]
            block = mm_rows(block, low).reshape(n_ex, r, lat_cols)
            pack[:, d * r : (d + 1) * r, :KVR] = block[:, :, :KVR].astype(BF)
            block = block[:, :, KVR:] + router_ref[:, d * r : (d + 1) * r].astype(F32)
            pack[:, d * r : (d + 1) * r, KVR:] = block.astype(BF)
        pack_near, pack_far = [], []
        for i in list(range(1, chips)) + [0]:
            chip = lax.rem(c + i, chips)
            copy = remote(pack.at[chip * 2 + 1 - k], psib.at[chip], pn_s.at[i], pn_r.at[i], sibling)
            copy.start()
            pack_near.append(copy)
        for copy in heads_far:
            copy.wait_recv()
        heads_col = []
        for i in range(1, n_dp):
            d = lax.rem(z + i, n_dp)
            copy = remote(
                heads_mid.at[d], heads_out.at[z], hz_s.at[i], hz_r.at[i], column[i - 1]
            )
            copy.start()
            heads_col.append(copy)
        copy = pltpu.make_async_copy(heads_mid.at[z], heads_out.at[z], local.at[4])
        copy.start()
        heads_col.append(copy)
        for i in range(1, chips):
            chip = lax.rem(c + i, chips)
            pack_near[i - 1].wait_recv()
            pout[i] = (pack[chip * 2 + k].astype(F32) + psib[chip].astype(F32)).astype(BF)
            copy = remote(pout.at[i], pfar.at[i], pf_s.at[i], pf_r.at[i], same_core[i - 1])
            copy.start()
            pack_far.append(copy)
        for copy in vec_far:
            copy.wait_recv()
            copy.wait_send()
        for i in range(1, n_ex):
            vec[...] += vbuf[i]
        vec_col = []
        for i in range(1, n_dp):
            copy = remote(vec, vzbuf.at[i], vz_s.at[i], vz_r.at[i], column[i - 1])
            copy.start()
            vec_col.append(copy)
        pack_near[chips - 1].wait_recv()
        total = pack[e].astype(F32) + psib[c].astype(F32)
        for i in range(1, chips):
            pack_far[i - 1].wait_recv()
            total = total + pfar[i].astype(F32)
        psum[...] = total.astype(BF).reshape(n_dp, r, lat_cols)
        pack_col = []
        for i in range(1, n_dp):
            copy = remote(
                psum.at[lax.rem(z + i, n_dp)], pbuf.at[i], pc_s.at[i], pc_r.at[i], column[i - 1]
            )
            copy.start()
            pack_col.append(copy)
        result = vec[...]
        for i in range(1, n_dp):
            vec_col[i - 1].wait_recv()
            result = result + vzbuf[i]
        vec_out[...] = result
        result = psum[z].astype(F32)
        for i in range(1, n_dp):
            pack_col[i - 1].wait_recv()
            result = result + pbuf[i].astype(F32)
        pack_out[...] = result

        for i in range(n_dp):
            here = jnp.logical_and(z // hp == part, z == i)

            @pl.when(here)
            def _(i=i):
                pltpu.make_async_copy(
                    wsrc.at[lax.rem(z, hp), part], wout_out.at[i], w_r.at[i]
                ).wait()

            @pl.when(jnp.logical_not(here))
            def _(i=i):
                wait_recv(wout_out.at[i], w_r.at[i], sibling)

        wout_sends(False)
        for copy in list(near.values()) + list(far.values()) + heads_far:
            copy.wait_send()
        for copy in pack_near + pack_far + vec_col + pack_col:
            copy.wait_send()
        for copy in heads_col + others:
            copy.wait()
        for back in backs:
            back.end()

    dma = pltpu.SemaphoreType.DMA
    sds = jax.ShapeDtypeStruct
    vmem = pltpu.VMEM
    scratch = [
        vmem((n_ex, rows, width), BF),
        vmem((seq, 2 * DV), BF),
        vmem((2 * DV, width), F32),
        vmem((seq, 2 * DH), F32),
        vmem((seq, DV), F32),
        vmem((seq, wq.shape[1]), BF),
        vmem((seq, we.shape[1]), BF),
        vmem((seq, 2 * DR), F32),
        vmem((n_ex, rows, lat_cols), BF),
    ]
    scratch += [vmem((chips, rows, width), BF)] * 3 + [vmem((chips, rows, lat_cols), BF)] * 3
    scratch += [
        vmem((rows, width), F32),
        vmem((rows, lat_cols), F32),
        vmem((n_dev, r, head_cols), BF),
        vmem((hp, parts, r, width), BF),
        vmem((n_ex, n_dp * r, lat_cols), BF),
        vmem((chips, n_dp * r, lat_cols), BF),
        vmem((chips, n_dp * r, lat_cols), BF),
        vmem((chips, n_dp * r, lat_cols), BF),
        vmem((n_dp, r, lat_cols), BF),
        vmem((n_dp, r, lat_cols), BF),
        vmem((8, width), F32),
        vmem((n_ex, 8, width), F32),
        vmem((n_dp, 8, width), F32),
    ]
    scratch += [dma((chips,))] * 4 + [dma((6,))] + [dma((chips,))] * 8
    scratch += [dma((n_ex, n_dp))] * 2 + [dma((n_dp,))] * 2 + [dma((hp, parts)), dma((n_dp,))]
    scratch += [dma((chips,))] * 4 + [dma((n_dp,))] * 2 + [dma((3, n_dp))] * 2
    scratch += [dma((n_ex,))] * 2 + [dma((n_dp,))] * 2 + [dma((inner,))] * 2
    scratch += like([given_arrays[j] for j in big]) + [dma((len(big),))]
    for total in totals:
        scratch += ExpertsBack.scratch(total, n_dp, inner)
    outs = pl.pallas_call(
        kernel,
        out_shape=[
            sds((rows, width), F32),
            sds((8, width), F32),
            sds((r, lat_cols), F32),
            sds((n_dp, n_ex, r, head_cols), BF),
            sds((n_dp, n_ex, r, head_cols), BF),
            sds((n_dp, r, width), BF),
            sds(out.shape, BF),
        ]
        + [sds(array.shape, BF) for array in shared]
        + [ExpertsBack.out(total, n_dp, inner) for total in totals],
        in_specs=[ANY]
        + [ANY if j in big else VMEM for j in range(21)]
        + [ANY] * (4 + extra),
        out_specs=[VMEM] * 3 + [ANY] * (7 + extra),
        scratch_shapes=scratch,
        compiler_params=params(collective_id),
    )(grad, *attend, hidden, latent_low, *own, out, *shared, *totals)
    return outs[:3], outs[4], outs[5], outs[6], outs[7:10], outs[10:]


def finish(heads, wout, out, residual, shared, order, hp, rl, wq_cols):
    n_dp, n_ex, r, cols = heads.shape
    we_cols = cols - wq_cols
    count = len(order)
    per = (DH + DV) // we_cols
    width = wout.shape[2]
    inner, _, ff = shared[0].shape

    def natural(values, t):
        tile = values[:, :128]
        lane = lax.broadcasted_iota(jnp.int32, tile.shape, 1)
        for p in range(128 // r):
            at = t * (128 // r) + p
            start = (at % n_ex * n_dp + at // n_ex) * r
            piece = values[:, start // 128 * 128 : start // 128 * 128 + 128]
            turn_by = (p * r - start) % 128
            piece = pltpu.roll(piece, turn_by, 1) if turn_by else piece
            tile = jnp.where(lane // r == p, piece, tile) if p else piece
        return tile

    def kernel(x_ref, w_ref, y_ref, res_ref, s_a, s_b, s_c, q_ref, e_ref, wo_ref, out_ref, *s_out):
        for pair in range(count // 2):
            pieces = []
            for h in (2 * pair, 2 * pair + 1):
                device, i = order[h] // hp, order[h] % hp
                total = x_ref[0, device].astype(F32)
                for d in range(1, n_dp):
                    total = total + x_ref[d, device].astype(F32)
                rope = total[:, hp * DH : hp * DH + 2 * DR]
                pieces.append((total[:, i * DH : (i + 1) * DH], rope, i))
                for j in range(per):
                    at = (h * per + j) * we_cols
                    e_ref[:, at : at + we_cols] = total[
                        (i * per + j) * rl : (i * per + j + 1) * rl, wq_cols:
                    ]
            (plain, rope, i), (plain_b, rope_b, i_b) = pieces
            lane = lax.broadcasted_iota(jnp.int32, plain.shape, 1)
            rope = pltpu.roll(rope, DR, 1) if i else rope
            rope_b = rope_b if i_b else pltpu.roll(rope_b, DR, 1)
            turned = pltpu.roll(plain_b, DR, 1)
            at = pair * 2 * (DH + DR)
            q_ref[:, at : at + DH] = plain
            q_ref[:, at + DH : at + 2 * DH] = jnp.where(lane < DR, rope, turned)
            q_ref[:, at + 2 * DH : at + 3 * DH] = jnp.where(lane < DR, turned, rope_b)
        total = w_ref[0].astype(F32)
        for d in range(1, n_dp):
            total = total + w_ref[d].astype(F32)
        for t in range(width // 128):
            wo_ref[:, t * 128 : (t + 1) * 128] = natural(total, t)
        total = res_ref[...]
        for d in range(inner):
            total = total + y_ref[d].astype(F32)
        for t in range(width // 128):
            out_ref[:, t * 128 : (t + 1) * 128] = natural(total, t).astype(BF)
        for source, target in zip((s_a, s_b, s_c), s_out):
            for j in range(inner):
                total = source[j].astype(F32)
                target[:, j * ff : (j + 1) * ff] = total

    sds = jax.ShapeDtypeStruct
    return pl.pallas_call(
        kernel,
        out_shape=[
            sds((r, count * (DH + DR)), F32),
            sds((rl, count * (DH + DV)), F32),
            sds((r, width), F32),
            sds(residual.shape, BF),
        ]
        + [sds((r, inner * ff), F32)] * 3,
        in_specs=[VMEM] * 7,
        out_specs=[VMEM] * 7,
        compiler_params=pltpu.CompilerParams(vmem_limit_bytes=40 << 20),
    )(heads, wout, out, residual, *shared)


def shards(
    tokens,
    cotangent,
    lengths,
    routes,
    place_order,
    attn_gain,
    w_query,
    w_latent,
    latent_gain,
    w_expand,
    w_out,
    ffn_gain,
    w_router,
    shared_gate,
    shared_up,
    shared_down,
    expert_gate,
    expert_up,
    expert_down,
):
    rows, width = tokens.shape
    n_dp = lax.axis_size("dp")
    n_ex = lax.axis_size("expert")
    chips = n_ex // 2
    z = lax.axis_index("dp")
    e = lax.axis_index("expert")
    chip = e // 2
    n_experts = w_router.shape[1]
    top_k = routes.shape[1]
    capacity = (rows * top_k * 5 + 4 * n_experts - 1) // (4 * n_experts)
    cap = (capacity + 15) // 16 * 16
    seq = rows * n_ex
    r = w_query.shape[0]
    rl = w_expand.shape[0]
    hp = H // n_ex
    parts = DV // r
    heads = [
        (d * n_ex + (j // parts) * parts) * r // DV
        for j in range(n_ex)
        for d in range(j % parts * hp, j % parts * hp + hp)
    ]
    heads_back = [heads.index(h) for h in range(H)]
    inner = n_experts // chips
    my_local = lax.rem(z, inner)
    ff_e = expert_gate.shape[2]
    ff_s = shared_gate.shape[1] // inner
    lat = KVR + DR
    head_cols = hp * (DH + DR)
    kv_cols = hp * (DH + DV)

    def to_owner_order(values):
        cut = values.reshape(values.shape[0], n_dp, n_ex, r)
        return cut.transpose(0, 2, 1, 3).reshape(values.shape)

    def from_owner_order(values):
        cut = values.reshape(values.shape[0], n_ex, n_dp, r)
        return cut.transpose(0, 2, 1, 3).reshape(values.shape)

    def pick(values, index, axis=0):
        return lax.dynamic_index_in_dim(values, index, axis, keepdims=False)

    wq_send = jnp.take(w_query.reshape(r, H, DH + DR), jnp.array(heads), axis=1)
    wq_send = wq_send.reshape(r, n_ex, hp, DH + DR)
    wq_send = jnp.concatenate(
        [
            wq_send[..., :DH].reshape(r, n_ex, hp * DH),
            wq_send[..., DH:].reshape(r, n_ex, hp * DR),
        ],
        axis=-1,
    ).transpose(1, 0, 2)
    we_send = jnp.take(w_expand.reshape(rl, H, DH + DV), jnp.array(heads), axis=1)
    we_cols = rl * kv_cols // r
    we_send = we_send.reshape(rl, n_ex, r // rl, we_cols).transpose(1, 2, 0, 3)
    we_send = we_send.reshape(n_ex, r, we_cols)
    wa_send = jnp.concatenate([wq_send, we_send], axis=-1)
    slot_own = slot_places(routes, place_order[0], capacity)
    slot_place = jnp.where(slot_own >= 0, slot_own - routes * capacity, -1)
    slot_cols = 2 * rows * top_k // r
    slot_pack = jnp.stack([routes, slot_place]).astype(BF).reshape(2, r, slot_cols // 2)
    small_cols = lat + n_experts
    pack_cols = (small_cols + slot_cols + 127) // 128 * 128
    pack = jnp.concatenate(
        [
            w_latent,
            w_router,
            slot_pack[0],
            slot_pack[1],
            jnp.zeros((r, pack_cols - small_cols - slot_cols), BF),
        ],
        axis=1,
    )
    cot_owner = to_owner_order(cotangent)
    gains = jnp.stack(
        [jnp.pad(gain, (0, 128 - gain.shape[0])) for gain in (attn_gain, ffn_gain, latent_gain)]
    )
    gains = jnp.pad(gains, ((0, 13), (0, 0)))

    positions = jnp.arange(seq)
    lane = np.arange(2 * DR) % (DR // 2)
    angles = np.arange(seq)[:, None] * (10000.0 ** (-2.0 * lane / DR))[None, :]
    cos_wide, sine_wide = (jnp.asarray(f(angles), F32) for f in (np.cos, np.sin))
    keep = (positions < lengths[0]).astype(F32)[None]
    attend_out, (wq, wexp, wo_rows, pk_all), gain_outs, rows_outs, (wg,), shared_w = (
        forward_exchange(
            [tokens, wa_send, pack, gains],
            [cos_wide, sine_wide, keep],
            to_owner_order(w_out),
            to_owner_order(tokens),
            cot_owner,
            [expert_gate.reshape(-1, n_ex, r, ff_e)],
            [
                w.reshape(r, inner, ff_s).transpose(1, 0, 2)
                for w in (shared_gate, shared_up, shared_down)
            ],
            n_dp,
            n_ex,
            inner,
            2,
        )
    )
    residual, x_col, cot_col = rows_outs
    gain_two = gain_outs[1][1]
    hidden_one, latent_raw, latent_low, qcat, kcat, value, lse, attended = attend_out
    wo_rows = wo_rows.reshape(hp * DV, width)
    cot_col = cot_col.reshape(inner * rows, width)
    hidden_two = pick(x_col, my_local)
    x_col = x_col.reshape(inner * rows, width)

    router = pk_all[..., lat : lat + n_experts].transpose(1, 0, 2, 3).reshape(width, n_experts)
    pk_flat = pk_all.reshape(width, pack_cols)

    slots_all = n_experts * capacity
    slot_col = pick(pk_all[..., small_cols : small_cols + slot_cols], e, 1)
    slot_col = lax.dynamic_slice_in_dim(slot_col, z - my_local, inner, 0).astype(jnp.int32)
    slot_col = slot_col.reshape(inner, r, 2, slot_cols // 2).transpose(2, 0, 1, 3)
    slot_col = slot_col.reshape(2, inner, rows, top_k)
    slot_ids = jnp.where(
        slot_col[1] >= 0,
        slot_col[0] * capacity + slot_col[1] + (jnp.arange(inner) * slots_all)[:, None, None],
        -1,
    ).reshape(inner * rows, top_k)
    place = jnp.arange(cap)
    far_experts = [lax.rem(chip + m, chips) * inner + my_local for m in range(chips)]
    wanted = (
        jnp.stack(far_experts)[:, None, None] * capacity
        + (jnp.arange(inner) * slots_all)[None, :, None]
        + place[None, None, :]
    )
    wanted = jnp.where(place[None, None, :] < capacity, wanted, -2).reshape(-1)
    n_slots = wanted.shape[0]
    per_far = n_slots // chips
    hot = sum((wanted[:, None] == slot_ids[None, :, j]).astype(BF) for j in range(top_k))
    hot_t = sum((slot_ids[:, j][:, None] == wanted[None, :]).astype(BF) for j in range(top_k))

    (x_in, grad_in), (wu, wd), shared_out, shared_dx, shared_grads = dispatch(
        hot,
        x_col,
        cot_col,
        [w.reshape(width, ff_s) for w in shared_w],
        [w.reshape(-1, n_ex, r, ff_e) for w in (expert_up, expert_down)],
        n_dp,
        n_ex,
        inner,
        8,
    )
    x_in = x_in.reshape(n_slots, width)
    grad_in = grad_in.reshape(n_slots, width)
    wg, wu, wd = (w.reshape(width, ff_e) for w in (wg, wu, wd))

    def probs_of(logits):
        top = jnp.max(logits, axis=-1, keepdims=True)
        exp_logits = jnp.exp(logits - top)
        return exp_logits / jnp.sum(exp_logits, axis=-1, keepdims=True)

    dx_back, dots_back, expert_rows, down_back, expert_totals = experts_run(
        x_in,
        grad_in,
        [wg, wu, wd],
        jnp.pad(router, ((0, 0), (0, 128 - n_experts))),
        n_dp,
        n_ex,
        inner,
        9,
    )
    dx_back = dx_back.reshape(n_slots, width)

    col_probs = probs_of(mm(x_col, router))
    expert_axis = jnp.arange(n_experts)[None, :]
    gates = [
        jnp.sum(jnp.where(expert_axis == expert, col_probs, 0.0), axis=1, keepdims=True)
        for expert in far_experts
    ]
    gate_hot = jnp.concatenate(
        [hot_t[:, m * per_far : (m + 1) * per_far] * gates[m].astype(BF) for m in range(chips)],
        axis=1,
    )
    dots = dots_back.reshape(n_slots, 128)[:, 0].astype(F32)[None] * hot_t.astype(F32)
    dots = jnp.sum(dots.reshape(inner * rows, chips, per_far), axis=-1)
    grad_probs_col = sum(
        jnp.where(expert_axis == far_experts[m], dots[:, m : m + 1], 0.0) for m in range(chips)
    )
    dx_col = mm(hot_t, dx_back) + shared_dx
    dx_send = jnp.concatenate(
        [dx_col, grad_probs_col, jnp.zeros((inner * rows, 128 - n_experts), F32)], axis=1
    ).astype(BF)
    dx_sum, shared_sums, rows_back, (gate_back,) = column_sum(
        dx_send.reshape(inner, rows, width + 128),
        expert_rows,
        [grad.reshape(n_ex, n_dp, r, ff_s) for grad in shared_grads],
        expert_totals[:1],
        n_dp,
        n_ex,
        inner,
        3,
    )
    router_probs = lax.dynamic_slice_in_dim(col_probs, my_local * rows, rows, 0)
    grad_probs = dx_sum[:, width : width + n_experts]
    grad_logits = (
        router_probs * (grad_probs - jnp.sum(grad_probs * router_probs, axis=-1, keepdims=True))
    ).astype(BF)
    grad_router = mm_rows(hidden_two, grad_logits)
    grad_hidden_two = dx_sum[:, :width] + mm_cols(grad_logits, router)
    _, norm_two_back = jax.vjp(rms_norm, residual, gain_two)
    grad_resid_norm, grad_gain_two = norm_two_back(grad_hidden_two)
    grad_residual = cot_owner.astype(F32) + grad_resid_norm

    out_col = mm(gate_hot, rows_back.reshape(n_slots, width)) + shared_out
    latent_own = lax.dynamic_slice_in_dim(latent_raw, e * rows, rows, 0)
    router_back = jnp.pad(
        grad_router.reshape(n_ex, n_dp * r, n_experts),
        ((0, 0), (0, 0), (DR, DR - n_experts)),
    ).astype(BF)
    (grad_tokens, vec_sum, pack_sum), heads_got, wout_got, out_got, shared_got, (up_back,) = (
        backward_exchange(
            grad_residual.astype(BF),
            [wo_rows, wq, wexp, cos_wide, sine_wide, keep, qcat, kcat, value, lse, attended],
            hidden_one,
            latent_low,
            [
                pk_flat,
                latent_own,
                tokens,
                gain_outs[0],
                gain_outs[2],
                from_owner_order(grad_residual),
                router_back,
                grad_gain_two[None],
            ],
            out_col.astype(BF).reshape(inner, rows, width),
            shared_sums,
            expert_totals[1:2],
            n_dp,
            n_ex,
            inner,
            5,
        )
    )

    def added(values):
        return jnp.sum(values.astype(F32), axis=0)

    outer = n_dp // inner
    if outer > 1:
        shared_got = [
            added(got.reshape(outer, inner, r, ff_s)).astype(BF) for got in shared_got
        ]
    sum_wq, sum_we, sum_wout, out_tokens, sum_sgate, sum_sup, sum_sdown = finish(
        heads_got, wout_got, out_got, residual, shared_got, heads_back, hp, rl, head_cols
    )
    device = z * n_ex + e
    sum_gain_one = lax.dynamic_slice_in_dim(vec_sum[0], device * r, r, 0)
    sum_gain_two = lax.dynamic_slice_in_dim(vec_sum[1], (e * n_dp + z) * r, r, 0)
    sum_gain_lat = lax.dynamic_slice_in_dim(vec_sum[2], device * rl, rl, 0)
    sum_egate, sum_eup, sum_edown = (
        added(back).reshape(-1, n_ex * r, ff_e) for back in (gate_back, up_back, down_back)
    )
    return (
        out_tokens,
        grad_tokens,
        sum_gain_one,
        sum_wq,
        pack_sum[:, :lat],
        sum_gain_lat,
        sum_we,
        sum_wout,
        sum_gain_two,
        pack_sum[:, lat : lat + n_experts],
        sum_sgate,
        sum_sup,
        sum_sdown,
        sum_egate,
        sum_eup,
        sum_edown,
    )


def solution(mesh):
    both = ("dp", "expert")
    in_specs = (
        P(both, None),
        P(both, None),
        P("dp"),
        P(both, None),
        P(both, None),
        P(both),
        P(both, None),
        P(both, None),
        P(both),
        P(both, None),
        P(both, None),
        P(both),
        P(both, None),
        P(both, None),
        P(both, None),
        P(both, None),
        P("expert", "dp", None),
        P("expert", "dp", None),
        P("expert", "dp", None),
    )
    out_specs = (
        P(both, None),
        P(both, None),
        P(both),
        P(both, None),
        P(both, None),
        P(both),
        P(both, None),
        P(both, None),
        P(both),
        P(both, None),
        P(both, None),
        P(both, None),
        P(both, None),
        P("expert", "dp", None),
        P("expert", "dp", None),
        P("expert", "dp", None),
    )
    return jax.shard_map(shards, mesh=mesh, in_specs=in_specs, out_specs=out_specs, check_vma=False)
```

```python
import jax
import jax.numpy as jnp
import numpy as np
from jax import lax
from jax.experimental import pallas as pl
from jax.experimental.pallas import tpu as pltpu
from jax.sharding import PartitionSpec as P

H = 16
DH = 128
DR = 64
DV = 128
KVR = 512

norm_eps = 1e-06
masked_score = -1e30
MESH = pl.DeviceIdType.MESH
ANY = pl.BlockSpec(memory_space=pl.ANY)
VMEM = pl.BlockSpec(memory_space=pltpu.VMEM)
BF = jnp.bfloat16
F32 = jnp.float32


def rms_norm(values, scale_gain):
    return (
        values
        * lax.rsqrt(jnp.mean(values * values, axis=-1, keepdims=True) + norm_eps)
        * scale_gain
    )


def mm(left, right):
    return jnp.dot(left, right, preferred_element_type=F32)


def mm_rows(left, right):
    return lax.dot_general(left, right, (((0,), (0,)), ((), ())), preferred_element_type=F32)


def mm_cols(left, right):
    return lax.dot_general(left, right, (((1,), (1,)), ((), ())), preferred_element_type=F32)


def slot_places(route_rows, pair_order, capacity):
    pair_expert = route_rows.reshape(-1)
    earlier = pair_order[None, :] < pair_order[:, None]
    same_expert = pair_expert[None, :] == pair_expert[:, None]
    places = jnp.sum((earlier & same_expert).astype(jnp.int32), axis=1)
    slot_index = jnp.where(places < capacity, pair_expert * capacity + places, -1)
    return slot_index.reshape(route_rows.shape)


def turn(values, cos, sin, sign):
    half = DR // 2
    first = lax.rem(lax.broadcasted_iota(jnp.int32, values.shape, 1), DR) < half
    partner = jnp.where(
        first, -pltpu.roll(values, 2 * DR - half, 1), pltpu.roll(values, half, 1)
    )
    return values * cos + sign * (partner * sin)


def causal(i, tile, keep_ref):
    shape = (tile, (i + 1) * tile)
    query = lax.broadcasted_iota(jnp.int32, shape, 0) + i * tile
    key = lax.broadcasted_iota(jnp.int32, shape, 1)
    return (key <= query) & (keep_ref[:, : shape[1]] > 0.5)


def attend_forward(
    tok, gain, wq, wl, gain_lat, we, cos, sin, keep,
    hidden, latent, latent_low, qcat, kcat, value, lse, attended,
):
    per, rows, width = tok.shape
    seq = per * rows
    tile = 2 * rows
    scale = (DH + DR) ** (-0.5)

    def project(i, carry):
        at = pl.ds(pl.multiple_of(i * tile, tile), tile)
        x = tok[pl.ds(2 * i, 2)].reshape(tile, width).astype(F32)
        root = lax.rsqrt(jnp.mean(x * x, axis=-1, keepdims=True) + norm_eps)
        hid = (x * root * gain[...]).astype(BF)
        hidden[at, :] = hid
        c, s = cos[at, :], sin[at, :]
        query = mm(hid, wq[...])
        rope_q = turn(query[:, 2 * DH :], c, s, 1.0).astype(BF)
        lat = mm(hid, wl[...])
        latent[at, :] = lat
        plain = lat[:, :KVR]
        root = lax.rsqrt(jnp.mean(plain * plain, axis=-1, keepdims=True) + norm_eps)
        low = (plain * root * gain_lat[...]).astype(BF)
        latent_low[at, :] = low
        rope = lat[:, KVR : KVR + 2 * DR]
        lane = lax.broadcasted_iota(jnp.int32, rope.shape, 1)
        rope = jnp.where(lane < DR, rope, pltpu.roll(rope, DR, 1))
        rope = turn(rope, c, s, 1.0)
        expanded = mm(low, we[...]).astype(BF)
        for h in range(2):
            qcat[h, at, :DH] = query[:, h * DH : (h + 1) * DH].astype(BF)
            qcat[h, at, DH:] = rope_q
            mine = (lane < DR) if h == 0 else (lane >= DR)
            kcat[h, at, :DH] = expanded[:, h * (DH + DV) : h * (DH + DV) + DH]
            kcat[h, at, DH:] = jnp.where(mine, rope, 0.0).astype(BF)
            value[h, at, :] = expanded[:, h * (DH + DV) + DH : (h + 1) * (DH + DV)]
        return carry

    lax.fori_loop(0, seq // tile, project, 0)
    for h in range(2):
        for i in range(seq // tile):
            at, upto = slice(i * tile, (i + 1) * tile), slice(0, (i + 1) * tile)
            scores = mm_cols(qcat[h, at, :], kcat[h, upto, :]) * scale
            scores = jnp.where(causal(i, tile, keep), scores, masked_score)
            top = jnp.max(scores, axis=-1, keepdims=True)
            exp_scores = jnp.exp(scores - top)
            total = jnp.sum(exp_scores, axis=-1, keepdims=True)
            probs = (exp_scores / total).astype(BF)
            attended[at, h * DV : (h + 1) * DV] = mm(probs, value[h, upto, :]).astype(BF)
            lse[h, at, :] = jnp.broadcast_to(top + jnp.log(total), (tile, lse.shape[2]))


def attend_backward(
    grad, wo, wq, we, cos, sin, keep, qcat, kcat, value, lse, attended,
    gat, grad_wout, dk, dv, grad_query, grad_expanded, grad_rope,
):
    per, rows, width = grad.shape
    seq = per * rows
    tile = 2 * rows
    scale = (DH + DR) ** (-0.5)
    count = seq // tile
    grad_wout[...] = jnp.zeros_like(grad_wout)

    def project(i, carry):
        at = pl.ds(pl.multiple_of(i * tile, tile), tile)
        block = grad[pl.ds(2 * i, 2)].reshape(tile, width)
        gat[at, :] = mm_cols(block, wo[...]).astype(BF)
        grad_wout[...] += mm_rows(attended[at, :], block)
        return carry

    lax.fori_loop(0, count, project, 0)
    for h in range(2):
        dk[...] = jnp.zeros_like(dk)
        dv[...] = jnp.zeros_like(dv)
        for i in range(count):
            at, upto = slice(i * tile, (i + 1) * tile), slice(0, (i + 1) * tile)
            g = gat[at, h * DV : (h + 1) * DV]
            scores = mm_cols(qcat[h, at, :], kcat[h, upto, :]) * scale
            scores = jnp.where(causal(i, tile, keep), scores, masked_score)
            probs = jnp.exp(scores - lse[h, at, 0:1])
            grad_probs = mm_cols(g, value[h, upto, :])
            inner = jnp.sum(grad_probs * probs, axis=-1, keepdims=True)
            raw = (probs * (grad_probs - inner) * scale).astype(BF)
            grad_q = mm(raw, kcat[h, upto, :])
            grad_query[at, h * DH : (h + 1) * DH] = grad_q[:, :DH].astype(BF)
            rope = grad_q[:, DH:]
            lane = lax.broadcasted_iota(jnp.int32, rope.shape, 1)
            mine = (lane < DR) if h == 0 else (lane >= DR)
            rope = turn(rope, cos[at, :], sin[at, :], -1.0).astype(BF)
            if h == 0:
                grad_query[at, 2 * DH :] = rope
            else:
                grad_query[at, 2 * DH :] = jnp.where(mine, rope, grad_query[at, 2 * DH :])
            dk[upto, :] += mm_rows(raw, qcat[h, at, :])
            dv[upto, :] += mm_rows(probs.astype(BF), g)
        grad_expanded[:, h * (DH + DV) : h * (DH + DV) + DH] = dk[:, :DH].astype(BF)
        grad_expanded[:, h * (DH + DV) + DH : (h + 1) * (DH + DV)] = dv[...].astype(BF)
        rope = dk[:, DH:]
        if h == 0:
            grad_rope[...] = rope
        else:
            grad_rope[...] += pltpu.roll(rope, DR, 1)


def params(collective_id):
    return pltpu.CompilerParams(
        collective_id=collective_id, has_side_effects=True, vmem_limit_bytes=60 << 20
    )


def remote(src, dst, send_sem, recv_sem, device):
    return pltpu.make_async_remote_copy(
        src_ref=src,
        dst_ref=dst,
        send_sem=send_sem,
        recv_sem=recv_sem,
        device_id=device,
        device_id_type=MESH,
    )


def greet(devices):
    barrier = pltpu.get_barrier_semaphore()
    for device in devices:
        pl.semaphore_signal(barrier, inc=1, device_id=device, device_id_type=MESH)
    pl.semaphore_wait(barrier, len(devices))


def places(n_dp, n_ex):
    z = lax.axis_index("dp")
    e = lax.axis_index("expert")
    chips = n_ex // 2
    c, k = e // 2, lax.rem(e, 2)
    sibling = (z, e + 1 - 2 * k)
    same_core = [(z, lax.rem(c + i, chips) * 2 + k) for i in range(1, chips)]
    column = [(lax.rem(z + i, n_dp), e) for i in range(1, n_dp)]
    return z, e, c, k, sibling, same_core, column


def wait_recv(region, sem, device):
    remote(region, region, sem, sem, device).wait_recv()


def column_sum(array, rows_out, shared, totals, n_dp, n_ex, inner, collective_id):
    chips = n_ex // 2
    shape = array.shape[1:]
    extra = len(totals)
    _, _, r, ff_s = shared[0].shape

    def kernel(x_hbm, *refs):
        s_in, r_ref, t_refs, refs = refs[:3], refs[3], refs[4 : 4 + extra], refs[4 + extra :]
        o_ref, s_out, r_out, back_refs = refs[0], refs[1:4], refs[4], refs[5 : 5 + extra]
        refs = refs[5 + extra :]
        x_ref, s_v, from_sib, out_buf, from_far = refs[0], refs[1:4], *refs[4:7]
        loads, near_s, near_r, far_s, far_r, r_s, r_r, local = refs[7:15]
        relay_refs, rest = refs[15:18], refs[18:]
        moves = stage([x_hbm, *s_in], [x_ref, *s_v], loads)
        z, e, c, k, sibling, same_core, column = places(n_dp, n_ex)
        greet(same_core + [sibling] + column + [(d[0], sibling[1]) for d in column])
        backs = [
            ExpertsBack(t_refs[m], back_refs[m], rest[7 * m : 7 * m + 7], n_dp, n_ex, inner)
            for m in range(extra)
        ]
        relay = RelaySum(x_ref, relay_refs, n_dp, n_ex, inner)
        near, far, rows_back = {}, {}, []
        for i in list(range(1, chips)) + [0]:
            chip = lax.rem(c + i, chips)
            for m in range(3):
                near[i, m] = remote(
                    s_in[m].at[chip * 2 + 1 - k], from_sib.at[m, i],
                    near_s.at[m, i], near_r.at[m, i], sibling,
                )
                near[i, m].start()
        for back in backs:
            back.begin()
        for i in range(1, chips):
            copy = remote(
                r_ref.at[i], r_out.at[i], r_s.at[i], r_r.at[i], same_core[chips - i - 1]
            )
            copy.start()
            rows_back.append(copy)
        copy = pltpu.make_async_copy(r_ref.at[0], r_out.at[0], local)
        copy.start()
        rows_back.append(copy)
        moves[0].wait()
        relay.begin()
        relay.run()
        for back in backs:
            back.pass_on()

        def pair(i, m):
            chip = lax.rem(c + i, chips)
            near[i, m].wait_recv()

            def row(d, carry):
                out_buf[m, i, d] = (
                    s_v[m][chip * 2 + k, d].astype(F32) + from_sib[m, i, d].astype(F32)
                ).astype(BF)
                return carry

            lax.fori_loop(0, n_dp, row, 0)

        for move in moves[1:]:
            move.wait()
        for i in range(1, chips):
            for m in range(3):
                pair(i, m)
                far[i, m] = remote(
                    out_buf.at[m, i], from_far.at[m, i], far_s.at[m, i], far_r.at[m, i],
                    same_core[i - 1],
                )
                far[i, m].start()
        for m in range(3):
            pair(0, m)
        relay.finish(o_ref)
        for m in range(3):
            for i in range(1, chips):
                far[i, m].wait_recv()

            def row(d, carry, m=m):
                total = out_buf[m, 0, d].astype(F32)
                for i in range(1, chips):
                    total = total + from_far[m, i, d].astype(F32)
                s_out[m][d] = total.astype(BF)
                return carry

            lax.fori_loop(0, n_dp, row, 0)
        for copy in list(near.values()) + list(far.values()):
            copy.wait_send()
        for copy in rows_back:
            copy.wait()
        relay.end()
        for back in backs:
            back.end()

    dma = pltpu.SemaphoreType.DMA
    scratch = like([array, *shared])
    scratch += [pltpu.VMEM((3, chips, n_dp, r, ff_s), BF)] * 3
    scratch += [dma((4,))] + [dma((3, chips))] * 4 + [dma((chips,))] * 2 + [dma]
    scratch += RelaySum.scratch(shape, inner)
    for total in totals:
        scratch += ExpertsBack.scratch(total, n_dp, inner)
    outs = pl.pallas_call(
        kernel,
        out_shape=[jax.ShapeDtypeStruct(shape, F32)]
        + [jax.ShapeDtypeStruct((n_dp, r, ff_s), BF)] * 3
        + [jax.ShapeDtypeStruct(rows_out.shape, BF)]
        + [ExpertsBack.out(total, n_dp, inner) for total in totals],
        in_specs=[ANY] * (5 + extra),
        out_specs=[VMEM] * 4 + [ANY] * (1 + extra),
        scratch_shapes=scratch,
        compiler_params=params(collective_id),
    )(array, *shared, rows_out, *totals)
    return outs[0], outs[1:4], outs[4], outs[5:]


class Relay:
    @staticmethod
    def scratch(inner):
        dma = pltpu.SemaphoreType.DMA
        return [dma((inner,)), dma((inner,)), dma((inner,)), dma]

    def __init__(self, block, out, scratch, n_dp, n_ex, inner):
        self.block, self.out, self.inner = block, out, inner
        self.up_s, self.down_s, self.recv, self.local = scratch
        self.z, self.e, *_ = places(n_dp, n_ex)
        self.mine = lax.rem(self.z, inner)

    def copy(self, source, src, step):
        sem = self.up_s if step > 0 else self.down_s
        return remote(
            src, self.out.at[source], sem.at[source], self.recv.at[source], (self.z + step, self.e)
        )

    def keep(self):
        return pltpu.make_async_copy(self.block, self.out.at[self.mine], self.local)

    def begin(self):
        pl.when(self.mine < self.inner - 1)(lambda: self.copy(self.mine, self.block, 1).start())
        pl.when(self.mine > 0)(lambda: self.copy(self.mine, self.block, -1).start())
        self.keep().start()

    def pass_on(self):
        for t in range(1, self.inner):
            for step in (1, -1):
                source = self.mine - step * t
                exists = source >= 0 if step > 0 else source < self.inner
                more = self.mine < self.inner - 1 if step > 0 else self.mine > 0

                @pl.when(exists)
                def _(source=source, step=step):
                    self.copy(source, self.out.at[source], step).wait_recv()

                @pl.when(jnp.logical_and(exists, more))
                def _(source=source, step=step):
                    self.copy(source, self.out.at[source], step).start()

    def end(self):
        self.keep().wait()
        pl.when(self.mine < self.inner - 1)(
            lambda: self.copy(self.mine, self.block, 1).wait_send()
        )
        pl.when(self.mine > 0)(lambda: self.copy(self.mine, self.block, -1).wait_send())
        for t in range(1, self.inner):
            for step in (1, -1):
                source = self.mine - step * t
                exists = source >= 0 if step > 0 else source < self.inner
                more = self.mine < self.inner - 1 if step > 0 else self.mine > 0

                @pl.when(jnp.logical_and(exists, more))
                def _(source=source, step=step):
                    self.copy(source, self.out.at[source], step).wait_send()


class RelaySum:
    @staticmethod
    def scratch(shape, inner):
        dma = pltpu.SemaphoreType.DMA
        return [pltpu.VMEM((inner + 1,) + shape, BF), dma((inner,)), dma((inner + 1,))]

    def __init__(self, blocks, scratch, n_dp, n_ex, inner):
        self.blocks, self.inner = blocks, inner
        self.buf, self.send, self.recv = scratch
        self.z, self.e, *_ = places(n_dp, n_ex)
        self.mine = lax.rem(self.z, inner)

    def copy(self, t, src, slot, step):
        return remote(
            src, self.buf.at[slot], self.send.at[t], self.recv.at[slot], (self.z + step, self.e)
        )

    def routes(self, t, step):
        inner, mine = self.inner, self.mine
        if step > 0:
            return [(mine < t, mine == 0, t)]
        last = mine == inner - 1
        return [
            (jnp.logical_and(mine > t, mine - 1 != t), last, t),
            (mine - 1 == t, last, inner),
        ]

    def hop(self, t, step, start, edge):
        for active, first, slot in self.routes(t, step):
            if edge:
                pl.when(jnp.logical_and(active, first))(
                    lambda slot=slot: self.copy(t, self.blocks.at[t], slot, step).start()
                )
                continue

            @pl.when(jnp.logical_and(active, first))
            def _(slot=slot):
                if not start:
                    self.copy(t, self.blocks.at[t], slot, step).wait_send()

            @pl.when(jnp.logical_and(active, jnp.logical_not(first)))
            def _(slot=slot):
                copy = self.copy(t, self.buf.at[t], slot, step)
                if start:
                    self.copy(t, self.buf.at[t], t, step).wait_recv()
                    total = self.buf[t].astype(F32) + self.blocks[t].astype(F32)
                    self.buf[t] = total.astype(BF)
                    copy.start()
                else:
                    copy.wait_send()

    def begin(self):
        for t in range(self.inner - 1, 0, -1):
            self.hop(t, 1, True, True)
        for t in range(self.inner - 1):
            self.hop(t, -1, True, True)

    def run(self):
        inner = self.inner

        def up():
            for t in range(inner - 1, 0, -1):
                self.hop(t, 1, True, False)

        def down():
            for t in range(inner - 1):
                self.hop(t, -1, True, False)

        @pl.when(self.mine < inner // 2)
        def _():
            up()
            down()

        @pl.when(self.mine >= inner // 2)
        def _():
            down()
            up()

    def finish(self, out):
        out[...] = self.blocks[self.mine].astype(F32)

        @pl.when(self.mine > 0)
        def _():
            self.copy(0, self.buf.at[self.mine], self.mine, 1).wait_recv()
            out[...] += self.buf[self.mine].astype(F32)

        @pl.when(self.mine < self.inner - 1)
        def _():
            self.copy(0, self.buf.at[self.inner], self.inner, 1).wait_recv()
            out[...] += self.buf[self.inner].astype(F32)

    def end(self):
        for t in range(self.inner):
            if t:
                self.hop(t, 1, False, False)
            if t < self.inner - 1:
                self.hop(t, -1, False, False)


def stage(sources, targets, sems):
    copies = [
        pltpu.make_async_copy(source, target, sems.at[j])
        for j, (source, target) in enumerate(zip(sources, targets))
    ]
    for copy in copies:
        copy.start()
    return copies


def like(arrays):
    return [pltpu.VMEM(array.shape, array.dtype) for array in arrays]


def column_group(z, e, inner):
    start = z // inner * inner
    return [(start + lax.rem(z - start + i, inner), e) for i in range(inner)]


class ExpertsIn:
    @staticmethod
    def scratch(n_dp):
        dma = pltpu.SemaphoreType.DMA
        return [dma((n_dp, 2)), dma((n_dp,)), dma((n_dp,)), dma((n_dp,))]

    @staticmethod
    def out(weight, n_dp, n_ex):
        return jax.ShapeDtypeStruct((n_ex, n_dp) + weight.shape[2:], BF)

    def __init__(self, weight, out, scratch, n_dp, n_ex, inner):
        self.weight, self.out, self.n_dp, self.inner = weight, out, n_dp, inner
        self.send, self.recv, self.sib_send, self.sib_recv = scratch
        self.z, self.e, self.c, self.k, self.sibling, _, _ = places(n_dp, n_ex)
        self.hh = n_ex // 2
        self.local = weight.shape[0]

    def sends(self, start):
        for i in list(range(1, self.n_dp)) + [0]:
            to = lax.rem(self.z + i, self.n_dp)
            expert = lax.rem(to, self.inner)

            def go(i=i, to=to, expert=expert):
                for h in range(2):
                    src = self.weight.at[lax.rem(expert, self.local), pl.ds(h * self.hh, self.hh)]
                    dst = self.out.at[pl.ds(h * self.hh, self.hh), self.z]
                    sem = self.recv.at[self.z]

                    def far(src=src, dst=dst, h=h):
                        copy = remote(src, dst, self.send.at[i, h], sem, (to, 2 * self.c + h))
                        if start:
                            copy.start()
                        else:
                            copy.wait_send()

                    if i:
                        far()
                    else:
                        pl.when(self.k != h)(far)
                        if start:

                            @pl.when(self.k == h)
                            def _(src=src, dst=dst):
                                pltpu.make_async_copy(src, dst, sem).start()

            pl.when(expert // self.local == self.k)(go)

    def begin(self):
        self.sends(True)

    def pass_on(self):
        mine = lax.rem(self.z, self.inner)
        for i in range(self.n_dp):
            d = lax.rem(self.z + self.n_dp - i, self.n_dp)
            region = self.out.at[pl.ds(self.k * self.hh, self.hh), d]
            if i:
                wait_recv(region, self.recv.at[d], self.sibling)
            else:
                from_here = mine // self.local == self.k

                @pl.when(from_here)
                def _(region=region, d=d):
                    src = self.weight.at[
                        lax.rem(mine, self.local), pl.ds(self.k * self.hh, self.hh)
                    ]
                    pltpu.make_async_copy(src, region, self.recv.at[d]).wait()

                @pl.when(jnp.logical_not(from_here))
                def _(region=region, d=d):
                    wait_recv(region, self.recv.at[d], self.sibling)

            remote(
                region, region, self.sib_send.at[i], self.sib_recv.at[i], self.sibling
            ).start()

    def end(self):
        self.sends(False)
        for i in range(self.n_dp):
            d = lax.rem(self.z + self.n_dp - i, self.n_dp)
            mine = self.out.at[pl.ds(self.k * self.hh, self.hh), d]
            remote(
                mine, mine, self.sib_send.at[i], self.sib_recv.at[i], self.sibling
            ).wait_send()
            region = self.out.at[pl.ds((1 - self.k) * self.hh, self.hh), d]
            wait_recv(region, self.sib_recv.at[i], self.sibling)


def gain_rows(gains, target, width, order):
    per = 128 // width
    for t in range(len(order) // per):
        tile = jnp.zeros((8, 128), F32)
        for q in range(per):
            d, e = order[t * per + q]
            piece = gains[d, e, 0:8].astype(F32)
            lane = lax.broadcasted_iota(jnp.int32, piece.shape, 1)
            if q:
                piece = pltpu.roll(piece, q * width, 1)
            tile = jnp.where(lane // width == q, piece, tile)
        target[:, t * 128 : (t + 1) * 128] = tile


def forward_exchange(
    first, tables, w_out, tok, cot, experts, shared, n_dp, n_ex, inner, collective_id
):
    chips = n_ex // 2
    rows, width = tok.shape
    count = len(experts)
    r = w_out.shape[0]
    parts = DV // r
    hp = n_dp // parts
    seq = n_ex * rows
    rl = KVR // (n_dp * n_ex)
    we_cols = rl * hp * (DH + DV) // r
    wq_cols = hp * (DH + DR)

    natural = [(d, j) for d in range(n_dp) for j in range(n_ex)]
    by_owner = [(d, j) for j in range(n_ex) for d in range(n_dp)]

    def kernel(*refs):
        first_in, tables_hbm, keep, refs = refs[:4], refs[4:6], refs[6], refs[7:]
        wo_in, tok_ref, cot_in = refs[:3]
        e_in, s_in = refs[3 : 3 + count], refs[3 + count : 6 + count]
        refs = refs[6 + count :]
        kept_hbm, refs = refs[:12], refs[12:]
        gain_one, gain_ref, gain_lat, res_ref, xcol_ref, cot_out = refs[:6]
        refs = refs[6:]
        w_out, s_out = refs[:count], refs[count : 3 + count]
        refs = refs[3 + count :]
        (cos, sin), (tok_all, wa_ref, gr_ref), refs = refs[:2], refs[2:5], refs[5:]
        kept, refs = refs[:12], refs[12:]
        stage_sem, kept_sem, refs = refs[0], refs[1], refs[2:]
        first_sems, own_sem, refs = refs[:14], refs[14], refs[15:]
        att_out, (wq_ref, we_ref, wo_out, pk_ref) = kept[:8], kept[8:]
        moves = stage(tables_hbm, (cos, sin), stage_sem)
        x_ref, from_sib, out_buf, from_far, xbuf = refs[:5]
        (
            near_s, near_r, far_s, far_r,
            sh_s, sh_r, sp_s, sp_r, sf_s, sf_r, wo_s, wo_r, local,
        ) = refs[5:18]
        x_sems, co_sems, refs = refs[18:22], refs[22:26], refs[26:]
        z, e, c, k, sibling, same_core, column = places(n_dp, n_ex)
        part = lax.rem(e, parts)
        members = [
            (lax.rem(z + i, n_dp), e - part + lax.rem(part + j, parts))
            for i in range(n_dp)
            for j in range(parts)
        ]
        plane = [(z, lax.rem(e + i, n_ex)) for i in range(1, n_ex)]
        greet(plane + column + [(device[0], sibling[1]) for device in column] + members[1:])

        def wo_sends(start):
            for i in range(n_dp):
                target = (lax.rem(z + i, n_dp), e - part + z // hp)
                dst, sem = wo_out.at[lax.rem(z, hp), part], wo_r.at[lax.rem(z, hp), part]

                def far(i=i, target=target, dst=dst, sem=sem):
                    copy = remote(wo_in, dst, wo_s.at[i], sem, target)
                    if start:
                        copy.start()
                    else:
                        copy.wait_send()

                if i:
                    far()
                else:
                    pl.when(z // hp != part)(far)
                    if start:

                        @pl.when(z // hp == part)
                        def _(dst=dst, sem=sem):
                            pltpu.make_async_copy(wo_in, dst, sem).start()

        def wo_arrivals():
            for h in range(hp):
                for p in range(parts):
                    here = jnp.logical_and(part * hp + h == z, part == p)

                    @pl.when(here)
                    def _(h=h, p=p):
                        pltpu.make_async_copy(wo_in, wo_out.at[h, p], wo_r.at[h, p]).wait()

                    @pl.when(jnp.logical_not(here))
                    def _(h=h, p=p):
                        wait_recv(wo_out.at[h, p], wo_r.at[h, p], sibling)

        my_l = lax.rem(z, inner)
        matrices = [
            ExpertsIn(e_in[m], w_out[m], refs[4 * m : 4 * m + 4], n_dp, n_ex, inner)
            for m in range(count)
        ]
        tok_in, wa_in, *packs_in = first_in
        packs = (pk_ref, gr_ref)
        (
            t_send, t_recv, ts_send, ts_recv, a_send, a_recv, az_send, az_recv,
            p_send, p_recv, pf_send, pf_recv, ps_send, ps_recv,
        ) = first_sems
        wa_far, pk_col, tok_far, first_near = [], [], [], []
        for i in range(1, n_ex):
            copy = remote(
                wa_in.at[lax.rem(e + i, n_ex)], wa_ref.at[z, e],
                a_send.at[i], a_recv.at[i], plane[i - 1],
            )
            copy.start()
            wa_far.append(copy)
        for i in range(1, n_dp):
            for m in range(2):
                copy = remote(
                    packs_in[m], packs[m].at[z, e], p_send.at[m, i], p_recv.at[m, i],
                    column[i - 1],
                )
                copy.start()
                pk_col.append(copy)
        for i in range(1, chips):
            copy = remote(tok_in, tok_all.at[e], t_send.at[i], t_recv.at[i], same_core[i - 1])
            copy.start()
            tok_far.append(copy)
        copy = remote(tok_in, tok_all.at[e], ts_send.at[0], ts_recv.at[0], sibling)
        copy.start()
        first_near.append(copy)
        first_own = stage(
            [wa_in.at[e], packs_in[0], packs_in[1], tok_in],
            [wa_ref.at[z, e], pk_ref.at[z, e], gr_ref.at[z, e], tok_all.at[e]],
            own_sem,
        )
        for copy in first_own:
            copy.wait()
        for copy in wa_far:
            copy.wait_recv()
        wa_col = []
        for i in range(1, n_dp):
            copy = remote(
                wa_ref.at[z], wa_ref.at[z], az_send.at[i], az_recv.at[i], column[i - 1]
            )
            copy.start()
            wa_col.append(copy)
        wo_sends(True)
        shared_copies = []
        for i in range(1, n_dp):
            for m in range(3):
                copy = remote(
                    s_in[m].at[lax.rem(lax.rem(z + i, n_dp), inner)], s_out[m].at[e, z],
                    sh_s.at[m, i], sh_r.at[m, i], column[i - 1],
                )
                copy.start()
                shared_copies.append(copy)
        own = [
            pltpu.make_async_copy(s_in[m].at[my_l], s_out[m].at[e, z], local.at[m])
            for m in range(3)
        ]
        for copy in own:
            copy.start()
        matrices[0].begin()
        for copy in pk_col:
            copy.wait_recv()
        pk_far = []
        for m in range(2):
            block = packs[m].at[:, e]
            for i in range(1, chips):
                copy = remote(block, block, pf_send.at[m, i], pf_recv.at[m, i], same_core[i - 1])
                copy.start()
                pk_far.append((i, m, copy))
            copy = remote(block, block, ps_send.at[m, 0], ps_recv.at[m, 0], sibling)
            copy.start()
            first_near.append(copy)
        for i in range(1, chips):
            source = lax.rem(c + chips - i, chips) * 2 + k
            tok_far[i - 1].wait_recv()
            copy = remote(
                tok_all.at[source], tok_all.at[source], ts_send.at[i], ts_recv.at[i], sibling
            )
            copy.start()
            first_near.append(copy)
        for i, m, copy in pk_far:
            copy.wait_recv()
            block = packs[m].at[:, lax.rem(c + chips - i, chips) * 2 + k]
            copy = remote(block, block, ps_send.at[m, i], ps_recv.at[m, i], sibling)
            copy.start()
            first_near.append(copy)
        for copy in first_near + wa_col:
            copy.wait()
        for copy in wa_far + pk_col + tok_far + [copy for _, _, copy in pk_far]:
            copy.wait_send()
        for move in moves:
            move.wait()
        gain_rows(gr_ref, gain_one, r, natural)
        gain_rows(gr_ref, gain_ref, r, by_owner)
        gain_rows(gr_ref, gain_lat, rl, natural)
        wl_ref = pk_ref.reshape(width, pk_ref.shape[3])
        wq_ref[...] = wa_ref[:, :, :, :wq_cols].reshape(width, wq_cols)
        for j in range(r // rl):
            block = wa_ref[:, :, j * rl : (j + 1) * rl, wq_cols:].reshape(KVR, we_cols)
            we_ref[:, j * we_cols : (j + 1) * we_cols] = block
        attend_forward(
            tok_all, gain_one.at[0:1], wq_ref, wl_ref, gain_lat.at[2:3], we_ref, cos, sin, keep,
            *att_out,
        )
        wo_arrivals()
        kept_moves = stage(kept, kept_hbm, kept_sem)
        wo = wo_out[...].reshape(hp * DV, width)

        def project(i, carry):
            at = pl.ds(pl.multiple_of(i * 2 * rows, 2 * rows), 2 * rows)
            block = mm(att_out[7][at, :], wo).astype(BF)
            x_ref[pl.ds(2 * i, 2)] = block.reshape(2, rows, width)
            return carry

        lax.fori_loop(0, chips, project, 0)
        near = []
        for i in list(range(1, chips)) + [0]:
            chip = lax.rem(c + i, chips)
            copy = remote(
                x_ref.at[chip * 2 + 1 - k], from_sib.at[chip], near_s.at[i], near_r.at[i], sibling
            )
            copy.start()
            near.append(copy)
        far = []
        for i in range(1, chips):
            chip = lax.rem(c + i, chips)
            near[i - 1].wait_recv()
            out_buf[i] = (
                x_ref[chip * 2 + k].astype(F32) + from_sib[chip].astype(F32)
            ).astype(BF)
            copy = remote(out_buf.at[i], from_far.at[i], far_s.at[i], far_r.at[i], same_core[i - 1])
            copy.start()
            far.append(copy)
        near[chips - 1].wait_recv()
        res_ref[...] = x_ref[e].astype(F32) + from_sib[c].astype(F32) + tok_ref[...].astype(F32)
        for i in range(1, chips):
            far[i - 1].wait_recv()
            res_ref[...] += from_far[i].astype(F32)
        residual = res_ref[...]
        scale = lax.rsqrt(jnp.mean(residual * residual, axis=-1, keepdims=True) + norm_eps)
        xbuf[...] = (residual * scale * gain_ref[1:2, :]).astype(BF)
        relays = [
            Relay(xbuf, xcol_ref, x_sems, n_dp, n_ex, inner),
            Relay(cot_in, cot_out, co_sems, n_dp, n_ex, inner),
        ]
        relays[0].begin()
        relays[0].pass_on()
        relays[1].begin()
        for matrix in matrices[1:]:
            matrix.begin()
        for copy in own:
            copy.wait()
        for copy in shared_copies:
            copy.wait_recv()
        plane, to_sib = [], []
        for m in range(3):
            block = s_out[m].at[e]
            for i in range(1, chips):
                copy = remote(block, block, sp_s.at[m, i], sp_r.at[m, i], same_core[i - 1])
                copy.start()
                plane.append(copy)
            copy = remote(block, block, sf_s.at[m, 0], sf_r.at[m, 0], sibling)
            copy.start()
            to_sib.append(copy)
        for m in range(3):
            for i in range(1, chips):
                plane[m * (chips - 1) + i - 1].wait_recv()
                block = s_out[m].at[lax.rem(c + chips - i, chips) * 2 + k]
                copy = remote(block, block, sf_s.at[m, i], sf_r.at[m, i], sibling)
                copy.start()
                to_sib.append(copy)
        relays[1].pass_on()
        for matrix in matrices:
            matrix.pass_on()
        for copy in to_sib:
            copy.wait()
        for relay in relays:
            relay.end()
        for copy in plane + shared_copies + near + far:
            copy.wait_send()
        wo_sends(False)
        for move in kept_moves:
            move.wait()
        for matrix in matrices:
            matrix.end()

    dma = pltpu.SemaphoreType.DMA
    ff_s = shared[0].shape[2]
    scratch = []
    for _ in experts:
        scratch += ExpertsIn.scratch(n_dp)
    sds = jax.ShapeDtypeStruct
    kept = [
        sds((seq, width), BF),
        sds((seq, first[2].shape[1]), F32),
        sds((seq, KVR), BF),
        sds((2, seq, 2 * DH), BF),
        sds((2, seq, 2 * DH), BF),
        sds((2, seq, DV), BF),
        sds((2, seq, 128), F32),
        sds((seq, 2 * DV), BF),
        sds((width, wq_cols), BF),
        sds((KVR, hp * (DH + DV)), BF),
        sds((hp, parts, r, width), BF),
        sds((n_dp, n_ex) + first[2].shape, BF),
    ]
    outs = pl.pallas_call(
        kernel,
        out_shape=kept
        + [
            sds((8, width), F32),
            sds((8, width), F32),
            sds((8, KVR), F32),
            sds((rows, width), F32),
            sds((inner, rows, width), BF),
            sds((inner, rows, width), BF),
        ]
        + [ExpertsIn.out(w, n_dp, n_ex) for w in experts]
        + [sds((n_ex, n_dp, r, ff_s), BF)] * 3,
        in_specs=[ANY] * 6 + [VMEM, ANY, VMEM] + [ANY] * (4 + count),
        out_specs=[ANY] * 12 + [VMEM] * 4 + [ANY] * (5 + count),
        scratch_shapes=like(tables[:2])
        + [
            pltpu.VMEM((n_ex, rows, width), BF),
            pltpu.VMEM((n_dp,) + first[1].shape, BF),
            pltpu.VMEM((n_dp, n_ex) + first[3].shape, BF),
        ]
        + like(kept)
        + [dma((2,)), dma((12,))]
        + [dma((chips,))] * 4
        + [dma((n_ex,))] * 2
        + [dma((n_dp,))] * 2
        + [dma((2, n_dp))] * 2
        + [dma((2, chips))] * 4
        + [dma((4,))]
        + [pltpu.VMEM((n_ex, rows, width), BF)]
        + [pltpu.VMEM((chips, rows, width), BF)] * 3
        + [pltpu.VMEM((rows, width), BF)]
        + [dma((chips,))] * 4
        + [dma((3, n_dp))] * 2
        + [dma((3, chips))] * 4
        + [dma((n_dp,)), dma((hp, parts)), dma((3,))]
        + Relay.scratch(inner) * 2
        + scratch,
        compiler_params=params(collective_id),
    )(*first, *tables, w_out, tok, cot, *experts, *shared)
    return outs[:8], outs[8:12], outs[12:15], outs[15:18], outs[18 : 18 + count], outs[18 + count :]


def silu_parts(a):
    sig = 1.0 / (1.0 + jnp.exp(-a))
    return a * sig, sig * (1.0 + a * (1.0 - sig))


def dispatch(hot, x, cot, shared, weights, n_dp, n_ex, inner, collective_id):
    chips = n_ex // 2
    rows, width = x.shape
    ff = shared[0].shape[1]
    tile = 256

    per_far = hot.shape[0] // chips
    count = len(weights)

    def kernel(hot_ref, x_hbm, c_hbm, g_hbm, u_hbm, d_hbm, *refs):
        w_in, refs = refs[:count], refs[count:]
        o_ref, go_ref, w_out, refs = refs[0], refs[1], refs[2 : 2 + count], refs[2 + count :]
        results, refs = refs[:5], refs[5:]
        hot_v, x_v, c_v, g_v, u_v, d_v, hid, ga, gb, b_v, send, recv, loads, keep = refs[:14]
        out_ref, dx_ref, gg_ref, gu_ref, gd_ref = refs[14:19]
        results_sem, rest = refs[19], refs[20:]
        z, e, c, k, sibling, same_core, column = places(n_dp, n_ex)
        moves = [
            pltpu.make_async_copy(src, dst, loads.at[j])
            for j, (src, dst) in enumerate(
                [
                    (hot_ref, hot_v), (x_hbm, x_v), (c_hbm, c_v),
                    (g_hbm, g_v), (u_hbm, u_v), (d_hbm, d_v),
                ]
            )
        ]
        for copy in moves:
            copy.start()
        greet(same_core + [sibling] + column + [(device[0], sibling[1]) for device in column])
        matrices = [
            ExpertsIn(w_in[m], w_out[m], rest[4 * m : 4 * m + 4], n_dp, n_ex, inner)
            for m in range(count)
        ]
        for matrix in matrices:
            matrix.begin()
        copies = []
        for j, (source, target) in enumerate(((x_v, o_ref), (c_v, go_ref))):
            if not j:
                moves[0].wait()
            moves[1 + j].wait()
            for i in list(range(1, chips)) + [0]:
                block = mm(hot_v[i * per_far : (i + 1) * per_far, :], source[...])
                b_v[j, i] = block.astype(BF)
                if i:
                    copy = remote(
                        b_v.at[j, i], target.at[i], send.at[j, i], recv.at[j, i],
                        same_core[i - 1],
                    )
                else:
                    copy = pltpu.make_async_copy(b_v.at[j, 0], target.at[0], keep.at[j])
                copy.start()
                copies.append(copy)
        for copy in moves[3:]:
            copy.wait()

        def rows_of(i, carry):
            at = pl.ds(pl.multiple_of(i * tile, tile), tile)
            first = mm(x_v[at, :], g_v[...])
            second = mm(x_v[at, :], u_v[...])
            silu, slope = silu_parts(first)
            low = (silu * second).astype(BF)
            hid[at, :] = low
            out_ref[at, :] = mm_cols(low, d_v[...])
            back = mm(c_v[at, :], d_v[...])
            low_a = (back * second * slope).astype(BF)
            low_b = (back * silu).astype(BF)
            ga[at, :] = low_a
            gb[at, :] = low_b
            dx_ref[at, :] = mm_cols(low_a, g_v[...]) + mm_cols(low_b, u_v[...])
            return carry

        lax.fori_loop(0, rows // tile, rows_of, 0)

        def columns_of(j, carry):
            at = pl.ds(pl.multiple_of(j * tile, tile), tile)
            gg_ref[at, :] = mm_rows(x_v[:, at], ga[...]).astype(BF)
            gu_ref[at, :] = mm_rows(x_v[:, at], gb[...]).astype(BF)
            gd_ref[at, :] = mm_rows(c_v[:, at], hid[...]).astype(BF)
            return carry

        lax.fori_loop(0, width // tile, columns_of, 0)
        result_moves = stage([out_ref, dx_ref, gg_ref, gu_ref, gd_ref], results, results_sem)
        for matrix in matrices:
            matrix.pass_on()
        for copy in copies + result_moves:
            copy.wait()
        for matrix in matrices:
            matrix.end()

    dma = pltpu.SemaphoreType.DMA
    sds = jax.ShapeDtypeStruct
    vmem = pltpu.VMEM
    scratch = []
    for _ in weights:
        scratch += ExpertsIn.scratch(n_dp)
    results = [sds((rows, width), F32)] * 2 + [sds((width, ff), BF)] * 3
    outs = pl.pallas_call(
        kernel,
        out_shape=[sds((chips, per_far, width), BF)] * 2
        + [ExpertsIn.out(weight, n_dp, n_ex) for weight in weights]
        + results,
        in_specs=[ANY] * (6 + count),
        out_specs=[ANY] * (7 + count),
        scratch_shapes=[vmem(hot.shape, BF)]
        + [vmem((rows, width), BF)] * 2
        + [vmem((width, ff), BF)] * 3
        + [vmem((rows, ff), BF)] * 3
        + [vmem((2, chips, per_far, width), BF)]
        + [dma((2, chips)), dma((2, chips)), dma((6,)), dma((2,))]
        + like(results)
        + [dma((5,))]
        + scratch,
        compiler_params=params(collective_id),
    )(hot, x, cot, *shared, *weights)
    return outs[:2], outs[2 : 2 + count], outs[2 + count], outs[3 + count], outs[4 + count :]


def experts_run(x_in, grad_in, weights, router, n_dp, n_ex, inner, collective_id):
    chips = n_ex // 2
    n_slots, width = x_in.shape
    ff = weights[0].shape[1]
    per_far = n_slots // chips
    r = width // (n_dp * n_ex)
    tile = per_far
    span = n_dp * r
    n_experts = inner * chips

    def kernel(*refs):
        in_hbm, refs = refs[:6], refs[6:]
        dx_out, dots_out, rows_out, back_out, g_out, refs = *refs[:4], refs[4:6], refs[6:]
        x_v, s_v, wg, wu, wd, route, a_v, b_v, h_v, dx_v, total, stage, dots_v, g_v = refs[:14]
        loads, send, recv, d_send, d_recv, local, rows_sem, out_sem = refs[14:22]
        z, e, c, k, sibling, same_core, column = places(n_dp, n_ex)
        moves = [
            pltpu.make_async_copy(src, dst, loads.at[j])
            for j, (src, dst) in enumerate(zip(in_hbm, (x_v, s_v, wg, wu, wd, route)))
        ]
        for j in (5, 0, 2, 3, 4, 1):
            moves[j].start()
        greet(same_core + [sibling] + column + [(device[0], sibling[1]) for device in column])
        back = ExpertsBack(total, back_out, refs[22:], n_dp, n_ex, inner, True)
        expert = c * inner + lax.rem(z, inner)
        for j in (5, 0, 2, 3, 4, 1):
            moves[j].wait()

        def forward(i, carry):
            at = pl.ds(pl.multiple_of(i * tile, tile), tile)
            x = x_v[at, :]
            logits = mm(x, route[...])
            lane = lax.broadcasted_iota(jnp.int32, logits.shape, 1)
            logits = jnp.where(lane < n_experts, logits, masked_score)
            chances = jnp.exp(logits - jnp.max(logits, axis=-1, keepdims=True))
            gate = jnp.sum(jnp.where(lane == expert, chances, 0.0), axis=-1, keepdims=True)
            gate = gate / jnp.sum(chances, axis=-1, keepdims=True)
            first = mm(x, wg[...])
            second = mm(x, wu[...])
            a_v[at, :] = first.astype(BF)
            b_v[at, :] = second.astype(BF)
            hid = (silu_parts(first)[0] * second).astype(BF)
            h_v[at, :] = hid
            g_v[at, :] = s_v[at, :]
            s_v[at, :] = (gate * s_v[at, :].astype(F32)).astype(BF)
            return carry

        lax.fori_loop(0, chips, forward, 0)

        for j in range(n_ex // 2):
            at = pl.ds(pl.multiple_of(((1 - k) * (n_ex // 2) + j) * span, span), span)
            block = mm_rows(s_v[:, at], h_v[...]).astype(BF)
            total[j] = block.reshape(n_dp, r, ff)
            back.near(j).start()
        for j in range(n_ex // 2):
            at = pl.ds(pl.multiple_of((k * (n_ex // 2) + j) * span, span), span)
            block = mm_rows(s_v[:, at], h_v[...]).astype(BF)
            back.own[j] = block.reshape(n_dp, r, ff)
        back.pass_on()

        def rows_of(i, carry):
            at = pl.ds(pl.multiple_of(i * tile, tile), tile)
            rows = mm_cols(h_v[at, :], wd[...]).astype(BF)
            dx_v[i] = rows
            dots = jnp.sum(
                g_v[at, :].astype(F32) * rows.astype(F32), axis=-1, keepdims=True
            )
            dots_v[i] = jnp.broadcast_to(dots, (tile, 128)).astype(BF)
            pltpu.make_async_copy(dx_v.at[i], rows_out.at[i], rows_sem.at[i]).start()
            return carry

        lax.fori_loop(0, chips, rows_of, 0)
        dot_copies = []
        for i in range(1, chips):
            copy = remote(
                dots_v.at[i], dots_out.at[i], d_send.at[i], d_recv.at[i], same_core[chips - i - 1]
            )
            copy.start()
            dot_copies.append(copy)
        copy = pltpu.make_async_copy(dots_v.at[0], dots_out.at[0], local.at[0])
        copy.start()
        dot_copies.append(copy)

        def hidden_rows(i, carry):
            at = pl.ds(pl.multiple_of(i * tile, tile), tile)
            grad = mm(s_v[at, :], wd[...])
            silu, slope = silu_parts(a_v[at, :].astype(F32))
            second = b_v[at, :].astype(F32)
            a_v[at, :] = (grad * second * slope).astype(BF)
            b_v[at, :] = (grad * silu).astype(BF)
            return carry

        lax.fori_loop(0, chips, hidden_rows, 0)
        copies = []
        for i in list(range(1, chips)) + [0]:
            at = slice(i * per_far, (i + 1) * per_far)
            block = mm_cols(a_v[at, :], wg[...]) + mm_cols(b_v[at, :], wu[...])
            pltpu.make_async_copy(dx_v.at[i], rows_out.at[i], rows_sem.at[i]).wait()
            dx_v[i] = block.astype(BF)
            if i:
                copy = remote(
                    dx_v.at[i], dx_out.at[i], send.at[i], recv.at[i], same_core[chips - i - 1]
                )
            else:
                copy = pltpu.make_async_copy(dx_v.at[0], dx_out.at[0], local.at[1])
            copy.start()
            copies.append(copy)

        def other_rows(j, carry):
            at = pl.ds(pl.multiple_of(j * span, span), span)
            for m, side in enumerate((a_v, b_v)):

                @pl.when(j > 0)
                def _(m=m):
                    pltpu.make_async_copy(stage.at[m], g_out[m].at[j - 1], out_sem.at[m]).wait()

                block = mm_rows(x_v[:, at], side[...]).astype(BF)
                stage[m] = block.reshape(n_dp, r, ff)
                pltpu.make_async_copy(stage.at[m], g_out[m].at[j], out_sem.at[m]).start()
            return carry

        lax.fori_loop(0, n_ex, other_rows, 0)
        for m in range(2):
            pltpu.make_async_copy(stage.at[m], g_out[m].at[n_ex - 1], out_sem.at[m]).wait()
        for copy in copies + dot_copies:
            copy.wait()
        back.end()

    dma = pltpu.SemaphoreType.DMA
    sds = jax.ShapeDtypeStruct
    vmem = pltpu.VMEM
    total = sds((n_ex, n_dp, r, ff), BF)
    blocks = sds((chips, per_far, width), BF)
    dots = sds((chips, per_far, 128), BF)
    outs = pl.pallas_call(
        kernel,
        out_shape=[blocks, dots, blocks, ExpertsBack.out(total, n_dp, inner), total, total],
        in_specs=[ANY] * 6,
        out_specs=[ANY] * 6,
        scratch_shapes=[vmem((n_slots, width), BF)] * 2
        + [vmem((width, ff), BF)] * 3
        + [vmem((width, 128), BF)]
        + [vmem((n_slots, ff), BF)] * 3
        + [
            vmem(blocks.shape, BF),
            vmem((n_ex // 2,) + total.shape[1:], BF),
            vmem((2, n_dp, r, ff), BF),
            vmem(dots.shape, BF),
            vmem((n_slots, width), BF),
            dma((6,)),
        ]
        + [dma((chips,))] * 4
        + [dma((2,)), dma((chips,)), dma((2,))]
        + ExpertsBack.scratch(total, n_dp, inner),
        compiler_params=params(collective_id),
    )(x_in, grad_in, *weights, router)
    return outs[0], outs[1], outs[2], outs[3], outs[4:]


class ExpertsBack:
    @staticmethod
    def scratch(total, n_dp, inner):
        n_ex, _, r, ff = total.shape
        dma = pltpu.SemaphoreType.DMA
        hh = n_ex // 2
        return [
            pltpu.VMEM((hh, n_dp, r, ff), BF),
            pltpu.VMEM((hh, n_dp, r, ff), BF),
            dma((hh,)),
            dma((hh,)),
            dma((hh,)),
            dma((hh, n_dp)),
            dma((n_dp // inner, 2, 2, hh)),
        ]

    @staticmethod
    def out(total, n_dp, inner):
        n_ex, _, r, ff = total.shape
        return jax.ShapeDtypeStruct((n_dp // inner, 2, n_ex, r, ff), BF)

    def __init__(self, total, out, scratch, n_dp, n_ex, inner, halved=False):
        self.total, self.out, self.n_dp, self.inner, self.halved = total, out, n_dp, inner, halved
        self.own, self.sib, self.near_s, self.near_r, self.load, self.send, self.recv = scratch
        self.z, self.e, self.c, self.k, self.sibling, _, _ = places(n_dp, n_ex)
        self.hh = n_ex // 2

    def near(self, j):
        return remote(
            self.total.at[j if self.halved else (1 - self.k) * self.hh + j], self.sib.at[j],
            self.near_s.at[j], self.near_r.at[j], self.sibling,
        )

    def loads(self, j):
        return pltpu.make_async_copy(
            self.total.at[self.k * self.hh + j], self.own.at[j], self.load.at[j]
        )

    def begin(self):
        for j in range(self.hh):
            self.near(j).start()
            self.loads(j).start()

    def route(self, j, i):
        d = lax.rem(self.z + i, self.n_dp)
        expert = lax.rem(self.z, self.inner)
        o = self.z // self.inner
        dst = self.out.at[o, lax.rem(expert, 2), self.k * self.hh + j]
        sem = self.recv.at[o, lax.rem(expert, 2), self.k, j]
        return self.own.at[j, d], dst, sem, (d, 2 * self.c + expert // 2)

    def stay(self, j):
        src, dst, sem, _ = self.route(j, 0)
        return pltpu.make_async_copy(src, dst, sem)

    def go(self, j, i):
        src, dst, sem, device = self.route(j, i)
        return remote(src, dst, self.send.at[j, i], sem, device)

    def here(self):
        return lax.rem(self.z, self.inner) // 2 == self.k

    def pass_on(self):
        for j in range(self.hh):
            self.near(j).wait_recv()
            if not self.halved:
                self.loads(j).wait()
            for d in range(self.n_dp):
                self.own[j, d] = (
                    self.own[j, d].astype(F32) + self.sib[j, d].astype(F32)
                ).astype(BF)
            for i in range(1, self.n_dp):
                self.go(j, i).start()
            pl.when(self.here())(lambda j=j: self.stay(j).start())
            pl.when(jnp.logical_not(self.here()))(lambda j=j: self.go(j, 0).start())

    def end(self):
        for j in range(self.hh):
            self.near(j).wait_send()
            for i in range(1, self.n_dp):
                self.go(j, i).wait_send()
            pl.when(jnp.logical_not(self.here()))(lambda j=j: self.go(j, 0).wait_send())
        for o in range(self.n_dp // self.inner):
            for i in range(2):
                for h in range(2):
                    source = o * self.inner + 2 * self.k + i
                    here = jnp.logical_and(source == self.z, self.k == h)
                    for j in range(self.hh):
                        region = self.out.at[o, i, h * self.hh + j]
                        sem = self.recv.at[o, i, h, j]

                        @pl.when(here)
                        def _(region=region, sem=sem, j=j):
                            pltpu.make_async_copy(self.own.at[j, self.z], region, sem).wait()

                        @pl.when(jnp.logical_not(here))
                        def _(region=region, sem=sem):
                            wait_recv(region, sem, self.sibling)


def rms_back(x, gain, grad):
    root = lax.rsqrt(jnp.mean(x * x, axis=-1, keepdims=True) + norm_eps)
    scaled = grad * gain
    along = jnp.mean(x * scaled, axis=-1, keepdims=True)
    return root * scaled - x * (root * root * root) * along, grad * x * root


def backward_exchange(
    grad, attend, hidden, latent_low, own, out, shared, totals, n_dp, n_ex, inner, collective_id
):
    chips = n_ex // 2
    rows, width = grad.shape
    seq = n_ex * rows
    extra = len(totals)
    wq, we = attend[1], attend[2]
    lat_cols = KVR + 2 * DR
    r = width // (n_dp * n_ex)
    rl = KVR // (n_dp * n_ex)
    parts = DV // r
    hp = n_dp // parts
    n_dev = n_dp * n_ex
    wq_cols = wq.shape[1]
    we_cols = rl * we.shape[1] // r
    head_cols = wq_cols + we_cols
    given_arrays = [*attend, hidden, latent_low, *own]
    big = [j for j, array in enumerate(given_arrays) if array.shape[0] > 8 or array.ndim > 2]

    def kernel(*refs):
        grad_ref, given, refs = refs[0], list(refs[1:22]), refs[22:]
        out_ref, sh_in, refs = refs[0], refs[1:4], refs[4:]
        t_refs, refs = refs[:extra], refs[extra:]
        tok_out, vec_out, pack_out, heads_mid, heads_out, wout_out, out_got = refs[:7]
        sh_out, back_refs, refs = refs[7:10], refs[10 : 10 + extra], refs[10 + extra :]
        gbuf, att_tmp, refs = refs[0], refs[1:8], refs[8:]
        part_l, bufs, sums, refs = refs[0], refs[1:7], refs[7:9], refs[9:]
        hsrc, wsrc, pack, psib, pout, pfar, psum, pbuf, vec, vbuf, vzbuf = refs[:11]
        refs = refs[11:]
        t_s, t_r, ts_s, ts_r, local = refs[:5]
        sems, refs = refs[5:13], refs[13:]
        (
            h_s, h_r, hz_s, hz_r, w_s, w_r, pn_s, pn_r, pf_s, pf_r, pc_s, pc_r, s_s, s_r,
            v_s, v_r, vz_s, vz_r, o_s, o_r,
        ) = refs[:20]
        staged, stage_sem, rest = refs[20 : 20 + len(big)], refs[20 + len(big)], refs[21 + len(big) :]
        moves = stage([given[j] for j in big], staged, stage_sem)
        for j, ref in zip(big, staged):
            given[j] = ref
        att_in, hidden_ref, low_ref = given[:11], given[11], given[12]
        wl_ref, lat_ref, tok_ref, gain_ref, glat_ref, gnat_ref, router_ref, gtwo_ref = given[13:]
        gain_ref, glat_ref = gain_ref.at[0:1], glat_ref.at[2:3]
        x_refs = (gbuf, part_l)
        group = column_group(lax.axis_index("dp"), lax.axis_index("expert"), inner)
        z, e, c, k, sibling, same_core, column = places(n_dp, n_ex)
        plane = [(z, lax.rem(e + i, n_ex)) for i in range(1, n_ex)]
        part = lax.rem(e, parts)
        members = [
            (lax.rem(z + i, n_dp), e - part + lax.rem(part + j, parts))
            for i in range(n_dp)
            for j in range(parts)
        ]
        greet(plane + column + [(d[0], sibling[1]) for d in column] + members[1:])
        backs = [
            ExpertsBack(t_refs[m], back_refs[m], rest[7 * m : 7 * m + 7], n_dp, n_ex, inner)
            for m in range(extra)
        ]
        gather, to_sib, others = [], [], []
        for i in range(1, chips):
            copy = remote(grad_ref, gbuf.at[e], t_s.at[i], t_r.at[i], same_core[i - 1])
            copy.start()
            gather.append(copy)
        copy = remote(grad_ref, gbuf.at[e], ts_s.at[0], ts_r.at[0], sibling)
        copy.start()
        to_sib.append(copy)
        keep = pltpu.make_async_copy(grad_ref, gbuf.at[e], local.at[0])
        keep.start()
        for back in backs:
            back.begin()
        for m in range(3):
            for i in range(1, n_dp):
                copy = remote(
                    sh_in[m].at[lax.rem(z + i, n_dp)], sh_out[m].at[z],
                    s_s.at[m, i], s_r.at[m, i], column[i - 1],
                )
                copy.start()
                others.append(copy)
            copy = pltpu.make_async_copy(sh_in[m].at[z], sh_out[m].at[z], local.at[1 + m])
            copy.start()
            others.append(copy)
        mine = lax.rem(z, inner)
        for i in range(1, inner):
            copy = remote(
                out_ref.at[lax.rem(mine + i, inner)], out_got.at[mine], o_s.at[i], o_r.at[i],
                group[i],
            )
            copy.start()
            others.append(copy)
        copy = pltpu.make_async_copy(out_ref.at[mine], out_got.at[mine], local.at[5])
        copy.start()
        others.append(copy)
        for i in range(1, chips):
            gather[i - 1].wait_recv()
            block = gbuf.at[lax.rem(c + chips - i, chips) * 2 + k]
            copy = remote(block, block, ts_s.at[i], ts_r.at[i], sibling)
            copy.start()
            to_sib.append(copy)
        for back in backs:
            back.pass_on()
        keep.wait()
        for copy in to_sib:
            copy.wait_recv()
        for copy in gather + to_sib:
            copy.wait_send()
        gat, grad_wout, dk, dv, grad_query, grad_expanded, grad_rope = att_tmp
        for move in moves:
            move.wait()
        attend_backward(gbuf, *att_in, *att_tmp)

        wsrc[...] = grad_wout[...].astype(BF).reshape(hp, parts, r, width)

        def wout_sends(start):
            for h in range(hp):
                for p in range(parts):
                    target = (part * hp + h, e - part + p)
                    here = jnp.logical_and(part * hp + h == z, p == part)

                    def far(h=h, p=p, target=target):
                        copy = remote(
                            wsrc.at[h, p], wout_out.at[z], w_s.at[h, p], w_r.at[z], target
                        )
                        if start:
                            copy.start()
                        else:
                            copy.wait_send()

                    pl.when(jnp.logical_not(here))(far)
                    if start:

                        @pl.when(here)
                        def _(h=h, p=p):
                            pltpu.make_async_copy(
                                wsrc.at[h, p], wout_out.at[z], w_r.at[z]
                            ).start()

        wout_sends(True)

        def spread(i, carry):
            at = pl.ds(pl.multiple_of(i * 2 * rows, 2 * rows), 2 * rows)
            block = mm_cols(grad_query[at, :], att_in[1][...]).astype(BF)
            gbuf[pl.ds(2 * i, 2)] = block.reshape(2, rows, width)
            block = mm_cols(grad_expanded[at, :], att_in[2][...]).astype(BF)
            part_l[pl.ds(2 * i, 2), :, :KVR] = block.reshape(2, rows, KVR)
            block = grad_rope[at, :].astype(BF)
            part_l[pl.ds(2 * i, 2), :, KVR:] = block.reshape(2, rows, 2 * DR)
            return carry

        lax.fori_loop(0, chips, spread, 0)
        near, far = {}, {}
        for i in list(range(1, chips)) + [0]:
            chip = lax.rem(c + i, chips)
            for j in range(2):
                near[i, j] = remote(
                    x_refs[j].at[chip * 2 + 1 - k],
                    bufs[3 * j].at[chip],
                    sems[4 * j].at[i],
                    sems[4 * j + 1].at[i],
                    sibling,
                )
                near[i, j].start()
        for i in range(1, chips):
            chip = lax.rem(c + i, chips)
            for j in range(2):
                from_sib, out_buf, from_far = bufs[3 * j : 3 * j + 3]
                near[i, j].wait_recv()
                out_buf[i] = (
                    x_refs[j][chip * 2 + k].astype(F32) + from_sib[chip].astype(F32)
                ).astype(BF)
                far[i, j] = remote(
                    out_buf.at[i],
                    from_far.at[i],
                    sems[4 * j + 2].at[i],
                    sems[4 * j + 3].at[i],
                    same_core[i - 1],
                )
                far[i, j].start()

        per_tile = 256 // r

        def wq_rows(i, carry):
            at = pl.ds(pl.multiple_of(i * 256, 256), 256)
            block = mm_rows(hidden_ref[:, at], grad_query[...]).astype(BF)
            hsrc[pl.ds(i * per_tile, per_tile), :, :wq_cols] = block.reshape(
                per_tile, r, wq_cols
            )
            return carry

        lax.fori_loop(0, width // 256, wq_rows, 0)
        grad_we = mm_rows(low_ref[...], grad_expanded[...]).astype(BF)
        for j in range(r // rl):
            block = grad_we[:, j * we_cols : (j + 1) * we_cols]
            hsrc[:, j * rl : (j + 1) * rl, wq_cols:] = block.reshape(n_dev, rl, we_cols)
        heads_far = []
        for i in range(1, n_ex):
            for d in range(n_dp):
                copy = remote(
                    hsrc.at[d * n_ex + lax.rem(e + i, n_ex)], heads_mid.at[d, e],
                    h_s.at[i, d], h_r.at[i, d], plane[i - 1],
                )
                copy.start()
                heads_far.append(copy)
        for d in range(n_dp):
            copy = pltpu.make_async_copy(
                hsrc.at[d * n_ex + e], heads_mid.at[d, e], h_r.at[0, d]
            )
            copy.start()
            copy.wait()
        for j in range(2):
            near[0, j].wait_recv()
            sums[j][...] = x_refs[j][e].astype(F32) + bufs[3 * j][c].astype(F32)
        for i in range(1, chips):
            for j in range(2):
                far[i, j].wait_recv()
                sums[j][...] += bufs[3 * j + 2][i].astype(F32)

        at = pl.ds(pl.multiple_of(e * rows, rows), rows)
        cos, sin = att_in[3][at, :], att_in[4][at, :]
        lat_grad, lat_gain = rms_back(lat_ref[:, :KVR], glat_ref[...], sums[1][:, :KVR])
        rope = turn(sums[1][:, KVR:], cos, sin, -1.0)
        lane = lax.broadcasted_iota(jnp.int32, rope.shape, 1)
        rope = jnp.where(lane < DR, rope, 0.0)
        low = jnp.concatenate([lat_grad, rope], axis=1).astype(BF)
        total = sums[0][...] + mm_cols(low, wl_ref[:, :lat_cols])
        tok_grad, tok_gain = rms_back(tok_ref[...].astype(F32), gain_ref[...], total)
        tok_out[...] = gnat_ref[...] + tok_grad
        vec[...] = jnp.zeros_like(vec)
        vec[0:1, :] = jnp.sum(tok_gain, axis=0, keepdims=True)
        vec[1:2, :] = gtwo_ref[...]
        vec[2:3, :KVR] = jnp.sum(lat_gain, axis=0, keepdims=True)
        vec_far = []
        for i in range(1, n_ex):
            copy = remote(vec, vbuf.at[i], v_s.at[i], v_r.at[i], plane[i - 1])
            copy.start()
            vec_far.append(copy)
        for d in range(n_dp):
            block = hidden_ref[at, d * n_ex * r : (d + 1) * n_ex * r]
            block = mm_rows(block, low).reshape(n_ex, r, lat_cols)
            pack[:, d * r : (d + 1) * r, :KVR] = block[:, :, :KVR].astype(BF)
            block = block[:, :, KVR:] + router_ref[:, d * r : (d + 1) * r].astype(F32)
            pack[:, d * r : (d + 1) * r, KVR:] = block.astype(BF)
        pack_near, pack_far = [], []
        for i in list(range(1, chips)) + [0]:
            chip = lax.rem(c + i, chips)
            copy = remote(pack.at[chip * 2 + 1 - k], psib.at[chip], pn_s.at[i], pn_r.at[i], sibling)
            copy.start()
            pack_near.append(copy)
        for copy in heads_far:
            copy.wait_recv()
        heads_col = []
        for i in range(1, n_dp):
            d = lax.rem(z + i, n_dp)
            copy = remote(
                heads_mid.at[d], heads_out.at[z], hz_s.at[i], hz_r.at[i], column[i - 1]
            )
            copy.start()
            heads_col.append(copy)
        copy = pltpu.make_async_copy(heads_mid.at[z], heads_out.at[z], local.at[4])
        copy.start()
        heads_col.append(copy)
        for i in range(1, chips):
            chip = lax.rem(c + i, chips)
            pack_near[i - 1].wait_recv()
            pout[i] = (pack[chip * 2 + k].astype(F32) + psib[chip].astype(F32)).astype(BF)
            copy = remote(pout.at[i], pfar.at[i], pf_s.at[i], pf_r.at[i], same_core[i - 1])
            copy.start()
            pack_far.append(copy)
        for copy in vec_far:
            copy.wait_recv()
            copy.wait_send()
        for i in range(1, n_ex):
            vec[...] += vbuf[i]
        vec_col = []
        for i in range(1, n_dp):
            copy = remote(vec, vzbuf.at[i], vz_s.at[i], vz_r.at[i], column[i - 1])
            copy.start()
            vec_col.append(copy)
        pack_near[chips - 1].wait_recv()
        total = pack[e].astype(F32) + psib[c].astype(F32)
        for i in range(1, chips):
            pack_far[i - 1].wait_recv()
            total = total + pfar[i].astype(F32)
        psum[...] = total.astype(BF).reshape(n_dp, r, lat_cols)
        pack_col = []
        for i in range(1, n_dp):
            copy = remote(
                psum.at[lax.rem(z + i, n_dp)], pbuf.at[i], pc_s.at[i], pc_r.at[i], column[i - 1]
            )
            copy.start()
            pack_col.append(copy)
        result = vec[...]
        for i in range(1, n_dp):
            vec_col[i - 1].wait_recv()
            result = result + vzbuf[i]
        vec_out[...] = result
        result = psum[z].astype(F32)
        for i in range(1, n_dp):
            pack_col[i - 1].wait_recv()
            result = result + pbuf[i].astype(F32)
        pack_out[...] = result

        for i in range(n_dp):
            here = jnp.logical_and(z // hp == part, z == i)

            @pl.when(here)
            def _(i=i):
                pltpu.make_async_copy(
                    wsrc.at[lax.rem(z, hp), part], wout_out.at[i], w_r.at[i]
                ).wait()

            @pl.when(jnp.logical_not(here))
            def _(i=i):
                wait_recv(wout_out.at[i], w_r.at[i], sibling)

        wout_sends(False)
        for copy in list(near.values()) + list(far.values()) + heads_far:
            copy.wait_send()
        for copy in pack_near + pack_far + vec_col + pack_col:
            copy.wait_send()
        for copy in heads_col + others:
            copy.wait()
        for back in backs:
            back.end()

    dma = pltpu.SemaphoreType.DMA
    sds = jax.ShapeDtypeStruct
    vmem = pltpu.VMEM
    scratch = [
        vmem((n_ex, rows, width), BF),
        vmem((seq, 2 * DV), BF),
        vmem((2 * DV, width), F32),
        vmem((seq, 2 * DH), F32),
        vmem((seq, DV), F32),
        vmem((seq, wq.shape[1]), BF),
        vmem((seq, we.shape[1]), BF),
        vmem((seq, 2 * DR), F32),
        vmem((n_ex, rows, lat_cols), BF),
    ]
    scratch += [vmem((chips, rows, width), BF)] * 3 + [vmem((chips, rows, lat_cols), BF)] * 3
    scratch += [
        vmem((rows, width), F32),
        vmem((rows, lat_cols), F32),
        vmem((n_dev, r, head_cols), BF),
        vmem((hp, parts, r, width), BF),
        vmem((n_ex, n_dp * r, lat_cols), BF),
        vmem((chips, n_dp * r, lat_cols), BF),
        vmem((chips, n_dp * r, lat_cols), BF),
        vmem((chips, n_dp * r, lat_cols), BF),
        vmem((n_dp, r, lat_cols), BF),
        vmem((n_dp, r, lat_cols), BF),
        vmem((8, width), F32),
        vmem((n_ex, 8, width), F32),
        vmem((n_dp, 8, width), F32),
    ]
    scratch += [dma((chips,))] * 4 + [dma((6,))] + [dma((chips,))] * 8
    scratch += [dma((n_ex, n_dp))] * 2 + [dma((n_dp,))] * 2 + [dma((hp, parts)), dma((n_dp,))]
    scratch += [dma((chips,))] * 4 + [dma((n_dp,))] * 2 + [dma((3, n_dp))] * 2
    scratch += [dma((n_ex,))] * 2 + [dma((n_dp,))] * 2 + [dma((inner,))] * 2
    scratch += like([given_arrays[j] for j in big]) + [dma((len(big),))]
    for total in totals:
        scratch += ExpertsBack.scratch(total, n_dp, inner)
    outs = pl.pallas_call(
        kernel,
        out_shape=[
            sds((rows, width), F32),
            sds((8, width), F32),
            sds((r, lat_cols), F32),
            sds((n_dp, n_ex, r, head_cols), BF),
            sds((n_dp, n_ex, r, head_cols), BF),
            sds((n_dp, r, width), BF),
            sds(out.shape, BF),
        ]
        + [sds(array.shape, BF) for array in shared]
        + [ExpertsBack.out(total, n_dp, inner) for total in totals],
        in_specs=[ANY]
        + [ANY if j in big else VMEM for j in range(21)]
        + [ANY] * (4 + extra),
        out_specs=[VMEM] * 3 + [ANY] * (7 + extra),
        scratch_shapes=scratch,
        compiler_params=params(collective_id),
    )(grad, *attend, hidden, latent_low, *own, out, *shared, *totals)
    return outs[:3], outs[4], outs[5], outs[6], outs[7:10], outs[10:]


def finish(heads, wout, out, residual, shared, order, hp, rl, wq_cols):
    n_dp, n_ex, r, cols = heads.shape
    we_cols = cols - wq_cols
    count = len(order)
    per = (DH + DV) // we_cols
    width = wout.shape[2]
    inner, _, ff = shared[0].shape

    def natural(values, t):
        tile = values[:, :128]
        lane = lax.broadcasted_iota(jnp.int32, tile.shape, 1)
        for p in range(128 // r):
            at = t * (128 // r) + p
            start = (at % n_ex * n_dp + at // n_ex) * r
            piece = values[:, start // 128 * 128 : start // 128 * 128 + 128]
            turn_by = (p * r - start) % 128
            piece = pltpu.roll(piece, turn_by, 1) if turn_by else piece
            tile = jnp.where(lane // r == p, piece, tile) if p else piece
        return tile

    def kernel(x_ref, w_ref, y_ref, res_ref, s_a, s_b, s_c, q_ref, e_ref, wo_ref, out_ref, *s_out):
        for pair in range(count // 2):
            pieces = []
            for h in (2 * pair, 2 * pair + 1):
                device, i = order[h] // hp, order[h] % hp
                total = x_ref[0, device].astype(F32)
                for d in range(1, n_dp):
                    total = total + x_ref[d, device].astype(F32)
                rope = total[:, hp * DH : hp * DH + 2 * DR]
                pieces.append((total[:, i * DH : (i + 1) * DH], rope, i))
                for j in range(per):
                    at = (h * per + j) * we_cols
                    e_ref[:, at : at + we_cols] = total[
                        (i * per + j) * rl : (i * per + j + 1) * rl, wq_cols:
                    ]
            (plain, rope, i), (plain_b, rope_b, i_b) = pieces
            lane = lax.broadcasted_iota(jnp.int32, plain.shape, 1)
            rope = pltpu.roll(rope, DR, 1) if i else rope
            rope_b = rope_b if i_b else pltpu.roll(rope_b, DR, 1)
            turned = pltpu.roll(plain_b, DR, 1)
            at = pair * 2 * (DH + DR)
            q_ref[:, at : at + DH] = plain
            q_ref[:, at + DH : at + 2 * DH] = jnp.where(lane < DR, rope, turned)
            q_ref[:, at + 2 * DH : at + 3 * DH] = jnp.where(lane < DR, turned, rope_b)
        total = w_ref[0].astype(F32)
        for d in range(1, n_dp):
            total = total + w_ref[d].astype(F32)
        for t in range(width // 128):
            wo_ref[:, t * 128 : (t + 1) * 128] = natural(total, t)
        total = res_ref[...]
        for d in range(inner):
            total = total + y_ref[d].astype(F32)
        for t in range(width // 128):
            out_ref[:, t * 128 : (t + 1) * 128] = natural(total, t).astype(BF)
        for source, target in zip((s_a, s_b, s_c), s_out):
            for j in range(inner):
                total = source[j].astype(F32)
                target[:, j * ff : (j + 1) * ff] = total

    sds = jax.ShapeDtypeStruct
    return pl.pallas_call(
        kernel,
        out_shape=[
            sds((r, count * (DH + DR)), F32),
            sds((rl, count * (DH + DV)), F32),
            sds((r, width), F32),
            sds(residual.shape, BF),
        ]
        + [sds((r, inner * ff), F32)] * 3,
        in_specs=[VMEM] * 7,
        out_specs=[VMEM] * 7,
        compiler_params=pltpu.CompilerParams(vmem_limit_bytes=40 << 20),
    )(heads, wout, out, residual, *shared)


def shards(
    tokens,
    cotangent,
    lengths,
    routes,
    place_order,
    attn_gain,
    w_query,
    w_latent,
    latent_gain,
    w_expand,
    w_out,
    ffn_gain,
    w_router,
    shared_gate,
    shared_up,
    shared_down,
    expert_gate,
    expert_up,
    expert_down,
):
    rows, width = tokens.shape
    n_dp = lax.axis_size("dp")
    n_ex = lax.axis_size("expert")
    chips = n_ex // 2
    z = lax.axis_index("dp")
    e = lax.axis_index("expert")
    chip = e // 2
    n_experts = w_router.shape[1]
    top_k = routes.shape[1]
    capacity = (rows * top_k * 5 + 4 * n_experts - 1) // (4 * n_experts)
    cap = (capacity + 15) // 16 * 16
    seq = rows * n_ex
    r = w_query.shape[0]
    rl = w_expand.shape[0]
    hp = H // n_ex
    parts = DV // r
    heads = [
        (d * n_ex + (j // parts) * parts) * r // DV
        for j in range(n_ex)
        for d in range(j % parts * hp, j % parts * hp + hp)
    ]
    heads_back = [heads.index(h) for h in range(H)]
    inner = n_experts // chips
    my_local = lax.rem(z, inner)
    ff_e = expert_gate.shape[2]
    ff_s = shared_gate.shape[1] // inner
    lat = KVR + DR
    head_cols = hp * (DH + DR)
    kv_cols = hp * (DH + DV)

    def to_owner_order(values):
        cut = values.reshape(values.shape[0], n_dp, n_ex, r)
        return cut.transpose(0, 2, 1, 3).reshape(values.shape)

    def from_owner_order(values):
        cut = values.reshape(values.shape[0], n_ex, n_dp, r)
        return cut.transpose(0, 2, 1, 3).reshape(values.shape)

    def pick(values, index, axis=0):
        return lax.dynamic_index_in_dim(values, index, axis, keepdims=False)

    wq_send = jnp.take(w_query.reshape(r, H, DH + DR), jnp.array(heads), axis=1)
    wq_send = wq_send.reshape(r, n_ex, hp, DH + DR)
    wq_send = jnp.concatenate(
        [
            wq_send[..., :DH].reshape(r, n_ex, hp * DH),
            wq_send[..., DH:].reshape(r, n_ex, hp * DR),
        ],
        axis=-1,
    ).transpose(1, 0, 2)
    we_send = jnp.take(w_expand.reshape(rl, H, DH + DV), jnp.array(heads), axis=1)
    we_cols = rl * kv_cols // r
    we_send = we_send.reshape(rl, n_ex, r // rl, we_cols).transpose(1, 2, 0, 3)
    we_send = we_send.reshape(n_ex, r, we_cols)
    wa_send = jnp.concatenate([wq_send, we_send], axis=-1)
    slot_own = slot_places(routes, place_order[0], capacity)
    slot_place = jnp.where(slot_own >= 0, slot_own - routes * capacity, -1)
    slot_cols = 2 * rows * top_k // r
    slot_pack = jnp.stack([routes, slot_place]).astype(BF).reshape(2, r, slot_cols // 2)
    small_cols = lat + n_experts
    pack_cols = (small_cols + slot_cols + 127) // 128 * 128
    pack = jnp.concatenate(
        [
            w_latent,
            w_router,
            slot_pack[0],
            slot_pack[1],
            jnp.zeros((r, pack_cols - small_cols - slot_cols), BF),
        ],
        axis=1,
    )
    cot_owner = to_owner_order(cotangent)
    gains = jnp.stack(
        [jnp.pad(gain, (0, 128 - gain.shape[0])) for gain in (attn_gain, ffn_gain, latent_gain)]
    )
    gains = jnp.pad(gains, ((0, 13), (0, 0)))

    positions = jnp.arange(seq)
    lane = np.arange(2 * DR) % (DR // 2)
    angles = np.arange(seq)[:, None] * (10000.0 ** (-2.0 * lane / DR))[None, :]
    cos_wide, sine_wide = (jnp.asarray(f(angles), F32) for f in (np.cos, np.sin))
    keep = (positions < lengths[0]).astype(F32)[None]
    attend_out, (wq, wexp, wo_rows, pk_all), gain_outs, rows_outs, (wg,), shared_w = (
        forward_exchange(
            [tokens, wa_send, pack, gains],
            [cos_wide, sine_wide, keep],
            to_owner_order(w_out),
            to_owner_order(tokens),
            cot_owner,
            [expert_gate.reshape(-1, n_ex, r, ff_e)],
            [
                w.reshape(r, inner, ff_s).transpose(1, 0, 2)
                for w in (shared_gate, shared_up, shared_down)
            ],
            n_dp,
            n_ex,
            inner,
            2,
        )
    )
    residual, x_col, cot_col = rows_outs
    gain_two = gain_outs[1][1]
    hidden_one, latent_raw, latent_low, qcat, kcat, value, lse, attended = attend_out
    wo_rows = wo_rows.reshape(hp * DV, width)
    cot_col = cot_col.reshape(inner * rows, width)
    hidden_two = pick(x_col, my_local)
    x_col = x_col.reshape(inner * rows, width)

    router = pk_all[..., lat : lat + n_experts].transpose(1, 0, 2, 3).reshape(width, n_experts)
    pk_flat = pk_all.reshape(width, pack_cols)

    slots_all = n_experts * capacity
    slot_col = pick(pk_all[..., small_cols : small_cols + slot_cols], e, 1)
    slot_col = lax.dynamic_slice_in_dim(slot_col, z - my_local, inner, 0).astype(jnp.int32)
    slot_col = slot_col.reshape(inner, r, 2, slot_cols // 2).transpose(2, 0, 1, 3)
    slot_col = slot_col.reshape(2, inner, rows, top_k)
    slot_ids = jnp.where(
        slot_col[1] >= 0,
        slot_col[0] * capacity + slot_col[1] + (jnp.arange(inner) * slots_all)[:, None, None],
        -1,
    ).reshape(inner * rows, top_k)
    place = jnp.arange(cap)
    far_experts = [lax.rem(chip + m, chips) * inner + my_local for m in range(chips)]
    wanted = (
        jnp.stack(far_experts)[:, None, None] * capacity
        + (jnp.arange(inner) * slots_all)[None, :, None]
        + place[None, None, :]
    )
    wanted = jnp.where(place[None, None, :] < capacity, wanted, -2).reshape(-1)
    n_slots = wanted.shape[0]
    per_far = n_slots // chips
    hot = sum((wanted[:, None] == slot_ids[None, :, j]).astype(BF) for j in range(top_k))
    hot_t = sum((slot_ids[:, j][:, None] == wanted[None, :]).astype(BF) for j in range(top_k))

    (x_in, grad_in), (wu, wd), shared_out, shared_dx, shared_grads = dispatch(
        hot,
        x_col,
        cot_col,
        [w.reshape(width, ff_s) for w in shared_w],
        [w.reshape(-1, n_ex, r, ff_e) for w in (expert_up, expert_down)],
        n_dp,
        n_ex,
        inner,
        8,
    )
    x_in = x_in.reshape(n_slots, width)
    grad_in = grad_in.reshape(n_slots, width)
    wg, wu, wd = (w.reshape(width, ff_e) for w in (wg, wu, wd))

    def probs_of(logits):
        top = jnp.max(logits, axis=-1, keepdims=True)
        exp_logits = jnp.exp(logits - top)
        return exp_logits / jnp.sum(exp_logits, axis=-1, keepdims=True)

    dx_back, dots_back, expert_rows, down_back, expert_totals = experts_run(
        x_in,
        grad_in,
        [wg, wu, wd],
        jnp.pad(router, ((0, 0), (0, 128 - n_experts))),
        n_dp,
        n_ex,
        inner,
        9,
    )
    dx_back = dx_back.reshape(n_slots, width)

    col_probs = probs_of(mm(x_col, router))
    expert_axis = jnp.arange(n_experts)[None, :]
    gates = [
        jnp.sum(jnp.where(expert_axis == expert, col_probs, 0.0), axis=1, keepdims=True)
        for expert in far_experts
    ]
    gate_hot = jnp.concatenate(
        [hot_t[:, m * per_far : (m + 1) * per_far] * gates[m].astype(BF) for m in range(chips)],
        axis=1,
    )
    dots = dots_back.reshape(n_slots, 128)[:, 0].astype(F32)[None] * hot_t.astype(F32)
    dots = jnp.sum(dots.reshape(inner * rows, chips, per_far), axis=-1)
    grad_probs_col = sum(
        jnp.where(expert_axis == far_experts[m], dots[:, m : m + 1], 0.0) for m in range(chips)
    )
    dx_col = mm(hot_t, dx_back) + shared_dx
    dx_send = jnp.concatenate(
        [dx_col, grad_probs_col, jnp.zeros((inner * rows, 128 - n_experts), F32)], axis=1
    ).astype(BF)
    dx_sum, shared_sums, rows_back, (gate_back,) = column_sum(
        dx_send.reshape(inner, rows, width + 128),
        expert_rows,
        [grad.reshape(n_ex, n_dp, r, ff_s) for grad in shared_grads],
        expert_totals[:1],
        n_dp,
        n_ex,
        inner,
        3,
    )
    router_probs = lax.dynamic_slice_in_dim(col_probs, my_local * rows, rows, 0)
    grad_probs = dx_sum[:, width : width + n_experts]
    grad_logits = (
        router_probs * (grad_probs - jnp.sum(grad_probs * router_probs, axis=-1, keepdims=True))
    ).astype(BF)
    grad_router = mm_rows(hidden_two, grad_logits)
    grad_hidden_two = dx_sum[:, :width] + mm_cols(grad_logits, router)
    _, norm_two_back = jax.vjp(rms_norm, residual, gain_two)
    grad_resid_norm, grad_gain_two = norm_two_back(grad_hidden_two)
    grad_residual = cot_owner.astype(F32) + grad_resid_norm

    out_col = mm(gate_hot, rows_back.reshape(n_slots, width)) + shared_out
    latent_own = lax.dynamic_slice_in_dim(latent_raw, e * rows, rows, 0)
    router_back = jnp.pad(
        grad_router.reshape(n_ex, n_dp * r, n_experts),
        ((0, 0), (0, 0), (DR, DR - n_experts)),
    ).astype(BF)
    (grad_tokens, vec_sum, pack_sum), heads_got, wout_got, out_got, shared_got, (up_back,) = (
        backward_exchange(
            grad_residual.astype(BF),
            [wo_rows, wq, wexp, cos_wide, sine_wide, keep, qcat, kcat, value, lse, attended],
            hidden_one,
            latent_low,
            [
                pk_flat,
                latent_own,
                tokens,
                gain_outs[0],
                gain_outs[2],
                from_owner_order(grad_residual),
                router_back,
                grad_gain_two[None],
            ],
            out_col.astype(BF).reshape(inner, rows, width),
            shared_sums,
            expert_totals[1:2],
            n_dp,
            n_ex,
            inner,
            5,
        )
    )

    def added(values):
        return jnp.sum(values.astype(F32), axis=0)

    outer = n_dp // inner
    if outer > 1:
        shared_got = [
            added(got.reshape(outer, inner, r, ff_s)).astype(BF) for got in shared_got
        ]
    sum_wq, sum_we, sum_wout, out_tokens, sum_sgate, sum_sup, sum_sdown = finish(
        heads_got, wout_got, out_got, residual, shared_got, heads_back, hp, rl, head_cols
    )
    device = z * n_ex + e
    sum_gain_one = lax.dynamic_slice_in_dim(vec_sum[0], device * r, r, 0)
    sum_gain_two = lax.dynamic_slice_in_dim(vec_sum[1], (e * n_dp + z) * r, r, 0)
    sum_gain_lat = lax.dynamic_slice_in_dim(vec_sum[2], device * rl, rl, 0)
    sum_egate, sum_eup, sum_edown = (
        added(back).reshape(-1, n_ex * r, ff_e) for back in (gate_back, up_back, down_back)
    )
    return (
        out_tokens,
        grad_tokens,
        sum_gain_one,
        sum_wq,
        pack_sum[:, :lat],
        sum_gain_lat,
        sum_we,
        sum_wout,
        sum_gain_two,
        pack_sum[:, lat : lat + n_experts],
        sum_sgate,
        sum_sup,
        sum_sdown,
        sum_egate,
        sum_eup,
        sum_edown,
    )


def solution(mesh):
    both = ("dp", "expert")
    in_specs = (
        P(both, None),
        P(both, None),
        P("dp"),
        P(both, None),
        P(both, None),
        P(both),
        P(both, None),
        P(both, None),
        P(both),
        P(both, None),
        P(both, None),
        P(both),
        P(both, None),
        P(both, None),
        P(both, None),
        P(both, None),
        P("expert", "dp", None),
        P("expert", "dp", None),
        P("expert", "dp", None),
    )
    out_specs = (
        P(both, None),
        P(both, None),
        P(both),
        P(both, None),
        P(both, None),
        P(both),
        P(both, None),
        P(both, None),
        P(both),
        P(both, None),
        P(both, None),
        P(both, None),
        P(both, None),
        P("expert", "dp", None),
        P("expert", "dp", None),
        P("expert", "dp", None),
    )
    return jax.shard_map(shards, mesh=mesh, in_specs=in_specs, out_specs=out_specs, check_vma=False)
```
